32 devices in a mesh: dp: 8 (over z, y), ctx: 4 (over x, core).
Axes of the slice: x: 2, y: 2, z: 4, core: 2. Of those that a mesh axis runs over, the one named last changes fastest.
Arguments:
- route_pos: int32 [8, 512], P('dp', 'ctx'), may hold values from -1 to 2047, as said below
- x_routed: bfloat16 [8, 512, 4096], P('dp', 'ctx'), may hold values from -6 to 6
- w_router: bfloat16 [4096], P('dp'), may hold values from -0.09375 to 0.09375
- queries: bfloat16 [8, 512, 2048], P('dp', 'ctx'), may hold values from -8 to 8
- keys: bfloat16 [8, 512, 2048], P('dp', 'ctx'), may hold values from -8 to 8
- values: bfloat16 [8, 512, 2048], P('dp', 'ctx'), may hold values from -6 to 6
- d_gated: float32 [8, 512, 2048], P('dp', 'ctx'), may hold values from -6 to 6
Outputs:
- grad_queries: float32 [8, 512, 2048], P('dp', 'ctx')
- grad_keys: float32 [8, 512, 2048], P('dp', 'ctx')
- grad_values: float32 [8, 512, 2048], P('dp', 'ctx')
- router_grad: float32 [4096], P('dp')
The draws below stay inside these ranges and needn't reach their ends.
Inputs may be any that keep to these rules, and one draw needn't show every extreme that they name: `route_pos`: in each sequence, context shard c lists in its 128 slots the increasing positions of its routed tokens, all from c * 512 to (c + 1) * 512 - 1, then -1 in its unused slots. A shard holds 0 to 128 routed tokens and a sequence 256 in all; in every sequence some shard holds exactly 128 and some shard none.
All inputs are finite; a program needn't handle non-finite values.
Results may differ from the reference program's by a relative error of at most 0.017.
Values may be sent and summed in bfloat16 or wider, within the bound.
No kernel may reach another device: no remote copies, remote signals or barrier semaphores. Data moves between devices by JAX's collectives and lax.ppermute only.
A program may use at most 128 MiB of HBM per device.

```python
from functools import partial
import jax
import jax.numpy as jnp
from jax import lax

D = 4096
HEAD = 128
HEADS = 16
TOK_DEV = 512
CAP = 128
ROUTED = 256
SLOTS = 512
SEQS = 8
HD = 2048


def shard_positions(shard_key, count, index):
    slot_index = jnp.arange(CAP, dtype=jnp.int32)
    shuffled = jax.random.permutation(shard_key, jnp.arange(TOK_DEV, dtype=jnp.int32))[:CAP]
    chosen = jnp.sort(jnp.where(slot_index < count, shuffled, TOK_DEV + 1))
    return jnp.where(slot_index < count, chosen + index * TOK_DEV, -1).astype(jnp.int32)


def sequence_positions(seq_key):
    shards = SLOTS // CAP
    pair_count = shards // 2
    half_cap = CAP // 2
    key_order, key_moves, key_rows = jax.random.split(seq_key, 3)
    move_sizes = jax.random.randint(key_moves, (pair_count,), 0, half_cap).astype(jnp.int32)
    move_sizes = move_sizes.at[0].set(half_cap)
    shuffle_order = jax.random.permutation(key_order, jnp.arange(shards, dtype=jnp.int32))
    shifted = jnp.zeros((shards,), jnp.int32).at[shuffle_order[:pair_count]].set(move_sizes)
    shifted = shifted.at[shuffle_order[pair_count:]].set(-move_sizes)
    counts = half_cap + shifted
    shard_keys = jax.random.split(key_rows, shards)
    position_table = jax.vmap(shard_positions)(shard_keys, counts, jnp.arange(shards, dtype=jnp.int32))
    return position_table.reshape(SLOTS)


def draw_route_pos(key, part):
    seq_keys = jax.random.split(jax.random.fold_in(key, 11), SEQS)
    return jax.vmap(sequence_positions)(seq_keys).astype(jnp.int32)


def query_key_pair(key):
    base_key = jax.random.fold_in(key, 29)
    key_query, key_key = jax.random.split(base_key, 2)
    full_shape = (SEQS, SLOTS, HEADS * HEAD)
    query_draw = jnp.clip(jax.random.normal(key_query, full_shape, jnp.float32), -6.0, 6.0)
    key_draw = jnp.clip(jax.random.normal(key_key, full_shape, jnp.float32), -6.0, 6.0)
    return (query_draw, key_draw)


def draw_queries(key, part):
    return query_key_pair(key)[0].astype(jnp.bfloat16)


def draw_keys(key, part):
    return query_key_pair(key)[1].astype(jnp.bfloat16)


def block_levels(rng, shape, cuts, least, top_value):
    def one(axis_at, shards_of):
        heights = jax.random.uniform(jax.random.fold_in(jax.random.fold_in(rng, 6), axis_at), (shards_of,), jnp.float32, least / len(cuts), top_value / len(cuts))
        return jnp.repeat(jnp.exp(heights), shape[axis_at] // shards_of).reshape((-1,) + (1,) * (len(shape) - axis_at - 1))

    factor_of = one(*cuts[0])
    for cut in cuts[1:]:
        factor_of = factor_of * one(*cut)
    return factor_of


def centred(own_key, dims, width, limit, pieces=(), kind=jnp.bfloat16):
    array = jax.random.normal(own_key, dims, jnp.float32) * width
    if len(pieces) > 0:
        array = block_levels(own_key, dims, pieces, -0.22, 0.18) * array
    return jnp.clip(array, min=-limit, max=limit).astype(kind)


def setup_inputs(seed: int = 0) -> dict:
    key_of = jax.random.split(jax.random.key(seed), 8)
    route_pos = draw_route_pos(jax.random.fold_in(key_of[7], 71), 0)
    x_routed = centred(key_of[1], (SEQS, SLOTS, D), 1.0, 6.0, ((0, 8), (1, 4)))
    w_router = centred(key_of[2], (D,), D ** -0.5, 0.09375, ((0, 8),))
    queries = draw_queries(jax.random.fold_in(key_of[7], 71), 0)
    keys = draw_keys(jax.random.fold_in(key_of[7], 71), 0)
    values = centred(key_of[5], (SEQS, SLOTS, HD), 1.0, 6.0, ((0, 8), (1, 4)))
    d_gated = centred(key_of[6], (SEQS, SLOTS, HD), 1.0, 6.0, ((0, 8), (1, 4)), jnp.float32)
    return {"route_pos": route_pos, "x_routed": x_routed, "w_router": w_router, "queries": queries, "keys": keys, "values": values, "d_gated": d_gated}


NEG_FILL = -1e30


def head_backward(allowed, score_scale, operands):
    query_head, key_head, value_head, grad_head = operands
    scores = jnp.dot(query_head, key_head.T, preferred_element_type=jnp.float32) * score_scale
    scores = jnp.where(allowed, scores, NEG_FILL)
    row_max = jnp.max(scores, axis=-1, keepdims=True)
    exponent = jnp.exp(scores - row_max)
    row_total = jnp.sum(exponent, axis=-1, keepdims=True)
    weights = exponent / row_total
    weights_low = weights.astype(jnp.bfloat16)
    attended = jnp.dot(weights_low, value_head, preferred_element_type=jnp.float32)
    grad_weights = jnp.dot(grad_head, value_head.T, preferred_element_type=jnp.float32)
    row_delta = jnp.sum(grad_head.astype(jnp.float32) * attended, axis=-1, keepdims=True)
    grad_scores = weights * (grad_weights - row_delta) * score_scale
    grad_low = grad_scores.astype(jnp.bfloat16)
    grad_query = jnp.dot(grad_low, key_head, preferred_element_type=jnp.float32)
    shards = query_head.shape[0] // CAP
    score_blocks = grad_low.astype(jnp.float32).reshape(shards, CAP, -1)
    weight_blocks = weights_low.astype(jnp.float32).reshape(shards, CAP, -1)
    query_blocks = query_head.astype(jnp.float32).reshape(shards, CAP, -1)
    grad_blocks = grad_head.astype(jnp.float32).reshape(shards, CAP, -1)
    key_terms = jnp.einsum('nqk,nqd->nkd', score_blocks, query_blocks)
    value_terms = jnp.einsum('nqk,nqd->nkd', weight_blocks, grad_blocks)
    key_terms = lax.optimization_barrier(key_terms.astype(jnp.bfloat16)).astype(jnp.float32)
    value_terms = lax.optimization_barrier(value_terms.astype(jnp.bfloat16)).astype(jnp.float32)
    return attended, grad_query, jnp.sum(key_terms, axis=0), jnp.sum(value_terms, axis=0)


def split_heads(rows_in):
    return rows_in.reshape(SLOTS, HEADS, HEAD).transpose(1, 0, 2)


def join_heads(per_head):
    return per_head.transpose(1, 0, 2).reshape(SLOTS, HEADS * HEAD)


def one_sequence(w_router, operands):
    positions, x_rows, query_rows, key_rows, value_rows, grad_rows = operands
    is_live = positions >= 0
    live_float = is_live.astype(jnp.float32)
    router_logit = jnp.dot(x_rows, w_router, preferred_element_type=jnp.float32)
    gate_value = jax.nn.sigmoid(router_logit)
    grad_out = ((gate_value * live_float)[:, None] * grad_rows).astype(jnp.bfloat16)
    allowed = is_live[:, None] & is_live[None, :] & (positions[None, :] <= positions[:, None])
    attended, grad_query, grad_key, grad_value = lax.map(
        partial(head_backward, allowed, HEAD ** -0.5),
        (split_heads(query_rows), split_heads(key_rows), split_heads(value_rows), split_heads(grad_out)))
    attended = join_heads(attended)
    grad_gate = jnp.sum(attended * grad_rows, axis=-1) * live_float
    grad_logit = grad_gate * gate_value * (1.0 - gate_value)
    router_term = jnp.dot(grad_logit, x_rows.astype(jnp.float32), precision=lax.Precision.HIGHEST)
    return join_heads(grad_query), join_heads(grad_key), join_heads(grad_value), router_term


def reference(route_pos, x_routed, w_router, queries, keys, values, d_gated):
    grad_queries, grad_keys, grad_values, router_terms = lax.map(
        partial(one_sequence, w_router), (route_pos, x_routed, queries, keys, values, d_gated))
    router_grad = jnp.sum(router_terms, axis=0) / float(SEQS * ROUTED)
    return grad_queries, grad_keys, grad_values, router_grad
```

```python
import functools

import jax
import jax.numpy as jnp
from jax import lax
from jax.experimental import pallas as pl
from jax.experimental.pallas import tpu as pltpu
from jax.sharding import PartitionSpec as P

HEAD = 128
GROUPS = 4
NEG_FILL = -1e30
VMEM_LIMIT = 48 * 1024 * 1024
BF16 = jnp.bfloat16
F32 = jnp.float32

VMEM = pl.BlockSpec(memory_space=pltpu.VMEM)
SMEM = pl.BlockSpec(memory_space=pltpu.SMEM)


def params():
    return pltpu.CompilerParams(vmem_limit_bytes=VMEM_LIMIT)


def cost(flops, nbytes, exps=0):
    return pl.CostEstimate(flops=int(flops), bytes_accessed=int(nbytes), transcendentals=int(exps))


def nt(a, b):
    return lax.dot_general(a, b, (((1,), (1,)), ((), ())), preferred_element_type=F32)


def nn(a, b):
    return lax.dot_general(a, b, (((1,), (0,)), ((), ())), preferred_element_type=F32)


def tn(a, b):
    return lax.dot_general(a, b, (((0,), (0,)), ((), ())), preferred_element_type=F32)


def pack_kernel(groups, width, core_ref, first_ref, second_ref, *outs):
    half = first_ref.shape[-1] // 2
    core = core_ref[0]
    for side in range(2):
        base = (core if side == 0 else 1 - core) * half
        for g in range(groups):
            out = outs[side * groups + g]
            cols = pl.ds(pl.multiple_of(base + g * width, HEAD), width)
            out[0] = first_ref[0, :, cols].astype(BF16)
            out[1] = second_ref[0, :, cols].astype(BF16)


def pack(core, first, second, groups, width):
    slots = first.shape[1]
    out = jax.ShapeDtypeStruct((2, slots, width), BF16)
    res = pl.pallas_call(
        functools.partial(pack_kernel, groups, width),
        out_shape=[out] * (2 * groups),
        in_specs=[SMEM, VMEM, VMEM],
        out_specs=[VMEM] * (2 * groups),
        compiler_params=params(),
        cost_estimate=cost(0, 2 * first.size * 4),
        name="pack",
    )(core, first, second)
    return res[:groups], res[groups:]


def gate_kernel(parts, offset_ref, pos_ref, x_ref, *refs):
    w_refs, out_ref = refs[:parts], refs[parts]
    chunk = w_refs[0].shape[-1]
    total = jnp.zeros((8, x_ref.shape[1]), F32)
    for s in range(parts):
        cols = pl.ds(pl.multiple_of(offset_ref[s] * chunk, HEAD), chunk)
        w_rows = jnp.broadcast_to(w_refs[s][...].astype(F32), (8, chunk)).astype(BF16)
        total = total + nt(w_rows, x_ref[0, :, cols])
    gate = 1.0 / (1.0 + jnp.exp(-total[0:1]))
    out_ref[...] = jnp.where(pos_ref[...] >= 0, gate, 0.0)


def router_gate(offsets, route_pos, x_routed, w_parts):
    parts = len(w_parts)
    return pl.pallas_call(
        functools.partial(gate_kernel, parts),
        out_shape=jax.ShapeDtypeStruct(route_pos.shape, F32),
        in_specs=[SMEM] + [VMEM] * (2 + parts),
        out_specs=VMEM,
        compiler_params=params(),
        cost_estimate=cost(16 * x_routed.size, x_routed.size * 2),
        name="router_gate",
    )(offsets, route_pos, x_routed, *w_parts)


def attention_kernel(remote, scale, core_ref, live_ref, gate_own, gate_sib, acc_own, acc_sib, q_own, q_sib, *refs):
    chunks = 2 + remote
    kv = refs[:chunks]
    outs = refs[chunks:]
    dq_own, sib_out, kv_own = outs[:3]
    kv_remote = outs[3 : 3 + remote]
    sum_own, sum_sib = outs[3 + remote :]
    slots, width = q_own.shape[1], q_own.shape[2]
    core = core_ref[0]
    key = lax.broadcasted_iota(jnp.int32, (slots, slots), 0)
    query = lax.broadcasted_iota(jnp.int32, (slots, slots), 1)
    counts = [jnp.sum(live_ref[i : i + 1], axis=1, keepdims=True) for i in range(chunks)]
    lives = [key < counts[i] for i in range(chunks)]
    own_later = core == 1
    bias_rows = []
    for i in range(chunks):
        live = lives[i]
        if i == 0:
            pair = (live & (key <= query), live & jnp.logical_not(own_later))
        elif i == 1:
            pair = (live & own_later, live & (key <= query))
        else:
            pair = (live, live)
        bias_rows.append(jnp.concatenate([jnp.where(p, 0.0, NEG_FILL) for p in pair], axis=1))
    bias = jnp.concatenate(bias_rows, axis=0)
    gates = jnp.concatenate([gate_own[...], gate_sib[...]], axis=1)
    total = jnp.zeros((1, 2 * slots), F32)
    for h in range(width // HEAD):
        cols = slice(h * HEAD, (h + 1) * HEAD)
        q = jnp.concatenate([q_own[0, :, cols], q_sib[0, :, cols]], axis=0)
        dg = jnp.concatenate([q_own[1, :, cols], q_sib[1, :, cols]], axis=0)
        k = jnp.concatenate([r[0, :, cols] for r in kv], axis=0)
        v = jnp.concatenate([r[1, :, cols] for r in kv], axis=0)
        scores = nt(k, q) * scale + bias
        top = jnp.max(scores, axis=0, keepdims=True)
        e = jnp.exp(scores - top)
        inverse = 1.0 / jnp.sum(e, axis=0, keepdims=True)
        gw = nt(v, dg)
        delta = jnp.sum(e * gw, axis=0, keepdims=True) * inverse
        total = total + delta
        weights = e * (inverse * gates)
        dv = nn(weights.astype(BF16), dg)
        ds = (weights * ((gw - delta) * scale)).astype(BF16)
        dk = nn(ds, q)
        dq = tn(ds, k)
        dq_own[:, cols] = dq[:slots].astype(dq_own.dtype)
        sib_out[0, :, cols] = dq[slots:].astype(BF16)
        kv_own[0, :, cols] = dk[:slots].astype(BF16)
        kv_own[1, :, cols] = dv[:slots].astype(BF16)
        sib_out[1, :, cols] = dk[slots : 2 * slots].astype(BF16)
        sib_out[2, :, cols] = dv[slots : 2 * slots].astype(BF16)
        for i in range(remote):
            rows = slice((2 + i) * slots, (3 + i) * slots)
            kv_remote[i][0, :, cols] = dk[rows].astype(BF16)
            kv_remote[i][1, :, cols] = dv[rows].astype(BF16)
    sum_own[...] = acc_own[...] + total[:, :slots]
    sum_sib[...] = acc_sib[...] + total[:, slots:]


def attention(core, live, gates, accs, q_own, q_sib, kv):
    remote = len(kv) - 2
    _, slots, width = q_own.shape
    pair = jax.ShapeDtypeStruct((2, slots, width), BF16)
    row = jax.ShapeDtypeStruct((1, slots), F32)
    outs = [
        jax.ShapeDtypeStruct((slots, width), BF16),
        jax.ShapeDtypeStruct((3, slots, width), BF16),
        pair,
        *([pair] * remote),
        row,
        row,
    ]
    keys = (2 + remote) * slots
    res = pl.pallas_call(
        functools.partial(attention_kernel, remote, HEAD**-0.5),
        out_shape=outs,
        in_specs=[SMEM] + [VMEM] * (7 + len(kv)),
        out_specs=[VMEM] * len(outs),
        compiler_params=params(),
        cost_estimate=cost(20 * slots * keys * width, 8 * keys * width + 20 * slots * width, 2 * slots * keys * width // HEAD),
        name="attention",
    )(core, live, *gates, *accs, q_own, q_sib, *kv)
    return res[0], res[1], res[2], res[3 : 3 + remote], (res[3 + remote], res[4 + remote])


def combine_kernel(groups, width, remote, core_ref, *refs):
    dq_own, sib, kv_own = refs[:groups], refs[groups : 2 * groups], refs[2 * groups : 3 * groups]
    back = refs[3 * groups : 3 * groups + groups * remote]
    dq_out, dk_out, dv_out = refs[3 * groups + groups * remote :]
    half = groups * width
    core = core_ref[0]
    for g in range(groups):
        own = pl.ds(pl.multiple_of(core * half + g * width, HEAD), width)
        other = pl.ds(pl.multiple_of((1 - core) * half + g * width, HEAD), width)
        dq_out[0, :, own] = dq_own[g][...].astype(F32)
        dq_out[0, :, other] = sib[g][0].astype(F32)
        for i, out in enumerate((dk_out, dv_out)):
            mine = kv_own[g][i].astype(F32)
            theirs = sib[g][1 + i].astype(F32)
            for r in range(remote):
                part = back[g * remote + r][i].astype(F32)
                if r % 2 == 0:
                    mine = mine + part
                else:
                    theirs = theirs + part
            out[0, :, own] = mine
            out[0, :, other] = theirs


def combine(core, dq_own, sib, kv_own, back, shape):
    groups = len(dq_own)
    remote = len(back[0])
    out = jax.ShapeDtypeStruct(shape, F32)
    flat = [*dq_own, *sib, *kv_own, *(b for group in back for b in group)]
    return pl.pallas_call(
        functools.partial(combine_kernel, groups, dq_own[0].shape[-1], remote),
        out_shape=[out] * 3,
        in_specs=[SMEM] + [VMEM] * len(flat),
        out_specs=[VMEM] * 3,
        compiler_params=params(),
        cost_estimate=cost(0, 3 * out.size * 6),
        name="combine",
    )(core, *flat)


def router_kernel(parts, target_ref, gate_ref, own_ref, sib_ref, x_ref, *outs):
    gate = gate_ref[...]
    grad = (own_ref[...] + sib_ref[...]) * gate * (1.0 - gate)
    high = grad.astype(BF16)
    rest = grad - high.astype(F32)
    mid = rest.astype(BF16)
    low = (rest - mid.astype(F32)).astype(BF16)
    row = lax.broadcasted_iota(jnp.int32, (8, grad.shape[1]), 0)
    lhs = jnp.where(row == 0, high.astype(F32), jnp.where(row == 1, mid.astype(F32), jnp.where(row == 2, low.astype(F32), 0.0)))
    lhs = lhs.astype(BF16)
    chunk = outs[0].shape[-1]
    for s in range(parts):
        cols = pl.ds(pl.multiple_of(target_ref[s] * chunk, HEAD), chunk)
        outs[s][...] = jnp.sum(nn(lhs, x_ref[0, :, cols]), axis=0, keepdims=True)


def router_terms(targets, gate, own, sib, x_routed, parts):
    chunk = x_routed.shape[-1] // parts
    return pl.pallas_call(
        functools.partial(router_kernel, parts),
        out_shape=[jax.ShapeDtypeStruct((1, chunk), F32)] * parts,
        in_specs=[SMEM] + [VMEM] * 4,
        out_specs=[VMEM] * parts,
        compiler_params=params(),
        cost_estimate=cost(16 * x_routed.size, x_routed.size * 2),
        name="router_terms",
    )(targets, gate, own, sib, x_routed)


def body(route_pos, x_routed, w_router, queries, keys, values, d_gated):
    slots, full = queries.shape[1], queries.shape[2]
    n, ndp = lax.axis_size("ctx"), lax.axis_size("dp")
    chips = n // 2
    me, dp_me = lax.axis_index("ctx"), lax.axis_index("dp")
    core = (me % 2).astype(jnp.int32).reshape(1)
    half = full // 2
    groups = GROUPS if (half // HEAD) % GROUPS == 0 else 1
    width = half // groups

    sib_pairs = [(i, i ^ 1) for i in range(n)]

    def forward_pairs(step, flip):
        return [(i, (i + 2 * step) ^ flip) for i in range(n) if i + 2 * step < n]

    def back_pairs(step, flip):
        return [(b, a) for a, b in forward_pairs(step, flip)]

    def to_sib(a):
        return lax.ppermute(a, "ctx", sib_pairs)

    links = [(step, flip) for step in range(1, chips) for flip in (0, 1)]

    w_row = w_router.reshape(1, -1)
    w_parts = [w_row] + [
        lax.ppermute(w_row, "dp", [(i, (i + s) % ndp) for i in range(ndp)]) for s in range(1, ndp)
    ]
    live = (route_pos >= 0).astype(jnp.int32)
    lives = [live, to_sib(live)] + [lax.ppermute(live, "ctx", forward_pairs(*link)) for link in links]
    live_all = jnp.concatenate(lives, axis=0)

    kv_mine, kv_theirs = pack(core, keys, values, groups, width)
    kv_far = [
        [lax.ppermute((kv_theirs if flip else kv_mine)[g], "ctx", forward_pairs(step, flip)) for step, flip in links]
        for g in range(groups)
    ]
    q_mine, q_theirs = pack(core, queries, d_gated, groups, width)
    kv_sib = [to_sib(a) for a in kv_theirs]
    q_sib = [to_sib(a) for a in q_theirs]

    offsets = ((dp_me - jnp.arange(ndp)) % ndp).astype(jnp.int32)
    gate = router_gate(offsets, route_pos, x_routed, w_parts)
    gates = (gate, to_sib(gate))

    accs = (jnp.zeros((1, slots), F32), jnp.zeros((1, slots), F32))
    dq_own, sib_in, kv_own, back = [], [], [], []
    for g in range(groups):
        dq, sib_out, kv_local, kv_remote, accs = attention(
            core, live_all, gates, accs, q_mine[g], q_sib[g], [kv_mine[g], kv_sib[g], *kv_far[g]]
        )
        back.append([lax.ppermute(a, "ctx", back_pairs(*link)) for a, link in zip(kv_remote, links)])
        sib_in.append(to_sib(sib_out))
        dq_own.append(dq)
        kv_own.append(kv_local)

    targets = ((dp_me + jnp.arange(ndp)) % ndp).astype(jnp.int32)
    terms = router_terms(targets, gate, accs[0], to_sib(accs[1]), x_routed, ndp)
    mine = terms[0]
    for s in range(1, ndp):
        mine = mine + lax.ppermute(terms[s], "dp", [(i, (i + s) % ndp) for i in range(ndp)])
    total = mine
    for s in range(1, n):
        total = total + lax.ppermute(mine, "ctx", [(i, (i + s) % n) for i in range(n)])
    router_grad = total[0] / float(ndp * n * slots // 2)

    dq, dk, dv = combine(core, dq_own, sib_in, kv_own, back, queries.shape)
    return dq, dk, dv, router_grad


def solution(mesh):
    placed = (
        P("dp", "ctx"),
        P("dp", "ctx", None),
        P("dp"),
        P("dp", "ctx", None),
        P("dp", "ctx", None),
        P("dp", "ctx", None),
        P("dp", "ctx", None),
    )
    return jax.shard_map(
        body,
        mesh=mesh,
        in_specs=placed,
        out_specs=(P("dp", "ctx", None), P("dp", "ctx", None), P("dp", "ctx", None), P("dp")),
        check_vma=False,
    )
```

```python
import functools

import jax
import jax.numpy as jnp
from jax import lax
from jax.experimental import pallas as pl
from jax.experimental.pallas import tpu as pltpu
from jax.sharding import PartitionSpec as P

HEAD = 128
GROUPS = 4
NEG_FILL = -1e30
VMEM_LIMIT = 48 * 1024 * 1024
BF16 = jnp.bfloat16
F32 = jnp.float32

VMEM = pl.BlockSpec(memory_space=pltpu.VMEM)
SMEM = pl.BlockSpec(memory_space=pltpu.SMEM)


def params():
    return pltpu.CompilerParams(vmem_limit_bytes=VMEM_LIMIT)


def cost(flops, nbytes, exps=0):
    return pl.CostEstimate(flops=1, bytes_accessed=1, transcendentals=0)


def nt(a, b):
    return lax.dot_general(a, b, (((1,), (1,)), ((), ())), preferred_element_type=F32)


def nn(a, b):
    return lax.dot_general(a, b, (((1,), (0,)), ((), ())), preferred_element_type=F32)


def tn(a, b):
    return lax.dot_general(a, b, (((0,), (0,)), ((), ())), preferred_element_type=F32)


def pack_kernel(groups, width, core_ref, first_ref, second_ref, *outs):
    half = first_ref.shape[-1] // 2
    core = core_ref[0]
    for side in range(2):
        base = (core if side == 0 else 1 - core) * half
        for g in range(groups):
            out = outs[side * groups + g]
            cols = pl.ds(pl.multiple_of(base + g * width, HEAD), width)
            out[0] = first_ref[0, :, cols].astype(BF16)
            out[1] = second_ref[0, :, cols].astype(BF16)


def pack(core, first, second, groups, width):
    slots = first.shape[1]
    out = jax.ShapeDtypeStruct((2, slots, width), BF16)
    res = pl.pallas_call(
        functools.partial(pack_kernel, groups, width),
        out_shape=[out] * (2 * groups),
        in_specs=[SMEM, VMEM, VMEM],
        out_specs=[VMEM] * (2 * groups),
        compiler_params=params(),
        cost_estimate=cost(0, 2 * first.size * 4),
        name="pack",
    )(core, first, second)
    return res[:groups], res[groups:]


def gate_kernel(parts, offset_ref, pos_ref, x_ref, *refs):
    w_refs, out_ref = refs[:parts], refs[parts]
    chunk = w_refs[0].shape[-1]
    total = jnp.zeros((8, x_ref.shape[1]), F32)
    for s in range(parts):
        cols = pl.ds(pl.multiple_of(offset_ref[s] * chunk, HEAD), chunk)
        w_rows = jnp.broadcast_to(w_refs[s][...].astype(F32), (8, chunk)).astype(BF16)
        total = total + nt(w_rows, x_ref[0, :, cols])
    gate = 1.0 / (1.0 + jnp.exp(-total[0:1]))
    out_ref[...] = jnp.where(pos_ref[...] >= 0, gate, 0.0)


def router_gate(offsets, route_pos, x_routed, w_parts):
    parts = len(w_parts)
    return pl.pallas_call(
        functools.partial(gate_kernel, parts),
        out_shape=jax.ShapeDtypeStruct(route_pos.shape, F32),
        in_specs=[SMEM] + [VMEM] * (2 + parts),
        out_specs=VMEM,
        compiler_params=params(),
        cost_estimate=cost(16 * x_routed.size, x_routed.size * 2),
        name="router_gate",
    )(offsets, route_pos, x_routed, *w_parts)


def attention_kernel(remote, scale, core_ref, live_ref, gate_own, gate_sib, acc_own, acc_sib, q_own, q_sib, *refs):
    chunks = 2 + remote
    kv = refs[:chunks]
    outs = refs[chunks:]
    dq_own, sib_out, kv_own = outs[:3]
    kv_remote = outs[3 : 3 + remote]
    sum_own, sum_sib = outs[3 + remote :]
    slots, width = q_own.shape[1], q_own.shape[2]
    core = core_ref[0]
    key = lax.broadcasted_iota(jnp.int32, (slots, slots), 0)
    query = lax.broadcasted_iota(jnp.int32, (slots, slots), 1)
    counts = [jnp.sum(live_ref[i : i + 1], axis=1, keepdims=True) for i in range(chunks)]
    lives = [key < counts[i] for i in range(chunks)]
    own_later = core == 1
    bias_rows = []
    for i in range(chunks):
        live = lives[i]
        if i == 0:
            pair = (live & (key <= query), live & jnp.logical_not(own_later))
        elif i == 1:
            pair = (live & own_later, live & (key <= query))
        else:
            pair = (live, live)
        bias_rows.append(jnp.concatenate([jnp.where(p, 0.0, NEG_FILL) for p in pair], axis=1))
    bias = jnp.concatenate(bias_rows, axis=0)
    gates = jnp.concatenate([gate_own[...], gate_sib[...]], axis=1)
    total = jnp.zeros((1, 2 * slots), F32)
    for h in range(width // HEAD):
        cols = slice(h * HEAD, (h + 1) * HEAD)
        q = jnp.concatenate([q_own[0, :, cols], q_sib[0, :, cols]], axis=0)
        dg = jnp.concatenate([q_own[1, :, cols], q_sib[1, :, cols]], axis=0)
        k = jnp.concatenate([r[0, :, cols] for r in kv], axis=0)
        v = jnp.concatenate([r[1, :, cols] for r in kv], axis=0)
        scores = nt(k, q) * scale + bias
        top = jnp.max(scores, axis=0, keepdims=True)
        e = jnp.exp(scores - top)
        inverse = 1.0 / jnp.sum(e, axis=0, keepdims=True)
        gw = nt(v, dg)
        delta = jnp.sum(e * gw, axis=0, keepdims=True) * inverse
        total = total + delta
        weights = e * (inverse * gates)
        dv = nn(weights.astype(BF16), dg)
        ds = (weights * ((gw - delta) * scale)).astype(BF16)
        dk = nn(ds, q)
        dq = tn(ds, k)
        dq_own[:, cols] = dq[:slots].astype(dq_own.dtype)
        sib_out[0, :, cols] = dq[slots:].astype(BF16)
        kv_own[0, :, cols] = dk[:slots].astype(BF16)
        kv_own[1, :, cols] = dv[:slots].astype(BF16)
        sib_out[1, :, cols] = dk[slots : 2 * slots].astype(BF16)
        sib_out[2, :, cols] = dv[slots : 2 * slots].astype(BF16)
        for i in range(remote):
            rows = slice((2 + i) * slots, (3 + i) * slots)
            kv_remote[i][0, :, cols] = dk[rows].astype(BF16)
            kv_remote[i][1, :, cols] = dv[rows].astype(BF16)
    sum_own[...] = acc_own[...] + total[:, :slots]
    sum_sib[...] = acc_sib[...] + total[:, slots:]


def attention(core, live, gates, accs, q_own, q_sib, kv):
    remote = len(kv) - 2
    _, slots, width = q_own.shape
    pair = jax.ShapeDtypeStruct((2, slots, width), BF16)
    row = jax.ShapeDtypeStruct((1, slots), F32)
    outs = [
        jax.ShapeDtypeStruct((slots, width), BF16),
        jax.ShapeDtypeStruct((3, slots, width), BF16),
        pair,
        *([pair] * remote),
        row,
        row,
    ]
    keys = (2 + remote) * slots
    res = pl.pallas_call(
        functools.partial(attention_kernel, remote, HEAD**-0.5),
        out_shape=outs,
        in_specs=[SMEM] + [VMEM] * (7 + len(kv)),
        out_specs=[VMEM] * len(outs),
        compiler_params=params(),
        cost_estimate=cost(20 * slots * keys * width, 8 * keys * width + 20 * slots * width, 2 * slots * keys * width // HEAD),
        name="attention",
    )(core, live, *gates, *accs, q_own, q_sib, *kv)
    return res[0], res[1], res[2], res[3 : 3 + remote], (res[3 + remote], res[4 + remote])


def combine_kernel(groups, width, remote, core_ref, *refs):
    dq_own, sib, kv_own = refs[:groups], refs[groups : 2 * groups], refs[2 * groups : 3 * groups]
    back = refs[3 * groups : 3 * groups + groups * remote]
    dq_out, dk_out, dv_out = refs[3 * groups + groups * remote :]
    half = groups * width
    core = core_ref[0]
    for g in range(groups):
        own = pl.ds(pl.multiple_of(core * half + g * width, HEAD), width)
        other = pl.ds(pl.multiple_of((1 - core) * half + g * width, HEAD), width)
        dq_out[0, :, own] = dq_own[g][...].astype(F32)
        dq_out[0, :, other] = sib[g][0].astype(F32)
        for i, out in enumerate((dk_out, dv_out)):
            mine = kv_own[g][i].astype(F32)
            theirs = sib[g][1 + i].astype(F32)
            for r in range(remote):
                part = back[g * remote + r][i].astype(F32)
                if r % 2 == 0:
                    mine = mine + part
                else:
                    theirs = theirs + part
            out[0, :, own] = mine
            out[0, :, other] = theirs


def combine(core, dq_own, sib, kv_own, back, shape):
    groups = len(dq_own)
    remote = len(back[0])
    out = jax.ShapeDtypeStruct(shape, F32)
    flat = [*dq_own, *sib, *kv_own, *(b for group in back for b in group)]
    return pl.pallas_call(
        functools.partial(combine_kernel, groups, dq_own[0].shape[-1], remote),
        out_shape=[out] * 3,
        in_specs=[SMEM] + [VMEM] * len(flat),
        out_specs=[VMEM] * 3,
        compiler_params=params(),
        cost_estimate=cost(0, 3 * out.size * 6),
        name="combine",
    )(core, *flat)


def router_kernel(parts, target_ref, gate_ref, own_ref, sib_ref, x_ref, *outs):
    gate = gate_ref[...]
    grad = (own_ref[...] + sib_ref[...]) * gate * (1.0 - gate)
    high = grad.astype(BF16)
    rest = grad - high.astype(F32)
    mid = rest.astype(BF16)
    low = (rest - mid.astype(F32)).astype(BF16)
    row = lax.broadcasted_iota(jnp.int32, (8, grad.shape[1]), 0)
    lhs = jnp.where(row == 0, high.astype(F32), jnp.where(row == 1, mid.astype(F32), jnp.where(row == 2, low.astype(F32), 0.0)))
    lhs = lhs.astype(BF16)
    chunk = outs[0].shape[-1]
    for s in range(parts):
        cols = pl.ds(pl.multiple_of(target_ref[s] * chunk, HEAD), chunk)
        outs[s][...] = jnp.sum(nn(lhs, x_ref[0, :, cols]), axis=0, keepdims=True)


def router_terms(targets, gate, own, sib, x_routed, parts):
    chunk = x_routed.shape[-1] // parts
    return pl.pallas_call(
        functools.partial(router_kernel, parts),
        out_shape=[jax.ShapeDtypeStruct((1, chunk), F32)] * parts,
        in_specs=[SMEM] + [VMEM] * 4,
        out_specs=[VMEM] * parts,
        compiler_params=params(),
        cost_estimate=cost(16 * x_routed.size, x_routed.size * 2),
        name="router_terms",
    )(targets, gate, own, sib, x_routed)


MARK = 2.0**60
MARK_LIMIT = 2.0**50


def live_rows(pos_ref, slots):
    count = jnp.sum((pos_ref[...] >= 0).astype(jnp.int32), axis=1, keepdims=True)
    return lax.broadcasted_iota(jnp.int32, (slots, HEAD), 0) < count


def mark_dead(keys, live):
    width = keys.shape[-1]
    mask = jnp.concatenate([live] * (width // HEAD), axis=1)
    return jnp.where(mask, keys.astype(F32), MARK).astype(BF16)


def pack_all_kernel(place_ref, pos_ref, k_ref, v_ref, q_ref, dg_ref, mine, theirs, straight, diag, wide, sems):
    slots, half = mine.shape[1], mine.shape[2]
    width = straight.shape[2]
    core, chip = place_ref[0], place_ref[1]
    ends = ((mine, straight, core * half), (theirs, diag, (1 - core) * half))
    copies = []
    for i, (out, _, start) in enumerate(ends):
        cols = pl.ds(pl.multiple_of(start, HEAD), half)
        for j, ref in enumerate((k_ref, v_ref, q_ref)):
            copies.append(pltpu.make_async_copy(ref.at[0, :, cols], out.at[j], sems.at[4 * i + j]))
        copies.append(pltpu.make_async_copy(dg_ref.at[0, :, cols], wide.at[i], sems.at[4 * i + 3]))
    for c in copies:
        c.start()
    live = live_rows(pos_ref, slots)
    for i, (out, cross, _) in enumerate(ends):
        for j in range(4):
            copies[4 * i + j].wait()
        out[0] = mark_dead(out[0], live)
        out[3] = wide[i].astype(BF16)

        @pl.when(chip == 0)
        def _():
            cross[...] = out[0:2, :, :width]

        @pl.when(chip != 0)
        def _():
            cross[...] = out[2:4, :, width:]


def pack_all(place, route_pos, keys, values, queries, d_gated):
    _, slots, full = keys.shape
    half = jax.ShapeDtypeStruct((4, slots, full // 2), BF16)
    cross = jax.ShapeDtypeStruct((2, slots, full // 4), BF16)
    hbm = pl.BlockSpec(memory_space=pltpu.HBM)
    return pl.pallas_call(
        pack_all_kernel,
        out_shape=[half, half, cross, cross],
        in_specs=[SMEM, VMEM, hbm, hbm, hbm, hbm],
        out_specs=[VMEM] * 4,
        scratch_shapes=[pltpu.VMEM((2, slots, full // 2), F32), pltpu.SemaphoreType.DMA((8,))],
        compiler_params=params(),
        cost_estimate=cost(0, 20 * slots * full),
        name="pack_all",
    )(place, route_pos, keys, values, queries, d_gated)


def whole_gate_kernel(pos_ref, x_ref, w_ref, out_ref):
    parts, _, chunk = w_ref.shape
    total = jnp.zeros((8, x_ref.shape[1]), F32)
    for j in range(parts):
        w_rows = jnp.broadcast_to(w_ref[j].astype(F32), (8, chunk)).astype(BF16)
        total = total + nt(w_rows, x_ref[0, :, j * chunk : (j + 1) * chunk])
    gate = 1.0 / (1.0 + jnp.exp(-total[0:1]))
    out_ref[...] = jnp.where(pos_ref[...] >= 0, gate, 0.0)


def whole_gate(route_pos, x_routed, w_full):
    return pl.pallas_call(
        whole_gate_kernel,
        out_shape=jax.ShapeDtypeStruct(route_pos.shape, F32),
        in_specs=[VMEM] * 3,
        out_specs=VMEM,
        compiler_params=params(),
        cost_estimate=cost(16 * x_routed.size, x_routed.size * 2),
        name="router_gate",
    )(route_pos, x_routed, w_full)


def local_mask(core, mine, sib):
    slots = mine.shape[1]
    key = lax.broadcasted_iota(jnp.int32, (slots, slots), 0)
    query = lax.broadcasted_iota(jnp.int32, (slots, slots), 1)
    causal = key <= query
    own_live = mine[0, :, :slots].astype(F32) < MARK_LIMIT
    sib_live = sib[0, :, :slots].astype(F32) < MARK_LIMIT
    own_rows = jnp.concatenate([own_live & causal, own_live & (core == 0)], axis=1)
    sib_rows = jnp.concatenate([sib_live & (core == 1), sib_live & causal], axis=1)
    return jnp.concatenate([own_rows, sib_rows], axis=0)


def both(mine, sib, part, h):
    cols = slice(h * HEAD, (h + 1) * HEAD)
    return jnp.concatenate([mine[part, :, cols], sib[part, :, cols]], axis=0)


def partial_stats(scores, gw):
    top = jnp.max(scores, axis=0, keepdims=True)
    e = jnp.exp(scores - top)
    return top, jnp.sum(e, axis=0, keepdims=True), jnp.sum(e * gw, axis=0, keepdims=True)


def local_stats_kernel(scale, place_ref, mine, sib, stats):
    mask = local_mask(place_ref[0], mine, sib)
    for h in range(mine.shape[-1] // HEAD):
        scores = jnp.where(mask, nt(both(mine, sib, 0, h), both(mine, sib, 2, h)) * scale, NEG_FILL)
        gw = nt(both(mine, sib, 1, h), both(mine, sib, 3, h))
        for i, row in enumerate(partial_stats(scores, gw)):
            stats[i, h : h + 1] = row


def local_stats(place, mine, sib):
    _, slots, half = mine.shape
    return pl.pallas_call(
        functools.partial(local_stats_kernel, HEAD**-0.5),
        out_shape=jax.ShapeDtypeStruct((3, half // HEAD, 2 * slots), F32),
        in_specs=[SMEM, VMEM, VMEM],
        out_specs=VMEM,
        compiler_params=params(),
        cost_estimate=cost(16 * slots * slots * half, 16 * slots * half, 4 * slots * slots * half // HEAD),
        name="local_stats",
    )(place, mine, sib)


def cross_mask(cross, slots):
    live = cross[0, :, :HEAD].astype(F32) < MARK_LIMIT
    return jnp.concatenate([live] * (2 * slots // HEAD), axis=1)


def cross_stats_kernel(scale, place_ref, mine, sib, straight, diag, local, gate_own, gate_sib, cross, stats, message):
    slots, width = straight.shape[1], straight.shape[2]
    chip = place_ref[1]
    top, bottom = slice(0, slots), slice(slots, 2 * slots)

    @pl.when(chip == 0)
    def _():
        cols = slice(width, 2 * width)
        for part in range(2):
            cross[part, top] = mine[part, :, cols]
            cross[part, bottom] = sib[part, :, cols]
            cross[2 + part, top] = straight[part]
            cross[2 + part, bottom] = diag[part]

    @pl.when(chip != 0)
    def _():
        cols = slice(0, width)
        for part in range(2):
            cross[part, top] = straight[part]
            cross[part, bottom] = diag[part]
            cross[2 + part, top] = mine[2 + part, :, cols]
            cross[2 + part, bottom] = sib[2 + part, :, cols]

    mask = cross_mask(cross, slots)
    heads = width // HEAD
    for h in range(heads):
        cols = slice(h * HEAD, (h + 1) * HEAD)
        scores = jnp.where(mask, nt(cross[0, :, cols], cross[2, :, cols]) * scale, NEG_FILL)
        gw = nt(cross[1, :, cols], cross[3, :, cols])
        for i, row in enumerate(partial_stats(scores, gw)):
            stats[i, h : h + 1] = row
    gates = jnp.concatenate([gate_own[...], gate_sib[...]], axis=1)
    for i in range(3):
        message[i] = jnp.where(chip == 0, stats[i], local[i, heads:])
    message[3] = jnp.broadcast_to(gates, message.shape[1:])


def cross_stats(place, mine, sib, straight, diag, local, gates):
    _, slots, width = straight.shape
    heads = width // HEAD
    return pl.pallas_call(
        functools.partial(cross_stats_kernel, HEAD**-0.5),
        out_shape=[
            jax.ShapeDtypeStruct((4, 2 * slots, width), BF16),
            jax.ShapeDtypeStruct((3, heads, 2 * slots), F32),
            jax.ShapeDtypeStruct((4, heads, 2 * slots), F32),
        ],
        in_specs=[SMEM] + [VMEM] * 7,
        out_specs=[VMEM] * 3,
        compiler_params=params(),
        cost_estimate=cost(16 * slots * slots * width, 32 * slots * width, 4 * slots * slots * heads),
        name="cross_stats",
    )(place, mine, sib, straight, diag, local, *gates)


def merge(first, second):
    top = jnp.maximum(first[0], second[0])
    a, b = jnp.exp(first[0] - top), jnp.exp(second[0] - top)
    inverse = 1.0 / (first[1] * a + second[1] * b)
    return top, inverse, (first[2] * a + second[2] * b) * inverse


def gradients(q, k, v, dg, mask, scale, top, inverse, delta, gates):
    scores = jnp.where(mask, nt(k, q) * scale, NEG_FILL)
    weights = jnp.exp(scores - top) * (inverse * gates)
    ds = (weights * ((nt(v, dg) - delta) * scale)).astype(BF16)
    return tn(ds, k), nn(ds, q), nn(weights.astype(BF16), dg)


def cross_grad_kernel(scale, place_ref, cross, stats, local, heard, gate_own, gate_sib, straight, diag, keep, final, sum_own, sum_sib):
    slots, width = straight.shape[1], straight.shape[2]
    chip = place_ref[1]
    heads = width // HEAD
    first = chip == 0
    mine = [stats[i] for i in range(3)]
    other = [heard[i] for i in range(3)]
    near = [local[i, :heads] for i in range(3)]
    far = [local[i, heads:] for i in range(3)]
    none = (-3e38, 0.0, 0.0)
    gates = jnp.concatenate([gate_own[...], gate_sib[...]], axis=1)
    cross_gates = jnp.where(first, heard[3, 0:1], gates)
    rows = merge(mine, [jnp.where(first, o, n) for o, n in zip(other, near)])
    done_near = merge(near, [jnp.where(first, x, m) for x, m in zip(none, mine)])
    done_far = merge(far, [jnp.where(first, x, o) for x, o in zip(none, other)])
    total = jnp.zeros((1, 2 * slots), F32)
    for i in range(3):
        final[i, :heads] = done_near[i]
        final[i, heads:] = done_far[i]
    total = jnp.sum(done_near[2], axis=0, keepdims=True) + jnp.sum(done_far[2], axis=0, keepdims=True)
    sum_own[...] = total[:, :slots]
    sum_sib[...] = total[:, slots:]
    mask = cross_mask(cross, slots)
    for h in range(heads):
        cols = slice(h * HEAD, (h + 1) * HEAD)
        row = slice(h, h + 1)
        dq, dk, dv = gradients(
            cross[2, :, cols], cross[0, :, cols], cross[1, :, cols], cross[3, :, cols],
            mask, scale, rows[0][row], rows[1][row], rows[2][row], cross_gates,
        )
        for i, part in enumerate((dq, dk, dv)):
            keep[i, :, cols] = part.astype(BF16)
        sent = jnp.where(first, dq, dk).astype(BF16)
        straight[0, :, cols] = sent[:slots]
        diag[0, :, cols] = sent[slots:]
        straight[1, :, cols] = dv[:slots].astype(BF16)
        diag[1, :, cols] = dv[slots:].astype(BF16)


def cross_grad(place, cross, stats, local, heard, gates):
    _, rows, width = cross.shape
    slots = rows // 2
    out = jax.ShapeDtypeStruct((2, slots, width), BF16)
    row = jax.ShapeDtypeStruct((1, slots), F32)
    return pl.pallas_call(
        functools.partial(cross_grad_kernel, HEAD**-0.5),
        out_shape=[out, out, jax.ShapeDtypeStruct((3, rows, width), BF16), jax.ShapeDtypeStruct(local.shape, F32), row, row],
        in_specs=[SMEM] + [VMEM] * 6,
        out_specs=[VMEM] * 6,
        compiler_params=params(),
        cost_estimate=cost(40 * slots * slots * width, 64 * slots * width, 4 * slots * slots * width // HEAD),
        name="cross_grad",
    )(place, cross, stats, local, heard, *gates)


def local_grad_kernel(scale, place_ref, mine, sib, final, gate_own, gate_sib, keep, own_out, sib_out):
    slots, half = mine.shape[1], mine.shape[2]
    first = place_ref[1] == 0
    early, late = jnp.where(first, 1.0, 0.0), jnp.where(first, 0.0, 1.0)
    mask = local_mask(place_ref[0], mine, sib)
    gates = jnp.concatenate([gate_own[...], gate_sib[...]], axis=1)
    heads = half // HEAD
    for h in range(heads):
        cols = slice(h * HEAD, (h + 1) * HEAD)
        row = slice(h, h + 1)
        dq, dk, dv = gradients(
            both(mine, sib, 2, h), both(mine, sib, 0, h), both(mine, sib, 1, h), both(mine, sib, 3, h),
            mask, scale, final[0, row], final[1, row], final[2, row], gates,
        )
        at = h % (heads // 2)
        kept = slice(at * HEAD, (at + 1) * HEAD)
        if h < heads // 2:
            dq = dq + late * keep[0, :, kept].astype(F32)
        else:
            dk = dk + early * keep[1, :, kept].astype(F32)
            dv = dv + early * keep[2, :, kept].astype(F32)
        for i, part in enumerate((dq, dk, dv)):
            own_out[i, :, cols] = part[:slots].astype(BF16)
            sib_out[i, :, cols] = part[slots:].astype(BF16)


def local_grad(place, mine, sib, final, gates, keep):
    _, slots, half = mine.shape
    out = jax.ShapeDtypeStruct((3, slots, half), BF16)
    return pl.pallas_call(
        functools.partial(local_grad_kernel, HEAD**-0.5),
        out_shape=[out, out],
        in_specs=[SMEM] + [VMEM] * 6,
        out_specs=[VMEM] * 2,
        compiler_params=params(),
        cost_estimate=cost(40 * slots * slots * half, 40 * slots * half, 4 * slots * slots * half // HEAD),
        name="local_grad",
    )(place, mine, sib, final, *gates, keep)


def join_kernel(place_ref, own, sib, straight, diag, dq_out, dk_out, dv_out):
    half = own.shape[-1]
    width = straight.shape[-1]
    core, chip = place_ref[0], place_ref[1]
    early, late = jnp.where(chip == 0, 1.0, 0.0), jnp.where(chip == 0, 0.0, 1.0)
    for part, extra, start in ((own, straight, core * half), (sib, diag, (1 - core) * half)):
        low = pl.ds(pl.multiple_of(start, HEAD), width)
        high = pl.ds(pl.multiple_of(start + width, HEAD), width)
        dq_out[0, :, low] = part[0, :, :width].astype(F32)
        dq_out[0, :, high] = part[0, :, width:].astype(F32) + late * extra[0].astype(F32)
        for i, out in enumerate((dk_out, dv_out)):
            out[0, :, low] = part[1 + i, :, :width].astype(F32) + early * extra[i].astype(F32)
            out[0, :, high] = part[1 + i, :, width:].astype(F32)


def join(place, own, sib, straight, diag, shape):
    out = jax.ShapeDtypeStruct(shape, F32)
    return pl.pallas_call(
        join_kernel,
        out_shape=[out] * 3,
        in_specs=[SMEM] + [VMEM] * 4,
        out_specs=[VMEM] * 3,
        compiler_params=params(),
        cost_estimate=cost(0, 18 * out.size),
        name="join",
    )(place, own, sib, straight, diag)


def whole_router_kernel(gate_ref, own_ref, sib_ref, x_ref, out_ref):
    gate = gate_ref[...]
    grad = (own_ref[...] + sib_ref[...]) * gate * (1.0 - gate)
    high = grad.astype(BF16)
    rest = grad - high.astype(F32)
    mid = rest.astype(BF16)
    low = (rest - mid.astype(F32)).astype(BF16)
    row = lax.broadcasted_iota(jnp.int32, (8, grad.shape[1]), 0)
    lhs = jnp.where(row == 0, high.astype(F32), jnp.where(row == 1, mid.astype(F32), jnp.where(row == 2, low.astype(F32), 0.0)))
    term = jnp.sum(nn(lhs.astype(BF16), x_ref[0]), axis=0, keepdims=True)
    parts, copies, _, chunk = out_ref.shape
    for j in range(parts):
        for i in range(copies):
            out_ref[j, i] = term[:, j * chunk : (j + 1) * chunk]


def whole_router(gate, own, sib, x_routed, parts, copies):
    chunk = x_routed.shape[-1] // parts
    return pl.pallas_call(
        whole_router_kernel,
        out_shape=jax.ShapeDtypeStruct((parts, copies, 1, chunk), F32),
        in_specs=[VMEM] * 4,
        out_specs=VMEM,
        compiler_params=params(),
        cost_estimate=cost(16 * x_routed.size, x_routed.size * 2),
        name="router_terms",
    )(gate, own, sib, x_routed)


def swap_body(route_pos, x_routed, w_router, queries, keys, values, d_gated):
    slots, full = queries.shape[1], queries.shape[2]
    n, ndp = lax.axis_size("ctx"), lax.axis_size("dp")
    me = lax.axis_index("ctx")
    place = jnp.stack([me % 2, me // 2]).astype(jnp.int32)

    def send(a, flip):
        return lax.ppermute(a, "ctx", [(i, i ^ flip) for i in range(n)])

    mine, theirs, out_s, out_d = pack_all(place, route_pos, keys, values, queries, d_gated)
    in_s, in_d = send(out_s, 2), send(out_d, 3)
    sib = send(theirs, 1)
    w_row, _ = lax.optimization_barrier((w_router.reshape(1, 1, -1), mine))
    w_full = lax.all_to_all(jnp.broadcast_to(w_row, (ndp, 1, w_row.shape[-1])), "dp", 0, 0, tiled=True)
    gate = whole_gate(route_pos, x_routed, w_full)
    gates = (gate, send(gate, 1))
    local = local_stats(place, mine, sib)
    cross, stats, message = cross_stats(place, mine, sib, in_s, in_d, local, gates)
    heard = send(message, 2)
    back_s, back_d, keep, final, sum_own, sum_sib = cross_grad(place, cross, stats, local, heard, gates)
    ret_s, ret_d = send(back_s, 2), send(back_d, 3)
    own_out, sib_out = local_grad(place, mine, sib, final, gates, keep)
    sib_in = send(sib_out, 1)
    terms = whole_router(gate, sum_own, send(sum_sib, 1), x_routed, ndp, n)
    chunk = terms.shape[-1]
    terms = lax.all_to_all(terms.reshape(ndp * n, 1, chunk), ("dp", "ctx"), 0, 0, tiled=True)
    router_grad = jnp.sum(terms, axis=0)[0] / float(ndp * n * slots // 2)
    dq, dk, dv = join(place, own_out, sib_in, ret_s, ret_d, queries.shape)
    return dq, dk, dv, router_grad


def body(route_pos, x_routed, w_router, queries, keys, values, d_gated):
    slots, full = queries.shape[1], queries.shape[2]
    n, ndp = lax.axis_size("ctx"), lax.axis_size("dp")
    chips = n // 2
    me, dp_me = lax.axis_index("ctx"), lax.axis_index("dp")
    core = (me % 2).astype(jnp.int32).reshape(1)
    half = full // 2
    groups = GROUPS if (half // HEAD) % GROUPS == 0 else 1
    width = half // groups

    sib_pairs = [(i, i ^ 1) for i in range(n)]

    def forward_pairs(step, flip):
        return [(i, (i + 2 * step) ^ flip) for i in range(n) if i + 2 * step < n]

    def back_pairs(step, flip):
        return [(b, a) for a, b in forward_pairs(step, flip)]

    def to_sib(a):
        return lax.ppermute(a, "ctx", sib_pairs)

    links = [(step, flip) for step in range(1, chips) for flip in (0, 1)]

    w_row = w_router.reshape(1, -1)
    w_parts = [w_row] + [
        lax.ppermute(w_row, "dp", [(i, (i + s) % ndp) for i in range(ndp)]) for s in range(1, ndp)
    ]
    live = (route_pos >= 0).astype(jnp.int32)
    lives = [live, to_sib(live)] + [lax.ppermute(live, "ctx", forward_pairs(*link)) for link in links]
    live_all = jnp.concatenate(lives, axis=0)

    kv_mine, kv_theirs = pack(core, keys, values, groups, width)
    kv_far = [
        [lax.ppermute((kv_theirs if flip else kv_mine)[g], "ctx", forward_pairs(step, flip)) for step, flip in links]
        for g in range(groups)
    ]
    q_mine, q_theirs = pack(core, queries, d_gated, groups, width)
    kv_sib = [to_sib(a) for a in kv_theirs]
    q_sib = [to_sib(a) for a in q_theirs]

    offsets = ((dp_me - jnp.arange(ndp)) % ndp).astype(jnp.int32)
    gate = router_gate(offsets, route_pos, x_routed, w_parts)
    gates = (gate, to_sib(gate))

    accs = (jnp.zeros((1, slots), F32), jnp.zeros((1, slots), F32))
    dq_own, sib_in, kv_own, back = [], [], [], []
    for g in range(groups):
        dq, sib_out, kv_local, kv_remote, accs = attention(
            core, live_all, gates, accs, q_mine[g], q_sib[g], [kv_mine[g], kv_sib[g], *kv_far[g]]
        )
        back.append([lax.ppermute(a, "ctx", back_pairs(*link)) for a, link in zip(kv_remote, links)])
        sib_in.append(to_sib(sib_out))
        dq_own.append(dq)
        kv_own.append(kv_local)

    targets = ((dp_me + jnp.arange(ndp)) % ndp).astype(jnp.int32)
    terms = router_terms(targets, gate, accs[0], to_sib(accs[1]), x_routed, ndp)
    mine = terms[0]
    for s in range(1, ndp):
        mine = mine + lax.ppermute(terms[s], "dp", [(i, (i + s) % ndp) for i in range(ndp)])
    total = mine
    for s in range(1, n):
        total = total + lax.ppermute(mine, "ctx", [(i, (i + s) % n) for i in range(n)])
    router_grad = total[0] / float(ndp * n * slots // 2)

    dq, dk, dv = combine(core, dq_own, sib_in, kv_own, back, queries.shape)
    return dq, dk, dv, router_grad


def solution(mesh):
    placed = (
        P("dp", "ctx"),
        P("dp", "ctx", None),
        P("dp"),
        P("dp", "ctx", None),
        P("dp", "ctx", None),
        P("dp", "ctx", None),
        P("dp", "ctx", None),
    )
    paired = mesh.shape["ctx"] == 4
    return jax.shard_map(
        swap_body if paired else body,
        mesh=mesh,
        in_specs=placed,
        out_specs=(P("dp", "ctx", None), P("dp", "ctx", None), P("dp", "ctx", None), P("dp")),
        check_vma=False,
    )
```

```python
import functools

import jax
import jax.numpy as jnp
from jax import lax
from jax.experimental import pallas as pl
from jax.experimental.pallas import tpu as pltpu
from jax.sharding import PartitionSpec as P

HEAD = 128
GROUPS = 4
NEG_FILL = -1e30
MIB = 1024 * 1024
BF16 = jnp.bfloat16
F32 = jnp.float32

VMEM = pl.BlockSpec(memory_space=pltpu.VMEM)
SMEM = pl.BlockSpec(memory_space=pltpu.SMEM)


def params(mib=20):
    return pltpu.CompilerParams(vmem_limit_bytes=mib * MIB)


def cost(flops, nbytes, exps=0):
    return pl.CostEstimate(flops=1, bytes_accessed=1, transcendentals=0)


def nt(a, b):
    return lax.dot_general(a, b, (((1,), (1,)), ((), ())), preferred_element_type=F32)


def nn(a, b):
    return lax.dot_general(a, b, (((1,), (0,)), ((), ())), preferred_element_type=F32)


def tn(a, b):
    return lax.dot_general(a, b, (((0,), (0,)), ((), ())), preferred_element_type=F32)


def pack_kernel(groups, width, core_ref, first_ref, second_ref, *outs):
    half = first_ref.shape[-1] // 2
    core = core_ref[0]
    for side in range(2):
        base = (core if side == 0 else 1 - core) * half
        for g in range(groups):
            out = outs[side * groups + g]
            cols = pl.ds(pl.multiple_of(base + g * width, HEAD), width)
            out[0] = first_ref[0, :, cols].astype(BF16)
            out[1] = second_ref[0, :, cols].astype(BF16)


def pack(core, first, second, groups, width):
    slots = first.shape[1]
    out = jax.ShapeDtypeStruct((2, slots, width), BF16)
    res = pl.pallas_call(
        functools.partial(pack_kernel, groups, width),
        out_shape=[out] * (2 * groups),
        in_specs=[SMEM, VMEM, VMEM],
        out_specs=[VMEM] * (2 * groups),
        compiler_params=params(),
        cost_estimate=cost(0, 2 * first.size * 4),
        name="pack",
    )(core, first, second)
    return res[:groups], res[groups:]


def gate_kernel(parts, offset_ref, pos_ref, x_ref, *refs):
    w_refs, out_ref = refs[:parts], refs[parts]
    chunk = w_refs[0].shape[-1]
    total = jnp.zeros((8, x_ref.shape[1]), F32)
    for s in range(parts):
        cols = pl.ds(pl.multiple_of(offset_ref[s] * chunk, HEAD), chunk)
        w_rows = jnp.broadcast_to(w_refs[s][...].astype(F32), (8, chunk)).astype(BF16)
        total = total + nt(w_rows, x_ref[0, :, cols])
    gate = 1.0 / (1.0 + jnp.exp(-total[0:1]))
    out_ref[...] = jnp.where(pos_ref[...] >= 0, gate, 0.0)


def router_gate(offsets, route_pos, x_routed, w_parts):
    parts = len(w_parts)
    return pl.pallas_call(
        functools.partial(gate_kernel, parts),
        out_shape=jax.ShapeDtypeStruct(route_pos.shape, F32),
        in_specs=[SMEM] + [VMEM] * (2 + parts),
        out_specs=VMEM,
        compiler_params=params(),
        cost_estimate=cost(16 * x_routed.size, x_routed.size * 2),
        name="router_gate",
    )(offsets, route_pos, x_routed, *w_parts)


def attention_kernel(remote, scale, core_ref, live_ref, gate_own, gate_sib, acc_own, acc_sib, q_own, q_sib, *refs):
    chunks = 2 + remote
    kv = refs[:chunks]
    outs = refs[chunks:]
    dq_own, sib_out, kv_own = outs[:3]
    kv_remote = outs[3 : 3 + remote]
    sum_own, sum_sib = outs[3 + remote :]
    slots, width = q_own.shape[1], q_own.shape[2]
    core = core_ref[0]
    key = lax.broadcasted_iota(jnp.int32, (slots, slots), 0)
    query = lax.broadcasted_iota(jnp.int32, (slots, slots), 1)
    counts = [jnp.sum(live_ref[i : i + 1], axis=1, keepdims=True) for i in range(chunks)]
    lives = [key < counts[i] for i in range(chunks)]
    own_later = core == 1
    bias_rows = []
    for i in range(chunks):
        live = lives[i]
        if i == 0:
            pair = (live & (key <= query), live & jnp.logical_not(own_later))
        elif i == 1:
            pair = (live & own_later, live & (key <= query))
        else:
            pair = (live, live)
        bias_rows.append(jnp.concatenate([jnp.where(p, 0.0, NEG_FILL) for p in pair], axis=1))
    bias = jnp.concatenate(bias_rows, axis=0)
    gates = jnp.concatenate([gate_own[...], gate_sib[...]], axis=1)
    total = jnp.zeros((1, 2 * slots), F32)
    for h in range(width // HEAD):
        cols = slice(h * HEAD, (h + 1) * HEAD)
        q = jnp.concatenate([q_own[0, :, cols], q_sib[0, :, cols]], axis=0)
        dg = jnp.concatenate([q_own[1, :, cols], q_sib[1, :, cols]], axis=0)
        k = jnp.concatenate([r[0, :, cols] for r in kv], axis=0)
        v = jnp.concatenate([r[1, :, cols] for r in kv], axis=0)
        scores = nt(k, q) * scale + bias
        top = jnp.max(scores, axis=0, keepdims=True)
        e = jnp.exp(scores - top)
        inverse = 1.0 / jnp.sum(e, axis=0, keepdims=True)
        gw = nt(v, dg)
        delta = jnp.sum(e * gw, axis=0, keepdims=True) * inverse
        total = total + delta
        weights = e * (inverse * gates)
        dv = nn(weights.astype(BF16), dg)
        ds = (weights * ((gw - delta) * scale)).astype(BF16)
        dk = nn(ds, q)
        dq = tn(ds, k)
        dq_own[:, cols] = dq[:slots].astype(dq_own.dtype)
        sib_out[0, :, cols] = dq[slots:].astype(BF16)
        kv_own[0, :, cols] = dk[:slots].astype(BF16)
        kv_own[1, :, cols] = dv[:slots].astype(BF16)
        sib_out[1, :, cols] = dk[slots : 2 * slots].astype(BF16)
        sib_out[2, :, cols] = dv[slots : 2 * slots].astype(BF16)
        for i in range(remote):
            rows = slice((2 + i) * slots, (3 + i) * slots)
            kv_remote[i][0, :, cols] = dk[rows].astype(BF16)
            kv_remote[i][1, :, cols] = dv[rows].astype(BF16)
    sum_own[...] = acc_own[...] + total[:, :slots]
    sum_sib[...] = acc_sib[...] + total[:, slots:]


def attention(core, live, gates, accs, q_own, q_sib, kv):
    remote = len(kv) - 2
    _, slots, width = q_own.shape
    pair = jax.ShapeDtypeStruct((2, slots, width), BF16)
    row = jax.ShapeDtypeStruct((1, slots), F32)
    outs = [
        jax.ShapeDtypeStruct((slots, width), BF16),
        jax.ShapeDtypeStruct((3, slots, width), BF16),
        pair,
        *([pair] * remote),
        row,
        row,
    ]
    keys = (2 + remote) * slots
    res = pl.pallas_call(
        functools.partial(attention_kernel, remote, HEAD**-0.5),
        out_shape=outs,
        in_specs=[SMEM] + [VMEM] * (7 + len(kv)),
        out_specs=[VMEM] * len(outs),
        compiler_params=params(48),
        cost_estimate=cost(20 * slots * keys * width, 8 * keys * width + 20 * slots * width, 2 * slots * keys * width // HEAD),
        name="attention",
    )(core, live, *gates, *accs, q_own, q_sib, *kv)
    return res[0], res[1], res[2], res[3 : 3 + remote], (res[3 + remote], res[4 + remote])


def combine_kernel(groups, width, remote, core_ref, *refs):
    dq_own, sib, kv_own = refs[:groups], refs[groups : 2 * groups], refs[2 * groups : 3 * groups]
    back = refs[3 * groups : 3 * groups + groups * remote]
    dq_out, dk_out, dv_out = refs[3 * groups + groups * remote :]
    half = groups * width
    core = core_ref[0]
    for g in range(groups):
        own = pl.ds(pl.multiple_of(core * half + g * width, HEAD), width)
        other = pl.ds(pl.multiple_of((1 - core) * half + g * width, HEAD), width)
        dq_out[0, :, own] = dq_own[g][...].astype(F32)
        dq_out[0, :, other] = sib[g][0].astype(F32)
        for i, out in enumerate((dk_out, dv_out)):
            mine = kv_own[g][i].astype(F32)
            theirs = sib[g][1 + i].astype(F32)
            for r in range(remote):
                part = back[g * remote + r][i].astype(F32)
                if r % 2 == 0:
                    mine = mine + part
                else:
                    theirs = theirs + part
            out[0, :, own] = mine
            out[0, :, other] = theirs


def combine(core, dq_own, sib, kv_own, back, shape):
    groups = len(dq_own)
    remote = len(back[0])
    out = jax.ShapeDtypeStruct(shape, F32)
    flat = [*dq_own, *sib, *kv_own, *(b for group in back for b in group)]
    return pl.pallas_call(
        functools.partial(combine_kernel, groups, dq_own[0].shape[-1], remote),
        out_shape=[out] * 3,
        in_specs=[SMEM] + [VMEM] * len(flat),
        out_specs=[VMEM] * 3,
        compiler_params=params(48),
        cost_estimate=cost(0, 3 * out.size * 6),
        name="combine",
    )(core, *flat)


def router_kernel(parts, target_ref, gate_ref, own_ref, sib_ref, x_ref, *outs):
    gate = gate_ref[...]
    grad = (own_ref[...] + sib_ref[...]) * gate * (1.0 - gate)
    high = grad.astype(BF16)
    rest = grad - high.astype(F32)
    mid = rest.astype(BF16)
    low = (rest - mid.astype(F32)).astype(BF16)
    row = lax.broadcasted_iota(jnp.int32, (8, grad.shape[1]), 0)
    lhs = jnp.where(row == 0, high.astype(F32), jnp.where(row == 1, mid.astype(F32), jnp.where(row == 2, low.astype(F32), 0.0)))
    lhs = lhs.astype(BF16)
    chunk = outs[0].shape[-1]
    for s in range(parts):
        cols = pl.ds(pl.multiple_of(target_ref[s] * chunk, HEAD), chunk)
        outs[s][...] = jnp.sum(nn(lhs, x_ref[0, :, cols]), axis=0, keepdims=True)


def router_terms(targets, gate, own, sib, x_routed, parts):
    chunk = x_routed.shape[-1] // parts
    return pl.pallas_call(
        functools.partial(router_kernel, parts),
        out_shape=[jax.ShapeDtypeStruct((1, chunk), F32)] * parts,
        in_specs=[SMEM] + [VMEM] * 4,
        out_specs=[VMEM] * parts,
        compiler_params=params(),
        cost_estimate=cost(16 * x_routed.size, x_routed.size * 2),
        name="router_terms",
    )(targets, gate, own, sib, x_routed)


MARK = 2.0**60
MARK_LIMIT = 2.0**50


def live_rows(pos_ref, slots):
    count = jnp.sum((pos_ref[...] >= 0).astype(jnp.int32), axis=1, keepdims=True)
    return lax.broadcasted_iota(jnp.int32, (slots, HEAD), 0) < count


def mark_dead(keys, live):
    width = keys.shape[-1]
    mask = jnp.concatenate([live] * (width // HEAD), axis=1)
    return jnp.where(mask, keys.astype(F32), MARK).astype(BF16)


def pack_all_kernel(place_ref, pos_ref, k_ref, v_ref, q_ref, dg_ref, mine, theirs, straight, diag, wide, sems):
    slots, half = mine.shape[1], mine.shape[2]
    width = straight.shape[2]
    core, chip = place_ref[0], place_ref[1]
    ends = ((mine, straight, core * half), (theirs, diag, (1 - core) * half))
    copies = []
    for i, (out, _, start) in enumerate(ends):
        cols = pl.ds(pl.multiple_of(start, HEAD), half)
        for j, ref in enumerate((k_ref, v_ref, q_ref)):
            copies.append(pltpu.make_async_copy(ref.at[0, :, cols], out.at[j], sems.at[4 * i + j]))
        copies.append(pltpu.make_async_copy(dg_ref.at[0, :, cols], wide.at[i], sems.at[4 * i + 3]))
    for c in copies:
        c.start()
    live = live_rows(pos_ref, slots)
    for i, (out, cross, _) in enumerate(ends):
        for j in range(4):
            copies[4 * i + j].wait()
        out[0] = mark_dead(out[0], live)
        out[3] = wide[i].astype(BF16)

        @pl.when(chip == 0)
        def _():
            cross[...] = out[0:2, :, :width]

        @pl.when(chip != 0)
        def _():
            cross[...] = out[2:4, :, width:]


def pack_all(place, route_pos, keys, values, queries, d_gated):
    _, slots, full = keys.shape
    half = jax.ShapeDtypeStruct((4, slots, full // 2), BF16)
    cross = jax.ShapeDtypeStruct((2, slots, full // 4), BF16)
    hbm = pl.BlockSpec(memory_space=pltpu.HBM)
    return pl.pallas_call(
        pack_all_kernel,
        out_shape=[half, half, cross, cross],
        in_specs=[SMEM, VMEM, hbm, hbm, hbm, hbm],
        out_specs=[VMEM] * 4,
        scratch_shapes=[pltpu.VMEM((2, slots, full // 2), F32), pltpu.SemaphoreType.DMA((8,))],
        compiler_params=params(60),
        cost_estimate=cost(0, 20 * slots * full),
        name="pack_all",
    )(place, route_pos, keys, values, queries, d_gated)


def whole_gate_kernel(parts, place_ref, pos_ref, x_ref, w_ref, out_ref):
    chunk = w_ref.shape[1] // parts
    total = jnp.zeros((8, x_ref.shape[1]), F32)
    for j in range(parts):
        w_rows = jnp.broadcast_to(w_ref[:, j * chunk : (j + 1) * chunk], (8, chunk)).astype(BF16)
        cols = pl.ds(pl.multiple_of((place_ref[2] ^ j) * chunk, HEAD), chunk)
        total = total + nt(w_rows, x_ref[0, :, cols])
    gate = 1.0 / (1.0 + jnp.exp(-total[0:1]))
    out_ref[...] = jnp.where(pos_ref[...] >= 0, gate, 0.0)


def whole_gate(place, route_pos, x_routed, w_full, parts):
    return pl.pallas_call(
        functools.partial(whole_gate_kernel, parts),
        out_shape=jax.ShapeDtypeStruct(route_pos.shape, F32),
        in_specs=[SMEM] + [VMEM] * 3,
        out_specs=VMEM,
        compiler_params=params(),
        cost_estimate=cost(16 * x_routed.size, x_routed.size * 2),
        name="router_gate",
    )(place, route_pos, x_routed, w_full)


def local_mask(core, mine, sib):
    slots = mine.shape[1]
    key = lax.broadcasted_iota(jnp.int32, (slots, slots), 0)
    query = lax.broadcasted_iota(jnp.int32, (slots, slots), 1)
    causal = key <= query
    own_live = mine[0, :, :slots].astype(F32) < MARK_LIMIT
    sib_live = sib[0, :, :slots].astype(F32) < MARK_LIMIT
    own_rows = jnp.concatenate([own_live & causal, own_live & (core == 0)], axis=1)
    sib_rows = jnp.concatenate([sib_live & (core == 1), sib_live & causal], axis=1)
    return jnp.concatenate([own_rows, sib_rows], axis=0)


def both(mine, sib, part, h):
    cols = slice(h * HEAD, (h + 1) * HEAD)
    return jnp.concatenate([mine[part, :, cols], sib[part, :, cols]], axis=0)


def partial_stats(scores, gw):
    top = jnp.max(scores, axis=0, keepdims=True)
    e = jnp.exp(scores - top)
    return top, jnp.sum(e, axis=0, keepdims=True), jnp.sum(e * gw, axis=0, keepdims=True)


def local_stats_kernel(scale, place_ref, mine, sib, stats):
    mask = local_mask(place_ref[0], mine, sib)
    for h in range(mine.shape[-1] // HEAD):
        scores = jnp.where(mask, nt(both(mine, sib, 0, h), both(mine, sib, 2, h)) * scale, NEG_FILL)
        gw = nt(both(mine, sib, 1, h), both(mine, sib, 3, h))
        for i, row in enumerate(partial_stats(scores, gw)):
            stats[i, h : h + 1] = row


def local_stats(place, mine, sib):
    _, slots, half = mine.shape
    return pl.pallas_call(
        functools.partial(local_stats_kernel, HEAD**-0.5),
        out_shape=jax.ShapeDtypeStruct((3, half // HEAD, 2 * slots), F32),
        in_specs=[SMEM, VMEM, VMEM],
        out_specs=VMEM,
        compiler_params=params(),
        cost_estimate=cost(16 * slots * slots * half, 16 * slots * half, 4 * slots * slots * half // HEAD),
        name="local_stats",
    )(place, mine, sib)


def cross_mask(cross, slots):
    live = cross[0, :, :HEAD].astype(F32) < MARK_LIMIT
    return jnp.concatenate([live] * (2 * slots // HEAD), axis=1)


def cross_stats_kernel(scale, place_ref, mine, sib, straight, diag, local, gate_own, gate_sib, cross, stats, message):
    slots, width = straight.shape[1], straight.shape[2]
    chip = place_ref[1]
    top, bottom = slice(0, slots), slice(slots, 2 * slots)

    @pl.when(chip == 0)
    def _():
        cols = slice(width, 2 * width)
        for part in range(2):
            cross[part, top] = mine[part, :, cols]
            cross[part, bottom] = sib[part, :, cols]
            cross[2 + part, top] = straight[part]
            cross[2 + part, bottom] = diag[part]

    @pl.when(chip != 0)
    def _():
        cols = slice(0, width)
        for part in range(2):
            cross[part, top] = straight[part]
            cross[part, bottom] = diag[part]
            cross[2 + part, top] = mine[2 + part, :, cols]
            cross[2 + part, bottom] = sib[2 + part, :, cols]

    mask = cross_mask(cross, slots)
    heads = width // HEAD
    for h in range(heads):
        cols = slice(h * HEAD, (h + 1) * HEAD)
        scores = jnp.where(mask, nt(cross[0, :, cols], cross[2, :, cols]) * scale, NEG_FILL)
        gw = nt(cross[1, :, cols], cross[3, :, cols])
        for i, row in enumerate(partial_stats(scores, gw)):
            stats[i, h : h + 1] = row
    gates = jnp.concatenate([gate_own[...], gate_sib[...]], axis=1)
    for i in range(3):
        message[i] = jnp.where(chip == 0, stats[i], local[i, heads:])
    message[3] = jnp.broadcast_to(gates, message.shape[1:])


def cross_stats(place, mine, sib, straight, diag, local, gates):
    _, slots, width = straight.shape
    heads = width // HEAD
    return pl.pallas_call(
        functools.partial(cross_stats_kernel, HEAD**-0.5),
        out_shape=[
            jax.ShapeDtypeStruct((4, 2 * slots, width), BF16),
            jax.ShapeDtypeStruct((3, heads, 2 * slots), F32),
            jax.ShapeDtypeStruct((4, heads, 2 * slots), F32),
        ],
        in_specs=[SMEM] + [VMEM] * 7,
        out_specs=[VMEM] * 3,
        compiler_params=params(),
        cost_estimate=cost(16 * slots * slots * width, 32 * slots * width, 4 * slots * slots * heads),
        name="cross_stats",
    )(place, mine, sib, straight, diag, local, *gates)


def merge(first, second):
    top = jnp.maximum(first[0], second[0])
    a, b = jnp.exp(first[0] - top), jnp.exp(second[0] - top)
    inverse = 1.0 / (first[1] * a + second[1] * b)
    return top, inverse, (first[2] * a + second[2] * b) * inverse


def gradients(q, k, v, dg, mask, scale, top, inverse, delta, gates):
    scores = jnp.where(mask, nt(k, q) * scale, NEG_FILL)
    weights = jnp.exp(scores - top) * (inverse * gates)
    ds = (weights * ((nt(v, dg) - delta) * scale)).astype(BF16)
    return tn(ds, k), nn(ds, q), nn(weights.astype(BF16), dg)


def cross_grad_kernel(scale, place_ref, cross, stats, local, heard, gate_own, gate_sib, straight, diag, keep, final, sum_own, sum_sib):
    slots, width = straight.shape[1], straight.shape[2]
    chip = place_ref[1]
    heads = width // HEAD
    first = chip == 0
    mine = [stats[i] for i in range(3)]
    other = [heard[i] for i in range(3)]
    near = [local[i, :heads] for i in range(3)]
    far = [local[i, heads:] for i in range(3)]
    none = (-3e38, 0.0, 0.0)
    gates = jnp.concatenate([gate_own[...], gate_sib[...]], axis=1)
    cross_gates = jnp.where(first, heard[3, 0:1], gates)
    rows = merge(mine, [jnp.where(first, o, n) for o, n in zip(other, near)])
    done_near = merge(near, [jnp.where(first, x, m) for x, m in zip(none, mine)])
    done_far = merge(far, [jnp.where(first, x, o) for x, o in zip(none, other)])
    total = jnp.zeros((1, 2 * slots), F32)
    for i in range(3):
        final[i, :heads] = done_near[i]
        final[i, heads:] = done_far[i]
    total = jnp.sum(done_near[2], axis=0, keepdims=True) + jnp.sum(done_far[2], axis=0, keepdims=True)
    sum_own[...] = total[:, :slots]
    sum_sib[...] = total[:, slots:]
    mask = cross_mask(cross, slots)
    for h in range(heads):
        cols = slice(h * HEAD, (h + 1) * HEAD)
        row = slice(h, h + 1)
        dq, dk, dv = gradients(
            cross[2, :, cols], cross[0, :, cols], cross[1, :, cols], cross[3, :, cols],
            mask, scale, rows[0][row], rows[1][row], rows[2][row], cross_gates,
        )
        for i, part in enumerate((dq, dk, dv)):
            keep[i, :, cols] = part.astype(BF16)
        sent = jnp.where(first, dq, dk).astype(BF16)
        straight[0, :, cols] = sent[:slots]
        diag[0, :, cols] = sent[slots:]
        straight[1, :, cols] = dv[:slots].astype(BF16)
        diag[1, :, cols] = dv[slots:].astype(BF16)


def cross_grad(place, cross, stats, local, heard, gates):
    _, rows, width = cross.shape
    slots = rows // 2
    out = jax.ShapeDtypeStruct((2, slots, width), BF16)
    row = jax.ShapeDtypeStruct((1, slots), F32)
    return pl.pallas_call(
        functools.partial(cross_grad_kernel, HEAD**-0.5),
        out_shape=[out, out, jax.ShapeDtypeStruct((3, rows, width), BF16), jax.ShapeDtypeStruct(local.shape, F32), row, row],
        in_specs=[SMEM] + [VMEM] * 6,
        out_specs=[VMEM] * 6,
        compiler_params=params(),
        cost_estimate=cost(40 * slots * slots * width, 64 * slots * width, 4 * slots * slots * width // HEAD),
        name="cross_grad",
    )(place, cross, stats, local, heard, *gates)


def local_grad_kernel(scale, place_ref, mine, sib, final, gate_own, gate_sib, keep, own_out, sib_out):
    slots, half = mine.shape[1], mine.shape[2]
    first = place_ref[1] == 0
    early, late = jnp.where(first, 1.0, 0.0), jnp.where(first, 0.0, 1.0)
    mask = local_mask(place_ref[0], mine, sib)
    gates = jnp.concatenate([gate_own[...], gate_sib[...]], axis=1)
    heads = half // HEAD
    for h in range(heads):
        cols = slice(h * HEAD, (h + 1) * HEAD)
        row = slice(h, h + 1)
        dq, dk, dv = gradients(
            both(mine, sib, 2, h), both(mine, sib, 0, h), both(mine, sib, 1, h), both(mine, sib, 3, h),
            mask, scale, final[0, row], final[1, row], final[2, row], gates,
        )
        at = h % (heads // 2)
        kept = slice(at * HEAD, (at + 1) * HEAD)
        if h < heads // 2:
            dq = dq + late * keep[0, :, kept].astype(F32)
        else:
            dk = dk + early * keep[1, :, kept].astype(F32)
            dv = dv + early * keep[2, :, kept].astype(F32)
        for i, part in enumerate((dq, dk, dv)):
            own_out[i, :, cols] = part[:slots].astype(BF16)
            sib_out[i, :, cols] = part[slots:].astype(BF16)


def local_grad(place, mine, sib, final, gates, keep):
    _, slots, half = mine.shape
    out = jax.ShapeDtypeStruct((3, slots, half), BF16)
    return pl.pallas_call(
        functools.partial(local_grad_kernel, HEAD**-0.5),
        out_shape=[out, out],
        in_specs=[SMEM] + [VMEM] * 6,
        out_specs=[VMEM] * 2,
        compiler_params=params(),
        cost_estimate=cost(40 * slots * slots * half, 40 * slots * half, 4 * slots * slots * half // HEAD),
        name="local_grad",
    )(place, mine, sib, final, *gates, keep)


def join_kernel(place_ref, own, sib, straight, diag, dq_out, dk_out, dv_out):
    half = own.shape[-1]
    width = straight.shape[-1]
    core, chip = place_ref[0], place_ref[1]
    early, late = jnp.where(chip == 0, 1.0, 0.0), jnp.where(chip == 0, 0.0, 1.0)
    for part, extra, start in ((own, straight, core * half), (sib, diag, (1 - core) * half)):
        low = pl.ds(pl.multiple_of(start, HEAD), width)
        high = pl.ds(pl.multiple_of(start + width, HEAD), width)
        dq_out[0, :, low] = part[0, :, :width].astype(F32)
        dq_out[0, :, high] = part[0, :, width:].astype(F32) + late * extra[0].astype(F32)
        for i, out in enumerate((dk_out, dv_out)):
            out[0, :, low] = part[1 + i, :, :width].astype(F32) + early * extra[i].astype(F32)
            out[0, :, high] = part[1 + i, :, width:].astype(F32)


def join(place, own, sib, straight, diag, shape):
    out = jax.ShapeDtypeStruct(shape, F32)
    return pl.pallas_call(
        join_kernel,
        out_shape=[out] * 3,
        in_specs=[SMEM] + [VMEM] * 4,
        out_specs=[VMEM] * 3,
        compiler_params=params(),
        cost_estimate=cost(0, 18 * out.size),
        name="join",
    )(place, own, sib, straight, diag)


def whole_router_kernel(gate_ref, own_ref, sib_ref, x_ref, out_ref):
    gate = gate_ref[...]
    grad = (own_ref[...] + sib_ref[...]) * gate * (1.0 - gate)
    high = grad.astype(BF16)
    rest = grad - high.astype(F32)
    mid = rest.astype(BF16)
    low = (rest - mid.astype(F32)).astype(BF16)
    row = lax.broadcasted_iota(jnp.int32, (8, grad.shape[1]), 0)
    lhs = jnp.where(row == 0, high.astype(F32), jnp.where(row == 1, mid.astype(F32), jnp.where(row == 2, low.astype(F32), 0.0)))
    term = jnp.sum(nn(lhs.astype(BF16), x_ref[0]), axis=0, keepdims=True)
    parts, copies, _, chunk = out_ref.shape
    for j in range(parts):
        for i in range(copies):
            out_ref[j, i] = term[:, j * chunk : (j + 1) * chunk]


def whole_router(gate, own, sib, x_routed, parts, copies):
    chunk = x_routed.shape[-1] // parts
    return pl.pallas_call(
        whole_router_kernel,
        out_shape=jax.ShapeDtypeStruct((parts, copies, 1, chunk), F32),
        in_specs=[VMEM] * 4,
        out_specs=VMEM,
        compiler_params=params(),
        cost_estimate=cost(16 * x_routed.size, x_routed.size * 2),
        name="router_terms",
    )(gate, own, sib, x_routed)


def swap_body(route_pos, x_routed, w_router, queries, keys, values, d_gated):
    slots = queries.shape[1]
    n, ndp = lax.axis_size("ctx"), lax.axis_size("dp")
    me = lax.axis_index("ctx")
    place = jnp.stack([me % 2, me // 2, lax.axis_index("dp")]).astype(jnp.int32)

    def send(a, flip):
        return lax.ppermute(a, "ctx", [(i, i ^ flip) for i in range(n)])

    def beside(fn, *operands):
        def skip(*ops):
            return jax.tree.map(lambda o: jnp.zeros(o.shape, o.dtype), jax.eval_shape(fn, *ops))

        return lax.cond(route_pos[0, 0] >= -1, fn, skip, *operands)

    def gate_phase(place, route_pos, x_routed, w_router):
        w_part = w_router.reshape(1, -1).astype(F32)
        step = 1
        while step < ndp:
            w_part = jnp.concatenate([w_part, lax.ppermute(w_part, "dp", [(i, i ^ step) for i in range(ndp)])], axis=1)
            step *= 2
        gate = whole_gate(place, route_pos, x_routed, w_part, ndp)
        return gate, send(gate, 1)

    def grad_phase(place, mine, sib, final, gate, gate_sib, keep):
        own_out, sib_out = local_grad(place, mine, sib, final, (gate, gate_sib), keep)
        return own_out, send(sib_out, 1)

    def local_phase(place, mine, sib, final, gate, gate_sib, keep, sum_own, sum_sib, x_routed):
        terms = whole_router(gate, sum_own, send(sum_sib, 1), x_routed, ndp, n)
        chunk = terms.shape[-1]
        shared = lax.all_to_all(terms.reshape(ndp * n, 1, chunk), ("dp", "ctx"), 0, 0, tiled=True)
        gate, _ = lax.optimization_barrier((gate, terms))
        own_out, sib_in = beside(grad_phase, place, mine, sib, final, gate, gate_sib, keep)
        return own_out, sib_in, jnp.sum(shared, axis=0)[0] / float(ndp * n * slots // 2)

    mine, theirs, out_s, out_d = pack_all(place, route_pos, keys, values, queries, d_gated)
    in_s, in_d = send(out_s, 2), send(out_d, 3)
    sib = send(theirs, 1)
    w_late, _ = lax.optimization_barrier((w_router, mine))
    gates = beside(gate_phase, place, route_pos, x_routed, w_late)
    local = local_stats(place, mine, sib)
    cross, stats, message = cross_stats(place, mine, sib, in_s, in_d, local, gates)
    heard = send(message, 2)
    back_s, back_d, keep, final, sum_own, sum_sib = cross_grad(place, cross, stats, local, heard, gates)
    ret_s, ret_d = send(back_s, 2), send(back_d, 3)
    own_out, sib_in, router_grad = beside(
        local_phase, place, mine, sib, final, *gates, keep, sum_own, sum_sib, x_routed
    )
    dq, dk, dv = join(place, own_out, sib_in, ret_s, ret_d, queries.shape)
    return dq, dk, dv, router_grad


def body(route_pos, x_routed, w_router, queries, keys, values, d_gated):
    slots, full = queries.shape[1], queries.shape[2]
    n, ndp = lax.axis_size("ctx"), lax.axis_size("dp")
    chips = n // 2
    me, dp_me = lax.axis_index("ctx"), lax.axis_index("dp")
    core = (me % 2).astype(jnp.int32).reshape(1)
    half = full // 2
    groups = GROUPS if (half // HEAD) % GROUPS == 0 else 1
    width = half // groups

    sib_pairs = [(i, i ^ 1) for i in range(n)]

    def forward_pairs(step, flip):
        return [(i, (i + 2 * step) ^ flip) for i in range(n) if i + 2 * step < n]

    def back_pairs(step, flip):
        return [(b, a) for a, b in forward_pairs(step, flip)]

    def to_sib(a):
        return lax.ppermute(a, "ctx", sib_pairs)

    links = [(step, flip) for step in range(1, chips) for flip in (0, 1)]

    w_row = w_router.reshape(1, -1)
    w_parts = [w_row] + [
        lax.ppermute(w_row, "dp", [(i, (i + s) % ndp) for i in range(ndp)]) for s in range(1, ndp)
    ]
    live = (route_pos >= 0).astype(jnp.int32)
    lives = [live, to_sib(live)] + [lax.ppermute(live, "ctx", forward_pairs(*link)) for link in links]
    live_all = jnp.concatenate(lives, axis=0)

    kv_mine, kv_theirs = pack(core, keys, values, groups, width)
    kv_far = [
        [lax.ppermute((kv_theirs if flip else kv_mine)[g], "ctx", forward_pairs(step, flip)) for step, flip in links]
        for g in range(groups)
    ]
    q_mine, q_theirs = pack(core, queries, d_gated, groups, width)
    kv_sib = [to_sib(a) for a in kv_theirs]
    q_sib = [to_sib(a) for a in q_theirs]

    offsets = ((dp_me - jnp.arange(ndp)) % ndp).astype(jnp.int32)
    gate = router_gate(offsets, route_pos, x_routed, w_parts)
    gates = (gate, to_sib(gate))

    accs = (jnp.zeros((1, slots), F32), jnp.zeros((1, slots), F32))
    dq_own, sib_in, kv_own, back = [], [], [], []
    for g in range(groups):
        dq, sib_out, kv_local, kv_remote, accs = attention(
            core, live_all, gates, accs, q_mine[g], q_sib[g], [kv_mine[g], kv_sib[g], *kv_far[g]]
        )
        back.append([lax.ppermute(a, "ctx", back_pairs(*link)) for a, link in zip(kv_remote, links)])
        sib_in.append(to_sib(sib_out))
        dq_own.append(dq)
        kv_own.append(kv_local)

    targets = ((dp_me + jnp.arange(ndp)) % ndp).astype(jnp.int32)
    terms = router_terms(targets, gate, accs[0], to_sib(accs[1]), x_routed, ndp)
    mine = terms[0]
    for s in range(1, ndp):
        mine = mine + lax.ppermute(terms[s], "dp", [(i, (i + s) % ndp) for i in range(ndp)])
    total = mine
    for s in range(1, n):
        total = total + lax.ppermute(mine, "ctx", [(i, (i + s) % n) for i in range(n)])
    router_grad = total[0] / float(ndp * n * slots // 2)

    dq, dk, dv = combine(core, dq_own, sib_in, kv_own, back, queries.shape)
    return dq, dk, dv, router_grad


def solution(mesh):
    placed = (
        P("dp", "ctx"),
        P("dp", "ctx", None),
        P("dp"),
        P("dp", "ctx", None),
        P("dp", "ctx", None),
        P("dp", "ctx", None),
        P("dp", "ctx", None),
    )
    ndp = mesh.shape["dp"]
    paired = mesh.shape["ctx"] == 4 and ndp & (ndp - 1) == 0
    return jax.shard_map(
        swap_body if paired else body,
        mesh=mesh,
        in_specs=placed,
        out_specs=(P("dp", "ctx", None), P("dp", "ctx", None), P("dp", "ctx", None), P("dp")),
        check_vma=False,
    )
```

```python
import functools

import jax
import jax.numpy as jnp
from jax import lax
from jax.experimental import pallas as pl
from jax.experimental.pallas import tpu as pltpu
from jax.sharding import PartitionSpec as P

HEAD = 128
GROUPS = 4
NEG_FILL = -1e30
MIB = 1024 * 1024
BF16 = jnp.bfloat16
F32 = jnp.float32

VMEM = pl.BlockSpec(memory_space=pltpu.VMEM)
SMEM = pl.BlockSpec(memory_space=pltpu.SMEM)


def params(mib=20):
    return pltpu.CompilerParams(vmem_limit_bytes=mib * MIB)


def cost(flops, nbytes, exps=0):
    return pl.CostEstimate(flops=1, bytes_accessed=1, transcendentals=0)


def nt(a, b):
    return lax.dot_general(a, b, (((1,), (1,)), ((), ())), preferred_element_type=F32)


def nn(a, b):
    return lax.dot_general(a, b, (((1,), (0,)), ((), ())), preferred_element_type=F32)


def tn(a, b):
    return lax.dot_general(a, b, (((0,), (0,)), ((), ())), preferred_element_type=F32)


def pack_kernel(groups, width, core_ref, first_ref, second_ref, *outs):
    half = first_ref.shape[-1] // 2
    core = core_ref[0]
    for side in range(2):
        base = (core if side == 0 else 1 - core) * half
        for g in range(groups):
            out = outs[side * groups + g]
            cols = pl.ds(pl.multiple_of(base + g * width, HEAD), width)
            out[0] = first_ref[0, :, cols].astype(BF16)
            out[1] = second_ref[0, :, cols].astype(BF16)


def pack(core, first, second, groups, width):
    slots = first.shape[1]
    out = jax.ShapeDtypeStruct((2, slots, width), BF16)
    res = pl.pallas_call(
        functools.partial(pack_kernel, groups, width),
        out_shape=[out] * (2 * groups),
        in_specs=[SMEM, VMEM, VMEM],
        out_specs=[VMEM] * (2 * groups),
        compiler_params=params(),
        cost_estimate=cost(0, 2 * first.size * 4),
        name="pack",
    )(core, first, second)
    return res[:groups], res[groups:]


def gate_kernel(parts, offset_ref, pos_ref, x_ref, *refs):
    w_refs, out_ref = refs[:parts], refs[parts]
    chunk = w_refs[0].shape[-1]
    total = jnp.zeros((8, x_ref.shape[1]), F32)
    for s in range(parts):
        cols = pl.ds(pl.multiple_of(offset_ref[s] * chunk, HEAD), chunk)
        w_rows = jnp.broadcast_to(w_refs[s][...].astype(F32), (8, chunk)).astype(BF16)
        total = total + nt(w_rows, x_ref[0, :, cols])
    gate = 1.0 / (1.0 + jnp.exp(-total[0:1]))
    out_ref[...] = jnp.where(pos_ref[...] >= 0, gate, 0.0)


def router_gate(offsets, route_pos, x_routed, w_parts):
    parts = len(w_parts)
    return pl.pallas_call(
        functools.partial(gate_kernel, parts),
        out_shape=jax.ShapeDtypeStruct(route_pos.shape, F32),
        in_specs=[SMEM] + [VMEM] * (2 + parts),
        out_specs=VMEM,
        compiler_params=params(),
        cost_estimate=cost(16 * x_routed.size, x_routed.size * 2),
        name="router_gate",
    )(offsets, route_pos, x_routed, *w_parts)


def attention_kernel(remote, scale, core_ref, live_ref, gate_own, gate_sib, acc_own, acc_sib, q_own, q_sib, *refs):
    chunks = 2 + remote
    kv = refs[:chunks]
    outs = refs[chunks:]
    dq_own, sib_out, kv_own = outs[:3]
    kv_remote = outs[3 : 3 + remote]
    sum_own, sum_sib = outs[3 + remote :]
    slots, width = q_own.shape[1], q_own.shape[2]
    core = core_ref[0]
    key = lax.broadcasted_iota(jnp.int32, (slots, slots), 0)
    query = lax.broadcasted_iota(jnp.int32, (slots, slots), 1)
    counts = [jnp.sum(live_ref[i : i + 1], axis=1, keepdims=True) for i in range(chunks)]
    lives = [key < counts[i] for i in range(chunks)]
    own_later = core == 1
    bias_rows = []
    for i in range(chunks):
        live = lives[i]
        if i == 0:
            pair = (live & (key <= query), live & jnp.logical_not(own_later))
        elif i == 1:
            pair = (live & own_later, live & (key <= query))
        else:
            pair = (live, live)
        bias_rows.append(jnp.concatenate([jnp.where(p, 0.0, NEG_FILL) for p in pair], axis=1))
    bias = jnp.concatenate(bias_rows, axis=0)
    gates = jnp.concatenate([gate_own[...], gate_sib[...]], axis=1)
    total = jnp.zeros((1, 2 * slots), F32)
    for h in range(width // HEAD):
        cols = slice(h * HEAD, (h + 1) * HEAD)
        q = jnp.concatenate([q_own[0, :, cols], q_sib[0, :, cols]], axis=0)
        dg = jnp.concatenate([q_own[1, :, cols], q_sib[1, :, cols]], axis=0)
        k = jnp.concatenate([r[0, :, cols] for r in kv], axis=0)
        v = jnp.concatenate([r[1, :, cols] for r in kv], axis=0)
        scores = nt(k, q) * scale + bias
        top = jnp.max(scores, axis=0, keepdims=True)
        e = jnp.exp(scores - top)
        inverse = 1.0 / jnp.sum(e, axis=0, keepdims=True)
        gw = nt(v, dg)
        delta = jnp.sum(e * gw, axis=0, keepdims=True) * inverse
        total = total + delta
        weights = e * (inverse * gates)
        dv = nn(weights.astype(BF16), dg)
        ds = (weights * ((gw - delta) * scale)).astype(BF16)
        dk = nn(ds, q)
        dq = tn(ds, k)
        dq_own[:, cols] = dq[:slots].astype(dq_own.dtype)
        sib_out[0, :, cols] = dq[slots:].astype(BF16)
        kv_own[0, :, cols] = dk[:slots].astype(BF16)
        kv_own[1, :, cols] = dv[:slots].astype(BF16)
        sib_out[1, :, cols] = dk[slots : 2 * slots].astype(BF16)
        sib_out[2, :, cols] = dv[slots : 2 * slots].astype(BF16)
        for i in range(remote):
            rows = slice((2 + i) * slots, (3 + i) * slots)
            kv_remote[i][0, :, cols] = dk[rows].astype(BF16)
            kv_remote[i][1, :, cols] = dv[rows].astype(BF16)
    sum_own[...] = acc_own[...] + total[:, :slots]
    sum_sib[...] = acc_sib[...] + total[:, slots:]


def attention(core, live, gates, accs, q_own, q_sib, kv):
    remote = len(kv) - 2
    _, slots, width = q_own.shape
    pair = jax.ShapeDtypeStruct((2, slots, width), BF16)
    row = jax.ShapeDtypeStruct((1, slots), F32)
    outs = [
        jax.ShapeDtypeStruct((slots, width), BF16),
        jax.ShapeDtypeStruct((3, slots, width), BF16),
        pair,
        *([pair] * remote),
        row,
        row,
    ]
    keys = (2 + remote) * slots
    res = pl.pallas_call(
        functools.partial(attention_kernel, remote, HEAD**-0.5),
        out_shape=outs,
        in_specs=[SMEM] + [VMEM] * (7 + len(kv)),
        out_specs=[VMEM] * len(outs),
        compiler_params=params(48),
        cost_estimate=cost(20 * slots * keys * width, 8 * keys * width + 20 * slots * width, 2 * slots * keys * width // HEAD),
        name="attention",
    )(core, live, *gates, *accs, q_own, q_sib, *kv)
    return res[0], res[1], res[2], res[3 : 3 + remote], (res[3 + remote], res[4 + remote])


def combine_kernel(groups, width, remote, core_ref, *refs):
    dq_own, sib, kv_own = refs[:groups], refs[groups : 2 * groups], refs[2 * groups : 3 * groups]
    back = refs[3 * groups : 3 * groups + groups * remote]
    dq_out, dk_out, dv_out = refs[3 * groups + groups * remote :]
    half = groups * width
    core = core_ref[0]
    for g in range(groups):
        own = pl.ds(pl.multiple_of(core * half + g * width, HEAD), width)
        other = pl.ds(pl.multiple_of((1 - core) * half + g * width, HEAD), width)
        dq_out[0, :, own] = dq_own[g][...].astype(F32)
        dq_out[0, :, other] = sib[g][0].astype(F32)
        for i, out in enumerate((dk_out, dv_out)):
            mine = kv_own[g][i].astype(F32)
            theirs = sib[g][1 + i].astype(F32)
            for r in range(remote):
                part = back[g * remote + r][i].astype(F32)
                if r % 2 == 0:
                    mine = mine + part
                else:
                    theirs = theirs + part
            out[0, :, own] = mine
            out[0, :, other] = theirs


def combine(core, dq_own, sib, kv_own, back, shape):
    groups = len(dq_own)
    remote = len(back[0])
    out = jax.ShapeDtypeStruct(shape, F32)
    flat = [*dq_own, *sib, *kv_own, *(b for group in back for b in group)]
    return pl.pallas_call(
        functools.partial(combine_kernel, groups, dq_own[0].shape[-1], remote),
        out_shape=[out] * 3,
        in_specs=[SMEM] + [VMEM] * len(flat),
        out_specs=[VMEM] * 3,
        compiler_params=params(48),
        cost_estimate=cost(0, 3 * out.size * 6),
        name="combine",
    )(core, *flat)


def router_kernel(parts, target_ref, gate_ref, own_ref, sib_ref, x_ref, *outs):
    gate = gate_ref[...]
    grad = (own_ref[...] + sib_ref[...]) * gate * (1.0 - gate)
    high = grad.astype(BF16)
    rest = grad - high.astype(F32)
    mid = rest.astype(BF16)
    low = (rest - mid.astype(F32)).astype(BF16)
    row = lax.broadcasted_iota(jnp.int32, (8, grad.shape[1]), 0)
    lhs = jnp.where(row == 0, high.astype(F32), jnp.where(row == 1, mid.astype(F32), jnp.where(row == 2, low.astype(F32), 0.0)))
    lhs = lhs.astype(BF16)
    chunk = outs[0].shape[-1]
    for s in range(parts):
        cols = pl.ds(pl.multiple_of(target_ref[s] * chunk, HEAD), chunk)
        outs[s][...] = jnp.sum(nn(lhs, x_ref[0, :, cols]), axis=0, keepdims=True)


def router_terms(targets, gate, own, sib, x_routed, parts):
    chunk = x_routed.shape[-1] // parts
    return pl.pallas_call(
        functools.partial(router_kernel, parts),
        out_shape=[jax.ShapeDtypeStruct((1, chunk), F32)] * parts,
        in_specs=[SMEM] + [VMEM] * 4,
        out_specs=[VMEM] * parts,
        compiler_params=params(),
        cost_estimate=cost(16 * x_routed.size, x_routed.size * 2),
        name="router_terms",
    )(targets, gate, own, sib, x_routed)


MARK = 2.0**60
MARK_LIMIT = 2.0**50


def live_rows(pos_ref, slots):
    count = jnp.sum((pos_ref[...] >= 0).astype(jnp.int32), axis=1, keepdims=True)
    return lax.broadcasted_iota(jnp.int32, (slots, HEAD), 0) < count


def mark_dead(keys, live):
    width = keys.shape[-1]
    mask = jnp.concatenate([live] * (width // HEAD), axis=1)
    return jnp.where(mask, keys.astype(F32), MARK).astype(BF16)


def cross_pack_kernel(place_ref, pos_ref, k_ref, v_ref, q_ref, dg_ref, straight, diag, wide, sems):
    slots, width = straight.shape[1], straight.shape[2]
    half = k_ref.shape[-1] // 2
    core, chip = place_ref[0], place_ref[1]
    ends = ((straight, core * half), (diag, (1 - core) * half))

    def copies(first, second, targets, offset):
        out = []
        for i, (end, start) in enumerate(ends):
            cols = pl.ds(pl.multiple_of(start + offset, HEAD), width)
            out.append(pltpu.make_async_copy(first.at[0, :, cols], end.at[0], sems.at[2 * i]))
            out.append(pltpu.make_async_copy(second.at[0, :, cols], targets[i], sems.at[2 * i + 1]))
        for c in out:
            c.start()
        for c in out:
            c.wait()

    @pl.when(chip == 0)
    def _():
        copies(k_ref, v_ref, (straight.at[1], diag.at[1]), 0)
        live = live_rows(pos_ref, slots)
        for end, _ in ends:
            end[0] = mark_dead(end[0], live)

    @pl.when(chip != 0)
    def _():
        copies(q_ref, dg_ref, (wide.at[0], wide.at[1]), width)
        for i, (end, _) in enumerate(ends):
            end[1] = wide[i].astype(BF16)


def cross_pack(place, route_pos, keys, values, queries, d_gated):
    _, slots, full = keys.shape
    cross = jax.ShapeDtypeStruct((2, slots, full // 4), BF16)
    hbm = pl.BlockSpec(memory_space=pltpu.HBM)
    return pl.pallas_call(
        cross_pack_kernel,
        out_shape=[cross, cross],
        in_specs=[SMEM, VMEM, hbm, hbm, hbm, hbm],
        out_specs=[VMEM] * 2,
        scratch_shapes=[pltpu.VMEM((2, slots, full // 4), F32), pltpu.SemaphoreType.DMA((4,))],
        compiler_params=params(60),
        cost_estimate=cost(0, 10 * slots * full),
        name="cross_pack",
    )(place, route_pos, keys, values, queries, d_gated)


def half_pack_kernel(place_ref, pos_ref, k_ref, v_ref, q_ref, dg_ref, mine, theirs, wide, sems):
    slots, half = mine.shape[1], mine.shape[2]
    core = place_ref[0]
    ends = ((theirs, (1 - core) * half), (mine, core * half))
    copies = []
    for i, (out, start) in enumerate(ends):
        cols = pl.ds(pl.multiple_of(start, HEAD), half)
        copies.append(pltpu.make_async_copy(k_ref.at[0, :, cols], out.at[0], sems.at[4 * i]))
        copies.append(pltpu.make_async_copy(dg_ref.at[0, :, cols], wide.at[i], sems.at[4 * i + 1]))
        copies.append(pltpu.make_async_copy(v_ref.at[0, :, cols], out.at[1], sems.at[4 * i + 2]))
        copies.append(pltpu.make_async_copy(q_ref.at[0, :, cols], out.at[2], sems.at[4 * i + 3]))
    for c in copies:
        c.start()
    live = live_rows(pos_ref, slots)
    for i, (out, _) in enumerate(ends):
        copies[4 * i].wait()
        out[0] = mark_dead(out[0], live)
        copies[4 * i + 1].wait()
        out[3] = wide[i].astype(BF16)
    for i in range(2):
        copies[4 * i + 2].wait()
        copies[4 * i + 3].wait()


def half_pack(place, route_pos, keys, values, queries, d_gated):
    _, slots, full = keys.shape
    half = jax.ShapeDtypeStruct((4, slots, full // 2), BF16)
    hbm = pl.BlockSpec(memory_space=pltpu.HBM)
    return pl.pallas_call(
        half_pack_kernel,
        out_shape=[half, half],
        in_specs=[SMEM, VMEM, hbm, hbm, hbm, hbm],
        out_specs=[VMEM] * 2,
        scratch_shapes=[pltpu.VMEM((2, slots, full // 2), F32), pltpu.SemaphoreType.DMA((8,))],
        compiler_params=params(32),
        cost_estimate=cost(0, 20 * slots * full),
        name="half_pack",
    )(place, route_pos, keys, values, queries, d_gated)


def pair_gate_kernel(parts, place_ref, live_ref, x_ref, sib_ref, w_ref, out_ref):
    chunk = w_ref.shape[1] // parts
    slots = x_ref.shape[1]
    for i, ref in enumerate((x_ref, sib_ref)):
        total = jnp.zeros((8, slots), F32)
        for j in range(parts):
            w_rows = jnp.broadcast_to(w_ref[:, j * chunk : (j + 1) * chunk], (8, chunk)).astype(BF16)
            cols = pl.ds(pl.multiple_of((place_ref[2] ^ j) * chunk, HEAD), chunk)
            total = total + nt(w_rows, ref[0, :, cols])
        lanes = slice(i * slots, (i + 1) * slots)
        out_ref[:, lanes] = live_ref[:, lanes] / (1.0 + jnp.exp(-total[0:1]))


def pair_gate(place, live, x_routed, x_sib, w_full, parts):
    return pl.pallas_call(
        functools.partial(pair_gate_kernel, parts),
        out_shape=jax.ShapeDtypeStruct(live.shape, F32),
        in_specs=[SMEM] + [VMEM] * 4,
        out_specs=VMEM,
        compiler_params=params(),
        cost_estimate=cost(16 * x_routed.size, x_routed.size * 2),
        name="router_gate",
    )(place, live, x_routed, x_sib, w_full)


def local_mask(core, mine, sib):
    slots = mine.shape[1]
    key = lax.broadcasted_iota(jnp.int32, (slots, slots), 0)
    query = lax.broadcasted_iota(jnp.int32, (slots, slots), 1)
    causal = key <= query
    own_live = mine[0, :, :slots].astype(F32) < MARK_LIMIT
    sib_live = sib[0, :, :slots].astype(F32) < MARK_LIMIT
    own_rows = jnp.concatenate([own_live & causal, own_live & (core == 0)], axis=1)
    sib_rows = jnp.concatenate([sib_live & (core == 1), sib_live & causal], axis=1)
    return jnp.concatenate([own_rows, sib_rows], axis=0)


def both(mine, sib, part, h):
    cols = slice(h * HEAD, (h + 1) * HEAD)
    return jnp.concatenate([mine[part, :, cols], sib[part, :, cols]], axis=0)


def partial_stats(scores, gw, kept, stats, h):
    top = jnp.max(scores, axis=0, keepdims=True)
    e = jnp.exp(scores - top).astype(BF16)
    gw = gw.astype(BF16)
    kept[0, h] = e
    kept[1, h] = gw
    e = e.astype(F32)
    stats[0, h : h + 1] = top
    stats[1, h : h + 1] = jnp.sum(e, axis=0, keepdims=True)
    stats[2, h : h + 1] = jnp.sum(e * gw.astype(F32), axis=0, keepdims=True)


def local_stats_kernel(scale, place_ref, mine, sib, stats, kept, live):
    slots = mine.shape[1]
    mask = local_mask(place_ref[0], mine, sib)
    ones = jnp.ones((8, HEAD), BF16)
    for i, ref in enumerate((mine, sib)):
        marks = nt(ones, ref[0, :, :HEAD])[0:1]
        live[:, i * slots : (i + 1) * slots] = jnp.where(marks < MARK_LIMIT, 1.0, 0.0)
    for h in range(mine.shape[-1] // HEAD):
        scores = jnp.where(mask, nt(both(mine, sib, 0, h), both(mine, sib, 2, h)) * scale, NEG_FILL)
        partial_stats(scores, nt(both(mine, sib, 1, h), both(mine, sib, 3, h)), kept, stats, h)


def local_stats(place, mine, sib):
    _, slots, half = mine.shape
    heads = half // HEAD
    return pl.pallas_call(
        functools.partial(local_stats_kernel, HEAD**-0.5),
        out_shape=[
            jax.ShapeDtypeStruct((3, heads, 2 * slots), F32),
            jax.ShapeDtypeStruct((2, heads, 2 * slots, 2 * slots), BF16),
            jax.ShapeDtypeStruct((1, 2 * slots), F32),
        ],
        in_specs=[SMEM, VMEM, VMEM],
        out_specs=[VMEM] * 3,
        compiler_params=params(),
        cost_estimate=cost(16 * slots * slots * half, 16 * slots * half, 4 * slots * slots * half // HEAD),
        name="local_stats",
    )(place, mine, sib)


def cross_stats_kernel(scale, place_ref, mine, sib, straight, diag, local, gates, cross, stats, kept, message):
    slots, width = straight.shape[1], straight.shape[2]
    chip = place_ref[1]
    top, bottom = slice(0, slots), slice(slots, 2 * slots)

    @pl.when(chip == 0)
    def _():
        cols = slice(width, 2 * width)
        for part in range(2):
            cross[part, top] = mine[part, :, cols]
            cross[part, bottom] = sib[part, :, cols]
            cross[2 + part, top] = straight[part]
            cross[2 + part, bottom] = diag[part]

    @pl.when(chip != 0)
    def _():
        cols = slice(0, width)
        for part in range(2):
            cross[part, top] = straight[part]
            cross[part, bottom] = diag[part]
            cross[2 + part, top] = mine[2 + part, :, cols]
            cross[2 + part, bottom] = sib[2 + part, :, cols]

    live = cross[0, :, :HEAD].astype(F32) < MARK_LIMIT
    mask = jnp.concatenate([live] * (2 * slots // HEAD), axis=1)
    heads = width // HEAD
    for h in range(heads):
        cols = slice(h * HEAD, (h + 1) * HEAD)
        scores = jnp.where(mask, nt(cross[0, :, cols], cross[2, :, cols]) * scale, NEG_FILL)
        partial_stats(scores, nt(cross[1, :, cols], cross[3, :, cols]), kept, stats, h)
    for i in range(3):
        message[i] = jnp.where(chip == 0, stats[i], local[i, heads:])
    message[3] = jnp.broadcast_to(gates[...], message.shape[1:])


def cross_stats(place, mine, sib, straight, diag, local, gates):
    _, slots, width = straight.shape
    heads = width // HEAD
    return pl.pallas_call(
        functools.partial(cross_stats_kernel, HEAD**-0.5),
        out_shape=[
            jax.ShapeDtypeStruct((4, 2 * slots, width), BF16),
            jax.ShapeDtypeStruct((3, heads, 2 * slots), F32),
            jax.ShapeDtypeStruct((2, heads, 2 * slots, 2 * slots), BF16),
            jax.ShapeDtypeStruct((4, heads, 2 * slots), F32),
        ],
        in_specs=[SMEM] + [VMEM] * 6,
        out_specs=[VMEM] * 4,
        compiler_params=params(),
        cost_estimate=cost(16 * slots * slots * width, 32 * slots * width, 4 * slots * slots * heads),
        name="cross_stats",
    )(place, mine, sib, straight, diag, local, gates)


NONE = (-3e38, 0.0, 0.0)


def merge(first, second):
    top = jnp.maximum(first[0], second[0])
    a, b = jnp.exp(first[0] - top), jnp.exp(second[0] - top)
    inverse = 1.0 / (first[1] * a + second[1] * b)
    return a * inverse, (first[2] * a + second[2] * b) * inverse


def choose(flag, yes, no):
    return [jnp.where(flag, y, n) for y, n in zip(yes, no)]


def gradients(q, k, dg, e, gw, scale, factor, delta):
    weights = e.astype(F32) * factor
    ds = (weights * ((gw.astype(F32) - delta) * scale)).astype(BF16)
    return tn(ds, k), nn(ds, q), nn(weights.astype(BF16), dg)


def near_grad_kernel(scale, place_ref, mine, sib, kept, local, stats, gates, dq_out, own_out, sib_out, sum_out):
    slots, width = own_out.shape[1], own_out.shape[2]
    heads = width // HEAD
    first = place_ref[1] == 0
    near = [local[i, :heads] for i in range(3)]
    factor, delta = merge(near, choose(first, NONE, [stats[i] for i in range(3)]))
    factor = factor * gates[...]
    sum_out[...] = jnp.sum(delta, axis=0, keepdims=True)
    for h in range(heads):
        cols = slice(h * HEAD, (h + 1) * HEAD)
        row = slice(h, h + 1)
        dq, dk, dv = gradients(
            both(mine, sib, 2, h), both(mine, sib, 0, h), both(mine, sib, 3, h),
            kept[0, h], kept[1, h], scale, factor[row], delta[row],
        )
        dq_out[:, cols] = dq
        for i, part in enumerate((dk, dv)):
            own_out[i, :, cols] = part[:slots].astype(BF16)
            sib_out[i, :, cols] = part[slots:].astype(BF16)


def near_grad(place, mine, sib, kept, local, stats, gates):
    _, slots, half = mine.shape
    width = half // 2
    out = jax.ShapeDtypeStruct((2, slots, width), BF16)
    return pl.pallas_call(
        functools.partial(near_grad_kernel, HEAD**-0.5),
        out_shape=[jax.ShapeDtypeStruct((2 * slots, width), F32), out, out, jax.ShapeDtypeStruct(gates.shape, F32)],
        in_specs=[SMEM] + [VMEM] * 6,
        out_specs=[VMEM] * 4,
        compiler_params=params(),
        cost_estimate=cost(20 * slots * slots * half, 40 * slots * half),
        name="near_grad",
    )(place, mine, sib, kept, local, stats, gates)


def cross_grad_kernel(scale, place_ref, cross, kept, stats, local, heard, gates, near_dq, near_sum, straight, diag, dq_out, keep, final, sum_out):
    slots, width = straight.shape[1], straight.shape[2]
    heads = width // HEAD
    first = place_ref[1] == 0
    late = jnp.where(first, 0.0, 1.0)
    mine = [stats[i] for i in range(3)]
    other = [heard[i] for i in range(3)]
    near = [local[i, :heads] for i in range(3)]
    far = [local[i, heads:] for i in range(3)]
    factor, delta = merge(mine, choose(first, other, near))
    factor = factor * jnp.where(first, heard[3], jnp.broadcast_to(gates[...], factor.shape))
    final[0], final[1] = merge(far, choose(first, NONE, other))
    sum_out[...] = near_sum[...] + jnp.sum(final[1], axis=0, keepdims=True)
    for h in range(heads):
        cols = slice(h * HEAD, (h + 1) * HEAD)
        row = slice(h, h + 1)
        dq, dk, dv = gradients(
            cross[2, :, cols], cross[0, :, cols], cross[3, :, cols],
            kept[0, h], kept[1, h], scale, factor[row], delta[row],
        )
        dq_out[:, cols] = (near_dq[:, cols] + late * dq).astype(BF16)
        keep[0, :, cols] = dk.astype(BF16)
        keep[1, :, cols] = dv.astype(BF16)
        sent = jnp.where(first, dq, dk).astype(BF16)
        straight[0, :, cols] = sent[:slots]
        diag[0, :, cols] = sent[slots:]
        straight[1, :, cols] = dv[:slots].astype(BF16)
        diag[1, :, cols] = dv[slots:].astype(BF16)


def cross_grad(place, cross, kept, stats, local, heard, gates, near_dq, near_sum):
    _, rows, width = cross.shape
    slots = rows // 2
    out = jax.ShapeDtypeStruct((2, slots, width), BF16)
    return pl.pallas_call(
        functools.partial(cross_grad_kernel, HEAD**-0.5),
        out_shape=[
            out,
            out,
            jax.ShapeDtypeStruct((rows, width), BF16),
            jax.ShapeDtypeStruct((2, rows, width), BF16),
            jax.ShapeDtypeStruct((2, width // HEAD, rows), F32),
            jax.ShapeDtypeStruct((1, rows), F32),
        ],
        in_specs=[SMEM] + [VMEM] * 8,
        out_specs=[VMEM] * 6,
        compiler_params=params(),
        cost_estimate=cost(24 * slots * slots * width, 64 * slots * width),
        name="cross_grad",
    )(place, cross, kept, stats, local, heard, gates, near_dq, near_sum)


def far_grad_kernel(scale, place_ref, mine, sib, kept, final, gates, keep, near_dq, near_own, near_sib, own_out, sib_out):
    slots, half = mine.shape[1], mine.shape[2]
    width = half // 2
    heads = width // HEAD
    early = jnp.where(place_ref[1] == 0, 1.0, 0.0)
    factor = final[0] * gates[...]
    own_out[0, :, :width] = near_dq[:slots]
    sib_out[0, :, :width] = near_dq[slots:]
    for i in range(2):
        own_out[1 + i, :, :width] = near_own[i]
        sib_out[1 + i, :, :width] = near_sib[i]
    for h in range(heads):
        cols = slice(width + h * HEAD, width + (h + 1) * HEAD)
        at = slice(h * HEAD, (h + 1) * HEAD)
        dq, dk, dv = gradients(
            both(mine, sib, 2, heads + h), both(mine, sib, 0, heads + h), both(mine, sib, 3, heads + h),
            kept[0, heads + h], kept[1, heads + h], scale, factor[h : h + 1], final[1, h : h + 1],
        )
        dk = dk + early * keep[0, :, at].astype(F32)
        dv = dv + early * keep[1, :, at].astype(F32)
        for i, part in enumerate((dq, dk, dv)):
            own_out[i, :, cols] = part[:slots].astype(BF16)
            sib_out[i, :, cols] = part[slots:].astype(BF16)


def far_grad(place, mine, sib, kept, final, gates, keep, near_dq, near_own, near_sib):
    _, slots, half = mine.shape
    out = jax.ShapeDtypeStruct((3, slots, half), BF16)
    return pl.pallas_call(
        functools.partial(far_grad_kernel, HEAD**-0.5),
        out_shape=[out, out],
        in_specs=[SMEM] + [VMEM] * 9,
        out_specs=[VMEM] * 2,
        compiler_params=params(),
        cost_estimate=cost(20 * slots * slots * half, 40 * slots * half),
        name="far_grad",
    )(place, mine, sib, kept, final, gates, keep, near_dq, near_own, near_sib)


def join_kernel(place_ref, own, sib, straight, diag, dq_out, dk_out, dv_out):
    half = own.shape[-1]
    width = straight.shape[-1]
    core, chip = place_ref[0], place_ref[1]
    early, late = jnp.where(chip == 0, 1.0, 0.0), jnp.where(chip == 0, 0.0, 1.0)
    for part, extra, start in ((own, straight, core * half), (sib, diag, (1 - core) * half)):
        low = pl.ds(pl.multiple_of(start, HEAD), width)
        high = pl.ds(pl.multiple_of(start + width, HEAD), width)
        dq_out[0, :, low] = part[0, :, :width].astype(F32)
        dq_out[0, :, high] = part[0, :, width:].astype(F32) + late * extra[0].astype(F32)
        for i, out in enumerate((dk_out, dv_out)):
            out[0, :, low] = part[1 + i, :, :width].astype(F32) + early * extra[i].astype(F32)
            out[0, :, high] = part[1 + i, :, width:].astype(F32)


def join(place, own, sib, straight, diag, shape):
    out = jax.ShapeDtypeStruct(shape, F32)
    return pl.pallas_call(
        join_kernel,
        out_shape=[out] * 3,
        in_specs=[SMEM] + [VMEM] * 4,
        out_specs=[VMEM] * 3,
        compiler_params=params(),
        cost_estimate=cost(0, 18 * out.size),
        name="join",
    )(place, own, sib, straight, diag)


def pair_router_kernel(gates_ref, sum_ref, x_ref, sib_ref, out_ref):
    gates = gates_ref[...]
    grad = sum_ref[...] * gates * (1.0 - gates)
    high = grad.astype(BF16)
    rest = grad - high.astype(F32)
    mid = rest.astype(BF16)
    low = (rest - mid.astype(F32)).astype(BF16)
    slots = x_ref.shape[1]
    row = lax.broadcasted_iota(jnp.int32, (8, grad.shape[1]), 0)
    lhs = jnp.where(row == 0, high.astype(F32), jnp.where(row == 1, mid.astype(F32), jnp.where(row == 2, low.astype(F32), 0.0)))
    lhs = lhs.astype(BF16)
    term = jnp.sum(nn(lhs[:, :slots], x_ref[0]) + nn(lhs[:, slots:], sib_ref[0]), axis=0, keepdims=True)
    parts, copies, _, chunk = out_ref.shape
    for j in range(parts):
        for i in range(copies):
            out_ref[j, i] = term[:, j * chunk : (j + 1) * chunk]


def pair_router(gates, sums, x_routed, x_sib, parts, copies):
    chunk = x_routed.shape[-1] // parts
    return pl.pallas_call(
        pair_router_kernel,
        out_shape=jax.ShapeDtypeStruct((parts, copies, 1, chunk), F32),
        in_specs=[VMEM] * 4,
        out_specs=VMEM,
        compiler_params=params(),
        cost_estimate=cost(32 * x_routed.size, x_routed.size * 4),
        name="router_terms",
    )(gates, sums, x_routed, x_sib)


def swap_body(route_pos, x_routed, w_router, queries, keys, values, d_gated):
    slots = queries.shape[1]
    n, ndp = lax.axis_size("ctx"), lax.axis_size("dp")
    me = lax.axis_index("ctx")
    place = jnp.stack([me % 2, me // 2, lax.axis_index("dp")]).astype(jnp.int32)

    def send(a, flip):
        return lax.ppermute(a, "ctx", [(i, i ^ flip) for i in range(n)])

    def widen(part, step):
        other = lax.ppermute(part, "dp", [(i, i ^ step) for i in range(ndp)])
        return jnp.concatenate([part, other], axis=1)

    def beside(fn, *operands):
        def skip(*ops):
            return jax.tree.map(lambda o: jnp.zeros(o.shape, o.dtype), jax.eval_shape(fn, *ops))

        return lax.cond(route_pos[0, 0] >= -1, fn, skip, *operands)

    def local_phase(place, route_pos, x_routed, w_part, keys, values, queries, d_gated):
        mine, theirs = half_pack(place, route_pos, keys, values, queries, d_gated)
        sib, x_sib = send(theirs, 1), send(x_routed, 1)
        step = 2
        while step < ndp:
            w_part = widen(w_part, step)
            if step == 2:
                w_part, _ = lax.optimization_barrier((w_part, mine))
            step *= 2
        local, kept, live = local_stats(place, mine, sib)
        gates = pair_gate(place, live, x_routed, x_sib, w_part, ndp)
        return mine, sib, x_sib, local, kept, gates

    def grad_phase(*operands):
        own_out, sib_out = far_grad(*operands)
        return own_out, send(sib_out, 1)

    def router_phase(gates, sums, x_routed, x_sib, place, *operands):
        terms = pair_router(gates, sums, x_routed, x_sib, ndp, n)
        chunk = terms.shape[-1]
        shared = lax.all_to_all(terms.reshape(ndp * n, 1, chunk), ("dp", "ctx"), 0, 0, tiled=True)
        place, _ = lax.optimization_barrier((place, terms))
        own_out, sib_in = beside(grad_phase, place, *operands)
        return own_out, sib_in, jnp.sum(shared, axis=0)[0] / float(ndp * n * slots // 2)

    w_part = w_router.reshape(1, -1).astype(F32)
    if ndp > 1:
        w_part = widen(w_part, 1)
    out_s, out_d = cross_pack(place, route_pos, keys, values, queries, d_gated)
    in_s, in_d = send(out_s, 2), send(out_d, 3)
    late_pos, _ = lax.optimization_barrier((route_pos, out_s))
    mine, sib, x_sib, local, kept, gates = beside(
        local_phase, place, late_pos, x_routed, w_part, keys, values, queries, d_gated
    )
    cross, stats, kept_cross, message = cross_stats(place, mine, sib, in_s, in_d, local, gates)
    heard = send(message, 2)
    near_dq, near_own, near_sib, near_sum = near_grad(place, mine, sib, kept, local, stats, gates)
    back_s, back_d, dq_low, keep, final, sums = cross_grad(
        place, cross, kept_cross, stats, local, heard, gates, near_dq, near_sum
    )
    ret_s, ret_d = send(back_s, 2), send(back_d, 3)
    own_out, sib_in, router_grad = beside(
        router_phase, gates, sums, x_routed, x_sib, place, mine, sib, kept, final, gates, keep, dq_low, near_own, near_sib
    )
    dq, dk, dv = join(place, own_out, sib_in, ret_s, ret_d, queries.shape)
    return dq, dk, dv, router_grad


def body(route_pos, x_routed, w_router, queries, keys, values, d_gated):
    slots, full = queries.shape[1], queries.shape[2]
    n, ndp = lax.axis_size("ctx"), lax.axis_size("dp")
    chips = n // 2
    me, dp_me = lax.axis_index("ctx"), lax.axis_index("dp")
    core = (me % 2).astype(jnp.int32).reshape(1)
    half = full // 2
    groups = GROUPS if (half // HEAD) % GROUPS == 0 else 1
    width = half // groups

    sib_pairs = [(i, i ^ 1) for i in range(n)]

    def forward_pairs(step, flip):
        return [(i, (i + 2 * step) ^ flip) for i in range(n) if i + 2 * step < n]

    def back_pairs(step, flip):
        return [(b, a) for a, b in forward_pairs(step, flip)]

    def to_sib(a):
        return lax.ppermute(a, "ctx", sib_pairs)

    links = [(step, flip) for step in range(1, chips) for flip in (0, 1)]

    w_row = w_router.reshape(1, -1)
    w_parts = [w_row] + [
        lax.ppermute(w_row, "dp", [(i, (i + s) % ndp) for i in range(ndp)]) for s in range(1, ndp)
    ]
    live = (route_pos >= 0).astype(jnp.int32)
    lives = [live, to_sib(live)] + [lax.ppermute(live, "ctx", forward_pairs(*link)) for link in links]
    live_all = jnp.concatenate(lives, axis=0)

    kv_mine, kv_theirs = pack(core, keys, values, groups, width)
    kv_far = [
        [lax.ppermute((kv_theirs if flip else kv_mine)[g], "ctx", forward_pairs(step, flip)) for step, flip in links]
        for g in range(groups)
    ]
    q_mine, q_theirs = pack(core, queries, d_gated, groups, width)
    kv_sib = [to_sib(a) for a in kv_theirs]
    q_sib = [to_sib(a) for a in q_theirs]

    offsets = ((dp_me - jnp.arange(ndp)) % ndp).astype(jnp.int32)
    gate = router_gate(offsets, route_pos, x_routed, w_parts)
    gates = (gate, to_sib(gate))

    accs = (jnp.zeros((1, slots), F32), jnp.zeros((1, slots), F32))
    dq_own, sib_in, kv_own, back = [], [], [], []
    for g in range(groups):
        dq, sib_out, kv_local, kv_remote, accs = attention(
            core, live_all, gates, accs, q_mine[g], q_sib[g], [kv_mine[g], kv_sib[g], *kv_far[g]]
        )
        back.append([lax.ppermute(a, "ctx", back_pairs(*link)) for a, link in zip(kv_remote, links)])
        sib_in.append(to_sib(sib_out))
        dq_own.append(dq)
        kv_own.append(kv_local)

    targets = ((dp_me + jnp.arange(ndp)) % ndp).astype(jnp.int32)
    terms = router_terms(targets, gate, accs[0], to_sib(accs[1]), x_routed, ndp)
    mine = terms[0]
    for s in range(1, ndp):
        mine = mine + lax.ppermute(terms[s], "dp", [(i, (i + s) % ndp) for i in range(ndp)])
    total = mine
    for s in range(1, n):
        total = total + lax.ppermute(mine, "ctx", [(i, (i + s) % n) for i in range(n)])
    router_grad = total[0] / float(ndp * n * slots // 2)

    dq, dk, dv = combine(core, dq_own, sib_in, kv_own, back, queries.shape)
    return dq, dk, dv, router_grad


def solution(mesh):
    placed = (
        P("dp", "ctx"),
        P("dp", "ctx", None),
        P("dp"),
        P("dp", "ctx", None),
        P("dp", "ctx", None),
        P("dp", "ctx", None),
        P("dp", "ctx", None),
    )
    ndp = mesh.shape["dp"]
    paired = mesh.shape["ctx"] == 4 and ndp & (ndp - 1) == 0
    return jax.shard_map(
        swap_body if paired else body,
        mesh=mesh,
        in_specs=placed,
        out_specs=(P("dp", "ctx", None), P("dp", "ctx", None), P("dp", "ctx", None), P("dp")),
        check_vma=False,
    )
```

```python
import functools

import jax
import jax.numpy as jnp
from jax import lax
from jax.experimental import pallas as pl
from jax.experimental.pallas import tpu as pltpu
from jax.sharding import PartitionSpec as P

HEAD = 128
GROUPS = 4
NEG_FILL = -1e30
MIB = 1024 * 1024
BF16 = jnp.bfloat16
F32 = jnp.float32

VMEM = pl.BlockSpec(memory_space=pltpu.VMEM)
SMEM = pl.BlockSpec(memory_space=pltpu.SMEM)


def params(mib=20):
    return pltpu.CompilerParams(vmem_limit_bytes=mib * MIB)


def cost(flops, nbytes, exps=0):
    return pl.CostEstimate(flops=1, bytes_accessed=1, transcendentals=0)


def nt(a, b):
    return lax.dot_general(a, b, (((1,), (1,)), ((), ())), preferred_element_type=F32)


def nn(a, b):
    return lax.dot_general(a, b, (((1,), (0,)), ((), ())), preferred_element_type=F32)


def tn(a, b):
    return lax.dot_general(a, b, (((0,), (0,)), ((), ())), preferred_element_type=F32)


def pack_kernel(groups, width, core_ref, first_ref, second_ref, *outs):
    half = first_ref.shape[-1] // 2
    core = core_ref[0]
    for side in range(2):
        base = (core if side == 0 else 1 - core) * half
        for g in range(groups):
            out = outs[side * groups + g]
            cols = pl.ds(pl.multiple_of(base + g * width, HEAD), width)
            out[0] = first_ref[0, :, cols].astype(BF16)
            out[1] = second_ref[0, :, cols].astype(BF16)


def pack(core, first, second, groups, width):
    slots = first.shape[1]
    out = jax.ShapeDtypeStruct((2, slots, width), BF16)
    res = pl.pallas_call(
        functools.partial(pack_kernel, groups, width),
        out_shape=[out] * (2 * groups),
        in_specs=[SMEM, VMEM, VMEM],
        out_specs=[VMEM] * (2 * groups),
        compiler_params=params(),
        cost_estimate=cost(0, 2 * first.size * 4),
        name="pack",
    )(core, first, second)
    return res[:groups], res[groups:]


def gate_kernel(parts, offset_ref, pos_ref, x_ref, *refs):
    w_refs, out_ref = refs[:parts], refs[parts]
    chunk = w_refs[0].shape[-1]
    total = jnp.zeros((8, x_ref.shape[1]), F32)
    for s in range(parts):
        cols = pl.ds(pl.multiple_of(offset_ref[s] * chunk, HEAD), chunk)
        w_rows = jnp.broadcast_to(w_refs[s][...].astype(F32), (8, chunk)).astype(BF16)
        total = total + nt(w_rows, x_ref[0, :, cols])
    gate = 1.0 / (1.0 + jnp.exp(-total[0:1]))
    out_ref[...] = jnp.where(pos_ref[...] >= 0, gate, 0.0)


def router_gate(offsets, route_pos, x_routed, w_parts):
    parts = len(w_parts)
    return pl.pallas_call(
        functools.partial(gate_kernel, parts),
        out_shape=jax.ShapeDtypeStruct(route_pos.shape, F32),
        in_specs=[SMEM] + [VMEM] * (2 + parts),
        out_specs=VMEM,
        compiler_params=params(),
        cost_estimate=cost(16 * x_routed.size, x_routed.size * 2),
        name="router_gate",
    )(offsets, route_pos, x_routed, *w_parts)


def attention_kernel(remote, scale, core_ref, live_ref, gate_own, gate_sib, acc_own, acc_sib, q_own, q_sib, *refs):
    chunks = 2 + remote
    kv = refs[:chunks]
    outs = refs[chunks:]
    dq_own, sib_out, kv_own = outs[:3]
    kv_remote = outs[3 : 3 + remote]
    sum_own, sum_sib = outs[3 + remote :]
    slots, width = q_own.shape[1], q_own.shape[2]
    core = core_ref[0]
    key = lax.broadcasted_iota(jnp.int32, (slots, slots), 0)
    query = lax.broadcasted_iota(jnp.int32, (slots, slots), 1)
    counts = [jnp.sum(live_ref[i : i + 1], axis=1, keepdims=True) for i in range(chunks)]
    lives = [key < counts[i] for i in range(chunks)]
    own_later = core == 1
    bias_rows = []
    for i in range(chunks):
        live = lives[i]
        if i == 0:
            pair = (live & (key <= query), live & jnp.logical_not(own_later))
        elif i == 1:
            pair = (live & own_later, live & (key <= query))
        else:
            pair = (live, live)
        bias_rows.append(jnp.concatenate([jnp.where(p, 0.0, NEG_FILL) for p in pair], axis=1))
    bias = jnp.concatenate(bias_rows, axis=0)
    gates = jnp.concatenate([gate_own[...], gate_sib[...]], axis=1)
    total = jnp.zeros((1, 2 * slots), F32)
    for h in range(width // HEAD):
        cols = slice(h * HEAD, (h + 1) * HEAD)
        q = jnp.concatenate([q_own[0, :, cols], q_sib[0, :, cols]], axis=0)
        dg = jnp.concatenate([q_own[1, :, cols], q_sib[1, :, cols]], axis=0)
        k = jnp.concatenate([r[0, :, cols] for r in kv], axis=0)
        v = jnp.concatenate([r[1, :, cols] for r in kv], axis=0)
        scores = nt(k, q) * scale + bias
        top = jnp.max(scores, axis=0, keepdims=True)
        e = jnp.exp(scores - top)
        inverse = 1.0 / jnp.sum(e, axis=0, keepdims=True)
        gw = nt(v, dg)
        delta = jnp.sum(e * gw, axis=0, keepdims=True) * inverse
        total = total + delta
        weights = e * (inverse * gates)
        dv = nn(weights.astype(BF16), dg)
        ds = (weights * ((gw - delta) * scale)).astype(BF16)
        dk = nn(ds, q)
        dq = tn(ds, k)
        dq_own[:, cols] = dq[:slots].astype(dq_own.dtype)
        sib_out[0, :, cols] = dq[slots:].astype(BF16)
        kv_own[0, :, cols] = dk[:slots].astype(BF16)
        kv_own[1, :, cols] = dv[:slots].astype(BF16)
        sib_out[1, :, cols] = dk[slots : 2 * slots].astype(BF16)
        sib_out[2, :, cols] = dv[slots : 2 * slots].astype(BF16)
        for i in range(remote):
            rows = slice((2 + i) * slots, (3 + i) * slots)
            kv_remote[i][0, :, cols] = dk[rows].astype(BF16)
            kv_remote[i][1, :, cols] = dv[rows].astype(BF16)
    sum_own[...] = acc_own[...] + total[:, :slots]
    sum_sib[...] = acc_sib[...] + total[:, slots:]


def attention(core, live, gates, accs, q_own, q_sib, kv):
    remote = len(kv) - 2
    _, slots, width = q_own.shape
    pair = jax.ShapeDtypeStruct((2, slots, width), BF16)
    row = jax.ShapeDtypeStruct((1, slots), F32)
    outs = [
        jax.ShapeDtypeStruct((slots, width), BF16),
        jax.ShapeDtypeStruct((3, slots, width), BF16),
        pair,
        *([pair] * remote),
        row,
        row,
    ]
    keys = (2 + remote) * slots
    res = pl.pallas_call(
        functools.partial(attention_kernel, remote, HEAD**-0.5),
        out_shape=outs,
        in_specs=[SMEM] + [VMEM] * (7 + len(kv)),
        out_specs=[VMEM] * len(outs),
        compiler_params=params(48),
        cost_estimate=cost(20 * slots * keys * width, 8 * keys * width + 20 * slots * width, 2 * slots * keys * width // HEAD),
        name="attention",
    )(core, live, *gates, *accs, q_own, q_sib, *kv)
    return res[0], res[1], res[2], res[3 : 3 + remote], (res[3 + remote], res[4 + remote])


def combine_kernel(groups, width, remote, core_ref, *refs):
    dq_own, sib, kv_own = refs[:groups], refs[groups : 2 * groups], refs[2 * groups : 3 * groups]
    back = refs[3 * groups : 3 * groups + groups * remote]
    dq_out, dk_out, dv_out = refs[3 * groups + groups * remote :]
    half = groups * width
    core = core_ref[0]
    for g in range(groups):
        own = pl.ds(pl.multiple_of(core * half + g * width, HEAD), width)
        other = pl.ds(pl.multiple_of((1 - core) * half + g * width, HEAD), width)
        dq_out[0, :, own] = dq_own[g][...].astype(F32)
        dq_out[0, :, other] = sib[g][0].astype(F32)
        for i, out in enumerate((dk_out, dv_out)):
            mine = kv_own[g][i].astype(F32)
            theirs = sib[g][1 + i].astype(F32)
            for r in range(remote):
                part = back[g * remote + r][i].astype(F32)
                if r % 2 == 0:
                    mine = mine + part
                else:
                    theirs = theirs + part
            out[0, :, own] = mine
            out[0, :, other] = theirs


def combine(core, dq_own, sib, kv_own, back, shape):
    groups = len(dq_own)
    remote = len(back[0])
    out = jax.ShapeDtypeStruct(shape, F32)
    flat = [*dq_own, *sib, *kv_own, *(b for group in back for b in group)]
    return pl.pallas_call(
        functools.partial(combine_kernel, groups, dq_own[0].shape[-1], remote),
        out_shape=[out] * 3,
        in_specs=[SMEM] + [VMEM] * len(flat),
        out_specs=[VMEM] * 3,
        compiler_params=params(48),
        cost_estimate=cost(0, 3 * out.size * 6),
        name="combine",
    )(core, *flat)


def router_kernel(parts, target_ref, gate_ref, own_ref, sib_ref, x_ref, *outs):
    gate = gate_ref[...]
    grad = (own_ref[...] + sib_ref[...]) * gate * (1.0 - gate)
    high = grad.astype(BF16)
    rest = grad - high.astype(F32)
    mid = rest.astype(BF16)
    low = (rest - mid.astype(F32)).astype(BF16)
    row = lax.broadcasted_iota(jnp.int32, (8, grad.shape[1]), 0)
    lhs = jnp.where(row == 0, high.astype(F32), jnp.where(row == 1, mid.astype(F32), jnp.where(row == 2, low.astype(F32), 0.0)))
    lhs = lhs.astype(BF16)
    chunk = outs[0].shape[-1]
    for s in range(parts):
        cols = pl.ds(pl.multiple_of(target_ref[s] * chunk, HEAD), chunk)
        outs[s][...] = jnp.sum(nn(lhs, x_ref[0, :, cols]), axis=0, keepdims=True)


def router_terms(targets, gate, own, sib, x_routed, parts):
    chunk = x_routed.shape[-1] // parts
    return pl.pallas_call(
        functools.partial(router_kernel, parts),
        out_shape=[jax.ShapeDtypeStruct((1, chunk), F32)] * parts,
        in_specs=[SMEM] + [VMEM] * 4,
        out_specs=[VMEM] * parts,
        compiler_params=params(),
        cost_estimate=cost(16 * x_routed.size, x_routed.size * 2),
        name="router_terms",
    )(targets, gate, own, sib, x_routed)


MARK = 2.0**60
MARK_LIMIT = 2.0**50


def live_rows(pos_ref, slots):
    count = jnp.sum((pos_ref[...] >= 0).astype(jnp.int32), axis=1, keepdims=True)
    return lax.broadcasted_iota(jnp.int32, (slots, HEAD), 0) < count


def mark_dead(keys, live):
    width = keys.shape[-1]
    mask = jnp.concatenate([live] * (width // HEAD), axis=1)
    return jnp.where(mask, keys.astype(F32), MARK).astype(BF16)


def cross_pack_kernel(place_ref, pos_ref, k_ref, v_ref, q_ref, dg_ref, straight, diag, wide, sems):
    slots, width = straight.shape[1], straight.shape[2]
    half = k_ref.shape[-1] // 2
    core, chip = place_ref[0], place_ref[1]
    ends = ((straight, core * half), (diag, (1 - core) * half))

    def copies(first, second, targets, offset):
        out = []
        for i, (end, start) in enumerate(ends):
            cols = pl.ds(pl.multiple_of(start + offset, HEAD), width)
            out.append(pltpu.make_async_copy(first.at[0, :, cols], end.at[0], sems.at[2 * i]))
            out.append(pltpu.make_async_copy(second.at[0, :, cols], targets[i], sems.at[2 * i + 1]))
        for c in out:
            c.start()
        for c in out:
            c.wait()

    @pl.when(chip == 0)
    def _():
        copies(k_ref, v_ref, (straight.at[1], diag.at[1]), 0)
        live = live_rows(pos_ref, slots)
        for end, _ in ends:
            end[0] = mark_dead(end[0], live)

    @pl.when(chip != 0)
    def _():
        copies(q_ref, dg_ref, (wide.at[0], wide.at[1]), width)
        for i, (end, _) in enumerate(ends):
            end[1] = wide[i].astype(BF16)


def cross_pack(place, route_pos, keys, values, queries, d_gated):
    _, slots, full = keys.shape
    cross = jax.ShapeDtypeStruct((2, slots, full // 4), BF16)
    hbm = pl.BlockSpec(memory_space=pltpu.HBM)
    return pl.pallas_call(
        cross_pack_kernel,
        out_shape=[cross, cross],
        in_specs=[SMEM, VMEM, hbm, hbm, hbm, hbm],
        out_specs=[VMEM] * 2,
        scratch_shapes=[pltpu.VMEM((2, slots, full // 4), F32), pltpu.SemaphoreType.DMA((4,))],
        compiler_params=params(60),
        cost_estimate=cost(0, 10 * slots * full),
        name="cross_pack",
    )(place, route_pos, keys, values, queries, d_gated)


def sib_pack_kernel(place_ref, pos_ref, k_ref, v_ref, q_ref, dg_ref, out, wide, sems):
    slots, half = out.shape[1], out.shape[2]
    cols = pl.ds(pl.multiple_of((1 - place_ref[0]) * half, HEAD), half)
    sources = ((k_ref, out.at[0]), (dg_ref, wide), (v_ref, out.at[1]), (q_ref, out.at[2]))
    copies = [pltpu.make_async_copy(src.at[0, :, cols], dst, sems.at[i]) for i, (src, dst) in enumerate(sources)]
    for c in copies:
        c.start()
    live = live_rows(pos_ref, slots)
    copies[0].wait()
    out[0] = mark_dead(out[0], live)
    copies[1].wait()
    out[3] = wide[...].astype(BF16)
    copies[2].wait()
    copies[3].wait()


def sib_pack(place, route_pos, keys, values, queries, d_gated):
    _, slots, full = keys.shape
    hbm = pl.BlockSpec(memory_space=pltpu.HBM)
    return pl.pallas_call(
        sib_pack_kernel,
        out_shape=jax.ShapeDtypeStruct((4, slots, full // 2), BF16),
        in_specs=[SMEM, VMEM, hbm, hbm, hbm, hbm],
        out_specs=VMEM,
        scratch_shapes=[pltpu.VMEM((slots, full // 2), F32), pltpu.SemaphoreType.DMA((4,))],
        compiler_params=params(60),
        cost_estimate=cost(0, 20 * slots * full),
        name="sib_pack",
    )(place, route_pos, keys, values, queries, d_gated)


def pair_gate_kernel(parts, place_ref, live_ref, x_ref, sib_ref, w_ref, out_ref):
    chunk = w_ref.shape[1] // parts
    slots = x_ref.shape[1]
    for i, ref in enumerate((x_ref, sib_ref)):
        total = jnp.zeros((8, slots), F32)
        for j in range(parts):
            w_rows = jnp.broadcast_to(w_ref[:, j * chunk : (j + 1) * chunk], (8, chunk)).astype(BF16)
            cols = pl.ds(pl.multiple_of((place_ref[2] ^ j) * chunk, HEAD), chunk)
            total = total + nt(w_rows, ref[0, :, cols])
        lanes = slice(i * slots, (i + 1) * slots)
        out_ref[:, lanes] = live_ref[:, lanes] / (1.0 + jnp.exp(-total[0:1]))


def pair_gate(place, live, x_routed, x_sib, w_full, parts):
    return pl.pallas_call(
        functools.partial(pair_gate_kernel, parts),
        out_shape=jax.ShapeDtypeStruct(live.shape, F32),
        in_specs=[SMEM] + [VMEM] * 4,
        out_specs=VMEM,
        compiler_params=params(),
        cost_estimate=cost(16 * x_routed.size, x_routed.size * 2),
        name="router_gate",
    )(place, live, x_routed, x_sib, w_full)


def local_mask(core, pair):
    slots = pair.shape[1] // 2
    key = lax.broadcasted_iota(jnp.int32, (slots, slots), 0)
    query = lax.broadcasted_iota(jnp.int32, (slots, slots), 1)
    causal = key <= query
    own_live = pair[0, :slots, :slots].astype(F32) < MARK_LIMIT
    sib_live = pair[0, slots:, :slots].astype(F32) < MARK_LIMIT
    own_rows = jnp.concatenate([own_live & causal, own_live & (core == 0)], axis=1)
    sib_rows = jnp.concatenate([sib_live & (core == 1), sib_live & causal], axis=1)
    return jnp.concatenate([own_rows, sib_rows], axis=0)


def partial_stats(scores, gw, kept, stats, h):
    top = jnp.max(scores, axis=0, keepdims=True)
    e = jnp.exp(scores - top).astype(BF16)
    gw = gw.astype(BF16)
    kept[0, h] = e
    kept[1, h] = gw
    e = e.astype(F32)
    stats[0, h : h + 1] = top
    stats[1, h : h + 1] = jnp.sum(e, axis=0, keepdims=True)
    stats[2, h : h + 1] = jnp.sum(e * gw.astype(F32), axis=0, keepdims=True)


def local_stats_kernel(scale, place_ref, pos_ref, k_ref, v_ref, q_ref, dg_ref, sib, stats, kept, live, pair, wide, sems):
    slots, half = sib.shape[1], sib.shape[2]
    width = half // 2
    core = place_ref[0]
    own, other = slice(0, slots), slice(slots, 2 * slots)
    stages = []
    for g in range(2):
        cols = slice(g * width, (g + 1) * width)
        held = pl.ds(pl.multiple_of(core * half + g * width, HEAD), width)
        copies = [
            pltpu.make_async_copy(ref.at[0, :, held], pair.at[j, own, cols], sems.at[8 * g + j])
            for j, ref in enumerate((k_ref, v_ref, q_ref))
        ]
        copies.append(pltpu.make_async_copy(dg_ref.at[0, :, held], wide.at[:, cols], sems.at[8 * g + 3]))
        for j in range(4):
            copies.append(pltpu.make_async_copy(sib.at[j, :, cols], pair.at[j, other, cols], sems.at[8 * g + 4 + j]))
        for c in copies:
            c.start()
        stages.append(copies)
    rows_live = live_rows(pos_ref, slots)
    mask = None
    for g in range(2):
        cols = slice(g * width, (g + 1) * width)
        for c in stages[g]:
            c.wait()
        pair[0, own, cols] = mark_dead(pair[0, own, cols], rows_live)
        pair[3, own, cols] = wide[:, cols].astype(BF16)
        if mask is None:
            mask = local_mask(core, pair)
            marks = nt(jnp.ones((8, HEAD), BF16), pair[0, :, :HEAD])[0:1]
            live[...] = jnp.where(marks < MARK_LIMIT, 1.0, 0.0)
        for h in range(g * width // HEAD, (g + 1) * width // HEAD):
            at = slice(h * HEAD, (h + 1) * HEAD)
            scores = jnp.where(mask, nt(pair[0, :, at], pair[2, :, at]) * scale, NEG_FILL)
            partial_stats(scores, nt(pair[1, :, at], pair[3, :, at]), kept, stats, h)


def local_stats(place, route_pos, keys, values, queries, d_gated, sib):
    _, slots, half = sib.shape
    heads = half // HEAD
    anywhere = pl.BlockSpec(memory_space=pl.ANY)
    return pl.pallas_call(
        functools.partial(local_stats_kernel, HEAD**-0.5),
        out_shape=[
            jax.ShapeDtypeStruct((3, heads, 2 * slots), F32),
            jax.ShapeDtypeStruct((2, heads, 2 * slots, 2 * slots), BF16),
            jax.ShapeDtypeStruct((1, 2 * slots), F32),
            jax.ShapeDtypeStruct((4, 2 * slots, half), BF16),
        ],
        in_specs=[SMEM, VMEM] + [anywhere] * 5,
        out_specs=[VMEM] * 4,
        scratch_shapes=[pltpu.VMEM((slots, half), F32), pltpu.SemaphoreType.DMA((16,))],
        compiler_params=params(24),
        cost_estimate=cost(16 * slots * slots * half, 16 * slots * half, 4 * slots * slots * half // HEAD),
        name="local_stats",
    )(place, route_pos, keys, values, queries, d_gated, sib)


def cross_stats_kernel(scale, place_ref, pair, straight, diag, local, gates, cross, stats, kept, message):
    slots, width = straight.shape[1], straight.shape[2]
    chip = place_ref[1]
    top, bottom = slice(0, slots), slice(slots, 2 * slots)

    @pl.when(chip == 0)
    def _():
        cols = slice(width, 2 * width)
        for part in range(2):
            cross[part] = pair[part, :, cols]
            cross[2 + part, top] = straight[part]
            cross[2 + part, bottom] = diag[part]

    @pl.when(chip != 0)
    def _():
        cols = slice(0, width)
        for part in range(2):
            cross[part, top] = straight[part]
            cross[part, bottom] = diag[part]
            cross[2 + part] = pair[2 + part, :, cols]

    live = cross[0, :, :HEAD].astype(F32) < MARK_LIMIT
    mask = jnp.concatenate([live] * (2 * slots // HEAD), axis=1)
    heads = width // HEAD
    for h in range(heads):
        cols = slice(h * HEAD, (h + 1) * HEAD)
        scores = jnp.where(mask, nt(cross[0, :, cols], cross[2, :, cols]) * scale, NEG_FILL)
        partial_stats(scores, nt(cross[1, :, cols], cross[3, :, cols]), kept, stats, h)
    for i in range(3):
        message[i] = jnp.where(chip == 0, stats[i], local[i, heads:])
    message[3] = jnp.broadcast_to(gates[...], message.shape[1:])


def cross_stats(place, pair, straight, diag, local, gates):
    _, slots, width = straight.shape
    heads = width // HEAD
    return pl.pallas_call(
        functools.partial(cross_stats_kernel, HEAD**-0.5),
        out_shape=[
            jax.ShapeDtypeStruct((4, 2 * slots, width), BF16),
            jax.ShapeDtypeStruct((3, heads, 2 * slots), F32),
            jax.ShapeDtypeStruct((2, heads, 2 * slots, 2 * slots), BF16),
            jax.ShapeDtypeStruct((4, heads, 2 * slots), F32),
        ],
        in_specs=[SMEM] + [VMEM] * 5,
        out_specs=[VMEM] * 4,
        compiler_params=params(),
        cost_estimate=cost(16 * slots * slots * width, 32 * slots * width, 4 * slots * slots * heads),
        name="cross_stats",
    )(place, pair, straight, diag, local, gates)


NONE = (-3e38, 0.0, 0.0)


def merge(first, second):
    top = jnp.maximum(first[0], second[0])
    a, b = jnp.exp(first[0] - top), jnp.exp(second[0] - top)
    inverse = 1.0 / (first[1] * a + second[1] * b)
    return a * inverse, (first[2] * a + second[2] * b) * inverse


def choose(flag, yes, no):
    return [jnp.where(flag, y, n) for y, n in zip(yes, no)]


def gradients(q, k, dg, e, gw, scale, factor, delta):
    weights = e.astype(F32) * factor
    ds = (weights * ((gw.astype(F32) - delta) * scale)).astype(BF16)
    return tn(ds, k), nn(ds, q), nn(weights.astype(BF16), dg)


def near_grad_kernel(scale, place_ref, pair, kept, local, stats, gates, dq_out, own_out, sib_out, sum_out):
    slots, width = own_out.shape[1], own_out.shape[2]
    heads = width // HEAD
    first = place_ref[1] == 0
    near = [local[i, :heads] for i in range(3)]
    factor, delta = merge(near, choose(first, NONE, [stats[i] for i in range(3)]))
    factor = factor * gates[...]
    sum_out[...] = jnp.sum(delta, axis=0, keepdims=True)
    for h in range(heads):
        cols = slice(h * HEAD, (h + 1) * HEAD)
        row = slice(h, h + 1)
        dq, dk, dv = gradients(
            pair[2, :, cols], pair[0, :, cols], pair[3, :, cols],
            kept[0, h], kept[1, h], scale, factor[row], delta[row],
        )
        dq_out[:, cols] = dq
        for i, part in enumerate((dk, dv)):
            own_out[i, :, cols] = part[:slots].astype(BF16)
            sib_out[i, :, cols] = part[slots:].astype(BF16)


def near_grad(place, pair, kept, local, stats, gates):
    _, rows, half = pair.shape
    slots = rows // 2
    width = half // 2
    out = jax.ShapeDtypeStruct((2, slots, width), BF16)
    return pl.pallas_call(
        functools.partial(near_grad_kernel, HEAD**-0.5),
        out_shape=[jax.ShapeDtypeStruct((2 * slots, width), F32), out, out, jax.ShapeDtypeStruct(gates.shape, F32)],
        in_specs=[SMEM] + [VMEM] * 5,
        out_specs=[VMEM] * 4,
        compiler_params=params(),
        cost_estimate=cost(20 * slots * slots * half, 40 * slots * half),
        name="near_grad",
    )(place, pair, kept, local, stats, gates)


def cross_grad_kernel(scale, place_ref, cross, kept, stats, local, heard, gates, near_dq, near_sum, straight, diag, dq_out, keep, final, sum_out):
    slots, width = straight.shape[1], straight.shape[2]
    heads = width // HEAD
    first = place_ref[1] == 0
    late = jnp.where(first, 0.0, 1.0)
    mine = [stats[i] for i in range(3)]
    other = [heard[i] for i in range(3)]
    near = [local[i, :heads] for i in range(3)]
    far = [local[i, heads:] for i in range(3)]
    factor, delta = merge(mine, choose(first, other, near))
    factor = factor * jnp.where(first, heard[3], jnp.broadcast_to(gates[...], factor.shape))
    final[0], final[1] = merge(far, choose(first, NONE, other))
    sum_out[...] = near_sum[...] + jnp.sum(final[1], axis=0, keepdims=True)
    for h in range(heads):
        cols = slice(h * HEAD, (h + 1) * HEAD)
        row = slice(h, h + 1)
        dq, dk, dv = gradients(
            cross[2, :, cols], cross[0, :, cols], cross[3, :, cols],
            kept[0, h], kept[1, h], scale, factor[row], delta[row],
        )
        dq_out[:, cols] = (near_dq[:, cols] + late * dq).astype(BF16)
        keep[0, :, cols] = dk.astype(BF16)
        keep[1, :, cols] = dv.astype(BF16)
        sent = jnp.where(first, dq, dk).astype(BF16)
        straight[0, :, cols] = sent[:slots]
        diag[0, :, cols] = sent[slots:]
        straight[1, :, cols] = dv[:slots].astype(BF16)
        diag[1, :, cols] = dv[slots:].astype(BF16)


def cross_grad(place, cross, kept, stats, local, heard, gates, near_dq, near_sum):
    _, rows, width = cross.shape
    slots = rows // 2
    out = jax.ShapeDtypeStruct((2, slots, width), BF16)
    return pl.pallas_call(
        functools.partial(cross_grad_kernel, HEAD**-0.5),
        out_shape=[
            out,
            out,
            jax.ShapeDtypeStruct((rows, width), BF16),
            jax.ShapeDtypeStruct((2, rows, width), BF16),
            jax.ShapeDtypeStruct((2, width // HEAD, rows), F32),
            jax.ShapeDtypeStruct((1, rows), F32),
        ],
        in_specs=[SMEM] + [VMEM] * 8,
        out_specs=[VMEM] * 6,
        compiler_params=params(),
        cost_estimate=cost(24 * slots * slots * width, 64 * slots * width),
        name="cross_grad",
    )(place, cross, kept, stats, local, heard, gates, near_dq, near_sum)


def far_grad_kernel(scale, place_ref, pair, kept, final, gates, keep, near_dq, near_own, near_sib, own_out, sib_out):
    slots, half = pair.shape[1] // 2, pair.shape[2]
    width = half // 2
    heads = width // HEAD
    early = jnp.where(place_ref[1] == 0, 1.0, 0.0)
    factor = final[0] * gates[...]
    own_out[0, :, :width] = near_dq[:slots]
    sib_out[0, :, :width] = near_dq[slots:]
    for i in range(2):
        own_out[1 + i, :, :width] = near_own[i]
        sib_out[1 + i, :, :width] = near_sib[i]
    for h in range(heads):
        cols = slice(width + h * HEAD, width + (h + 1) * HEAD)
        at = slice(h * HEAD, (h + 1) * HEAD)
        dq, dk, dv = gradients(
            pair[2, :, cols], pair[0, :, cols], pair[3, :, cols],
            kept[0, heads + h], kept[1, heads + h], scale, factor[h : h + 1], final[1, h : h + 1],
        )
        dk = dk + early * keep[0, :, at].astype(F32)
        dv = dv + early * keep[1, :, at].astype(F32)
        for i, part in enumerate((dq, dk, dv)):
            own_out[i, :, cols] = part[:slots].astype(BF16)
            sib_out[i, :, cols] = part[slots:].astype(BF16)


def far_grad(place, pair, kept, final, gates, keep, near_dq, near_own, near_sib):
    _, rows, half = pair.shape
    slots = rows // 2
    out = jax.ShapeDtypeStruct((3, slots, half), BF16)
    return pl.pallas_call(
        functools.partial(far_grad_kernel, HEAD**-0.5),
        out_shape=[out, out],
        in_specs=[SMEM] + [VMEM] * 8,
        out_specs=[VMEM] * 2,
        compiler_params=params(),
        cost_estimate=cost(20 * slots * slots * half, 40 * slots * half),
        name="far_grad",
    )(place, pair, kept, final, gates, keep, near_dq, near_own, near_sib)


def join_kernel(place_ref, own, sib, straight, diag, dq_out, dk_out, dv_out, low, back, total, in_sems, out_sems):
    slots, half = own.shape[1], own.shape[2]
    width = straight.shape[2]
    core, chip = place_ref[0], place_ref[1]
    early, late = jnp.where(chip == 0, 1.0, 0.0), jnp.where(chip == 0, 0.0, 1.0)
    ends = ((own, straight, core * half), (sib, diag, (1 - core) * half))
    loads = []
    for i, (part, extra, _) in enumerate(ends):
        extras = [pltpu.make_async_copy(extra.at[j], back.at[i, j], in_sems.at[5 * i + j]) for j in range(2)]
        parts = [pltpu.make_async_copy(part.at[j], low.at[i, j], in_sems.at[5 * i + 2 + j]) for j in range(3)]
        loads.append((parts, extras))
    for parts, extras in loads:
        for c in (parts[0], extras[0], parts[1], extras[1], parts[2]):
            c.start()
    stores = []
    for i, (_, _, start) in enumerate(ends):
        parts, extras = loads[i]
        for j, out in enumerate((dq_out, dk_out, dv_out)):
            parts[j].wait()
            if j < 2:
                extras[j].wait()
            at = total.at[i, j]
            first, second = low[i, j, :, :width].astype(F32), low[i, j, :, width:].astype(F32)
            if j == 0:
                at[:, :width] = first
                at[:, width:] = second + late * back[i, 0].astype(F32)
            else:
                at[:, :width] = first + early * back[i, j - 1].astype(F32)
                at[:, width:] = second
            cols = pl.ds(pl.multiple_of(start, HEAD), half)
            stores.append(pltpu.make_async_copy(at, out.at[0, :, cols], out_sems.at[3 * i + j]))
            stores[-1].start()
    for c in stores:
        c.wait()


def join(place, own, sib, straight, diag, shape):
    out = jax.ShapeDtypeStruct(shape, F32)
    _, slots, half = own.shape
    anywhere = pl.BlockSpec(memory_space=pl.ANY)
    hbm = pl.BlockSpec(memory_space=pltpu.HBM)
    return pl.pallas_call(
        join_kernel,
        out_shape=[out] * 3,
        in_specs=[SMEM] + [anywhere] * 4,
        out_specs=[hbm] * 3,
        scratch_shapes=[
            pltpu.VMEM((2, 3, slots, half), BF16),
            pltpu.VMEM((2, 2, slots, half // 2), BF16),
            pltpu.VMEM((2, 3, slots, half), F32),
            pltpu.SemaphoreType.DMA((10,)),
            pltpu.SemaphoreType.DMA((6,)),
        ],
        compiler_params=params(),
        cost_estimate=cost(0, 18 * out.size),
        name="join",
    )(place, own, sib, straight, diag)


def pair_router_kernel(gates_ref, sum_ref, x_ref, sib_ref, out_ref):
    gates = gates_ref[...]
    grad = sum_ref[...] * gates * (1.0 - gates)
    high = grad.astype(BF16)
    rest = grad - high.astype(F32)
    mid = rest.astype(BF16)
    low = (rest - mid.astype(F32)).astype(BF16)
    slots = x_ref.shape[1]
    row = lax.broadcasted_iota(jnp.int32, (8, grad.shape[1]), 0)
    lhs = jnp.where(row == 0, high.astype(F32), jnp.where(row == 1, mid.astype(F32), jnp.where(row == 2, low.astype(F32), 0.0)))
    lhs = lhs.astype(BF16)
    term = jnp.sum(nn(lhs[:, :slots], x_ref[0]) + nn(lhs[:, slots:], sib_ref[0]), axis=0, keepdims=True)
    parts, copies, _, chunk = out_ref.shape
    for j in range(parts):
        for i in range(copies):
            out_ref[j, i] = term[:, j * chunk : (j + 1) * chunk]


def pair_router(gates, sums, x_routed, x_sib, parts, copies):
    chunk = x_routed.shape[-1] // parts
    return pl.pallas_call(
        pair_router_kernel,
        out_shape=jax.ShapeDtypeStruct((parts, copies, 1, chunk), F32),
        in_specs=[VMEM] * 4,
        out_specs=VMEM,
        compiler_params=params(),
        cost_estimate=cost(32 * x_routed.size, x_routed.size * 4),
        name="router_terms",
    )(gates, sums, x_routed, x_sib)


def swap_body(route_pos, x_routed, w_router, queries, keys, values, d_gated):
    slots = queries.shape[1]
    n, ndp = lax.axis_size("ctx"), lax.axis_size("dp")
    me = lax.axis_index("ctx")
    place = jnp.stack([me % 2, me // 2, lax.axis_index("dp")]).astype(jnp.int32)

    def send(a, flip):
        return lax.ppermute(a, "ctx", [(i, i ^ flip) for i in range(n)])

    def beside(fn, *operands):
        def skip(*ops):
            return jax.tree.map(lambda o: jnp.zeros(o.shape, o.dtype), jax.eval_shape(fn, *ops))

        return lax.cond(route_pos[0, 0] >= -1, fn, skip, *operands)

    def after(value, *others):
        return lax.optimization_barrier((value, *others))[0]

    def near_dp(part, step):
        return lax.ppermute(part, "dp", [(i, i ^ step) for i in range(ndp)])

    def local_phase(place, route_pos, x_routed, w_part, theirs, keys, values, queries, d_gated):
        sib, x_sib = send(theirs, 1), send(x_routed, 1)
        results = ()
        step = 2
        while step < ndp:
            other = near_dp(w_part, step)
            if 2 * step == ndp:
                results = local_stats(place, route_pos, keys, values, queries, d_gated, sib)
                other = after(other, *results)
            w_part = jnp.concatenate([w_part, other], axis=1)
            step *= 2
        local, kept, live, pair = results or local_stats(place, route_pos, keys, values, queries, d_gated, sib)
        gates = pair_gate(place, live, x_routed, x_sib, w_part, ndp)
        return pair, x_sib, local, kept, gates

    def grad_phase(*operands):
        own_out, sib_out = far_grad(*operands)
        return own_out, send(sib_out, 1)

    def router_phase(gates, sums, x_routed, x_sib, place, *operands):
        terms = pair_router(gates, sums, x_routed, x_sib, ndp, n)
        chunk = terms.shape[-1]
        shared = lax.all_to_all(terms.reshape(ndp * n, 1, chunk), ("dp", "ctx"), 0, 0, tiled=True)
        own_out, sib_in = beside(grad_phase, after(place, terms), *operands)
        return own_out, sib_in, jnp.sum(shared, axis=0)[0] / float(ndp * n * slots // 2)

    w_part = w_router.reshape(1, -1).astype(F32)
    out_s, out_d = cross_pack(place, route_pos, keys, values, queries, d_gated)
    in_s, in_d = send(out_s, 2), send(out_d, 3)
    theirs = sib_pack(place, after(route_pos, out_s), keys, values, queries, d_gated)
    if ndp > 1:
        w_part = jnp.concatenate([w_part, after(near_dp(w_part, 1), theirs)], axis=1)
    pair, x_sib, local, kept, gates = beside(
        local_phase, place, route_pos, x_routed, w_part, theirs, keys, values, queries, d_gated
    )
    cross, stats, kept_cross, message = cross_stats(place, pair, in_s, in_d, local, gates)
    heard = send(message, 2)
    near_dq, near_own, near_sib, near_sum = near_grad(place, pair, kept, local, stats, gates)
    back_s, back_d, dq_low, keep, final, sums = cross_grad(
        place, cross, kept_cross, stats, local, heard, gates, near_dq, near_sum
    )
    ret_s, ret_d = send(back_s, 2), send(back_d, 3)
    own_out, sib_in, router_grad = beside(
        router_phase, gates, sums, x_routed, x_sib, place, pair, kept, final, gates, keep, dq_low, near_own, near_sib
    )
    dq, dk, dv = join(place, own_out, sib_in, ret_s, ret_d, queries.shape)
    return dq, dk, dv, router_grad


def body(route_pos, x_routed, w_router, queries, keys, values, d_gated):
    slots, full = queries.shape[1], queries.shape[2]
    n, ndp = lax.axis_size("ctx"), lax.axis_size("dp")
    chips = n // 2
    me, dp_me = lax.axis_index("ctx"), lax.axis_index("dp")
    core = (me % 2).astype(jnp.int32).reshape(1)
    half = full // 2
    groups = GROUPS if (half // HEAD) % GROUPS == 0 else 1
    width = half // groups

    sib_pairs = [(i, i ^ 1) for i in range(n)]

    def forward_pairs(step, flip):
        return [(i, (i + 2 * step) ^ flip) for i in range(n) if i + 2 * step < n]

    def back_pairs(step, flip):
        return [(b, a) for a, b in forward_pairs(step, flip)]

    def to_sib(a):
        return lax.ppermute(a, "ctx", sib_pairs)

    links = [(step, flip) for step in range(1, chips) for flip in (0, 1)]

    w_row = w_router.reshape(1, -1)
    w_parts = [w_row] + [
        lax.ppermute(w_row, "dp", [(i, (i + s) % ndp) for i in range(ndp)]) for s in range(1, ndp)
    ]
    live = (route_pos >= 0).astype(jnp.int32)
    lives = [live, to_sib(live)] + [lax.ppermute(live, "ctx", forward_pairs(*link)) for link in links]
    live_all = jnp.concatenate(lives, axis=0)

    kv_mine, kv_theirs = pack(core, keys, values, groups, width)
    kv_far = [
        [lax.ppermute((kv_theirs if flip else kv_mine)[g], "ctx", forward_pairs(step, flip)) for step, flip in links]
        for g in range(groups)
    ]
    q_mine, q_theirs = pack(core, queries, d_gated, groups, width)
    kv_sib = [to_sib(a) for a in kv_theirs]
    q_sib = [to_sib(a) for a in q_theirs]

    offsets = ((dp_me - jnp.arange(ndp)) % ndp).astype(jnp.int32)
    gate = router_gate(offsets, route_pos, x_routed, w_parts)
    gates = (gate, to_sib(gate))

    accs = (jnp.zeros((1, slots), F32), jnp.zeros((1, slots), F32))
    dq_own, sib_in, kv_own, back = [], [], [], []
    for g in range(groups):
        dq, sib_out, kv_local, kv_remote, accs = attention(
            core, live_all, gates, accs, q_mine[g], q_sib[g], [kv_mine[g], kv_sib[g], *kv_far[g]]
        )
        back.append([lax.ppermute(a, "ctx", back_pairs(*link)) for a, link in zip(kv_remote, links)])
        sib_in.append(to_sib(sib_out))
        dq_own.append(dq)
        kv_own.append(kv_local)

    targets = ((dp_me + jnp.arange(ndp)) % ndp).astype(jnp.int32)
    terms = router_terms(targets, gate, accs[0], to_sib(accs[1]), x_routed, ndp)
    mine = terms[0]
    for s in range(1, ndp):
        mine = mine + lax.ppermute(terms[s], "dp", [(i, (i + s) % ndp) for i in range(ndp)])
    total = mine
    for s in range(1, n):
        total = total + lax.ppermute(mine, "ctx", [(i, (i + s) % n) for i in range(n)])
    router_grad = total[0] / float(ndp * n * slots // 2)

    dq, dk, dv = combine(core, dq_own, sib_in, kv_own, back, queries.shape)
    return dq, dk, dv, router_grad


def solution(mesh):
    placed = (
        P("dp", "ctx"),
        P("dp", "ctx", None),
        P("dp"),
        P("dp", "ctx", None),
        P("dp", "ctx", None),
        P("dp", "ctx", None),
        P("dp", "ctx", None),
    )
    ndp = mesh.shape["dp"]
    paired = mesh.shape["ctx"] == 4 and ndp & (ndp - 1) == 0
    return jax.shard_map(
        swap_body if paired else body,
        mesh=mesh,
        in_specs=placed,
        out_specs=(P("dp", "ctx", None), P("dp", "ctx", None), P("dp", "ctx", None), P("dp")),
        check_vma=False,
    )
```

```python
import functools

import jax
import jax.numpy as jnp
from jax import lax
from jax.experimental import pallas as pl
from jax.experimental.pallas import tpu as pltpu
from jax.sharding import PartitionSpec as P

HEAD = 128
GROUPS = 4
NEG_FILL = -1e30
MIB = 1024 * 1024
BF16 = jnp.bfloat16
F32 = jnp.float32

VMEM = pl.BlockSpec(memory_space=pltpu.VMEM)
SMEM = pl.BlockSpec(memory_space=pltpu.SMEM)


def params(mib=16):
    return pltpu.CompilerParams(vmem_limit_bytes=mib * MIB)


def cost(flops, nbytes, exps=0):
    return pl.CostEstimate(flops=1, bytes_accessed=1, transcendentals=0)


def in_hbm(*arrays):
    return [pltpu.with_memory_space_constraint(a, pltpu.HBM) for a in arrays]


def nt(a, b):
    return lax.dot_general(a, b, (((1,), (1,)), ((), ())), preferred_element_type=F32)


def nn(a, b):
    return lax.dot_general(a, b, (((1,), (0,)), ((), ())), preferred_element_type=F32)


def tn(a, b):
    return lax.dot_general(a, b, (((0,), (0,)), ((), ())), preferred_element_type=F32)


def pack_kernel(groups, width, core_ref, first_ref, second_ref, *outs):
    half = first_ref.shape[-1] // 2
    core = core_ref[0]
    for side in range(2):
        base = (core if side == 0 else 1 - core) * half
        for g in range(groups):
            out = outs[side * groups + g]
            cols = pl.ds(pl.multiple_of(base + g * width, HEAD), width)
            out[0] = first_ref[0, :, cols].astype(BF16)
            out[1] = second_ref[0, :, cols].astype(BF16)


def pack(core, first, second, groups, width):
    slots = first.shape[1]
    out = jax.ShapeDtypeStruct((2, slots, width), BF16)
    res = pl.pallas_call(
        functools.partial(pack_kernel, groups, width),
        out_shape=[out] * (2 * groups),
        in_specs=[SMEM, VMEM, VMEM],
        out_specs=[VMEM] * (2 * groups),
        compiler_params=params(),
        cost_estimate=cost(0, 2 * first.size * 4),
        name="pack",
    )(core, first, second)
    return res[:groups], res[groups:]


def gate_kernel(parts, offset_ref, pos_ref, x_ref, *refs):
    w_refs, out_ref = refs[:parts], refs[parts]
    chunk = w_refs[0].shape[-1]
    total = jnp.zeros((8, x_ref.shape[1]), F32)
    for s in range(parts):
        cols = pl.ds(pl.multiple_of(offset_ref[s] * chunk, HEAD), chunk)
        w_rows = jnp.broadcast_to(w_refs[s][...].astype(F32), (8, chunk)).astype(BF16)
        total = total + nt(w_rows, x_ref[0, :, cols])
    gate = 1.0 / (1.0 + jnp.exp(-total[0:1]))
    out_ref[...] = jnp.where(pos_ref[...] >= 0, gate, 0.0)


def router_gate(offsets, route_pos, x_routed, w_parts):
    parts = len(w_parts)
    return pl.pallas_call(
        functools.partial(gate_kernel, parts),
        out_shape=jax.ShapeDtypeStruct(route_pos.shape, F32),
        in_specs=[SMEM] + [VMEM] * (2 + parts),
        out_specs=VMEM,
        compiler_params=params(),
        cost_estimate=cost(16 * x_routed.size, x_routed.size * 2),
        name="router_gate",
    )(offsets, route_pos, x_routed, *w_parts)


def attention_kernel(remote, scale, core_ref, live_ref, gate_own, gate_sib, acc_own, acc_sib, q_own, q_sib, *refs):
    chunks = 2 + remote
    kv = refs[:chunks]
    outs = refs[chunks:]
    dq_own, sib_out, kv_own = outs[:3]
    kv_remote = outs[3 : 3 + remote]
    sum_own, sum_sib = outs[3 + remote :]
    slots, width = q_own.shape[1], q_own.shape[2]
    core = core_ref[0]
    key = lax.broadcasted_iota(jnp.int32, (slots, slots), 0)
    query = lax.broadcasted_iota(jnp.int32, (slots, slots), 1)
    counts = [jnp.sum(live_ref[i : i + 1], axis=1, keepdims=True) for i in range(chunks)]
    lives = [key < counts[i] for i in range(chunks)]
    own_later = core == 1
    bias_rows = []
    for i in range(chunks):
        live = lives[i]
        if i == 0:
            pair = (live & (key <= query), live & jnp.logical_not(own_later))
        elif i == 1:
            pair = (live & own_later, live & (key <= query))
        else:
            pair = (live, live)
        bias_rows.append(jnp.concatenate([jnp.where(p, 0.0, NEG_FILL) for p in pair], axis=1))
    bias = jnp.concatenate(bias_rows, axis=0)
    gates = jnp.concatenate([gate_own[...], gate_sib[...]], axis=1)
    total = jnp.zeros((1, 2 * slots), F32)
    for h in range(width // HEAD):
        cols = slice(h * HEAD, (h + 1) * HEAD)
        q = jnp.concatenate([q_own[0, :, cols], q_sib[0, :, cols]], axis=0)
        dg = jnp.concatenate([q_own[1, :, cols], q_sib[1, :, cols]], axis=0)
        k = jnp.concatenate([r[0, :, cols] for r in kv], axis=0)
        v = jnp.concatenate([r[1, :, cols] for r in kv], axis=0)
        scores = nt(k, q) * scale + bias
        top = jnp.max(scores, axis=0, keepdims=True)
        e = jnp.exp(scores - top)
        inverse = 1.0 / jnp.sum(e, axis=0, keepdims=True)
        gw = nt(v, dg)
        delta = jnp.sum(e * gw, axis=0, keepdims=True) * inverse
        total = total + delta
        weights = e * (inverse * gates)
        dv = nn(weights.astype(BF16), dg)
        ds = (weights * ((gw - delta) * scale)).astype(BF16)
        dk = nn(ds, q)
        dq = tn(ds, k)
        dq_own[:, cols] = dq[:slots].astype(dq_own.dtype)
        sib_out[0, :, cols] = dq[slots:].astype(BF16)
        kv_own[0, :, cols] = dk[:slots].astype(BF16)
        kv_own[1, :, cols] = dv[:slots].astype(BF16)
        sib_out[1, :, cols] = dk[slots : 2 * slots].astype(BF16)
        sib_out[2, :, cols] = dv[slots : 2 * slots].astype(BF16)
        for i in range(remote):
            rows = slice((2 + i) * slots, (3 + i) * slots)
            kv_remote[i][0, :, cols] = dk[rows].astype(BF16)
            kv_remote[i][1, :, cols] = dv[rows].astype(BF16)
    sum_own[...] = acc_own[...] + total[:, :slots]
    sum_sib[...] = acc_sib[...] + total[:, slots:]


def attention(core, live, gates, accs, q_own, q_sib, kv):
    remote = len(kv) - 2
    _, slots, width = q_own.shape
    pair = jax.ShapeDtypeStruct((2, slots, width), BF16)
    row = jax.ShapeDtypeStruct((1, slots), F32)
    outs = [
        jax.ShapeDtypeStruct((slots, width), BF16),
        jax.ShapeDtypeStruct((3, slots, width), BF16),
        pair,
        *([pair] * remote),
        row,
        row,
    ]
    keys = (2 + remote) * slots
    res = pl.pallas_call(
        functools.partial(attention_kernel, remote, HEAD**-0.5),
        out_shape=outs,
        in_specs=[SMEM] + [VMEM] * (7 + len(kv)),
        out_specs=[VMEM] * len(outs),
        compiler_params=params(48),
        cost_estimate=cost(20 * slots * keys * width, 8 * keys * width + 20 * slots * width, 2 * slots * keys * width // HEAD),
        name="attention",
    )(core, live, *gates, *accs, q_own, q_sib, *kv)
    return res[0], res[1], res[2], res[3 : 3 + remote], (res[3 + remote], res[4 + remote])


def combine_kernel(groups, width, remote, core_ref, *refs):
    dq_own, sib, kv_own = refs[:groups], refs[groups : 2 * groups], refs[2 * groups : 3 * groups]
    back = refs[3 * groups : 3 * groups + groups * remote]
    dq_out, dk_out, dv_out = refs[3 * groups + groups * remote :]
    half = groups * width
    core = core_ref[0]
    for g in range(groups):
        own = pl.ds(pl.multiple_of(core * half + g * width, HEAD), width)
        other = pl.ds(pl.multiple_of((1 - core) * half + g * width, HEAD), width)
        dq_out[0, :, own] = dq_own[g][...].astype(F32)
        dq_out[0, :, other] = sib[g][0].astype(F32)
        for i, out in enumerate((dk_out, dv_out)):
            mine = kv_own[g][i].astype(F32)
            theirs = sib[g][1 + i].astype(F32)
            for r in range(remote):
                part = back[g * remote + r][i].astype(F32)
                if r % 2 == 0:
                    mine = mine + part
                else:
                    theirs = theirs + part
            out[0, :, own] = mine
            out[0, :, other] = theirs


def combine(core, dq_own, sib, kv_own, back, shape):
    groups = len(dq_own)
    remote = len(back[0])
    out = jax.ShapeDtypeStruct(shape, F32)
    flat = [*dq_own, *sib, *kv_own, *(b for group in back for b in group)]
    return pl.pallas_call(
        functools.partial(combine_kernel, groups, dq_own[0].shape[-1], remote),
        out_shape=[out] * 3,
        in_specs=[SMEM] + [VMEM] * len(flat),
        out_specs=[VMEM] * 3,
        compiler_params=params(48),
        cost_estimate=cost(0, 3 * out.size * 6),
        name="combine",
    )(core, *flat)


def router_kernel(parts, target_ref, gate_ref, own_ref, sib_ref, x_ref, *outs):
    gate = gate_ref[...]
    grad = (own_ref[...] + sib_ref[...]) * gate * (1.0 - gate)
    high = grad.astype(BF16)
    rest = grad - high.astype(F32)
    mid = rest.astype(BF16)
    low = (rest - mid.astype(F32)).astype(BF16)
    row = lax.broadcasted_iota(jnp.int32, (8, grad.shape[1]), 0)
    lhs = jnp.where(row == 0, high.astype(F32), jnp.where(row == 1, mid.astype(F32), jnp.where(row == 2, low.astype(F32), 0.0)))
    lhs = lhs.astype(BF16)
    chunk = outs[0].shape[-1]
    for s in range(parts):
        cols = pl.ds(pl.multiple_of(target_ref[s] * chunk, HEAD), chunk)
        outs[s][...] = jnp.sum(nn(lhs, x_ref[0, :, cols]), axis=0, keepdims=True)


def router_terms(targets, gate, own, sib, x_routed, parts):
    chunk = x_routed.shape[-1] // parts
    return pl.pallas_call(
        functools.partial(router_kernel, parts),
        out_shape=[jax.ShapeDtypeStruct((1, chunk), F32)] * parts,
        in_specs=[SMEM] + [VMEM] * 4,
        out_specs=[VMEM] * parts,
        compiler_params=params(),
        cost_estimate=cost(16 * x_routed.size, x_routed.size * 2),
        name="router_terms",
    )(targets, gate, own, sib, x_routed)


MARK = 2.0**60
MARK_LIMIT = 2.0**50


def live_rows(pos_ref, slots):
    count = jnp.sum((pos_ref[...] >= 0).astype(jnp.int32), axis=1, keepdims=True)
    return lax.broadcasted_iota(jnp.int32, (slots, HEAD), 0) < count


def mark_dead(keys, live):
    width = keys.shape[-1]
    mask = jnp.concatenate([live] * (width // HEAD), axis=1)
    return jnp.where(mask, keys.astype(F32), MARK).astype(BF16)


def cross_pack_kernel(place_ref, pos_ref, k_ref, v_ref, q_ref, dg_ref, straight, diag, wide, sems):
    slots, width = straight.shape[1], straight.shape[2]
    half = k_ref.shape[-1] // 2
    core, chip = place_ref[0], place_ref[1]
    ends = ((straight, core * half), (diag, (1 - core) * half))

    def copies(first, second, targets, offset):
        out = []
        for i, (end, start) in enumerate(ends):
            cols = pl.ds(pl.multiple_of(start + offset, HEAD), width)
            out.append(pltpu.make_async_copy(first.at[0, :, cols], end.at[0], sems.at[2 * i]))
            out.append(pltpu.make_async_copy(second.at[0, :, cols], targets[i], sems.at[2 * i + 1]))
        for c in out:
            c.start()
        for c in out:
            c.wait()

    @pl.when(chip == 0)
    def _():
        copies(k_ref, v_ref, (straight.at[1], diag.at[1]), 0)
        live = live_rows(pos_ref, slots)
        for end, _ in ends:
            end[0] = mark_dead(end[0], live)

    @pl.when(chip != 0)
    def _():
        copies(q_ref, dg_ref, (wide.at[0], wide.at[1]), width)
        for i, (end, _) in enumerate(ends):
            end[1] = wide[i].astype(BF16)


def cross_pack(place, route_pos, keys, values, queries, d_gated):
    _, slots, full = keys.shape
    cross = pltpu.VMEM((2, slots, full // 4), BF16)
    hbm = pl.BlockSpec(memory_space=pltpu.HBM)
    return pl.pallas_call(
        cross_pack_kernel,
        out_shape=[cross, cross],
        in_specs=[SMEM, VMEM, hbm, hbm, hbm, hbm],
        out_specs=[VMEM] * 2,
        scratch_shapes=[pltpu.VMEM((2, slots, full // 4), F32), pltpu.SemaphoreType.DMA((4,))],
        compiler_params=params(),
        cost_estimate=cost(0, 10 * slots * full),
        name="cross_pack",
    )(place, route_pos, *in_hbm(keys, values, queries, d_gated))


def sib_pack_kernel(place_ref, pos_ref, k_ref, v_ref, q_ref, dg_ref, out, wide, sems):
    slots, half = out.shape[1], out.shape[2]
    cols = pl.ds(pl.multiple_of((1 - place_ref[0]) * half, HEAD), half)
    sources = ((k_ref, out.at[0]), (dg_ref, wide), (v_ref, out.at[1]), (q_ref, out.at[2]))
    copies = [pltpu.make_async_copy(src.at[0, :, cols], dst, sems.at[i]) for i, (src, dst) in enumerate(sources)]
    for c in copies:
        c.start()
    live = live_rows(pos_ref, slots)
    copies[0].wait()
    out[0] = mark_dead(out[0], live)
    copies[1].wait()
    out[3] = wide[...].astype(BF16)
    copies[2].wait()
    copies[3].wait()


def sib_pack(place, route_pos, keys, values, queries, d_gated):
    _, slots, full = keys.shape
    hbm = pl.BlockSpec(memory_space=pltpu.HBM)
    return pl.pallas_call(
        sib_pack_kernel,
        out_shape=pltpu.VMEM((4, slots, full // 2), BF16),
        in_specs=[SMEM, VMEM, hbm, hbm, hbm, hbm],
        out_specs=VMEM,
        scratch_shapes=[pltpu.VMEM((slots, full // 2), F32), pltpu.SemaphoreType.DMA((4,))],
        compiler_params=params(),
        cost_estimate=cost(0, 20 * slots * full),
        name="sib_pack",
    )(place, route_pos, *in_hbm(keys, values, queries, d_gated))


def sib_chunks(sib_ref, held, sems):
    parts = sems.shape[0]
    chunk = held.shape[1] // parts
    copies = []
    for j in range(parts):
        cols = slice(j * chunk, (j + 1) * chunk)
        copies.append(pltpu.make_async_copy(sib_ref.at[0, :, cols], held.at[:, cols], sems.at[j]))
    for c in copies:
        c.start()
    return copies


def pair_gate_kernel(parts, place_ref, live_ref, x_ref, sib_ref, w_ref, out_ref, held, sems):
    chunk = w_ref.shape[1] // parts
    slots = x_ref.shape[1]
    copies = sib_chunks(sib_ref, held, sems)
    for i in range(2):
        total = jnp.zeros((8, slots), F32)
        if i == 1:
            for c in copies:
                c.wait()
        for j in range(parts):
            w_rows = jnp.broadcast_to(w_ref[:, j * chunk : (j + 1) * chunk], (8, chunk)).astype(BF16)
            cols = pl.ds(pl.multiple_of((place_ref[2] ^ j) * chunk, HEAD), chunk)
            total = total + nt(w_rows, x_ref[0, :, cols] if i == 0 else held[:, cols])
        lanes = slice(i * slots, (i + 1) * slots)
        out_ref[:, lanes] = live_ref[:, lanes] / (1.0 + jnp.exp(-total[0:1]))


def pair_gate(place, live, x_routed, x_sib, w_full, parts):
    _, slots, depth = x_routed.shape
    return pl.pallas_call(
        functools.partial(pair_gate_kernel, parts),
        out_shape=jax.ShapeDtypeStruct(live.shape, F32),
        in_specs=[SMEM, VMEM, VMEM, pl.BlockSpec(memory_space=pl.ANY), VMEM],
        out_specs=VMEM,
        scratch_shapes=[pltpu.VMEM((slots, depth), BF16), pltpu.SemaphoreType.DMA((4,))],
        compiler_params=params(),
        cost_estimate=cost(16 * x_routed.size, x_routed.size * 2),
        name="router_gate",
    )(place, live, x_routed, x_sib, w_full)


def local_mask(core, pair):
    slots = pair.shape[1] // 2
    key = lax.broadcasted_iota(jnp.int32, (slots, slots), 0)
    query = lax.broadcasted_iota(jnp.int32, (slots, slots), 1)
    causal = key <= query
    own_live = pair[0, :slots, :slots].astype(F32) < MARK_LIMIT
    sib_live = pair[0, slots:, :slots].astype(F32) < MARK_LIMIT
    own_rows = jnp.concatenate([own_live & causal, own_live & (core == 0)], axis=1)
    sib_rows = jnp.concatenate([sib_live & (core == 1), sib_live & causal], axis=1)
    return jnp.concatenate([own_rows, sib_rows], axis=0)


def kept_stats(scores, gw, kept, stats, h):
    top = jnp.max(scores, axis=0, keepdims=True)
    e = jnp.exp(scores - top).astype(BF16)
    gw = gw.astype(BF16)
    kept[0, h] = e
    kept[1, h] = gw
    e = e.astype(F32)
    stats[0, h : h + 1] = top
    stats[1, h : h + 1] = jnp.sum(e, axis=0, keepdims=True)
    stats[2, h : h + 1] = jnp.sum(e * gw.astype(F32), axis=0, keepdims=True)


def partial_stats(scores, gw, stats, h):
    top = jnp.max(scores, axis=0, keepdims=True)
    e = jnp.exp(scores - top)
    stats[0, h : h + 1] = top
    stats[1, h : h + 1] = jnp.sum(e, axis=0, keepdims=True)
    stats[2, h : h + 1] = jnp.sum(e * gw, axis=0, keepdims=True)


def local_stats_kernel(scale, place_ref, pos_ref, k_ref, v_ref, q_ref, dg_ref, sib, stats, live, pair, wide, sems):
    slots, half = sib.shape[1], sib.shape[2]
    width = half // 2
    core = place_ref[0]
    own, other = slice(0, slots), slice(slots, 2 * slots)
    stages = []
    for g in range(2):
        cols = slice(g * width, (g + 1) * width)
        held = pl.ds(pl.multiple_of(core * half + g * width, HEAD), width)
        copies = [
            pltpu.make_async_copy(ref.at[0, :, held], pair.at[j, own, cols], sems.at[8 * g + j])
            for j, ref in enumerate((k_ref, v_ref, q_ref))
        ]
        copies.append(pltpu.make_async_copy(dg_ref.at[0, :, held], wide.at[:, cols], sems.at[8 * g + 3]))
        for j in range(4):
            copies.append(pltpu.make_async_copy(sib.at[j, :, cols], pair.at[j, other, cols], sems.at[8 * g + 4 + j]))
        for c in copies:
            c.start()
        stages.append(copies)
    rows_live = live_rows(pos_ref, slots)
    mask = None
    for g in range(2):
        cols = slice(g * width, (g + 1) * width)
        for c in stages[g]:
            c.wait()
        pair[0, own, cols] = mark_dead(pair[0, own, cols], rows_live)
        pair[3, own, cols] = wide[:, cols].astype(BF16)
        if mask is None:
            mask = local_mask(core, pair)
            marks = nt(jnp.ones((8, HEAD), BF16), pair[0, :, :HEAD])[0:1]
            live[...] = jnp.where(marks < MARK_LIMIT, 1.0, 0.0)
        for h in range(g * width // HEAD, (g + 1) * width // HEAD):
            at = slice(h * HEAD, (h + 1) * HEAD)
            scores = jnp.where(mask, nt(pair[0, :, at], pair[2, :, at]) * scale, NEG_FILL)
            partial_stats(scores, nt(pair[1, :, at], pair[3, :, at]), stats, h)


def local_stats(place, route_pos, keys, values, queries, d_gated, sib):
    _, slots, half = sib.shape
    heads = half // HEAD
    anywhere = pl.BlockSpec(memory_space=pl.ANY)
    return pl.pallas_call(
        functools.partial(local_stats_kernel, HEAD**-0.5),
        out_shape=[
            jax.ShapeDtypeStruct((3, heads, 2 * slots), F32),
            jax.ShapeDtypeStruct((1, 2 * slots), F32),
            jax.ShapeDtypeStruct((4, 2 * slots, half), BF16),
        ],
        in_specs=[SMEM, VMEM] + [anywhere] * 5,
        out_specs=[VMEM] * 3,
        scratch_shapes=[pltpu.VMEM((slots, half), F32), pltpu.SemaphoreType.DMA((16,))],
        compiler_params=params(),
        cost_estimate=cost(16 * slots * slots * half, 16 * slots * half, 4 * slots * slots * half // HEAD),
        name="local_stats",
    )(place, route_pos, *in_hbm(keys, values, queries, d_gated), sib)


def cross_stats_kernel(scale, place_ref, pair, straight, diag, local, gates, cross, stats, kept, message):
    slots, width = straight.shape[1], straight.shape[2]
    chip = place_ref[1]
    top, bottom = slice(0, slots), slice(slots, 2 * slots)

    @pl.when(chip == 0)
    def _():
        cols = slice(width, 2 * width)
        for part in range(2):
            cross[part] = pair[part, :, cols]
            cross[2 + part, top] = straight[part]
            cross[2 + part, bottom] = diag[part]

    @pl.when(chip != 0)
    def _():
        cols = slice(0, width)
        for part in range(2):
            cross[part, top] = straight[part]
            cross[part, bottom] = diag[part]
            cross[2 + part] = pair[2 + part, :, cols]

    live = cross[0, :, :HEAD].astype(F32) < MARK_LIMIT
    mask = jnp.concatenate([live] * (2 * slots // HEAD), axis=1)
    heads = width // HEAD
    for h in range(heads):
        cols = slice(h * HEAD, (h + 1) * HEAD)
        scores = jnp.where(mask, nt(cross[0, :, cols], cross[2, :, cols]) * scale, NEG_FILL)
        kept_stats(scores, nt(cross[1, :, cols], cross[3, :, cols]), kept, stats, h)
    for i in range(3):
        message[i] = jnp.where(chip == 0, stats[i], local[i, heads:])
    message[3] = jnp.broadcast_to(gates[...], message.shape[1:])


def cross_stats(place, pair, straight, diag, local, gates):
    _, slots, width = straight.shape
    heads = width // HEAD
    return pl.pallas_call(
        functools.partial(cross_stats_kernel, HEAD**-0.5),
        out_shape=[
            jax.ShapeDtypeStruct((4, 2 * slots, width), BF16),
            jax.ShapeDtypeStruct((3, heads, 2 * slots), F32),
            jax.ShapeDtypeStruct((2, heads, 2 * slots, 2 * slots), BF16),
            jax.ShapeDtypeStruct((4, heads, 2 * slots), F32),
        ],
        in_specs=[SMEM] + [VMEM] * 5,
        out_specs=[VMEM] * 4,
        compiler_params=params(),
        cost_estimate=cost(16 * slots * slots * width, 32 * slots * width, 4 * slots * slots * heads),
        name="cross_stats",
    )(place, pair, straight, diag, local, gates)


NONE = (-3e38, 0.0, 0.0)


def merge(first, second):
    top = jnp.maximum(first[0], second[0])
    a, b = jnp.exp(first[0] - top), jnp.exp(second[0] - top)
    inverse = 1.0 / (first[1] * a + second[1] * b)
    return a * inverse, (first[2] * a + second[2] * b) * inverse


def choose(flag, yes, no):
    return [jnp.where(flag, y, n) for y, n in zip(yes, no)]


def gradients(q, k, dg, e, gw, scale, factor, delta):
    weights = e * factor
    ds = (weights * ((gw - delta) * scale)).astype(BF16)
    return tn(ds, k), nn(ds, q), nn(weights.astype(BF16), dg)


def local_gradients(pair, h, mask, scale, top, factor, delta):
    cols = slice(h * HEAD, (h + 1) * HEAD)
    k, v, q, dg = [pair[i, :, cols] for i in range(4)]
    e = jnp.exp(jnp.where(mask, nt(k, q) * scale, NEG_FILL) - top)
    return gradients(q, k, dg, e, nt(v, dg), scale, factor, delta)


def near_grad_kernel(scale, place_ref, pair, local, stats, gates, dq_out, own_out, sib_out, sum_out):
    slots, width = own_out.shape[1], own_out.shape[2]
    heads = width // HEAD
    first = place_ref[1] == 0
    near = [local[i, :heads] for i in range(3)]
    factor, delta = merge(near, choose(first, NONE, [stats[i] for i in range(3)]))
    factor = factor * gates[...]
    sum_out[...] = jnp.sum(delta, axis=0, keepdims=True)
    mask = local_mask(place_ref[0], pair)
    for h in range(heads):
        cols = slice(h * HEAD, (h + 1) * HEAD)
        row = slice(h, h + 1)
        dq, dk, dv = local_gradients(pair, h, mask, scale, near[0][row], factor[row], delta[row])
        dq_out[:, cols] = dq
        for i, part in enumerate((dk, dv)):
            own_out[i, :, cols] = part[:slots].astype(BF16)
            sib_out[i, :, cols] = part[slots:].astype(BF16)


def near_grad(place, pair, local, stats, gates):
    _, rows, half = pair.shape
    slots = rows // 2
    width = half // 2
    out = jax.ShapeDtypeStruct((2, slots, width), BF16)
    return pl.pallas_call(
        functools.partial(near_grad_kernel, HEAD**-0.5),
        out_shape=[jax.ShapeDtypeStruct((2 * slots, width), F32), out, out, jax.ShapeDtypeStruct(gates.shape, F32)],
        in_specs=[SMEM] + [VMEM] * 4,
        out_specs=[VMEM] * 4,
        compiler_params=params(),
        cost_estimate=cost(20 * slots * slots * half, 40 * slots * half),
        name="near_grad",
    )(place, pair, local, stats, gates)


def cross_grad_kernel(scale, place_ref, cross, kept, stats, local, heard, gates, near_dq, near_sum, straight, diag, dq_out, keep, final, sum_out):
    slots, width = straight.shape[1], straight.shape[2]
    heads = width // HEAD
    first = place_ref[1] == 0
    late = jnp.where(first, 0.0, 1.0)
    mine = [stats[i] for i in range(3)]
    other = [heard[i] for i in range(3)]
    near = [local[i, :heads] for i in range(3)]
    far = [local[i, heads:] for i in range(3)]
    factor, delta = merge(mine, choose(first, other, near))
    factor = factor * jnp.where(first, heard[3], jnp.broadcast_to(gates[...], factor.shape))
    final[0], final[1] = merge(far, choose(first, NONE, other))
    sum_out[...] = near_sum[...] + jnp.sum(final[1], axis=0, keepdims=True)
    for h in range(heads):
        cols = slice(h * HEAD, (h + 1) * HEAD)
        row = slice(h, h + 1)
        dq, dk, dv = gradients(
            cross[2, :, cols], cross[0, :, cols], cross[3, :, cols],
            kept[0, h].astype(F32), kept[1, h].astype(F32), scale, factor[row], delta[row],
        )
        dq_out[:, cols] = (near_dq[:, cols] + late * dq).astype(BF16)
        keep[0, :, cols] = dk.astype(BF16)
        keep[1, :, cols] = dv.astype(BF16)
        sent = jnp.where(first, dq, dk).astype(BF16)
        straight[0, :, cols] = sent[:slots]
        diag[0, :, cols] = sent[slots:]
        straight[1, :, cols] = dv[:slots].astype(BF16)
        diag[1, :, cols] = dv[slots:].astype(BF16)


def cross_grad(place, cross, kept, stats, local, heard, gates, near_dq, near_sum):
    _, rows, width = cross.shape
    slots = rows // 2
    out = jax.ShapeDtypeStruct((2, slots, width), BF16)
    return pl.pallas_call(
        functools.partial(cross_grad_kernel, HEAD**-0.5),
        out_shape=[
            out,
            out,
            pltpu.VMEM((rows, width), BF16),
            pltpu.VMEM((2, rows, width), BF16),
            jax.ShapeDtypeStruct((2, width // HEAD, rows), F32),
            jax.ShapeDtypeStruct((1, rows), F32),
        ],
        in_specs=[SMEM] + [VMEM] * 8,
        out_specs=[VMEM] * 6,
        compiler_params=params(),
        cost_estimate=cost(24 * slots * slots * width, 64 * slots * width),
        name="cross_grad",
    )(place, cross, kept, stats, local, heard, gates, near_dq, near_sum)


def far_grad_kernel(scale, place_ref, pair, local, final, gates, keep, near_dq, near_own, near_sib, own_out, sib_out):
    slots, half = pair.shape[1] // 2, pair.shape[2]
    width = half // 2
    heads = width // HEAD
    early = jnp.where(place_ref[1] == 0, 1.0, 0.0)
    factor = final[0] * gates[...]
    mask = local_mask(place_ref[0], pair)
    own_out[0, :, :width] = near_dq[:slots]
    sib_out[0, :, :width] = near_dq[slots:]
    for i in range(2):
        own_out[1 + i, :, :width] = near_own[i]
        sib_out[1 + i, :, :width] = near_sib[i]
    for h in range(heads):
        cols = slice(width + h * HEAD, width + (h + 1) * HEAD)
        at = slice(h * HEAD, (h + 1) * HEAD)
        row = slice(h, h + 1)
        top = local[0, heads + h : heads + h + 1]
        dq, dk, dv = local_gradients(pair, heads + h, mask, scale, top, factor[row], final[1, row])
        dk = dk + early * keep[0, :, at].astype(F32)
        dv = dv + early * keep[1, :, at].astype(F32)
        for i, part in enumerate((dq, dk, dv)):
            own_out[i, :, cols] = part[:slots].astype(BF16)
            sib_out[i, :, cols] = part[slots:].astype(BF16)


def far_grad(place, pair, local, final, gates, keep, near_dq, near_own, near_sib):
    _, rows, half = pair.shape
    slots = rows // 2
    out = jax.ShapeDtypeStruct((3, slots, half), BF16)
    return pl.pallas_call(
        functools.partial(far_grad_kernel, HEAD**-0.5),
        out_shape=[out, out],
        in_specs=[SMEM] + [VMEM] * 8,
        out_specs=[VMEM] * 2,
        compiler_params=params(),
        cost_estimate=cost(20 * slots * slots * half, 40 * slots * half),
        name="far_grad",
    )(place, pair, local, final, gates, keep, near_dq, near_own, near_sib)


def join_kernel(place_ref, own, sib, straight, diag, dq_out, dk_out, dv_out, low, back, total, in_sems, out_sems):
    slots, half = own.shape[1], own.shape[2]
    width = straight.shape[2]
    core, chip = place_ref[0], place_ref[1]
    early, late = jnp.where(chip == 0, 1.0, 0.0), jnp.where(chip == 0, 0.0, 1.0)
    ends = ((own, straight, core * half), (sib, diag, (1 - core) * half))
    loads = []
    for i, (part, extra, _) in enumerate(ends):
        extras = [pltpu.make_async_copy(extra.at[j], back.at[i, j], in_sems.at[5 * i + j]) for j in range(2)]
        parts = [pltpu.make_async_copy(part.at[j], low.at[i, j], in_sems.at[5 * i + 2 + j]) for j in range(3)]
        loads.append((parts, extras))
    for parts, extras in loads:
        for c in (parts[0], extras[0], parts[1], extras[1], parts[2]):
            c.start()
    stores = []
    for i, (_, _, start) in enumerate(ends):
        parts, extras = loads[i]
        for j, out in enumerate((dq_out, dk_out, dv_out)):
            parts[j].wait()
            if j < 2:
                extras[j].wait()
            at = total.at[i, j]
            first, second = low[i, j, :, :width].astype(F32), low[i, j, :, width:].astype(F32)
            if j == 0:
                at[:, :width] = first
                at[:, width:] = second + late * back[i, 0].astype(F32)
            else:
                at[:, :width] = first + early * back[i, j - 1].astype(F32)
                at[:, width:] = second
            cols = pl.ds(pl.multiple_of(start, HEAD), half)
            stores.append(pltpu.make_async_copy(at, out.at[0, :, cols], out_sems.at[3 * i + j]))
            stores[-1].start()
    for c in stores:
        c.wait()


def join(place, own, sib, straight, diag, shape):
    out = jax.ShapeDtypeStruct(shape, F32)
    _, slots, half = own.shape
    anywhere = pl.BlockSpec(memory_space=pl.ANY)
    hbm = pl.BlockSpec(memory_space=pltpu.HBM)
    return pl.pallas_call(
        join_kernel,
        out_shape=[out] * 3,
        in_specs=[SMEM] + [anywhere] * 4,
        out_specs=[hbm] * 3,
        scratch_shapes=[
            pltpu.VMEM((2, 3, slots, half), BF16),
            pltpu.VMEM((2, 2, slots, half // 2), BF16),
            pltpu.VMEM((2, 3, slots, half), F32),
            pltpu.SemaphoreType.DMA((10,)),
            pltpu.SemaphoreType.DMA((6,)),
        ],
        compiler_params=params(),
        cost_estimate=cost(0, 18 * out.size),
        name="join",
    )(place, own, sib, straight, diag)


def pair_router_kernel(gates_ref, sum_ref, x_ref, sib_ref, out_ref, held, sems):
    arriving = sib_chunks(sib_ref, held, sems)
    gates = gates_ref[...]
    grad = sum_ref[...] * gates * (1.0 - gates)
    high = grad.astype(BF16)
    rest = grad - high.astype(F32)
    mid = rest.astype(BF16)
    low = (rest - mid.astype(F32)).astype(BF16)
    slots = x_ref.shape[1]
    row = lax.broadcasted_iota(jnp.int32, (8, grad.shape[1]), 0)
    lhs = jnp.where(row == 0, high.astype(F32), jnp.where(row == 1, mid.astype(F32), jnp.where(row == 2, low.astype(F32), 0.0)))
    lhs = lhs.astype(BF16)
    near = nn(lhs[:, :slots], x_ref[0])
    parts, copies, _, chunk = out_ref.shape
    for c in arriving:
        c.wait()
    term = jnp.sum(near + nn(lhs[:, slots:], held[...]), axis=0, keepdims=True)
    for j in range(parts):
        for i in range(copies):
            out_ref[j, i] = term[:, j * chunk : (j + 1) * chunk]


def pair_router(gates, sums, x_routed, x_sib, parts, copies):
    chunk = x_routed.shape[-1] // parts
    return pl.pallas_call(
        pair_router_kernel,
        out_shape=jax.ShapeDtypeStruct((parts, copies, 1, chunk), F32),
        in_specs=[VMEM] * 3 + [pl.BlockSpec(memory_space=pl.ANY)],
        out_specs=VMEM,
        scratch_shapes=[pltpu.VMEM(x_routed.shape[1:], BF16), pltpu.SemaphoreType.DMA((4,))],
        compiler_params=params(),
        cost_estimate=cost(32 * x_routed.size, x_routed.size * 4),
        name="router_terms",
    )(gates, sums, x_routed, x_sib)


def swap_body(route_pos, x_routed, w_router, queries, keys, values, d_gated):
    slots = queries.shape[1]
    n, ndp = lax.axis_size("ctx"), lax.axis_size("dp")
    me = lax.axis_index("ctx")
    place = jnp.stack([me % 2, me // 2, lax.axis_index("dp")]).astype(jnp.int32)

    def send(a, flip):
        return lax.ppermute(a, "ctx", [(i, i ^ flip) for i in range(n)])

    def beside(fn, *operands):
        def skip(*ops):
            return jax.tree.map(lambda o: jnp.zeros(o.shape, o.dtype), jax.eval_shape(fn, *ops))

        return lax.cond(route_pos[0, 0] >= -1, fn, skip, *operands)

    def after(value, *others):
        return lax.optimization_barrier((value, *others))[0]

    def near_dp(part, step):
        return lax.ppermute(part, "dp", [(i, i ^ step) for i in range(ndp)])

    def local_phase(place, route_pos, x_routed, w_part, theirs, keys, values, queries, d_gated):
        sib, x_sib = send(theirs, 1), send(x_routed, 1)
        results = ()
        step = 2
        while step < ndp:
            other = near_dp(w_part, step)
            if 2 * step == ndp:
                results = local_stats(place, route_pos, keys, values, queries, d_gated, sib)
                other = after(other, *results)
            w_part = jnp.concatenate([w_part, other], axis=1)
            step *= 2
        local, live, pair = results or local_stats(place, route_pos, keys, values, queries, d_gated, sib)
        gates = pair_gate(place, live, x_routed, x_sib, w_part, ndp)
        return pair, x_sib, local, gates

    def grad_phase(*operands):
        own_out, sib_out = far_grad(*operands)
        return own_out, send(sib_out, 1)

    def router_phase(gates, sums, x_routed, x_sib, place, *operands):
        terms = pair_router(gates, sums, x_routed, x_sib, ndp, n)
        chunk = terms.shape[-1]
        shared = lax.all_to_all(terms.reshape(ndp * n, 1, chunk), ("dp", "ctx"), 0, 0, tiled=True)
        own_out, sib_in = beside(grad_phase, after(place, terms), *operands)
        return own_out, sib_in, jnp.sum(shared, axis=0)[0] / float(ndp * n * slots // 2)

    w_part = w_router.reshape(1, -1).astype(F32)
    out_s, out_d = cross_pack(place, route_pos, keys, values, queries, d_gated)
    in_s, in_d = send(out_s, 2), send(out_d, 3)
    theirs = sib_pack(place, after(route_pos, out_s), keys, values, queries, d_gated)
    if ndp > 1:
        w_part = jnp.concatenate([w_part, after(near_dp(w_part, 1), theirs)], axis=1)
    pair, x_sib, local, gates = beside(
        local_phase, place, route_pos, x_routed, w_part, theirs, keys, values, queries, d_gated
    )
    cross, stats, kept_cross, message = cross_stats(place, pair, in_s, in_d, local, gates)
    heard = send(message, 2)
    near_dq, near_own, near_sib, near_sum = near_grad(place, pair, local, stats, gates)
    back_s, back_d, dq_low, keep, final, sums = cross_grad(
        place, cross, kept_cross, stats, local, heard, gates, near_dq, near_sum
    )
    ret_s, ret_d = send(back_s, 2), send(back_d, 3)
    own_out, sib_in, router_grad = beside(
        router_phase, gates, sums, x_routed, x_sib, place, pair, local, final, gates, keep, dq_low, near_own, near_sib
    )
    dq, dk, dv = join(place, own_out, sib_in, ret_s, ret_d, queries.shape)
    return dq, dk, dv, router_grad


def body(route_pos, x_routed, w_router, queries, keys, values, d_gated):
    slots, full = queries.shape[1], queries.shape[2]
    n, ndp = lax.axis_size("ctx"), lax.axis_size("dp")
    chips = n // 2
    me, dp_me = lax.axis_index("ctx"), lax.axis_index("dp")
    core = (me % 2).astype(jnp.int32).reshape(1)
    half = full // 2
    groups = GROUPS if (half // HEAD) % GROUPS == 0 else 1
    width = half // groups

    sib_pairs = [(i, i ^ 1) for i in range(n)]

    def forward_pairs(step, flip):
        return [(i, (i + 2 * step) ^ flip) for i in range(n) if i + 2 * step < n]

    def back_pairs(step, flip):
        return [(b, a) for a, b in forward_pairs(step, flip)]

    def to_sib(a):
        return lax.ppermute(a, "ctx", sib_pairs)

    links = [(step, flip) for step in range(1, chips) for flip in (0, 1)]

    w_row = w_router.reshape(1, -1)
    w_parts = [w_row] + [
        lax.ppermute(w_row, "dp", [(i, (i + s) % ndp) for i in range(ndp)]) for s in range(1, ndp)
    ]
    live = (route_pos >= 0).astype(jnp.int32)
    lives = [live, to_sib(live)] + [lax.ppermute(live, "ctx", forward_pairs(*link)) for link in links]
    live_all = jnp.concatenate(lives, axis=0)

    kv_mine, kv_theirs = pack(core, keys, values, groups, width)
    kv_far = [
        [lax.ppermute((kv_theirs if flip else kv_mine)[g], "ctx", forward_pairs(step, flip)) for step, flip in links]
        for g in range(groups)
    ]
    q_mine, q_theirs = pack(core, queries, d_gated, groups, width)
    kv_sib = [to_sib(a) for a in kv_theirs]
    q_sib = [to_sib(a) for a in q_theirs]

    offsets = ((dp_me - jnp.arange(ndp)) % ndp).astype(jnp.int32)
    gate = router_gate(offsets, route_pos, x_routed, w_parts)
    gates = (gate, to_sib(gate))

    accs = (jnp.zeros((1, slots), F32), jnp.zeros((1, slots), F32))
    dq_own, sib_in, kv_own, back = [], [], [], []
    for g in range(groups):
        dq, sib_out, kv_local, kv_remote, accs = attention(
            core, live_all, gates, accs, q_mine[g], q_sib[g], [kv_mine[g], kv_sib[g], *kv_far[g]]
        )
        back.append([lax.ppermute(a, "ctx", back_pairs(*link)) for a, link in zip(kv_remote, links)])
        sib_in.append(to_sib(sib_out))
        dq_own.append(dq)
        kv_own.append(kv_local)

    targets = ((dp_me + jnp.arange(ndp)) % ndp).astype(jnp.int32)
    terms = router_terms(targets, gate, accs[0], to_sib(accs[1]), x_routed, ndp)
    mine = terms[0]
    for s in range(1, ndp):
        mine = mine + lax.ppermute(terms[s], "dp", [(i, (i + s) % ndp) for i in range(ndp)])
    total = mine
    for s in range(1, n):
        total = total + lax.ppermute(mine, "ctx", [(i, (i + s) % n) for i in range(n)])
    router_grad = total[0] / float(ndp * n * slots // 2)

    dq, dk, dv = combine(core, dq_own, sib_in, kv_own, back, queries.shape)
    return dq, dk, dv, router_grad


def solution(mesh):
    placed = (
        P("dp", "ctx"),
        P("dp", "ctx", None),
        P("dp"),
        P("dp", "ctx", None),
        P("dp", "ctx", None),
        P("dp", "ctx", None),
        P("dp", "ctx", None),
    )
    ndp = mesh.shape["dp"]
    paired = mesh.shape["ctx"] == 4 and ndp & (ndp - 1) == 0
    return jax.shard_map(
        swap_body if paired else body,
        mesh=mesh,
        in_specs=placed,
        out_specs=(P("dp", "ctx", None), P("dp", "ctx", None), P("dp", "ctx", None), P("dp")),
        check_vma=False,
    )
```

```python
import functools

import jax
import jax.numpy as jnp
from jax import lax
from jax.experimental import pallas as pl
from jax.experimental.pallas import tpu as pltpu
from jax.sharding import PartitionSpec as P

HEAD = 128
GROUPS = 4
NEG_FILL = -1e30
MIB = 1024 * 1024
BF16 = jnp.bfloat16
F32 = jnp.float32

VMEM = pl.BlockSpec(memory_space=pltpu.VMEM)
SMEM = pl.BlockSpec(memory_space=pltpu.SMEM)


def params(mib=16):
    return pltpu.CompilerParams(vmem_limit_bytes=mib * MIB)


def cost(flops, nbytes, exps=0):
    return pl.CostEstimate(flops=1, bytes_accessed=1, transcendentals=0)


def in_hbm(*arrays):
    return [pltpu.with_memory_space_constraint(a, pltpu.HBM) for a in arrays]


def nt(a, b):
    return lax.dot_general(a, b, (((1,), (1,)), ((), ())), preferred_element_type=F32)


def nn(a, b):
    return lax.dot_general(a, b, (((1,), (0,)), ((), ())), preferred_element_type=F32)


def tn(a, b):
    return lax.dot_general(a, b, (((0,), (0,)), ((), ())), preferred_element_type=F32)


def pack_kernel(groups, width, core_ref, first_ref, second_ref, *outs):
    half = first_ref.shape[-1] // 2
    core = core_ref[0]
    for side in range(2):
        base = (core if side == 0 else 1 - core) * half
        for g in range(groups):
            out = outs[side * groups + g]
            cols = pl.ds(pl.multiple_of(base + g * width, HEAD), width)
            out[0] = first_ref[0, :, cols].astype(BF16)
            out[1] = second_ref[0, :, cols].astype(BF16)


def pack(core, first, second, groups, width):
    slots = first.shape[1]
    out = jax.ShapeDtypeStruct((2, slots, width), BF16)
    res = pl.pallas_call(
        functools.partial(pack_kernel, groups, width),
        out_shape=[out] * (2 * groups),
        in_specs=[SMEM, VMEM, VMEM],
        out_specs=[VMEM] * (2 * groups),
        compiler_params=params(),
        cost_estimate=cost(0, 2 * first.size * 4),
        name="pack",
    )(core, first, second)
    return res[:groups], res[groups:]


def gate_kernel(parts, offset_ref, pos_ref, x_ref, *refs):
    w_refs, out_ref = refs[:parts], refs[parts]
    chunk = w_refs[0].shape[-1]
    total = jnp.zeros((8, x_ref.shape[1]), F32)
    for s in range(parts):
        cols = pl.ds(pl.multiple_of(offset_ref[s] * chunk, HEAD), chunk)
        w_rows = jnp.broadcast_to(w_refs[s][...].astype(F32), (8, chunk)).astype(BF16)
        total = total + nt(w_rows, x_ref[0, :, cols])
    gate = 1.0 / (1.0 + jnp.exp(-total[0:1]))
    out_ref[...] = jnp.where(pos_ref[...] >= 0, gate, 0.0)


def router_gate(offsets, route_pos, x_routed, w_parts):
    parts = len(w_parts)
    return pl.pallas_call(
        functools.partial(gate_kernel, parts),
        out_shape=jax.ShapeDtypeStruct(route_pos.shape, F32),
        in_specs=[SMEM] + [VMEM] * (2 + parts),
        out_specs=VMEM,
        compiler_params=params(),
        cost_estimate=cost(16 * x_routed.size, x_routed.size * 2),
        name="router_gate",
    )(offsets, route_pos, x_routed, *w_parts)


def attention_kernel(remote, scale, core_ref, live_ref, gate_own, gate_sib, acc_own, acc_sib, q_own, q_sib, *refs):
    chunks = 2 + remote
    kv = refs[:chunks]
    outs = refs[chunks:]
    dq_own, sib_out, kv_own = outs[:3]
    kv_remote = outs[3 : 3 + remote]
    sum_own, sum_sib = outs[3 + remote :]
    slots, width = q_own.shape[1], q_own.shape[2]
    core = core_ref[0]
    key = lax.broadcasted_iota(jnp.int32, (slots, slots), 0)
    query = lax.broadcasted_iota(jnp.int32, (slots, slots), 1)
    counts = [jnp.sum(live_ref[i : i + 1], axis=1, keepdims=True) for i in range(chunks)]
    lives = [key < counts[i] for i in range(chunks)]
    own_later = core == 1
    bias_rows = []
    for i in range(chunks):
        live = lives[i]
        if i == 0:
            pair = (live & (key <= query), live & jnp.logical_not(own_later))
        elif i == 1:
            pair = (live & own_later, live & (key <= query))
        else:
            pair = (live, live)
        bias_rows.append(jnp.concatenate([jnp.where(p, 0.0, NEG_FILL) for p in pair], axis=1))
    bias = jnp.concatenate(bias_rows, axis=0)
    gates = jnp.concatenate([gate_own[...], gate_sib[...]], axis=1)
    total = jnp.zeros((1, 2 * slots), F32)
    for h in range(width // HEAD):
        cols = slice(h * HEAD, (h + 1) * HEAD)
        q = jnp.concatenate([q_own[0, :, cols], q_sib[0, :, cols]], axis=0)
        dg = jnp.concatenate([q_own[1, :, cols], q_sib[1, :, cols]], axis=0)
        k = jnp.concatenate([r[0, :, cols] for r in kv], axis=0)
        v = jnp.concatenate([r[1, :, cols] for r in kv], axis=0)
        scores = nt(k, q) * scale + bias
        top = jnp.max(scores, axis=0, keepdims=True)
        e = jnp.exp(scores - top)
        inverse = 1.0 / jnp.sum(e, axis=0, keepdims=True)
        gw = nt(v, dg)
        delta = jnp.sum(e * gw, axis=0, keepdims=True) * inverse
        total = total + delta
        weights = e * (inverse * gates)
        dv = nn(weights.astype(BF16), dg)
        ds = (weights * ((gw - delta) * scale)).astype(BF16)
        dk = nn(ds, q)
        dq = tn(ds, k)
        dq_own[:, cols] = dq[:slots].astype(dq_own.dtype)
        sib_out[0, :, cols] = dq[slots:].astype(BF16)
        kv_own[0, :, cols] = dk[:slots].astype(BF16)
        kv_own[1, :, cols] = dv[:slots].astype(BF16)
        sib_out[1, :, cols] = dk[slots : 2 * slots].astype(BF16)
        sib_out[2, :, cols] = dv[slots : 2 * slots].astype(BF16)
        for i in range(remote):
            rows = slice((2 + i) * slots, (3 + i) * slots)
            kv_remote[i][0, :, cols] = dk[rows].astype(BF16)
            kv_remote[i][1, :, cols] = dv[rows].astype(BF16)
    sum_own[...] = acc_own[...] + total[:, :slots]
    sum_sib[...] = acc_sib[...] + total[:, slots:]


def attention(core, live, gates, accs, q_own, q_sib, kv):
    remote = len(kv) - 2
    _, slots, width = q_own.shape
    pair = jax.ShapeDtypeStruct((2, slots, width), BF16)
    row = jax.ShapeDtypeStruct((1, slots), F32)
    outs = [
        jax.ShapeDtypeStruct((slots, width), BF16),
        jax.ShapeDtypeStruct((3, slots, width), BF16),
        pair,
        *([pair] * remote),
        row,
        row,
    ]
    keys = (2 + remote) * slots
    res = pl.pallas_call(
        functools.partial(attention_kernel, remote, HEAD**-0.5),
        out_shape=outs,
        in_specs=[SMEM] + [VMEM] * (7 + len(kv)),
        out_specs=[VMEM] * len(outs),
        compiler_params=params(48),
        cost_estimate=cost(20 * slots * keys * width, 8 * keys * width + 20 * slots * width, 2 * slots * keys * width // HEAD),
        name="attention",
    )(core, live, *gates, *accs, q_own, q_sib, *kv)
    return res[0], res[1], res[2], res[3 : 3 + remote], (res[3 + remote], res[4 + remote])


def combine_kernel(groups, width, remote, core_ref, *refs):
    dq_own, sib, kv_own = refs[:groups], refs[groups : 2 * groups], refs[2 * groups : 3 * groups]
    back = refs[3 * groups : 3 * groups + groups * remote]
    dq_out, dk_out, dv_out = refs[3 * groups + groups * remote :]
    half = groups * width
    core = core_ref[0]
    for g in range(groups):
        own = pl.ds(pl.multiple_of(core * half + g * width, HEAD), width)
        other = pl.ds(pl.multiple_of((1 - core) * half + g * width, HEAD), width)
        dq_out[0, :, own] = dq_own[g][...].astype(F32)
        dq_out[0, :, other] = sib[g][0].astype(F32)
        for i, out in enumerate((dk_out, dv_out)):
            mine = kv_own[g][i].astype(F32)
            theirs = sib[g][1 + i].astype(F32)
            for r in range(remote):
                part = back[g * remote + r][i].astype(F32)
                if r % 2 == 0:
                    mine = mine + part
                else:
                    theirs = theirs + part
            out[0, :, own] = mine
            out[0, :, other] = theirs


def combine(core, dq_own, sib, kv_own, back, shape):
    groups = len(dq_own)
    remote = len(back[0])
    out = jax.ShapeDtypeStruct(shape, F32)
    flat = [*dq_own, *sib, *kv_own, *(b for group in back for b in group)]
    return pl.pallas_call(
        functools.partial(combine_kernel, groups, dq_own[0].shape[-1], remote),
        out_shape=[out] * 3,
        in_specs=[SMEM] + [VMEM] * len(flat),
        out_specs=[VMEM] * 3,
        compiler_params=params(48),
        cost_estimate=cost(0, 3 * out.size * 6),
        name="combine",
    )(core, *flat)


def router_kernel(parts, target_ref, gate_ref, own_ref, sib_ref, x_ref, *outs):
    gate = gate_ref[...]
    grad = (own_ref[...] + sib_ref[...]) * gate * (1.0 - gate)
    high = grad.astype(BF16)
    rest = grad - high.astype(F32)
    mid = rest.astype(BF16)
    low = (rest - mid.astype(F32)).astype(BF16)
    row = lax.broadcasted_iota(jnp.int32, (8, grad.shape[1]), 0)
    lhs = jnp.where(row == 0, high.astype(F32), jnp.where(row == 1, mid.astype(F32), jnp.where(row == 2, low.astype(F32), 0.0)))
    lhs = lhs.astype(BF16)
    chunk = outs[0].shape[-1]
    for s in range(parts):
        cols = pl.ds(pl.multiple_of(target_ref[s] * chunk, HEAD), chunk)
        outs[s][...] = jnp.sum(nn(lhs, x_ref[0, :, cols]), axis=0, keepdims=True)


def router_terms(targets, gate, own, sib, x_routed, parts):
    chunk = x_routed.shape[-1] // parts
    return pl.pallas_call(
        functools.partial(router_kernel, parts),
        out_shape=[jax.ShapeDtypeStruct((1, chunk), F32)] * parts,
        in_specs=[SMEM] + [VMEM] * 4,
        out_specs=[VMEM] * parts,
        compiler_params=params(),
        cost_estimate=cost(16 * x_routed.size, x_routed.size * 2),
        name="router_terms",
    )(targets, gate, own, sib, x_routed)


MARK = 2.0**60
MARK_LIMIT = 2.0**50


def live_rows(pos_ref, slots):
    count = jnp.sum((pos_ref[...] >= 0).astype(jnp.int32), axis=1, keepdims=True)
    return lax.broadcasted_iota(jnp.int32, (slots, HEAD), 0) < count


def mark_dead(keys, live):
    width = keys.shape[-1]
    mask = jnp.concatenate([live] * (width // HEAD), axis=1)
    return jnp.where(mask, keys.astype(F32), MARK).astype(BF16)


def cross_pack_kernel(place_ref, pos_ref, k_ref, v_ref, q_ref, dg_ref, straight, diag, wide, sems):
    slots, width = straight.shape[1], straight.shape[2]
    half = k_ref.shape[-1] // 2
    core, chip = place_ref[0], place_ref[1]
    ends = ((straight, core * half), (diag, (1 - core) * half))

    def copies(first, second, targets, offset):
        out = []
        for i, (end, start) in enumerate(ends):
            cols = pl.ds(pl.multiple_of(start + offset, HEAD), width)
            out.append(pltpu.make_async_copy(first.at[0, :, cols], end.at[0], sems.at[2 * i]))
            out.append(pltpu.make_async_copy(second.at[0, :, cols], targets[i], sems.at[2 * i + 1]))
        for c in out:
            c.start()
        for c in out:
            c.wait()

    @pl.when(chip == 0)
    def _():
        copies(k_ref, v_ref, (straight.at[1], diag.at[1]), 0)
        live = live_rows(pos_ref, slots)
        for end, _ in ends:
            end[0] = mark_dead(end[0], live)

    @pl.when(chip != 0)
    def _():
        copies(q_ref, dg_ref, (wide.at[0], wide.at[1]), width)
        for i, (end, _) in enumerate(ends):
            end[1] = wide[i].astype(BF16)


def cross_pack(place, route_pos, keys, values, queries, d_gated):
    _, slots, full = keys.shape
    cross = pltpu.VMEM((2, slots, full // 4), BF16)
    hbm = pl.BlockSpec(memory_space=pltpu.HBM)
    return pl.pallas_call(
        cross_pack_kernel,
        out_shape=[cross, cross],
        in_specs=[SMEM, VMEM, hbm, hbm, hbm, hbm],
        out_specs=[VMEM] * 2,
        scratch_shapes=[pltpu.VMEM((2, slots, full // 4), F32), pltpu.SemaphoreType.DMA((4,))],
        compiler_params=params(),
        cost_estimate=cost(0, 10 * slots * full),
        name="cross_pack",
    )(place, route_pos, *in_hbm(keys, values, queries, d_gated))


def sib_pack_kernel(place_ref, pos_ref, k_ref, v_ref, q_ref, dg_ref, out, wide, sems):
    slots, half = out.shape[1], out.shape[2]
    cols = pl.ds(pl.multiple_of((1 - place_ref[0]) * half, HEAD), half)
    sources = ((k_ref, out.at[0]), (dg_ref, wide), (v_ref, out.at[1]), (q_ref, out.at[2]))
    copies = [pltpu.make_async_copy(src.at[0, :, cols], dst, sems.at[i]) for i, (src, dst) in enumerate(sources)]
    for c in copies:
        c.start()
    live = live_rows(pos_ref, slots)
    copies[0].wait()
    out[0] = mark_dead(out[0], live)
    copies[1].wait()
    out[3] = wide[...].astype(BF16)
    copies[2].wait()
    copies[3].wait()


def sib_pack(place, route_pos, keys, values, queries, d_gated):
    _, slots, full = keys.shape
    hbm = pl.BlockSpec(memory_space=pltpu.HBM)
    return pl.pallas_call(
        sib_pack_kernel,
        out_shape=pltpu.VMEM((4, slots, full // 2), BF16),
        in_specs=[SMEM, VMEM, hbm, hbm, hbm, hbm],
        out_specs=VMEM,
        scratch_shapes=[pltpu.VMEM((slots, full // 2), F32), pltpu.SemaphoreType.DMA((4,))],
        compiler_params=params(),
        cost_estimate=cost(0, 20 * slots * full),
        name="sib_pack",
    )(place, route_pos, *in_hbm(keys, values, queries, d_gated))


def pair_gate_kernel(parts, place_ref, live_ref, rows_x, w_ref, out_ref):
    chunk = w_ref.shape[1] // parts
    slots = rows_x.shape[1]
    for i in range(2):
        total = jnp.zeros((8, slots), F32)
        for j in range(parts):
            w_rows = jnp.broadcast_to(w_ref[:, j * chunk : (j + 1) * chunk], (8, chunk)).astype(BF16)
            cols = pl.ds(pl.multiple_of((place_ref[2] ^ j) * chunk, HEAD), chunk)
            total = total + nt(w_rows, rows_x[i, :, cols])
        lanes = slice(i * slots, (i + 1) * slots)
        out_ref[:, lanes] = live_ref[:, lanes] / (1.0 + jnp.exp(-total[0:1]))


def pair_gate(place, live, rows_x, w_full, parts):
    return pl.pallas_call(
        functools.partial(pair_gate_kernel, parts),
        out_shape=jax.ShapeDtypeStruct(live.shape, F32),
        in_specs=[SMEM] + [VMEM] * 3,
        out_specs=VMEM,
        compiler_params=params(),
        cost_estimate=cost(16 * rows_x.size, rows_x.size * 2),
        name="router_gate",
    )(place, live, rows_x, w_full)


def local_mask(core, pair):
    slots = pair.shape[1] // 2
    key = lax.broadcasted_iota(jnp.int32, (slots, slots), 0)
    query = lax.broadcasted_iota(jnp.int32, (slots, slots), 1)
    causal = key <= query
    own_live = pair[0, :slots, :slots].astype(F32) < MARK_LIMIT
    sib_live = pair[0, slots:, :slots].astype(F32) < MARK_LIMIT
    own_rows = jnp.concatenate([own_live & causal, own_live & (core == 0)], axis=1)
    sib_rows = jnp.concatenate([sib_live & (core == 1), sib_live & causal], axis=1)
    return jnp.concatenate([own_rows, sib_rows], axis=0)


def kept_stats(scores, gw, kept, stats, h):
    top = jnp.max(scores, axis=0, keepdims=True)
    e = jnp.exp(scores - top).astype(BF16)
    gw = gw.astype(BF16)
    kept[0, h] = e
    kept[1, h] = gw
    e = e.astype(F32)
    stats[0, h : h + 1] = top
    stats[1, h : h + 1] = jnp.sum(e, axis=0, keepdims=True)
    stats[2, h : h + 1] = jnp.sum(e * gw.astype(F32), axis=0, keepdims=True)


def partial_stats(scores, gw, stats, h):
    top = jnp.max(scores, axis=0, keepdims=True)
    e = jnp.exp(scores - top)
    stats[0, h : h + 1] = top
    stats[1, h : h + 1] = jnp.sum(e, axis=0, keepdims=True)
    stats[2, h : h + 1] = jnp.sum(e * gw, axis=0, keepdims=True)


def local_stats_kernel(scale, place_ref, pos_ref, k_ref, v_ref, q_ref, dg_ref, sib, x_ref, x_sib, stats, live, pair, rows_x, wide, sems, x_sems):
    slots, half = sib.shape[1], sib.shape[2]
    width = half // 2
    core = place_ref[0]
    own, other = slice(0, slots), slice(slots, 2 * slots)
    stages = []
    for g in range(2):
        cols = slice(g * width, (g + 1) * width)
        held = pl.ds(pl.multiple_of(core * half + g * width, HEAD), width)
        copies = [
            pltpu.make_async_copy(ref.at[0, :, held], pair.at[j, own, cols], sems.at[8 * g + j])
            for j, ref in enumerate((k_ref, v_ref, q_ref))
        ]
        copies.append(pltpu.make_async_copy(dg_ref.at[0, :, held], wide.at[:, cols], sems.at[8 * g + 3]))
        for j in range(4):
            copies.append(pltpu.make_async_copy(sib.at[j, :, cols], pair.at[j, other, cols], sems.at[8 * g + 4 + j]))
        for c in copies:
            c.start()
        stages.append(copies)
    x_copies = []
    depth = x_ref.shape[2] // 2
    for i, ref in enumerate((x_ref, x_sib)):
        for g in range(2):
            cols = slice(g * depth, (g + 1) * depth)
            x_copies.append(pltpu.make_async_copy(ref.at[0, :, cols], rows_x.at[i, :, cols], x_sems.at[2 * i + g]))
    for c in x_copies:
        c.start()
    rows_live = live_rows(pos_ref, slots)
    mask = None
    for g in range(2):
        cols = slice(g * width, (g + 1) * width)
        for c in stages[g]:
            c.wait()
        pair[0, own, cols] = mark_dead(pair[0, own, cols], rows_live)
        pair[3, own, cols] = wide[:, cols].astype(BF16)
        if mask is None:
            mask = local_mask(core, pair)
            marks = nt(jnp.ones((8, HEAD), BF16), pair[0, :, :HEAD])[0:1]
            live[...] = jnp.where(marks < MARK_LIMIT, 1.0, 0.0)
        for h in range(g * width // HEAD, (g + 1) * width // HEAD):
            at = slice(h * HEAD, (h + 1) * HEAD)
            scores = jnp.where(mask, nt(pair[0, :, at], pair[2, :, at]) * scale, NEG_FILL)
            partial_stats(scores, nt(pair[1, :, at], pair[3, :, at]), stats, h)
    for c in x_copies:
        c.wait()


def local_stats(place, route_pos, keys, values, queries, d_gated, sib, x_routed, x_sib):
    _, slots, half = sib.shape
    heads = half // HEAD
    anywhere = pl.BlockSpec(memory_space=pl.ANY)
    return pl.pallas_call(
        functools.partial(local_stats_kernel, HEAD**-0.5),
        out_shape=[
            jax.ShapeDtypeStruct((3, heads, 2 * slots), F32),
            jax.ShapeDtypeStruct((1, 2 * slots), F32),
            pltpu.VMEM((4, 2 * slots, half), BF16),
            pltpu.VMEM((2, slots, x_routed.shape[2]), BF16),
        ],
        in_specs=[SMEM, VMEM] + [anywhere] * 7,
        out_specs=[VMEM] * 4,
        scratch_shapes=[pltpu.VMEM((slots, half), F32), pltpu.SemaphoreType.DMA((16,)), pltpu.SemaphoreType.DMA((4,))],
        compiler_params=params(),
        cost_estimate=cost(16 * slots * slots * half, 16 * slots * half, 4 * slots * slots * half // HEAD),
        name="local_stats",
    )(place, route_pos, *in_hbm(keys, values, queries, d_gated), sib, x_routed, x_sib)


def cross_stats_kernel(scale, place_ref, pair, straight, diag, local, gates, cross, stats, kept, message):
    slots, width = straight.shape[1], straight.shape[2]
    chip = place_ref[1]
    top, bottom = slice(0, slots), slice(slots, 2 * slots)

    @pl.when(chip == 0)
    def _():
        cols = slice(width, 2 * width)
        for part in range(2):
            cross[part] = pair[part, :, cols]
            cross[2 + part, top] = straight[part]
            cross[2 + part, bottom] = diag[part]

    @pl.when(chip != 0)
    def _():
        cols = slice(0, width)
        for part in range(2):
            cross[part, top] = straight[part]
            cross[part, bottom] = diag[part]
            cross[2 + part] = pair[2 + part, :, cols]

    live = cross[0, :, :HEAD].astype(F32) < MARK_LIMIT
    mask = jnp.concatenate([live] * (2 * slots // HEAD), axis=1)
    heads = width // HEAD
    for h in range(heads):
        cols = slice(h * HEAD, (h + 1) * HEAD)
        scores = jnp.where(mask, nt(cross[0, :, cols], cross[2, :, cols]) * scale, NEG_FILL)
        kept_stats(scores, nt(cross[1, :, cols], cross[3, :, cols]), kept, stats, h)
    for i in range(3):
        message[i] = jnp.where(chip == 0, stats[i], local[i, heads:])
    message[3] = jnp.broadcast_to(gates[...], message.shape[1:])


def cross_stats(place, pair, straight, diag, local, gates):
    _, slots, width = straight.shape
    heads = width // HEAD
    return pl.pallas_call(
        functools.partial(cross_stats_kernel, HEAD**-0.5),
        out_shape=[
            jax.ShapeDtypeStruct((4, 2 * slots, width), BF16),
            jax.ShapeDtypeStruct((3, heads, 2 * slots), F32),
            jax.ShapeDtypeStruct((2, heads, 2 * slots, 2 * slots), BF16),
            jax.ShapeDtypeStruct((4, heads, 2 * slots), F32),
        ],
        in_specs=[SMEM] + [VMEM] * 5,
        out_specs=[VMEM] * 4,
        compiler_params=params(),
        cost_estimate=cost(16 * slots * slots * width, 32 * slots * width, 4 * slots * slots * heads),
        name="cross_stats",
    )(place, pair, straight, diag, local, gates)


NONE = (-3e38, 0.0, 0.0)


def merge(first, second):
    top = jnp.maximum(first[0], second[0])
    a, b = jnp.exp(first[0] - top), jnp.exp(second[0] - top)
    inverse = 1.0 / (first[1] * a + second[1] * b)
    return a * inverse, (first[2] * a + second[2] * b) * inverse


def choose(flag, yes, no):
    return [jnp.where(flag, y, n) for y, n in zip(yes, no)]


def gradients(q, k, dg, e, gw, scale, factor, delta):
    weights = e * factor
    ds = (weights * ((gw - delta) * scale)).astype(BF16)
    return tn(ds, k), nn(ds, q), nn(weights.astype(BF16), dg)


def local_gradients(pair, h, mask, scale, top, factor, delta):
    cols = slice(h * HEAD, (h + 1) * HEAD)
    k, v, q, dg = [pair[i, :, cols] for i in range(4)]
    e = jnp.exp(jnp.where(mask, nt(k, q) * scale, NEG_FILL) - top)
    return gradients(q, k, dg, e, nt(v, dg), scale, factor, delta)


def near_grad_kernel(scale, place_ref, pair, local, stats, gates, dq_out, own_out, sib_out, sum_out):
    slots, width = own_out.shape[1], own_out.shape[2]
    heads = width // HEAD
    first = place_ref[1] == 0
    near = [local[i, :heads] for i in range(3)]
    factor, delta = merge(near, choose(first, NONE, [stats[i] for i in range(3)]))
    factor = factor * gates[...]
    sum_out[...] = jnp.sum(delta, axis=0, keepdims=True)
    mask = local_mask(place_ref[0], pair)
    for h in range(heads):
        cols = slice(h * HEAD, (h + 1) * HEAD)
        row = slice(h, h + 1)
        dq, dk, dv = local_gradients(pair, h, mask, scale, near[0][row], factor[row], delta[row])
        dq_out[:, cols] = dq
        for i, part in enumerate((dk, dv)):
            own_out[i, :, cols] = part[:slots].astype(BF16)
            sib_out[i, :, cols] = part[slots:].astype(BF16)


def near_grad(place, pair, local, stats, gates):
    _, rows, half = pair.shape
    slots = rows // 2
    width = half // 2
    out = jax.ShapeDtypeStruct((2, slots, width), BF16)
    return pl.pallas_call(
        functools.partial(near_grad_kernel, HEAD**-0.5),
        out_shape=[jax.ShapeDtypeStruct((2 * slots, width), F32), out, out, jax.ShapeDtypeStruct(gates.shape, F32)],
        in_specs=[SMEM] + [VMEM] * 4,
        out_specs=[VMEM] * 4,
        compiler_params=params(),
        cost_estimate=cost(20 * slots * slots * half, 40 * slots * half),
        name="near_grad",
    )(place, pair, local, stats, gates)


def cross_grad_kernel(scale, place_ref, cross, kept, stats, local, heard, gates, near_dq, near_sum, straight, diag, dq_out, keep, final, sum_out):
    slots, width = straight.shape[1], straight.shape[2]
    heads = width // HEAD
    first = place_ref[1] == 0
    late = jnp.where(first, 0.0, 1.0)
    mine = [stats[i] for i in range(3)]
    other = [heard[i] for i in range(3)]
    near = [local[i, :heads] for i in range(3)]
    far = [local[i, heads:] for i in range(3)]
    factor, delta = merge(mine, choose(first, other, near))
    factor = factor * jnp.where(first, heard[3], jnp.broadcast_to(gates[...], factor.shape))
    final[0], final[1] = merge(far, choose(first, NONE, other))
    sum_out[...] = near_sum[...] + jnp.sum(final[1], axis=0, keepdims=True)
    for h in range(heads):
        cols = slice(h * HEAD, (h + 1) * HEAD)
        row = slice(h, h + 1)
        dq, dk, dv = gradients(
            cross[2, :, cols], cross[0, :, cols], cross[3, :, cols],
            kept[0, h].astype(F32), kept[1, h].astype(F32), scale, factor[row], delta[row],
        )
        dq_out[:, cols] = (near_dq[:, cols] + late * dq).astype(BF16)
        keep[0, :, cols] = dk.astype(BF16)
        keep[1, :, cols] = dv.astype(BF16)
        sent = jnp.where(first, dq, dk).astype(BF16)
        straight[0, :, cols] = sent[:slots]
        diag[0, :, cols] = sent[slots:]
        straight[1, :, cols] = dv[:slots].astype(BF16)
        diag[1, :, cols] = dv[slots:].astype(BF16)


def cross_grad(place, cross, kept, stats, local, heard, gates, near_dq, near_sum):
    _, rows, width = cross.shape
    slots = rows // 2
    out = jax.ShapeDtypeStruct((2, slots, width), BF16)
    return pl.pallas_call(
        functools.partial(cross_grad_kernel, HEAD**-0.5),
        out_shape=[
            out,
            out,
            pltpu.VMEM((rows, width), BF16),
            pltpu.VMEM((2, rows, width), BF16),
            jax.ShapeDtypeStruct((2, width // HEAD, rows), F32),
            jax.ShapeDtypeStruct((1, rows), F32),
        ],
        in_specs=[SMEM] + [VMEM] * 8,
        out_specs=[VMEM] * 6,
        compiler_params=params(),
        cost_estimate=cost(24 * slots * slots * width, 64 * slots * width),
        name="cross_grad",
    )(place, cross, kept, stats, local, heard, gates, near_dq, near_sum)


def far_grad_kernel(scale, place_ref, pair, local, final, gates, keep, near_dq, near_own, near_sib, own_out, sib_out):
    slots, half = pair.shape[1] // 2, pair.shape[2]
    width = half // 2
    heads = width // HEAD
    early = jnp.where(place_ref[1] == 0, 1.0, 0.0)
    factor = final[0] * gates[...]
    mask = local_mask(place_ref[0], pair)
    own_out[0, :, :width] = near_dq[:slots]
    sib_out[0, :, :width] = near_dq[slots:]
    for i in range(2):
        own_out[1 + i, :, :width] = near_own[i]
        sib_out[1 + i, :, :width] = near_sib[i]
    for h in range(heads):
        cols = slice(width + h * HEAD, width + (h + 1) * HEAD)
        at = slice(h * HEAD, (h + 1) * HEAD)
        row = slice(h, h + 1)
        top = local[0, heads + h : heads + h + 1]
        dq, dk, dv = local_gradients(pair, heads + h, mask, scale, top, factor[row], final[1, row])
        dk = dk + early * keep[0, :, at].astype(F32)
        dv = dv + early * keep[1, :, at].astype(F32)
        for i, part in enumerate((dq, dk, dv)):
            own_out[i, :, cols] = part[:slots].astype(BF16)
            sib_out[i, :, cols] = part[slots:].astype(BF16)


def far_grad(place, pair, local, final, gates, keep, near_dq, near_own, near_sib):
    _, rows, half = pair.shape
    slots = rows // 2
    out = jax.ShapeDtypeStruct((3, slots, half), BF16)
    return pl.pallas_call(
        functools.partial(far_grad_kernel, HEAD**-0.5),
        out_shape=[out, out],
        in_specs=[SMEM] + [VMEM] * 8,
        out_specs=[VMEM] * 2,
        compiler_params=params(),
        cost_estimate=cost(20 * slots * slots * half, 40 * slots * half),
        name="far_grad",
    )(place, pair, local, final, gates, keep, near_dq, near_own, near_sib)


def join_kernel(place_ref, own, sib, straight, diag, dq_out, dk_out, dv_out, low, back, total, in_sems, out_sems):
    slots, half = own.shape[1], own.shape[2]
    width = straight.shape[2]
    core, chip = place_ref[0], place_ref[1]
    early, late = jnp.where(chip == 0, 1.0, 0.0), jnp.where(chip == 0, 0.0, 1.0)
    ends = ((own, straight, core * half), (sib, diag, (1 - core) * half))
    loads = []
    for i, (part, extra, _) in enumerate(ends):
        extras = [pltpu.make_async_copy(extra.at[j], back.at[i, j], in_sems.at[5 * i + j]) for j in range(2)]
        parts = [pltpu.make_async_copy(part.at[j], low.at[i, j], in_sems.at[5 * i + 2 + j]) for j in range(3)]
        loads.append((parts, extras))
    for parts, extras in loads:
        for c in (parts[0], extras[0], parts[1], extras[1], parts[2]):
            c.start()
    stores = []
    for i, (_, _, start) in enumerate(ends):
        parts, extras = loads[i]
        for j, out in enumerate((dq_out, dk_out, dv_out)):
            parts[j].wait()
            if j < 2:
                extras[j].wait()
            at = total.at[i, j]
            first, second = low[i, j, :, :width].astype(F32), low[i, j, :, width:].astype(F32)
            if j == 0:
                at[:, :width] = first
                at[:, width:] = second + late * back[i, 0].astype(F32)
            else:
                at[:, :width] = first + early * back[i, j - 1].astype(F32)
                at[:, width:] = second
            cols = pl.ds(pl.multiple_of(start, HEAD), half)
            stores.append(pltpu.make_async_copy(at, out.at[0, :, cols], out_sems.at[3 * i + j]))
            stores[-1].start()
    for c in stores:
        c.wait()


def join(place, own, sib, straight, diag, shape):
    out = jax.ShapeDtypeStruct(shape, F32)
    _, slots, half = own.shape
    anywhere = pl.BlockSpec(memory_space=pl.ANY)
    hbm = pl.BlockSpec(memory_space=pltpu.HBM)
    return pl.pallas_call(
        join_kernel,
        out_shape=[out] * 3,
        in_specs=[SMEM] + [anywhere] * 4,
        out_specs=[hbm] * 3,
        scratch_shapes=[
            pltpu.VMEM((2, 3, slots, half), BF16),
            pltpu.VMEM((2, 2, slots, half // 2), BF16),
            pltpu.VMEM((2, 3, slots, half), F32),
            pltpu.SemaphoreType.DMA((10,)),
            pltpu.SemaphoreType.DMA((6,)),
        ],
        compiler_params=params(),
        cost_estimate=cost(0, 18 * out.size),
        name="join",
    )(place, own, sib, straight, diag)


def pair_router_kernel(gates_ref, sum_ref, rows_x, out_ref):
    gates = gates_ref[...]
    grad = sum_ref[...] * gates * (1.0 - gates)
    high = grad.astype(BF16)
    rest = grad - high.astype(F32)
    mid = rest.astype(BF16)
    low = (rest - mid.astype(F32)).astype(BF16)
    slots = rows_x.shape[1]
    row = lax.broadcasted_iota(jnp.int32, (8, grad.shape[1]), 0)
    lhs = jnp.where(row == 0, high.astype(F32), jnp.where(row == 1, mid.astype(F32), jnp.where(row == 2, low.astype(F32), 0.0)))
    lhs = lhs.astype(BF16)
    term = jnp.sum(nn(lhs[:, :slots], rows_x[0]) + nn(lhs[:, slots:], rows_x[1]), axis=0, keepdims=True)
    parts, copies, _, chunk = out_ref.shape
    for j in range(parts):
        for i in range(copies):
            out_ref[j, i] = term[:, j * chunk : (j + 1) * chunk]


def pair_router(gates, sums, rows_x, parts, copies):
    chunk = rows_x.shape[-1] // parts
    return pl.pallas_call(
        pair_router_kernel,
        out_shape=jax.ShapeDtypeStruct((parts, copies, 1, chunk), F32),
        in_specs=[VMEM] * 3,
        out_specs=VMEM,
        compiler_params=params(),
        cost_estimate=cost(32 * rows_x.size, rows_x.size * 4),
        name="router_terms",
    )(gates, sums, rows_x)


def swap_body(route_pos, x_routed, w_router, queries, keys, values, d_gated):
    slots = queries.shape[1]
    n, ndp = lax.axis_size("ctx"), lax.axis_size("dp")
    me = lax.axis_index("ctx")
    place = jnp.stack([me % 2, me // 2, lax.axis_index("dp")]).astype(jnp.int32)

    def send(a, flip):
        return lax.ppermute(a, "ctx", [(i, i ^ flip) for i in range(n)])

    def beside(fn, *operands):
        def skip(*ops):
            return jax.tree.map(lambda o: jnp.zeros(o.shape, o.dtype), jax.eval_shape(fn, *ops))

        return lax.cond(route_pos[0, 0] >= -1, fn, skip, *operands)

    def after(value, *others):
        return lax.optimization_barrier((value, *others))[0]

    def near_dp(part, step):
        return lax.ppermute(part, "dp", [(i, i ^ step) for i in range(ndp)])

    def widen(part, step, *first):
        return jnp.concatenate([part, after(near_dp(part, step), *first)], axis=1)

    def exchange_phase(x_routed, w_part, theirs):
        sib, x_sib = send(theirs, 1), send(x_routed, 1)
        step = 4
        while step < ndp:
            w_part = widen(w_part, step)
            step *= 2
        return sib, x_sib, w_part

    def grad_phase(*operands):
        own_out, sib_out = far_grad(*operands)
        return own_out, send(sib_out, 1)

    def router_phase(gates, sums, rows_x, place, *operands):
        terms = pair_router(gates, sums, rows_x, ndp, n)
        chunk = terms.shape[-1]
        shared = lax.all_to_all(terms.reshape(ndp * n, 1, chunk), ("dp", "ctx"), 0, 0, tiled=True)
        own_out, sib_in = beside(grad_phase, after(place, terms), *operands)
        return own_out, sib_in, jnp.sum(shared, axis=0)[0] / float(ndp * n * slots // 2)

    w_part = w_router.reshape(1, -1).astype(F32)
    out_s, out_d = cross_pack(place, route_pos, keys, values, queries, d_gated)
    in_s, in_d = send(out_s, 2), send(out_d, 3)
    theirs = sib_pack(place, after(route_pos, out_s), keys, values, queries, d_gated)
    if ndp > 1:
        w_part = widen(w_part, 1)
    if ndp > 2:
        w_part = widen(w_part, 2, theirs)
    sib, x_sib, w_part = beside(exchange_phase, x_routed, w_part, theirs)
    local, live, pair, rows_x = local_stats(place, route_pos, keys, values, queries, d_gated, sib, x_routed, x_sib)
    gates = pair_gate(place, live, rows_x, w_part, ndp)
    cross, stats, kept_cross, message = cross_stats(place, pair, in_s, in_d, local, gates)
    heard = send(message, 2)
    near_dq, near_own, near_sib, near_sum = near_grad(place, pair, local, stats, gates)
    back_s, back_d, dq_low, keep, final, sums = cross_grad(
        place, cross, kept_cross, stats, local, heard, gates, near_dq, near_sum
    )
    ret_s, ret_d = send(back_s, 2), send(back_d, 3)
    own_out, sib_in, router_grad = beside(
        router_phase, gates, sums, rows_x, place, pair, local, final, gates, keep, dq_low, near_own, near_sib
    )
    dq, dk, dv = join(place, own_out, sib_in, ret_s, ret_d, queries.shape)
    return dq, dk, dv, router_grad


def body(route_pos, x_routed, w_router, queries, keys, values, d_gated):
    slots, full = queries.shape[1], queries.shape[2]
    n, ndp = lax.axis_size("ctx"), lax.axis_size("dp")
    chips = n // 2
    me, dp_me = lax.axis_index("ctx"), lax.axis_index("dp")
    core = (me % 2).astype(jnp.int32).reshape(1)
    half = full // 2
    groups = GROUPS if (half // HEAD) % GROUPS == 0 else 1
    width = half // groups

    sib_pairs = [(i, i ^ 1) for i in range(n)]

    def forward_pairs(step, flip):
        return [(i, (i + 2 * step) ^ flip) for i in range(n) if i + 2 * step < n]

    def back_pairs(step, flip):
        return [(b, a) for a, b in forward_pairs(step, flip)]

    def to_sib(a):
        return lax.ppermute(a, "ctx", sib_pairs)

    links = [(step, flip) for step in range(1, chips) for flip in (0, 1)]

    w_row = w_router.reshape(1, -1)
    w_parts = [w_row] + [
        lax.ppermute(w_row, "dp", [(i, (i + s) % ndp) for i in range(ndp)]) for s in range(1, ndp)
    ]
    live = (route_pos >= 0).astype(jnp.int32)
    lives = [live, to_sib(live)] + [lax.ppermute(live, "ctx", forward_pairs(*link)) for link in links]
    live_all = jnp.concatenate(lives, axis=0)

    kv_mine, kv_theirs = pack(core, keys, values, groups, width)
    kv_far = [
        [lax.ppermute((kv_theirs if flip else kv_mine)[g], "ctx", forward_pairs(step, flip)) for step, flip in links]
        for g in range(groups)
    ]
    q_mine, q_theirs = pack(core, queries, d_gated, groups, width)
    kv_sib = [to_sib(a) for a in kv_theirs]
    q_sib = [to_sib(a) for a in q_theirs]

    offsets = ((dp_me - jnp.arange(ndp)) % ndp).astype(jnp.int32)
    gate = router_gate(offsets, route_pos, x_routed, w_parts)
    gates = (gate, to_sib(gate))

    accs = (jnp.zeros((1, slots), F32), jnp.zeros((1, slots), F32))
    dq_own, sib_in, kv_own, back = [], [], [], []
    for g in range(groups):
        dq, sib_out, kv_local, kv_remote, accs = attention(
            core, live_all, gates, accs, q_mine[g], q_sib[g], [kv_mine[g], kv_sib[g], *kv_far[g]]
        )
        back.append([lax.ppermute(a, "ctx", back_pairs(*link)) for a, link in zip(kv_remote, links)])
        sib_in.append(to_sib(sib_out))
        dq_own.append(dq)
        kv_own.append(kv_local)

    targets = ((dp_me + jnp.arange(ndp)) % ndp).astype(jnp.int32)
    terms = router_terms(targets, gate, accs[0], to_sib(accs[1]), x_routed, ndp)
    mine = terms[0]
    for s in range(1, ndp):
        mine = mine + lax.ppermute(terms[s], "dp", [(i, (i + s) % ndp) for i in range(ndp)])
    total = mine
    for s in range(1, n):
        total = total + lax.ppermute(mine, "ctx", [(i, (i + s) % n) for i in range(n)])
    router_grad = total[0] / float(ndp * n * slots // 2)

    dq, dk, dv = combine(core, dq_own, sib_in, kv_own, back, queries.shape)
    return dq, dk, dv, router_grad


def solution(mesh):
    placed = (
        P("dp", "ctx"),
        P("dp", "ctx", None),
        P("dp"),
        P("dp", "ctx", None),
        P("dp", "ctx", None),
        P("dp", "ctx", None),
        P("dp", "ctx", None),
    )
    ndp = mesh.shape["dp"]
    paired = mesh.shape["ctx"] == 4 and ndp & (ndp - 1) == 0
    return jax.shard_map(
        swap_body if paired else body,
        mesh=mesh,
        in_specs=placed,
        out_specs=(P("dp", "ctx", None), P("dp", "ctx", None), P("dp", "ctx", None), P("dp")),
        check_vma=False,
    )
```

```python
import functools

import jax
import jax.numpy as jnp
from jax import lax
from jax.experimental import pallas as pl
from jax.experimental.pallas import tpu as pltpu
from jax.sharding import PartitionSpec as P

HEAD = 128
GROUPS = 4
NEG_FILL = -1e30
MIB = 1024 * 1024
BF16 = jnp.bfloat16
F32 = jnp.float32

VMEM = pl.BlockSpec(memory_space=pltpu.VMEM)
SMEM = pl.BlockSpec(memory_space=pltpu.SMEM)


def params(mib=16):
    return pltpu.CompilerParams(vmem_limit_bytes=mib * MIB)


def cost(flops, nbytes, exps=0):
    return pl.CostEstimate(flops=1, bytes_accessed=1, transcendentals=0)


def in_hbm(*arrays):
    return [pltpu.with_memory_space_constraint(a, pltpu.HBM) for a in arrays]


def nt(a, b):
    return lax.dot_general(a, b, (((1,), (1,)), ((), ())), preferred_element_type=F32)


def nn(a, b):
    return lax.dot_general(a, b, (((1,), (0,)), ((), ())), preferred_element_type=F32)


def tn(a, b):
    return lax.dot_general(a, b, (((0,), (0,)), ((), ())), preferred_element_type=F32)


def pack_kernel(groups, width, core_ref, first_ref, second_ref, *outs):
    half = first_ref.shape[-1] // 2
    core = core_ref[0]
    for side in range(2):
        base = (core if side == 0 else 1 - core) * half
        for g in range(groups):
            out = outs[side * groups + g]
            cols = pl.ds(pl.multiple_of(base + g * width, HEAD), width)
            out[0] = first_ref[0, :, cols].astype(BF16)
            out[1] = second_ref[0, :, cols].astype(BF16)


def pack(core, first, second, groups, width):
    slots = first.shape[1]
    out = jax.ShapeDtypeStruct((2, slots, width), BF16)
    res = pl.pallas_call(
        functools.partial(pack_kernel, groups, width),
        out_shape=[out] * (2 * groups),
        in_specs=[SMEM, VMEM, VMEM],
        out_specs=[VMEM] * (2 * groups),
        compiler_params=params(),
        cost_estimate=cost(0, 2 * first.size * 4),
        name="pack",
    )(core, first, second)
    return res[:groups], res[groups:]


def gate_kernel(parts, offset_ref, pos_ref, x_ref, *refs):
    w_refs, out_ref = refs[:parts], refs[parts]
    chunk = w_refs[0].shape[-1]
    total = jnp.zeros((8, x_ref.shape[1]), F32)
    for s in range(parts):
        cols = pl.ds(pl.multiple_of(offset_ref[s] * chunk, HEAD), chunk)
        w_rows = jnp.broadcast_to(w_refs[s][...].astype(F32), (8, chunk)).astype(BF16)
        total = total + nt(w_rows, x_ref[0, :, cols])
    gate = 1.0 / (1.0 + jnp.exp(-total[0:1]))
    out_ref[...] = jnp.where(pos_ref[...] >= 0, gate, 0.0)


def router_gate(offsets, route_pos, x_routed, w_parts):
    parts = len(w_parts)
    return pl.pallas_call(
        functools.partial(gate_kernel, parts),
        out_shape=jax.ShapeDtypeStruct(route_pos.shape, F32),
        in_specs=[SMEM] + [VMEM] * (2 + parts),
        out_specs=VMEM,
        compiler_params=params(),
        cost_estimate=cost(16 * x_routed.size, x_routed.size * 2),
        name="router_gate",
    )(offsets, route_pos, x_routed, *w_parts)


def attention_kernel(remote, scale, core_ref, live_ref, gate_own, gate_sib, acc_own, acc_sib, q_own, q_sib, *refs):
    chunks = 2 + remote
    kv = refs[:chunks]
    outs = refs[chunks:]
    dq_own, sib_out, kv_own = outs[:3]
    kv_remote = outs[3 : 3 + remote]
    sum_own, sum_sib = outs[3 + remote :]
    slots, width = q_own.shape[1], q_own.shape[2]
    core = core_ref[0]
    key = lax.broadcasted_iota(jnp.int32, (slots, slots), 0)
    query = lax.broadcasted_iota(jnp.int32, (slots, slots), 1)
    counts = [jnp.sum(live_ref[i : i + 1], axis=1, keepdims=True) for i in range(chunks)]
    lives = [key < counts[i] for i in range(chunks)]
    own_later = core == 1
    bias_rows = []
    for i in range(chunks):
        live = lives[i]
        if i == 0:
            pair = (live & (key <= query), live & jnp.logical_not(own_later))
        elif i == 1:
            pair = (live & own_later, live & (key <= query))
        else:
            pair = (live, live)
        bias_rows.append(jnp.concatenate([jnp.where(p, 0.0, NEG_FILL) for p in pair], axis=1))
    bias = jnp.concatenate(bias_rows, axis=0)
    gates = jnp.concatenate([gate_own[...], gate_sib[...]], axis=1)
    total = jnp.zeros((1, 2 * slots), F32)
    for h in range(width // HEAD):
        cols = slice(h * HEAD, (h + 1) * HEAD)
        q = jnp.concatenate([q_own[0, :, cols], q_sib[0, :, cols]], axis=0)
        dg = jnp.concatenate([q_own[1, :, cols], q_sib[1, :, cols]], axis=0)
        k = jnp.concatenate([r[0, :, cols] for r in kv], axis=0)
        v = jnp.concatenate([r[1, :, cols] for r in kv], axis=0)
        scores = nt(k, q) * scale + bias
        top = jnp.max(scores, axis=0, keepdims=True)
        e = jnp.exp(scores - top)
        inverse = 1.0 / jnp.sum(e, axis=0, keepdims=True)
        gw = nt(v, dg)
        delta = jnp.sum(e * gw, axis=0, keepdims=True) * inverse
        total = total + delta
        weights = e * (inverse * gates)
        dv = nn(weights.astype(BF16), dg)
        ds = (weights * ((gw - delta) * scale)).astype(BF16)
        dk = nn(ds, q)
        dq = tn(ds, k)
        dq_own[:, cols] = dq[:slots].astype(dq_own.dtype)
        sib_out[0, :, cols] = dq[slots:].astype(BF16)
        kv_own[0, :, cols] = dk[:slots].astype(BF16)
        kv_own[1, :, cols] = dv[:slots].astype(BF16)
        sib_out[1, :, cols] = dk[slots : 2 * slots].astype(BF16)
        sib_out[2, :, cols] = dv[slots : 2 * slots].astype(BF16)
        for i in range(remote):
            rows = slice((2 + i) * slots, (3 + i) * slots)
            kv_remote[i][0, :, cols] = dk[rows].astype(BF16)
            kv_remote[i][1, :, cols] = dv[rows].astype(BF16)
    sum_own[...] = acc_own[...] + total[:, :slots]
    sum_sib[...] = acc_sib[...] + total[:, slots:]


def attention(core, live, gates, accs, q_own, q_sib, kv):
    remote = len(kv) - 2
    _, slots, width = q_own.shape
    pair = jax.ShapeDtypeStruct((2, slots, width), BF16)
    row = jax.ShapeDtypeStruct((1, slots), F32)
    outs = [
        jax.ShapeDtypeStruct((slots, width), BF16),
        jax.ShapeDtypeStruct((3, slots, width), BF16),
        pair,
        *([pair] * remote),
        row,
        row,
    ]
    keys = (2 + remote) * slots
    res = pl.pallas_call(
        functools.partial(attention_kernel, remote, HEAD**-0.5),
        out_shape=outs,
        in_specs=[SMEM] + [VMEM] * (7 + len(kv)),
        out_specs=[VMEM] * len(outs),
        compiler_params=params(48),
        cost_estimate=cost(20 * slots * keys * width, 8 * keys * width + 20 * slots * width, 2 * slots * keys * width // HEAD),
        name="attention",
    )(core, live, *gates, *accs, q_own, q_sib, *kv)
    return res[0], res[1], res[2], res[3 : 3 + remote], (res[3 + remote], res[4 + remote])


def combine_kernel(groups, width, remote, core_ref, *refs):
    dq_own, sib, kv_own = refs[:groups], refs[groups : 2 * groups], refs[2 * groups : 3 * groups]
    back = refs[3 * groups : 3 * groups + groups * remote]
    dq_out, dk_out, dv_out = refs[3 * groups + groups * remote :]
    half = groups * width
    core = core_ref[0]
    for g in range(groups):
        own = pl.ds(pl.multiple_of(core * half + g * width, HEAD), width)
        other = pl.ds(pl.multiple_of((1 - core) * half + g * width, HEAD), width)
        dq_out[0, :, own] = dq_own[g][...].astype(F32)
        dq_out[0, :, other] = sib[g][0].astype(F32)
        for i, out in enumerate((dk_out, dv_out)):
            mine = kv_own[g][i].astype(F32)
            theirs = sib[g][1 + i].astype(F32)
            for r in range(remote):
                part = back[g * remote + r][i].astype(F32)
                if r % 2 == 0:
                    mine = mine + part
                else:
                    theirs = theirs + part
            out[0, :, own] = mine
            out[0, :, other] = theirs


def combine(core, dq_own, sib, kv_own, back, shape):
    groups = len(dq_own)
    remote = len(back[0])
    out = jax.ShapeDtypeStruct(shape, F32)
    flat = [*dq_own, *sib, *kv_own, *(b for group in back for b in group)]
    return pl.pallas_call(
        functools.partial(combine_kernel, groups, dq_own[0].shape[-1], remote),
        out_shape=[out] * 3,
        in_specs=[SMEM] + [VMEM] * len(flat),
        out_specs=[VMEM] * 3,
        compiler_params=params(48),
        cost_estimate=cost(0, 3 * out.size * 6),
        name="combine",
    )(core, *flat)


def router_kernel(parts, target_ref, gate_ref, own_ref, sib_ref, x_ref, *outs):
    gate = gate_ref[...]
    grad = (own_ref[...] + sib_ref[...]) * gate * (1.0 - gate)
    high = grad.astype(BF16)
    rest = grad - high.astype(F32)
    mid = rest.astype(BF16)
    low = (rest - mid.astype(F32)).astype(BF16)
    row = lax.broadcasted_iota(jnp.int32, (8, grad.shape[1]), 0)
    lhs = jnp.where(row == 0, high.astype(F32), jnp.where(row == 1, mid.astype(F32), jnp.where(row == 2, low.astype(F32), 0.0)))
    lhs = lhs.astype(BF16)
    chunk = outs[0].shape[-1]
    for s in range(parts):
        cols = pl.ds(pl.multiple_of(target_ref[s] * chunk, HEAD), chunk)
        outs[s][...] = jnp.sum(nn(lhs, x_ref[0, :, cols]), axis=0, keepdims=True)


def router_terms(targets, gate, own, sib, x_routed, parts):
    chunk = x_routed.shape[-1] // parts
    return pl.pallas_call(
        functools.partial(router_kernel, parts),
        out_shape=[jax.ShapeDtypeStruct((1, chunk), F32)] * parts,
        in_specs=[SMEM] + [VMEM] * 4,
        out_specs=[VMEM] * parts,
        compiler_params=params(),
        cost_estimate=cost(16 * x_routed.size, x_routed.size * 2),
        name="router_terms",
    )(targets, gate, own, sib, x_routed)


MARK = 2.0**60
MARK_LIMIT = 2.0**50


def live_rows(pos_ref, slots):
    count = jnp.sum((pos_ref[...] >= 0).astype(jnp.int32), axis=1, keepdims=True)
    return lax.broadcasted_iota(jnp.int32, (slots, HEAD), 0) < count


def mark_dead(keys, live):
    width = keys.shape[-1]
    mask = jnp.concatenate([live] * (width // HEAD), axis=1)
    return jnp.where(mask, keys.astype(F32), MARK).astype(BF16)


def cross_pack_kernel(place_ref, pos_ref, w_ref, k_ref, v_ref, q_ref, dg_ref, straight, diag, w_out, wide, sems):
    w_out[...] = w_ref[...].astype(F32).reshape(w_out.shape)
    slots, width = straight.shape[1], straight.shape[2]
    half = k_ref.shape[-1] // 2
    core, chip = place_ref[0], place_ref[1]
    ends = ((straight, core * half), (diag, (1 - core) * half))

    def copies(first, second, targets, offset):
        out = []
        for i, (end, start) in enumerate(ends):
            cols = pl.ds(pl.multiple_of(start + offset, HEAD), width)
            out.append(pltpu.make_async_copy(first.at[0, :, cols], end.at[0], sems.at[2 * i]))
            out.append(pltpu.make_async_copy(second.at[0, :, cols], targets[i], sems.at[2 * i + 1]))
        for c in out:
            c.start()
        for c in out:
            c.wait()

    @pl.when(chip == 0)
    def _():
        copies(k_ref, v_ref, (straight.at[1], diag.at[1]), 0)
        live = live_rows(pos_ref, slots)
        for end, _ in ends:
            end[0] = mark_dead(end[0], live)

    @pl.when(chip != 0)
    def _():
        copies(q_ref, dg_ref, (wide.at[0], wide.at[1]), width)
        for i, (end, _) in enumerate(ends):
            end[1] = wide[i].astype(BF16)


def cross_pack(place, route_pos, w_router, keys, values, queries, d_gated):
    _, slots, full = keys.shape
    cross = pltpu.VMEM((2, slots, full // 4), BF16)
    hbm = pl.BlockSpec(memory_space=pltpu.HBM)
    return pl.pallas_call(
        cross_pack_kernel,
        out_shape=[cross, cross, jax.ShapeDtypeStruct((1, w_router.shape[0]), F32)],
        in_specs=[SMEM, VMEM, VMEM, hbm, hbm, hbm, hbm],
        out_specs=[VMEM] * 3,
        scratch_shapes=[pltpu.VMEM((2, slots, full // 4), F32), pltpu.SemaphoreType.DMA((4,))],
        compiler_params=params(),
        cost_estimate=cost(0, 10 * slots * full),
        name="cross_pack",
    )(place, route_pos, w_router, *in_hbm(keys, values, queries, d_gated))


def sib_pack_kernel(place_ref, pos_ref, k_ref, v_ref, q_ref, dg_ref, out, wide, sems):
    slots, half = out.shape[1], out.shape[2]
    cols = pl.ds(pl.multiple_of((1 - place_ref[0]) * half, HEAD), half)
    sources = ((k_ref, out.at[0]), (dg_ref, wide), (v_ref, out.at[1]), (q_ref, out.at[2]))
    copies = [pltpu.make_async_copy(src.at[0, :, cols], dst, sems.at[i]) for i, (src, dst) in enumerate(sources)]
    for c in copies:
        c.start()
    live = live_rows(pos_ref, slots)
    copies[0].wait()
    out[0] = mark_dead(out[0], live)
    copies[1].wait()
    out[3] = wide[...].astype(BF16)
    copies[2].wait()
    copies[3].wait()


def sib_pack(place, route_pos, keys, values, queries, d_gated):
    _, slots, full = keys.shape
    hbm = pl.BlockSpec(memory_space=pltpu.HBM)
    return pl.pallas_call(
        sib_pack_kernel,
        out_shape=pltpu.VMEM((4, slots, full // 2), BF16),
        in_specs=[SMEM, VMEM, hbm, hbm, hbm, hbm],
        out_specs=VMEM,
        scratch_shapes=[pltpu.VMEM((slots, full // 2), F32), pltpu.SemaphoreType.DMA((4,))],
        compiler_params=params(),
        cost_estimate=cost(0, 20 * slots * full),
        name="sib_pack",
    )(place, route_pos, *in_hbm(keys, values, queries, d_gated))


def pair_gate_kernel(parts, place_ref, live_ref, rows_x, w_ref, local, stats, out_ref, message):
    chunk = w_ref.shape[1] // parts
    slots = rows_x.shape[1]
    for i in range(2):
        total = jnp.zeros((8, slots), F32)
        for j in range(parts):
            w_rows = jnp.broadcast_to(w_ref[:, j * chunk : (j + 1) * chunk], (8, chunk)).astype(BF16)
            cols = pl.ds(pl.multiple_of((place_ref[2] ^ j) * chunk, HEAD), chunk)
            total = total + nt(w_rows, rows_x[i, :, cols])
        lanes = slice(i * slots, (i + 1) * slots)
        out_ref[:, lanes] = live_ref[:, lanes] / (1.0 + jnp.exp(-total[0:1]))
    first = place_ref[1] == 0
    heads = stats.shape[1]
    for i in range(3):
        message[i] = jnp.where(first, stats[i], local[i, heads:])
    message[3] = jnp.broadcast_to(out_ref[...], message.shape[1:])


def pair_gate(place, live, rows_x, w_full, local, stats, parts):
    _, heads, lanes = stats.shape
    return pl.pallas_call(
        functools.partial(pair_gate_kernel, parts),
        out_shape=[jax.ShapeDtypeStruct(live.shape, F32), jax.ShapeDtypeStruct((4, heads, lanes), F32)],
        in_specs=[SMEM] + [VMEM] * 5,
        out_specs=[VMEM] * 2,
        compiler_params=params(),
        cost_estimate=cost(16 * rows_x.size, rows_x.size * 2),
        name="router_gate",
    )(place, live, rows_x, w_full, local, stats)


def local_mask(core, pair):
    slots = pair.shape[1] // 2
    key = lax.broadcasted_iota(jnp.int32, (slots, slots), 0)
    query = lax.broadcasted_iota(jnp.int32, (slots, slots), 1)
    causal = key <= query
    own_live = pair[0, :slots, :slots].astype(F32) < MARK_LIMIT
    sib_live = pair[0, slots:, :slots].astype(F32) < MARK_LIMIT
    own_rows = jnp.concatenate([own_live & causal, own_live & (core == 0)], axis=1)
    sib_rows = jnp.concatenate([sib_live & (core == 1), sib_live & causal], axis=1)
    return jnp.concatenate([own_rows, sib_rows], axis=0)


def kept_stats(scores, gw, kept, stats, h):
    top = jnp.max(scores, axis=0, keepdims=True)
    e = jnp.exp(scores - top).astype(BF16)
    gw = gw.astype(BF16)
    kept[0, h] = e
    kept[1, h] = gw
    e = e.astype(F32)
    stats[0, h : h + 1] = top
    stats[1, h : h + 1] = jnp.sum(e, axis=0, keepdims=True)
    stats[2, h : h + 1] = jnp.sum(e * gw.astype(F32), axis=0, keepdims=True)


def partial_stats(scores, gw, stats, h):
    top = jnp.max(scores, axis=0, keepdims=True)
    e = jnp.exp(scores - top)
    stats[0, h : h + 1] = top
    stats[1, h : h + 1] = jnp.sum(e, axis=0, keepdims=True)
    stats[2, h : h + 1] = jnp.sum(e * gw, axis=0, keepdims=True)


def local_stats_kernel(scale, place_ref, pos_ref, k_ref, v_ref, q_ref, dg_ref, sib, x_ref, x_sib, stats, live, pair, rows_x, wide, sems, x_sems):
    slots, half = sib.shape[1], sib.shape[2]
    width = half // 2
    core = place_ref[0]
    own, other = slice(0, slots), slice(slots, 2 * slots)
    stages = []
    for g in range(2):
        cols = slice(g * width, (g + 1) * width)
        held = pl.ds(pl.multiple_of(core * half + g * width, HEAD), width)
        copies = [
            pltpu.make_async_copy(ref.at[0, :, held], pair.at[j, own, cols], sems.at[8 * g + j])
            for j, ref in enumerate((k_ref, v_ref, q_ref))
        ]
        copies.append(pltpu.make_async_copy(dg_ref.at[0, :, held], wide.at[:, cols], sems.at[8 * g + 3]))
        for j in range(4):
            copies.append(pltpu.make_async_copy(sib.at[j, :, cols], pair.at[j, other, cols], sems.at[8 * g + 4 + j]))
        for c in copies:
            c.start()
        stages.append(copies)
    x_copies = []
    depth = x_ref.shape[2] // 2
    for i, ref in enumerate((x_ref, x_sib)):
        for g in range(2):
            cols = slice(g * depth, (g + 1) * depth)
            x_copies.append(pltpu.make_async_copy(ref.at[0, :, cols], rows_x.at[i, :, cols], x_sems.at[2 * i + g]))
    for c in x_copies:
        c.start()
    rows_live = live_rows(pos_ref, slots)
    mask = None
    for g in range(2):
        cols = slice(g * width, (g + 1) * width)
        for c in stages[g]:
            c.wait()
        pair[0, own, cols] = mark_dead(pair[0, own, cols], rows_live)
        pair[3, own, cols] = wide[:, cols].astype(BF16)
        if mask is None:
            mask = local_mask(core, pair)
            marks = nt(jnp.ones((8, HEAD), BF16), pair[0, :, :HEAD])[0:1]
            live[...] = jnp.where(marks < MARK_LIMIT, 1.0, 0.0)
        for h in range(g * width // HEAD, (g + 1) * width // HEAD):
            at = slice(h * HEAD, (h + 1) * HEAD)
            scores = jnp.where(mask, nt(pair[0, :, at], pair[2, :, at]) * scale, NEG_FILL)
            partial_stats(scores, nt(pair[1, :, at], pair[3, :, at]), stats, h)
    for c in x_copies:
        c.wait()


def local_stats(place, route_pos, keys, values, queries, d_gated, sib, x_routed, x_sib):
    _, slots, half = sib.shape
    heads = half // HEAD
    anywhere = pl.BlockSpec(memory_space=pl.ANY)
    return pl.pallas_call(
        functools.partial(local_stats_kernel, HEAD**-0.5),
        out_shape=[
            jax.ShapeDtypeStruct((3, heads, 2 * slots), F32),
            jax.ShapeDtypeStruct((1, 2 * slots), F32),
            pltpu.VMEM((4, 2 * slots, half), BF16),
            pltpu.VMEM((2, slots, x_routed.shape[2]), BF16),
        ],
        in_specs=[SMEM, VMEM] + [anywhere] * 7,
        out_specs=[VMEM] * 4,
        scratch_shapes=[pltpu.VMEM((slots, half), F32), pltpu.SemaphoreType.DMA((16,)), pltpu.SemaphoreType.DMA((4,))],
        compiler_params=params(),
        cost_estimate=cost(16 * slots * slots * half, 16 * slots * half, 4 * slots * slots * half // HEAD),
        name="local_stats",
    )(place, route_pos, *in_hbm(keys, values, queries, d_gated), sib, x_routed, x_sib)


def cross_stats_kernel(scale, place_ref, pair, straight, diag, cross, stats, kept):
    slots, width = straight.shape[1], straight.shape[2]
    chip = place_ref[1]
    top, bottom = slice(0, slots), slice(slots, 2 * slots)

    @pl.when(chip == 0)
    def _():
        cols = slice(width, 2 * width)
        for part in range(2):
            cross[part] = pair[part, :, cols]
            cross[2 + part, top] = straight[part]
            cross[2 + part, bottom] = diag[part]

    @pl.when(chip != 0)
    def _():
        cols = slice(0, width)
        for part in range(2):
            cross[part, top] = straight[part]
            cross[part, bottom] = diag[part]
            cross[2 + part] = pair[2 + part, :, cols]

    live = cross[0, :, :HEAD].astype(F32) < MARK_LIMIT
    mask = jnp.concatenate([live] * (2 * slots // HEAD), axis=1)
    heads = width // HEAD
    for h in range(heads):
        cols = slice(h * HEAD, (h + 1) * HEAD)
        scores = jnp.where(mask, nt(cross[0, :, cols], cross[2, :, cols]) * scale, NEG_FILL)
        kept_stats(scores, nt(cross[1, :, cols], cross[3, :, cols]), kept, stats, h)


def cross_stats(place, pair, straight, diag):
    _, slots, width = straight.shape
    heads = width // HEAD
    return pl.pallas_call(
        functools.partial(cross_stats_kernel, HEAD**-0.5),
        out_shape=[
            pltpu.VMEM((4, 2 * slots, width), BF16),
            jax.ShapeDtypeStruct((3, heads, 2 * slots), F32),
            pltpu.VMEM((2, heads, 2 * slots, 2 * slots), BF16),
        ],
        in_specs=[SMEM] + [VMEM] * 3,
        out_specs=[VMEM] * 3,
        compiler_params=params(),
        cost_estimate=cost(16 * slots * slots * width, 32 * slots * width, 4 * slots * slots * heads),
        name="cross_stats",
    )(place, pair, straight, diag)


NONE = (-3e38, 0.0, 0.0)


def merge(first, second):
    top = jnp.maximum(first[0], second[0])
    a, b = jnp.exp(first[0] - top), jnp.exp(second[0] - top)
    inverse = 1.0 / (first[1] * a + second[1] * b)
    return a * inverse, (first[2] * a + second[2] * b) * inverse


def choose(flag, yes, no):
    return [jnp.where(flag, y, n) for y, n in zip(yes, no)]


def gradients(q, k, dg, e, gw, scale, factor, delta):
    weights = e * factor
    ds = (weights * ((gw - delta) * scale)).astype(BF16)
    return tn(ds, k), nn(ds, q), nn(weights.astype(BF16), dg)


def local_gradients(pair, h, mask, scale, top, factor, delta):
    cols = slice(h * HEAD, (h + 1) * HEAD)
    k, v, q, dg = [pair[i, :, cols] for i in range(4)]
    e = jnp.exp(jnp.where(mask, nt(k, q) * scale, NEG_FILL) - top)
    return gradients(q, k, dg, e, nt(v, dg), scale, factor, delta)


def near_grad_kernel(scale, place_ref, pair, local, stats, gates, dq_out, own_out, sib_out, sum_out):
    slots, width = own_out.shape[1], own_out.shape[2]
    heads = width // HEAD
    first = place_ref[1] == 0
    near = [local[i, :heads] for i in range(3)]
    factor, delta = merge(near, choose(first, NONE, [stats[i] for i in range(3)]))
    factor = factor * gates[...]
    sum_out[...] = jnp.sum(delta, axis=0, keepdims=True)
    mask = local_mask(place_ref[0], pair)
    for h in range(heads):
        cols = slice(h * HEAD, (h + 1) * HEAD)
        row = slice(h, h + 1)
        dq, dk, dv = local_gradients(pair, h, mask, scale, near[0][row], factor[row], delta[row])
        dq_out[:, cols] = dq
        for i, part in enumerate((dk, dv)):
            own_out[i, :, cols] = part[:slots].astype(BF16)
            sib_out[i, :, cols] = part[slots:].astype(BF16)


def near_grad(place, pair, local, stats, gates):
    _, rows, half = pair.shape
    slots = rows // 2
    width = half // 2
    out = pltpu.VMEM((2, slots, width), BF16)
    return pl.pallas_call(
        functools.partial(near_grad_kernel, HEAD**-0.5),
        out_shape=[pltpu.VMEM((2 * slots, width), F32), out, out, jax.ShapeDtypeStruct(gates.shape, F32)],
        in_specs=[SMEM] + [VMEM] * 4,
        out_specs=[VMEM] * 4,
        compiler_params=params(),
        cost_estimate=cost(20 * slots * slots * half, 40 * slots * half),
        name="near_grad",
    )(place, pair, local, stats, gates)


def cross_grad_kernel(scale, place_ref, cross, kept, stats, local, heard, gates, near_dq, near_sum, straight, diag, dq_out, keep, final, sum_out):
    slots, width = straight.shape[1], straight.shape[2]
    heads = width // HEAD
    first = place_ref[1] == 0
    late = jnp.where(first, 0.0, 1.0)
    mine = [stats[i] for i in range(3)]
    other = [heard[i] for i in range(3)]
    near = [local[i, :heads] for i in range(3)]
    far = [local[i, heads:] for i in range(3)]
    factor, delta = merge(mine, choose(first, other, near))
    factor = factor * jnp.where(first, heard[3], jnp.broadcast_to(gates[...], factor.shape))
    final[0], final[1] = merge(far, choose(first, NONE, other))
    sum_out[...] = near_sum[...] + jnp.sum(final[1], axis=0, keepdims=True)
    for h in range(heads):
        cols = slice(h * HEAD, (h + 1) * HEAD)
        row = slice(h, h + 1)
        dq, dk, dv = gradients(
            cross[2, :, cols], cross[0, :, cols], cross[3, :, cols],
            kept[0, h].astype(F32), kept[1, h].astype(F32), scale, factor[row], delta[row],
        )
        dq_out[:, cols] = (near_dq[:, cols] + late * dq).astype(BF16)
        keep[0, :, cols] = dk.astype(BF16)
        keep[1, :, cols] = dv.astype(BF16)
        sent = jnp.where(first, dq, dk).astype(BF16)
        straight[0, :, cols] = sent[:slots]
        diag[0, :, cols] = sent[slots:]
        straight[1, :, cols] = dv[:slots].astype(BF16)
        diag[1, :, cols] = dv[slots:].astype(BF16)


def cross_grad(place, cross, kept, stats, local, heard, gates, near_dq, near_sum):
    _, rows, width = cross.shape
    slots = rows // 2
    out = pltpu.VMEM((2, slots, width), BF16)
    return pl.pallas_call(
        functools.partial(cross_grad_kernel, HEAD**-0.5),
        out_shape=[
            out,
            out,
            pltpu.VMEM((rows, width), BF16),
            pltpu.VMEM((2, rows, width), BF16),
            jax.ShapeDtypeStruct((2, width // HEAD, rows), F32),
            jax.ShapeDtypeStruct((1, rows), F32),
        ],
        in_specs=[SMEM] + [VMEM] * 8,
        out_specs=[VMEM] * 6,
        compiler_params=params(),
        cost_estimate=cost(24 * slots * slots * width, 64 * slots * width),
        name="cross_grad",
    )(place, cross, kept, stats, local, heard, gates, near_dq, near_sum)


def far_grad_kernel(scale, place_ref, pair, local, final, gates, keep, near_dq, near_own, near_sib, own_out, sib_out):
    slots, half = pair.shape[1] // 2, pair.shape[2]
    width = half // 2
    heads = width // HEAD
    early = jnp.where(place_ref[1] == 0, 1.0, 0.0)
    factor = final[0] * gates[...]
    mask = local_mask(place_ref[0], pair)
    own_out[0, :, :width] = near_dq[:slots]
    sib_out[0, :, :width] = near_dq[slots:]
    for i in range(2):
        own_out[1 + i, :, :width] = near_own[i]
        sib_out[1 + i, :, :width] = near_sib[i]
    for h in range(heads):
        cols = slice(width + h * HEAD, width + (h + 1) * HEAD)
        at = slice(h * HEAD, (h + 1) * HEAD)
        row = slice(h, h + 1)
        top = local[0, heads + h : heads + h + 1]
        dq, dk, dv = local_gradients(pair, heads + h, mask, scale, top, factor[row], final[1, row])
        dk = dk + early * keep[0, :, at].astype(F32)
        dv = dv + early * keep[1, :, at].astype(F32)
        for i, part in enumerate((dq, dk, dv)):
            own_out[i, :, cols] = part[:slots].astype(BF16)
            sib_out[i, :, cols] = part[slots:].astype(BF16)


def far_grad(place, pair, local, final, gates, keep, near_dq, near_own, near_sib):
    _, rows, half = pair.shape
    slots = rows // 2
    out = jax.ShapeDtypeStruct((3, slots, half), BF16)
    return pl.pallas_call(
        functools.partial(far_grad_kernel, HEAD**-0.5),
        out_shape=[out, out],
        in_specs=[SMEM] + [VMEM] * 8,
        out_specs=[VMEM] * 2,
        compiler_params=params(),
        cost_estimate=cost(20 * slots * slots * half, 40 * slots * half),
        name="far_grad",
    )(place, pair, local, final, gates, keep, near_dq, near_own, near_sib)


def join_kernel(place_ref, own, sib, straight, diag, dq_out, dk_out, dv_out, low, back, total, in_sems, out_sems):
    slots, half = own.shape[1], own.shape[2]
    width = straight.shape[2]
    core, chip = place_ref[0], place_ref[1]
    early, late = jnp.where(chip == 0, 1.0, 0.0), jnp.where(chip == 0, 0.0, 1.0)
    ends = ((own, straight, core * half), (sib, diag, (1 - core) * half))
    loads = []
    for i, (part, extra, _) in enumerate(ends):
        extras = [pltpu.make_async_copy(extra.at[j], back.at[i, j], in_sems.at[5 * i + j]) for j in range(2)]
        parts = [pltpu.make_async_copy(part.at[j], low.at[i, j], in_sems.at[5 * i + 2 + j]) for j in range(3)]
        loads.append((parts, extras))
    for parts, extras in loads:
        for c in (parts[0], extras[0], parts[1], extras[1], parts[2]):
            c.start()
    stores = []
    for i, (_, _, start) in enumerate(ends):
        parts, extras = loads[i]
        for j, out in enumerate((dq_out, dk_out, dv_out)):
            parts[j].wait()
            if j < 2:
                extras[j].wait()
            at = total.at[i, j]
            first, second = low[i, j, :, :width].astype(F32), low[i, j, :, width:].astype(F32)
            if j == 0:
                at[:, :width] = first
                at[:, width:] = second + late * back[i, 0].astype(F32)
            else:
                at[:, :width] = first + early * back[i, j - 1].astype(F32)
                at[:, width:] = second
            cols = pl.ds(pl.multiple_of(start, HEAD), half)
            stores.append(pltpu.make_async_copy(at, out.at[0, :, cols], out_sems.at[3 * i + j]))
            stores[-1].start()
    for c in stores:
        c.wait()


def join(place, own, sib, straight, diag, shape):
    out = jax.ShapeDtypeStruct(shape, F32)
    _, slots, half = own.shape
    anywhere = pl.BlockSpec(memory_space=pl.ANY)
    hbm = pl.BlockSpec(memory_space=pltpu.HBM)
    return pl.pallas_call(
        join_kernel,
        out_shape=[out] * 3,
        in_specs=[SMEM] + [anywhere] * 4,
        out_specs=[hbm] * 3,
        scratch_shapes=[
            pltpu.VMEM((2, 3, slots, half), BF16),
            pltpu.VMEM((2, 2, slots, half // 2), BF16),
            pltpu.VMEM((2, 3, slots, half), F32),
            pltpu.SemaphoreType.DMA((10,)),
            pltpu.SemaphoreType.DMA((6,)),
        ],
        compiler_params=params(),
        cost_estimate=cost(0, 18 * out.size),
        name="join",
    )(place, own, sib, straight, diag)


def pair_router_kernel(gates_ref, sum_ref, rows_x, out_ref):
    gates = gates_ref[...]
    grad = sum_ref[...] * gates * (1.0 - gates)
    high = grad.astype(BF16)
    rest = grad - high.astype(F32)
    mid = rest.astype(BF16)
    low = (rest - mid.astype(F32)).astype(BF16)
    slots = rows_x.shape[1]
    row = lax.broadcasted_iota(jnp.int32, (8, grad.shape[1]), 0)
    lhs = jnp.where(row == 0, high.astype(F32), jnp.where(row == 1, mid.astype(F32), jnp.where(row == 2, low.astype(F32), 0.0)))
    lhs = lhs.astype(BF16)
    term = jnp.sum(nn(lhs[:, :slots], rows_x[0]) + nn(lhs[:, slots:], rows_x[1]), axis=0, keepdims=True)
    parts, copies, _, chunk = out_ref.shape
    for j in range(parts):
        for i in range(copies):
            out_ref[j, i] = term[:, j * chunk : (j + 1) * chunk]


def pair_router(gates, sums, rows_x, parts, copies):
    chunk = rows_x.shape[-1] // parts
    return pl.pallas_call(
        pair_router_kernel,
        out_shape=jax.ShapeDtypeStruct((parts, copies, 1, chunk), F32),
        in_specs=[VMEM] * 3,
        out_specs=VMEM,
        compiler_params=params(),
        cost_estimate=cost(32 * rows_x.size, rows_x.size * 4),
        name="router_terms",
    )(gates, sums, rows_x)


def swap_body(route_pos, x_routed, w_router, queries, keys, values, d_gated):
    slots = queries.shape[1]
    n, ndp = lax.axis_size("ctx"), lax.axis_size("dp")
    me = lax.axis_index("ctx")
    place = jnp.stack([me % 2, me // 2, lax.axis_index("dp")]).astype(jnp.int32)

    def send(a, flip):
        return lax.ppermute(a, "ctx", [(i, i ^ flip) for i in range(n)])

    def beside(fn, *operands):
        def skip(*ops):
            return jax.tree.map(lambda o: jnp.zeros(o.shape, o.dtype), jax.eval_shape(fn, *ops))

        return lax.cond(route_pos[0, 0] >= -1, fn, skip, *operands)

    def after(value, *others):
        return lax.optimization_barrier((value, *others))[0]

    def near_dp(part, step):
        return lax.ppermute(part, "dp", [(i, i ^ step) for i in range(ndp)])

    def widen(part, step, *first):
        return jnp.concatenate([part, after(near_dp(part, step), *first)], axis=1)

    def exchange_phase(x_routed, w_part, theirs):
        sib, x_sib = send(theirs, 1), send(x_routed, 1)
        step = 2
        while 2 * step < ndp:
            w_part = widen(w_part, step)
            step *= 2
        return sib, x_sib, w_part

    def grad_phase(*operands):
        own_out, sib_out = far_grad(*operands)
        return own_out, send(sib_out, 1)

    def router_phase(gates, sums, rows_x, place, *operands):
        terms = pair_router(gates, sums, rows_x, ndp, n)
        chunk = terms.shape[-1]
        shared = lax.all_to_all(terms.reshape(ndp * n, 1, chunk), ("dp", "ctx"), 0, 0, tiled=True)
        own_out, sib_in = beside(grad_phase, after(place, terms), *operands)
        return own_out, sib_in, jnp.sum(shared, axis=0)[0] / float(ndp * n * slots // 2)

    out_s, out_d, w_part = cross_pack(place, route_pos, w_router, keys, values, queries, d_gated)
    in_s, in_d = send(out_s, 2), send(out_d, 3)
    theirs = sib_pack(place, after(route_pos, out_s), keys, values, queries, d_gated)
    if ndp > 1:
        w_part = widen(w_part, 1, theirs)
    sib, x_sib, w_part = beside(exchange_phase, x_routed, w_part, theirs)
    local, live, pair, rows_x = local_stats(place, route_pos, keys, values, queries, d_gated, sib, x_routed, x_sib)
    cross, stats, kept_cross = cross_stats(place, pair, in_s, in_d)
    if ndp > 2:
        w_part = widen(w_part, ndp // 2, stats)
    gates, message = pair_gate(place, live, rows_x, w_part, local, stats, ndp)
    heard = send(message, 2)
    near_dq, near_own, near_sib, near_sum = near_grad(place, pair, local, stats, gates)
    back_s, back_d, dq_low, keep, final, sums = cross_grad(
        place, cross, kept_cross, stats, local, heard, gates, near_dq, near_sum
    )
    ret_s, ret_d = send(back_s, 2), send(back_d, 3)
    own_out, sib_in, router_grad = beside(
        router_phase, gates, sums, rows_x, place, pair, local, final, gates, keep, dq_low, near_own, near_sib
    )
    dq, dk, dv = join(place, own_out, sib_in, ret_s, ret_d, queries.shape)
    return dq, dk, dv, router_grad


def body(route_pos, x_routed, w_router, queries, keys, values, d_gated):
    slots, full = queries.shape[1], queries.shape[2]
    n, ndp = lax.axis_size("ctx"), lax.axis_size("dp")
    chips = n // 2
    me, dp_me = lax.axis_index("ctx"), lax.axis_index("dp")
    core = (me % 2).astype(jnp.int32).reshape(1)
    half = full // 2
    groups = GROUPS if (half // HEAD) % GROUPS == 0 else 1
    width = half // groups

    sib_pairs = [(i, i ^ 1) for i in range(n)]

    def forward_pairs(step, flip):
        return [(i, (i + 2 * step) ^ flip) for i in range(n) if i + 2 * step < n]

    def back_pairs(step, flip):
        return [(b, a) for a, b in forward_pairs(step, flip)]

    def to_sib(a):
        return lax.ppermute(a, "ctx", sib_pairs)

    links = [(step, flip) for step in range(1, chips) for flip in (0, 1)]

    w_row = w_router.reshape(1, -1)
    w_parts = [w_row] + [
        lax.ppermute(w_row, "dp", [(i, (i + s) % ndp) for i in range(ndp)]) for s in range(1, ndp)
    ]
    live = (route_pos >= 0).astype(jnp.int32)
    lives = [live, to_sib(live)] + [lax.ppermute(live, "ctx", forward_pairs(*link)) for link in links]
    live_all = jnp.concatenate(lives, axis=0)

    kv_mine, kv_theirs = pack(core, keys, values, groups, width)
    kv_far = [
        [lax.ppermute((kv_theirs if flip else kv_mine)[g], "ctx", forward_pairs(step, flip)) for step, flip in links]
        for g in range(groups)
    ]
    q_mine, q_theirs = pack(core, queries, d_gated, groups, width)
    kv_sib = [to_sib(a) for a in kv_theirs]
    q_sib = [to_sib(a) for a in q_theirs]

    offsets = ((dp_me - jnp.arange(ndp)) % ndp).astype(jnp.int32)
    gate = router_gate(offsets, route_pos, x_routed, w_parts)
    gates = (gate, to_sib(gate))

    accs = (jnp.zeros((1, slots), F32), jnp.zeros((1, slots), F32))
    dq_own, sib_in, kv_own, back = [], [], [], []
    for g in range(groups):
        dq, sib_out, kv_local, kv_remote, accs = attention(
            core, live_all, gates, accs, q_mine[g], q_sib[g], [kv_mine[g], kv_sib[g], *kv_far[g]]
        )
        back.append([lax.ppermute(a, "ctx", back_pairs(*link)) for a, link in zip(kv_remote, links)])
        sib_in.append(to_sib(sib_out))
        dq_own.append(dq)
        kv_own.append(kv_local)

    targets = ((dp_me + jnp.arange(ndp)) % ndp).astype(jnp.int32)
    terms = router_terms(targets, gate, accs[0], to_sib(accs[1]), x_routed, ndp)
    mine = terms[0]
    for s in range(1, ndp):
        mine = mine + lax.ppermute(terms[s], "dp", [(i, (i + s) % ndp) for i in range(ndp)])
    total = mine
    for s in range(1, n):
        total = total + lax.ppermute(mine, "ctx", [(i, (i + s) % n) for i in range(n)])
    router_grad = total[0] / float(ndp * n * slots // 2)

    dq, dk, dv = combine(core, dq_own, sib_in, kv_own, back, queries.shape)
    return dq, dk, dv, router_grad


def solution(mesh):
    placed = (
        P("dp", "ctx"),
        P("dp", "ctx", None),
        P("dp"),
        P("dp", "ctx", None),
        P("dp", "ctx", None),
        P("dp", "ctx", None),
        P("dp", "ctx", None),
    )
    ndp = mesh.shape["dp"]
    paired = mesh.shape["ctx"] == 4 and ndp & (ndp - 1) == 0
    return jax.shard_map(
        swap_body if paired else body,
        mesh=mesh,
        in_specs=placed,
        out_specs=(P("dp", "ctx", None), P("dp", "ctx", None), P("dp", "ctx", None), P("dp")),
        check_vma=False,
    )
```

```python
import functools

import jax
import jax.numpy as jnp
from jax import lax
from jax.experimental import pallas as pl
from jax.experimental.pallas import tpu as pltpu
from jax.sharding import PartitionSpec as P

HEAD = 128
GROUPS = 4
NEG_FILL = -1e30
MIB = 1024 * 1024
BF16 = jnp.bfloat16
F32 = jnp.float32

VMEM = pl.BlockSpec(memory_space=pltpu.VMEM)
SMEM = pl.BlockSpec(memory_space=pltpu.SMEM)


def params(mib=16):
    return pltpu.CompilerParams(vmem_limit_bytes=mib * MIB)


def cost(flops, nbytes, exps=0):
    return pl.CostEstimate(flops=1, bytes_accessed=1, transcendentals=0)


def in_hbm(*arrays):
    return [pltpu.with_memory_space_constraint(a, pltpu.HBM) for a in arrays]


def nt(a, b):
    return lax.dot_general(a, b, (((1,), (1,)), ((), ())), preferred_element_type=F32)


def nn(a, b):
    return lax.dot_general(a, b, (((1,), (0,)), ((), ())), preferred_element_type=F32)


def tn(a, b):
    return lax.dot_general(a, b, (((0,), (0,)), ((), ())), preferred_element_type=F32)


def pack_kernel(groups, width, core_ref, first_ref, second_ref, *outs):
    half = first_ref.shape[-1] // 2
    core = core_ref[0]
    for side in range(2):
        base = (core if side == 0 else 1 - core) * half
        for g in range(groups):
            out = outs[side * groups + g]
            cols = pl.ds(pl.multiple_of(base + g * width, HEAD), width)
            out[0] = first_ref[0, :, cols].astype(BF16)
            out[1] = second_ref[0, :, cols].astype(BF16)


def pack(core, first, second, groups, width):
    slots = first.shape[1]
    out = jax.ShapeDtypeStruct((2, slots, width), BF16)
    res = pl.pallas_call(
        functools.partial(pack_kernel, groups, width),
        out_shape=[out] * (2 * groups),
        in_specs=[SMEM, VMEM, VMEM],
        out_specs=[VMEM] * (2 * groups),
        compiler_params=params(),
        cost_estimate=cost(0, 2 * first.size * 4),
        name="pack",
    )(core, first, second)
    return res[:groups], res[groups:]


def gate_kernel(parts, offset_ref, pos_ref, x_ref, *refs):
    w_refs, out_ref = refs[:parts], refs[parts]
    chunk = w_refs[0].shape[-1]
    total = jnp.zeros((8, x_ref.shape[1]), F32)
    for s in range(parts):
        cols = pl.ds(pl.multiple_of(offset_ref[s] * chunk, HEAD), chunk)
        w_rows = jnp.broadcast_to(w_refs[s][...].astype(F32), (8, chunk)).astype(BF16)
        total = total + nt(w_rows, x_ref[0, :, cols])
    gate = 1.0 / (1.0 + jnp.exp(-total[0:1]))
    out_ref[...] = jnp.where(pos_ref[...] >= 0, gate, 0.0)


def router_gate(offsets, route_pos, x_routed, w_parts):
    parts = len(w_parts)
    return pl.pallas_call(
        functools.partial(gate_kernel, parts),
        out_shape=jax.ShapeDtypeStruct(route_pos.shape, F32),
        in_specs=[SMEM] + [VMEM] * (2 + parts),
        out_specs=VMEM,
        compiler_params=params(),
        cost_estimate=cost(16 * x_routed.size, x_routed.size * 2),
        name="router_gate",
    )(offsets, route_pos, x_routed, *w_parts)


def attention_kernel(remote, scale, core_ref, live_ref, gate_own, gate_sib, acc_own, acc_sib, q_own, q_sib, *refs):
    chunks = 2 + remote
    kv = refs[:chunks]
    outs = refs[chunks:]
    dq_own, sib_out, kv_own = outs[:3]
    kv_remote = outs[3 : 3 + remote]
    sum_own, sum_sib = outs[3 + remote :]
    slots, width = q_own.shape[1], q_own.shape[2]
    core = core_ref[0]
    key = lax.broadcasted_iota(jnp.int32, (slots, slots), 0)
    query = lax.broadcasted_iota(jnp.int32, (slots, slots), 1)
    counts = [jnp.sum(live_ref[i : i + 1], axis=1, keepdims=True) for i in range(chunks)]
    lives = [key < counts[i] for i in range(chunks)]
    own_later = core == 1
    bias_rows = []
    for i in range(chunks):
        live = lives[i]
        if i == 0:
            pair = (live & (key <= query), live & jnp.logical_not(own_later))
        elif i == 1:
            pair = (live & own_later, live & (key <= query))
        else:
            pair = (live, live)
        bias_rows.append(jnp.concatenate([jnp.where(p, 0.0, NEG_FILL) for p in pair], axis=1))
    bias = jnp.concatenate(bias_rows, axis=0)
    gates = jnp.concatenate([gate_own[...], gate_sib[...]], axis=1)
    total = jnp.zeros((1, 2 * slots), F32)
    for h in range(width // HEAD):
        cols = slice(h * HEAD, (h + 1) * HEAD)
        q = jnp.concatenate([q_own[0, :, cols], q_sib[0, :, cols]], axis=0)
        dg = jnp.concatenate([q_own[1, :, cols], q_sib[1, :, cols]], axis=0)
        k = jnp.concatenate([r[0, :, cols] for r in kv], axis=0)
        v = jnp.concatenate([r[1, :, cols] for r in kv], axis=0)
        scores = nt(k, q) * scale + bias
        top = jnp.max(scores, axis=0, keepdims=True)
        e = jnp.exp(scores - top)
        inverse = 1.0 / jnp.sum(e, axis=0, keepdims=True)
        gw = nt(v, dg)
        delta = jnp.sum(e * gw, axis=0, keepdims=True) * inverse
        total = total + delta
        weights = e * (inverse * gates)
        dv = nn(weights.astype(BF16), dg)
        ds = (weights * ((gw - delta) * scale)).astype(BF16)
        dk = nn(ds, q)
        dq = tn(ds, k)
        dq_own[:, cols] = dq[:slots].astype(dq_own.dtype)
        sib_out[0, :, cols] = dq[slots:].astype(BF16)
        kv_own[0, :, cols] = dk[:slots].astype(BF16)
        kv_own[1, :, cols] = dv[:slots].astype(BF16)
        sib_out[1, :, cols] = dk[slots : 2 * slots].astype(BF16)
        sib_out[2, :, cols] = dv[slots : 2 * slots].astype(BF16)
        for i in range(remote):
            rows = slice((2 + i) * slots, (3 + i) * slots)
            kv_remote[i][0, :, cols] = dk[rows].astype(BF16)
            kv_remote[i][1, :, cols] = dv[rows].astype(BF16)
    sum_own[...] = acc_own[...] + total[:, :slots]
    sum_sib[...] = acc_sib[...] + total[:, slots:]


def attention(core, live, gates, accs, q_own, q_sib, kv):
    remote = len(kv) - 2
    _, slots, width = q_own.shape
    pair = jax.ShapeDtypeStruct((2, slots, width), BF16)
    row = jax.ShapeDtypeStruct((1, slots), F32)
    outs = [
        jax.ShapeDtypeStruct((slots, width), BF16),
        jax.ShapeDtypeStruct((3, slots, width), BF16),
        pair,
        *([pair] * remote),
        row,
        row,
    ]
    keys = (2 + remote) * slots
    res = pl.pallas_call(
        functools.partial(attention_kernel, remote, HEAD**-0.5),
        out_shape=outs,
        in_specs=[SMEM] + [VMEM] * (7 + len(kv)),
        out_specs=[VMEM] * len(outs),
        compiler_params=params(48),
        cost_estimate=cost(20 * slots * keys * width, 8 * keys * width + 20 * slots * width, 2 * slots * keys * width // HEAD),
        name="attention",
    )(core, live, *gates, *accs, q_own, q_sib, *kv)
    return res[0], res[1], res[2], res[3 : 3 + remote], (res[3 + remote], res[4 + remote])


def combine_kernel(groups, width, remote, core_ref, *refs):
    dq_own, sib, kv_own = refs[:groups], refs[groups : 2 * groups], refs[2 * groups : 3 * groups]
    back = refs[3 * groups : 3 * groups + groups * remote]
    dq_out, dk_out, dv_out = refs[3 * groups + groups * remote :]
    half = groups * width
    core = core_ref[0]
    for g in range(groups):
        own = pl.ds(pl.multiple_of(core * half + g * width, HEAD), width)
        other = pl.ds(pl.multiple_of((1 - core) * half + g * width, HEAD), width)
        dq_out[0, :, own] = dq_own[g][...].astype(F32)
        dq_out[0, :, other] = sib[g][0].astype(F32)
        for i, out in enumerate((dk_out, dv_out)):
            mine = kv_own[g][i].astype(F32)
            theirs = sib[g][1 + i].astype(F32)
            for r in range(remote):
                part = back[g * remote + r][i].astype(F32)
                if r % 2 == 0:
                    mine = mine + part
                else:
                    theirs = theirs + part
            out[0, :, own] = mine
            out[0, :, other] = theirs


def combine(core, dq_own, sib, kv_own, back, shape):
    groups = len(dq_own)
    remote = len(back[0])
    out = jax.ShapeDtypeStruct(shape, F32)
    flat = [*dq_own, *sib, *kv_own, *(b for group in back for b in group)]
    return pl.pallas_call(
        functools.partial(combine_kernel, groups, dq_own[0].shape[-1], remote),
        out_shape=[out] * 3,
        in_specs=[SMEM] + [VMEM] * len(flat),
        out_specs=[VMEM] * 3,
        compiler_params=params(48),
        cost_estimate=cost(0, 3 * out.size * 6),
        name="combine",
    )(core, *flat)


def router_kernel(parts, target_ref, gate_ref, own_ref, sib_ref, x_ref, *outs):
    gate = gate_ref[...]
    grad = (own_ref[...] + sib_ref[...]) * gate * (1.0 - gate)
    high = grad.astype(BF16)
    rest = grad - high.astype(F32)
    mid = rest.astype(BF16)
    low = (rest - mid.astype(F32)).astype(BF16)
    row = lax.broadcasted_iota(jnp.int32, (8, grad.shape[1]), 0)
    lhs = jnp.where(row == 0, high.astype(F32), jnp.where(row == 1, mid.astype(F32), jnp.where(row == 2, low.astype(F32), 0.0)))
    lhs = lhs.astype(BF16)
    chunk = outs[0].shape[-1]
    for s in range(parts):
        cols = pl.ds(pl.multiple_of(target_ref[s] * chunk, HEAD), chunk)
        outs[s][...] = jnp.sum(nn(lhs, x_ref[0, :, cols]), axis=0, keepdims=True)


def router_terms(targets, gate, own, sib, x_routed, parts):
    chunk = x_routed.shape[-1] // parts
    return pl.pallas_call(
        functools.partial(router_kernel, parts),
        out_shape=[jax.ShapeDtypeStruct((1, chunk), F32)] * parts,
        in_specs=[SMEM] + [VMEM] * 4,
        out_specs=[VMEM] * parts,
        compiler_params=params(),
        cost_estimate=cost(16 * x_routed.size, x_routed.size * 2),
        name="router_terms",
    )(targets, gate, own, sib, x_routed)


def here():
    me = lax.axis_index("ctx")
    return lax.rem(me, 2), lax.div(me, 2)


MARK = 2.0**60
MARK_LIMIT = 2.0**50


def live_rows(pos_ref, slots):
    count = jnp.sum((pos_ref[...] >= 0).astype(jnp.int32), axis=1, keepdims=True)
    return lax.broadcasted_iota(jnp.int32, (slots, HEAD), 0) < count


def mark_dead(keys, live):
    width = keys.shape[-1]
    mask = jnp.concatenate([live] * (width // HEAD), axis=1)
    return jnp.where(mask, keys.astype(F32), MARK).astype(BF16)


def cross_pack_kernel(pos_any, w_any, k_ref, v_ref, q_ref, dg_ref, straight, diag, w_out, wide, pos_ref, w_ref, sems):
    small = [pltpu.make_async_copy(pos_any, pos_ref, sems.at[4]), pltpu.make_async_copy(w_any, w_ref, sems.at[5])]
    for c in small:
        c.start()
    slots, width = straight.shape[1], straight.shape[2]
    half = k_ref.shape[-1] // 2
    core, chip = here()
    ends = ((straight, core * half), (diag, (1 - core) * half))

    def copies(first, second, targets, offset):
        out = []
        for i, (end, start) in enumerate(ends):
            cols = pl.ds(pl.multiple_of(start + offset, HEAD), width)
            out.append(pltpu.make_async_copy(first.at[0, :, cols], end.at[0], sems.at[2 * i]))
            out.append(pltpu.make_async_copy(second.at[0, :, cols], targets[i], sems.at[2 * i + 1]))
        for c in out:
            c.start()
        for c in out:
            c.wait()

    @pl.when(chip == 0)
    def _():
        copies(k_ref, v_ref, (straight.at[1], diag.at[1]), 0)
        small[0].wait()
        live = live_rows(pos_ref, slots)
        for end, _ in ends:
            end[0] = mark_dead(end[0], live)

    @pl.when(chip != 0)
    def _():
        copies(q_ref, dg_ref, (wide.at[0], wide.at[1]), width)
        small[0].wait()
        for i, (end, _) in enumerate(ends):
            end[1] = wide[i].astype(BF16)

    small[1].wait()
    w_out[...] = w_ref[...].astype(F32).reshape(w_out.shape)


def cross_pack(route_pos, w_router, keys, values, queries, d_gated):
    _, slots, full = keys.shape
    cross = pltpu.VMEM((2, slots, full // 4), BF16)
    hbm = pl.BlockSpec(memory_space=pltpu.HBM)
    return pl.pallas_call(
        cross_pack_kernel,
        out_shape=[cross, cross, jax.ShapeDtypeStruct((1, w_router.shape[0]), F32)],
        in_specs=[hbm] * 6,
        out_specs=[VMEM] * 3,
        scratch_shapes=[
            pltpu.VMEM((2, slots, full // 4), F32),
            pltpu.VMEM(route_pos.shape, jnp.int32),
            pltpu.VMEM(w_router.shape, BF16),
            pltpu.SemaphoreType.DMA((6,)),
        ],
        compiler_params=params(),
        cost_estimate=cost(0, 10 * slots * full),
        name="cross_pack",
    )(*in_hbm(route_pos, w_router, keys, values, queries, d_gated))


def sib_pack_kernel(pos_ref, k_ref, v_ref, q_ref, dg_ref, out, wide, sems):
    slots, half = out.shape[1], out.shape[2]
    cols = pl.ds(pl.multiple_of((1 - here()[0]) * half, HEAD), half)
    sources = ((k_ref, out.at[0]), (dg_ref, wide), (v_ref, out.at[1]), (q_ref, out.at[2]))
    copies = [pltpu.make_async_copy(src.at[0, :, cols], dst, sems.at[i]) for i, (src, dst) in enumerate(sources)]
    for c in copies:
        c.start()
    live = live_rows(pos_ref, slots)
    copies[0].wait()
    out[0] = mark_dead(out[0], live)
    copies[1].wait()
    out[3] = wide[...].astype(BF16)
    copies[2].wait()
    copies[3].wait()


def sib_pack(route_pos, keys, values, queries, d_gated):
    _, slots, full = keys.shape
    hbm = pl.BlockSpec(memory_space=pltpu.HBM)
    return pl.pallas_call(
        sib_pack_kernel,
        out_shape=pltpu.VMEM((4, slots, full // 2), BF16),
        in_specs=[VMEM, hbm, hbm, hbm, hbm],
        out_specs=VMEM,
        scratch_shapes=[pltpu.VMEM((slots, full // 2), F32), pltpu.SemaphoreType.DMA((4,))],
        compiler_params=params(),
        cost_estimate=cost(0, 20 * slots * full),
        name="sib_pack",
    )(route_pos, *in_hbm(keys, values, queries, d_gated))


def pair_gate_kernel(parts, live_ref, rows_x, w_ref, local, stats, out_ref, message):
    chunk = w_ref.shape[1] // parts
    slots = rows_x.shape[1]
    for i in range(2):
        total = jnp.zeros((8, slots), F32)
        for j in range(parts):
            w_rows = jnp.broadcast_to(w_ref[:, j * chunk : (j + 1) * chunk], (8, chunk)).astype(BF16)
            cols = pl.ds(pl.multiple_of((lax.axis_index("dp") ^ j) * chunk, HEAD), chunk)
            total = total + nt(w_rows, rows_x[i, :, cols])
        lanes = slice(i * slots, (i + 1) * slots)
        out_ref[:, lanes] = live_ref[:, lanes] / (1.0 + jnp.exp(-total[0:1]))
    first = here()[1] == 0
    heads = stats.shape[1]
    for i in range(3):
        message[i] = jnp.where(first, stats[i], local[i, heads:])
    message[3] = jnp.broadcast_to(out_ref[...], message.shape[1:])


def pair_gate(live, rows_x, w_full, local, stats, parts):
    _, heads, lanes = stats.shape
    return pl.pallas_call(
        functools.partial(pair_gate_kernel, parts),
        out_shape=[jax.ShapeDtypeStruct(live.shape, F32), jax.ShapeDtypeStruct((4, heads, lanes), F32)],
        in_specs=[VMEM] * 5,
        out_specs=[VMEM] * 2,
        compiler_params=params(),
        cost_estimate=cost(16 * rows_x.size, rows_x.size * 2),
        name="router_gate",
    )(live, rows_x, w_full, local, stats)


def local_mask(core, pair):
    slots = pair.shape[1] // 2
    key = lax.broadcasted_iota(jnp.int32, (slots, slots), 0)
    query = lax.broadcasted_iota(jnp.int32, (slots, slots), 1)
    causal = key <= query
    own_live = pair[0, :slots, :slots].astype(F32) < MARK_LIMIT
    sib_live = pair[0, slots:, :slots].astype(F32) < MARK_LIMIT
    own_rows = jnp.concatenate([own_live & causal, own_live & (core == 0)], axis=1)
    sib_rows = jnp.concatenate([sib_live & (core == 1), sib_live & causal], axis=1)
    return jnp.concatenate([own_rows, sib_rows], axis=0)


def kept_stats(scores, gw, kept, stats, h):
    top = jnp.max(scores, axis=0, keepdims=True)
    e = jnp.exp(scores - top).astype(BF16)
    gw = gw.astype(BF16)
    kept[0, h] = e
    kept[1, h] = gw
    e = e.astype(F32)
    stats[0, h : h + 1] = top
    stats[1, h : h + 1] = jnp.sum(e, axis=0, keepdims=True)
    stats[2, h : h + 1] = jnp.sum(e * gw.astype(F32), axis=0, keepdims=True)


def partial_stats(scores, gw, stats, h):
    top = jnp.max(scores, axis=0, keepdims=True)
    e = jnp.exp(scores - top)
    stats[0, h : h + 1] = top
    stats[1, h : h + 1] = jnp.sum(e, axis=0, keepdims=True)
    stats[2, h : h + 1] = jnp.sum(e * gw, axis=0, keepdims=True)


def local_stats_kernel(scale, pos_ref, k_ref, v_ref, q_ref, dg_ref, sib, x_ref, x_sib, stats, live, near, far, rows_x, wide, sems, x_sems):
    slots, half = sib.shape[1], sib.shape[2]
    width = half // 2
    core = here()[0]
    own, other = slice(0, slots), slice(slots, 2 * slots)
    stages = []
    for g, pair in enumerate((near, far)):
        cols = slice(g * width, (g + 1) * width)
        held = pl.ds(pl.multiple_of(core * half + g * width, HEAD), width)
        copies = [
            pltpu.make_async_copy(ref.at[0, :, held], pair.at[j, own], sems.at[8 * g + j])
            for j, ref in enumerate((k_ref, v_ref, q_ref))
        ]
        copies.append(pltpu.make_async_copy(dg_ref.at[0, :, held], wide.at[:, cols], sems.at[8 * g + 3]))
        for j in range(4):
            copies.append(pltpu.make_async_copy(sib.at[j, :, cols], pair.at[j, other], sems.at[8 * g + 4 + j]))
        for c in copies:
            c.start()
        stages.append(copies)
    x_copies = []
    depth = x_ref.shape[2] // 2
    for i, ref in enumerate((x_ref, x_sib)):
        for g in range(2):
            cols = slice(g * depth, (g + 1) * depth)
            x_copies.append(pltpu.make_async_copy(ref.at[0, :, cols], rows_x.at[i, :, cols], x_sems.at[2 * i + g]))
    for c in x_copies:
        c.start()
    rows_live = live_rows(pos_ref, slots)
    mask = None
    for g, pair in enumerate((near, far)):
        cols = slice(g * width, (g + 1) * width)
        for c in stages[g]:
            c.wait()
        pair[0, own] = mark_dead(pair[0, own], rows_live)
        pair[3, own] = wide[:, cols].astype(BF16)
        if mask is None:
            mask = local_mask(core, pair)
            marks = nt(jnp.ones((8, HEAD), BF16), pair[0, :, :HEAD])[0:1]
            live[...] = jnp.where(marks < MARK_LIMIT, 1.0, 0.0)
        for h in range(width // HEAD):
            at = slice(h * HEAD, (h + 1) * HEAD)
            scores = jnp.where(mask, nt(pair[0, :, at], pair[2, :, at]) * scale, NEG_FILL)
            partial_stats(scores, nt(pair[1, :, at], pair[3, :, at]), stats, g * width // HEAD + h)
    for c in x_copies:
        c.wait()


def local_stats(route_pos, keys, values, queries, d_gated, sib, x_routed, x_sib):
    _, slots, half = sib.shape
    heads = half // HEAD
    anywhere = pl.BlockSpec(memory_space=pl.ANY)
    return pl.pallas_call(
        functools.partial(local_stats_kernel, HEAD**-0.5),
        out_shape=[
            jax.ShapeDtypeStruct((3, heads, 2 * slots), F32),
            jax.ShapeDtypeStruct((1, 2 * slots), F32),
            pltpu.VMEM((4, 2 * slots, half // 2), BF16),
            pltpu.VMEM((4, 2 * slots, half // 2), BF16),
            pltpu.VMEM((2, slots, x_routed.shape[2]), BF16),
        ],
        in_specs=[VMEM] + [anywhere] * 7,
        out_specs=[VMEM] * 5,
        scratch_shapes=[pltpu.VMEM((slots, half), F32), pltpu.SemaphoreType.DMA((16,)), pltpu.SemaphoreType.DMA((4,))],
        compiler_params=params(),
        cost_estimate=cost(16 * slots * slots * half, 16 * slots * half, 4 * slots * slots * half // HEAD),
        name="local_stats",
    )(route_pos, *in_hbm(keys, values, queries, d_gated), sib, x_routed, x_sib)


def cross_stats_kernel(scale, near, far, straight, diag, cross, stats, kept):
    slots, width = straight.shape[1], straight.shape[2]
    chip = here()[1]
    top, bottom = slice(0, slots), slice(slots, 2 * slots)

    @pl.when(chip == 0)
    def _():
        for part in range(2):
            cross[part] = far[part]
            cross[2 + part, top] = straight[part]
            cross[2 + part, bottom] = diag[part]

    @pl.when(chip != 0)
    def _():
        for part in range(2):
            cross[part, top] = straight[part]
            cross[part, bottom] = diag[part]
            cross[2 + part] = near[2 + part]

    live = cross[0, :, :HEAD].astype(F32) < MARK_LIMIT
    mask = jnp.concatenate([live] * (2 * slots // HEAD), axis=1)
    heads = width // HEAD
    for h in range(heads):
        cols = slice(h * HEAD, (h + 1) * HEAD)
        scores = jnp.where(mask, nt(cross[0, :, cols], cross[2, :, cols]) * scale, NEG_FILL)
        kept_stats(scores, nt(cross[1, :, cols], cross[3, :, cols]), kept, stats, h)


def cross_stats(near, far, straight, diag):
    _, slots, width = straight.shape
    heads = width // HEAD
    return pl.pallas_call(
        functools.partial(cross_stats_kernel, HEAD**-0.5),
        out_shape=[
            pltpu.VMEM((4, 2 * slots, width), BF16),
            jax.ShapeDtypeStruct((3, heads, 2 * slots), F32),
            pltpu.VMEM((2, heads, 2 * slots, 2 * slots), BF16),
        ],
        in_specs=[VMEM] * 4,
        out_specs=[VMEM] * 3,
        compiler_params=params(),
        cost_estimate=cost(16 * slots * slots * width, 32 * slots * width, 4 * slots * slots * heads),
        name="cross_stats",
    )(near, far, straight, diag)


NONE = (-3e38, 0.0, 0.0)


def merge(first, second):
    top = jnp.maximum(first[0], second[0])
    a, b = jnp.exp(first[0] - top), jnp.exp(second[0] - top)
    inverse = 1.0 / (first[1] * a + second[1] * b)
    return a * inverse, (first[2] * a + second[2] * b) * inverse


def choose(flag, yes, no):
    return [jnp.where(flag, y, n) for y, n in zip(yes, no)]


def gradients(q, k, dg, e, gw, scale, factor, delta):
    weights = e * factor
    ds = (weights * ((gw - delta) * scale)).astype(BF16)
    return tn(ds, k), nn(ds, q), nn(weights.astype(BF16), dg)


def local_gradients(pair, h, mask, scale, top, factor, delta):
    cols = slice(h * HEAD, (h + 1) * HEAD)
    k, v, q, dg = [pair[i, :, cols] for i in range(4)]
    e = jnp.exp(jnp.where(mask, nt(k, q) * scale, NEG_FILL) - top)
    return gradients(q, k, dg, e, nt(v, dg), scale, factor, delta)


def near_grad_kernel(scale, pair, local, stats, gates, dq_out, own_out, sib_out, sum_out):
    slots, width = own_out.shape[1], own_out.shape[2]
    heads = width // HEAD
    first = here()[1] == 0
    near = [local[i, :heads] for i in range(3)]
    factor, delta = merge(near, choose(first, NONE, [stats[i] for i in range(3)]))
    factor = factor * gates[...]
    sum_out[...] = jnp.sum(delta, axis=0, keepdims=True)
    mask = local_mask(here()[0], pair)
    for h in range(heads):
        cols = slice(h * HEAD, (h + 1) * HEAD)
        row = slice(h, h + 1)
        dq, dk, dv = local_gradients(pair, h, mask, scale, near[0][row], factor[row], delta[row])
        dq_out[:, cols] = dq
        for i, part in enumerate((dk, dv)):
            own_out[i, :, cols] = part[:slots].astype(BF16)
            sib_out[i, :, cols] = part[slots:].astype(BF16)


def near_grad(pair, local, stats, gates):
    _, rows, width = pair.shape
    slots = rows // 2
    out = pltpu.VMEM((2, slots, width), BF16)
    return pl.pallas_call(
        functools.partial(near_grad_kernel, HEAD**-0.5),
        out_shape=[pltpu.VMEM((2 * slots, width), F32), out, out, jax.ShapeDtypeStruct(gates.shape, F32)],
        in_specs=[VMEM] * 4,
        out_specs=[VMEM] * 4,
        compiler_params=params(),
        cost_estimate=cost(20 * slots * slots * width, 40 * slots * width),
        name="near_grad",
    )(pair, local, stats, gates)


def cross_grad_kernel(scale, cross, kept, stats, local, heard, gates, near_dq, near_sum, straight, diag, dq_out, keep, final, sum_out):
    slots, width = straight.shape[1], straight.shape[2]
    heads = width // HEAD
    first = here()[1] == 0
    late = jnp.where(first, 0.0, 1.0)
    mine = [stats[i] for i in range(3)]
    other = [heard[i] for i in range(3)]
    near = [local[i, :heads] for i in range(3)]
    far = [local[i, heads:] for i in range(3)]
    factor, delta = merge(mine, choose(first, other, near))
    factor = factor * jnp.where(first, heard[3], jnp.broadcast_to(gates[...], factor.shape))
    final[0], final[1] = merge(far, choose(first, NONE, other))
    sum_out[...] = near_sum[...] + jnp.sum(final[1], axis=0, keepdims=True)
    for h in range(heads):
        cols = slice(h * HEAD, (h + 1) * HEAD)
        row = slice(h, h + 1)
        dq, dk, dv = gradients(
            cross[2, :, cols], cross[0, :, cols], cross[3, :, cols],
            kept[0, h].astype(F32), kept[1, h].astype(F32), scale, factor[row], delta[row],
        )
        dq_out[:, cols] = (near_dq[:, cols] + late * dq).astype(BF16)
        keep[0, :, cols] = dk.astype(BF16)
        keep[1, :, cols] = dv.astype(BF16)
        sent = jnp.where(first, dq, dk).astype(BF16)
        straight[0, :, cols] = sent[:slots]
        diag[0, :, cols] = sent[slots:]
        straight[1, :, cols] = dv[:slots].astype(BF16)
        diag[1, :, cols] = dv[slots:].astype(BF16)


def cross_grad(cross, kept, stats, local, heard, gates, near_dq, near_sum):
    _, rows, width = cross.shape
    slots = rows // 2
    out = pltpu.VMEM((2, slots, width), BF16)
    return pl.pallas_call(
        functools.partial(cross_grad_kernel, HEAD**-0.5),
        out_shape=[
            out,
            out,
            pltpu.VMEM((rows, width), BF16),
            pltpu.VMEM((2, rows, width), BF16),
            jax.ShapeDtypeStruct((2, width // HEAD, rows), F32),
            jax.ShapeDtypeStruct((1, rows), F32),
        ],
        in_specs=[VMEM] * 8,
        out_specs=[VMEM] * 6,
        compiler_params=params(),
        cost_estimate=cost(24 * slots * slots * width, 64 * slots * width),
        name="cross_grad",
    )(cross, kept, stats, local, heard, gates, near_dq, near_sum)


def far_grad_kernel(scale, pair, local, final, gates, keep, near_dq, near_own, near_sib, own_out, sib_out):
    slots, width = pair.shape[1] // 2, pair.shape[2]
    heads = width // HEAD
    early = jnp.where(here()[1] == 0, 1.0, 0.0)
    factor = final[0] * gates[...]
    mask = local_mask(here()[0], pair)
    own_out[0, :, :width] = near_dq[:slots]
    sib_out[0, :, :width] = near_dq[slots:]
    for i in range(2):
        own_out[1 + i, :, :width] = near_own[i]
        sib_out[1 + i, :, :width] = near_sib[i]
    for h in range(heads):
        cols = slice(width + h * HEAD, width + (h + 1) * HEAD)
        at = slice(h * HEAD, (h + 1) * HEAD)
        row = slice(h, h + 1)
        top = local[0, heads + h : heads + h + 1]
        dq, dk, dv = local_gradients(pair, h, mask, scale, top, factor[row], final[1, row])
        dk = dk + early * keep[0, :, at].astype(F32)
        dv = dv + early * keep[1, :, at].astype(F32)
        for i, part in enumerate((dq, dk, dv)):
            own_out[i, :, cols] = part[:slots].astype(BF16)
            sib_out[i, :, cols] = part[slots:].astype(BF16)


def far_grad(pair, local, final, gates, keep, near_dq, near_own, near_sib):
    _, rows, width = pair.shape
    slots, half = rows // 2, 2 * width
    out = jax.ShapeDtypeStruct((3, slots, half), BF16)
    return pl.pallas_call(
        functools.partial(far_grad_kernel, HEAD**-0.5),
        out_shape=[out, out],
        in_specs=[VMEM] * 8,
        out_specs=[VMEM] * 2,
        compiler_params=params(),
        cost_estimate=cost(20 * slots * slots * half, 40 * slots * half),
        name="far_grad",
    )(pair, local, final, gates, keep, near_dq, near_own, near_sib)


def join_kernel(own, sib, dq_out, dk_out, dv_out, waiting, low, total, in_sems, out_sems):
    slots, half = own.shape[1], own.shape[2]
    width = half // 2
    core, chip = here()
    ends = ((own, core * half), (sib, (1 - core) * half))
    loads = [
        [pltpu.make_async_copy(part.at[j], low.at[i, j], in_sems.at[3 * i + j]) for j in range(3)]
        for i, (part, _) in enumerate(ends)
    ]
    for c in loads[0] + loads[1]:
        c.start()
    stores = []
    for i, (_, start) in enumerate(ends):
        cols = pl.ds(pl.multiple_of(start, HEAD), half)
        for j, out in enumerate((dq_out, dk_out, dv_out)):
            loads[i][j].wait()
            total[i, j] = low[i, j].astype(F32)
            stores.append(pltpu.make_async_copy(total.at[i, j], out.at[0, :, cols], out_sems.at[3 * i + j]))
            stores[-1].start()
        waiting[i, 0] = jnp.where(chip == 0, total[i, 1, :, :width], total[i, 0, :, width:])
        waiting[i, 1] = total[i, 2, :, :width]
    for c in stores:
        c.wait()


def join(own, sib, shape):
    out = jax.ShapeDtypeStruct(shape, F32)
    _, slots, half = own.shape
    anywhere = pl.BlockSpec(memory_space=pl.ANY)
    hbm = pl.BlockSpec(memory_space=pltpu.HBM)
    return pl.pallas_call(
        join_kernel,
        out_shape=[out] * 3 + [pltpu.VMEM((2, 2, slots, half // 2), F32)],
        in_specs=[anywhere] * 2,
        out_specs=[hbm] * 3 + [VMEM],
        scratch_shapes=[
            pltpu.VMEM((2, 3, slots, half), BF16),
            pltpu.VMEM((2, 3, slots, half), F32),
            pltpu.SemaphoreType.DMA((6,)),
            pltpu.SemaphoreType.DMA((6,)),
        ],
        compiler_params=params(),
        cost_estimate=cost(0, 18 * out.size),
        name="join",
    )(own, sib)


def add_back_kernel(waiting, straight, diag, dq_in, dk_in, dv_in, dq_out, dk_out, dv_out, total, sems):
    width = straight.shape[2]
    core, chip = here()
    ends = ((straight, 2 * core * width), (diag, 2 * (1 - core) * width))

    def store(i, j, out, offset):
        cols = pl.ds(pl.multiple_of(ends[i][1] + offset, HEAD), width)
        copy = pltpu.make_async_copy(total.at[i, j], out.at[0, :, cols], sems.at[2 * i + j])
        copy.start()
        return copy

    for i, (back, _) in enumerate(ends):
        for j in range(2):
            total[i, j] = waiting[i, j] + back[j].astype(F32)

    @pl.when(chip == 0)
    def _():
        copies = [store(i, j, out, 0) for i in range(2) for j, out in enumerate((dk_out, dv_out))]
        for c in copies:
            c.wait()

    @pl.when(chip != 0)
    def _():
        copies = [store(i, 0, dq_out, width) for i in range(2)]
        for c in copies:
            c.wait()


def add_back(waiting, straight, diag, outs):
    hbm = pl.BlockSpec(memory_space=pltpu.HBM)
    return pl.pallas_call(
        add_back_kernel,
        out_shape=[jax.ShapeDtypeStruct(o.shape, F32) for o in outs],
        in_specs=[VMEM] * 3 + [hbm] * 3,
        out_specs=[hbm] * 3,
        scratch_shapes=[pltpu.VMEM(waiting.shape, F32), pltpu.SemaphoreType.DMA((4,))],
        input_output_aliases={3: 0, 4: 1, 5: 2},
        compiler_params=params(),
        cost_estimate=cost(0, 12 * waiting.size),
        name="add_back",
    )(waiting, straight, diag, *outs)


def pair_router_kernel(gates_ref, sum_ref, rows_x, out_ref):
    gates = gates_ref[...]
    grad = sum_ref[...] * gates * (1.0 - gates)
    high = grad.astype(BF16)
    rest = grad - high.astype(F32)
    mid = rest.astype(BF16)
    low = (rest - mid.astype(F32)).astype(BF16)
    slots = rows_x.shape[1]
    row = lax.broadcasted_iota(jnp.int32, (8, grad.shape[1]), 0)
    lhs = jnp.where(row == 0, high.astype(F32), jnp.where(row == 1, mid.astype(F32), jnp.where(row == 2, low.astype(F32), 0.0)))
    lhs = lhs.astype(BF16)
    term = jnp.sum(nn(lhs[:, :slots], rows_x[0]) + nn(lhs[:, slots:], rows_x[1]), axis=0, keepdims=True)
    parts, copies, _, chunk = out_ref.shape
    for j in range(parts):
        for i in range(copies):
            out_ref[j, i] = term[:, j * chunk : (j + 1) * chunk]


def pair_router(gates, sums, rows_x, parts, copies):
    chunk = rows_x.shape[-1] // parts
    return pl.pallas_call(
        pair_router_kernel,
        out_shape=jax.ShapeDtypeStruct((parts, copies, 1, chunk), F32),
        in_specs=[VMEM] * 3,
        out_specs=VMEM,
        compiler_params=params(),
        cost_estimate=cost(32 * rows_x.size, rows_x.size * 4),
        name="router_terms",
    )(gates, sums, rows_x)


def swap_body(route_pos, x_routed, w_router, queries, keys, values, d_gated):
    slots = queries.shape[1]
    n, ndp = lax.axis_size("ctx"), lax.axis_size("dp")

    def send(a, flip):
        return lax.ppermute(a, "ctx", [(i, i ^ flip) for i in range(n)])

    def beside(fn, *operands):
        def skip(*ops):
            return jax.tree.map(lambda o: jnp.zeros(o.shape, o.dtype), jax.eval_shape(fn, *ops))

        return lax.cond(route_pos[0, 0] >= -1, fn, skip, *operands)

    def after(value, *others):
        return lax.optimization_barrier((value, *others))[0]

    def widen(part, step, *first):
        other = lax.ppermute(part, "dp", [(i, i ^ step) for i in range(ndp)])
        return jnp.concatenate([part, after(other, *first)], axis=1)

    def exchange_phase(x_routed, w_part, theirs):
        sib, x_sib = send(theirs, 1), send(x_routed, 1)
        step = 2
        while 2 * step < ndp:
            w_part = widen(w_part, step)
            step *= 2
        return sib, x_sib, w_part

    def far_phase(*operands):
        own_out, sib_out = far_grad(*operands)
        return own_out, send(sib_out, 1)

    def router_phase(terms):
        shared = lax.all_to_all(terms.reshape(ndp * n, 1, -1), ("dp", "ctx"), 0, 0, tiled=True)
        return jnp.sum(shared, axis=0)[0] / float(ndp * n * slots // 2)

    out_s, out_d, w_part = cross_pack(route_pos, w_router, keys, values, queries, d_gated)
    in_s, in_d = send(out_s, 2), send(out_d, 3)

    theirs = sib_pack(after(route_pos, out_s), keys, values, queries, d_gated)
    if ndp > 1:
        w_part = widen(w_part, 1, theirs)
    sib, x_sib, w_part = beside(exchange_phase, x_routed, w_part, theirs)
    local, live, near, far, rows_x = local_stats(route_pos, keys, values, queries, d_gated, sib, x_routed, x_sib)
    cross, stats, kept = cross_stats(near, far, in_s, in_d)
    if ndp > 2:
        w_part = widen(w_part, ndp // 2, stats)
    gates, message = pair_gate(live, rows_x, w_part, local, stats, ndp)

    heard = send(message, 2)
    near_dq, near_own, near_sib, near_sum = near_grad(near, local, stats, gates)
    back_s, back_d, dq_low, keep, final, sums = cross_grad(
        cross, kept, stats, local, heard, gates, near_dq, near_sum
    )

    ret_s, ret_d = send(back_s, 2), send(back_d, 3)
    terms = pair_router(gates, sums, rows_x, ndp, n)
    own_out, sib_in = beside(
        far_phase, far, local, final, after(gates, terms), keep, dq_low, near_own, near_sib
    )
    *outs, waiting = join(own_out, sib_in, queries.shape)
    router_grad = beside(router_phase, after(terms, waiting))
    dq, dk, dv = add_back(waiting, ret_s, ret_d, outs)
    return dq, dk, dv, router_grad


def body(route_pos, x_routed, w_router, queries, keys, values, d_gated):
    slots, full = queries.shape[1], queries.shape[2]
    n, ndp = lax.axis_size("ctx"), lax.axis_size("dp")
    chips = n // 2
    me, dp_me = lax.axis_index("ctx"), lax.axis_index("dp")
    core = (me % 2).astype(jnp.int32).reshape(1)
    half = full // 2
    groups = GROUPS if (half // HEAD) % GROUPS == 0 else 1
    width = half // groups

    sib_pairs = [(i, i ^ 1) for i in range(n)]

    def forward_pairs(step, flip):
        return [(i, (i + 2 * step) ^ flip) for i in range(n) if i + 2 * step < n]

    def back_pairs(step, flip):
        return [(b, a) for a, b in forward_pairs(step, flip)]

    def to_sib(a):
        return lax.ppermute(a, "ctx", sib_pairs)

    links = [(step, flip) for step in range(1, chips) for flip in (0, 1)]

    w_row = w_router.reshape(1, -1)
    w_parts = [w_row] + [
        lax.ppermute(w_row, "dp", [(i, (i + s) % ndp) for i in range(ndp)]) for s in range(1, ndp)
    ]
    live = (route_pos >= 0).astype(jnp.int32)
    lives = [live, to_sib(live)] + [lax.ppermute(live, "ctx", forward_pairs(*link)) for link in links]
    live_all = jnp.concatenate(lives, axis=0)

    kv_mine, kv_theirs = pack(core, keys, values, groups, width)
    kv_far = [
        [lax.ppermute((kv_theirs if flip else kv_mine)[g], "ctx", forward_pairs(step, flip)) for step, flip in links]
        for g in range(groups)
    ]
    q_mine, q_theirs = pack(core, queries, d_gated, groups, width)
    kv_sib = [to_sib(a) for a in kv_theirs]
    q_sib = [to_sib(a) for a in q_theirs]

    offsets = ((dp_me - jnp.arange(ndp)) % ndp).astype(jnp.int32)
    gate = router_gate(offsets, route_pos, x_routed, w_parts)
    gates = (gate, to_sib(gate))

    accs = (jnp.zeros((1, slots), F32), jnp.zeros((1, slots), F32))
    dq_own, sib_in, kv_own, back = [], [], [], []
    for g in range(groups):
        dq, sib_out, kv_local, kv_remote, accs = attention(
            core, live_all, gates, accs, q_mine[g], q_sib[g], [kv_mine[g], kv_sib[g], *kv_far[g]]
        )
        back.append([lax.ppermute(a, "ctx", back_pairs(*link)) for a, link in zip(kv_remote, links)])
        sib_in.append(to_sib(sib_out))
        dq_own.append(dq)
        kv_own.append(kv_local)

    targets = ((dp_me + jnp.arange(ndp)) % ndp).astype(jnp.int32)
    terms = router_terms(targets, gate, accs[0], to_sib(accs[1]), x_routed, ndp)
    mine = terms[0]
    for s in range(1, ndp):
        mine = mine + lax.ppermute(terms[s], "dp", [(i, (i + s) % ndp) for i in range(ndp)])
    total = mine
    for s in range(1, n):
        total = total + lax.ppermute(mine, "ctx", [(i, (i + s) % n) for i in range(n)])
    router_grad = total[0] / float(ndp * n * slots // 2)

    dq, dk, dv = combine(core, dq_own, sib_in, kv_own, back, queries.shape)
    return dq, dk, dv, router_grad


def solution(mesh):
    placed = (
        P("dp", "ctx"),
        P("dp", "ctx", None),
        P("dp"),
        P("dp", "ctx", None),
        P("dp", "ctx", None),
        P("dp", "ctx", None),
        P("dp", "ctx", None),
    )
    ndp = mesh.shape["dp"]
    paired = mesh.shape["ctx"] == 4 and ndp & (ndp - 1) == 0
    return jax.shard_map(
        swap_body if paired else body,
        mesh=mesh,
        in_specs=placed,
        out_specs=(P("dp", "ctx", None), P("dp", "ctx", None), P("dp", "ctx", None), P("dp")),
        check_vma=False,
    )
```

```python
import functools

import jax
import jax.numpy as jnp
from jax import lax
from jax.experimental import pallas as pl
from jax.experimental.pallas import tpu as pltpu
from jax.sharding import PartitionSpec as P

HEAD = 128
GROUPS = 4
NEG_FILL = -1e30
MIB = 1024 * 1024
BF16 = jnp.bfloat16
F32 = jnp.float32

VMEM = pl.BlockSpec(memory_space=pltpu.VMEM)
SMEM = pl.BlockSpec(memory_space=pltpu.SMEM)


def params(mib=16):
    return pltpu.CompilerParams(vmem_limit_bytes=mib * MIB)


def cost(flops, nbytes, exps=0):
    return pl.CostEstimate(flops=1, bytes_accessed=1, transcendentals=0)


def in_hbm(*arrays):
    return [pltpu.with_memory_space_constraint(a, pltpu.HBM) for a in arrays]


def nt(a, b):
    return lax.dot_general(a, b, (((1,), (1,)), ((), ())), preferred_element_type=F32)


def nn(a, b):
    return lax.dot_general(a, b, (((1,), (0,)), ((), ())), preferred_element_type=F32)


def tn(a, b):
    return lax.dot_general(a, b, (((0,), (0,)), ((), ())), preferred_element_type=F32)


def pack_kernel(groups, width, core_ref, first_ref, second_ref, *outs):
    half = first_ref.shape[-1] // 2
    core = core_ref[0]
    for side in range(2):
        base = (core if side == 0 else 1 - core) * half
        for g in range(groups):
            out = outs[side * groups + g]
            cols = pl.ds(pl.multiple_of(base + g * width, HEAD), width)
            out[0] = first_ref[0, :, cols].astype(BF16)
            out[1] = second_ref[0, :, cols].astype(BF16)


def pack(core, first, second, groups, width):
    slots = first.shape[1]
    out = jax.ShapeDtypeStruct((2, slots, width), BF16)
    res = pl.pallas_call(
        functools.partial(pack_kernel, groups, width),
        out_shape=[out] * (2 * groups),
        in_specs=[SMEM, VMEM, VMEM],
        out_specs=[VMEM] * (2 * groups),
        compiler_params=params(),
        cost_estimate=cost(0, 2 * first.size * 4),
        name="pack",
    )(core, first, second)
    return res[:groups], res[groups:]


def gate_kernel(parts, offset_ref, pos_ref, x_ref, *refs):
    w_refs, out_ref = refs[:parts], refs[parts]
    chunk = w_refs[0].shape[-1]
    total = jnp.zeros((8, x_ref.shape[1]), F32)
    for s in range(parts):
        cols = pl.ds(pl.multiple_of(offset_ref[s] * chunk, HEAD), chunk)
        w_rows = jnp.broadcast_to(w_refs[s][...].astype(F32), (8, chunk)).astype(BF16)
        total = total + nt(w_rows, x_ref[0, :, cols])
    gate = 1.0 / (1.0 + jnp.exp(-total[0:1]))
    out_ref[...] = jnp.where(pos_ref[...] >= 0, gate, 0.0)


def router_gate(offsets, route_pos, x_routed, w_parts):
    parts = len(w_parts)
    return pl.pallas_call(
        functools.partial(gate_kernel, parts),
        out_shape=jax.ShapeDtypeStruct(route_pos.shape, F32),
        in_specs=[SMEM] + [VMEM] * (2 + parts),
        out_specs=VMEM,
        compiler_params=params(),
        cost_estimate=cost(16 * x_routed.size, x_routed.size * 2),
        name="router_gate",
    )(offsets, route_pos, x_routed, *w_parts)


def attention_kernel(remote, scale, core_ref, live_ref, gate_own, gate_sib, acc_own, acc_sib, q_own, q_sib, *refs):
    chunks = 2 + remote
    kv = refs[:chunks]
    outs = refs[chunks:]
    dq_own, sib_out, kv_own = outs[:3]
    kv_remote = outs[3 : 3 + remote]
    sum_own, sum_sib = outs[3 + remote :]
    slots, width = q_own.shape[1], q_own.shape[2]
    core = core_ref[0]
    key = lax.broadcasted_iota(jnp.int32, (slots, slots), 0)
    query = lax.broadcasted_iota(jnp.int32, (slots, slots), 1)
    counts = [jnp.sum(live_ref[i : i + 1], axis=1, keepdims=True) for i in range(chunks)]
    lives = [key < counts[i] for i in range(chunks)]
    own_later = core == 1
    bias_rows = []
    for i in range(chunks):
        live = lives[i]
        if i == 0:
            pair = (live & (key <= query), live & jnp.logical_not(own_later))
        elif i == 1:
            pair = (live & own_later, live & (key <= query))
        else:
            pair = (live, live)
        bias_rows.append(jnp.concatenate([jnp.where(p, 0.0, NEG_FILL) for p in pair], axis=1))
    bias = jnp.concatenate(bias_rows, axis=0)
    gates = jnp.concatenate([gate_own[...], gate_sib[...]], axis=1)
    total = jnp.zeros((1, 2 * slots), F32)
    for h in range(width // HEAD):
        cols = slice(h * HEAD, (h + 1) * HEAD)
        q = jnp.concatenate([q_own[0, :, cols], q_sib[0, :, cols]], axis=0)
        dg = jnp.concatenate([q_own[1, :, cols], q_sib[1, :, cols]], axis=0)
        k = jnp.concatenate([r[0, :, cols] for r in kv], axis=0)
        v = jnp.concatenate([r[1, :, cols] for r in kv], axis=0)
        scores = nt(k, q) * scale + bias
        top = jnp.max(scores, axis=0, keepdims=True)
        e = jnp.exp(scores - top)
        inverse = 1.0 / jnp.sum(e, axis=0, keepdims=True)
        gw = nt(v, dg)
        delta = jnp.sum(e * gw, axis=0, keepdims=True) * inverse
        total = total + delta
        weights = e * (inverse * gates)
        dv = nn(weights.astype(BF16), dg)
        ds = (weights * ((gw - delta) * scale)).astype(BF16)
        dk = nn(ds, q)
        dq = tn(ds, k)
        dq_own[:, cols] = dq[:slots].astype(dq_own.dtype)
        sib_out[0, :, cols] = dq[slots:].astype(BF16)
        kv_own[0, :, cols] = dk[:slots].astype(BF16)
        kv_own[1, :, cols] = dv[:slots].astype(BF16)
        sib_out[1, :, cols] = dk[slots : 2 * slots].astype(BF16)
        sib_out[2, :, cols] = dv[slots : 2 * slots].astype(BF16)
        for i in range(remote):
            rows = slice((2 + i) * slots, (3 + i) * slots)
            kv_remote[i][0, :, cols] = dk[rows].astype(BF16)
            kv_remote[i][1, :, cols] = dv[rows].astype(BF16)
    sum_own[...] = acc_own[...] + total[:, :slots]
    sum_sib[...] = acc_sib[...] + total[:, slots:]


def attention(core, live, gates, accs, q_own, q_sib, kv):
    remote = len(kv) - 2
    _, slots, width = q_own.shape
    pair = jax.ShapeDtypeStruct((2, slots, width), BF16)
    row = jax.ShapeDtypeStruct((1, slots), F32)
    outs = [
        jax.ShapeDtypeStruct((slots, width), BF16),
        jax.ShapeDtypeStruct((3, slots, width), BF16),
        pair,
        *([pair] * remote),
        row,
        row,
    ]
    keys = (2 + remote) * slots
    res = pl.pallas_call(
        functools.partial(attention_kernel, remote, HEAD**-0.5),
        out_shape=outs,
        in_specs=[SMEM] + [VMEM] * (7 + len(kv)),
        out_specs=[VMEM] * len(outs),
        compiler_params=params(48),
        cost_estimate=cost(20 * slots * keys * width, 8 * keys * width + 20 * slots * width, 2 * slots * keys * width // HEAD),
        name="attention",
    )(core, live, *gates, *accs, q_own, q_sib, *kv)
    return res[0], res[1], res[2], res[3 : 3 + remote], (res[3 + remote], res[4 + remote])


def combine_kernel(groups, width, remote, core_ref, *refs):
    dq_own, sib, kv_own = refs[:groups], refs[groups : 2 * groups], refs[2 * groups : 3 * groups]
    back = refs[3 * groups : 3 * groups + groups * remote]
    dq_out, dk_out, dv_out = refs[3 * groups + groups * remote :]
    half = groups * width
    core = core_ref[0]
    for g in range(groups):
        own = pl.ds(pl.multiple_of(core * half + g * width, HEAD), width)
        other = pl.ds(pl.multiple_of((1 - core) * half + g * width, HEAD), width)
        dq_out[0, :, own] = dq_own[g][...].astype(F32)
        dq_out[0, :, other] = sib[g][0].astype(F32)
        for i, out in enumerate((dk_out, dv_out)):
            mine = kv_own[g][i].astype(F32)
            theirs = sib[g][1 + i].astype(F32)
            for r in range(remote):
                part = back[g * remote + r][i].astype(F32)
                if r % 2 == 0:
                    mine = mine + part
                else:
                    theirs = theirs + part
            out[0, :, own] = mine
            out[0, :, other] = theirs


def combine(core, dq_own, sib, kv_own, back, shape):
    groups = len(dq_own)
    remote = len(back[0])
    out = jax.ShapeDtypeStruct(shape, F32)
    flat = [*dq_own, *sib, *kv_own, *(b for group in back for b in group)]
    return pl.pallas_call(
        functools.partial(combine_kernel, groups, dq_own[0].shape[-1], remote),
        out_shape=[out] * 3,
        in_specs=[SMEM] + [VMEM] * len(flat),
        out_specs=[VMEM] * 3,
        compiler_params=params(48),
        cost_estimate=cost(0, 3 * out.size * 6),
        name="combine",
    )(core, *flat)


def router_kernel(parts, target_ref, gate_ref, own_ref, sib_ref, x_ref, *outs):
    gate = gate_ref[...]
    grad = (own_ref[...] + sib_ref[...]) * gate * (1.0 - gate)
    high = grad.astype(BF16)
    rest = grad - high.astype(F32)
    mid = rest.astype(BF16)
    low = (rest - mid.astype(F32)).astype(BF16)
    row = lax.broadcasted_iota(jnp.int32, (8, grad.shape[1]), 0)
    lhs = jnp.where(row == 0, high.astype(F32), jnp.where(row == 1, mid.astype(F32), jnp.where(row == 2, low.astype(F32), 0.0)))
    lhs = lhs.astype(BF16)
    chunk = outs[0].shape[-1]
    for s in range(parts):
        cols = pl.ds(pl.multiple_of(target_ref[s] * chunk, HEAD), chunk)
        outs[s][...] = jnp.sum(nn(lhs, x_ref[0, :, cols]), axis=0, keepdims=True)


def router_terms(targets, gate, own, sib, x_routed, parts):
    chunk = x_routed.shape[-1] // parts
    return pl.pallas_call(
        functools.partial(router_kernel, parts),
        out_shape=[jax.ShapeDtypeStruct((1, chunk), F32)] * parts,
        in_specs=[SMEM] + [VMEM] * 4,
        out_specs=[VMEM] * parts,
        compiler_params=params(),
        cost_estimate=cost(16 * x_routed.size, x_routed.size * 2),
        name="router_terms",
    )(targets, gate, own, sib, x_routed)


def here():
    me = lax.axis_index("ctx")
    return lax.rem(me, 2), lax.div(me, 2)


MARK = 2.0**60
MARK_LIMIT = 2.0**50


def live_rows(pos_ref, slots):
    count = jnp.sum((pos_ref[...] >= 0).astype(jnp.int32), axis=1, keepdims=True)
    return lax.broadcasted_iota(jnp.int32, (slots, HEAD), 0) < count


def mark_dead(keys, live):
    width = keys.shape[-1]
    mask = jnp.concatenate([live] * (width // HEAD), axis=1)
    return jnp.where(mask, keys.astype(F32), MARK).astype(BF16)


def cross_pack_kernel(pos_any, w_any, k_ref, v_ref, q_ref, dg_ref, straight, diag, w_out, wide, pos_ref, w_ref, sems):
    small = [pltpu.make_async_copy(pos_any, pos_ref, sems.at[4]), pltpu.make_async_copy(w_any, w_ref, sems.at[5])]
    for c in small:
        c.start()
    slots, width = straight.shape[1], straight.shape[2]
    half = k_ref.shape[-1] // 2
    core, chip = here()
    ends = ((straight, core * half), (diag, (1 - core) * half))

    def copies(first, second, targets, offset):
        out = []
        for i, (end, start) in enumerate(ends):
            cols = pl.ds(pl.multiple_of(start + offset, HEAD), width)
            out.append(pltpu.make_async_copy(first.at[0, :, cols], end.at[0], sems.at[2 * i]))
            out.append(pltpu.make_async_copy(second.at[0, :, cols], targets[i], sems.at[2 * i + 1]))
        for c in out:
            c.start()
        for c in out:
            c.wait()

    @pl.when(chip == 0)
    def _():
        copies(k_ref, v_ref, (straight.at[1], diag.at[1]), 0)
        small[0].wait()
        live = live_rows(pos_ref, slots)
        for end, _ in ends:
            end[0] = mark_dead(end[0], live)

    @pl.when(chip != 0)
    def _():
        copies(q_ref, dg_ref, (wide.at[0], wide.at[1]), width)
        small[0].wait()
        for i, (end, _) in enumerate(ends):
            end[1] = wide[i].astype(BF16)

    small[1].wait()
    w_out[...] = w_ref[...].astype(F32).reshape(w_out.shape)


def cross_pack(route_pos, w_router, keys, values, queries, d_gated):
    _, slots, full = keys.shape
    cross = pltpu.VMEM((2, slots, full // 4), BF16)
    hbm = pl.BlockSpec(memory_space=pltpu.HBM)
    return pl.pallas_call(
        cross_pack_kernel,
        out_shape=[cross, cross, jax.ShapeDtypeStruct((1, w_router.shape[0]), F32)],
        in_specs=[hbm] * 6,
        out_specs=[VMEM] * 3,
        scratch_shapes=[
            pltpu.VMEM((2, slots, full // 4), F32),
            pltpu.VMEM(route_pos.shape, jnp.int32),
            pltpu.VMEM(w_router.shape, BF16),
            pltpu.SemaphoreType.DMA((6,)),
        ],
        compiler_params=params(),
        cost_estimate=cost(0, 10 * slots * full),
        name="cross_pack",
    )(*in_hbm(route_pos, w_router, keys, values, queries, d_gated))


def sib_pack_kernel(pos_ref, k_ref, v_ref, q_ref, dg_ref, out, wide, sems):
    slots, half = out.shape[1], out.shape[2]
    cols = pl.ds(pl.multiple_of((1 - here()[0]) * half, HEAD), half)
    sources = ((k_ref, out.at[0]), (dg_ref, wide), (v_ref, out.at[1]), (q_ref, out.at[2]))
    copies = [pltpu.make_async_copy(src.at[0, :, cols], dst, sems.at[i]) for i, (src, dst) in enumerate(sources)]
    for c in copies:
        c.start()
    live = live_rows(pos_ref, slots)
    copies[0].wait()
    out[0] = mark_dead(out[0], live)
    copies[1].wait()
    out[3] = wide[...].astype(BF16)
    copies[2].wait()
    copies[3].wait()


def sib_pack(route_pos, keys, values, queries, d_gated):
    _, slots, full = keys.shape
    hbm = pl.BlockSpec(memory_space=pltpu.HBM)
    return pl.pallas_call(
        sib_pack_kernel,
        out_shape=pltpu.VMEM((4, slots, full // 2), BF16),
        in_specs=[VMEM, hbm, hbm, hbm, hbm],
        out_specs=VMEM,
        scratch_shapes=[pltpu.VMEM((slots, full // 2), F32), pltpu.SemaphoreType.DMA((4,))],
        compiler_params=params(),
        cost_estimate=cost(0, 20 * slots * full),
        name="sib_pack",
    )(route_pos, *in_hbm(keys, values, queries, d_gated))


def pair_gate_kernel(parts, live_ref, rows_x, w_ref, local, stats, out_ref, message):
    chunk = w_ref.shape[1] // parts
    slots = rows_x.shape[1]
    for i in range(2):
        total = jnp.zeros((8, slots), F32)
        for j in range(parts):
            w_rows = jnp.broadcast_to(w_ref[:, j * chunk : (j + 1) * chunk], (8, chunk)).astype(BF16)
            cols = pl.ds(pl.multiple_of((lax.axis_index("dp") ^ j) * chunk, HEAD), chunk)
            total = total + nt(w_rows, rows_x[i, :, cols])
        lanes = slice(i * slots, (i + 1) * slots)
        out_ref[:, lanes] = live_ref[:, lanes] / (1.0 + jnp.exp(-total[0:1]))
    first = here()[1] == 0
    heads = stats.shape[1]
    for i in range(3):
        message[i] = jnp.where(first, stats[i], local[i, heads:])
    message[3] = jnp.broadcast_to(out_ref[...], message.shape[1:])


def pair_gate(live, rows_x, w_full, local, stats, parts):
    _, heads, lanes = stats.shape
    return pl.pallas_call(
        functools.partial(pair_gate_kernel, parts),
        out_shape=[jax.ShapeDtypeStruct(live.shape, F32), jax.ShapeDtypeStruct((4, heads, lanes), F32)],
        in_specs=[VMEM] * 5,
        out_specs=[VMEM] * 2,
        compiler_params=params(),
        cost_estimate=cost(16 * rows_x.size, rows_x.size * 2),
        name="router_gate",
    )(live, rows_x, w_full, local, stats)


def local_mask(core, pair):
    slots = pair.shape[1] // 2
    key = lax.broadcasted_iota(jnp.int32, (slots, slots), 0)
    query = lax.broadcasted_iota(jnp.int32, (slots, slots), 1)
    causal = key <= query
    own_live = pair[0, :slots, :slots].astype(F32) < MARK_LIMIT
    sib_live = pair[0, slots:, :slots].astype(F32) < MARK_LIMIT
    own_rows = jnp.concatenate([own_live & causal, own_live & (core == 0)], axis=1)
    sib_rows = jnp.concatenate([sib_live & (core == 1), sib_live & causal], axis=1)
    return jnp.concatenate([own_rows, sib_rows], axis=0)


def kept_stats(scores, gw, kept, stats, h):
    top = jnp.max(scores, axis=0, keepdims=True)
    e = jnp.exp(scores - top).astype(BF16)
    gw = gw.astype(BF16)
    kept[0, h] = e
    kept[1, h] = gw
    e = e.astype(F32)
    stats[0, h : h + 1] = top
    stats[1, h : h + 1] = jnp.sum(e, axis=0, keepdims=True)
    stats[2, h : h + 1] = jnp.sum(e * gw.astype(F32), axis=0, keepdims=True)


def partial_stats(scores, gw, stats, h):
    top = jnp.max(scores, axis=0, keepdims=True)
    e = jnp.exp(scores - top)
    stats[0, h : h + 1] = top
    stats[1, h : h + 1] = jnp.sum(e, axis=0, keepdims=True)
    stats[2, h : h + 1] = jnp.sum(e * gw, axis=0, keepdims=True)


def local_stats_kernel(scale, pos_ref, k_ref, v_ref, q_ref, dg_ref, sib, x_ref, x_sib, stats, live, near, far, rows_x, wide, sems, x_sems):
    slots, half = sib.shape[1], sib.shape[2]
    width = half // 2
    core = here()[0]
    own, other = slice(0, slots), slice(slots, 2 * slots)
    stages = []
    for g, pair in enumerate((near, far)):
        cols = slice(g * width, (g + 1) * width)
        held = pl.ds(pl.multiple_of(core * half + g * width, HEAD), width)
        copies = [
            pltpu.make_async_copy(ref.at[0, :, held], pair.at[j, own], sems.at[8 * g + j])
            for j, ref in enumerate((k_ref, v_ref, q_ref))
        ]
        copies.append(pltpu.make_async_copy(dg_ref.at[0, :, held], wide.at[:, cols], sems.at[8 * g + 3]))
        for j in range(4):
            copies.append(pltpu.make_async_copy(sib.at[j, :, cols], pair.at[j, other], sems.at[8 * g + 4 + j]))
        for c in copies:
            c.start()
        stages.append(copies)
    x_copies = []
    depth = x_ref.shape[2] // 2
    for i, ref in enumerate((x_ref, x_sib)):
        for g in range(2):
            cols = slice(g * depth, (g + 1) * depth)
            x_copies.append(pltpu.make_async_copy(ref.at[0, :, cols], rows_x.at[i, :, cols], x_sems.at[2 * i + g]))
    for c in x_copies:
        c.start()
    rows_live = live_rows(pos_ref, slots)
    mask = None
    for g, pair in enumerate((near, far)):
        cols = slice(g * width, (g + 1) * width)
        for c in stages[g]:
            c.wait()
        pair[0, own] = mark_dead(pair[0, own], rows_live)
        pair[3, own] = wide[:, cols].astype(BF16)
        if mask is None:
            mask = local_mask(core, pair)
            marks = nt(jnp.ones((8, HEAD), BF16), pair[0, :, :HEAD])[0:1]
            live[...] = jnp.where(marks < MARK_LIMIT, 1.0, 0.0)
        for h in range(width // HEAD):
            at = slice(h * HEAD, (h + 1) * HEAD)
            scores = jnp.where(mask, nt(pair[0, :, at], pair[2, :, at]) * scale, NEG_FILL)
            partial_stats(scores, nt(pair[1, :, at], pair[3, :, at]), stats, g * width // HEAD + h)
    for c in x_copies:
        c.wait()


def local_stats(route_pos, keys, values, queries, d_gated, sib, x_routed, x_sib):
    _, slots, half = sib.shape
    heads = half // HEAD
    anywhere = pl.BlockSpec(memory_space=pl.ANY)
    return pl.pallas_call(
        functools.partial(local_stats_kernel, HEAD**-0.5),
        out_shape=[
            jax.ShapeDtypeStruct((3, heads, 2 * slots), F32),
            jax.ShapeDtypeStruct((1, 2 * slots), F32),
            pltpu.VMEM((4, 2 * slots, half // 2), BF16),
            pltpu.VMEM((4, 2 * slots, half // 2), BF16),
            pltpu.VMEM((2, slots, x_routed.shape[2]), BF16),
        ],
        in_specs=[VMEM] + [anywhere] * 7,
        out_specs=[VMEM] * 5,
        scratch_shapes=[pltpu.VMEM((slots, half), F32), pltpu.SemaphoreType.DMA((16,)), pltpu.SemaphoreType.DMA((4,))],
        compiler_params=params(),
        cost_estimate=cost(16 * slots * slots * half, 16 * slots * half, 4 * slots * slots * half // HEAD),
        name="local_stats",
    )(route_pos, *in_hbm(keys, values, queries, d_gated), sib, x_routed, x_sib)


def cross_stats_kernel(scale, near, far, straight, diag, cross, stats, kept):
    slots, width = straight.shape[1], straight.shape[2]
    chip = here()[1]
    top, bottom = slice(0, slots), slice(slots, 2 * slots)

    @pl.when(chip == 0)
    def _():
        for part in range(2):
            cross[part] = far[part]
            cross[2 + part, top] = straight[part]
            cross[2 + part, bottom] = diag[part]

    @pl.when(chip != 0)
    def _():
        for part in range(2):
            cross[part, top] = straight[part]
            cross[part, bottom] = diag[part]
            cross[2 + part] = near[2 + part]

    live = cross[0, :, :HEAD].astype(F32) < MARK_LIMIT
    mask = jnp.concatenate([live] * (2 * slots // HEAD), axis=1)
    heads = width // HEAD
    for h in range(heads):
        cols = slice(h * HEAD, (h + 1) * HEAD)
        scores = jnp.where(mask, nt(cross[0, :, cols], cross[2, :, cols]) * scale, NEG_FILL)
        kept_stats(scores, nt(cross[1, :, cols], cross[3, :, cols]), kept, stats, h)


def cross_stats(near, far, straight, diag):
    _, slots, width = straight.shape
    heads = width // HEAD
    return pl.pallas_call(
        functools.partial(cross_stats_kernel, HEAD**-0.5),
        out_shape=[
            pltpu.VMEM((4, 2 * slots, width), BF16),
            jax.ShapeDtypeStruct((3, heads, 2 * slots), F32),
            pltpu.VMEM((2, heads, 2 * slots, 2 * slots), BF16),
        ],
        in_specs=[VMEM] * 4,
        out_specs=[VMEM] * 3,
        compiler_params=params(),
        cost_estimate=cost(16 * slots * slots * width, 32 * slots * width, 4 * slots * slots * heads),
        name="cross_stats",
    )(near, far, straight, diag)


NONE = (-3e38, 0.0, 0.0)


def merge(first, second):
    top = jnp.maximum(first[0], second[0])
    a, b = jnp.exp(first[0] - top), jnp.exp(second[0] - top)
    inverse = 1.0 / (first[1] * a + second[1] * b)
    return a * inverse, (first[2] * a + second[2] * b) * inverse


def choose(flag, yes, no):
    return [jnp.where(flag, y, n) for y, n in zip(yes, no)]


def gradients(q, k, dg, e, gw, scale, factor, delta):
    weights = e * factor
    ds = (weights * ((gw - delta) * scale)).astype(BF16)
    return tn(ds, k), nn(ds, q), nn(weights.astype(BF16), dg)


def local_gradients(pair, h, mask, scale, top, factor, delta):
    cols = slice(h * HEAD, (h + 1) * HEAD)
    k, v, q, dg = [pair[i, :, cols] for i in range(4)]
    e = jnp.exp(jnp.where(mask, nt(k, q) * scale, NEG_FILL) - top)
    return gradients(q, k, dg, e, nt(v, dg), scale, factor, delta)


def near_grad_kernel(scale, pair, local, stats, gates, dq_out, own_out, sib_out, sum_out):
    slots, width = own_out.shape[1], own_out.shape[2]
    heads = width // HEAD
    first = here()[1] == 0
    near = [local[i, :heads] for i in range(3)]
    factor, delta = merge(near, choose(first, NONE, [stats[i] for i in range(3)]))
    factor = factor * gates[...]
    sum_out[...] = jnp.sum(delta, axis=0, keepdims=True)
    mask = local_mask(here()[0], pair)
    for h in range(heads):
        cols = slice(h * HEAD, (h + 1) * HEAD)
        row = slice(h, h + 1)
        dq, dk, dv = local_gradients(pair, h, mask, scale, near[0][row], factor[row], delta[row])
        dq_out[:, cols] = dq
        for i, part in enumerate((dk, dv)):
            own_out[i, :, cols] = part[:slots].astype(BF16)
            sib_out[i, :, cols] = part[slots:].astype(BF16)


def near_grad(pair, local, stats, gates):
    _, rows, width = pair.shape
    slots = rows // 2
    out = pltpu.VMEM((2, slots, width), BF16)
    return pl.pallas_call(
        functools.partial(near_grad_kernel, HEAD**-0.5),
        out_shape=[pltpu.VMEM((2 * slots, width), F32), out, out, jax.ShapeDtypeStruct(gates.shape, F32)],
        in_specs=[VMEM] * 4,
        out_specs=[VMEM] * 4,
        compiler_params=params(),
        cost_estimate=cost(20 * slots * slots * width, 40 * slots * width),
        name="near_grad",
    )(pair, local, stats, gates)


def cross_grad_kernel(scale, cross, kept, stats, local, heard, gates, near_dq, near_sum, straight, diag, dq_out, keep, final, sum_out):
    slots, width = straight.shape[1], straight.shape[2]
    heads = width // HEAD
    first = here()[1] == 0
    late = jnp.where(first, 0.0, 1.0)
    mine = [stats[i] for i in range(3)]
    other = [heard[i] for i in range(3)]
    near = [local[i, :heads] for i in range(3)]
    far = [local[i, heads:] for i in range(3)]
    factor, delta = merge(mine, choose(first, other, near))
    factor = factor * jnp.where(first, heard[3], jnp.broadcast_to(gates[...], factor.shape))
    final[0], final[1] = merge(far, choose(first, NONE, other))
    sum_out[...] = near_sum[...] + jnp.sum(final[1], axis=0, keepdims=True)
    for h in range(heads):
        cols = slice(h * HEAD, (h + 1) * HEAD)
        row = slice(h, h + 1)
        dq, dk, dv = gradients(
            cross[2, :, cols], cross[0, :, cols], cross[3, :, cols],
            kept[0, h].astype(F32), kept[1, h].astype(F32), scale, factor[row], delta[row],
        )
        dq_out[:, cols] = (near_dq[:, cols] + late * dq).astype(BF16)
        keep[0, :, cols] = dk.astype(BF16)
        keep[1, :, cols] = dv.astype(BF16)
        sent = jnp.where(first, dq, dk).astype(BF16)
        straight[0, :, cols] = sent[:slots]
        diag[0, :, cols] = sent[slots:]
        straight[1, :, cols] = dv[:slots].astype(BF16)
        diag[1, :, cols] = dv[slots:].astype(BF16)


def cross_grad(cross, kept, stats, local, heard, gates, near_dq, near_sum):
    _, rows, width = cross.shape
    slots = rows // 2
    out = pltpu.VMEM((2, slots, width), BF16)
    return pl.pallas_call(
        functools.partial(cross_grad_kernel, HEAD**-0.5),
        out_shape=[
            out,
            out,
            pltpu.VMEM((rows, width), BF16),
            pltpu.VMEM((2, rows, width), BF16),
            jax.ShapeDtypeStruct((2, width // HEAD, rows), F32),
            jax.ShapeDtypeStruct((1, rows), F32),
        ],
        in_specs=[VMEM] * 8,
        out_specs=[VMEM] * 6,
        compiler_params=params(),
        cost_estimate=cost(24 * slots * slots * width, 64 * slots * width),
        name="cross_grad",
    )(cross, kept, stats, local, heard, gates, near_dq, near_sum)


def far_grad_kernel(scale, pair, local, final, gates, keep, near_dq, near_own, near_sib, own_out, sib_out):
    slots, width = pair.shape[1] // 2, pair.shape[2]
    heads = width // HEAD
    early = jnp.where(here()[1] == 0, 1.0, 0.0)
    factor = final[0] * gates[...]
    mask = local_mask(here()[0], pair)
    own_out[0, :, :width] = near_dq[:slots]
    sib_out[0, :, :width] = near_dq[slots:]
    for i in range(2):
        own_out[1 + i, :, :width] = near_own[i]
        sib_out[1 + i, :, :width] = near_sib[i]
    for h in range(heads):
        cols = slice(width + h * HEAD, width + (h + 1) * HEAD)
        at = slice(h * HEAD, (h + 1) * HEAD)
        row = slice(h, h + 1)
        top = local[0, heads + h : heads + h + 1]
        dq, dk, dv = local_gradients(pair, h, mask, scale, top, factor[row], final[1, row])
        dk = dk + early * keep[0, :, at].astype(F32)
        dv = dv + early * keep[1, :, at].astype(F32)
        for i, part in enumerate((dq, dk, dv)):
            own_out[i, :, cols] = part[:slots].astype(BF16)
            sib_out[i, :, cols] = part[slots:].astype(BF16)


def far_grad(pair, local, final, gates, keep, near_dq, near_own, near_sib):
    _, rows, width = pair.shape
    slots, half = rows // 2, 2 * width
    out = jax.ShapeDtypeStruct((3, slots, half), BF16)
    return pl.pallas_call(
        functools.partial(far_grad_kernel, HEAD**-0.5),
        out_shape=[out, out],
        in_specs=[VMEM] * 8,
        out_specs=[VMEM] * 2,
        compiler_params=params(),
        cost_estimate=cost(20 * slots * slots * half, 40 * slots * half),
        name="far_grad",
    )(pair, local, final, gates, keep, near_dq, near_own, near_sib)


def join_kernel(own, sib, dq_out, dk_out, dv_out, waiting, low, total, in_sems, out_sems):
    slots, half = own.shape[1], own.shape[2]
    width = half // 2
    core, chip = here()
    ends = ((own, core * half), (sib, (1 - core) * half))
    loads = [
        [pltpu.make_async_copy(part.at[j], low.at[i, j], in_sems.at[3 * i + j]) for j in range(3)]
        for i, (part, _) in enumerate(ends)
    ]
    for c in loads[0] + loads[1]:
        c.start()
    stores = []
    for i, (_, start) in enumerate(ends):
        cols = pl.ds(pl.multiple_of(start, HEAD), half)
        for j, out in enumerate((dq_out, dk_out, dv_out)):
            loads[i][j].wait()
            total[i, j] = low[i, j].astype(F32)
            stores.append(pltpu.make_async_copy(total.at[i, j], out.at[0, :, cols], out_sems.at[3 * i + j]))
            stores[-1].start()
        waiting[i, 0] = jnp.where(chip == 0, total[i, 1, :, :width], total[i, 0, :, width:])
        waiting[i, 1] = total[i, 2, :, :width]
    for c in stores:
        c.wait()


def join(own, sib, shape):
    out = pltpu.HBM(shape, F32)
    _, slots, half = own.shape
    anywhere = pl.BlockSpec(memory_space=pl.ANY)
    hbm = pl.BlockSpec(memory_space=pltpu.HBM)
    return pl.pallas_call(
        join_kernel,
        out_shape=[out] * 3 + [pltpu.VMEM((2, 2, slots, half // 2), F32)],
        in_specs=[anywhere] * 2,
        out_specs=[hbm] * 3 + [VMEM],
        scratch_shapes=[
            pltpu.VMEM((2, 3, slots, half), BF16),
            pltpu.VMEM((2, 3, slots, half), F32),
            pltpu.SemaphoreType.DMA((6,)),
            pltpu.SemaphoreType.DMA((6,)),
        ],
        compiler_params=params(),
        cost_estimate=cost(0, 72 * own.size),
        name="join",
    )(own, sib)


def add_back_kernel(waiting, straight, diag, dq_in, dk_in, dv_in, dq_out, dk_out, dv_out, total, sems):
    width = straight.shape[2]
    core, chip = here()
    ends = ((straight, 2 * core * width), (diag, 2 * (1 - core) * width))

    def store(i, j, out, offset):
        cols = pl.ds(pl.multiple_of(ends[i][1] + offset, HEAD), width)
        copy = pltpu.make_async_copy(total.at[i, j], out.at[0, :, cols], sems.at[2 * i + j])
        copy.start()
        return copy

    for i, (back, _) in enumerate(ends):
        for j in range(2):
            total[i, j] = waiting[i, j] + back[j].astype(F32)

    @pl.when(chip == 0)
    def _():
        copies = [store(i, j, out, 0) for i in range(2) for j, out in enumerate((dk_out, dv_out))]
        for c in copies:
            c.wait()

    @pl.when(chip != 0)
    def _():
        copies = [store(i, 0, dq_out, width) for i in range(2)]
        for c in copies:
            c.wait()


def add_back(waiting, straight, diag, outs):
    hbm = pl.BlockSpec(memory_space=pltpu.HBM)
    return pl.pallas_call(
        add_back_kernel,
        out_shape=[pltpu.HBM(o.shape, F32) for o in outs],
        in_specs=[VMEM] * 3 + [hbm] * 3,
        out_specs=[hbm] * 3,
        scratch_shapes=[pltpu.VMEM(waiting.shape, F32), pltpu.SemaphoreType.DMA((4,))],
        input_output_aliases={3: 0, 4: 1, 5: 2},
        compiler_params=params(),
        cost_estimate=cost(0, 12 * waiting.size),
        name="add_back",
    )(waiting, straight, diag, *in_hbm(*outs))


def pair_router_kernel(gates_ref, sum_ref, rows_x, out_ref):
    gates = gates_ref[...]
    grad = sum_ref[...] * gates * (1.0 - gates)
    high = grad.astype(BF16)
    rest = grad - high.astype(F32)
    mid = rest.astype(BF16)
    low = (rest - mid.astype(F32)).astype(BF16)
    slots = rows_x.shape[1]
    row = lax.broadcasted_iota(jnp.int32, (8, grad.shape[1]), 0)
    lhs = jnp.where(row == 0, high.astype(F32), jnp.where(row == 1, mid.astype(F32), jnp.where(row == 2, low.astype(F32), 0.0)))
    lhs = lhs.astype(BF16)
    term = jnp.sum(nn(lhs[:, :slots], rows_x[0]) + nn(lhs[:, slots:], rows_x[1]), axis=0, keepdims=True)
    parts, copies, _, chunk = out_ref.shape
    for j in range(parts):
        for i in range(copies):
            out_ref[j, i] = term[:, j * chunk : (j + 1) * chunk]


def pair_router(gates, sums, rows_x, parts, copies):
    chunk = rows_x.shape[-1] // parts
    return pl.pallas_call(
        pair_router_kernel,
        out_shape=jax.ShapeDtypeStruct((parts, copies, 1, chunk), F32),
        in_specs=[VMEM] * 3,
        out_specs=VMEM,
        compiler_params=params(),
        cost_estimate=cost(32 * rows_x.size, rows_x.size * 4),
        name="router_terms",
    )(gates, sums, rows_x)


def swap_body(route_pos, x_routed, w_router, queries, keys, values, d_gated):
    slots = queries.shape[1]
    n, ndp = lax.axis_size("ctx"), lax.axis_size("dp")

    def send(a, flip):
        return lax.ppermute(a, "ctx", [(i, i ^ flip) for i in range(n)])

    def beside(fn, *operands):
        def skip(*ops):
            return jax.tree.map(lambda o: jnp.zeros(o.shape, o.dtype), jax.eval_shape(fn, *ops))

        return lax.cond(route_pos[0, 0] >= -1, fn, skip, *operands)

    def after(value, *others):
        return lax.optimization_barrier((value, *others))[0]

    def widen(part, step, *first):
        other = lax.ppermute(part, "dp", [(i, i ^ step) for i in range(ndp)])
        return jnp.concatenate([part, after(other, *first)], axis=1)

    def exchange_phase(x_routed, w_part, theirs):
        sib, x_sib = send(theirs, 1), send(x_routed, 1)
        step = 2
        while 2 * step < ndp:
            w_part = widen(w_part, step)
            step *= 2
        return sib, x_sib, w_part

    def tail_phase(terms, *operands):
        own_out, sib_out = far_grad(*operands)
        sib_in = send(sib_out, 1)
        shared = lax.all_to_all(after(terms, own_out).reshape(ndp * n, 1, -1), ("dp", "ctx"), 0, 0, tiled=True)
        *outs, waiting = join(own_out, sib_in, queries.shape)
        return outs, waiting, jnp.sum(shared, axis=0)[0] / float(ndp * n * slots // 2)

    out_s, out_d, w_part = cross_pack(route_pos, w_router, keys, values, queries, d_gated)
    in_s, in_d = send(out_s, 2), send(out_d, 3)

    theirs = sib_pack(after(route_pos, out_s), keys, values, queries, d_gated)
    if ndp > 1:
        w_part = widen(w_part, 1, theirs)
    sib, x_sib, w_part = beside(exchange_phase, x_routed, w_part, theirs)
    local, live, near, far, rows_x = local_stats(route_pos, keys, values, queries, d_gated, sib, x_routed, x_sib)
    cross, stats, kept = cross_stats(near, far, in_s, in_d)
    if ndp > 2:
        w_part = widen(w_part, ndp // 2, stats)
    gates, message = pair_gate(live, rows_x, w_part, local, stats, ndp)

    heard = send(message, 2)
    near_dq, near_own, near_sib, near_sum = near_grad(near, local, stats, gates)
    back_s, back_d, dq_low, keep, final, sums = cross_grad(
        cross, kept, stats, local, heard, gates, near_dq, near_sum
    )

    ret_s, ret_d = send(back_s, 2), send(back_d, 3)
    terms = pair_router(gates, sums, rows_x, ndp, n)
    outs, waiting, router_grad = beside(
        tail_phase, terms, far, local, final, gates, keep, dq_low, near_own, near_sib
    )
    dq, dk, dv = add_back(waiting, ret_s, ret_d, outs)
    return dq, dk, dv, router_grad


def body(route_pos, x_routed, w_router, queries, keys, values, d_gated):
    slots, full = queries.shape[1], queries.shape[2]
    n, ndp = lax.axis_size("ctx"), lax.axis_size("dp")
    chips = n // 2
    me, dp_me = lax.axis_index("ctx"), lax.axis_index("dp")
    core = (me % 2).astype(jnp.int32).reshape(1)
    half = full // 2
    groups = GROUPS if (half // HEAD) % GROUPS == 0 else 1
    width = half // groups

    sib_pairs = [(i, i ^ 1) for i in range(n)]

    def forward_pairs(step, flip):
        return [(i, (i + 2 * step) ^ flip) for i in range(n) if i + 2 * step < n]

    def back_pairs(step, flip):
        return [(b, a) for a, b in forward_pairs(step, flip)]

    def to_sib(a):
        return lax.ppermute(a, "ctx", sib_pairs)

    links = [(step, flip) for step in range(1, chips) for flip in (0, 1)]

    w_row = w_router.reshape(1, -1)
    w_parts = [w_row] + [
        lax.ppermute(w_row, "dp", [(i, (i + s) % ndp) for i in range(ndp)]) for s in range(1, ndp)
    ]
    live = (route_pos >= 0).astype(jnp.int32)
    lives = [live, to_sib(live)] + [lax.ppermute(live, "ctx", forward_pairs(*link)) for link in links]
    live_all = jnp.concatenate(lives, axis=0)

    kv_mine, kv_theirs = pack(core, keys, values, groups, width)
    kv_far = [
        [lax.ppermute((kv_theirs if flip else kv_mine)[g], "ctx", forward_pairs(step, flip)) for step, flip in links]
        for g in range(groups)
    ]
    q_mine, q_theirs = pack(core, queries, d_gated, groups, width)
    kv_sib = [to_sib(a) for a in kv_theirs]
    q_sib = [to_sib(a) for a in q_theirs]

    offsets = ((dp_me - jnp.arange(ndp)) % ndp).astype(jnp.int32)
    gate = router_gate(offsets, route_pos, x_routed, w_parts)
    gates = (gate, to_sib(gate))

    accs = (jnp.zeros((1, slots), F32), jnp.zeros((1, slots), F32))
    dq_own, sib_in, kv_own, back = [], [], [], []
    for g in range(groups):
        dq, sib_out, kv_local, kv_remote, accs = attention(
            core, live_all, gates, accs, q_mine[g], q_sib[g], [kv_mine[g], kv_sib[g], *kv_far[g]]
        )
        back.append([lax.ppermute(a, "ctx", back_pairs(*link)) for a, link in zip(kv_remote, links)])
        sib_in.append(to_sib(sib_out))
        dq_own.append(dq)
        kv_own.append(kv_local)

    targets = ((dp_me + jnp.arange(ndp)) % ndp).astype(jnp.int32)
    terms = router_terms(targets, gate, accs[0], to_sib(accs[1]), x_routed, ndp)
    mine = terms[0]
    for s in range(1, ndp):
        mine = mine + lax.ppermute(terms[s], "dp", [(i, (i + s) % ndp) for i in range(ndp)])
    total = mine
    for s in range(1, n):
        total = total + lax.ppermute(mine, "ctx", [(i, (i + s) % n) for i in range(n)])
    router_grad = total[0] / float(ndp * n * slots // 2)

    dq, dk, dv = combine(core, dq_own, sib_in, kv_own, back, queries.shape)
    return dq, dk, dv, router_grad


def solution(mesh):
    placed = (
        P("dp", "ctx"),
        P("dp", "ctx", None),
        P("dp"),
        P("dp", "ctx", None),
        P("dp", "ctx", None),
        P("dp", "ctx", None),
        P("dp", "ctx", None),
    )
    ndp = mesh.shape["dp"]
    paired = mesh.shape["ctx"] == 4 and ndp & (ndp - 1) == 0
    return jax.shard_map(
        swap_body if paired else body,
        mesh=mesh,
        in_specs=placed,
        out_specs=(P("dp", "ctx", None), P("dp", "ctx", None), P("dp", "ctx", None), P("dp")),
        check_vma=False,
    )
```

```python
import functools

import jax
import jax.numpy as jnp
from jax import lax
from jax.experimental import pallas as pl
from jax.experimental.pallas import tpu as pltpu
from jax.sharding import PartitionSpec as P

HEAD = 128
GROUPS = 4
NEG_FILL = -1e30
MIB = 1024 * 1024
BF16 = jnp.bfloat16
F32 = jnp.float32

VMEM = pl.BlockSpec(memory_space=pltpu.VMEM)
SMEM = pl.BlockSpec(memory_space=pltpu.SMEM)


def params(mib=16):
    return pltpu.CompilerParams(vmem_limit_bytes=mib * MIB)


def cost(flops, nbytes, exps=0):
    return pl.CostEstimate(flops=1, bytes_accessed=1, transcendentals=0)


def in_hbm(*arrays):
    return [pltpu.with_memory_space_constraint(a, pltpu.HBM) for a in arrays]


def nt(a, b):
    return lax.dot_general(a, b, (((1,), (1,)), ((), ())), preferred_element_type=F32)


def nn(a, b):
    return lax.dot_general(a, b, (((1,), (0,)), ((), ())), preferred_element_type=F32)


def tn(a, b):
    return lax.dot_general(a, b, (((0,), (0,)), ((), ())), preferred_element_type=F32)


def pack_kernel(groups, width, core_ref, first_ref, second_ref, *outs):
    half = first_ref.shape[-1] // 2
    core = core_ref[0]
    for side in range(2):
        base = (core if side == 0 else 1 - core) * half
        for g in range(groups):
            out = outs[side * groups + g]
            cols = pl.ds(pl.multiple_of(base + g * width, HEAD), width)
            out[0] = first_ref[0, :, cols].astype(BF16)
            out[1] = second_ref[0, :, cols].astype(BF16)


def pack(core, first, second, groups, width):
    slots = first.shape[1]
    out = jax.ShapeDtypeStruct((2, slots, width), BF16)
    res = pl.pallas_call(
        functools.partial(pack_kernel, groups, width),
        out_shape=[out] * (2 * groups),
        in_specs=[SMEM, VMEM, VMEM],
        out_specs=[VMEM] * (2 * groups),
        compiler_params=params(),
        cost_estimate=cost(0, 2 * first.size * 4),
        name="pack",
    )(core, first, second)
    return res[:groups], res[groups:]


def gate_kernel(parts, offset_ref, pos_ref, x_ref, *refs):
    w_refs, out_ref = refs[:parts], refs[parts]
    chunk = w_refs[0].shape[-1]
    total = jnp.zeros((8, x_ref.shape[1]), F32)
    for s in range(parts):
        cols = pl.ds(pl.multiple_of(offset_ref[s] * chunk, HEAD), chunk)
        w_rows = jnp.broadcast_to(w_refs[s][...].astype(F32), (8, chunk)).astype(BF16)
        total = total + nt(w_rows, x_ref[0, :, cols])
    gate = 1.0 / (1.0 + jnp.exp(-total[0:1]))
    out_ref[...] = jnp.where(pos_ref[...] >= 0, gate, 0.0)


def router_gate(offsets, route_pos, x_routed, w_parts):
    parts = len(w_parts)
    return pl.pallas_call(
        functools.partial(gate_kernel, parts),
        out_shape=jax.ShapeDtypeStruct(route_pos.shape, F32),
        in_specs=[SMEM] + [VMEM] * (2 + parts),
        out_specs=VMEM,
        compiler_params=params(),
        cost_estimate=cost(16 * x_routed.size, x_routed.size * 2),
        name="router_gate",
    )(offsets, route_pos, x_routed, *w_parts)


def attention_kernel(remote, scale, core_ref, live_ref, gate_own, gate_sib, acc_own, acc_sib, q_own, q_sib, *refs):
    chunks = 2 + remote
    kv = refs[:chunks]
    outs = refs[chunks:]
    dq_own, sib_out, kv_own = outs[:3]
    kv_remote = outs[3 : 3 + remote]
    sum_own, sum_sib = outs[3 + remote :]
    slots, width = q_own.shape[1], q_own.shape[2]
    core = core_ref[0]
    key = lax.broadcasted_iota(jnp.int32, (slots, slots), 0)
    query = lax.broadcasted_iota(jnp.int32, (slots, slots), 1)
    counts = [jnp.sum(live_ref[i : i + 1], axis=1, keepdims=True) for i in range(chunks)]
    lives = [key < counts[i] for i in range(chunks)]
    own_later = core == 1
    bias_rows = []
    for i in range(chunks):
        live = lives[i]
        if i == 0:
            pair = (live & (key <= query), live & jnp.logical_not(own_later))
        elif i == 1:
            pair = (live & own_later, live & (key <= query))
        else:
            pair = (live, live)
        bias_rows.append(jnp.concatenate([jnp.where(p, 0.0, NEG_FILL) for p in pair], axis=1))
    bias = jnp.concatenate(bias_rows, axis=0)
    gates = jnp.concatenate([gate_own[...], gate_sib[...]], axis=1)
    total = jnp.zeros((1, 2 * slots), F32)
    for h in range(width // HEAD):
        cols = slice(h * HEAD, (h + 1) * HEAD)
        q = jnp.concatenate([q_own[0, :, cols], q_sib[0, :, cols]], axis=0)
        dg = jnp.concatenate([q_own[1, :, cols], q_sib[1, :, cols]], axis=0)
        k = jnp.concatenate([r[0, :, cols] for r in kv], axis=0)
        v = jnp.concatenate([r[1, :, cols] for r in kv], axis=0)
        scores = nt(k, q) * scale + bias
        top = jnp.max(scores, axis=0, keepdims=True)
        e = jnp.exp(scores - top)
        inverse = 1.0 / jnp.sum(e, axis=0, keepdims=True)
        gw = nt(v, dg)
        delta = jnp.sum(e * gw, axis=0, keepdims=True) * inverse
        total = total + delta
        weights = e * (inverse * gates)
        dv = nn(weights.astype(BF16), dg)
        ds = (weights * ((gw - delta) * scale)).astype(BF16)
        dk = nn(ds, q)
        dq = tn(ds, k)
        dq_own[:, cols] = dq[:slots].astype(dq_own.dtype)
        sib_out[0, :, cols] = dq[slots:].astype(BF16)
        kv_own[0, :, cols] = dk[:slots].astype(BF16)
        kv_own[1, :, cols] = dv[:slots].astype(BF16)
        sib_out[1, :, cols] = dk[slots : 2 * slots].astype(BF16)
        sib_out[2, :, cols] = dv[slots : 2 * slots].astype(BF16)
        for i in range(remote):
            rows = slice((2 + i) * slots, (3 + i) * slots)
            kv_remote[i][0, :, cols] = dk[rows].astype(BF16)
            kv_remote[i][1, :, cols] = dv[rows].astype(BF16)
    sum_own[...] = acc_own[...] + total[:, :slots]
    sum_sib[...] = acc_sib[...] + total[:, slots:]


def attention(core, live, gates, accs, q_own, q_sib, kv):
    remote = len(kv) - 2
    _, slots, width = q_own.shape
    pair = jax.ShapeDtypeStruct((2, slots, width), BF16)
    row = jax.ShapeDtypeStruct((1, slots), F32)
    outs = [
        jax.ShapeDtypeStruct((slots, width), BF16),
        jax.ShapeDtypeStruct((3, slots, width), BF16),
        pair,
        *([pair] * remote),
        row,
        row,
    ]
    keys = (2 + remote) * slots
    res = pl.pallas_call(
        functools.partial(attention_kernel, remote, HEAD**-0.5),
        out_shape=outs,
        in_specs=[SMEM] + [VMEM] * (7 + len(kv)),
        out_specs=[VMEM] * len(outs),
        compiler_params=params(48),
        cost_estimate=cost(20 * slots * keys * width, 8 * keys * width + 20 * slots * width, 2 * slots * keys * width // HEAD),
        name="attention",
    )(core, live, *gates, *accs, q_own, q_sib, *kv)
    return res[0], res[1], res[2], res[3 : 3 + remote], (res[3 + remote], res[4 + remote])


def combine_kernel(groups, width, remote, core_ref, *refs):
    dq_own, sib, kv_own = refs[:groups], refs[groups : 2 * groups], refs[2 * groups : 3 * groups]
    back = refs[3 * groups : 3 * groups + groups * remote]
    dq_out, dk_out, dv_out = refs[3 * groups + groups * remote :]
    half = groups * width
    core = core_ref[0]
    for g in range(groups):
        own = pl.ds(pl.multiple_of(core * half + g * width, HEAD), width)
        other = pl.ds(pl.multiple_of((1 - core) * half + g * width, HEAD), width)
        dq_out[0, :, own] = dq_own[g][...].astype(F32)
        dq_out[0, :, other] = sib[g][0].astype(F32)
        for i, out in enumerate((dk_out, dv_out)):
            mine = kv_own[g][i].astype(F32)
            theirs = sib[g][1 + i].astype(F32)
            for r in range(remote):
                part = back[g * remote + r][i].astype(F32)
                if r % 2 == 0:
                    mine = mine + part
                else:
                    theirs = theirs + part
            out[0, :, own] = mine
            out[0, :, other] = theirs


def combine(core, dq_own, sib, kv_own, back, shape):
    groups = len(dq_own)
    remote = len(back[0])
    out = jax.ShapeDtypeStruct(shape, F32)
    flat = [*dq_own, *sib, *kv_own, *(b for group in back for b in group)]
    return pl.pallas_call(
        functools.partial(combine_kernel, groups, dq_own[0].shape[-1], remote),
        out_shape=[out] * 3,
        in_specs=[SMEM] + [VMEM] * len(flat),
        out_specs=[VMEM] * 3,
        compiler_params=params(48),
        cost_estimate=cost(0, 3 * out.size * 6),
        name="combine",
    )(core, *flat)


def router_kernel(parts, target_ref, gate_ref, own_ref, sib_ref, x_ref, *outs):
    gate = gate_ref[...]
    grad = (own_ref[...] + sib_ref[...]) * gate * (1.0 - gate)
    high = grad.astype(BF16)
    rest = grad - high.astype(F32)
    mid = rest.astype(BF16)
    low = (rest - mid.astype(F32)).astype(BF16)
    row = lax.broadcasted_iota(jnp.int32, (8, grad.shape[1]), 0)
    lhs = jnp.where(row == 0, high.astype(F32), jnp.where(row == 1, mid.astype(F32), jnp.where(row == 2, low.astype(F32), 0.0)))
    lhs = lhs.astype(BF16)
    chunk = outs[0].shape[-1]
    for s in range(parts):
        cols = pl.ds(pl.multiple_of(target_ref[s] * chunk, HEAD), chunk)
        outs[s][...] = jnp.sum(nn(lhs, x_ref[0, :, cols]), axis=0, keepdims=True)


def router_terms(targets, gate, own, sib, x_routed, parts):
    chunk = x_routed.shape[-1] // parts
    return pl.pallas_call(
        functools.partial(router_kernel, parts),
        out_shape=[jax.ShapeDtypeStruct((1, chunk), F32)] * parts,
        in_specs=[SMEM] + [VMEM] * 4,
        out_specs=[VMEM] * parts,
        compiler_params=params(),
        cost_estimate=cost(16 * x_routed.size, x_routed.size * 2),
        name="router_terms",
    )(targets, gate, own, sib, x_routed)


def here():
    me = lax.axis_index("ctx")
    return lax.rem(me, 2), lax.div(me, 2)


MARK = 2.0**60
MARK_LIMIT = 2.0**50


def live_rows(pos_ref, slots):
    count = jnp.sum((pos_ref[...] >= 0).astype(jnp.int32), axis=1, keepdims=True)
    return lax.broadcasted_iota(jnp.int32, (slots, HEAD), 0) < count


def mark_dead(keys, live):
    width = keys.shape[-1]
    mask = jnp.concatenate([live] * (width // HEAD), axis=1)
    return jnp.where(mask, keys.astype(F32), MARK).astype(BF16)


def cross_pack_kernel(pos_any, w_any, k_ref, v_ref, q_ref, dg_ref, straight, diag, w_out, wide, pos_ref, w_ref, sems):
    small = [pltpu.make_async_copy(pos_any, pos_ref, sems.at[4]), pltpu.make_async_copy(w_any, w_ref, sems.at[5])]
    for c in small:
        c.start()
    slots, width = straight.shape[1], straight.shape[2]
    half = k_ref.shape[-1] // 2
    core, chip = here()
    ends = ((straight, core * half), (diag, (1 - core) * half))

    def copies(first, second, targets, offset):
        out = []
        for i, (end, start) in enumerate(ends):
            cols = pl.ds(pl.multiple_of(start + offset, HEAD), width)
            out.append(pltpu.make_async_copy(first.at[0, :, cols], end.at[0], sems.at[2 * i]))
            out.append(pltpu.make_async_copy(second.at[0, :, cols], targets[i], sems.at[2 * i + 1]))
        for c in out:
            c.start()
        for c in out:
            c.wait()

    @pl.when(chip == 0)
    def _():
        copies(k_ref, v_ref, (straight.at[1], diag.at[1]), 0)
        small[0].wait()
        live = live_rows(pos_ref, slots)
        for end, _ in ends:
            end[0] = mark_dead(end[0], live)

    @pl.when(chip != 0)
    def _():
        copies(q_ref, dg_ref, (wide.at[0], wide.at[1]), width)
        small[0].wait()
        for i, (end, _) in enumerate(ends):
            end[1] = wide[i].astype(BF16)

    small[1].wait()
    w_out[...] = w_ref[...].astype(F32).reshape(w_out.shape)


def cross_pack(route_pos, w_router, keys, values, queries, d_gated):
    _, slots, full = keys.shape
    cross = pltpu.VMEM((2, slots, full // 4), BF16)
    hbm = pl.BlockSpec(memory_space=pltpu.HBM)
    return pl.pallas_call(
        cross_pack_kernel,
        out_shape=[cross, cross, jax.ShapeDtypeStruct((1, w_router.shape[0]), F32)],
        in_specs=[hbm] * 6,
        out_specs=[VMEM] * 3,
        scratch_shapes=[
            pltpu.VMEM((2, slots, full // 4), F32),
            pltpu.VMEM(route_pos.shape, jnp.int32),
            pltpu.VMEM(w_router.shape, BF16),
            pltpu.SemaphoreType.DMA((6,)),
        ],
        compiler_params=params(),
        cost_estimate=cost(0, 10 * slots * full),
        name="cross_pack",
    )(*in_hbm(route_pos, w_router, keys, values, queries, d_gated))


def sib_pack_kernel(pos_ref, k_ref, v_ref, q_ref, dg_ref, out, wide, sems):
    slots, half = out.shape[1], out.shape[2]
    cols = pl.ds(pl.multiple_of((1 - here()[0]) * half, HEAD), half)
    sources = ((k_ref, out.at[0]), (dg_ref, wide), (v_ref, out.at[1]), (q_ref, out.at[2]))
    copies = [pltpu.make_async_copy(src.at[0, :, cols], dst, sems.at[i]) for i, (src, dst) in enumerate(sources)]
    for c in copies:
        c.start()
    live = live_rows(pos_ref, slots)
    copies[0].wait()
    out[0] = mark_dead(out[0], live)
    copies[1].wait()
    out[3] = wide[...].astype(BF16)
    copies[2].wait()
    copies[3].wait()


def sib_pack(route_pos, keys, values, queries, d_gated):
    _, slots, full = keys.shape
    hbm = pl.BlockSpec(memory_space=pltpu.HBM)
    return pl.pallas_call(
        sib_pack_kernel,
        out_shape=pltpu.VMEM((4, slots, full // 2), BF16),
        in_specs=[VMEM, hbm, hbm, hbm, hbm],
        out_specs=VMEM,
        scratch_shapes=[pltpu.VMEM((slots, full // 2), F32), pltpu.SemaphoreType.DMA((4,))],
        compiler_params=params(),
        cost_estimate=cost(0, 20 * slots * full),
        name="sib_pack",
    )(route_pos, *in_hbm(keys, values, queries, d_gated))


def pair_gate_kernel(parts, live_ref, rows_x, w_ref, local, stats, out_ref, message):
    chunk = w_ref.shape[1] // parts
    slots = rows_x.shape[1]
    for i in range(2):
        total = jnp.zeros((8, slots), F32)
        for j in range(parts):
            w_rows = jnp.broadcast_to(w_ref[:, j * chunk : (j + 1) * chunk], (8, chunk)).astype(BF16)
            cols = pl.ds(pl.multiple_of((lax.axis_index("dp") ^ j) * chunk, HEAD), chunk)
            total = total + nt(w_rows, rows_x[i, :, cols])
        lanes = slice(i * slots, (i + 1) * slots)
        out_ref[:, lanes] = live_ref[:, lanes] / (1.0 + jnp.exp(-total[0:1]))
    first = here()[1] == 0
    heads = stats.shape[1]
    for i in range(3):
        message[i] = jnp.where(first, stats[i], local[i, heads:])
    message[3] = jnp.broadcast_to(out_ref[...], message.shape[1:])


def pair_gate(live, rows_x, w_full, local, stats, parts):
    _, heads, lanes = stats.shape
    return pl.pallas_call(
        functools.partial(pair_gate_kernel, parts),
        out_shape=[jax.ShapeDtypeStruct(live.shape, F32), jax.ShapeDtypeStruct((4, heads, lanes), F32)],
        in_specs=[VMEM] * 5,
        out_specs=[VMEM] * 2,
        compiler_params=params(),
        cost_estimate=cost(16 * rows_x.size, rows_x.size * 2),
        name="router_gate",
    )(live, rows_x, w_full, local, stats)


def local_mask(core, pair):
    slots = pair.shape[1] // 2
    key = lax.broadcasted_iota(jnp.int32, (slots, slots), 0)
    query = lax.broadcasted_iota(jnp.int32, (slots, slots), 1)
    causal = key <= query
    own_live = pair[0, :slots, :slots].astype(F32) < MARK_LIMIT
    sib_live = pair[0, slots:, :slots].astype(F32) < MARK_LIMIT
    own_rows = jnp.concatenate([own_live & causal, own_live & (core == 0)], axis=1)
    sib_rows = jnp.concatenate([sib_live & (core == 1), sib_live & causal], axis=1)
    return jnp.concatenate([own_rows, sib_rows], axis=0)


def kept_stats(scores, gw, kept, stats, h):
    top = jnp.max(scores, axis=0, keepdims=True)
    e = jnp.exp(scores - top).astype(BF16)
    gw = gw.astype(BF16)
    kept[0, h] = e
    kept[1, h] = gw
    e = e.astype(F32)
    stats[0, h : h + 1] = top
    stats[1, h : h + 1] = jnp.sum(e, axis=0, keepdims=True)
    stats[2, h : h + 1] = jnp.sum(e * gw.astype(F32), axis=0, keepdims=True)


def partial_stats(scores, gw, stats, h):
    top = jnp.max(scores, axis=0, keepdims=True)
    e = jnp.exp(scores - top)
    stats[0, h : h + 1] = top
    stats[1, h : h + 1] = jnp.sum(e, axis=0, keepdims=True)
    stats[2, h : h + 1] = jnp.sum(e * gw, axis=0, keepdims=True)


def local_stats_kernel(scale, pos_ref, k_ref, v_ref, q_ref, dg_ref, sib, x_ref, x_sib, stats, live, near, far, rows_x, wide, sems, x_sems):
    slots, half = sib.shape[1], sib.shape[2]
    width = half // 2
    core = here()[0]
    own, other = slice(0, slots), slice(slots, 2 * slots)
    stages = []
    for g, pair in enumerate((near, far)):
        cols = slice(g * width, (g + 1) * width)
        held = pl.ds(pl.multiple_of(core * half + g * width, HEAD), width)
        copies = [
            pltpu.make_async_copy(ref.at[0, :, held], pair.at[j, own], sems.at[8 * g + j])
            for j, ref in enumerate((k_ref, v_ref, q_ref))
        ]
        copies.append(pltpu.make_async_copy(dg_ref.at[0, :, held], wide.at[:, cols], sems.at[8 * g + 3]))
        for j in range(4):
            copies.append(pltpu.make_async_copy(sib.at[j, :, cols], pair.at[j, other], sems.at[8 * g + 4 + j]))
        for c in copies:
            c.start()
        stages.append(copies)
    x_copies = []
    depth = x_ref.shape[2] // 2
    for i, ref in enumerate((x_ref, x_sib)):
        for g in range(2):
            cols = slice(g * depth, (g + 1) * depth)
            x_copies.append(pltpu.make_async_copy(ref.at[0, :, cols], rows_x.at[i, :, cols], x_sems.at[2 * i + g]))
    for c in x_copies:
        c.start()
    rows_live = live_rows(pos_ref, slots)
    mask = None
    for g, pair in enumerate((near, far)):
        cols = slice(g * width, (g + 1) * width)
        for c in stages[g]:
            c.wait()
        pair[0, own] = mark_dead(pair[0, own], rows_live)
        pair[3, own] = wide[:, cols].astype(BF16)
        if mask is None:
            mask = local_mask(core, pair)
            marks = nt(jnp.ones((8, HEAD), BF16), pair[0, :, :HEAD])[0:1]
            live[...] = jnp.where(marks < MARK_LIMIT, 1.0, 0.0)
        for h in range(width // HEAD):
            at = slice(h * HEAD, (h + 1) * HEAD)
            scores = jnp.where(mask, nt(pair[0, :, at], pair[2, :, at]) * scale, NEG_FILL)
            partial_stats(scores, nt(pair[1, :, at], pair[3, :, at]), stats, g * width // HEAD + h)
    for c in x_copies:
        c.wait()


def local_stats(route_pos, keys, values, queries, d_gated, sib, x_routed, x_sib):
    _, slots, half = sib.shape
    heads = half // HEAD
    anywhere = pl.BlockSpec(memory_space=pl.ANY)
    return pl.pallas_call(
        functools.partial(local_stats_kernel, HEAD**-0.5),
        out_shape=[
            jax.ShapeDtypeStruct((3, heads, 2 * slots), F32),
            jax.ShapeDtypeStruct((1, 2 * slots), F32),
            pltpu.VMEM((4, 2 * slots, half // 2), BF16),
            pltpu.VMEM((4, 2 * slots, half // 2), BF16),
            pltpu.VMEM((2, slots, x_routed.shape[2]), BF16),
        ],
        in_specs=[VMEM] + [anywhere] * 7,
        out_specs=[VMEM] * 5,
        scratch_shapes=[pltpu.VMEM((slots, half), F32), pltpu.SemaphoreType.DMA((16,)), pltpu.SemaphoreType.DMA((4,))],
        compiler_params=params(),
        cost_estimate=cost(16 * slots * slots * half, 16 * slots * half, 4 * slots * slots * half // HEAD),
        name="local_stats",
    )(route_pos, *in_hbm(keys, values, queries, d_gated), sib, x_routed, x_sib)


def cross_stats_kernel(scale, near, far, straight, diag, cross, stats, kept):
    slots, width = straight.shape[1], straight.shape[2]
    chip = here()[1]
    top, bottom = slice(0, slots), slice(slots, 2 * slots)

    @pl.when(chip == 0)
    def _():
        for part in range(2):
            cross[part] = far[part]
            cross[2 + part, top] = straight[part]
            cross[2 + part, bottom] = diag[part]

    @pl.when(chip != 0)
    def _():
        for part in range(2):
            cross[part, top] = straight[part]
            cross[part, bottom] = diag[part]
            cross[2 + part] = near[2 + part]

    live = cross[0, :, :HEAD].astype(F32) < MARK_LIMIT
    mask = jnp.concatenate([live] * (2 * slots // HEAD), axis=1)
    heads = width // HEAD
    for h in range(heads):
        cols = slice(h * HEAD, (h + 1) * HEAD)
        scores = jnp.where(mask, nt(cross[0, :, cols], cross[2, :, cols]) * scale, NEG_FILL)
        kept_stats(scores, nt(cross[1, :, cols], cross[3, :, cols]), kept, stats, h)


def cross_stats(near, far, straight, diag):
    _, slots, width = straight.shape
    heads = width // HEAD
    return pl.pallas_call(
        functools.partial(cross_stats_kernel, HEAD**-0.5),
        out_shape=[
            pltpu.VMEM((4, 2 * slots, width), BF16),
            jax.ShapeDtypeStruct((3, heads, 2 * slots), F32),
            pltpu.VMEM((2, heads, 2 * slots, 2 * slots), BF16),
        ],
        in_specs=[VMEM] * 4,
        out_specs=[VMEM] * 3,
        compiler_params=params(),
        cost_estimate=cost(16 * slots * slots * width, 32 * slots * width, 4 * slots * slots * heads),
        name="cross_stats",
    )(near, far, straight, diag)


NONE = (-3e38, 0.0, 0.0)


def merge(first, second):
    top = jnp.maximum(first[0], second[0])
    a, b = jnp.exp(first[0] - top), jnp.exp(second[0] - top)
    inverse = 1.0 / (first[1] * a + second[1] * b)
    return a * inverse, (first[2] * a + second[2] * b) * inverse


def choose(flag, yes, no):
    return [jnp.where(flag, y, n) for y, n in zip(yes, no)]


def gradients(q, k, dg, e, gw, scale, factor, delta):
    weights = e * factor
    ds = (weights * ((gw - delta) * scale)).astype(BF16)
    return tn(ds, k), nn(ds, q), nn(weights.astype(BF16), dg)


def local_gradients(pair, h, mask, scale, top, factor, delta):
    cols = slice(h * HEAD, (h + 1) * HEAD)
    k, v, q, dg = [pair[i, :, cols] for i in range(4)]
    e = jnp.exp(jnp.where(mask, nt(k, q) * scale, NEG_FILL) - top)
    return gradients(q, k, dg, e, nt(v, dg), scale, factor, delta)


def near_grad_kernel(scale, pair, local, stats, gates, dq_out, own_out, sib_out, sum_out):
    slots, width = own_out.shape[1], own_out.shape[2]
    heads = width // HEAD
    first = here()[1] == 0
    near = [local[i, :heads] for i in range(3)]
    factor, delta = merge(near, choose(first, NONE, [stats[i] for i in range(3)]))
    factor = factor * gates[...]
    sum_out[...] = jnp.sum(delta, axis=0, keepdims=True)
    mask = local_mask(here()[0], pair)
    for h in range(heads):
        cols = slice(h * HEAD, (h + 1) * HEAD)
        row = slice(h, h + 1)
        dq, dk, dv = local_gradients(pair, h, mask, scale, near[0][row], factor[row], delta[row])
        dq_out[:, cols] = dq
        for i, part in enumerate((dk, dv)):
            own_out[i, :, cols] = part[:slots].astype(BF16)
            sib_out[i, :, cols] = part[slots:].astype(BF16)


def near_grad(pair, local, stats, gates):
    _, rows, width = pair.shape
    slots = rows // 2
    out = pltpu.VMEM((2, slots, width), BF16)
    return pl.pallas_call(
        functools.partial(near_grad_kernel, HEAD**-0.5),
        out_shape=[pltpu.VMEM((2 * slots, width), F32), out, out, jax.ShapeDtypeStruct(gates.shape, F32)],
        in_specs=[VMEM] * 4,
        out_specs=[VMEM] * 4,
        compiler_params=params(),
        cost_estimate=cost(20 * slots * slots * width, 40 * slots * width),
        name="near_grad",
    )(pair, local, stats, gates)


def cross_grad_kernel(scale, cross, kept, stats, local, heard, gates, near_dq, near_sum, straight, diag, dq_out, keep, final, sum_out):
    slots, width = straight.shape[1], straight.shape[2]
    heads = width // HEAD
    first = here()[1] == 0
    late = jnp.where(first, 0.0, 1.0)
    mine = [stats[i] for i in range(3)]
    other = [heard[i] for i in range(3)]
    near = [local[i, :heads] for i in range(3)]
    far = [local[i, heads:] for i in range(3)]
    factor, delta = merge(mine, choose(first, other, near))
    factor = factor * jnp.where(first, heard[3], jnp.broadcast_to(gates[...], factor.shape))
    final[0], final[1] = merge(far, choose(first, NONE, other))
    sum_out[...] = near_sum[...] + jnp.sum(final[1], axis=0, keepdims=True)
    for h in range(heads):
        cols = slice(h * HEAD, (h + 1) * HEAD)
        row = slice(h, h + 1)
        dq, dk, dv = gradients(
            cross[2, :, cols], cross[0, :, cols], cross[3, :, cols],
            kept[0, h].astype(F32), kept[1, h].astype(F32), scale, factor[row], delta[row],
        )
        dq_out[:, cols] = (near_dq[:, cols] + late * dq).astype(BF16)
        keep[0, :, cols] = dk.astype(BF16)
        keep[1, :, cols] = dv.astype(BF16)
        sent = jnp.where(first, dq, dk).astype(BF16)
        straight[0, :, cols] = sent[:slots]
        diag[0, :, cols] = sent[slots:]
        straight[1, :, cols] = dv[:slots].astype(BF16)
        diag[1, :, cols] = dv[slots:].astype(BF16)


def cross_grad(cross, kept, stats, local, heard, gates, near_dq, near_sum):
    _, rows, width = cross.shape
    slots = rows // 2
    out = pltpu.VMEM((2, slots, width), BF16)
    return pl.pallas_call(
        functools.partial(cross_grad_kernel, HEAD**-0.5),
        out_shape=[
            out,
            out,
            pltpu.VMEM((rows, width), BF16),
            pltpu.VMEM((2, rows, width), BF16),
            jax.ShapeDtypeStruct((2, width // HEAD, rows), F32),
            jax.ShapeDtypeStruct((1, rows), F32),
        ],
        in_specs=[VMEM] * 8,
        out_specs=[VMEM] * 6,
        compiler_params=params(),
        cost_estimate=cost(24 * slots * slots * width, 64 * slots * width),
        name="cross_grad",
    )(cross, kept, stats, local, heard, gates, near_dq, near_sum)


def far_grad_kernel(scale, pair, local, final, gates, keep, near_dq, near_own, near_sib, own_out, sib_out):
    slots, width = pair.shape[1] // 2, pair.shape[2]
    heads = width // HEAD
    early = jnp.where(here()[1] == 0, 1.0, 0.0)
    factor = final[0] * gates[...]
    mask = local_mask(here()[0], pair)
    own_out[0, :, :width] = near_dq[:slots]
    sib_out[0, :, :width] = near_dq[slots:]
    for i in range(2):
        own_out[1 + i, :, :width] = near_own[i]
        sib_out[1 + i, :, :width] = near_sib[i]
    for h in range(heads):
        cols = slice(width + h * HEAD, width + (h + 1) * HEAD)
        at = slice(h * HEAD, (h + 1) * HEAD)
        row = slice(h, h + 1)
        top = local[0, heads + h : heads + h + 1]
        dq, dk, dv = local_gradients(pair, h, mask, scale, top, factor[row], final[1, row])
        dk = dk + early * keep[0, :, at].astype(F32)
        dv = dv + early * keep[1, :, at].astype(F32)
        for i, part in enumerate((dq, dk, dv)):
            own_out[i, :, cols] = part[:slots].astype(BF16)
            sib_out[i, :, cols] = part[slots:].astype(BF16)


def far_grad(pair, local, final, gates, keep, near_dq, near_own, near_sib):
    _, rows, width = pair.shape
    slots, half = rows // 2, 2 * width
    out = jax.ShapeDtypeStruct((3, slots, half), BF16)
    return pl.pallas_call(
        functools.partial(far_grad_kernel, HEAD**-0.5),
        out_shape=[out, out],
        in_specs=[VMEM] * 8,
        out_specs=[VMEM] * 2,
        compiler_params=params(),
        cost_estimate=cost(20 * slots * slots * half, 40 * slots * half),
        name="far_grad",
    )(pair, local, final, gates, keep, near_dq, near_own, near_sib)


def join_kernel(own, sib, dq_out, dk_out, dv_out, waiting, low, total, in_sems, out_sems):
    slots, half = own.shape[1], own.shape[2]
    width = half // 2
    core, chip = here()
    ends = ((own, core * half), (sib, (1 - core) * half))
    loads = [
        [pltpu.make_async_copy(part.at[j], low.at[i, j], in_sems.at[3 * i + j]) for j in range(3)]
        for i, (part, _) in enumerate(ends)
    ]
    for c in loads[0] + loads[1]:
        c.start()
    stores = []
    for i, (_, start) in enumerate(ends):
        cols = pl.ds(pl.multiple_of(start, HEAD), half)
        for j, out in enumerate((dq_out, dk_out, dv_out)):
            loads[i][j].wait()
            total[i, j] = low[i, j].astype(F32)
            stores.append(pltpu.make_async_copy(total.at[i, j], out.at[0, :, cols], out_sems.at[3 * i + j]))
            stores[-1].start()
        waiting[i, 0] = jnp.where(chip == 0, total[i, 1, :, :width], total[i, 0, :, width:]).astype(BF16)
        waiting[i, 1] = low[i, 2, :, :width]
    for c in stores:
        c.wait()


def join(own, sib, shape):
    out = pltpu.HBM(shape, F32)
    _, slots, half = own.shape
    anywhere = pl.BlockSpec(memory_space=pl.ANY)
    hbm = pl.BlockSpec(memory_space=pltpu.HBM)
    return pl.pallas_call(
        join_kernel,
        out_shape=[out] * 3 + [pltpu.VMEM((2, 2, slots, half // 2), BF16)],
        in_specs=[anywhere] * 2,
        out_specs=[hbm] * 3 + [VMEM],
        scratch_shapes=[
            pltpu.VMEM((2, 3, slots, half), BF16),
            pltpu.VMEM((2, 3, slots, half), F32),
            pltpu.SemaphoreType.DMA((6,)),
            pltpu.SemaphoreType.DMA((6,)),
        ],
        compiler_params=params(),
        cost_estimate=cost(0, 72 * own.size),
        name="join",
    )(own, sib)


def add_back_kernel(waiting, straight, diag, dq_in, dk_in, dv_in, dq_out, dk_out, dv_out, total, sems):
    width = straight.shape[2]
    core, chip = here()
    ends = ((straight, 2 * core * width), (diag, 2 * (1 - core) * width))

    def store(i, j, out, offset):
        cols = pl.ds(pl.multiple_of(ends[i][1] + offset, HEAD), width)
        copy = pltpu.make_async_copy(total.at[i, j], out.at[0, :, cols], sems.at[2 * i + j])
        copy.start()
        return copy

    for i, (back, _) in enumerate(ends):
        for j in range(2):
            total[i, j] = waiting[i, j].astype(F32) + back[j].astype(F32)

    @pl.when(chip == 0)
    def _():
        copies = [store(i, j, out, 0) for i in range(2) for j, out in enumerate((dk_out, dv_out))]
        for c in copies:
            c.wait()

    @pl.when(chip != 0)
    def _():
        copies = [store(i, 0, dq_out, width) for i in range(2)]
        for c in copies:
            c.wait()


def add_back(waiting, straight, diag, outs):
    hbm = pl.BlockSpec(memory_space=pltpu.HBM)
    return pl.pallas_call(
        add_back_kernel,
        out_shape=[pltpu.HBM(o.shape, F32) for o in outs],
        in_specs=[VMEM] * 3 + [hbm] * 3,
        out_specs=[hbm] * 3,
        scratch_shapes=[pltpu.VMEM(waiting.shape, F32), pltpu.SemaphoreType.DMA((4,))],
        input_output_aliases={3: 0, 4: 1, 5: 2},
        compiler_params=params(),
        cost_estimate=cost(0, 12 * waiting.size),
        name="add_back",
    )(waiting, straight, diag, *in_hbm(*outs))


def pair_router_kernel(gates_ref, sum_ref, rows_x, out_ref):
    gates = gates_ref[...]
    grad = sum_ref[...] * gates * (1.0 - gates)
    high = grad.astype(BF16)
    rest = grad - high.astype(F32)
    mid = rest.astype(BF16)
    low = (rest - mid.astype(F32)).astype(BF16)
    slots = rows_x.shape[1]
    row = lax.broadcasted_iota(jnp.int32, (8, grad.shape[1]), 0)
    lhs = jnp.where(row == 0, high.astype(F32), jnp.where(row == 1, mid.astype(F32), jnp.where(row == 2, low.astype(F32), 0.0)))
    lhs = lhs.astype(BF16)
    term = jnp.sum(nn(lhs[:, :slots], rows_x[0]) + nn(lhs[:, slots:], rows_x[1]), axis=0, keepdims=True)
    parts, copies, _, chunk = out_ref.shape
    for j in range(parts):
        for i in range(copies):
            out_ref[j, i] = term[:, j * chunk : (j + 1) * chunk]


def pair_router(gates, sums, rows_x, parts, copies):
    chunk = rows_x.shape[-1] // parts
    return pl.pallas_call(
        pair_router_kernel,
        out_shape=jax.ShapeDtypeStruct((parts, copies, 1, chunk), F32),
        in_specs=[VMEM] * 3,
        out_specs=VMEM,
        compiler_params=params(),
        cost_estimate=cost(32 * rows_x.size, rows_x.size * 4),
        name="router_terms",
    )(gates, sums, rows_x)


def swap_body(route_pos, x_routed, w_router, queries, keys, values, d_gated):
    slots = queries.shape[1]
    n, ndp = lax.axis_size("ctx"), lax.axis_size("dp")

    def send(a, flip):
        return lax.ppermute(a, "ctx", [(i, i ^ flip) for i in range(n)])

    def beside(fn, *operands):
        def skip(*ops):
            return jax.tree.map(lambda o: jnp.zeros(o.shape, o.dtype), jax.eval_shape(fn, *ops))

        return lax.cond(route_pos[0, 0] >= -1, fn, skip, *operands)

    def after(value, *others):
        return lax.optimization_barrier((value, *others))[0]

    def widen(part, step, *first):
        other = lax.ppermute(part, "dp", [(i, i ^ step) for i in range(ndp)])
        return jnp.concatenate([part, after(other, *first)], axis=1)

    def exchange_phase(x_routed, w_part, theirs):
        sib, x_sib = send(theirs, 1), send(x_routed, 1)
        step = 2
        while 2 * step < ndp:
            w_part = widen(w_part, step)
            step *= 2
        return sib, x_sib, w_part

    def far_phase(*operands):
        own_out, sib_out = far_grad(*operands)
        *outs, waiting = join(own_out, send(sib_out, 1), queries.shape)
        return outs, waiting

    def tail_phase(terms, *operands):
        shared = lax.all_to_all(terms.reshape(ndp * n, 1, -1), ("dp", "ctx"), 0, 0, tiled=True)
        outs, waiting = beside(far_phase, *operands)
        return outs, waiting, jnp.sum(shared, axis=0)[0] / float(ndp * n * slots // 2)

    out_s, out_d, w_part = cross_pack(route_pos, w_router, keys, values, queries, d_gated)
    in_s, in_d = send(out_s, 2), send(out_d, 3)

    theirs = sib_pack(after(route_pos, out_s), keys, values, queries, d_gated)
    if ndp > 1:
        w_part = widen(w_part, 1, theirs)
    sib, x_sib, w_part = beside(exchange_phase, x_routed, w_part, theirs)
    local, live, near, far, rows_x = local_stats(route_pos, keys, values, queries, d_gated, sib, x_routed, x_sib)
    cross, stats, kept = cross_stats(near, far, in_s, in_d)
    if ndp > 2:
        w_part = widen(w_part, ndp // 2, stats)
    gates, message = pair_gate(live, rows_x, w_part, local, stats, ndp)

    heard = send(message, 2)
    near_dq, near_own, near_sib, near_sum = near_grad(near, local, stats, gates)
    back_s, back_d, dq_low, keep, final, sums = cross_grad(
        cross, kept, stats, local, heard, gates, near_dq, near_sum
    )

    ret_s, ret_d = send(back_s, 2), send(back_d, 3)
    terms = pair_router(gates, sums, rows_x, ndp, n)
    outs, waiting, router_grad = beside(
        tail_phase, terms, far, local, final, gates, keep, dq_low, near_own, near_sib
    )
    dq, dk, dv = add_back(waiting, ret_s, ret_d, outs)
    return dq, dk, dv, router_grad


def body(route_pos, x_routed, w_router, queries, keys, values, d_gated):
    slots, full = queries.shape[1], queries.shape[2]
    n, ndp = lax.axis_size("ctx"), lax.axis_size("dp")
    chips = n // 2
    me, dp_me = lax.axis_index("ctx"), lax.axis_index("dp")
    core = (me % 2).astype(jnp.int32).reshape(1)
    half = full // 2
    groups = GROUPS if (half // HEAD) % GROUPS == 0 else 1
    width = half // groups

    sib_pairs = [(i, i ^ 1) for i in range(n)]

    def forward_pairs(step, flip):
        return [(i, (i + 2 * step) ^ flip) for i in range(n) if i + 2 * step < n]

    def back_pairs(step, flip):
        return [(b, a) for a, b in forward_pairs(step, flip)]

    def to_sib(a):
        return lax.ppermute(a, "ctx", sib_pairs)

    links = [(step, flip) for step in range(1, chips) for flip in (0, 1)]

    w_row = w_router.reshape(1, -1)
    w_parts = [w_row] + [
        lax.ppermute(w_row, "dp", [(i, (i + s) % ndp) for i in range(ndp)]) for s in range(1, ndp)
    ]
    live = (route_pos >= 0).astype(jnp.int32)
    lives = [live, to_sib(live)] + [lax.ppermute(live, "ctx", forward_pairs(*link)) for link in links]
    live_all = jnp.concatenate(lives, axis=0)

    kv_mine, kv_theirs = pack(core, keys, values, groups, width)
    kv_far = [
        [lax.ppermute((kv_theirs if flip else kv_mine)[g], "ctx", forward_pairs(step, flip)) for step, flip in links]
        for g in range(groups)
    ]
    q_mine, q_theirs = pack(core, queries, d_gated, groups, width)
    kv_sib = [to_sib(a) for a in kv_theirs]
    q_sib = [to_sib(a) for a in q_theirs]

    offsets = ((dp_me - jnp.arange(ndp)) % ndp).astype(jnp.int32)
    gate = router_gate(offsets, route_pos, x_routed, w_parts)
    gates = (gate, to_sib(gate))

    accs = (jnp.zeros((1, slots), F32), jnp.zeros((1, slots), F32))
    dq_own, sib_in, kv_own, back = [], [], [], []
    for g in range(groups):
        dq, sib_out, kv_local, kv_remote, accs = attention(
            core, live_all, gates, accs, q_mine[g], q_sib[g], [kv_mine[g], kv_sib[g], *kv_far[g]]
        )
        back.append([lax.ppermute(a, "ctx", back_pairs(*link)) for a, link in zip(kv_remote, links)])
        sib_in.append(to_sib(sib_out))
        dq_own.append(dq)
        kv_own.append(kv_local)

    targets = ((dp_me + jnp.arange(ndp)) % ndp).astype(jnp.int32)
    terms = router_terms(targets, gate, accs[0], to_sib(accs[1]), x_routed, ndp)
    mine = terms[0]
    for s in range(1, ndp):
        mine = mine + lax.ppermute(terms[s], "dp", [(i, (i + s) % ndp) for i in range(ndp)])
    total = mine
    for s in range(1, n):
        total = total + lax.ppermute(mine, "ctx", [(i, (i + s) % n) for i in range(n)])
    router_grad = total[0] / float(ndp * n * slots // 2)

    dq, dk, dv = combine(core, dq_own, sib_in, kv_own, back, queries.shape)
    return dq, dk, dv, router_grad


def solution(mesh):
    placed = (
        P("dp", "ctx"),
        P("dp", "ctx", None),
        P("dp"),
        P("dp", "ctx", None),
        P("dp", "ctx", None),
        P("dp", "ctx", None),
        P("dp", "ctx", None),
    )
    ndp = mesh.shape["dp"]
    paired = mesh.shape["ctx"] == 4 and ndp & (ndp - 1) == 0
    return jax.shard_map(
        swap_body if paired else body,
        mesh=mesh,
        in_specs=placed,
        out_specs=(P("dp", "ctx", None), P("dp", "ctx", None), P("dp", "ctx", None), P("dp")),
        check_vma=False,
    )
```

```python
import functools

import jax
import jax.numpy as jnp
from jax import lax
from jax.experimental import pallas as pl
from jax.experimental.pallas import tpu as pltpu
from jax.sharding import PartitionSpec as P

HEAD = 128
GROUPS = 4
NEG_FILL = -1e30
MIB = 1024 * 1024
BF16 = jnp.bfloat16
F32 = jnp.float32

VMEM = pl.BlockSpec(memory_space=pltpu.VMEM)
SMEM = pl.BlockSpec(memory_space=pltpu.SMEM)


def params(mib=16):
    return pltpu.CompilerParams(vmem_limit_bytes=mib * MIB)


def cost(flops, nbytes, exps=0):
    return pl.CostEstimate(flops=1, bytes_accessed=1, transcendentals=0)


def in_hbm(*arrays):
    return [pltpu.with_memory_space_constraint(a, pltpu.HBM) for a in arrays]


def nt(a, b):
    return lax.dot_general(a, b, (((1,), (1,)), ((), ())), preferred_element_type=F32)


def nn(a, b):
    return lax.dot_general(a, b, (((1,), (0,)), ((), ())), preferred_element_type=F32)


def tn(a, b):
    return lax.dot_general(a, b, (((0,), (0,)), ((), ())), preferred_element_type=F32)


def pack_kernel(groups, width, core_ref, first_ref, second_ref, *outs):
    half = first_ref.shape[-1] // 2
    core = core_ref[0]
    for side in range(2):
        base = (core if side == 0 else 1 - core) * half
        for g in range(groups):
            out = outs[side * groups + g]
            cols = pl.ds(pl.multiple_of(base + g * width, HEAD), width)
            out[0] = first_ref[0, :, cols].astype(BF16)
            out[1] = second_ref[0, :, cols].astype(BF16)


def pack(core, first, second, groups, width):
    slots = first.shape[1]
    out = jax.ShapeDtypeStruct((2, slots, width), BF16)
    res = pl.pallas_call(
        functools.partial(pack_kernel, groups, width),
        out_shape=[out] * (2 * groups),
        in_specs=[SMEM, VMEM, VMEM],
        out_specs=[VMEM] * (2 * groups),
        compiler_params=params(),
        cost_estimate=cost(0, 2 * first.size * 4),
        name="pack",
    )(core, first, second)
    return res[:groups], res[groups:]


def gate_kernel(parts, offset_ref, pos_ref, x_ref, *refs):
    w_refs, out_ref = refs[:parts], refs[parts]
    chunk = w_refs[0].shape[-1]
    total = jnp.zeros((8, x_ref.shape[1]), F32)
    for s in range(parts):
        cols = pl.ds(pl.multiple_of(offset_ref[s] * chunk, HEAD), chunk)
        w_rows = jnp.broadcast_to(w_refs[s][...].astype(F32), (8, chunk)).astype(BF16)
        total = total + nt(w_rows, x_ref[0, :, cols])
    gate = 1.0 / (1.0 + jnp.exp(-total[0:1]))
    out_ref[...] = jnp.where(pos_ref[...] >= 0, gate, 0.0)


def router_gate(offsets, route_pos, x_routed, w_parts):
    parts = len(w_parts)
    return pl.pallas_call(
        functools.partial(gate_kernel, parts),
        out_shape=jax.ShapeDtypeStruct(route_pos.shape, F32),
        in_specs=[SMEM] + [VMEM] * (2 + parts),
        out_specs=VMEM,
        compiler_params=params(),
        cost_estimate=cost(16 * x_routed.size, x_routed.size * 2),
        name="router_gate",
    )(offsets, route_pos, x_routed, *w_parts)


def attention_kernel(remote, scale, core_ref, live_ref, gate_own, gate_sib, acc_own, acc_sib, q_own, q_sib, *refs):
    chunks = 2 + remote
    kv = refs[:chunks]
    outs = refs[chunks:]
    dq_own, sib_out, kv_own = outs[:3]
    kv_remote = outs[3 : 3 + remote]
    sum_own, sum_sib = outs[3 + remote :]
    slots, width = q_own.shape[1], q_own.shape[2]
    core = core_ref[0]
    key = lax.broadcasted_iota(jnp.int32, (slots, slots), 0)
    query = lax.broadcasted_iota(jnp.int32, (slots, slots), 1)
    counts = [jnp.sum(live_ref[i : i + 1], axis=1, keepdims=True) for i in range(chunks)]
    lives = [key < counts[i] for i in range(chunks)]
    own_later = core == 1
    bias_rows = []
    for i in range(chunks):
        live = lives[i]
        if i == 0:
            pair = (live & (key <= query), live & jnp.logical_not(own_later))
        elif i == 1:
            pair = (live & own_later, live & (key <= query))
        else:
            pair = (live, live)
        bias_rows.append(jnp.concatenate([jnp.where(p, 0.0, NEG_FILL) for p in pair], axis=1))
    bias = jnp.concatenate(bias_rows, axis=0)
    gates = jnp.concatenate([gate_own[...], gate_sib[...]], axis=1)
    total = jnp.zeros((1, 2 * slots), F32)
    for h in range(width // HEAD):
        cols = slice(h * HEAD, (h + 1) * HEAD)
        q = jnp.concatenate([q_own[0, :, cols], q_sib[0, :, cols]], axis=0)
        dg = jnp.concatenate([q_own[1, :, cols], q_sib[1, :, cols]], axis=0)
        k = jnp.concatenate([r[0, :, cols] for r in kv], axis=0)
        v = jnp.concatenate([r[1, :, cols] for r in kv], axis=0)
        scores = nt(k, q) * scale + bias
        top = jnp.max(scores, axis=0, keepdims=True)
        e = jnp.exp(scores - top)
        inverse = 1.0 / jnp.sum(e, axis=0, keepdims=True)
        gw = nt(v, dg)
        delta = jnp.sum(e * gw, axis=0, keepdims=True) * inverse
        total = total + delta
        weights = e * (inverse * gates)
        dv = nn(weights.astype(BF16), dg)
        ds = (weights * ((gw - delta) * scale)).astype(BF16)
        dk = nn(ds, q)
        dq = tn(ds, k)
        dq_own[:, cols] = dq[:slots].astype(dq_own.dtype)
        sib_out[0, :, cols] = dq[slots:].astype(BF16)
        kv_own[0, :, cols] = dk[:slots].astype(BF16)
        kv_own[1, :, cols] = dv[:slots].astype(BF16)
        sib_out[1, :, cols] = dk[slots : 2 * slots].astype(BF16)
        sib_out[2, :, cols] = dv[slots : 2 * slots].astype(BF16)
        for i in range(remote):
            rows = slice((2 + i) * slots, (3 + i) * slots)
            kv_remote[i][0, :, cols] = dk[rows].astype(BF16)
            kv_remote[i][1, :, cols] = dv[rows].astype(BF16)
    sum_own[...] = acc_own[...] + total[:, :slots]
    sum_sib[...] = acc_sib[...] + total[:, slots:]


def attention(core, live, gates, accs, q_own, q_sib, kv):
    remote = len(kv) - 2
    _, slots, width = q_own.shape
    pair = jax.ShapeDtypeStruct((2, slots, width), BF16)
    row = jax.ShapeDtypeStruct((1, slots), F32)
    outs = [
        jax.ShapeDtypeStruct((slots, width), BF16),
        jax.ShapeDtypeStruct((3, slots, width), BF16),
        pair,
        *([pair] * remote),
        row,
        row,
    ]
    keys = (2 + remote) * slots
    res = pl.pallas_call(
        functools.partial(attention_kernel, remote, HEAD**-0.5),
        out_shape=outs,
        in_specs=[SMEM] + [VMEM] * (7 + len(kv)),
        out_specs=[VMEM] * len(outs),
        compiler_params=params(48),
        cost_estimate=cost(20 * slots * keys * width, 8 * keys * width + 20 * slots * width, 2 * slots * keys * width // HEAD),
        name="attention",
    )(core, live, *gates, *accs, q_own, q_sib, *kv)
    return res[0], res[1], res[2], res[3 : 3 + remote], (res[3 + remote], res[4 + remote])


def combine_kernel(groups, width, remote, core_ref, *refs):
    dq_own, sib, kv_own = refs[:groups], refs[groups : 2 * groups], refs[2 * groups : 3 * groups]
    back = refs[3 * groups : 3 * groups + groups * remote]
    dq_out, dk_out, dv_out = refs[3 * groups + groups * remote :]
    half = groups * width
    core = core_ref[0]
    for g in range(groups):
        own = pl.ds(pl.multiple_of(core * half + g * width, HEAD), width)
        other = pl.ds(pl.multiple_of((1 - core) * half + g * width, HEAD), width)
        dq_out[0, :, own] = dq_own[g][...].astype(F32)
        dq_out[0, :, other] = sib[g][0].astype(F32)
        for i, out in enumerate((dk_out, dv_out)):
            mine = kv_own[g][i].astype(F32)
            theirs = sib[g][1 + i].astype(F32)
            for r in range(remote):
                part = back[g * remote + r][i].astype(F32)
                if r % 2 == 0:
                    mine = mine + part
                else:
                    theirs = theirs + part
            out[0, :, own] = mine
            out[0, :, other] = theirs


def combine(core, dq_own, sib, kv_own, back, shape):
    groups = len(dq_own)
    remote = len(back[0])
    out = jax.ShapeDtypeStruct(shape, F32)
    flat = [*dq_own, *sib, *kv_own, *(b for group in back for b in group)]
    return pl.pallas_call(
        functools.partial(combine_kernel, groups, dq_own[0].shape[-1], remote),
        out_shape=[out] * 3,
        in_specs=[SMEM] + [VMEM] * len(flat),
        out_specs=[VMEM] * 3,
        compiler_params=params(48),
        cost_estimate=cost(0, 3 * out.size * 6),
        name="combine",
    )(core, *flat)


def router_kernel(parts, target_ref, gate_ref, own_ref, sib_ref, x_ref, *outs):
    gate = gate_ref[...]
    grad = (own_ref[...] + sib_ref[...]) * gate * (1.0 - gate)
    high = grad.astype(BF16)
    rest = grad - high.astype(F32)
    mid = rest.astype(BF16)
    low = (rest - mid.astype(F32)).astype(BF16)
    row = lax.broadcasted_iota(jnp.int32, (8, grad.shape[1]), 0)
    lhs = jnp.where(row == 0, high.astype(F32), jnp.where(row == 1, mid.astype(F32), jnp.where(row == 2, low.astype(F32), 0.0)))
    lhs = lhs.astype(BF16)
    chunk = outs[0].shape[-1]
    for s in range(parts):
        cols = pl.ds(pl.multiple_of(target_ref[s] * chunk, HEAD), chunk)
        outs[s][...] = jnp.sum(nn(lhs, x_ref[0, :, cols]), axis=0, keepdims=True)


def router_terms(targets, gate, own, sib, x_routed, parts):
    chunk = x_routed.shape[-1] // parts
    return pl.pallas_call(
        functools.partial(router_kernel, parts),
        out_shape=[jax.ShapeDtypeStruct((1, chunk), F32)] * parts,
        in_specs=[SMEM] + [VMEM] * 4,
        out_specs=[VMEM] * parts,
        compiler_params=params(),
        cost_estimate=cost(16 * x_routed.size, x_routed.size * 2),
        name="router_terms",
    )(targets, gate, own, sib, x_routed)


def here():
    me = lax.axis_index("ctx")
    return lax.rem(me, 2), lax.div(me, 2)


MARK = 2.0**60
MARK_LIMIT = 2.0**50


def live_rows(pos_ref, slots):
    count = jnp.sum((pos_ref[...] >= 0).astype(jnp.int32), axis=1, keepdims=True)
    return lax.broadcasted_iota(jnp.int32, (slots, HEAD), 0) < count


def mark_dead(keys, live):
    width = keys.shape[-1]
    mask = jnp.concatenate([live] * (width // HEAD), axis=1)
    return jnp.where(mask, keys.astype(F32), MARK).astype(BF16)


def cross_pack_kernel(pos_any, w_any, k_ref, v_ref, q_ref, dg_ref, straight, diag, w_out, wide, pos_ref, w_ref, sems):
    small = [pltpu.make_async_copy(pos_any, pos_ref, sems.at[4]), pltpu.make_async_copy(w_any, w_ref, sems.at[5])]
    for c in small:
        c.start()
    slots, width = straight.shape[1], straight.shape[2]
    half = k_ref.shape[-1] // 2
    core, chip = here()
    ends = ((straight, core * half), (diag, (1 - core) * half))

    def copies(first, second, targets, offset):
        out = []
        for i, (end, start) in enumerate(ends):
            cols = pl.ds(pl.multiple_of(start + offset, HEAD), width)
            out.append(pltpu.make_async_copy(first.at[0, :, cols], end.at[0], sems.at[2 * i]))
            out.append(pltpu.make_async_copy(second.at[0, :, cols], targets[i], sems.at[2 * i + 1]))
        for c in out:
            c.start()
        for c in out:
            c.wait()

    @pl.when(chip == 0)
    def _():
        copies(k_ref, v_ref, (straight.at[1], diag.at[1]), 0)
        small[0].wait()
        live = live_rows(pos_ref, slots)
        for end, _ in ends:
            end[0] = mark_dead(end[0], live)

    @pl.when(chip != 0)
    def _():
        copies(q_ref, dg_ref, (wide.at[0], wide.at[1]), width)
        small[0].wait()
        for i, (end, _) in enumerate(ends):
            end[1] = wide[i].astype(BF16)

    small[1].wait()
    w_out[...] = w_ref[...].astype(F32).reshape(w_out.shape)


def cross_pack(route_pos, w_router, keys, values, queries, d_gated):
    _, slots, full = keys.shape
    cross = pltpu.VMEM((2, slots, full // 4), BF16)
    hbm = pl.BlockSpec(memory_space=pltpu.HBM)
    return pl.pallas_call(
        cross_pack_kernel,
        out_shape=[cross, cross, jax.ShapeDtypeStruct((1, w_router.shape[0]), F32)],
        in_specs=[hbm] * 6,
        out_specs=[VMEM] * 3,
        scratch_shapes=[
            pltpu.VMEM((2, slots, full // 4), F32),
            pltpu.VMEM(route_pos.shape, jnp.int32),
            pltpu.VMEM(w_router.shape, BF16),
            pltpu.SemaphoreType.DMA((6,)),
        ],
        compiler_params=params(),
        cost_estimate=cost(0, 10 * slots * full),
        name="cross_pack",
    )(*in_hbm(route_pos, w_router, keys, values, queries, d_gated))


def sib_pack_kernel(pos_ref, k_ref, v_ref, q_ref, dg_ref, out, wide, sems):
    slots, half = out.shape[1], out.shape[2]
    cols = pl.ds(pl.multiple_of((1 - here()[0]) * half, HEAD), half)
    sources = ((k_ref, out.at[0]), (dg_ref, wide), (v_ref, out.at[1]), (q_ref, out.at[2]))
    copies = [pltpu.make_async_copy(src.at[0, :, cols], dst, sems.at[i]) for i, (src, dst) in enumerate(sources)]
    for c in copies:
        c.start()
    live = live_rows(pos_ref, slots)
    copies[0].wait()
    out[0] = mark_dead(out[0], live)
    copies[1].wait()
    out[3] = wide[...].astype(BF16)
    copies[2].wait()
    copies[3].wait()


def sib_pack(route_pos, keys, values, queries, d_gated):
    _, slots, full = keys.shape
    hbm = pl.BlockSpec(memory_space=pltpu.HBM)
    return pl.pallas_call(
        sib_pack_kernel,
        out_shape=pltpu.VMEM((4, slots, full // 2), BF16),
        in_specs=[VMEM, hbm, hbm, hbm, hbm],
        out_specs=VMEM,
        scratch_shapes=[pltpu.VMEM((slots, full // 2), F32), pltpu.SemaphoreType.DMA((4,))],
        compiler_params=params(),
        cost_estimate=cost(0, 20 * slots * full),
        name="sib_pack",
    )(route_pos, *in_hbm(keys, values, queries, d_gated))


def pair_gate_kernel(parts, live_ref, rows_x, w_ref, local, stats, out_ref, message):
    chunk = w_ref.shape[1] // parts
    slots = rows_x.shape[1]
    for i in range(2):
        total = jnp.zeros((8, slots), F32)
        for j in range(parts):
            w_rows = jnp.broadcast_to(w_ref[:, j * chunk : (j + 1) * chunk], (8, chunk)).astype(BF16)
            cols = pl.ds(pl.multiple_of((lax.axis_index("dp") ^ j) * chunk, HEAD), chunk)
            total = total + nt(w_rows, rows_x[i, :, cols])
        lanes = slice(i * slots, (i + 1) * slots)
        out_ref[:, lanes] = live_ref[:, lanes] / (1.0 + jnp.exp(-total[0:1]))
    first = here()[1] == 0
    heads = stats.shape[1]
    for i in range(3):
        message[i] = jnp.where(first, stats[i], local[i, heads:])
    message[3] = jnp.broadcast_to(out_ref[...], message.shape[1:])


def pair_gate(live, rows_x, w_full, local, stats, parts):
    _, heads, lanes = stats.shape
    return pl.pallas_call(
        functools.partial(pair_gate_kernel, parts),
        out_shape=[jax.ShapeDtypeStruct(live.shape, F32), jax.ShapeDtypeStruct((4, heads, lanes), F32)],
        in_specs=[VMEM] * 5,
        out_specs=[VMEM] * 2,
        compiler_params=params(),
        cost_estimate=cost(16 * rows_x.size, rows_x.size * 2),
        name="router_gate",
    )(live, rows_x, w_full, local, stats)


def local_mask(core, pair):
    slots = pair.shape[1] // 2
    key = lax.broadcasted_iota(jnp.int32, (slots, slots), 0)
    query = lax.broadcasted_iota(jnp.int32, (slots, slots), 1)
    causal = key <= query
    own_live = pair[0, :slots, :slots].astype(F32) < MARK_LIMIT
    sib_live = pair[0, slots:, :slots].astype(F32) < MARK_LIMIT
    own_rows = jnp.concatenate([own_live & causal, own_live & (core == 0)], axis=1)
    sib_rows = jnp.concatenate([sib_live & (core == 1), sib_live & causal], axis=1)
    return jnp.concatenate([own_rows, sib_rows], axis=0)


def kept_stats(scores, gw, kept, stats, h):
    top = jnp.max(scores, axis=0, keepdims=True)
    e = jnp.exp(scores - top).astype(BF16)
    gw = gw.astype(BF16)
    kept[0, h] = e
    kept[1, h] = gw
    e = e.astype(F32)
    stats[0, h : h + 1] = top
    stats[1, h : h + 1] = jnp.sum(e, axis=0, keepdims=True)
    stats[2, h : h + 1] = jnp.sum(e * gw.astype(F32), axis=0, keepdims=True)


def partial_stats(scores, gw, stats, h):
    top = jnp.max(scores, axis=0, keepdims=True)
    e = jnp.exp(scores - top)
    stats[0, h : h + 1] = top
    stats[1, h : h + 1] = jnp.sum(e, axis=0, keepdims=True)
    stats[2, h : h + 1] = jnp.sum(e * gw, axis=0, keepdims=True)


def local_stats_kernel(scale, pos_ref, k_ref, v_ref, q_ref, dg_ref, sib, x_ref, x_sib, stats, live, near, far, rows_x, wide, sems, x_sems):
    slots, half = sib.shape[1], sib.shape[2]
    width = half // 2
    core = here()[0]
    own, other = slice(0, slots), slice(slots, 2 * slots)
    stages = []
    for g, pair in enumerate((near, far)):
        cols = slice(g * width, (g + 1) * width)
        held = pl.ds(pl.multiple_of(core * half + g * width, HEAD), width)
        copies = [
            pltpu.make_async_copy(ref.at[0, :, held], pair.at[j, own], sems.at[8 * g + j])
            for j, ref in enumerate((k_ref, v_ref, q_ref))
        ]
        copies.append(pltpu.make_async_copy(dg_ref.at[0, :, held], wide.at[:, cols], sems.at[8 * g + 3]))
        for j in range(4):
            copies.append(pltpu.make_async_copy(sib.at[j, :, cols], pair.at[j, other], sems.at[8 * g + 4 + j]))
        for c in copies:
            c.start()
        stages.append(copies)
    x_copies = []
    depth = x_ref.shape[2] // 2
    for i, ref in enumerate((x_ref, x_sib)):
        for g in range(2):
            cols = slice(g * depth, (g + 1) * depth)
            x_copies.append(pltpu.make_async_copy(ref.at[0, :, cols], rows_x.at[i, :, cols], x_sems.at[2 * i + g]))
    for c in x_copies:
        c.start()
    rows_live = live_rows(pos_ref, slots)
    mask = None
    for g, pair in enumerate((near, far)):
        cols = slice(g * width, (g + 1) * width)
        for c in stages[g]:
            c.wait()
        pair[0, own] = mark_dead(pair[0, own], rows_live)
        pair[3, own] = wide[:, cols].astype(BF16)
        if mask is None:
            mask = local_mask(core, pair)
            marks = nt(jnp.ones((8, HEAD), BF16), pair[0, :, :HEAD])[0:1]
            live[...] = jnp.where(marks < MARK_LIMIT, 1.0, 0.0)
        for h in range(width // HEAD):
            at = slice(h * HEAD, (h + 1) * HEAD)
            scores = jnp.where(mask, nt(pair[0, :, at], pair[2, :, at]) * scale, NEG_FILL)
            partial_stats(scores, nt(pair[1, :, at], pair[3, :, at]), stats, g * width // HEAD + h)
    for c in x_copies:
        c.wait()


def local_stats(route_pos, keys, values, queries, d_gated, sib, x_routed, x_sib):
    _, slots, half = sib.shape
    heads = half // HEAD
    anywhere = pl.BlockSpec(memory_space=pl.ANY)
    return pl.pallas_call(
        functools.partial(local_stats_kernel, HEAD**-0.5),
        out_shape=[
            jax.ShapeDtypeStruct((3, heads, 2 * slots), F32),
            jax.ShapeDtypeStruct((1, 2 * slots), F32),
            pltpu.VMEM((4, 2 * slots, half // 2), BF16),
            pltpu.VMEM((4, 2 * slots, half // 2), BF16),
            pltpu.VMEM((2, slots, x_routed.shape[2]), BF16),
        ],
        in_specs=[VMEM] + [anywhere] * 7,
        out_specs=[VMEM] * 5,
        scratch_shapes=[pltpu.VMEM((slots, half), F32), pltpu.SemaphoreType.DMA((16,)), pltpu.SemaphoreType.DMA((4,))],
        compiler_params=params(),
        cost_estimate=cost(16 * slots * slots * half, 16 * slots * half, 4 * slots * slots * half // HEAD),
        name="local_stats",
    )(route_pos, *in_hbm(keys, values, queries, d_gated), sib, x_routed, x_sib)


def cross_stats_kernel(scale, near, far, straight, diag, cross, stats, kept):
    slots, width = straight.shape[1], straight.shape[2]
    chip = here()[1]
    top, bottom = slice(0, slots), slice(slots, 2 * slots)

    @pl.when(chip == 0)
    def _():
        for part in range(2):
            cross[part] = far[part]
            cross[2 + part, top] = straight[part]
            cross[2 + part, bottom] = diag[part]

    @pl.when(chip != 0)
    def _():
        for part in range(2):
            cross[part, top] = straight[part]
            cross[part, bottom] = diag[part]
            cross[2 + part] = near[2 + part]

    live = cross[0, :, :HEAD].astype(F32) < MARK_LIMIT
    mask = jnp.concatenate([live] * (2 * slots // HEAD), axis=1)
    heads = width // HEAD
    for h in range(heads):
        cols = slice(h * HEAD, (h + 1) * HEAD)
        scores = jnp.where(mask, nt(cross[0, :, cols], cross[2, :, cols]) * scale, NEG_FILL)
        kept_stats(scores, nt(cross[1, :, cols], cross[3, :, cols]), kept, stats, h)


def cross_stats(near, far, straight, diag):
    _, slots, width = straight.shape
    heads = width // HEAD
    return pl.pallas_call(
        functools.partial(cross_stats_kernel, HEAD**-0.5),
        out_shape=[
            pltpu.VMEM((4, 2 * slots, width), BF16),
            jax.ShapeDtypeStruct((3, heads, 2 * slots), F32),
            pltpu.VMEM((2, heads, 2 * slots, 2 * slots), BF16),
        ],
        in_specs=[VMEM] * 4,
        out_specs=[VMEM] * 3,
        compiler_params=params(),
        cost_estimate=cost(16 * slots * slots * width, 32 * slots * width, 4 * slots * slots * heads),
        name="cross_stats",
    )(near, far, straight, diag)


NONE = (-3e38, 0.0, 0.0)


def merge(first, second):
    top = jnp.maximum(first[0], second[0])
    a, b = jnp.exp(first[0] - top), jnp.exp(second[0] - top)
    inverse = 1.0 / (first[1] * a + second[1] * b)
    return a * inverse, (first[2] * a + second[2] * b) * inverse


def choose(flag, yes, no):
    return [jnp.where(flag, y, n) for y, n in zip(yes, no)]


def gradients(q, k, dg, e, gw, scale, factor, delta):
    weights = e * factor
    ds = (weights * ((gw - delta) * scale)).astype(BF16)
    return tn(ds, k), nn(ds, q), nn(weights.astype(BF16), dg)


def local_gradients(pair, h, mask, scale, top, factor, delta):
    cols = slice(h * HEAD, (h + 1) * HEAD)
    k, v, q, dg = [pair[i, :, cols] for i in range(4)]
    e = jnp.exp(jnp.where(mask, nt(k, q) * scale, NEG_FILL) - top)
    return gradients(q, k, dg, e, nt(v, dg), scale, factor, delta)


def near_grad_kernel(scale, pair, local, stats, gates, dq_out, own_out, sib_out, sum_out):
    slots, width = own_out.shape[1], own_out.shape[2]
    heads = width // HEAD
    first = here()[1] == 0
    near = [local[i, :heads] for i in range(3)]
    factor, delta = merge(near, choose(first, NONE, [stats[i] for i in range(3)]))
    factor = factor * gates[...]
    sum_out[...] = jnp.sum(delta, axis=0, keepdims=True)
    mask = local_mask(here()[0], pair)
    for h in range(heads):
        cols = slice(h * HEAD, (h + 1) * HEAD)
        row = slice(h, h + 1)
        dq, dk, dv = local_gradients(pair, h, mask, scale, near[0][row], factor[row], delta[row])
        dq_out[:, cols] = dq
        for i, part in enumerate((dk, dv)):
            own_out[i, :, cols] = part[:slots].astype(BF16)
            sib_out[i, :, cols] = part[slots:].astype(BF16)


def near_grad(pair, local, stats, gates):
    _, rows, width = pair.shape
    slots = rows // 2
    out = pltpu.VMEM((2, slots, width), BF16)
    return pl.pallas_call(
        functools.partial(near_grad_kernel, HEAD**-0.5),
        out_shape=[pltpu.VMEM((2 * slots, width), F32), out, out, jax.ShapeDtypeStruct(gates.shape, F32)],
        in_specs=[VMEM] * 4,
        out_specs=[VMEM] * 4,
        compiler_params=params(),
        cost_estimate=cost(20 * slots * slots * width, 40 * slots * width),
        name="near_grad",
    )(pair, local, stats, gates)


def cross_grad_kernel(scale, cross, kept, stats, local, heard, gates, near_dq, near_sum, straight, diag, dq_out, keep, final, sum_out):
    slots, width = straight.shape[1], straight.shape[2]
    heads = width // HEAD
    first = here()[1] == 0
    late = jnp.where(first, 0.0, 1.0)
    mine = [stats[i] for i in range(3)]
    other = [heard[i] for i in range(3)]
    near = [local[i, :heads] for i in range(3)]
    far = [local[i, heads:] for i in range(3)]
    factor, delta = merge(mine, choose(first, other, near))
    factor = factor * jnp.where(first, heard[3], jnp.broadcast_to(gates[...], factor.shape))
    final[0], final[1] = merge(far, choose(first, NONE, other))
    sum_out[...] = near_sum[...] + jnp.sum(final[1], axis=0, keepdims=True)
    for h in range(heads):
        cols = slice(h * HEAD, (h + 1) * HEAD)
        row = slice(h, h + 1)
        dq, dk, dv = gradients(
            cross[2, :, cols], cross[0, :, cols], cross[3, :, cols],
            kept[0, h].astype(F32), kept[1, h].astype(F32), scale, factor[row], delta[row],
        )
        dq_out[:, cols] = (near_dq[:, cols] + late * dq).astype(BF16)
        keep[0, :, cols] = dk.astype(BF16)
        keep[1, :, cols] = dv.astype(BF16)
        sent = jnp.where(first, dq, dk).astype(BF16)
        straight[0, :, cols] = sent[:slots]
        diag[0, :, cols] = sent[slots:]
        straight[1, :, cols] = dv[:slots].astype(BF16)
        diag[1, :, cols] = dv[slots:].astype(BF16)


def cross_grad(cross, kept, stats, local, heard, gates, near_dq, near_sum):
    _, rows, width = cross.shape
    slots = rows // 2
    out = pltpu.VMEM((2, slots, width), BF16)
    return pl.pallas_call(
        functools.partial(cross_grad_kernel, HEAD**-0.5),
        out_shape=[
            out,
            out,
            pltpu.VMEM((rows, width), BF16),
            pltpu.VMEM((2, rows, width), BF16),
            jax.ShapeDtypeStruct((2, width // HEAD, rows), F32),
            jax.ShapeDtypeStruct((1, rows), F32),
        ],
        in_specs=[VMEM] * 8,
        out_specs=[VMEM] * 6,
        compiler_params=params(),
        cost_estimate=cost(24 * slots * slots * width, 64 * slots * width),
        name="cross_grad",
    )(cross, kept, stats, local, heard, gates, near_dq, near_sum)


def far_grad_kernel(scale, pair, local, final, gates, keep, near_dq, near_own, near_sib, own_out, sib_out):
    slots, width = pair.shape[1] // 2, pair.shape[2]
    heads = width // HEAD
    early = jnp.where(here()[1] == 0, 1.0, 0.0)
    factor = final[0] * gates[...]
    mask = local_mask(here()[0], pair)
    own_out[0, :, :width] = near_dq[:slots]
    sib_out[0, :, :width] = near_dq[slots:]
    for i in range(2):
        own_out[1 + i, :, :width] = near_own[i]
        sib_out[1 + i, :, :width] = near_sib[i]
    for h in range(heads):
        cols = slice(width + h * HEAD, width + (h + 1) * HEAD)
        at = slice(h * HEAD, (h + 1) * HEAD)
        row = slice(h, h + 1)
        top = local[0, heads + h : heads + h + 1]
        dq, dk, dv = local_gradients(pair, h, mask, scale, top, factor[row], final[1, row])
        dk = dk + early * keep[0, :, at].astype(F32)
        dv = dv + early * keep[1, :, at].astype(F32)
        for i, part in enumerate((dq, dk, dv)):
            own_out[i, :, cols] = part[:slots].astype(BF16)
            sib_out[i, :, cols] = part[slots:].astype(BF16)


def far_grad(pair, local, final, gates, keep, near_dq, near_own, near_sib):
    _, rows, width = pair.shape
    slots, half = rows // 2, 2 * width
    out = jax.ShapeDtypeStruct((3, slots, half), BF16)
    return pl.pallas_call(
        functools.partial(far_grad_kernel, HEAD**-0.5),
        out_shape=[out, out],
        in_specs=[VMEM] * 8,
        out_specs=[VMEM] * 2,
        compiler_params=params(),
        cost_estimate=cost(20 * slots * slots * half, 40 * slots * half),
        name="far_grad",
    )(pair, local, final, gates, keep, near_dq, near_own, near_sib)


def join_kernel(own, sib, dq_out, dk_out, dv_out, waiting, low, total, in_sems, out_sems):
    slots, half = own.shape[1], own.shape[2]
    width = half // 2
    core, chip = here()
    ends = ((own, core * half), (sib, (1 - core) * half))
    loads = [
        [pltpu.make_async_copy(part.at[j], low.at[i, j], in_sems.at[3 * i + j]) for j in range(3)]
        for i, (part, _) in enumerate(ends)
    ]
    for c in loads[0] + loads[1]:
        c.start()
    stores = []
    for i, (_, start) in enumerate(ends):
        cols = pl.ds(pl.multiple_of(start, HEAD), half)
        for j, out in enumerate((dq_out, dk_out, dv_out)):
            loads[i][j].wait()
            total[i, j] = low[i, j].astype(F32)
            stores.append(pltpu.make_async_copy(total.at[i, j], out.at[0, :, cols], out_sems.at[3 * i + j]))
            stores[-1].start()
        waiting[i, 0] = jnp.where(chip == 0, total[i, 1, :, :width], total[i, 0, :, width:]).astype(BF16)
        waiting[i, 1] = low[i, 2, :, :width]
    for c in stores:
        c.wait()


def join(own, sib, shape):
    out = pltpu.HBM(shape, F32)
    _, slots, half = own.shape
    anywhere = pl.BlockSpec(memory_space=pl.ANY)
    hbm = pl.BlockSpec(memory_space=pltpu.HBM)
    return pl.pallas_call(
        join_kernel,
        out_shape=[out] * 3 + [pltpu.VMEM((2, 2, slots, half // 2), BF16)],
        in_specs=[anywhere] * 2,
        out_specs=[hbm] * 3 + [VMEM],
        scratch_shapes=[
            pltpu.VMEM((2, 3, slots, half), BF16),
            pltpu.VMEM((2, 3, slots, half), F32),
            pltpu.SemaphoreType.DMA((6,)),
            pltpu.SemaphoreType.DMA((6,)),
        ],
        compiler_params=params(),
        cost_estimate=cost(0, 72 * own.size),
        name="join",
    )(own, sib)


def add_back_kernel(waiting, straight, diag, dq_in, dk_in, dv_in, dq_out, dk_out, dv_out, total, sems):
    width = straight.shape[2]
    core, chip = here()
    ends = ((straight, 2 * core * width), (diag, 2 * (1 - core) * width))

    def store(i, j, out, offset):
        cols = pl.ds(pl.multiple_of(ends[i][1] + offset, HEAD), width)
        copy = pltpu.make_async_copy(total.at[i, j], out.at[0, :, cols], sems.at[2 * i + j])
        copy.start()
        return copy

    for i, (back, _) in enumerate(ends):
        for j in range(2):
            total[i, j] = waiting[i, j].astype(F32) + back[j].astype(F32)

    @pl.when(chip == 0)
    def _():
        copies = [store(i, j, out, 0) for i in range(2) for j, out in enumerate((dk_out, dv_out))]
        for c in copies:
            c.wait()

    @pl.when(chip != 0)
    def _():
        copies = [store(i, 0, dq_out, width) for i in range(2)]
        for c in copies:
            c.wait()


def add_back(waiting, straight, diag, outs):
    hbm = pl.BlockSpec(memory_space=pltpu.HBM)
    return pl.pallas_call(
        add_back_kernel,
        out_shape=[pltpu.HBM(o.shape, F32) for o in outs],
        in_specs=[VMEM] * 3 + [hbm] * 3,
        out_specs=[hbm] * 3,
        scratch_shapes=[pltpu.VMEM(waiting.shape, F32), pltpu.SemaphoreType.DMA((4,))],
        input_output_aliases={3: 0, 4: 1, 5: 2},
        compiler_params=params(),
        cost_estimate=cost(0, 12 * waiting.size),
        name="add_back",
    )(waiting, straight, diag, *in_hbm(*outs))


def pair_router_kernel(gates_ref, sum_ref, rows_x, out_ref):
    gates = gates_ref[...]
    grad = sum_ref[...] * gates * (1.0 - gates)
    high = grad.astype(BF16)
    rest = grad - high.astype(F32)
    mid = rest.astype(BF16)
    low = (rest - mid.astype(F32)).astype(BF16)
    slots = rows_x.shape[1]
    row = lax.broadcasted_iota(jnp.int32, (8, grad.shape[1]), 0)
    lhs = jnp.where(row == 0, high.astype(F32), jnp.where(row == 1, mid.astype(F32), jnp.where(row == 2, low.astype(F32), 0.0)))
    lhs = lhs.astype(BF16)
    term = jnp.sum(nn(lhs[:, :slots], rows_x[0]) + nn(lhs[:, slots:], rows_x[1]), axis=0, keepdims=True)
    parts, copies, _, chunk = out_ref.shape
    for j in range(parts):
        for i in range(copies):
            out_ref[j, i] = term[:, j * chunk : (j + 1) * chunk]


def pair_router(gates, sums, rows_x, parts, copies):
    chunk = rows_x.shape[-1] // parts
    return pl.pallas_call(
        pair_router_kernel,
        out_shape=pltpu.VMEM((parts, copies, 1, chunk), F32),
        in_specs=[VMEM] * 3,
        out_specs=VMEM,
        compiler_params=params(),
        cost_estimate=cost(32 * rows_x.size, rows_x.size * 4),
        name="router_terms",
    )(gates, sums, rows_x)


def swap_body(route_pos, x_routed, w_router, queries, keys, values, d_gated):
    slots = queries.shape[1]
    n, ndp = lax.axis_size("ctx"), lax.axis_size("dp")

    def send(a, flip):
        return lax.ppermute(a, "ctx", [(i, i ^ flip) for i in range(n)])

    def beside(fn, *operands):
        def skip(*ops):
            return jax.tree.map(lambda o: jnp.zeros(o.shape, o.dtype), jax.eval_shape(fn, *ops))

        return lax.cond(route_pos[0, 0] >= -1, fn, skip, *operands)

    def after(value, *others):
        return lax.optimization_barrier((value, *others))[0]

    def widen(part, step, *first):
        other = lax.ppermute(part, "dp", [(i, i ^ step) for i in range(ndp)])
        return jnp.concatenate([part, after(other, *first)], axis=1)

    def exchange_phase(x_routed, w_part, theirs):
        sib, x_sib = send(theirs, 1), send(x_routed, 1)
        step = 2
        while 2 * step < ndp:
            w_part = widen(w_part, step)
            step *= 2
        return sib, x_sib, w_part

    def tail_phase(terms, *operands):
        own_out, sib_out = far_grad(*operands)
        sib_in = send(sib_out, 1)
        shared = lax.all_to_all(after(terms, own_out).reshape(ndp * n, 1, -1), ("dp", "ctx"), 0, 0, tiled=True)
        *outs, waiting = join(own_out, sib_in, queries.shape)
        return outs, waiting, jnp.sum(after(shared, waiting), axis=0)[0] / float(ndp * n * slots // 2)

    out_s, out_d, w_part = cross_pack(route_pos, w_router, keys, values, queries, d_gated)
    in_s, in_d = send(out_s, 2), send(out_d, 3)

    theirs = sib_pack(after(route_pos, out_s), keys, values, queries, d_gated)
    if ndp > 1:
        w_part = widen(w_part, 1, theirs)
    sib, x_sib, w_part = beside(exchange_phase, x_routed, w_part, theirs)
    local, live, near, far, rows_x = local_stats(route_pos, keys, values, queries, d_gated, sib, x_routed, x_sib)
    cross, stats, kept = cross_stats(near, far, in_s, in_d)
    if ndp > 2:
        w_part = widen(w_part, ndp // 2, stats)
    gates, message = pair_gate(live, rows_x, w_part, local, stats, ndp)

    heard = send(message, 2)
    near_dq, near_own, near_sib, near_sum = near_grad(near, local, stats, gates)
    back_s, back_d, dq_low, keep, final, sums = cross_grad(
        cross, kept, stats, local, heard, gates, near_dq, near_sum
    )

    ret_s, ret_d = send(back_s, 2), send(back_d, 3)
    terms = pair_router(gates, sums, rows_x, ndp, n)
    outs, waiting, router_grad = beside(
        tail_phase, terms, far, local, final, gates, keep, dq_low, near_own, near_sib
    )
    dq, dk, dv = add_back(waiting, ret_s, ret_d, outs)
    return dq, dk, dv, router_grad


def body(route_pos, x_routed, w_router, queries, keys, values, d_gated):
    slots, full = queries.shape[1], queries.shape[2]
    n, ndp = lax.axis_size("ctx"), lax.axis_size("dp")
    chips = n // 2
    me, dp_me = lax.axis_index("ctx"), lax.axis_index("dp")
    core = (me % 2).astype(jnp.int32).reshape(1)
    half = full // 2
    groups = GROUPS if (half // HEAD) % GROUPS == 0 else 1
    width = half // groups

    sib_pairs = [(i, i ^ 1) for i in range(n)]

    def forward_pairs(step, flip):
        return [(i, (i + 2 * step) ^ flip) for i in range(n) if i + 2 * step < n]

    def back_pairs(step, flip):
        return [(b, a) for a, b in forward_pairs(step, flip)]

    def to_sib(a):
        return lax.ppermute(a, "ctx", sib_pairs)

    links = [(step, flip) for step in range(1, chips) for flip in (0, 1)]

    w_row = w_router.reshape(1, -1)
    w_parts = [w_row] + [
        lax.ppermute(w_row, "dp", [(i, (i + s) % ndp) for i in range(ndp)]) for s in range(1, ndp)
    ]
    live = (route_pos >= 0).astype(jnp.int32)
    lives = [live, to_sib(live)] + [lax.ppermute(live, "ctx", forward_pairs(*link)) for link in links]
    live_all = jnp.concatenate(lives, axis=0)

    kv_mine, kv_theirs = pack(core, keys, values, groups, width)
    kv_far = [
        [lax.ppermute((kv_theirs if flip else kv_mine)[g], "ctx", forward_pairs(step, flip)) for step, flip in links]
        for g in range(groups)
    ]
    q_mine, q_theirs = pack(core, queries, d_gated, groups, width)
    kv_sib = [to_sib(a) for a in kv_theirs]
    q_sib = [to_sib(a) for a in q_theirs]

    offsets = ((dp_me - jnp.arange(ndp)) % ndp).astype(jnp.int32)
    gate = router_gate(offsets, route_pos, x_routed, w_parts)
    gates = (gate, to_sib(gate))

    accs = (jnp.zeros((1, slots), F32), jnp.zeros((1, slots), F32))
    dq_own, sib_in, kv_own, back = [], [], [], []
    for g in range(groups):
        dq, sib_out, kv_local, kv_remote, accs = attention(
            core, live_all, gates, accs, q_mine[g], q_sib[g], [kv_mine[g], kv_sib[g], *kv_far[g]]
        )
        back.append([lax.ppermute(a, "ctx", back_pairs(*link)) for a, link in zip(kv_remote, links)])
        sib_in.append(to_sib(sib_out))
        dq_own.append(dq)
        kv_own.append(kv_local)

    targets = ((dp_me + jnp.arange(ndp)) % ndp).astype(jnp.int32)
    terms = router_terms(targets, gate, accs[0], to_sib(accs[1]), x_routed, ndp)
    mine = terms[0]
    for s in range(1, ndp):
        mine = mine + lax.ppermute(terms[s], "dp", [(i, (i + s) % ndp) for i in range(ndp)])
    total = mine
    for s in range(1, n):
        total = total + lax.ppermute(mine, "ctx", [(i, (i + s) % n) for i in range(n)])
    router_grad = total[0] / float(ndp * n * slots // 2)

    dq, dk, dv = combine(core, dq_own, sib_in, kv_own, back, queries.shape)
    return dq, dk, dv, router_grad


def solution(mesh):
    placed = (
        P("dp", "ctx"),
        P("dp", "ctx", None),
        P("dp"),
        P("dp", "ctx", None),
        P("dp", "ctx", None),
        P("dp", "ctx", None),
        P("dp", "ctx", None),
    )
    ndp = mesh.shape["dp"]
    paired = mesh.shape["ctx"] == 4 and ndp & (ndp - 1) == 0
    return jax.shard_map(
        swap_body if paired else body,
        mesh=mesh,
        in_specs=placed,
        out_specs=(P("dp", "ctx", None), P("dp", "ctx", None), P("dp", "ctx", None), P("dp")),
        check_vma=False,
    )
```

```python
import functools

import jax
import jax.numpy as jnp
from jax import lax
from jax.experimental import pallas as pl
from jax.experimental.pallas import tpu as pltpu
from jax.sharding import PartitionSpec as P

HEAD = 128
GROUPS = 4
NEG_FILL = -1e30
MIB = 1024 * 1024
BF16 = jnp.bfloat16
F32 = jnp.float32

VMEM = pl.BlockSpec(memory_space=pltpu.VMEM)
SMEM = pl.BlockSpec(memory_space=pltpu.SMEM)


def params(mib=16):
    return pltpu.CompilerParams(vmem_limit_bytes=mib * MIB)


def cost(flops, nbytes, exps=0):
    return pl.CostEstimate(flops=1, bytes_accessed=1, transcendentals=0)


def in_hbm(*arrays):
    return [pltpu.with_memory_space_constraint(a, pltpu.HBM) for a in arrays]


def nt(a, b):
    return lax.dot_general(a, b, (((1,), (1,)), ((), ())), preferred_element_type=F32)


def nn(a, b):
    return lax.dot_general(a, b, (((1,), (0,)), ((), ())), preferred_element_type=F32)


def tn(a, b):
    return lax.dot_general(a, b, (((0,), (0,)), ((), ())), preferred_element_type=F32)


def pack_kernel(groups, width, core_ref, first_ref, second_ref, *outs):
    half = first_ref.shape[-1] // 2
    core = core_ref[0]
    for side in range(2):
        base = (core if side == 0 else 1 - core) * half
        for g in range(groups):
            out = outs[side * groups + g]
            cols = pl.ds(pl.multiple_of(base + g * width, HEAD), width)
            out[0] = first_ref[0, :, cols].astype(BF16)
            out[1] = second_ref[0, :, cols].astype(BF16)


def pack(core, first, second, groups, width):
    slots = first.shape[1]
    out = jax.ShapeDtypeStruct((2, slots, width), BF16)
    res = pl.pallas_call(
        functools.partial(pack_kernel, groups, width),
        out_shape=[out] * (2 * groups),
        in_specs=[SMEM, VMEM, VMEM],
        out_specs=[VMEM] * (2 * groups),
        compiler_params=params(),
        cost_estimate=cost(0, 2 * first.size * 4),
        name="pack",
    )(core, first, second)
    return res[:groups], res[groups:]


def gate_kernel(parts, offset_ref, pos_ref, x_ref, *refs):
    w_refs, out_ref = refs[:parts], refs[parts]
    chunk = w_refs[0].shape[-1]
    total = jnp.zeros((8, x_ref.shape[1]), F32)
    for s in range(parts):
        cols = pl.ds(pl.multiple_of(offset_ref[s] * chunk, HEAD), chunk)
        w_rows = jnp.broadcast_to(w_refs[s][...].astype(F32), (8, chunk)).astype(BF16)
        total = total + nt(w_rows, x_ref[0, :, cols])
    gate = 1.0 / (1.0 + jnp.exp(-total[0:1]))
    out_ref[...] = jnp.where(pos_ref[...] >= 0, gate, 0.0)


def router_gate(offsets, route_pos, x_routed, w_parts):
    parts = len(w_parts)
    return pl.pallas_call(
        functools.partial(gate_kernel, parts),
        out_shape=jax.ShapeDtypeStruct(route_pos.shape, F32),
        in_specs=[SMEM] + [VMEM] * (2 + parts),
        out_specs=VMEM,
        compiler_params=params(),
        cost_estimate=cost(16 * x_routed.size, x_routed.size * 2),
        name="router_gate",
    )(offsets, route_pos, x_routed, *w_parts)


def attention_kernel(remote, scale, core_ref, live_ref, gate_own, gate_sib, acc_own, acc_sib, q_own, q_sib, *refs):
    chunks = 2 + remote
    kv = refs[:chunks]
    outs = refs[chunks:]
    dq_own, sib_out, kv_own = outs[:3]
    kv_remote = outs[3 : 3 + remote]
    sum_own, sum_sib = outs[3 + remote :]
    slots, width = q_own.shape[1], q_own.shape[2]
    core = core_ref[0]
    key = lax.broadcasted_iota(jnp.int32, (slots, slots), 0)
    query = lax.broadcasted_iota(jnp.int32, (slots, slots), 1)
    counts = [jnp.sum(live_ref[i : i + 1], axis=1, keepdims=True) for i in range(chunks)]
    lives = [key < counts[i] for i in range(chunks)]
    own_later = core == 1
    bias_rows = []
    for i in range(chunks):
        live = lives[i]
        if i == 0:
            pair = (live & (key <= query), live & jnp.logical_not(own_later))
        elif i == 1:
            pair = (live & own_later, live & (key <= query))
        else:
            pair = (live, live)
        bias_rows.append(jnp.concatenate([jnp.where(p, 0.0, NEG_FILL) for p in pair], axis=1))
    bias = jnp.concatenate(bias_rows, axis=0)
    gates = jnp.concatenate([gate_own[...], gate_sib[...]], axis=1)
    total = jnp.zeros((1, 2 * slots), F32)
    for h in range(width // HEAD):
        cols = slice(h * HEAD, (h + 1) * HEAD)
        q = jnp.concatenate([q_own[0, :, cols], q_sib[0, :, cols]], axis=0)
        dg = jnp.concatenate([q_own[1, :, cols], q_sib[1, :, cols]], axis=0)
        k = jnp.concatenate([r[0, :, cols] for r in kv], axis=0)
        v = jnp.concatenate([r[1, :, cols] for r in kv], axis=0)
        scores = nt(k, q) * scale + bias
        top = jnp.max(scores, axis=0, keepdims=True)
        e = jnp.exp(scores - top)
        inverse = 1.0 / jnp.sum(e, axis=0, keepdims=True)
        gw = nt(v, dg)
        delta = jnp.sum(e * gw, axis=0, keepdims=True) * inverse
        total = total + delta
        weights = e * (inverse * gates)
        dv = nn(weights.astype(BF16), dg)
        ds = (weights * ((gw - delta) * scale)).astype(BF16)
        dk = nn(ds, q)
        dq = tn(ds, k)
        dq_own[:, cols] = dq[:slots].astype(dq_own.dtype)
        sib_out[0, :, cols] = dq[slots:].astype(BF16)
        kv_own[0, :, cols] = dk[:slots].astype(BF16)
        kv_own[1, :, cols] = dv[:slots].astype(BF16)
        sib_out[1, :, cols] = dk[slots : 2 * slots].astype(BF16)
        sib_out[2, :, cols] = dv[slots : 2 * slots].astype(BF16)
        for i in range(remote):
            rows = slice((2 + i) * slots, (3 + i) * slots)
            kv_remote[i][0, :, cols] = dk[rows].astype(BF16)
            kv_remote[i][1, :, cols] = dv[rows].astype(BF16)
    sum_own[...] = acc_own[...] + total[:, :slots]
    sum_sib[...] = acc_sib[...] + total[:, slots:]


def attention(core, live, gates, accs, q_own, q_sib, kv):
    remote = len(kv) - 2
    _, slots, width = q_own.shape
    pair = jax.ShapeDtypeStruct((2, slots, width), BF16)
    row = jax.ShapeDtypeStruct((1, slots), F32)
    outs = [
        jax.ShapeDtypeStruct((slots, width), BF16),
        jax.ShapeDtypeStruct((3, slots, width), BF16),
        pair,
        *([pair] * remote),
        row,
        row,
    ]
    keys = (2 + remote) * slots
    res = pl.pallas_call(
        functools.partial(attention_kernel, remote, HEAD**-0.5),
        out_shape=outs,
        in_specs=[SMEM] + [VMEM] * (7 + len(kv)),
        out_specs=[VMEM] * len(outs),
        compiler_params=params(48),
        cost_estimate=cost(20 * slots * keys * width, 8 * keys * width + 20 * slots * width, 2 * slots * keys * width // HEAD),
        name="attention",
    )(core, live, *gates, *accs, q_own, q_sib, *kv)
    return res[0], res[1], res[2], res[3 : 3 + remote], (res[3 + remote], res[4 + remote])


def combine_kernel(groups, width, remote, core_ref, *refs):
    dq_own, sib, kv_own = refs[:groups], refs[groups : 2 * groups], refs[2 * groups : 3 * groups]
    back = refs[3 * groups : 3 * groups + groups * remote]
    dq_out, dk_out, dv_out = refs[3 * groups + groups * remote :]
    half = groups * width
    core = core_ref[0]
    for g in range(groups):
        own = pl.ds(pl.multiple_of(core * half + g * width, HEAD), width)
        other = pl.ds(pl.multiple_of((1 - core) * half + g * width, HEAD), width)
        dq_out[0, :, own] = dq_own[g][...].astype(F32)
        dq_out[0, :, other] = sib[g][0].astype(F32)
        for i, out in enumerate((dk_out, dv_out)):
            mine = kv_own[g][i].astype(F32)
            theirs = sib[g][1 + i].astype(F32)
            for r in range(remote):
                part = back[g * remote + r][i].astype(F32)
                if r % 2 == 0:
                    mine = mine + part
                else:
                    theirs = theirs + part
            out[0, :, own] = mine
            out[0, :, other] = theirs


def combine(core, dq_own, sib, kv_own, back, shape):
    groups = len(dq_own)
    remote = len(back[0])
    out = jax.ShapeDtypeStruct(shape, F32)
    flat = [*dq_own, *sib, *kv_own, *(b for group in back for b in group)]
    return pl.pallas_call(
        functools.partial(combine_kernel, groups, dq_own[0].shape[-1], remote),
        out_shape=[out] * 3,
        in_specs=[SMEM] + [VMEM] * len(flat),
        out_specs=[VMEM] * 3,
        compiler_params=params(48),
        cost_estimate=cost(0, 3 * out.size * 6),
        name="combine",
    )(core, *flat)


def router_kernel(parts, target_ref, gate_ref, own_ref, sib_ref, x_ref, *outs):
    gate = gate_ref[...]
    grad = (own_ref[...] + sib_ref[...]) * gate * (1.0 - gate)
    high = grad.astype(BF16)
    rest = grad - high.astype(F32)
    mid = rest.astype(BF16)
    low = (rest - mid.astype(F32)).astype(BF16)
    row = lax.broadcasted_iota(jnp.int32, (8, grad.shape[1]), 0)
    lhs = jnp.where(row == 0, high.astype(F32), jnp.where(row == 1, mid.astype(F32), jnp.where(row == 2, low.astype(F32), 0.0)))
    lhs = lhs.astype(BF16)
    chunk = outs[0].shape[-1]
    for s in range(parts):
        cols = pl.ds(pl.multiple_of(target_ref[s] * chunk, HEAD), chunk)
        outs[s][...] = jnp.sum(nn(lhs, x_ref[0, :, cols]), axis=0, keepdims=True)


def router_terms(targets, gate, own, sib, x_routed, parts):
    chunk = x_routed.shape[-1] // parts
    return pl.pallas_call(
        functools.partial(router_kernel, parts),
        out_shape=[jax.ShapeDtypeStruct((1, chunk), F32)] * parts,
        in_specs=[SMEM] + [VMEM] * 4,
        out_specs=[VMEM] * parts,
        compiler_params=params(),
        cost_estimate=cost(16 * x_routed.size, x_routed.size * 2),
        name="router_terms",
    )(targets, gate, own, sib, x_routed)


def here():
    me = lax.axis_index("ctx")
    return lax.rem(me, 2), lax.div(me, 2)


MARK = 2.0**60
MARK_LIMIT = 2.0**50


def live_rows(pos_ref, slots):
    count = jnp.sum((pos_ref[...] >= 0).astype(jnp.int32), axis=1, keepdims=True)
    return lax.broadcasted_iota(jnp.int32, (slots, HEAD), 0) < count


def mark_dead(keys, live):
    width = keys.shape[-1]
    mask = jnp.concatenate([live] * (width // HEAD), axis=1)
    return jnp.where(mask, keys.astype(F32), MARK).astype(BF16)


def cross_pack_kernel(pos_any, w_any, k_ref, v_ref, q_ref, dg_ref, straight, diag, w_out, wide, pos_ref, w_ref, sems):
    small = [pltpu.make_async_copy(pos_any, pos_ref, sems.at[4]), pltpu.make_async_copy(w_any, w_ref, sems.at[5])]
    for c in small:
        c.start()
    slots, width = straight.shape[1], straight.shape[2]
    half = k_ref.shape[-1] // 2
    core, chip = here()
    ends = ((straight, core * half), (diag, (1 - core) * half))

    def copies(first, second, targets, offset):
        out = []
        for i, (end, start) in enumerate(ends):
            cols = pl.ds(pl.multiple_of(start + offset, HEAD), width)
            out.append(pltpu.make_async_copy(first.at[0, :, cols], end.at[0], sems.at[2 * i]))
            out.append(pltpu.make_async_copy(second.at[0, :, cols], targets[i], sems.at[2 * i + 1]))
        for c in out:
            c.start()
        for c in out:
            c.wait()

    @pl.when(chip == 0)
    def _():
        copies(k_ref, v_ref, (straight.at[1], diag.at[1]), 0)
        small[0].wait()
        live = live_rows(pos_ref, slots)
        for end, _ in ends:
            end[0] = mark_dead(end[0], live)

    @pl.when(chip != 0)
    def _():
        copies(q_ref, dg_ref, (wide.at[0], wide.at[1]), width)
        small[0].wait()
        for i, (end, _) in enumerate(ends):
            end[1] = wide[i].astype(BF16)

    small[1].wait()
    w_out[...] = w_ref[...].astype(F32).reshape(w_out.shape)


def cross_pack(route_pos, w_router, keys, values, queries, d_gated):
    _, slots, full = keys.shape
    cross = pltpu.VMEM((2, slots, full // 4), BF16)
    hbm = pl.BlockSpec(memory_space=pltpu.HBM)
    return pl.pallas_call(
        cross_pack_kernel,
        out_shape=[cross, cross, jax.ShapeDtypeStruct((1, w_router.shape[0]), F32)],
        in_specs=[hbm] * 6,
        out_specs=[VMEM] * 3,
        scratch_shapes=[
            pltpu.VMEM((2, slots, full // 4), F32),
            pltpu.VMEM(route_pos.shape, jnp.int32),
            pltpu.VMEM(w_router.shape, BF16),
            pltpu.SemaphoreType.DMA((6,)),
        ],
        compiler_params=params(),
        cost_estimate=cost(0, 10 * slots * full),
        name="cross_pack",
    )(*in_hbm(route_pos, w_router, keys, values, queries, d_gated))


def sib_pack_kernel(pos_ref, k_ref, v_ref, q_ref, dg_ref, out, wide, sems):
    slots, half = out.shape[1], out.shape[2]
    cols = pl.ds(pl.multiple_of((1 - here()[0]) * half, HEAD), half)
    sources = ((k_ref, out.at[0]), (dg_ref, wide), (v_ref, out.at[1]), (q_ref, out.at[2]))
    copies = [pltpu.make_async_copy(src.at[0, :, cols], dst, sems.at[i]) for i, (src, dst) in enumerate(sources)]
    for c in copies:
        c.start()
    live = live_rows(pos_ref, slots)
    copies[0].wait()
    out[0] = mark_dead(out[0], live)
    copies[1].wait()
    out[3] = wide[...].astype(BF16)
    copies[2].wait()
    copies[3].wait()


def sib_pack(route_pos, keys, values, queries, d_gated):
    _, slots, full = keys.shape
    hbm = pl.BlockSpec(memory_space=pltpu.HBM)
    return pl.pallas_call(
        sib_pack_kernel,
        out_shape=pltpu.VMEM((4, slots, full // 2), BF16),
        in_specs=[VMEM, hbm, hbm, hbm, hbm],
        out_specs=VMEM,
        scratch_shapes=[pltpu.VMEM((slots, full // 2), F32), pltpu.SemaphoreType.DMA((4,))],
        compiler_params=params(),
        cost_estimate=cost(0, 20 * slots * full),
        name="sib_pack",
    )(route_pos, *in_hbm(keys, values, queries, d_gated))


def pair_gate_kernel(parts, live_ref, rows_x, w_ref, local, stats, out_ref, message):
    chunk = w_ref.shape[1] // parts
    slots = rows_x.shape[1]
    for i in range(2):
        total = jnp.zeros((8, slots), F32)
        for j in range(parts):
            w_rows = jnp.broadcast_to(w_ref[:, j * chunk : (j + 1) * chunk], (8, chunk)).astype(BF16)
            cols = pl.ds(pl.multiple_of((lax.axis_index("dp") ^ j) * chunk, HEAD), chunk)
            total = total + nt(w_rows, rows_x[i, :, cols])
        lanes = slice(i * slots, (i + 1) * slots)
        out_ref[:, lanes] = live_ref[:, lanes] / (1.0 + jnp.exp(-total[0:1]))
    first = here()[1] == 0
    heads = stats.shape[1]
    for i in range(3):
        message[i] = jnp.where(first, stats[i], local[i, heads:])
    message[3] = jnp.broadcast_to(out_ref[...], message.shape[1:])


def pair_gate(live, rows_x, w_full, local, stats, parts):
    _, heads, lanes = stats.shape
    return pl.pallas_call(
        functools.partial(pair_gate_kernel, parts),
        out_shape=[jax.ShapeDtypeStruct(live.shape, F32), jax.ShapeDtypeStruct((4, heads, lanes), F32)],
        in_specs=[VMEM] * 5,
        out_specs=[VMEM] * 2,
        compiler_params=params(),
        cost_estimate=cost(16 * rows_x.size, rows_x.size * 2),
        name="router_gate",
    )(live, rows_x, w_full, local, stats)


def local_mask(core, pair):
    slots = pair.shape[1] // 2
    key = lax.broadcasted_iota(jnp.int32, (slots, slots), 0)
    query = lax.broadcasted_iota(jnp.int32, (slots, slots), 1)
    causal = key <= query
    own_live = pair[0, :slots, :slots].astype(F32) < MARK_LIMIT
    sib_live = pair[0, slots:, :slots].astype(F32) < MARK_LIMIT
    own_rows = jnp.concatenate([own_live & causal, own_live & (core == 0)], axis=1)
    sib_rows = jnp.concatenate([sib_live & (core == 1), sib_live & causal], axis=1)
    return jnp.concatenate([own_rows, sib_rows], axis=0)


def kept_stats(scores, gw, kept, stats, h):
    top = jnp.max(scores, axis=0, keepdims=True)
    e = jnp.exp(scores - top).astype(BF16)
    gw = gw.astype(BF16)
    kept[0, h] = e
    kept[1, h] = gw
    e = e.astype(F32)
    stats[0, h : h + 1] = top
    stats[1, h : h + 1] = jnp.sum(e, axis=0, keepdims=True)
    stats[2, h : h + 1] = jnp.sum(e * gw.astype(F32), axis=0, keepdims=True)


def partial_stats(scores, gw, stats, h):
    top = jnp.max(scores, axis=0, keepdims=True)
    e = jnp.exp(scores - top)
    stats[0, h : h + 1] = top
    stats[1, h : h + 1] = jnp.sum(e, axis=0, keepdims=True)
    stats[2, h : h + 1] = jnp.sum(e * gw, axis=0, keepdims=True)


def local_stats_kernel(scale, pos_ref, k_ref, v_ref, q_ref, dg_ref, sib, x_ref, x_sib, stats, live, near, far, rows_x, wide, sems, x_sems):
    slots, half = sib.shape[1], sib.shape[2]
    width = half // 2
    core = here()[0]
    own, other = slice(0, slots), slice(slots, 2 * slots)
    stages = []
    for g, pair in enumerate((near, far)):
        cols = slice(g * width, (g + 1) * width)
        held = pl.ds(pl.multiple_of(core * half + g * width, HEAD), width)
        copies = [
            pltpu.make_async_copy(ref.at[0, :, held], pair.at[j, own], sems.at[8 * g + j])
            for j, ref in enumerate((k_ref, v_ref, q_ref))
        ]
        copies.append(pltpu.make_async_copy(dg_ref.at[0, :, held], wide.at[:, cols], sems.at[8 * g + 3]))
        for j in range(4):
            copies.append(pltpu.make_async_copy(sib.at[j, :, cols], pair.at[j, other], sems.at[8 * g + 4 + j]))
        for c in copies:
            c.start()
        stages.append(copies)
    x_copies = []
    depth = x_ref.shape[2] // 2
    for i, ref in enumerate((x_ref, x_sib)):
        for g in range(2):
            cols = slice(g * depth, (g + 1) * depth)
            x_copies.append(pltpu.make_async_copy(ref.at[0, :, cols], rows_x.at[i, :, cols], x_sems.at[2 * i + g]))
    for c in x_copies:
        c.start()
    rows_live = live_rows(pos_ref, slots)
    mask = None
    for g, pair in enumerate((near, far)):
        cols = slice(g * width, (g + 1) * width)
        for c in stages[g]:
            c.wait()
        pair[0, own] = mark_dead(pair[0, own], rows_live)
        pair[3, own] = wide[:, cols].astype(BF16)
        if mask is None:
            mask = local_mask(core, pair)
            marks = nt(jnp.ones((8, HEAD), BF16), pair[0, :, :HEAD])[0:1]
            live[...] = jnp.where(marks < MARK_LIMIT, 1.0, 0.0)
        for h in range(width // HEAD):
            at = slice(h * HEAD, (h + 1) * HEAD)
            scores = jnp.where(mask, nt(pair[0, :, at], pair[2, :, at]) * scale, NEG_FILL)
            partial_stats(scores, nt(pair[1, :, at], pair[3, :, at]), stats, g * width // HEAD + h)
    for c in x_copies:
        c.wait()


def local_stats(route_pos, keys, values, queries, d_gated, sib, x_routed, x_sib):
    _, slots, half = sib.shape
    heads = half // HEAD
    anywhere = pl.BlockSpec(memory_space=pl.ANY)
    return pl.pallas_call(
        functools.partial(local_stats_kernel, HEAD**-0.5),
        out_shape=[
            jax.ShapeDtypeStruct((3, heads, 2 * slots), F32),
            jax.ShapeDtypeStruct((1, 2 * slots), F32),
            pltpu.VMEM((4, 2 * slots, half // 2), BF16),
            pltpu.VMEM((4, 2 * slots, half // 2), BF16),
            pltpu.VMEM((2, slots, x_routed.shape[2]), BF16),
        ],
        in_specs=[VMEM] + [anywhere] * 7,
        out_specs=[VMEM] * 5,
        scratch_shapes=[pltpu.VMEM((slots, half), F32), pltpu.SemaphoreType.DMA((16,)), pltpu.SemaphoreType.DMA((4,))],
        compiler_params=params(),
        cost_estimate=cost(16 * slots * slots * half, 16 * slots * half, 4 * slots * slots * half // HEAD),
        name="local_stats",
    )(route_pos, *in_hbm(keys, values, queries, d_gated), sib, x_routed, x_sib)


def cross_stats_kernel(scale, near, far, straight, diag, cross, stats, kept):
    slots, width = straight.shape[1], straight.shape[2]
    chip = here()[1]
    top, bottom = slice(0, slots), slice(slots, 2 * slots)

    @pl.when(chip == 0)
    def _():
        for part in range(2):
            cross[part] = far[part]
            cross[2 + part, top] = straight[part]
            cross[2 + part, bottom] = diag[part]

    @pl.when(chip != 0)
    def _():
        for part in range(2):
            cross[part, top] = straight[part]
            cross[part, bottom] = diag[part]
            cross[2 + part] = near[2 + part]

    live = cross[0, :, :HEAD].astype(F32) < MARK_LIMIT
    mask = jnp.concatenate([live] * (2 * slots // HEAD), axis=1)
    heads = width // HEAD
    for h in range(heads):
        cols = slice(h * HEAD, (h + 1) * HEAD)
        scores = jnp.where(mask, nt(cross[0, :, cols], cross[2, :, cols]) * scale, NEG_FILL)
        kept_stats(scores, nt(cross[1, :, cols], cross[3, :, cols]), kept, stats, h)


def cross_stats(near, far, straight, diag):
    _, slots, width = straight.shape
    heads = width // HEAD
    return pl.pallas_call(
        functools.partial(cross_stats_kernel, HEAD**-0.5),
        out_shape=[
            pltpu.VMEM((4, 2 * slots, width), BF16),
            jax.ShapeDtypeStruct((3, heads, 2 * slots), F32),
            pltpu.VMEM((2, heads, 2 * slots, 2 * slots), BF16),
        ],
        in_specs=[VMEM] * 4,
        out_specs=[VMEM] * 3,
        compiler_params=params(),
        cost_estimate=cost(16 * slots * slots * width, 32 * slots * width, 4 * slots * slots * heads),
        name="cross_stats",
    )(near, far, straight, diag)


NONE = (-3e38, 0.0, 0.0)


def merge(first, second):
    top = jnp.maximum(first[0], second[0])
    a, b = jnp.exp(first[0] - top), jnp.exp(second[0] - top)
    inverse = 1.0 / (first[1] * a + second[1] * b)
    return a * inverse, (first[2] * a + second[2] * b) * inverse


def choose(flag, yes, no):
    return [jnp.where(flag, y, n) for y, n in zip(yes, no)]


def gradients(q, k, dg, e, gw, scale, factor, delta):
    weights = e * factor
    ds = (weights * ((gw - delta) * scale)).astype(BF16)
    return tn(ds, k), nn(ds, q), nn(weights.astype(BF16), dg)


def local_gradients(pair, h, mask, scale, top, factor, delta):
    cols = slice(h * HEAD, (h + 1) * HEAD)
    k, v, q, dg = [pair[i, :, cols] for i in range(4)]
    e = jnp.exp(jnp.where(mask, nt(k, q) * scale, NEG_FILL) - top)
    return gradients(q, k, dg, e, nt(v, dg), scale, factor, delta)


def near_grad_kernel(scale, pair, local, stats, gates, dq_out, own_out, sib_out, sum_out):
    slots, width = own_out.shape[1], own_out.shape[2]
    heads = width // HEAD
    first = here()[1] == 0
    near = [local[i, :heads] for i in range(3)]
    factor, delta = merge(near, choose(first, NONE, [stats[i] for i in range(3)]))
    factor = factor * gates[...]
    sum_out[...] = jnp.sum(delta, axis=0, keepdims=True)
    mask = local_mask(here()[0], pair)
    for h in range(heads):
        cols = slice(h * HEAD, (h + 1) * HEAD)
        row = slice(h, h + 1)
        dq, dk, dv = local_gradients(pair, h, mask, scale, near[0][row], factor[row], delta[row])
        dq_out[:, cols] = dq
        for i, part in enumerate((dk, dv)):
            own_out[i, :, cols] = part[:slots].astype(BF16)
            sib_out[i, :, cols] = part[slots:].astype(BF16)


def near_grad(pair, local, stats, gates):
    _, rows, width = pair.shape
    slots = rows // 2
    out = pltpu.VMEM((2, slots, width), BF16)
    return pl.pallas_call(
        functools.partial(near_grad_kernel, HEAD**-0.5),
        out_shape=[pltpu.VMEM((2 * slots, width), F32), out, out, jax.ShapeDtypeStruct(gates.shape, F32)],
        in_specs=[VMEM] * 4,
        out_specs=[VMEM] * 4,
        compiler_params=params(),
        cost_estimate=cost(20 * slots * slots * width, 40 * slots * width),
        name="near_grad",
    )(pair, local, stats, gates)


def cross_grad_kernel(scale, cross, kept, stats, local, heard, gates, near_dq, near_sum, straight, diag, dq_out, keep, final, sum_out):
    slots, width = straight.shape[1], straight.shape[2]
    heads = width // HEAD
    first = here()[1] == 0
    late = jnp.where(first, 0.0, 1.0)
    mine = [stats[i] for i in range(3)]
    other = [heard[i] for i in range(3)]
    near = [local[i, :heads] for i in range(3)]
    far = [local[i, heads:] for i in range(3)]
    factor, delta = merge(mine, choose(first, other, near))
    factor = factor * jnp.where(first, heard[3], jnp.broadcast_to(gates[...], factor.shape))
    final[0], final[1] = merge(far, choose(first, NONE, other))
    sum_out[...] = near_sum[...] + jnp.sum(final[1], axis=0, keepdims=True)
    for h in range(heads):
        cols = slice(h * HEAD, (h + 1) * HEAD)
        row = slice(h, h + 1)
        dq, dk, dv = gradients(
            cross[2, :, cols], cross[0, :, cols], cross[3, :, cols],
            kept[0, h].astype(F32), kept[1, h].astype(F32), scale, factor[row], delta[row],
        )
        dq_out[:, cols] = (near_dq[:, cols] + late * dq).astype(BF16)
        keep[0, :, cols] = dk.astype(BF16)
        keep[1, :, cols] = dv.astype(BF16)
        sent = jnp.where(first, dq, dk).astype(BF16)
        straight[0, :, cols] = sent[:slots]
        diag[0, :, cols] = sent[slots:]
        straight[1, :, cols] = dv[:slots].astype(BF16)
        diag[1, :, cols] = dv[slots:].astype(BF16)


def cross_grad(cross, kept, stats, local, heard, gates, near_dq, near_sum):
    _, rows, width = cross.shape
    slots = rows // 2
    out = pltpu.VMEM((2, slots, width), BF16)
    return pl.pallas_call(
        functools.partial(cross_grad_kernel, HEAD**-0.5),
        out_shape=[
            out,
            out,
            pltpu.VMEM((rows, width), BF16),
            pltpu.VMEM((2, rows, width), BF16),
            jax.ShapeDtypeStruct((2, width // HEAD, rows), F32),
            jax.ShapeDtypeStruct((1, rows), F32),
        ],
        in_specs=[VMEM] * 8,
        out_specs=[VMEM] * 6,
        compiler_params=params(),
        cost_estimate=cost(24 * slots * slots * width, 64 * slots * width),
        name="cross_grad",
    )(cross, kept, stats, local, heard, gates, near_dq, near_sum)


def far_grad_kernel(scale, pair, local, final, gates, keep, near_dq, near_own, near_sib, own_out, sib_out):
    slots, width = pair.shape[1] // 2, pair.shape[2]
    heads = width // HEAD
    early = jnp.where(here()[1] == 0, 1.0, 0.0)
    factor = final[0] * gates[...]
    mask = local_mask(here()[0], pair)
    own_out[0, :, :width] = near_dq[:slots]
    sib_out[0, :, :width] = near_dq[slots:]
    for i in range(2):
        own_out[1 + i, :, :width] = near_own[i]
        sib_out[1 + i, :, :width] = near_sib[i]
    for h in range(heads):
        cols = slice(width + h * HEAD, width + (h + 1) * HEAD)
        at = slice(h * HEAD, (h + 1) * HEAD)
        row = slice(h, h + 1)
        top = local[0, heads + h : heads + h + 1]
        dq, dk, dv = local_gradients(pair, h, mask, scale, top, factor[row], final[1, row])
        dk = dk + early * keep[0, :, at].astype(F32)
        dv = dv + early * keep[1, :, at].astype(F32)
        for i, part in enumerate((dq, dk, dv)):
            own_out[i, :, cols] = part[:slots].astype(BF16)
            sib_out[i, :, cols] = part[slots:].astype(BF16)


def far_grad(pair, local, final, gates, keep, near_dq, near_own, near_sib):
    _, rows, width = pair.shape
    slots, half = rows // 2, 2 * width
    out = jax.ShapeDtypeStruct((3, slots, half), BF16)
    return pl.pallas_call(
        functools.partial(far_grad_kernel, HEAD**-0.5),
        out_shape=[out, out],
        in_specs=[VMEM] * 8,
        out_specs=[VMEM] * 2,
        compiler_params=params(),
        cost_estimate=cost(20 * slots * slots * half, 40 * slots * half),
        name="far_grad",
    )(pair, local, final, gates, keep, near_dq, near_own, near_sib)


def own_join_kernel(own, dq_out, dk_out, dv_out, waiting, total, sems):
    slots, half = own.shape[1], own.shape[2]
    width = half // 2
    core, chip = here()
    cols = pl.ds(pl.multiple_of(core * half, HEAD), half)
    stores = []
    for j, out in enumerate((dq_out, dk_out, dv_out)):
        total[j] = own[j].astype(F32)
        stores.append(pltpu.make_async_copy(total.at[j], out.at[0, :, cols], sems.at[j]))
        stores[-1].start()
    waiting[0] = jnp.where(chip == 0, total[1, :, :width], total[0, :, width:]).astype(BF16)
    waiting[1] = own[2, :, :width]
    for c in stores:
        c.wait()


def own_join(own, shape):
    out = pltpu.HBM(shape, F32)
    _, slots, half = own.shape
    hbm = pl.BlockSpec(memory_space=pltpu.HBM)
    return pl.pallas_call(
        own_join_kernel,
        out_shape=[out] * 3 + [jax.ShapeDtypeStruct((2, slots, half // 2), BF16)],
        in_specs=[VMEM],
        out_specs=[hbm] * 3 + [VMEM],
        scratch_shapes=[pltpu.VMEM((3, slots, half), F32), pltpu.SemaphoreType.DMA((3,))],
        compiler_params=params(),
        cost_estimate=cost(0, 18 * own.size),
        name="own_join",
    )(own)


def finish_kernel(waiting, sib, straight, diag, dq_in, dk_in, dv_in, dq_out, dk_out, dv_out, low, held, total, added, in_sems, out_sems):
    half = sib.shape[2]
    width = half // 2
    core, chip = here()
    early, late = jnp.where(chip == 0, 1.0, 0.0), jnp.where(chip == 0, 0.0, 1.0)
    loads = [pltpu.make_async_copy(sib.at[j], low.at[j], in_sems.at[j]) for j in range(3)]
    loads += [pltpu.make_async_copy(waiting.at[j], held.at[j], in_sems.at[3 + j]) for j in range(2)]
    for c in loads:
        c.start()
    cols = pl.ds(pl.multiple_of((1 - core) * half, HEAD), half)
    stores = []
    for j, out in enumerate((dq_out, dk_out, dv_out)):
        loads[j].wait()
        first, second = low[j, :, :width].astype(F32), low[j, :, width:].astype(F32)
        if j == 0:
            second = second + late * diag[0].astype(F32)
        else:
            first = first + early * diag[j - 1].astype(F32)
        total[j, :, :width] = first
        total[j, :, width:] = second
        stores.append(pltpu.make_async_copy(total.at[j], out.at[0, :, cols], out_sems.at[j]))
        stores[-1].start()
    for j in range(2):
        loads[3 + j].wait()
        added[j] = held[j].astype(F32) + straight[j].astype(F32)

    def store(j, out, offset):
        at = pl.ds(pl.multiple_of(core * half + offset, HEAD), width)
        copy = pltpu.make_async_copy(added.at[j], out.at[0, :, at], out_sems.at[3 + j])
        copy.start()
        return copy

    @pl.when(chip == 0)
    def _():
        copies = [store(0, dk_out, 0), store(1, dv_out, 0)]
        for c in copies:
            c.wait()

    @pl.when(chip != 0)
    def _():
        store(0, dq_out, width).wait()

    for c in stores:
        c.wait()


def finish(waiting, sib, straight, diag, outs):
    _, slots, half = sib.shape
    hbm = pl.BlockSpec(memory_space=pltpu.HBM)
    anywhere = pl.BlockSpec(memory_space=pl.ANY)
    return pl.pallas_call(
        finish_kernel,
        out_shape=[pltpu.HBM(o.shape, F32) for o in outs],
        in_specs=[anywhere] * 2 + [VMEM] * 2 + [hbm] * 3,
        out_specs=[hbm] * 3,
        scratch_shapes=[
            pltpu.VMEM((3, slots, half), BF16),
            pltpu.VMEM(waiting.shape, BF16),
            pltpu.VMEM((3, slots, half), F32),
            pltpu.VMEM(waiting.shape, F32),
            pltpu.SemaphoreType.DMA((5,)),
            pltpu.SemaphoreType.DMA((5,)),
        ],
        input_output_aliases={4: 0, 5: 1, 6: 2},
        compiler_params=params(),
        cost_estimate=cost(0, 12 * sib.size),
        name="finish",
    )(waiting, sib, straight, diag, *in_hbm(*outs))


def pair_router_kernel(gates_ref, sum_ref, rows_x, out_ref):
    gates = gates_ref[...]
    grad = sum_ref[...] * gates * (1.0 - gates)
    high = grad.astype(BF16)
    rest = grad - high.astype(F32)
    mid = rest.astype(BF16)
    low = (rest - mid.astype(F32)).astype(BF16)
    slots = rows_x.shape[1]
    row = lax.broadcasted_iota(jnp.int32, (8, grad.shape[1]), 0)
    lhs = jnp.where(row == 0, high.astype(F32), jnp.where(row == 1, mid.astype(F32), jnp.where(row == 2, low.astype(F32), 0.0)))
    lhs = lhs.astype(BF16)
    term = jnp.sum(nn(lhs[:, :slots], rows_x[0]) + nn(lhs[:, slots:], rows_x[1]), axis=0, keepdims=True)
    parts, copies, _, chunk = out_ref.shape
    for j in range(parts):
        for i in range(copies):
            out_ref[j, i] = term[:, j * chunk : (j + 1) * chunk]


def pair_router(gates, sums, rows_x, parts, copies):
    chunk = rows_x.shape[-1] // parts
    return pl.pallas_call(
        pair_router_kernel,
        out_shape=jax.ShapeDtypeStruct((parts, copies, 1, chunk), F32),
        in_specs=[VMEM] * 3,
        out_specs=VMEM,
        compiler_params=params(),
        cost_estimate=cost(32 * rows_x.size, rows_x.size * 4),
        name="router_terms",
    )(gates, sums, rows_x)


def swap_body(route_pos, x_routed, w_router, queries, keys, values, d_gated):
    slots = queries.shape[1]
    n, ndp = lax.axis_size("ctx"), lax.axis_size("dp")

    def send(a, flip):
        return lax.ppermute(a, "ctx", [(i, i ^ flip) for i in range(n)])

    def beside(fn, *operands):
        def skip(*ops):
            return jax.tree.map(lambda o: jnp.zeros(o.shape, o.dtype), jax.eval_shape(fn, *ops))

        return lax.cond(route_pos[0, 0] >= -1, fn, skip, *operands)

    def after(value, *others):
        return lax.optimization_barrier((value, *others))[0]

    def widen(part, step, *first):
        other = lax.ppermute(part, "dp", [(i, i ^ step) for i in range(ndp)])
        return jnp.concatenate([part, after(other, *first)], axis=1)

    def exchange_phase(x_routed, w_part, theirs):
        sib, x_sib = send(theirs, 1), send(x_routed, 1)
        step = 2
        while 2 * step < ndp:
            w_part = widen(w_part, step)
            step *= 2
        return sib, x_sib, w_part

    def far_phase(*operands):
        own_out, sib_out = far_grad(*operands)
        sib_in = send(sib_out, 1)
        *outs, waiting = own_join(own_out, queries.shape)
        return outs, waiting, sib_in

    def tail_phase(terms, *operands):
        shared = lax.all_to_all(terms.reshape(ndp * n, 1, -1), ("dp", "ctx"), 0, 0, tiled=True)
        results = beside(far_phase, *operands)
        return *results, jnp.sum(shared, axis=0)[0] / float(ndp * n * slots // 2)

    out_s, out_d, w_part = cross_pack(route_pos, w_router, keys, values, queries, d_gated)
    in_s, in_d = send(out_s, 2), send(out_d, 3)

    theirs = sib_pack(after(route_pos, out_s), keys, values, queries, d_gated)
    if ndp > 1:
        w_part = widen(w_part, 1, theirs)
    sib, x_sib, w_part = beside(exchange_phase, x_routed, w_part, theirs)
    local, live, near, far, rows_x = local_stats(route_pos, keys, values, queries, d_gated, sib, x_routed, x_sib)
    cross, stats, kept = cross_stats(near, far, in_s, in_d)
    if ndp > 2:
        w_part = widen(w_part, ndp // 2, stats)
    gates, message = pair_gate(live, rows_x, w_part, local, stats, ndp)

    heard = send(message, 2)
    near_dq, near_own, near_sib, near_sum = near_grad(near, local, stats, gates)
    back_s, back_d, dq_low, keep, final, sums = cross_grad(
        cross, kept, stats, local, heard, gates, near_dq, near_sum
    )

    ret_s, ret_d = send(back_s, 2), send(back_d, 3)
    terms = pair_router(gates, sums, rows_x, ndp, n)
    outs, waiting, sib_in, router_grad = beside(
        tail_phase, terms, far, local, final, gates, keep, dq_low, near_own, near_sib
    )
    dq, dk, dv = finish(waiting, sib_in, ret_s, ret_d, outs)
    return dq, dk, dv, router_grad


def body(route_pos, x_routed, w_router, queries, keys, values, d_gated):
    slots, full = queries.shape[1], queries.shape[2]
    n, ndp = lax.axis_size("ctx"), lax.axis_size("dp")
    chips = n // 2
    me, dp_me = lax.axis_index("ctx"), lax.axis_index("dp")
    core = (me % 2).astype(jnp.int32).reshape(1)
    half = full // 2
    groups = GROUPS if (half // HEAD) % GROUPS == 0 else 1
    width = half // groups

    sib_pairs = [(i, i ^ 1) for i in range(n)]

    def forward_pairs(step, flip):
        return [(i, (i + 2 * step) ^ flip) for i in range(n) if i + 2 * step < n]

    def back_pairs(step, flip):
        return [(b, a) for a, b in forward_pairs(step, flip)]

    def to_sib(a):
        return lax.ppermute(a, "ctx", sib_pairs)

    links = [(step, flip) for step in range(1, chips) for flip in (0, 1)]

    w_row = w_router.reshape(1, -1)
    w_parts = [w_row] + [
        lax.ppermute(w_row, "dp", [(i, (i + s) % ndp) for i in range(ndp)]) for s in range(1, ndp)
    ]
    live = (route_pos >= 0).astype(jnp.int32)
    lives = [live, to_sib(live)] + [lax.ppermute(live, "ctx", forward_pairs(*link)) for link in links]
    live_all = jnp.concatenate(lives, axis=0)

    kv_mine, kv_theirs = pack(core, keys, values, groups, width)
    kv_far = [
        [lax.ppermute((kv_theirs if flip else kv_mine)[g], "ctx", forward_pairs(step, flip)) for step, flip in links]
        for g in range(groups)
    ]
    q_mine, q_theirs = pack(core, queries, d_gated, groups, width)
    kv_sib = [to_sib(a) for a in kv_theirs]
    q_sib = [to_sib(a) for a in q_theirs]

    offsets = ((dp_me - jnp.arange(ndp)) % ndp).astype(jnp.int32)
    gate = router_gate(offsets, route_pos, x_routed, w_parts)
    gates = (gate, to_sib(gate))

    accs = (jnp.zeros((1, slots), F32), jnp.zeros((1, slots), F32))
    dq_own, sib_in, kv_own, back = [], [], [], []
    for g in range(groups):
        dq, sib_out, kv_local, kv_remote, accs = attention(
            core, live_all, gates, accs, q_mine[g], q_sib[g], [kv_mine[g], kv_sib[g], *kv_far[g]]
        )
        back.append([lax.ppermute(a, "ctx", back_pairs(*link)) for a, link in zip(kv_remote, links)])
        sib_in.append(to_sib(sib_out))
        dq_own.append(dq)
        kv_own.append(kv_local)

    targets = ((dp_me + jnp.arange(ndp)) % ndp).astype(jnp.int32)
    terms = router_terms(targets, gate, accs[0], to_sib(accs[1]), x_routed, ndp)
    mine = terms[0]
    for s in range(1, ndp):
        mine = mine + lax.ppermute(terms[s], "dp", [(i, (i + s) % ndp) for i in range(ndp)])
    total = mine
    for s in range(1, n):
        total = total + lax.ppermute(mine, "ctx", [(i, (i + s) % n) for i in range(n)])
    router_grad = total[0] / float(ndp * n * slots // 2)

    dq, dk, dv = combine(core, dq_own, sib_in, kv_own, back, queries.shape)
    return dq, dk, dv, router_grad


def solution(mesh):
    placed = (
        P("dp", "ctx"),
        P("dp", "ctx", None),
        P("dp"),
        P("dp", "ctx", None),
        P("dp", "ctx", None),
        P("dp", "ctx", None),
        P("dp", "ctx", None),
    )
    ndp = mesh.shape["dp"]
    paired = mesh.shape["ctx"] == 4 and ndp & (ndp - 1) == 0
    return jax.shard_map(
        swap_body if paired else body,
        mesh=mesh,
        in_specs=placed,
        out_specs=(P("dp", "ctx", None), P("dp", "ctx", None), P("dp", "ctx", None), P("dp")),
        check_vma=False,
    )
```

```python
import functools

import jax
import jax.numpy as jnp
from jax import lax
from jax.experimental import pallas as pl
from jax.experimental.pallas import tpu as pltpu
from jax.sharding import PartitionSpec as P

HEAD = 128
GROUPS = 4
NEG_FILL = -1e30
MIB = 1024 * 1024
BF16 = jnp.bfloat16
F32 = jnp.float32

VMEM = pl.BlockSpec(memory_space=pltpu.VMEM)
SMEM = pl.BlockSpec(memory_space=pltpu.SMEM)


def params(mib=16):
    return pltpu.CompilerParams(vmem_limit_bytes=mib * MIB)


def cost(flops, nbytes, exps=0):
    return pl.CostEstimate(flops=1, bytes_accessed=1, transcendentals=0)


def in_hbm(*arrays):
    return [pltpu.with_memory_space_constraint(a, pltpu.HBM) for a in arrays]


def nt(a, b):
    return lax.dot_general(a, b, (((1,), (1,)), ((), ())), preferred_element_type=F32)


def nn(a, b):
    return lax.dot_general(a, b, (((1,), (0,)), ((), ())), preferred_element_type=F32)


def tn(a, b):
    return lax.dot_general(a, b, (((0,), (0,)), ((), ())), preferred_element_type=F32)


def pack_kernel(groups, width, core_ref, first_ref, second_ref, *outs):
    half = first_ref.shape[-1] // 2
    core = core_ref[0]
    for side in range(2):
        base = (core if side == 0 else 1 - core) * half
        for g in range(groups):
            out = outs[side * groups + g]
            cols = pl.ds(pl.multiple_of(base + g * width, HEAD), width)
            out[0] = first_ref[0, :, cols].astype(BF16)
            out[1] = second_ref[0, :, cols].astype(BF16)


def pack(core, first, second, groups, width):
    slots = first.shape[1]
    out = jax.ShapeDtypeStruct((2, slots, width), BF16)
    res = pl.pallas_call(
        functools.partial(pack_kernel, groups, width),
        out_shape=[out] * (2 * groups),
        in_specs=[SMEM, VMEM, VMEM],
        out_specs=[VMEM] * (2 * groups),
        compiler_params=params(),
        cost_estimate=cost(0, 2 * first.size * 4),
        name="pack",
    )(core, first, second)
    return res[:groups], res[groups:]


def gate_kernel(parts, offset_ref, pos_ref, x_ref, *refs):
    w_refs, out_ref = refs[:parts], refs[parts]
    chunk = w_refs[0].shape[-1]
    total = jnp.zeros((8, x_ref.shape[1]), F32)
    for s in range(parts):
        cols = pl.ds(pl.multiple_of(offset_ref[s] * chunk, HEAD), chunk)
        w_rows = jnp.broadcast_to(w_refs[s][...].astype(F32), (8, chunk)).astype(BF16)
        total = total + nt(w_rows, x_ref[0, :, cols])
    gate = 1.0 / (1.0 + jnp.exp(-total[0:1]))
    out_ref[...] = jnp.where(pos_ref[...] >= 0, gate, 0.0)


def router_gate(offsets, route_pos, x_routed, w_parts):
    parts = len(w_parts)
    return pl.pallas_call(
        functools.partial(gate_kernel, parts),
        out_shape=jax.ShapeDtypeStruct(route_pos.shape, F32),
        in_specs=[SMEM] + [VMEM] * (2 + parts),
        out_specs=VMEM,
        compiler_params=params(),
        cost_estimate=cost(16 * x_routed.size, x_routed.size * 2),
        name="router_gate",
    )(offsets, route_pos, x_routed, *w_parts)


def attention_kernel(remote, scale, core_ref, live_ref, gate_own, gate_sib, acc_own, acc_sib, q_own, q_sib, *refs):
    chunks = 2 + remote
    kv = refs[:chunks]
    outs = refs[chunks:]
    dq_own, sib_out, kv_own = outs[:3]
    kv_remote = outs[3 : 3 + remote]
    sum_own, sum_sib = outs[3 + remote :]
    slots, width = q_own.shape[1], q_own.shape[2]
    core = core_ref[0]
    key = lax.broadcasted_iota(jnp.int32, (slots, slots), 0)
    query = lax.broadcasted_iota(jnp.int32, (slots, slots), 1)
    counts = [jnp.sum(live_ref[i : i + 1], axis=1, keepdims=True) for i in range(chunks)]
    lives = [key < counts[i] for i in range(chunks)]
    own_later = core == 1
    bias_rows = []
    for i in range(chunks):
        live = lives[i]
        if i == 0:
            pair = (live & (key <= query), live & jnp.logical_not(own_later))
        elif i == 1:
            pair = (live & own_later, live & (key <= query))
        else:
            pair = (live, live)
        bias_rows.append(jnp.concatenate([jnp.where(p, 0.0, NEG_FILL) for p in pair], axis=1))
    bias = jnp.concatenate(bias_rows, axis=0)
    gates = jnp.concatenate([gate_own[...], gate_sib[...]], axis=1)
    total = jnp.zeros((1, 2 * slots), F32)
    for h in range(width // HEAD):
        cols = slice(h * HEAD, (h + 1) * HEAD)
        q = jnp.concatenate([q_own[0, :, cols], q_sib[0, :, cols]], axis=0)
        dg = jnp.concatenate([q_own[1, :, cols], q_sib[1, :, cols]], axis=0)
        k = jnp.concatenate([r[0, :, cols] for r in kv], axis=0)
        v = jnp.concatenate([r[1, :, cols] for r in kv], axis=0)
        scores = nt(k, q) * scale + bias
        top = jnp.max(scores, axis=0, keepdims=True)
        e = jnp.exp(scores - top)
        inverse = 1.0 / jnp.sum(e, axis=0, keepdims=True)
        gw = nt(v, dg)
        delta = jnp.sum(e * gw, axis=0, keepdims=True) * inverse
        total = total + delta
        weights = e * (inverse * gates)
        dv = nn(weights.astype(BF16), dg)
        ds = (weights * ((gw - delta) * scale)).astype(BF16)
        dk = nn(ds, q)
        dq = tn(ds, k)
        dq_own[:, cols] = dq[:slots].astype(dq_own.dtype)
        sib_out[0, :, cols] = dq[slots:].astype(BF16)
        kv_own[0, :, cols] = dk[:slots].astype(BF16)
        kv_own[1, :, cols] = dv[:slots].astype(BF16)
        sib_out[1, :, cols] = dk[slots : 2 * slots].astype(BF16)
        sib_out[2, :, cols] = dv[slots : 2 * slots].astype(BF16)
        for i in range(remote):
            rows = slice((2 + i) * slots, (3 + i) * slots)
            kv_remote[i][0, :, cols] = dk[rows].astype(BF16)
            kv_remote[i][1, :, cols] = dv[rows].astype(BF16)
    sum_own[...] = acc_own[...] + total[:, :slots]
    sum_sib[...] = acc_sib[...] + total[:, slots:]


def attention(core, live, gates, accs, q_own, q_sib, kv):
    remote = len(kv) - 2
    _, slots, width = q_own.shape
    pair = jax.ShapeDtypeStruct((2, slots, width), BF16)
    row = jax.ShapeDtypeStruct((1, slots), F32)
    outs = [
        jax.ShapeDtypeStruct((slots, width), BF16),
        jax.ShapeDtypeStruct((3, slots, width), BF16),
        pair,
        *([pair] * remote),
        row,
        row,
    ]
    keys = (2 + remote) * slots
    res = pl.pallas_call(
        functools.partial(attention_kernel, remote, HEAD**-0.5),
        out_shape=outs,
        in_specs=[SMEM] + [VMEM] * (7 + len(kv)),
        out_specs=[VMEM] * len(outs),
        compiler_params=params(48),
        cost_estimate=cost(20 * slots * keys * width, 8 * keys * width + 20 * slots * width, 2 * slots * keys * width // HEAD),
        name="attention",
    )(core, live, *gates, *accs, q_own, q_sib, *kv)
    return res[0], res[1], res[2], res[3 : 3 + remote], (res[3 + remote], res[4 + remote])


def combine_kernel(groups, width, remote, core_ref, *refs):
    dq_own, sib, kv_own = refs[:groups], refs[groups : 2 * groups], refs[2 * groups : 3 * groups]
    back = refs[3 * groups : 3 * groups + groups * remote]
    dq_out, dk_out, dv_out = refs[3 * groups + groups * remote :]
    half = groups * width
    core = core_ref[0]
    for g in range(groups):
        own = pl.ds(pl.multiple_of(core * half + g * width, HEAD), width)
        other = pl.ds(pl.multiple_of((1 - core) * half + g * width, HEAD), width)
        dq_out[0, :, own] = dq_own[g][...].astype(F32)
        dq_out[0, :, other] = sib[g][0].astype(F32)
        for i, out in enumerate((dk_out, dv_out)):
            mine = kv_own[g][i].astype(F32)
            theirs = sib[g][1 + i].astype(F32)
            for r in range(remote):
                part = back[g * remote + r][i].astype(F32)
                if r % 2 == 0:
                    mine = mine + part
                else:
                    theirs = theirs + part
            out[0, :, own] = mine
            out[0, :, other] = theirs


def combine(core, dq_own, sib, kv_own, back, shape):
    groups = len(dq_own)
    remote = len(back[0])
    out = jax.ShapeDtypeStruct(shape, F32)
    flat = [*dq_own, *sib, *kv_own, *(b for group in back for b in group)]
    return pl.pallas_call(
        functools.partial(combine_kernel, groups, dq_own[0].shape[-1], remote),
        out_shape=[out] * 3,
        in_specs=[SMEM] + [VMEM] * len(flat),
        out_specs=[VMEM] * 3,
        compiler_params=params(48),
        cost_estimate=cost(0, 3 * out.size * 6),
        name="combine",
    )(core, *flat)


def router_kernel(parts, target_ref, gate_ref, own_ref, sib_ref, x_ref, *outs):
    gate = gate_ref[...]
    grad = (own_ref[...] + sib_ref[...]) * gate * (1.0 - gate)
    high = grad.astype(BF16)
    rest = grad - high.astype(F32)
    mid = rest.astype(BF16)
    low = (rest - mid.astype(F32)).astype(BF16)
    row = lax.broadcasted_iota(jnp.int32, (8, grad.shape[1]), 0)
    lhs = jnp.where(row == 0, high.astype(F32), jnp.where(row == 1, mid.astype(F32), jnp.where(row == 2, low.astype(F32), 0.0)))
    lhs = lhs.astype(BF16)
    chunk = outs[0].shape[-1]
    for s in range(parts):
        cols = pl.ds(pl.multiple_of(target_ref[s] * chunk, HEAD), chunk)
        outs[s][...] = jnp.sum(nn(lhs, x_ref[0, :, cols]), axis=0, keepdims=True)


def router_terms(targets, gate, own, sib, x_routed, parts):
    chunk = x_routed.shape[-1] // parts
    return pl.pallas_call(
        functools.partial(router_kernel, parts),
        out_shape=[jax.ShapeDtypeStruct((1, chunk), F32)] * parts,
        in_specs=[SMEM] + [VMEM] * 4,
        out_specs=[VMEM] * parts,
        compiler_params=params(),
        cost_estimate=cost(16 * x_routed.size, x_routed.size * 2),
        name="router_terms",
    )(targets, gate, own, sib, x_routed)


def here():
    me = lax.axis_index("ctx")
    return lax.rem(me, 2), lax.div(me, 2)


MARK = 2.0**60
MARK_LIMIT = 2.0**50


def live_rows(pos_ref, slots):
    count = jnp.sum((pos_ref[...] >= 0).astype(jnp.int32), axis=1, keepdims=True)
    return lax.broadcasted_iota(jnp.int32, (slots, HEAD), 0) < count


def mark_dead(keys, live):
    width = keys.shape[-1]
    mask = jnp.concatenate([live] * (width // HEAD), axis=1)
    return jnp.where(mask, keys.astype(F32), MARK).astype(BF16)


def cross_pack_kernel(pos_any, w_any, k_ref, v_ref, q_ref, dg_ref, straight, diag, w_out, wide, pos_ref, w_ref, sems):
    small = [pltpu.make_async_copy(pos_any, pos_ref, sems.at[4]), pltpu.make_async_copy(w_any, w_ref, sems.at[5])]
    for c in small:
        c.start()
    slots, width = straight.shape[1], straight.shape[2]
    half = k_ref.shape[-1] // 2
    core, chip = here()
    ends = ((straight, core * half), (diag, (1 - core) * half))

    def copies(first, second, targets, offset):
        out = []
        for i, (end, start) in enumerate(ends):
            cols = pl.ds(pl.multiple_of(start + offset, HEAD), width)
            out.append(pltpu.make_async_copy(first.at[0, :, cols], end.at[0], sems.at[2 * i]))
            out.append(pltpu.make_async_copy(second.at[0, :, cols], targets[i], sems.at[2 * i + 1]))
        for c in out:
            c.start()
        for c in out:
            c.wait()

    @pl.when(chip == 0)
    def _():
        copies(k_ref, v_ref, (straight.at[1], diag.at[1]), 0)
        small[0].wait()
        live = live_rows(pos_ref, slots)
        for end, _ in ends:
            end[0] = mark_dead(end[0], live)

    @pl.when(chip != 0)
    def _():
        copies(q_ref, dg_ref, (wide.at[0], wide.at[1]), width)
        small[0].wait()
        for i, (end, _) in enumerate(ends):
            end[1] = wide[i].astype(BF16)

    small[1].wait()
    w_out[...] = w_ref[...].astype(F32).reshape(w_out.shape)


def cross_pack(route_pos, w_router, keys, values, queries, d_gated):
    _, slots, full = keys.shape
    cross = pltpu.VMEM((2, slots, full // 4), BF16)
    hbm = pl.BlockSpec(memory_space=pltpu.HBM)
    return pl.pallas_call(
        cross_pack_kernel,
        out_shape=[cross, cross, jax.ShapeDtypeStruct((1, w_router.shape[0]), F32)],
        in_specs=[hbm] * 6,
        out_specs=[VMEM] * 3,
        scratch_shapes=[
            pltpu.VMEM((2, slots, full // 4), F32),
            pltpu.VMEM(route_pos.shape, jnp.int32),
            pltpu.VMEM(w_router.shape, BF16),
            pltpu.SemaphoreType.DMA((6,)),
        ],
        compiler_params=params(),
        cost_estimate=cost(0, 10 * slots * full),
        name="cross_pack",
    )(*in_hbm(route_pos, w_router, keys, values, queries, d_gated))


def sib_pack_kernel(pos_ref, k_ref, v_ref, q_ref, dg_ref, out, wide, sems):
    slots, half = out.shape[1], out.shape[2]
    cols = pl.ds(pl.multiple_of((1 - here()[0]) * half, HEAD), half)
    sources = ((k_ref, out.at[0]), (dg_ref, wide), (v_ref, out.at[1]), (q_ref, out.at[2]))
    copies = [pltpu.make_async_copy(src.at[0, :, cols], dst, sems.at[i]) for i, (src, dst) in enumerate(sources)]
    for c in copies:
        c.start()
    live = live_rows(pos_ref, slots)
    copies[0].wait()
    out[0] = mark_dead(out[0], live)
    copies[1].wait()
    out[3] = wide[...].astype(BF16)
    copies[2].wait()
    copies[3].wait()


def sib_pack(route_pos, keys, values, queries, d_gated):
    _, slots, full = keys.shape
    hbm = pl.BlockSpec(memory_space=pltpu.HBM)
    return pl.pallas_call(
        sib_pack_kernel,
        out_shape=pltpu.VMEM((4, slots, full // 2), BF16),
        in_specs=[VMEM, hbm, hbm, hbm, hbm],
        out_specs=VMEM,
        scratch_shapes=[pltpu.VMEM((slots, full // 2), F32), pltpu.SemaphoreType.DMA((4,))],
        compiler_params=params(),
        cost_estimate=cost(0, 20 * slots * full),
        name="sib_pack",
    )(route_pos, *in_hbm(keys, values, queries, d_gated))


def put_gates(live_ref, rows_x, w_ref, parts, out_ref):
    chunk = w_ref.shape[1] // parts
    slots = rows_x.shape[1]
    me = lax.axis_index("dp")
    for i in range(2):
        total = jnp.zeros((8, slots), F32)
        for j in range(parts):
            w_rows = jnp.broadcast_to(w_ref[:, j * chunk : (j + 1) * chunk], (8, chunk)).astype(BF16)
            cols = pl.ds(pl.multiple_of((me ^ j) * chunk, HEAD), chunk)
            total = total + nt(w_rows, rows_x[i, :, cols])
        lanes = slice(i * slots, (i + 1) * slots)
        out_ref[:, lanes] = live_ref[:, lanes] / (1.0 + jnp.exp(-total[0:1]))


def local_mask(core, pair):
    slots = pair.shape[1] // 2
    key = lax.broadcasted_iota(jnp.int32, (slots, slots), 0)
    query = lax.broadcasted_iota(jnp.int32, (slots, slots), 1)
    causal = key <= query
    own_live = pair[0, :slots, :slots].astype(F32) < MARK_LIMIT
    sib_live = pair[0, slots:, :slots].astype(F32) < MARK_LIMIT
    own_rows = jnp.concatenate([own_live & causal, own_live & (core == 0)], axis=1)
    sib_rows = jnp.concatenate([sib_live & (core == 1), sib_live & causal], axis=1)
    return jnp.concatenate([own_rows, sib_rows], axis=0)


def kept_stats(scores, gw, kept, stats, h):
    top = jnp.max(scores, axis=0, keepdims=True)
    e = jnp.exp(scores - top).astype(BF16)
    gw = gw.astype(BF16)
    kept[0, h] = e
    kept[1, h] = gw
    e = e.astype(F32)
    stats[0, h : h + 1] = top
    stats[1, h : h + 1] = jnp.sum(e, axis=0, keepdims=True)
    stats[2, h : h + 1] = jnp.sum(e * gw.astype(F32), axis=0, keepdims=True)


def partial_stats(scores, gw, stats, h):
    top = jnp.max(scores, axis=0, keepdims=True)
    e = jnp.exp(scores - top)
    stats[0, h : h + 1] = top
    stats[1, h : h + 1] = jnp.sum(e, axis=0, keepdims=True)
    stats[2, h : h + 1] = jnp.sum(e * gw, axis=0, keepdims=True)


def local_stats_kernel(scale, pos_ref, k_ref, v_ref, q_ref, dg_ref, sib, x_ref, x_sib, stats, live, near, far, rows_x, wide, sems, x_sems):
    slots, half = sib.shape[1], sib.shape[2]
    width = half // 2
    core = here()[0]
    own, other = slice(0, slots), slice(slots, 2 * slots)
    stages = []
    for g, pair in enumerate((near, far)):
        cols = slice(g * width, (g + 1) * width)
        held = pl.ds(pl.multiple_of(core * half + g * width, HEAD), width)
        copies = [
            pltpu.make_async_copy(ref.at[0, :, held], pair.at[j, own], sems.at[8 * g + j])
            for j, ref in enumerate((k_ref, v_ref, q_ref))
        ]
        copies.append(pltpu.make_async_copy(dg_ref.at[0, :, held], wide.at[:, cols], sems.at[8 * g + 3]))
        for j in range(4):
            copies.append(pltpu.make_async_copy(sib.at[j, :, cols], pair.at[j, other], sems.at[8 * g + 4 + j]))
        for c in copies:
            c.start()
        stages.append(copies)
    x_copies = []
    depth = x_ref.shape[2] // 2
    for i, ref in enumerate((x_ref, x_sib)):
        for g in range(2):
            cols = slice(g * depth, (g + 1) * depth)
            x_copies.append(pltpu.make_async_copy(ref.at[0, :, cols], rows_x.at[i, :, cols], x_sems.at[2 * i + g]))
    for c in x_copies:
        c.start()
    rows_live = live_rows(pos_ref, slots)
    mask = None
    for g, pair in enumerate((near, far)):
        cols = slice(g * width, (g + 1) * width)
        for c in stages[g]:
            c.wait()
        pair[0, own] = mark_dead(pair[0, own], rows_live)
        pair[3, own] = wide[:, cols].astype(BF16)
        if mask is None:
            mask = local_mask(core, pair)
            marks = nt(jnp.ones((8, HEAD), BF16), pair[0, :, :HEAD])[0:1]
            live[...] = jnp.where(marks < MARK_LIMIT, 1.0, 0.0)
        for h in range(width // HEAD):
            at = slice(h * HEAD, (h + 1) * HEAD)
            scores = jnp.where(mask, nt(pair[0, :, at], pair[2, :, at]) * scale, NEG_FILL)
            partial_stats(scores, nt(pair[1, :, at], pair[3, :, at]), stats, g * width // HEAD + h)
    for c in x_copies:
        c.wait()


def local_stats(route_pos, keys, values, queries, d_gated, sib, x_routed, x_sib):
    _, slots, half = sib.shape
    heads = half // HEAD
    anywhere = pl.BlockSpec(memory_space=pl.ANY)
    return pl.pallas_call(
        functools.partial(local_stats_kernel, HEAD**-0.5),
        out_shape=[
            jax.ShapeDtypeStruct((3, heads, 2 * slots), F32),
            jax.ShapeDtypeStruct((1, 2 * slots), F32),
            pltpu.VMEM((4, 2 * slots, half // 2), BF16),
            pltpu.VMEM((4, 2 * slots, half // 2), BF16),
            pltpu.VMEM((2, slots, x_routed.shape[2]), BF16),
        ],
        in_specs=[VMEM] + [anywhere] * 7,
        out_specs=[VMEM] * 5,
        scratch_shapes=[pltpu.VMEM((slots, half), F32), pltpu.SemaphoreType.DMA((16,)), pltpu.SemaphoreType.DMA((4,))],
        compiler_params=params(),
        cost_estimate=cost(16 * slots * slots * half, 16 * slots * half, 4 * slots * slots * half // HEAD),
        name="local_stats",
    )(route_pos, *in_hbm(keys, values, queries, d_gated), sib, x_routed, x_sib)


def cross_stats_kernel(scale, parts, near, far, straight, diag, live, rows_x, w_ref, local, cross, stats, kept, gates, message):
    put_gates(live, rows_x, w_ref, parts, gates)
    slots, width = straight.shape[1], straight.shape[2]
    chip = here()[1]
    top, bottom = slice(0, slots), slice(slots, 2 * slots)

    @pl.when(chip == 0)
    def _():
        for part in range(2):
            cross[part] = far[part]
            cross[2 + part, top] = straight[part]
            cross[2 + part, bottom] = diag[part]

    @pl.when(chip != 0)
    def _():
        for part in range(2):
            cross[part, top] = straight[part]
            cross[part, bottom] = diag[part]
            cross[2 + part] = near[2 + part]

    alive = cross[0, :, :HEAD].astype(F32) < MARK_LIMIT
    mask = jnp.concatenate([alive] * (2 * slots // HEAD), axis=1)
    heads = width // HEAD
    for h in range(heads):
        cols = slice(h * HEAD, (h + 1) * HEAD)
        scores = jnp.where(mask, nt(cross[0, :, cols], cross[2, :, cols]) * scale, NEG_FILL)
        kept_stats(scores, nt(cross[1, :, cols], cross[3, :, cols]), kept, stats, h)
    for i in range(3):
        message[i] = jnp.where(chip == 0, stats[i], local[i, heads:])
    message[3] = jnp.broadcast_to(gates[...], message.shape[1:])


def cross_stats(near, far, straight, diag, live, rows_x, w_full, local, parts):
    _, slots, width = straight.shape
    heads = width // HEAD
    return pl.pallas_call(
        functools.partial(cross_stats_kernel, HEAD**-0.5, parts),
        out_shape=[
            pltpu.VMEM((4, 2 * slots, width), BF16),
            jax.ShapeDtypeStruct((3, heads, 2 * slots), F32),
            pltpu.VMEM((2, heads, 2 * slots, 2 * slots), BF16),
            jax.ShapeDtypeStruct(live.shape, F32),
            jax.ShapeDtypeStruct((4, heads, 2 * slots), F32),
        ],
        in_specs=[VMEM] * 8,
        out_specs=[VMEM] * 5,
        compiler_params=params(),
        cost_estimate=cost(16 * slots * slots * width, 32 * slots * width, 4 * slots * slots * heads),
        name="cross_stats",
    )(near, far, straight, diag, live, rows_x, w_full, local)


NONE = (-3e38, 0.0, 0.0)


def merge(first, second):
    top = jnp.maximum(first[0], second[0])
    a, b = jnp.exp(first[0] - top), jnp.exp(second[0] - top)
    inverse = 1.0 / (first[1] * a + second[1] * b)
    return a * inverse, (first[2] * a + second[2] * b) * inverse


def choose(flag, yes, no):
    return [jnp.where(flag, y, n) for y, n in zip(yes, no)]


def gradients(q, k, dg, e, gw, scale, factor, delta):
    weights = e * factor
    ds = (weights * ((gw - delta) * scale)).astype(BF16)
    return tn(ds, k), nn(ds, q), nn(weights.astype(BF16), dg)


def local_gradients(pair, h, mask, scale, top, factor, delta):
    cols = slice(h * HEAD, (h + 1) * HEAD)
    k, v, q, dg = [pair[i, :, cols] for i in range(4)]
    e = jnp.exp(jnp.where(mask, nt(k, q) * scale, NEG_FILL) - top)
    return gradients(q, k, dg, e, nt(v, dg), scale, factor, delta)


def near_grad_kernel(scale, pair, local, stats, gates, dq_out, own_out, sib_out, sum_out):
    slots, width = own_out.shape[1], own_out.shape[2]
    heads = width // HEAD
    first = here()[1] == 0
    near = [local[i, :heads] for i in range(3)]
    factor, delta = merge(near, choose(first, NONE, [stats[i] for i in range(3)]))
    factor = factor * gates[...]
    sum_out[...] = jnp.sum(delta, axis=0, keepdims=True)
    mask = local_mask(here()[0], pair)
    for h in range(heads):
        cols = slice(h * HEAD, (h + 1) * HEAD)
        row = slice(h, h + 1)
        dq, dk, dv = local_gradients(pair, h, mask, scale, near[0][row], factor[row], delta[row])
        dq_out[:, cols] = dq
        for i, part in enumerate((dk, dv)):
            own_out[i, :, cols] = part[:slots].astype(BF16)
            sib_out[i, :, cols] = part[slots:].astype(BF16)


def near_grad(pair, local, stats, gates):
    _, rows, width = pair.shape
    slots = rows // 2
    out = pltpu.VMEM((2, slots, width), BF16)
    return pl.pallas_call(
        functools.partial(near_grad_kernel, HEAD**-0.5),
        out_shape=[pltpu.VMEM((2 * slots, width), F32), out, out, jax.ShapeDtypeStruct(gates.shape, F32)],
        in_specs=[VMEM] * 4,
        out_specs=[VMEM] * 4,
        compiler_params=params(),
        cost_estimate=cost(20 * slots * slots * width, 40 * slots * width),
        name="near_grad",
    )(pair, local, stats, gates)


def put_terms(grad, rows_x, out_ref):
    high = grad.astype(BF16)
    rest = grad - high.astype(F32)
    mid = rest.astype(BF16)
    low = (rest - mid.astype(F32)).astype(BF16)
    slots = rows_x.shape[1]
    row = lax.broadcasted_iota(jnp.int32, (8, grad.shape[1]), 0)
    lhs = jnp.where(row == 0, high.astype(F32), jnp.where(row == 1, mid.astype(F32), jnp.where(row == 2, low.astype(F32), 0.0)))
    lhs = lhs.astype(BF16)
    term = jnp.sum(nn(lhs[:, :slots], rows_x[0]) + nn(lhs[:, slots:], rows_x[1]), axis=0, keepdims=True)
    parts, copies, _, chunk = out_ref.shape
    for j in range(parts):
        for i in range(copies):
            out_ref[j, i] = term[:, j * chunk : (j + 1) * chunk]


def cross_grad_kernel(scale, cross, kept, stats, local, heard, gates, near_dq, near_sum, rows_x, straight, diag, dq_out, keep, final, terms):
    slots, width = straight.shape[1], straight.shape[2]
    heads = width // HEAD
    first = here()[1] == 0
    late = jnp.where(first, 0.0, 1.0)
    mine = [stats[i] for i in range(3)]
    other = [heard[i] for i in range(3)]
    near = [local[i, :heads] for i in range(3)]
    far = [local[i, heads:] for i in range(3)]
    factor, delta = merge(mine, choose(first, other, near))
    factor = factor * jnp.where(first, heard[3], jnp.broadcast_to(gates[...], factor.shape))
    final[0], final[1] = merge(far, choose(first, NONE, other))
    for h in range(heads):
        cols = slice(h * HEAD, (h + 1) * HEAD)
        row = slice(h, h + 1)
        dq, dk, dv = gradients(
            cross[2, :, cols], cross[0, :, cols], cross[3, :, cols],
            kept[0, h].astype(F32), kept[1, h].astype(F32), scale, factor[row], delta[row],
        )
        dq_out[:, cols] = (near_dq[:, cols] + late * dq).astype(BF16)
        keep[0, :, cols] = dk.astype(BF16)
        keep[1, :, cols] = dv.astype(BF16)
        sent = jnp.where(first, dq, dk).astype(BF16)
        straight[0, :, cols] = sent[:slots]
        diag[0, :, cols] = sent[slots:]
        straight[1, :, cols] = dv[:slots].astype(BF16)
        diag[1, :, cols] = dv[slots:].astype(BF16)
    sums = near_sum[...] + jnp.sum(final[1], axis=0, keepdims=True)
    put_terms(sums * gates[...] * (1.0 - gates[...]), rows_x, terms)


def cross_grad(cross, kept, stats, local, heard, gates, near_dq, near_sum, rows_x, parts, copies):
    _, rows, width = cross.shape
    slots = rows // 2
    out = pltpu.VMEM((2, slots, width), BF16)
    return pl.pallas_call(
        functools.partial(cross_grad_kernel, HEAD**-0.5),
        out_shape=[
            out,
            out,
            pltpu.VMEM((rows, width), BF16),
            pltpu.VMEM((2, rows, width), BF16),
            jax.ShapeDtypeStruct((2, width // HEAD, rows), F32),
            pltpu.VMEM((parts, copies, 1, rows_x.shape[2] // parts), F32),
        ],
        in_specs=[VMEM] * 9,
        out_specs=[VMEM] * 6,
        compiler_params=params(),
        cost_estimate=cost(24 * slots * slots * width, 64 * slots * width),
        name="cross_grad",
    )(cross, kept, stats, local, heard, gates, near_dq, near_sum, rows_x)


def far_grad_kernel(scale, pair, local, final, gates, keep, near_dq, near_own, near_sib, own_out, sib_out):
    slots, width = pair.shape[1] // 2, pair.shape[2]
    heads = width // HEAD
    early = jnp.where(here()[1] == 0, 1.0, 0.0)
    factor = final[0] * gates[...]
    mask = local_mask(here()[0], pair)
    own_out[0, :, :width] = near_dq[:slots]
    sib_out[0, :, :width] = near_dq[slots:]
    for i in range(2):
        own_out[1 + i, :, :width] = near_own[i]
        sib_out[1 + i, :, :width] = near_sib[i]
    for h in range(heads):
        cols = slice(width + h * HEAD, width + (h + 1) * HEAD)
        at = slice(h * HEAD, (h + 1) * HEAD)
        row = slice(h, h + 1)
        top = local[0, heads + h : heads + h + 1]
        dq, dk, dv = local_gradients(pair, h, mask, scale, top, factor[row], final[1, row])
        dk = dk + early * keep[0, :, at].astype(F32)
        dv = dv + early * keep[1, :, at].astype(F32)
        for i, part in enumerate((dq, dk, dv)):
            own_out[i, :, cols] = part[:slots].astype(BF16)
            sib_out[i, :, cols] = part[slots:].astype(BF16)


def far_grad(pair, local, final, gates, keep, near_dq, near_own, near_sib):
    _, rows, width = pair.shape
    slots, half = rows // 2, 2 * width
    out = jax.ShapeDtypeStruct((3, slots, half), BF16)
    return pl.pallas_call(
        functools.partial(far_grad_kernel, HEAD**-0.5),
        out_shape=[out, out],
        in_specs=[VMEM] * 8,
        out_specs=[VMEM] * 2,
        compiler_params=params(),
        cost_estimate=cost(20 * slots * slots * half, 40 * slots * half),
        name="far_grad",
    )(pair, local, final, gates, keep, near_dq, near_own, near_sib)


def own_join_kernel(own, dq_out, dk_out, dv_out, waiting, total, sems):
    slots, half = own.shape[1], own.shape[2]
    width = half // 2
    core, chip = here()
    cols = pl.ds(pl.multiple_of(core * half, HEAD), half)
    stores = []
    for j, out in enumerate((dq_out, dk_out, dv_out)):
        total[j] = own[j].astype(F32)
        stores.append(pltpu.make_async_copy(total.at[j], out.at[0, :, cols], sems.at[j]))
        stores[-1].start()
    waiting[0] = jnp.where(chip == 0, total[1, :, :width], total[0, :, width:]).astype(BF16)
    waiting[1] = own[2, :, :width]
    for c in stores:
        c.wait()


def own_join(own, shape):
    out = pltpu.HBM(shape, F32)
    _, slots, half = own.shape
    hbm = pl.BlockSpec(memory_space=pltpu.HBM)
    return pl.pallas_call(
        own_join_kernel,
        out_shape=[out] * 3 + [jax.ShapeDtypeStruct((2, slots, half // 2), BF16)],
        in_specs=[VMEM],
        out_specs=[hbm] * 3 + [VMEM],
        scratch_shapes=[pltpu.VMEM((3, slots, half), F32), pltpu.SemaphoreType.DMA((3,))],
        compiler_params=params(),
        cost_estimate=cost(0, 18 * own.size),
        name="own_join",
    )(own)


def finish_kernel(waiting, sib, straight, diag, dq_in, dk_in, dv_in, dq_out, dk_out, dv_out, low, held, total, added, in_sems, out_sems):
    half = sib.shape[2]
    width = half // 2
    core, chip = here()
    early, late = jnp.where(chip == 0, 1.0, 0.0), jnp.where(chip == 0, 0.0, 1.0)
    loads = [pltpu.make_async_copy(sib.at[j], low.at[j], in_sems.at[j]) for j in range(3)]
    loads += [pltpu.make_async_copy(waiting.at[j], held.at[j], in_sems.at[3 + j]) for j in range(2)]
    for c in loads:
        c.start()
    cols = pl.ds(pl.multiple_of((1 - core) * half, HEAD), half)
    stores = []
    for j, out in enumerate((dq_out, dk_out, dv_out)):
        loads[j].wait()
        first, second = low[j, :, :width].astype(F32), low[j, :, width:].astype(F32)
        if j == 0:
            second = second + late * diag[0].astype(F32)
        else:
            first = first + early * diag[j - 1].astype(F32)
        total[j, :, :width] = first
        total[j, :, width:] = second
        stores.append(pltpu.make_async_copy(total.at[j], out.at[0, :, cols], out_sems.at[j]))
        stores[-1].start()
    for j in range(2):
        loads[3 + j].wait()
        added[j] = held[j].astype(F32) + straight[j].astype(F32)

    def store(j, out, offset):
        at = pl.ds(pl.multiple_of(core * half + offset, HEAD), width)
        copy = pltpu.make_async_copy(added.at[j], out.at[0, :, at], out_sems.at[3 + j])
        copy.start()
        return copy

    @pl.when(chip == 0)
    def _():
        copies = [store(0, dk_out, 0), store(1, dv_out, 0)]
        for c in copies:
            c.wait()

    @pl.when(chip != 0)
    def _():
        store(0, dq_out, width).wait()

    for c in stores:
        c.wait()


def finish(waiting, sib, straight, diag, outs):
    _, slots, half = sib.shape
    hbm = pl.BlockSpec(memory_space=pltpu.HBM)
    anywhere = pl.BlockSpec(memory_space=pl.ANY)
    return pl.pallas_call(
        finish_kernel,
        out_shape=[pltpu.HBM(o.shape, F32) for o in outs],
        in_specs=[anywhere] * 2 + [VMEM] * 2 + [hbm] * 3,
        out_specs=[hbm] * 3,
        scratch_shapes=[
            pltpu.VMEM((3, slots, half), BF16),
            pltpu.VMEM(waiting.shape, BF16),
            pltpu.VMEM((3, slots, half), F32),
            pltpu.VMEM(waiting.shape, F32),
            pltpu.SemaphoreType.DMA((5,)),
            pltpu.SemaphoreType.DMA((5,)),
        ],
        input_output_aliases={4: 0, 5: 1, 6: 2},
        compiler_params=params(),
        cost_estimate=cost(0, 12 * sib.size),
        name="finish",
    )(waiting, sib, straight, diag, *in_hbm(*outs))


def swap_body(route_pos, x_routed, w_router, queries, keys, values, d_gated):
    slots = queries.shape[1]
    n, ndp = lax.axis_size("ctx"), lax.axis_size("dp")

    def send(a, flip):
        return lax.ppermute(a, "ctx", [(i, i ^ flip) for i in range(n)])

    def beside(fn, *operands):
        def skip(*ops):
            return jax.tree.map(lambda o: jnp.zeros(o.shape, o.dtype), jax.eval_shape(fn, *ops))

        return lax.cond(route_pos[0, 0] >= -1, fn, skip, *operands)

    def after(value, *others):
        return lax.optimization_barrier((value, *others))[0]

    def widen(part, step, *first):
        other = lax.ppermute(part, "dp", [(i, i ^ step) for i in range(ndp)])
        return jnp.concatenate([part, after(other, *first)], axis=1)

    def exchange_phase(x_routed, w_part, theirs):
        sib, x_sib = send(theirs, 1), send(x_routed, 1)
        step = 2
        while 2 * step < ndp:
            w_part = widen(w_part, step)
            step *= 2
        return sib, x_sib, w_part

    def far_phase(*operands):
        own_out, sib_out = far_grad(*operands)
        sib_in = send(sib_out, 1)
        *outs, waiting = own_join(own_out, queries.shape)
        return outs, waiting, sib_in

    def tail_phase(terms, *operands):
        shared = lax.all_to_all(terms.reshape(ndp * n, 1, -1), ("dp", "ctx"), 0, 0, tiled=True)
        results = beside(far_phase, *operands)
        return *results, jnp.sum(shared, axis=0)[0] / float(ndp * n * slots // 2)

    out_s, out_d, w_part = cross_pack(route_pos, w_router, keys, values, queries, d_gated)
    in_s, in_d = send(out_s, 2), send(out_d, 3)

    theirs = sib_pack(after(route_pos, out_s), keys, values, queries, d_gated)
    if ndp > 1:
        w_part = widen(w_part, 1, theirs)
    sib, x_sib, w_part = beside(exchange_phase, x_routed, w_part, theirs)
    local, live, near, far, rows_x = local_stats(route_pos, keys, values, queries, d_gated, sib, x_routed, x_sib)
    if ndp > 2:
        w_part = widen(w_part, ndp // 2, local, in_s, in_d)
    cross, stats, kept, gates, message = cross_stats(near, far, in_s, in_d, live, rows_x, w_part, local, ndp)

    heard = send(message, 2)
    near_dq, near_own, near_sib, near_sum = near_grad(near, local, stats, gates)
    back_s, back_d, dq_low, keep, final, terms = cross_grad(
        cross, kept, stats, local, heard, gates, near_dq, near_sum, rows_x, ndp, n
    )

    ret_s, ret_d = send(back_s, 2), send(back_d, 3)
    outs, waiting, sib_in, router_grad = beside(
        tail_phase, terms, far, local, final, gates, keep, dq_low, near_own, near_sib
    )
    dq, dk, dv = finish(waiting, sib_in, ret_s, ret_d, outs)
    return dq, dk, dv, router_grad


def body(route_pos, x_routed, w_router, queries, keys, values, d_gated):
    slots, full = queries.shape[1], queries.shape[2]
    n, ndp = lax.axis_size("ctx"), lax.axis_size("dp")
    chips = n // 2
    me, dp_me = lax.axis_index("ctx"), lax.axis_index("dp")
    core = (me % 2).astype(jnp.int32).reshape(1)
    half = full // 2
    groups = GROUPS if (half // HEAD) % GROUPS == 0 else 1
    width = half // groups

    sib_pairs = [(i, i ^ 1) for i in range(n)]

    def forward_pairs(step, flip):
        return [(i, (i + 2 * step) ^ flip) for i in range(n) if i + 2 * step < n]

    def back_pairs(step, flip):
        return [(b, a) for a, b in forward_pairs(step, flip)]

    def to_sib(a):
        return lax.ppermute(a, "ctx", sib_pairs)

    links = [(step, flip) for step in range(1, chips) for flip in (0, 1)]

    w_row = w_router.reshape(1, -1)
    w_parts = [w_row] + [
        lax.ppermute(w_row, "dp", [(i, (i + s) % ndp) for i in range(ndp)]) for s in range(1, ndp)
    ]
    live = (route_pos >= 0).astype(jnp.int32)
    lives = [live, to_sib(live)] + [lax.ppermute(live, "ctx", forward_pairs(*link)) for link in links]
    live_all = jnp.concatenate(lives, axis=0)

    kv_mine, kv_theirs = pack(core, keys, values, groups, width)
    kv_far = [
        [lax.ppermute((kv_theirs if flip else kv_mine)[g], "ctx", forward_pairs(step, flip)) for step, flip in links]
        for g in range(groups)
    ]
    q_mine, q_theirs = pack(core, queries, d_gated, groups, width)
    kv_sib = [to_sib(a) for a in kv_theirs]
    q_sib = [to_sib(a) for a in q_theirs]

    offsets = ((dp_me - jnp.arange(ndp)) % ndp).astype(jnp.int32)
    gate = router_gate(offsets, route_pos, x_routed, w_parts)
    gates = (gate, to_sib(gate))

    accs = (jnp.zeros((1, slots), F32), jnp.zeros((1, slots), F32))
    dq_own, sib_in, kv_own, back = [], [], [], []
    for g in range(groups):
        dq, sib_out, kv_local, kv_remote, accs = attention(
            core, live_all, gates, accs, q_mine[g], q_sib[g], [kv_mine[g], kv_sib[g], *kv_far[g]]
        )
        back.append([lax.ppermute(a, "ctx", back_pairs(*link)) for a, link in zip(kv_remote, links)])
        sib_in.append(to_sib(sib_out))
        dq_own.append(dq)
        kv_own.append(kv_local)

    targets = ((dp_me + jnp.arange(ndp)) % ndp).astype(jnp.int32)
    terms = router_terms(targets, gate, accs[0], to_sib(accs[1]), x_routed, ndp)
    mine = terms[0]
    for s in range(1, ndp):
        mine = mine + lax.ppermute(terms[s], "dp", [(i, (i + s) % ndp) for i in range(ndp)])
    total = mine
    for s in range(1, n):
        total = total + lax.ppermute(mine, "ctx", [(i, (i + s) % n) for i in range(n)])
    router_grad = total[0] / float(ndp * n * slots // 2)

    dq, dk, dv = combine(core, dq_own, sib_in, kv_own, back, queries.shape)
    return dq, dk, dv, router_grad


def solution(mesh):
    placed = (
        P("dp", "ctx"),
        P("dp", "ctx", None),
        P("dp"),
        P("dp", "ctx", None),
        P("dp", "ctx", None),
        P("dp", "ctx", None),
        P("dp", "ctx", None),
    )
    ndp = mesh.shape["dp"]
    paired = mesh.shape["ctx"] == 4 and ndp & (ndp - 1) == 0
    return jax.shard_map(
        swap_body if paired else body,
        mesh=mesh,
        in_specs=placed,
        out_specs=(P("dp", "ctx", None), P("dp", "ctx", None), P("dp", "ctx", None), P("dp")),
        check_vma=False,
    )
```

```python
import functools

import jax
import jax.numpy as jnp
from jax import lax
from jax.experimental import pallas as pl
from jax.experimental.pallas import tpu as pltpu
from jax.sharding import PartitionSpec as P

HEAD = 128
GROUPS = 4
NEG_FILL = -1e30
MIB = 1024 * 1024
BF16 = jnp.bfloat16
F32 = jnp.float32

VMEM = pl.BlockSpec(memory_space=pltpu.VMEM)
SMEM = pl.BlockSpec(memory_space=pltpu.SMEM)


def params(mib=16):
    return pltpu.CompilerParams(vmem_limit_bytes=mib * MIB)


def cost(flops, nbytes, exps=0):
    return pl.CostEstimate(flops=1, bytes_accessed=1, transcendentals=0)


def in_hbm(*arrays):
    return [pltpu.with_memory_space_constraint(a, pltpu.HBM) for a in arrays]


def nt(a, b):
    return lax.dot_general(a, b, (((1,), (1,)), ((), ())), preferred_element_type=F32)


def nn(a, b):
    return lax.dot_general(a, b, (((1,), (0,)), ((), ())), preferred_element_type=F32)


def tn(a, b):
    return lax.dot_general(a, b, (((0,), (0,)), ((), ())), preferred_element_type=F32)


def pack_kernel(groups, width, core_ref, first_ref, second_ref, *outs):
    half = first_ref.shape[-1] // 2
    core = core_ref[0]
    for side in range(2):
        base = (core if side == 0 else 1 - core) * half
        for g in range(groups):
            out = outs[side * groups + g]
            cols = pl.ds(pl.multiple_of(base + g * width, HEAD), width)
            out[0] = first_ref[0, :, cols].astype(BF16)
            out[1] = second_ref[0, :, cols].astype(BF16)


def pack(core, first, second, groups, width):
    slots = first.shape[1]
    out = jax.ShapeDtypeStruct((2, slots, width), BF16)
    res = pl.pallas_call(
        functools.partial(pack_kernel, groups, width),
        out_shape=[out] * (2 * groups),
        in_specs=[SMEM, VMEM, VMEM],
        out_specs=[VMEM] * (2 * groups),
        compiler_params=params(),
        cost_estimate=cost(0, 2 * first.size * 4),
        name="pack",
    )(core, first, second)
    return res[:groups], res[groups:]


def gate_kernel(parts, offset_ref, pos_ref, x_ref, *refs):
    w_refs, out_ref = refs[:parts], refs[parts]
    chunk = w_refs[0].shape[-1]
    total = jnp.zeros((8, x_ref.shape[1]), F32)
    for s in range(parts):
        cols = pl.ds(pl.multiple_of(offset_ref[s] * chunk, HEAD), chunk)
        w_rows = jnp.broadcast_to(w_refs[s][...].astype(F32), (8, chunk)).astype(BF16)
        total = total + nt(w_rows, x_ref[0, :, cols])
    gate = 1.0 / (1.0 + jnp.exp(-total[0:1]))
    out_ref[...] = jnp.where(pos_ref[...] >= 0, gate, 0.0)


def router_gate(offsets, route_pos, x_routed, w_parts):
    parts = len(w_parts)
    return pl.pallas_call(
        functools.partial(gate_kernel, parts),
        out_shape=jax.ShapeDtypeStruct(route_pos.shape, F32),
        in_specs=[SMEM] + [VMEM] * (2 + parts),
        out_specs=VMEM,
        compiler_params=params(),
        cost_estimate=cost(16 * x_routed.size, x_routed.size * 2),
        name="router_gate",
    )(offsets, route_pos, x_routed, *w_parts)


def attention_kernel(remote, scale, core_ref, live_ref, gate_own, gate_sib, acc_own, acc_sib, q_own, q_sib, *refs):
    chunks = 2 + remote
    kv = refs[:chunks]
    outs = refs[chunks:]
    dq_own, sib_out, kv_own = outs[:3]
    kv_remote = outs[3 : 3 + remote]
    sum_own, sum_sib = outs[3 + remote :]
    slots, width = q_own.shape[1], q_own.shape[2]
    core = core_ref[0]
    key = lax.broadcasted_iota(jnp.int32, (slots, slots), 0)
    query = lax.broadcasted_iota(jnp.int32, (slots, slots), 1)
    counts = [jnp.sum(live_ref[i : i + 1], axis=1, keepdims=True) for i in range(chunks)]
    lives = [key < counts[i] for i in range(chunks)]
    own_later = core == 1
    bias_rows = []
    for i in range(chunks):
        live = lives[i]
        if i == 0:
            pair = (live & (key <= query), live & jnp.logical_not(own_later))
        elif i == 1:
            pair = (live & own_later, live & (key <= query))
        else:
            pair = (live, live)
        bias_rows.append(jnp.concatenate([jnp.where(p, 0.0, NEG_FILL) for p in pair], axis=1))
    bias = jnp.concatenate(bias_rows, axis=0)
    gates = jnp.concatenate([gate_own[...], gate_sib[...]], axis=1)
    total = jnp.zeros((1, 2 * slots), F32)
    for h in range(width // HEAD):
        cols = slice(h * HEAD, (h + 1) * HEAD)
        q = jnp.concatenate([q_own[0, :, cols], q_sib[0, :, cols]], axis=0)
        dg = jnp.concatenate([q_own[1, :, cols], q_sib[1, :, cols]], axis=0)
        k = jnp.concatenate([r[0, :, cols] for r in kv], axis=0)
        v = jnp.concatenate([r[1, :, cols] for r in kv], axis=0)
        scores = nt(k, q) * scale + bias
        top = jnp.max(scores, axis=0, keepdims=True)
        e = jnp.exp(scores - top)
        inverse = 1.0 / jnp.sum(e, axis=0, keepdims=True)
        gw = nt(v, dg)
        delta = jnp.sum(e * gw, axis=0, keepdims=True) * inverse
        total = total + delta
        weights = e * (inverse * gates)
        dv = nn(weights.astype(BF16), dg)
        ds = (weights * ((gw - delta) * scale)).astype(BF16)
        dk = nn(ds, q)
        dq = tn(ds, k)
        dq_own[:, cols] = dq[:slots].astype(dq_own.dtype)
        sib_out[0, :, cols] = dq[slots:].astype(BF16)
        kv_own[0, :, cols] = dk[:slots].astype(BF16)
        kv_own[1, :, cols] = dv[:slots].astype(BF16)
        sib_out[1, :, cols] = dk[slots : 2 * slots].astype(BF16)
        sib_out[2, :, cols] = dv[slots : 2 * slots].astype(BF16)
        for i in range(remote):
            rows = slice((2 + i) * slots, (3 + i) * slots)
            kv_remote[i][0, :, cols] = dk[rows].astype(BF16)
            kv_remote[i][1, :, cols] = dv[rows].astype(BF16)
    sum_own[...] = acc_own[...] + total[:, :slots]
    sum_sib[...] = acc_sib[...] + total[:, slots:]


def attention(core, live, gates, accs, q_own, q_sib, kv):
    remote = len(kv) - 2
    _, slots, width = q_own.shape
    pair = jax.ShapeDtypeStruct((2, slots, width), BF16)
    row = jax.ShapeDtypeStruct((1, slots), F32)
    outs = [
        jax.ShapeDtypeStruct((slots, width), BF16),
        jax.ShapeDtypeStruct((3, slots, width), BF16),
        pair,
        *([pair] * remote),
        row,
        row,
    ]
    keys = (2 + remote) * slots
    res = pl.pallas_call(
        functools.partial(attention_kernel, remote, HEAD**-0.5),
        out_shape=outs,
        in_specs=[SMEM] + [VMEM] * (7 + len(kv)),
        out_specs=[VMEM] * len(outs),
        compiler_params=params(48),
        cost_estimate=cost(20 * slots * keys * width, 8 * keys * width + 20 * slots * width, 2 * slots * keys * width // HEAD),
        name="attention",
    )(core, live, *gates, *accs, q_own, q_sib, *kv)
    return res[0], res[1], res[2], res[3 : 3 + remote], (res[3 + remote], res[4 + remote])


def combine_kernel(groups, width, remote, core_ref, *refs):
    dq_own, sib, kv_own = refs[:groups], refs[groups : 2 * groups], refs[2 * groups : 3 * groups]
    back = refs[3 * groups : 3 * groups + groups * remote]
    dq_out, dk_out, dv_out = refs[3 * groups + groups * remote :]
    half = groups * width
    core = core_ref[0]
    for g in range(groups):
        own = pl.ds(pl.multiple_of(core * half + g * width, HEAD), width)
        other = pl.ds(pl.multiple_of((1 - core) * half + g * width, HEAD), width)
        dq_out[0, :, own] = dq_own[g][...].astype(F32)
        dq_out[0, :, other] = sib[g][0].astype(F32)
        for i, out in enumerate((dk_out, dv_out)):
            mine = kv_own[g][i].astype(F32)
            theirs = sib[g][1 + i].astype(F32)
            for r in range(remote):
                part = back[g * remote + r][i].astype(F32)
                if r % 2 == 0:
                    mine = mine + part
                else:
                    theirs = theirs + part
            out[0, :, own] = mine
            out[0, :, other] = theirs


def combine(core, dq_own, sib, kv_own, back, shape):
    groups = len(dq_own)
    remote = len(back[0])
    out = jax.ShapeDtypeStruct(shape, F32)
    flat = [*dq_own, *sib, *kv_own, *(b for group in back for b in group)]
    return pl.pallas_call(
        functools.partial(combine_kernel, groups, dq_own[0].shape[-1], remote),
        out_shape=[out] * 3,
        in_specs=[SMEM] + [VMEM] * len(flat),
        out_specs=[VMEM] * 3,
        compiler_params=params(48),
        cost_estimate=cost(0, 3 * out.size * 6),
        name="combine",
    )(core, *flat)


def router_kernel(parts, target_ref, gate_ref, own_ref, sib_ref, x_ref, *outs):
    gate = gate_ref[...]
    grad = (own_ref[...] + sib_ref[...]) * gate * (1.0 - gate)
    high = grad.astype(BF16)
    rest = grad - high.astype(F32)
    mid = rest.astype(BF16)
    low = (rest - mid.astype(F32)).astype(BF16)
    row = lax.broadcasted_iota(jnp.int32, (8, grad.shape[1]), 0)
    lhs = jnp.where(row == 0, high.astype(F32), jnp.where(row == 1, mid.astype(F32), jnp.where(row == 2, low.astype(F32), 0.0)))
    lhs = lhs.astype(BF16)
    chunk = outs[0].shape[-1]
    for s in range(parts):
        cols = pl.ds(pl.multiple_of(target_ref[s] * chunk, HEAD), chunk)
        outs[s][...] = jnp.sum(nn(lhs, x_ref[0, :, cols]), axis=0, keepdims=True)


def router_terms(targets, gate, own, sib, x_routed, parts):
    chunk = x_routed.shape[-1] // parts
    return pl.pallas_call(
        functools.partial(router_kernel, parts),
        out_shape=[jax.ShapeDtypeStruct((1, chunk), F32)] * parts,
        in_specs=[SMEM] + [VMEM] * 4,
        out_specs=[VMEM] * parts,
        compiler_params=params(),
        cost_estimate=cost(16 * x_routed.size, x_routed.size * 2),
        name="router_terms",
    )(targets, gate, own, sib, x_routed)


def here():
    me = lax.axis_index("ctx")
    return lax.rem(me, 2), lax.div(me, 2)


MARK = 2.0**60
MARK_LIMIT = 2.0**50


def live_rows(pos_ref, slots):
    count = jnp.sum((pos_ref[...] >= 0).astype(jnp.int32), axis=1, keepdims=True)
    return lax.broadcasted_iota(jnp.int32, (slots, HEAD), 0) < count


def mark_dead(keys, live):
    width = keys.shape[-1]
    mask = jnp.concatenate([live] * (width // HEAD), axis=1)
    return jnp.where(mask, keys.astype(F32), MARK).astype(BF16)


def cross_pack_kernel(pos_any, w_any, k_ref, v_ref, q_ref, dg_ref, straight, diag, w_out, wide, pos_ref, w_ref, sems):
    small = [pltpu.make_async_copy(pos_any, pos_ref, sems.at[4]), pltpu.make_async_copy(w_any, w_ref, sems.at[5])]
    for c in small:
        c.start()
    slots, width = straight.shape[1], straight.shape[2]
    half = k_ref.shape[-1] // 2
    core, chip = here()
    ends = ((straight, core * half), (diag, (1 - core) * half))

    def copies(first, second, targets, offset):
        out = []
        for i, (end, start) in enumerate(ends):
            cols = pl.ds(pl.multiple_of(start + offset, HEAD), width)
            out.append(pltpu.make_async_copy(first.at[0, :, cols], end.at[0], sems.at[2 * i]))
            out.append(pltpu.make_async_copy(second.at[0, :, cols], targets[i], sems.at[2 * i + 1]))
        for c in out:
            c.start()
        for c in out:
            c.wait()

    @pl.when(chip == 0)
    def _():
        copies(k_ref, v_ref, (straight.at[1], diag.at[1]), 0)
        small[0].wait()
        live = live_rows(pos_ref, slots)
        for end, _ in ends:
            end[0] = mark_dead(end[0], live)

    @pl.when(chip != 0)
    def _():
        copies(q_ref, dg_ref, (wide.at[0], wide.at[1]), width)
        small[0].wait()
        for i, (end, _) in enumerate(ends):
            end[1] = wide[i].astype(BF16)

    small[1].wait()
    w_out[...] = w_ref[...].astype(F32).reshape(w_out.shape)


def cross_pack(route_pos, w_router, keys, values, queries, d_gated):
    _, slots, full = keys.shape
    cross = pltpu.VMEM((2, slots, full // 4), BF16)
    hbm = pl.BlockSpec(memory_space=pltpu.HBM)
    return pl.pallas_call(
        cross_pack_kernel,
        out_shape=[cross, cross, jax.ShapeDtypeStruct((1, w_router.shape[0]), F32)],
        in_specs=[hbm] * 6,
        out_specs=[VMEM] * 3,
        scratch_shapes=[
            pltpu.VMEM((2, slots, full // 4), F32),
            pltpu.VMEM(route_pos.shape, jnp.int32),
            pltpu.VMEM(w_router.shape, BF16),
            pltpu.SemaphoreType.DMA((6,)),
        ],
        compiler_params=params(),
        cost_estimate=cost(0, 10 * slots * full),
        name="cross_pack",
    )(*in_hbm(route_pos, w_router, keys, values, queries, d_gated))


def sib_pack_kernel(pos_ref, k_ref, v_ref, q_ref, dg_ref, out, wide, sems):
    slots, half = out.shape[1], out.shape[2]
    cols = pl.ds(pl.multiple_of((1 - here()[0]) * half, HEAD), half)
    sources = ((k_ref, out.at[0]), (dg_ref, wide), (v_ref, out.at[1]), (q_ref, out.at[2]))
    copies = [pltpu.make_async_copy(src.at[0, :, cols], dst, sems.at[i]) for i, (src, dst) in enumerate(sources)]
    for c in copies:
        c.start()
    live = live_rows(pos_ref, slots)
    copies[0].wait()
    out[0] = mark_dead(out[0], live)
    copies[1].wait()
    out[3] = wide[...].astype(BF16)
    copies[2].wait()
    copies[3].wait()


def sib_pack(route_pos, keys, values, queries, d_gated):
    _, slots, full = keys.shape
    hbm = pl.BlockSpec(memory_space=pltpu.HBM)
    return pl.pallas_call(
        sib_pack_kernel,
        out_shape=pltpu.VMEM((4, slots, full // 2), BF16),
        in_specs=[VMEM, hbm, hbm, hbm, hbm],
        out_specs=VMEM,
        scratch_shapes=[pltpu.VMEM((slots, full // 2), F32), pltpu.SemaphoreType.DMA((4,))],
        compiler_params=params(),
        cost_estimate=cost(0, 20 * slots * full),
        name="sib_pack",
    )(route_pos, *in_hbm(keys, values, queries, d_gated))


def pair_gate_kernel(parts, live_ref, rows_x, w_ref, local, stats, out_ref, message):
    chunk = w_ref.shape[1] // parts
    slots = rows_x.shape[1]
    for i in range(2):
        total = jnp.zeros((8, slots), F32)
        for j in range(parts):
            w_rows = jnp.broadcast_to(w_ref[:, j * chunk : (j + 1) * chunk], (8, chunk)).astype(BF16)
            cols = pl.ds(pl.multiple_of((lax.axis_index("dp") ^ j) * chunk, HEAD), chunk)
            total = total + nt(w_rows, rows_x[i, :, cols])
        lanes = slice(i * slots, (i + 1) * slots)
        out_ref[:, lanes] = live_ref[:, lanes] / (1.0 + jnp.exp(-total[0:1]))
    first = here()[1] == 0
    heads = stats.shape[1]
    for i in range(3):
        message[i] = jnp.where(first, stats[i], local[i, heads:])
    message[3] = jnp.broadcast_to(out_ref[...], message.shape[1:])


def pair_gate(live, rows_x, w_full, local, stats, parts):
    _, heads, lanes = stats.shape
    return pl.pallas_call(
        functools.partial(pair_gate_kernel, parts),
        out_shape=[jax.ShapeDtypeStruct(live.shape, F32), jax.ShapeDtypeStruct((4, heads, lanes), F32)],
        in_specs=[VMEM] * 5,
        out_specs=[VMEM] * 2,
        compiler_params=params(),
        cost_estimate=cost(16 * rows_x.size, rows_x.size * 2),
        name="router_gate",
    )(live, rows_x, w_full, local, stats)


def local_mask(core, pair):
    slots = pair.shape[1] // 2
    key = lax.broadcasted_iota(jnp.int32, (slots, slots), 0)
    query = lax.broadcasted_iota(jnp.int32, (slots, slots), 1)
    causal = key <= query
    own_live = pair[0, :slots, :slots].astype(F32) < MARK_LIMIT
    sib_live = pair[0, slots:, :slots].astype(F32) < MARK_LIMIT
    own_rows = jnp.concatenate([own_live & causal, own_live & (core == 0)], axis=1)
    sib_rows = jnp.concatenate([sib_live & (core == 1), sib_live & causal], axis=1)
    return jnp.concatenate([own_rows, sib_rows], axis=0)


def kept_stats(scores, gw, kept, stats, h):
    top = jnp.max(scores, axis=0, keepdims=True)
    e = jnp.exp(scores - top).astype(BF16)
    gw = gw.astype(BF16)
    kept[0, h] = e
    kept[1, h] = gw
    e = e.astype(F32)
    stats[0, h : h + 1] = top
    stats[1, h : h + 1] = jnp.sum(e, axis=0, keepdims=True)
    stats[2, h : h + 1] = jnp.sum(e * gw.astype(F32), axis=0, keepdims=True)


def partial_stats(scores, gw, stats, h):
    top = jnp.max(scores, axis=0, keepdims=True)
    e = jnp.exp(scores - top)
    stats[0, h : h + 1] = top
    stats[1, h : h + 1] = jnp.sum(e, axis=0, keepdims=True)
    stats[2, h : h + 1] = jnp.sum(e * gw, axis=0, keepdims=True)


def local_stats_kernel(scale, pos_ref, k_ref, v_ref, q_ref, dg_ref, sib, x_ref, x_sib, stats, live, near, far, rows_x, wide, sems, x_sems):
    slots, half = sib.shape[1], sib.shape[2]
    width = half // 2
    core = here()[0]
    own, other = slice(0, slots), slice(slots, 2 * slots)
    stages = []
    for g, pair in enumerate((near, far)):
        cols = slice(g * width, (g + 1) * width)
        held = pl.ds(pl.multiple_of(core * half + g * width, HEAD), width)
        copies = [
            pltpu.make_async_copy(ref.at[0, :, held], pair.at[j, own], sems.at[8 * g + j])
            for j, ref in enumerate((k_ref, v_ref, q_ref))
        ]
        copies.append(pltpu.make_async_copy(dg_ref.at[0, :, held], wide.at[:, cols], sems.at[8 * g + 3]))
        for j in range(4):
            copies.append(pltpu.make_async_copy(sib.at[j, :, cols], pair.at[j, other], sems.at[8 * g + 4 + j]))
        for c in copies:
            c.start()
        stages.append(copies)
    x_copies = []
    depth = x_ref.shape[2] // 2
    for i, ref in enumerate((x_ref, x_sib)):
        for g in range(2):
            cols = slice(g * depth, (g + 1) * depth)
            x_copies.append(pltpu.make_async_copy(ref.at[0, :, cols], rows_x.at[i, :, cols], x_sems.at[2 * i + g]))
    for c in x_copies:
        c.start()
    rows_live = live_rows(pos_ref, slots)
    mask = None
    for g, pair in enumerate((near, far)):
        cols = slice(g * width, (g + 1) * width)
        for c in stages[g]:
            c.wait()
        pair[0, own] = mark_dead(pair[0, own], rows_live)
        pair[3, own] = wide[:, cols].astype(BF16)
        if mask is None:
            mask = local_mask(core, pair)
            marks = nt(jnp.ones((8, HEAD), BF16), pair[0, :, :HEAD])[0:1]
            live[...] = jnp.where(marks < MARK_LIMIT, 1.0, 0.0)
        for h in range(width // HEAD):
            at = slice(h * HEAD, (h + 1) * HEAD)
            scores = jnp.where(mask, nt(pair[0, :, at], pair[2, :, at]) * scale, NEG_FILL)
            partial_stats(scores, nt(pair[1, :, at], pair[3, :, at]), stats, g * width // HEAD + h)
    for c in x_copies:
        c.wait()


def local_stats(route_pos, keys, values, queries, d_gated, sib, x_routed, x_sib):
    _, slots, half = sib.shape
    heads = half // HEAD
    anywhere = pl.BlockSpec(memory_space=pl.ANY)
    return pl.pallas_call(
        functools.partial(local_stats_kernel, HEAD**-0.5),
        out_shape=[
            jax.ShapeDtypeStruct((3, heads, 2 * slots), F32),
            jax.ShapeDtypeStruct((1, 2 * slots), F32),
            pltpu.VMEM((4, 2 * slots, half // 2), BF16),
            pltpu.VMEM((4, 2 * slots, half // 2), BF16),
            pltpu.VMEM((2, slots, x_routed.shape[2]), BF16),
        ],
        in_specs=[VMEM] + [anywhere] * 7,
        out_specs=[VMEM] * 5,
        scratch_shapes=[pltpu.VMEM((slots, half), F32), pltpu.SemaphoreType.DMA((16,)), pltpu.SemaphoreType.DMA((4,))],
        compiler_params=params(),
        cost_estimate=cost(16 * slots * slots * half, 16 * slots * half, 4 * slots * slots * half // HEAD),
        name="local_stats",
    )(route_pos, *in_hbm(keys, values, queries, d_gated), sib, x_routed, x_sib)


def cross_stats_kernel(scale, near, far, straight, diag, cross, stats, kept):
    slots, width = straight.shape[1], straight.shape[2]
    chip = here()[1]
    top, bottom = slice(0, slots), slice(slots, 2 * slots)

    @pl.when(chip == 0)
    def _():
        for part in range(2):
            cross[part] = far[part]
            cross[2 + part, top] = straight[part]
            cross[2 + part, bottom] = diag[part]

    @pl.when(chip != 0)
    def _():
        for part in range(2):
            cross[part, top] = straight[part]
            cross[part, bottom] = diag[part]
            cross[2 + part] = near[2 + part]

    live = cross[0, :, :HEAD].astype(F32) < MARK_LIMIT
    mask = jnp.concatenate([live] * (2 * slots // HEAD), axis=1)
    heads = width // HEAD
    for h in range(heads):
        cols = slice(h * HEAD, (h + 1) * HEAD)
        scores = jnp.where(mask, nt(cross[0, :, cols], cross[2, :, cols]) * scale, NEG_FILL)
        kept_stats(scores, nt(cross[1, :, cols], cross[3, :, cols]), kept, stats, h)


def cross_stats(near, far, straight, diag):
    _, slots, width = straight.shape
    heads = width // HEAD
    return pl.pallas_call(
        functools.partial(cross_stats_kernel, HEAD**-0.5),
        out_shape=[
            pltpu.VMEM((4, 2 * slots, width), BF16),
            jax.ShapeDtypeStruct((3, heads, 2 * slots), F32),
            pltpu.VMEM((2, heads, 2 * slots, 2 * slots), BF16),
        ],
        in_specs=[VMEM] * 4,
        out_specs=[VMEM] * 3,
        compiler_params=params(),
        cost_estimate=cost(16 * slots * slots * width, 32 * slots * width, 4 * slots * slots * heads),
        name="cross_stats",
    )(near, far, straight, diag)


NONE = (-3e38, 0.0, 0.0)


def merge(first, second):
    top = jnp.maximum(first[0], second[0])
    a, b = jnp.exp(first[0] - top), jnp.exp(second[0] - top)
    inverse = 1.0 / (first[1] * a + second[1] * b)
    return a * inverse, (first[2] * a + second[2] * b) * inverse


def choose(flag, yes, no):
    return [jnp.where(flag, y, n) for y, n in zip(yes, no)]


def gradients(q, k, dg, e, gw, scale, factor, delta):
    weights = e * factor
    ds = (weights * ((gw - delta) * scale)).astype(BF16)
    return tn(ds, k), nn(ds, q), nn(weights.astype(BF16), dg)


def local_gradients(pair, h, mask, scale, top, factor, delta):
    cols = slice(h * HEAD, (h + 1) * HEAD)
    k, v, q, dg = [pair[i, :, cols] for i in range(4)]
    e = jnp.exp(jnp.where(mask, nt(k, q) * scale, NEG_FILL) - top)
    return gradients(q, k, dg, e, nt(v, dg), scale, factor, delta)


def near_grad_kernel(scale, pair, local, stats, gates, dq_out, own_out, sib_out, sum_out):
    slots, width = own_out.shape[1], own_out.shape[2]
    heads = width // HEAD
    first = here()[1] == 0
    near = [local[i, :heads] for i in range(3)]
    factor, delta = merge(near, choose(first, NONE, [stats[i] for i in range(3)]))
    factor = factor * gates[...]
    sum_out[...] = jnp.sum(delta, axis=0, keepdims=True)
    mask = local_mask(here()[0], pair)
    for h in range(heads):
        cols = slice(h * HEAD, (h + 1) * HEAD)
        row = slice(h, h + 1)
        dq, dk, dv = local_gradients(pair, h, mask, scale, near[0][row], factor[row], delta[row])
        dq_out[:, cols] = dq
        for i, part in enumerate((dk, dv)):
            own_out[i, :, cols] = part[:slots].astype(BF16)
            sib_out[i, :, cols] = part[slots:].astype(BF16)


def near_grad(pair, local, stats, gates):
    _, rows, width = pair.shape
    slots = rows // 2
    out = pltpu.VMEM((2, slots, width), BF16)
    return pl.pallas_call(
        functools.partial(near_grad_kernel, HEAD**-0.5),
        out_shape=[pltpu.VMEM((2 * slots, width), F32), out, out, jax.ShapeDtypeStruct(gates.shape, F32)],
        in_specs=[VMEM] * 4,
        out_specs=[VMEM] * 4,
        compiler_params=params(),
        cost_estimate=cost(20 * slots * slots * width, 40 * slots * width),
        name="near_grad",
    )(pair, local, stats, gates)


def cross_grad_kernel(scale, cross, kept, stats, local, heard, gates, near_dq, near_sum, straight, diag, dq_out, keep, final, sum_out):
    slots, width = straight.shape[1], straight.shape[2]
    heads = width // HEAD
    first = here()[1] == 0
    late = jnp.where(first, 0.0, 1.0)
    mine = [stats[i] for i in range(3)]
    other = [heard[i] for i in range(3)]
    near = [local[i, :heads] for i in range(3)]
    far = [local[i, heads:] for i in range(3)]
    factor, delta = merge(mine, choose(first, other, near))
    factor = factor * jnp.where(first, heard[3], jnp.broadcast_to(gates[...], factor.shape))
    final[0], final[1] = merge(far, choose(first, NONE, other))
    sum_out[...] = near_sum[...] + jnp.sum(final[1], axis=0, keepdims=True)
    for h in range(heads):
        cols = slice(h * HEAD, (h + 1) * HEAD)
        row = slice(h, h + 1)
        dq, dk, dv = gradients(
            cross[2, :, cols], cross[0, :, cols], cross[3, :, cols],
            kept[0, h].astype(F32), kept[1, h].astype(F32), scale, factor[row], delta[row],
        )
        dq_out[:, cols] = (near_dq[:, cols] + late * dq).astype(BF16)
        keep[0, :, cols] = dk.astype(BF16)
        keep[1, :, cols] = dv.astype(BF16)
        sent = jnp.where(first, dq, dk).astype(BF16)
        straight[0, :, cols] = sent[:slots]
        diag[0, :, cols] = sent[slots:]
        straight[1, :, cols] = dv[:slots].astype(BF16)
        diag[1, :, cols] = dv[slots:].astype(BF16)


def cross_grad(cross, kept, stats, local, heard, gates, near_dq, near_sum):
    _, rows, width = cross.shape
    slots = rows // 2
    out = pltpu.VMEM((2, slots, width), BF16)
    return pl.pallas_call(
        functools.partial(cross_grad_kernel, HEAD**-0.5),
        out_shape=[
            out,
            out,
            pltpu.VMEM((rows, width), BF16),
            pltpu.VMEM((2, rows, width), BF16),
            jax.ShapeDtypeStruct((2, width // HEAD, rows), F32),
            jax.ShapeDtypeStruct((1, rows), F32),
        ],
        in_specs=[VMEM] * 8,
        out_specs=[VMEM] * 6,
        compiler_params=params(),
        cost_estimate=cost(24 * slots * slots * width, 64 * slots * width),
        name="cross_grad",
    )(cross, kept, stats, local, heard, gates, near_dq, near_sum)


def far_grad_kernel(scale, pair, local, final, gates, keep, near_dq, near_own, near_sib, own_out, sib_out):
    slots, width = pair.shape[1] // 2, pair.shape[2]
    heads = width // HEAD
    early = jnp.where(here()[1] == 0, 1.0, 0.0)
    factor = final[0] * gates[...]
    mask = local_mask(here()[0], pair)
    own_out[0, :, :width] = near_dq[:slots]
    sib_out[0, :, :width] = near_dq[slots:]
    for i in range(2):
        own_out[1 + i, :, :width] = near_own[i]
        sib_out[1 + i, :, :width] = near_sib[i]
    for h in range(heads):
        cols = slice(width + h * HEAD, width + (h + 1) * HEAD)
        at = slice(h * HEAD, (h + 1) * HEAD)
        row = slice(h, h + 1)
        top = local[0, heads + h : heads + h + 1]
        dq, dk, dv = local_gradients(pair, h, mask, scale, top, factor[row], final[1, row])
        dk = dk + early * keep[0, :, at].astype(F32)
        dv = dv + early * keep[1, :, at].astype(F32)
        for i, part in enumerate((dq, dk, dv)):
            own_out[i, :, cols] = part[:slots].astype(BF16)
            sib_out[i, :, cols] = part[slots:].astype(BF16)


def far_grad(pair, local, final, gates, keep, near_dq, near_own, near_sib):
    _, rows, width = pair.shape
    slots, half = rows // 2, 2 * width
    out = jax.ShapeDtypeStruct((3, slots, half), BF16)
    return pl.pallas_call(
        functools.partial(far_grad_kernel, HEAD**-0.5),
        out_shape=[out, out],
        in_specs=[VMEM] * 8,
        out_specs=[VMEM] * 2,
        compiler_params=params(),
        cost_estimate=cost(20 * slots * slots * half, 40 * slots * half),
        name="far_grad",
    )(pair, local, final, gates, keep, near_dq, near_own, near_sib)


def own_join_kernel(own, dq_out, dk_out, dv_out, waiting, total, sems):
    slots, half = own.shape[1], own.shape[2]
    width = half // 2
    core, chip = here()
    cols = pl.ds(pl.multiple_of(core * half, HEAD), half)
    stores = []
    for j, out in enumerate((dq_out, dk_out, dv_out)):
        total[j] = own[j].astype(F32)
        stores.append(pltpu.make_async_copy(total.at[j], out.at[0, :, cols], sems.at[j]))
        stores[-1].start()
    waiting[0] = jnp.where(chip == 0, total[1, :, :width], total[0, :, width:]).astype(BF16)
    waiting[1] = own[2, :, :width]
    for c in stores:
        c.wait()


def own_join(own, shape):
    out = pltpu.HBM(shape, F32)
    _, slots, half = own.shape
    hbm = pl.BlockSpec(memory_space=pltpu.HBM)
    return pl.pallas_call(
        own_join_kernel,
        out_shape=[out] * 3 + [jax.ShapeDtypeStruct((2, slots, half // 2), BF16)],
        in_specs=[VMEM],
        out_specs=[hbm] * 3 + [VMEM],
        scratch_shapes=[pltpu.VMEM((3, slots, half), F32), pltpu.SemaphoreType.DMA((3,))],
        compiler_params=params(),
        cost_estimate=cost(0, 18 * own.size),
        name="own_join",
    )(own)


def finish_kernel(waiting, sib, straight, diag, dq_in, dk_in, dv_in, dq_out, dk_out, dv_out, low, held, total, added, in_sems, out_sems):
    half = sib.shape[2]
    width = half // 2
    core, chip = here()
    early, late = jnp.where(chip == 0, 1.0, 0.0), jnp.where(chip == 0, 0.0, 1.0)
    loads = [pltpu.make_async_copy(sib.at[j], low.at[j], in_sems.at[j]) for j in range(3)]
    loads += [pltpu.make_async_copy(waiting.at[j], held.at[j], in_sems.at[3 + j]) for j in range(2)]
    for c in loads:
        c.start()
    cols = pl.ds(pl.multiple_of((1 - core) * half, HEAD), half)
    stores = []
    for j, out in enumerate((dq_out, dk_out, dv_out)):
        loads[j].wait()
        first, second = low[j, :, :width].astype(F32), low[j, :, width:].astype(F32)
        if j == 0:
            second = second + late * diag[0].astype(F32)
        else:
            first = first + early * diag[j - 1].astype(F32)
        total[j, :, :width] = first
        total[j, :, width:] = second
        stores.append(pltpu.make_async_copy(total.at[j], out.at[0, :, cols], out_sems.at[j]))
        stores[-1].start()
    for j in range(2):
        loads[3 + j].wait()
        added[j] = held[j].astype(F32) + straight[j].astype(F32)

    def store(j, out, offset):
        at = pl.ds(pl.multiple_of(core * half + offset, HEAD), width)
        copy = pltpu.make_async_copy(added.at[j], out.at[0, :, at], out_sems.at[3 + j])
        copy.start()
        return copy

    @pl.when(chip == 0)
    def _():
        copies = [store(0, dk_out, 0), store(1, dv_out, 0)]
        for c in copies:
            c.wait()

    @pl.when(chip != 0)
    def _():
        store(0, dq_out, width).wait()

    for c in stores:
        c.wait()


def finish(waiting, sib, straight, diag, outs):
    _, slots, half = sib.shape
    hbm = pl.BlockSpec(memory_space=pltpu.HBM)
    anywhere = pl.BlockSpec(memory_space=pl.ANY)
    return pl.pallas_call(
        finish_kernel,
        out_shape=[pltpu.HBM(o.shape, F32) for o in outs],
        in_specs=[anywhere] * 2 + [VMEM] * 2 + [hbm] * 3,
        out_specs=[hbm] * 3,
        scratch_shapes=[
            pltpu.VMEM((3, slots, half), BF16),
            pltpu.VMEM(waiting.shape, BF16),
            pltpu.VMEM((3, slots, half), F32),
            pltpu.VMEM(waiting.shape, F32),
            pltpu.SemaphoreType.DMA((5,)),
            pltpu.SemaphoreType.DMA((5,)),
        ],
        input_output_aliases={4: 0, 5: 1, 6: 2},
        compiler_params=params(),
        cost_estimate=cost(0, 12 * sib.size),
        name="finish",
    )(waiting, sib, straight, diag, *in_hbm(*outs))


def pair_router_kernel(gates_ref, sum_ref, rows_x, out_ref):
    gates = gates_ref[...]
    grad = sum_ref[...] * gates * (1.0 - gates)
    high = grad.astype(BF16)
    rest = grad - high.astype(F32)
    mid = rest.astype(BF16)
    low = (rest - mid.astype(F32)).astype(BF16)
    slots = rows_x.shape[1]
    row = lax.broadcasted_iota(jnp.int32, (8, grad.shape[1]), 0)
    lhs = jnp.where(row == 0, high.astype(F32), jnp.where(row == 1, mid.astype(F32), jnp.where(row == 2, low.astype(F32), 0.0)))
    lhs = lhs.astype(BF16)
    term = jnp.sum(nn(lhs[:, :slots], rows_x[0]) + nn(lhs[:, slots:], rows_x[1]), axis=0, keepdims=True)
    parts, copies, _, chunk = out_ref.shape
    for j in range(parts):
        for i in range(copies):
            out_ref[j, i] = term[:, j * chunk : (j + 1) * chunk]


def pair_router(gates, sums, rows_x, parts, copies):
    chunk = rows_x.shape[-1] // parts
    return pl.pallas_call(
        pair_router_kernel,
        out_shape=jax.ShapeDtypeStruct((parts, copies, 1, chunk), F32),
        in_specs=[VMEM] * 3,
        out_specs=VMEM,
        compiler_params=params(),
        cost_estimate=cost(32 * rows_x.size, rows_x.size * 4),
        name="router_terms",
    )(gates, sums, rows_x)


def swap_body(route_pos, x_routed, w_router, queries, keys, values, d_gated):
    slots = queries.shape[1]
    n, ndp = lax.axis_size("ctx"), lax.axis_size("dp")

    def send(a, flip):
        return lax.ppermute(a, "ctx", [(i, i ^ flip) for i in range(n)])

    def beside(fn, *operands):
        def skip(*ops):
            return jax.tree.map(lambda o: jnp.zeros(o.shape, o.dtype), jax.eval_shape(fn, *ops))

        return lax.cond(route_pos[0, 0] >= -1, fn, skip, *operands)

    def after(value, *others):
        return lax.optimization_barrier((value, *others))[0]

    def widen(part, step, *first):
        other = lax.ppermute(part, "dp", [(i, i ^ step) for i in range(ndp)])
        return jnp.concatenate([part, after(other, *first)], axis=1)

    def exchange_phase(x_routed, w_part, theirs):
        sib, x_sib = send(theirs, 1), send(x_routed, 1)
        step = 2
        while 2 * step < ndp:
            w_part = widen(w_part, step)
            step *= 2
        return sib, x_sib, w_part

    def far_phase(*operands):
        own_out, sib_out = far_grad(*operands)
        sib_in = send(sib_out, 1)
        *outs, waiting = own_join(own_out, queries.shape)
        return outs, waiting, sib_in

    out_s, out_d, w_part = cross_pack(route_pos, w_router, keys, values, queries, d_gated)
    in_s, in_d = send(out_s, 2), send(out_d, 3)

    theirs = sib_pack(after(route_pos, out_s), keys, values, queries, d_gated)
    if ndp > 1:
        w_part = widen(w_part, 1, theirs)
    sib, x_sib, w_part = beside(exchange_phase, x_routed, w_part, theirs)
    local, live, near, far, rows_x = local_stats(route_pos, keys, values, queries, d_gated, sib, x_routed, x_sib)
    cross, stats, kept = cross_stats(near, far, in_s, in_d)
    if ndp > 2:
        w_part = widen(w_part, ndp // 2, stats)
    gates, message = pair_gate(live, rows_x, w_part, local, stats, ndp)

    heard = send(message, 2)
    near_dq, near_own, near_sib, near_sum = near_grad(near, local, stats, gates)
    back_s, back_d, dq_low, keep, final, sums = cross_grad(
        cross, kept, stats, local, heard, gates, near_dq, near_sum
    )

    ret_s, ret_d = send(back_s, 2), send(back_d, 3)
    terms = pair_router(gates, sums, rows_x, ndp, n)
    shared = lax.all_to_all(terms.reshape(ndp * n, 1, -1), ("dp", "ctx"), 0, 0, tiled=True)
    outs, waiting, sib_in = beside(far_phase, far, local, final, gates, keep, dq_low, near_own, near_sib)
    dq, dk, dv = finish(waiting, sib_in, ret_s, ret_d, outs)
    router_grad = jnp.sum(after(shared, dq), axis=0)[0] / float(ndp * n * slots // 2)
    return dq, dk, dv, router_grad


def body(route_pos, x_routed, w_router, queries, keys, values, d_gated):
    slots, full = queries.shape[1], queries.shape[2]
    n, ndp = lax.axis_size("ctx"), lax.axis_size("dp")
    chips = n // 2
    me, dp_me = lax.axis_index("ctx"), lax.axis_index("dp")
    core = (me % 2).astype(jnp.int32).reshape(1)
    half = full // 2
    groups = GROUPS if (half // HEAD) % GROUPS == 0 else 1
    width = half // groups

    sib_pairs = [(i, i ^ 1) for i in range(n)]

    def forward_pairs(step, flip):
        return [(i, (i + 2 * step) ^ flip) for i in range(n) if i + 2 * step < n]

    def back_pairs(step, flip):
        return [(b, a) for a, b in forward_pairs(step, flip)]

    def to_sib(a):
        return lax.ppermute(a, "ctx", sib_pairs)

    links = [(step, flip) for step in range(1, chips) for flip in (0, 1)]

    w_row = w_router.reshape(1, -1)
    w_parts = [w_row] + [
        lax.ppermute(w_row, "dp", [(i, (i + s) % ndp) for i in range(ndp)]) for s in range(1, ndp)
    ]
    live = (route_pos >= 0).astype(jnp.int32)
    lives = [live, to_sib(live)] + [lax.ppermute(live, "ctx", forward_pairs(*link)) for link in links]
    live_all = jnp.concatenate(lives, axis=0)

    kv_mine, kv_theirs = pack(core, keys, values, groups, width)
    kv_far = [
        [lax.ppermute((kv_theirs if flip else kv_mine)[g], "ctx", forward_pairs(step, flip)) for step, flip in links]
        for g in range(groups)
    ]
    q_mine, q_theirs = pack(core, queries, d_gated, groups, width)
    kv_sib = [to_sib(a) for a in kv_theirs]
    q_sib = [to_sib(a) for a in q_theirs]

    offsets = ((dp_me - jnp.arange(ndp)) % ndp).astype(jnp.int32)
    gate = router_gate(offsets, route_pos, x_routed, w_parts)
    gates = (gate, to_sib(gate))

    accs = (jnp.zeros((1, slots), F32), jnp.zeros((1, slots), F32))
    dq_own, sib_in, kv_own, back = [], [], [], []
    for g in range(groups):
        dq, sib_out, kv_local, kv_remote, accs = attention(
            core, live_all, gates, accs, q_mine[g], q_sib[g], [kv_mine[g], kv_sib[g], *kv_far[g]]
        )
        back.append([lax.ppermute(a, "ctx", back_pairs(*link)) for a, link in zip(kv_remote, links)])
        sib_in.append(to_sib(sib_out))
        dq_own.append(dq)
        kv_own.append(kv_local)

    targets = ((dp_me + jnp.arange(ndp)) % ndp).astype(jnp.int32)
    terms = router_terms(targets, gate, accs[0], to_sib(accs[1]), x_routed, ndp)
    mine = terms[0]
    for s in range(1, ndp):
        mine = mine + lax.ppermute(terms[s], "dp", [(i, (i + s) % ndp) for i in range(ndp)])
    total = mine
    for s in range(1, n):
        total = total + lax.ppermute(mine, "ctx", [(i, (i + s) % n) for i in range(n)])
    router_grad = total[0] / float(ndp * n * slots // 2)

    dq, dk, dv = combine(core, dq_own, sib_in, kv_own, back, queries.shape)
    return dq, dk, dv, router_grad


def solution(mesh):
    placed = (
        P("dp", "ctx"),
        P("dp", "ctx", None),
        P("dp"),
        P("dp", "ctx", None),
        P("dp", "ctx", None),
        P("dp", "ctx", None),
        P("dp", "ctx", None),
    )
    ndp = mesh.shape["dp"]
    paired = mesh.shape["ctx"] == 4 and ndp & (ndp - 1) == 0
    return jax.shard_map(
        swap_body if paired else body,
        mesh=mesh,
        in_specs=placed,
        out_specs=(P("dp", "ctx", None), P("dp", "ctx", None), P("dp", "ctx", None), P("dp")),
        check_vma=False,
    )
```

```python
import functools

import jax
import jax.numpy as jnp
from jax import lax
from jax.experimental import pallas as pl
from jax.experimental.pallas import tpu as pltpu
from jax.sharding import PartitionSpec as P

HEAD = 128
GROUPS = 4
NEG_FILL = -1e30
MIB = 1024 * 1024
BF16 = jnp.bfloat16
F32 = jnp.float32

VMEM = pl.BlockSpec(memory_space=pltpu.VMEM)
SMEM = pl.BlockSpec(memory_space=pltpu.SMEM)


def params(mib=16):
    return pltpu.CompilerParams(vmem_limit_bytes=mib * MIB)


def cost(flops, nbytes, exps=0):
    return pl.CostEstimate(flops=1, bytes_accessed=1, transcendentals=0)


def in_hbm(*arrays):
    return [pltpu.with_memory_space_constraint(a, pltpu.HBM) for a in arrays]


def nt(a, b):
    return lax.dot_general(a, b, (((1,), (1,)), ((), ())), preferred_element_type=F32)


def nn(a, b):
    return lax.dot_general(a, b, (((1,), (0,)), ((), ())), preferred_element_type=F32)


def tn(a, b):
    return lax.dot_general(a, b, (((0,), (0,)), ((), ())), preferred_element_type=F32)


def pack_kernel(groups, width, core_ref, first_ref, second_ref, *outs):
    half = first_ref.shape[-1] // 2
    core = core_ref[0]
    for side in range(2):
        base = (core if side == 0 else 1 - core) * half
        for g in range(groups):
            out = outs[side * groups + g]
            cols = pl.ds(pl.multiple_of(base + g * width, HEAD), width)
            out[0] = first_ref[0, :, cols].astype(BF16)
            out[1] = second_ref[0, :, cols].astype(BF16)


def pack(core, first, second, groups, width):
    slots = first.shape[1]
    out = jax.ShapeDtypeStruct((2, slots, width), BF16)
    res = pl.pallas_call(
        functools.partial(pack_kernel, groups, width),
        out_shape=[out] * (2 * groups),
        in_specs=[SMEM, VMEM, VMEM],
        out_specs=[VMEM] * (2 * groups),
        compiler_params=params(),
        cost_estimate=cost(0, 2 * first.size * 4),
        name="pack",
    )(core, first, second)
    return res[:groups], res[groups:]


def gate_kernel(parts, offset_ref, pos_ref, x_ref, *refs):
    w_refs, out_ref = refs[:parts], refs[parts]
    chunk = w_refs[0].shape[-1]
    total = jnp.zeros((8, x_ref.shape[1]), F32)
    for s in range(parts):
        cols = pl.ds(pl.multiple_of(offset_ref[s] * chunk, HEAD), chunk)
        w_rows = jnp.broadcast_to(w_refs[s][...].astype(F32), (8, chunk)).astype(BF16)
        total = total + nt(w_rows, x_ref[0, :, cols])
    gate = 1.0 / (1.0 + jnp.exp(-total[0:1]))
    out_ref[...] = jnp.where(pos_ref[...] >= 0, gate, 0.0)


def router_gate(offsets, route_pos, x_routed, w_parts):
    parts = len(w_parts)
    return pl.pallas_call(
        functools.partial(gate_kernel, parts),
        out_shape=jax.ShapeDtypeStruct(route_pos.shape, F32),
        in_specs=[SMEM] + [VMEM] * (2 + parts),
        out_specs=VMEM,
        compiler_params=params(),
        cost_estimate=cost(16 * x_routed.size, x_routed.size * 2),
        name="router_gate",
    )(offsets, route_pos, x_routed, *w_parts)


def attention_kernel(remote, scale, core_ref, live_ref, gate_own, gate_sib, acc_own, acc_sib, q_own, q_sib, *refs):
    chunks = 2 + remote
    kv = refs[:chunks]
    outs = refs[chunks:]
    dq_own, sib_out, kv_own = outs[:3]
    kv_remote = outs[3 : 3 + remote]
    sum_own, sum_sib = outs[3 + remote :]
    slots, width = q_own.shape[1], q_own.shape[2]
    core = core_ref[0]
    key = lax.broadcasted_iota(jnp.int32, (slots, slots), 0)
    query = lax.broadcasted_iota(jnp.int32, (slots, slots), 1)
    counts = [jnp.sum(live_ref[i : i + 1], axis=1, keepdims=True) for i in range(chunks)]
    lives = [key < counts[i] for i in range(chunks)]
    own_later = core == 1
    bias_rows = []
    for i in range(chunks):
        live = lives[i]
        if i == 0:
            pair = (live & (key <= query), live & jnp.logical_not(own_later))
        elif i == 1:
            pair = (live & own_later, live & (key <= query))
        else:
            pair = (live, live)
        bias_rows.append(jnp.concatenate([jnp.where(p, 0.0, NEG_FILL) for p in pair], axis=1))
    bias = jnp.concatenate(bias_rows, axis=0)
    gates = jnp.concatenate([gate_own[...], gate_sib[...]], axis=1)
    total = jnp.zeros((1, 2 * slots), F32)
    for h in range(width // HEAD):
        cols = slice(h * HEAD, (h + 1) * HEAD)
        q = jnp.concatenate([q_own[0, :, cols], q_sib[0, :, cols]], axis=0)
        dg = jnp.concatenate([q_own[1, :, cols], q_sib[1, :, cols]], axis=0)
        k = jnp.concatenate([r[0, :, cols] for r in kv], axis=0)
        v = jnp.concatenate([r[1, :, cols] for r in kv], axis=0)
        scores = nt(k, q) * scale + bias
        top = jnp.max(scores, axis=0, keepdims=True)
        e = jnp.exp(scores - top)
        inverse = 1.0 / jnp.sum(e, axis=0, keepdims=True)
        gw = nt(v, dg)
        delta = jnp.sum(e * gw, axis=0, keepdims=True) * inverse
        total = total + delta
        weights = e * (inverse * gates)
        dv = nn(weights.astype(BF16), dg)
        ds = (weights * ((gw - delta) * scale)).astype(BF16)
        dk = nn(ds, q)
        dq = tn(ds, k)
        dq_own[:, cols] = dq[:slots].astype(dq_own.dtype)
        sib_out[0, :, cols] = dq[slots:].astype(BF16)
        kv_own[0, :, cols] = dk[:slots].astype(BF16)
        kv_own[1, :, cols] = dv[:slots].astype(BF16)
        sib_out[1, :, cols] = dk[slots : 2 * slots].astype(BF16)
        sib_out[2, :, cols] = dv[slots : 2 * slots].astype(BF16)
        for i in range(remote):
            rows = slice((2 + i) * slots, (3 + i) * slots)
            kv_remote[i][0, :, cols] = dk[rows].astype(BF16)
            kv_remote[i][1, :, cols] = dv[rows].astype(BF16)
    sum_own[...] = acc_own[...] + total[:, :slots]
    sum_sib[...] = acc_sib[...] + total[:, slots:]


def attention(core, live, gates, accs, q_own, q_sib, kv):
    remote = len(kv) - 2
    _, slots, width = q_own.shape
    pair = jax.ShapeDtypeStruct((2, slots, width), BF16)
    row = jax.ShapeDtypeStruct((1, slots), F32)
    outs = [
        jax.ShapeDtypeStruct((slots, width), BF16),
        jax.ShapeDtypeStruct((3, slots, width), BF16),
        pair,
        *([pair] * remote),
        row,
        row,
    ]
    keys = (2 + remote) * slots
    res = pl.pallas_call(
        functools.partial(attention_kernel, remote, HEAD**-0.5),
        out_shape=outs,
        in_specs=[SMEM] + [VMEM] * (7 + len(kv)),
        out_specs=[VMEM] * len(outs),
        compiler_params=params(48),
        cost_estimate=cost(20 * slots * keys * width, 8 * keys * width + 20 * slots * width, 2 * slots * keys * width // HEAD),
        name="attention",
    )(core, live, *gates, *accs, q_own, q_sib, *kv)
    return res[0], res[1], res[2], res[3 : 3 + remote], (res[3 + remote], res[4 + remote])


def combine_kernel(groups, width, remote, core_ref, *refs):
    dq_own, sib, kv_own = refs[:groups], refs[groups : 2 * groups], refs[2 * groups : 3 * groups]
    back = refs[3 * groups : 3 * groups + groups * remote]
    dq_out, dk_out, dv_out = refs[3 * groups + groups * remote :]
    half = groups * width
    core = core_ref[0]
    for g in range(groups):
        own = pl.ds(pl.multiple_of(core * half + g * width, HEAD), width)
        other = pl.ds(pl.multiple_of((1 - core) * half + g * width, HEAD), width)
        dq_out[0, :, own] = dq_own[g][...].astype(F32)
        dq_out[0, :, other] = sib[g][0].astype(F32)
        for i, out in enumerate((dk_out, dv_out)):
            mine = kv_own[g][i].astype(F32)
            theirs = sib[g][1 + i].astype(F32)
            for r in range(remote):
                part = back[g * remote + r][i].astype(F32)
                if r % 2 == 0:
                    mine = mine + part
                else:
                    theirs = theirs + part
            out[0, :, own] = mine
            out[0, :, other] = theirs


def combine(core, dq_own, sib, kv_own, back, shape):
    groups = len(dq_own)
    remote = len(back[0])
    out = jax.ShapeDtypeStruct(shape, F32)
    flat = [*dq_own, *sib, *kv_own, *(b for group in back for b in group)]
    return pl.pallas_call(
        functools.partial(combine_kernel, groups, dq_own[0].shape[-1], remote),
        out_shape=[out] * 3,
        in_specs=[SMEM] + [VMEM] * len(flat),
        out_specs=[VMEM] * 3,
        compiler_params=params(48),
        cost_estimate=cost(0, 3 * out.size * 6),
        name="combine",
    )(core, *flat)


def router_kernel(parts, target_ref, gate_ref, own_ref, sib_ref, x_ref, *outs):
    gate = gate_ref[...]
    grad = (own_ref[...] + sib_ref[...]) * gate * (1.0 - gate)
    high = grad.astype(BF16)
    rest = grad - high.astype(F32)
    mid = rest.astype(BF16)
    low = (rest - mid.astype(F32)).astype(BF16)
    row = lax.broadcasted_iota(jnp.int32, (8, grad.shape[1]), 0)
    lhs = jnp.where(row == 0, high.astype(F32), jnp.where(row == 1, mid.astype(F32), jnp.where(row == 2, low.astype(F32), 0.0)))
    lhs = lhs.astype(BF16)
    chunk = outs[0].shape[-1]
    for s in range(parts):
        cols = pl.ds(pl.multiple_of(target_ref[s] * chunk, HEAD), chunk)
        outs[s][...] = jnp.sum(nn(lhs, x_ref[0, :, cols]), axis=0, keepdims=True)


def router_terms(targets, gate, own, sib, x_routed, parts):
    chunk = x_routed.shape[-1] // parts
    return pl.pallas_call(
        functools.partial(router_kernel, parts),
        out_shape=[jax.ShapeDtypeStruct((1, chunk), F32)] * parts,
        in_specs=[SMEM] + [VMEM] * 4,
        out_specs=[VMEM] * parts,
        compiler_params=params(),
        cost_estimate=cost(16 * x_routed.size, x_routed.size * 2),
        name="router_terms",
    )(targets, gate, own, sib, x_routed)


def here():
    me = lax.axis_index("ctx")
    return lax.rem(me, 2), lax.div(me, 2)


MARK = 2.0**60
MARK_LIMIT = 2.0**50


def live_rows(pos_ref, slots):
    count = jnp.sum((pos_ref[...] >= 0).astype(jnp.int32), axis=1, keepdims=True)
    return lax.broadcasted_iota(jnp.int32, (slots, HEAD), 0) < count


def mark_dead(keys, live):
    width = keys.shape[-1]
    mask = jnp.concatenate([live] * (width // HEAD), axis=1)
    return jnp.where(mask, keys.astype(F32), MARK).astype(BF16)


def cross_pack_kernel(pos_any, w_any, k_ref, v_ref, q_ref, dg_ref, straight, diag, w_out, wide, pos_ref, w_ref, sems):
    small = [pltpu.make_async_copy(pos_any, pos_ref, sems.at[4]), pltpu.make_async_copy(w_any, w_ref, sems.at[5])]
    for c in small:
        c.start()
    slots, width = straight.shape[1], straight.shape[2]
    half = k_ref.shape[-1] // 2
    core, chip = here()
    ends = ((straight, core * half), (diag, (1 - core) * half))

    def copies(first, second, targets, offset):
        out = []
        for i, (end, start) in enumerate(ends):
            cols = pl.ds(pl.multiple_of(start + offset, HEAD), width)
            out.append(pltpu.make_async_copy(first.at[0, :, cols], end.at[0], sems.at[2 * i]))
            out.append(pltpu.make_async_copy(second.at[0, :, cols], targets[i], sems.at[2 * i + 1]))
        for c in out:
            c.start()
        for c in out:
            c.wait()

    @pl.when(chip == 0)
    def _():
        copies(k_ref, v_ref, (straight.at[1], diag.at[1]), 0)
        small[0].wait()
        live = live_rows(pos_ref, slots)
        for end, _ in ends:
            end[0] = mark_dead(end[0], live)

    @pl.when(chip != 0)
    def _():
        copies(q_ref, dg_ref, (wide.at[0], wide.at[1]), width)
        small[0].wait()
        for i, (end, _) in enumerate(ends):
            end[1] = wide[i].astype(BF16)

    small[1].wait()
    w_out[...] = w_ref[...].astype(F32).reshape(w_out.shape)


def cross_pack(route_pos, w_router, keys, values, queries, d_gated):
    _, slots, full = keys.shape
    cross = pltpu.VMEM((2, slots, full // 4), BF16)
    hbm = pl.BlockSpec(memory_space=pltpu.HBM)
    return pl.pallas_call(
        cross_pack_kernel,
        out_shape=[cross, cross, jax.ShapeDtypeStruct((1, w_router.shape[0]), F32)],
        in_specs=[hbm] * 6,
        out_specs=[VMEM] * 3,
        scratch_shapes=[
            pltpu.VMEM((2, slots, full // 4), F32),
            pltpu.VMEM(route_pos.shape, jnp.int32),
            pltpu.VMEM(w_router.shape, BF16),
            pltpu.SemaphoreType.DMA((6,)),
        ],
        compiler_params=params(),
        cost_estimate=cost(0, 10 * slots * full),
        name="cross_pack",
    )(*in_hbm(route_pos, w_router, keys, values, queries, d_gated))


def sib_pack_kernel(pos_ref, k_ref, v_ref, q_ref, dg_ref, out, wide, sems):
    slots, half = out.shape[1], out.shape[2]
    cols = pl.ds(pl.multiple_of((1 - here()[0]) * half, HEAD), half)
    sources = ((k_ref, out.at[0]), (dg_ref, wide), (v_ref, out.at[1]), (q_ref, out.at[2]))
    copies = [pltpu.make_async_copy(src.at[0, :, cols], dst, sems.at[i]) for i, (src, dst) in enumerate(sources)]
    for c in copies:
        c.start()
    live = live_rows(pos_ref, slots)
    copies[0].wait()
    out[0] = mark_dead(out[0], live)
    copies[1].wait()
    out[3] = wide[...].astype(BF16)
    copies[2].wait()
    copies[3].wait()


def sib_pack(route_pos, keys, values, queries, d_gated):
    _, slots, full = keys.shape
    hbm = pl.BlockSpec(memory_space=pltpu.HBM)
    return pl.pallas_call(
        sib_pack_kernel,
        out_shape=pltpu.VMEM((4, slots, full // 2), BF16),
        in_specs=[VMEM, hbm, hbm, hbm, hbm],
        out_specs=VMEM,
        scratch_shapes=[pltpu.VMEM((slots, full // 2), F32), pltpu.SemaphoreType.DMA((4,))],
        compiler_params=params(),
        cost_estimate=cost(0, 20 * slots * full),
        name="sib_pack",
    )(route_pos, *in_hbm(keys, values, queries, d_gated))


def pair_gate_kernel(parts, live_ref, rows_x, w_ref, local, stats, out_ref, message):
    chunk = w_ref.shape[1] // parts
    slots = rows_x.shape[1]
    for i in range(2):
        total = jnp.zeros((8, slots), F32)
        for j in range(parts):
            w_rows = jnp.broadcast_to(w_ref[:, j * chunk : (j + 1) * chunk], (8, chunk)).astype(BF16)
            cols = pl.ds(pl.multiple_of((lax.axis_index("dp") ^ j) * chunk, HEAD), chunk)
            total = total + nt(w_rows, rows_x[i, :, cols])
        lanes = slice(i * slots, (i + 1) * slots)
        out_ref[:, lanes] = live_ref[:, lanes] / (1.0 + jnp.exp(-total[0:1]))
    first = here()[1] == 0
    heads = stats.shape[1]
    for i in range(3):
        message[i] = jnp.where(first, stats[i], local[i, heads:])
    message[3] = jnp.broadcast_to(out_ref[...], message.shape[1:])


def pair_gate(live, rows_x, w_full, local, stats, parts):
    _, heads, lanes = stats.shape
    return pl.pallas_call(
        functools.partial(pair_gate_kernel, parts),
        out_shape=[jax.ShapeDtypeStruct(live.shape, F32), jax.ShapeDtypeStruct((4, heads, lanes), F32)],
        in_specs=[VMEM] * 5,
        out_specs=[VMEM] * 2,
        compiler_params=params(),
        cost_estimate=cost(16 * rows_x.size, rows_x.size * 2),
        name="router_gate",
    )(live, rows_x, w_full, local, stats)


def local_mask(core, pair):
    slots = pair.shape[1] // 2
    key = lax.broadcasted_iota(jnp.int32, (slots, slots), 0)
    query = lax.broadcasted_iota(jnp.int32, (slots, slots), 1)
    causal = key <= query
    own_live = pair[0, :slots, :slots].astype(F32) < MARK_LIMIT
    sib_live = pair[0, slots:, :slots].astype(F32) < MARK_LIMIT
    own_rows = jnp.concatenate([own_live & causal, own_live & (core == 0)], axis=1)
    sib_rows = jnp.concatenate([sib_live & (core == 1), sib_live & causal], axis=1)
    return jnp.concatenate([own_rows, sib_rows], axis=0)


def kept_stats(scores, gw, kept, stats, h):
    top = jnp.max(scores, axis=0, keepdims=True)
    e = jnp.exp(scores - top).astype(BF16)
    gw = gw.astype(BF16)
    kept[0, h] = e
    kept[1, h] = gw
    e = e.astype(F32)
    stats[0, h : h + 1] = top
    stats[1, h : h + 1] = jnp.sum(e, axis=0, keepdims=True)
    stats[2, h : h + 1] = jnp.sum(e * gw.astype(F32), axis=0, keepdims=True)


def partial_stats(scores, gw, stats, h):
    top = jnp.max(scores, axis=0, keepdims=True)
    e = jnp.exp(scores - top)
    stats[0, h : h + 1] = top
    stats[1, h : h + 1] = jnp.sum(e, axis=0, keepdims=True)
    stats[2, h : h + 1] = jnp.sum(e * gw, axis=0, keepdims=True)


def local_stats_kernel(scale, pos_ref, k_ref, v_ref, q_ref, dg_ref, sib, x_ref, x_sib, stats, live, near, far, rows_x, wide, sems, x_sems):
    slots, half = sib.shape[1], sib.shape[2]
    width = half // 2
    core = here()[0]
    own, other = slice(0, slots), slice(slots, 2 * slots)
    stages = []
    for g, pair in enumerate((near, far)):
        cols = slice(g * width, (g + 1) * width)
        held = pl.ds(pl.multiple_of(core * half + g * width, HEAD), width)
        copies = [
            pltpu.make_async_copy(ref.at[0, :, held], pair.at[j, own], sems.at[8 * g + j])
            for j, ref in enumerate((k_ref, v_ref, q_ref))
        ]
        copies.append(pltpu.make_async_copy(dg_ref.at[0, :, held], wide.at[:, cols], sems.at[8 * g + 3]))
        for j in range(4):
            copies.append(pltpu.make_async_copy(sib.at[j, :, cols], pair.at[j, other], sems.at[8 * g + 4 + j]))
        for c in copies:
            c.start()
        stages.append(copies)
    x_copies = []
    depth = x_ref.shape[2] // 2
    for i, ref in enumerate((x_ref, x_sib)):
        for g in range(2):
            cols = slice(g * depth, (g + 1) * depth)
            x_copies.append(pltpu.make_async_copy(ref.at[0, :, cols], rows_x.at[i, :, cols], x_sems.at[2 * i + g]))
    for c in x_copies:
        c.start()
    rows_live = live_rows(pos_ref, slots)
    mask = None
    for g, pair in enumerate((near, far)):
        cols = slice(g * width, (g + 1) * width)
        for c in stages[g]:
            c.wait()
        pair[0, own] = mark_dead(pair[0, own], rows_live)
        pair[3, own] = wide[:, cols].astype(BF16)
        if mask is None:
            mask = local_mask(core, pair)
            marks = nt(jnp.ones((8, HEAD), BF16), pair[0, :, :HEAD])[0:1]
            live[...] = jnp.where(marks < MARK_LIMIT, 1.0, 0.0)
        for h in range(width // HEAD):
            at = slice(h * HEAD, (h + 1) * HEAD)
            scores = jnp.where(mask, nt(pair[0, :, at], pair[2, :, at]) * scale, NEG_FILL)
            partial_stats(scores, nt(pair[1, :, at], pair[3, :, at]), stats, g * width // HEAD + h)
    for c in x_copies:
        c.wait()


def local_stats(route_pos, keys, values, queries, d_gated, sib, x_routed, x_sib):
    _, slots, half = sib.shape
    heads = half // HEAD
    anywhere = pl.BlockSpec(memory_space=pl.ANY)
    return pl.pallas_call(
        functools.partial(local_stats_kernel, HEAD**-0.5),
        out_shape=[
            jax.ShapeDtypeStruct((3, heads, 2 * slots), F32),
            jax.ShapeDtypeStruct((1, 2 * slots), F32),
            pltpu.VMEM((4, 2 * slots, half // 2), BF16),
            pltpu.VMEM((4, 2 * slots, half // 2), BF16),
            pltpu.VMEM((2, slots, x_routed.shape[2]), BF16),
        ],
        in_specs=[VMEM] + [anywhere] * 7,
        out_specs=[VMEM] * 5,
        scratch_shapes=[pltpu.VMEM((slots, half), F32), pltpu.SemaphoreType.DMA((16,)), pltpu.SemaphoreType.DMA((4,))],
        compiler_params=params(),
        cost_estimate=cost(16 * slots * slots * half, 16 * slots * half, 4 * slots * slots * half // HEAD),
        name="local_stats",
    )(route_pos, *in_hbm(keys, values, queries, d_gated), sib, x_routed, x_sib)


def cross_stats_kernel(scale, near, far, straight, diag, cross, stats, kept):
    slots, width = straight.shape[1], straight.shape[2]
    chip = here()[1]
    top, bottom = slice(0, slots), slice(slots, 2 * slots)

    @pl.when(chip == 0)
    def _():
        for part in range(2):
            cross[part] = far[part]
            cross[2 + part, top] = straight[part]
            cross[2 + part, bottom] = diag[part]

    @pl.when(chip != 0)
    def _():
        for part in range(2):
            cross[part, top] = straight[part]
            cross[part, bottom] = diag[part]
            cross[2 + part] = near[2 + part]

    live = cross[0, :, :HEAD].astype(F32) < MARK_LIMIT
    mask = jnp.concatenate([live] * (2 * slots // HEAD), axis=1)
    heads = width // HEAD
    for h in range(heads):
        cols = slice(h * HEAD, (h + 1) * HEAD)
        scores = jnp.where(mask, nt(cross[0, :, cols], cross[2, :, cols]) * scale, NEG_FILL)
        kept_stats(scores, nt(cross[1, :, cols], cross[3, :, cols]), kept, stats, h)


def cross_stats(near, far, straight, diag):
    _, slots, width = straight.shape
    heads = width // HEAD
    return pl.pallas_call(
        functools.partial(cross_stats_kernel, HEAD**-0.5),
        out_shape=[
            pltpu.VMEM((4, 2 * slots, width), BF16),
            jax.ShapeDtypeStruct((3, heads, 2 * slots), F32),
            pltpu.VMEM((2, heads, 2 * slots, 2 * slots), BF16),
        ],
        in_specs=[VMEM] * 4,
        out_specs=[VMEM] * 3,
        compiler_params=params(),
        cost_estimate=cost(16 * slots * slots * width, 32 * slots * width, 4 * slots * slots * heads),
        name="cross_stats",
    )(near, far, straight, diag)


NONE = (-3e38, 0.0, 0.0)


def merge(first, second):
    top = jnp.maximum(first[0], second[0])
    a, b = jnp.exp(first[0] - top), jnp.exp(second[0] - top)
    inverse = 1.0 / (first[1] * a + second[1] * b)
    return a * inverse, (first[2] * a + second[2] * b) * inverse


def choose(flag, yes, no):
    return [jnp.where(flag, y, n) for y, n in zip(yes, no)]


def gradients(q, k, dg, e, gw, scale, factor, delta):
    weights = e * factor
    ds = (weights * ((gw - delta) * scale)).astype(BF16)
    return tn(ds, k), nn(ds, q), nn(weights.astype(BF16), dg)


def local_gradients(pair, h, mask, scale, top, factor, delta):
    cols = slice(h * HEAD, (h + 1) * HEAD)
    k, v, q, dg = [pair[i, :, cols] for i in range(4)]
    e = jnp.exp(jnp.where(mask, nt(k, q) * scale, NEG_FILL) - top)
    return gradients(q, k, dg, e, nt(v, dg), scale, factor, delta)


def near_grad_kernel(scale, pair, local, stats, gates, dq_out, own_out, sib_out, sum_out):
    slots, width = own_out.shape[1], own_out.shape[2]
    heads = width // HEAD
    first = here()[1] == 0
    near = [local[i, :heads] for i in range(3)]
    factor, delta = merge(near, choose(first, NONE, [stats[i] for i in range(3)]))
    factor = factor * gates[...]
    sum_out[...] = jnp.sum(delta, axis=0, keepdims=True)
    mask = local_mask(here()[0], pair)
    for h in range(heads):
        cols = slice(h * HEAD, (h + 1) * HEAD)
        row = slice(h, h + 1)
        dq, dk, dv = local_gradients(pair, h, mask, scale, near[0][row], factor[row], delta[row])
        dq_out[:, cols] = dq
        for i, part in enumerate((dk, dv)):
            own_out[i, :, cols] = part[:slots].astype(BF16)
            sib_out[i, :, cols] = part[slots:].astype(BF16)


def near_grad(pair, local, stats, gates):
    _, rows, width = pair.shape
    slots = rows // 2
    out = pltpu.VMEM((2, slots, width), BF16)
    return pl.pallas_call(
        functools.partial(near_grad_kernel, HEAD**-0.5),
        out_shape=[pltpu.VMEM((2 * slots, width), F32), out, out, jax.ShapeDtypeStruct(gates.shape, F32)],
        in_specs=[VMEM] * 4,
        out_specs=[VMEM] * 4,
        compiler_params=params(),
        cost_estimate=cost(20 * slots * slots * width, 40 * slots * width),
        name="near_grad",
    )(pair, local, stats, gates)


def put_terms(grad, rows_x, out_ref):
    high = grad.astype(BF16)
    rest = grad - high.astype(F32)
    mid = rest.astype(BF16)
    low = (rest - mid.astype(F32)).astype(BF16)
    slots = rows_x.shape[1]
    row = lax.broadcasted_iota(jnp.int32, (8, grad.shape[1]), 0)
    lhs = jnp.where(row == 0, high.astype(F32), jnp.where(row == 1, mid.astype(F32), jnp.where(row == 2, low.astype(F32), 0.0)))
    lhs = lhs.astype(BF16)
    term = jnp.sum(nn(lhs[:, :slots], rows_x[0]) + nn(lhs[:, slots:], rows_x[1]), axis=0, keepdims=True)
    parts, copies, _, chunk = out_ref.shape
    for j in range(parts):
        for i in range(copies):
            out_ref[j, i] = term[:, j * chunk : (j + 1) * chunk]


def cross_grad_kernel(scale, total, cross, kept, stats, local, heard, gates, near_dq, near_sum, rows_x, straight, diag, dq_out, keep, final, terms, held, sem):
    slots, width = straight.shape[1], straight.shape[2]
    heads = width // HEAD
    first = here()[1] == 0
    late = jnp.where(first, 0.0, 1.0)
    mine = [stats[i] for i in range(3)]
    other = [heard[i] for i in range(3)]
    near = [local[i, :heads] for i in range(3)]
    far = [local[i, heads:] for i in range(3)]
    factor, delta = merge(mine, choose(first, other, near))
    factor = factor * jnp.where(first, heard[3], jnp.broadcast_to(gates[...], factor.shape))
    final[0], final[1] = merge(far, choose(first, NONE, other))
    sums = near_sum[...] + jnp.sum(final[1], axis=0, keepdims=True)
    put_terms(sums * gates[...] * (1.0 - gates[...]) * (1.0 / total), rows_x, held)
    leaving = pltpu.make_async_copy(held, terms, sem)
    leaving.start()
    for h in range(heads):
        cols = slice(h * HEAD, (h + 1) * HEAD)
        row = slice(h, h + 1)
        dq, dk, dv = gradients(
            cross[2, :, cols], cross[0, :, cols], cross[3, :, cols],
            kept[0, h].astype(F32), kept[1, h].astype(F32), scale, factor[row], delta[row],
        )
        dq_out[:, cols] = (near_dq[:, cols] + late * dq).astype(BF16)
        keep[0, :, cols] = dk.astype(BF16)
        keep[1, :, cols] = dv.astype(BF16)
        sent = jnp.where(first, dq, dk).astype(BF16)
        straight[0, :, cols] = sent[:slots]
        diag[0, :, cols] = sent[slots:]
        straight[1, :, cols] = dv[:slots].astype(BF16)
        diag[1, :, cols] = dv[slots:].astype(BF16)
    leaving.wait()


def cross_grad(cross, kept, stats, local, heard, gates, near_dq, near_sum, rows_x, parts, copies, total):
    _, rows, width = cross.shape
    slots = rows // 2
    out = pltpu.VMEM((2, slots, width), BF16)
    spread = (parts, copies, 1, rows_x.shape[2] // parts)
    return pl.pallas_call(
        functools.partial(cross_grad_kernel, HEAD**-0.5, total),
        out_shape=[
            out,
            out,
            pltpu.VMEM((rows, width), BF16),
            pltpu.VMEM((2, rows, width), BF16),
            jax.ShapeDtypeStruct((2, width // HEAD, rows), F32),
            pltpu.HBM(spread, F32),
        ],
        in_specs=[VMEM] * 9,
        out_specs=[VMEM] * 5 + [pl.BlockSpec(memory_space=pltpu.HBM)],
        scratch_shapes=[pltpu.VMEM(spread, F32), pltpu.SemaphoreType.DMA],
        compiler_params=params(),
        cost_estimate=cost(24 * slots * slots * width, 64 * slots * width),
        name="cross_grad",
    )(cross, kept, stats, local, heard, gates, near_dq, near_sum, rows_x)


def far_grad_kernel(scale, pair, local, final, gates, keep, near_dq, near_own, near_sib, own_out, sib_out):
    slots, width = pair.shape[1] // 2, pair.shape[2]
    heads = width // HEAD
    early = jnp.where(here()[1] == 0, 1.0, 0.0)
    factor = final[0] * gates[...]
    mask = local_mask(here()[0], pair)
    own_out[0, :, :width] = near_dq[:slots]
    sib_out[0, :, :width] = near_dq[slots:]
    for i in range(2):
        own_out[1 + i, :, :width] = near_own[i]
        sib_out[1 + i, :, :width] = near_sib[i]
    for h in range(heads):
        cols = slice(width + h * HEAD, width + (h + 1) * HEAD)
        at = slice(h * HEAD, (h + 1) * HEAD)
        row = slice(h, h + 1)
        top = local[0, heads + h : heads + h + 1]
        dq, dk, dv = local_gradients(pair, h, mask, scale, top, factor[row], final[1, row])
        dk = dk + early * keep[0, :, at].astype(F32)
        dv = dv + early * keep[1, :, at].astype(F32)
        for i, part in enumerate((dq, dk, dv)):
            own_out[i, :, cols] = part[:slots].astype(BF16)
            sib_out[i, :, cols] = part[slots:].astype(BF16)


def far_grad(pair, local, final, gates, keep, near_dq, near_own, near_sib):
    _, rows, width = pair.shape
    slots, half = rows // 2, 2 * width
    out = jax.ShapeDtypeStruct((3, slots, half), BF16)
    return pl.pallas_call(
        functools.partial(far_grad_kernel, HEAD**-0.5),
        out_shape=[out, out],
        in_specs=[VMEM] * 8,
        out_specs=[VMEM] * 2,
        compiler_params=params(),
        cost_estimate=cost(20 * slots * slots * half, 40 * slots * half),
        name="far_grad",
    )(pair, local, final, gates, keep, near_dq, near_own, near_sib)


def own_join_kernel(own, dq_out, dk_out, dv_out, waiting, total, sems):
    slots, half = own.shape[1], own.shape[2]
    width = half // 2
    core, chip = here()
    cols = pl.ds(pl.multiple_of(core * half, HEAD), half)
    stores = []
    for j, out in enumerate((dq_out, dk_out, dv_out)):
        total[j] = own[j].astype(F32)
        stores.append(pltpu.make_async_copy(total.at[j], out.at[0, :, cols], sems.at[j]))
        stores[-1].start()
    waiting[0] = jnp.where(chip == 0, total[1, :, :width], total[0, :, width:]).astype(BF16)
    waiting[1] = own[2, :, :width]
    for c in stores:
        c.wait()


def own_join(own, shape):
    out = pltpu.HBM(shape, F32)
    _, slots, half = own.shape
    hbm = pl.BlockSpec(memory_space=pltpu.HBM)
    return pl.pallas_call(
        own_join_kernel,
        out_shape=[out] * 3 + [jax.ShapeDtypeStruct((2, slots, half // 2), BF16)],
        in_specs=[VMEM],
        out_specs=[hbm] * 3 + [VMEM],
        scratch_shapes=[pltpu.VMEM((3, slots, half), F32), pltpu.SemaphoreType.DMA((3,))],
        compiler_params=params(),
        cost_estimate=cost(0, 18 * own.size),
        name="own_join",
    )(own)


def finish_kernel(waiting, sib, straight, diag, dq_in, dk_in, dv_in, dq_out, dk_out, dv_out, low, held, total, added, in_sems, out_sems):
    half = sib.shape[2]
    width = half // 2
    core, chip = here()
    early, late = jnp.where(chip == 0, 1.0, 0.0), jnp.where(chip == 0, 0.0, 1.0)
    loads = [pltpu.make_async_copy(sib.at[j], low.at[j], in_sems.at[j]) for j in range(3)]
    loads += [pltpu.make_async_copy(waiting.at[j], held.at[j], in_sems.at[3 + j]) for j in range(2)]
    for c in loads:
        c.start()
    cols = pl.ds(pl.multiple_of((1 - core) * half, HEAD), half)
    stores = []
    for j, out in enumerate((dq_out, dk_out, dv_out)):
        loads[j].wait()
        first, second = low[j, :, :width].astype(F32), low[j, :, width:].astype(F32)
        if j == 0:
            second = second + late * diag[0].astype(F32)
        else:
            first = first + early * diag[j - 1].astype(F32)
        total[j, :, :width] = first
        total[j, :, width:] = second
        stores.append(pltpu.make_async_copy(total.at[j], out.at[0, :, cols], out_sems.at[j]))
        stores[-1].start()
    for j in range(2):
        loads[3 + j].wait()
        added[j] = held[j].astype(F32) + straight[j].astype(F32)

    def store(j, out, offset):
        at = pl.ds(pl.multiple_of(core * half + offset, HEAD), width)
        copy = pltpu.make_async_copy(added.at[j], out.at[0, :, at], out_sems.at[3 + j])
        copy.start()
        return copy

    @pl.when(chip == 0)
    def _():
        copies = [store(0, dk_out, 0), store(1, dv_out, 0)]
        for c in copies:
            c.wait()

    @pl.when(chip != 0)
    def _():
        store(0, dq_out, width).wait()

    for c in stores:
        c.wait()


def finish(waiting, sib, straight, diag, outs):
    _, slots, half = sib.shape
    hbm = pl.BlockSpec(memory_space=pltpu.HBM)
    anywhere = pl.BlockSpec(memory_space=pl.ANY)
    return pl.pallas_call(
        finish_kernel,
        out_shape=[pltpu.HBM(o.shape, F32) for o in outs],
        in_specs=[anywhere] * 2 + [VMEM] * 2 + [hbm] * 3,
        out_specs=[hbm] * 3,
        scratch_shapes=[
            pltpu.VMEM((3, slots, half), BF16),
            pltpu.VMEM(waiting.shape, BF16),
            pltpu.VMEM((3, slots, half), F32),
            pltpu.VMEM(waiting.shape, F32),
            pltpu.SemaphoreType.DMA((5,)),
            pltpu.SemaphoreType.DMA((5,)),
        ],
        input_output_aliases={4: 0, 5: 1, 6: 2},
        compiler_params=params(),
        cost_estimate=cost(0, 12 * sib.size),
        name="finish",
    )(waiting, sib, straight, diag, *in_hbm(*outs))


def swap_body(route_pos, x_routed, w_router, queries, keys, values, d_gated):
    slots = queries.shape[1]
    n, ndp = lax.axis_size("ctx"), lax.axis_size("dp")

    def send(a, flip):
        return lax.ppermute(a, "ctx", [(i, i ^ flip) for i in range(n)])

    def beside(fn, *operands):
        def skip(*ops):
            return jax.tree.map(lambda o: jnp.zeros(o.shape, o.dtype), jax.eval_shape(fn, *ops))

        return lax.cond(route_pos[0, 0] >= -1, fn, skip, *operands)

    def after(value, *others):
        return lax.optimization_barrier((value, *others))[0]

    def widen(part, step, *first):
        other = lax.ppermute(part, "dp", [(i, i ^ step) for i in range(ndp)])
        return jnp.concatenate([part, after(other, *first)], axis=1)

    def exchange_phase(x_routed, w_part, theirs):
        sib, x_sib = send(theirs, 1), send(x_routed, 1)
        step = 2
        while 2 * step < ndp:
            w_part = widen(w_part, step)
            step *= 2
        return sib, x_sib, w_part

    def far_phase(*operands):
        own_out, sib_out = far_grad(*operands)
        sib_in = send(sib_out, 1)
        *outs, waiting = own_join(own_out, queries.shape)
        return outs, waiting, sib_in

    out_s, out_d, w_part = cross_pack(route_pos, w_router, keys, values, queries, d_gated)
    in_s, in_d = send(out_s, 2), send(out_d, 3)

    theirs = sib_pack(after(route_pos, out_s), keys, values, queries, d_gated)
    if ndp > 1:
        w_part = widen(w_part, 1, theirs)
    sib, x_sib, w_part = beside(exchange_phase, x_routed, w_part, theirs)
    local, live, near, far, rows_x = local_stats(route_pos, keys, values, queries, d_gated, sib, x_routed, x_sib)
    cross, stats, kept = cross_stats(near, far, in_s, in_d)
    if ndp > 2:
        w_part = widen(w_part, ndp // 2, stats)
    gates, message = pair_gate(live, rows_x, w_part, local, stats, ndp)

    heard = send(message, 2)
    near_dq, near_own, near_sib, near_sum = near_grad(near, local, stats, gates)
    total = float(ndp * n * slots // 2)
    back_s, back_d, dq_low, keep, final, terms = cross_grad(
        cross, kept, stats, local, heard, gates, near_dq, near_sum, rows_x, ndp, n, total
    )

    ret_s, ret_d = send(back_s, 2), send(back_d, 3)
    shared = lax.all_to_all(terms.reshape(ndp * n, 1, -1), ("dp", "ctx"), 0, 0, tiled=True)
    outs, waiting, sib_in = beside(far_phase, far, local, final, gates, keep, dq_low, near_own, near_sib)
    dq, dk, dv = finish(waiting, sib_in, ret_s, ret_d, outs)
    router_grad = jnp.sum(after(shared, dq), axis=(0, 1))
    return dq, dk, dv, router_grad


def body(route_pos, x_routed, w_router, queries, keys, values, d_gated):
    slots, full = queries.shape[1], queries.shape[2]
    n, ndp = lax.axis_size("ctx"), lax.axis_size("dp")
    chips = n // 2
    me, dp_me = lax.axis_index("ctx"), lax.axis_index("dp")
    core = (me % 2).astype(jnp.int32).reshape(1)
    half = full // 2
    groups = GROUPS if (half // HEAD) % GROUPS == 0 else 1
    width = half // groups

    sib_pairs = [(i, i ^ 1) for i in range(n)]

    def forward_pairs(step, flip):
        return [(i, (i + 2 * step) ^ flip) for i in range(n) if i + 2 * step < n]

    def back_pairs(step, flip):
        return [(b, a) for a, b in forward_pairs(step, flip)]

    def to_sib(a):
        return lax.ppermute(a, "ctx", sib_pairs)

    links = [(step, flip) for step in range(1, chips) for flip in (0, 1)]

    w_row = w_router.reshape(1, -1)
    w_parts = [w_row] + [
        lax.ppermute(w_row, "dp", [(i, (i + s) % ndp) for i in range(ndp)]) for s in range(1, ndp)
    ]
    live = (route_pos >= 0).astype(jnp.int32)
    lives = [live, to_sib(live)] + [lax.ppermute(live, "ctx", forward_pairs(*link)) for link in links]
    live_all = jnp.concatenate(lives, axis=0)

    kv_mine, kv_theirs = pack(core, keys, values, groups, width)
    kv_far = [
        [lax.ppermute((kv_theirs if flip else kv_mine)[g], "ctx", forward_pairs(step, flip)) for step, flip in links]
        for g in range(groups)
    ]
    q_mine, q_theirs = pack(core, queries, d_gated, groups, width)
    kv_sib = [to_sib(a) for a in kv_theirs]
    q_sib = [to_sib(a) for a in q_theirs]

    offsets = ((dp_me - jnp.arange(ndp)) % ndp).astype(jnp.int32)
    gate = router_gate(offsets, route_pos, x_routed, w_parts)
    gates = (gate, to_sib(gate))

    accs = (jnp.zeros((1, slots), F32), jnp.zeros((1, slots), F32))
    dq_own, sib_in, kv_own, back = [], [], [], []
    for g in range(groups):
        dq, sib_out, kv_local, kv_remote, accs = attention(
            core, live_all, gates, accs, q_mine[g], q_sib[g], [kv_mine[g], kv_sib[g], *kv_far[g]]
        )
        back.append([lax.ppermute(a, "ctx", back_pairs(*link)) for a, link in zip(kv_remote, links)])
        sib_in.append(to_sib(sib_out))
        dq_own.append(dq)
        kv_own.append(kv_local)

    targets = ((dp_me + jnp.arange(ndp)) % ndp).astype(jnp.int32)
    terms = router_terms(targets, gate, accs[0], to_sib(accs[1]), x_routed, ndp)
    mine = terms[0]
    for s in range(1, ndp):
        mine = mine + lax.ppermute(terms[s], "dp", [(i, (i + s) % ndp) for i in range(ndp)])
    total = mine
    for s in range(1, n):
        total = total + lax.ppermute(mine, "ctx", [(i, (i + s) % n) for i in range(n)])
    router_grad = total[0] / float(ndp * n * slots // 2)

    dq, dk, dv = combine(core, dq_own, sib_in, kv_own, back, queries.shape)
    return dq, dk, dv, router_grad


def solution(mesh):
    placed = (
        P("dp", "ctx"),
        P("dp", "ctx", None),
        P("dp"),
        P("dp", "ctx", None),
        P("dp", "ctx", None),
        P("dp", "ctx", None),
        P("dp", "ctx", None),
    )
    ndp = mesh.shape["dp"]
    paired = mesh.shape["ctx"] == 4 and ndp & (ndp - 1) == 0
    return jax.shard_map(
        swap_body if paired else body,
        mesh=mesh,
        in_specs=placed,
        out_specs=(P("dp", "ctx", None), P("dp", "ctx", None), P("dp", "ctx", None), P("dp")),
        check_vma=False,
    )
```

```python
import functools

import jax
import jax.numpy as jnp
from jax import lax
from jax.experimental import pallas as pl
from jax.experimental.pallas import tpu as pltpu
from jax.sharding import PartitionSpec as P

HEAD = 128
GROUPS = 4
NEG_FILL = -1e30
MIB = 1024 * 1024
BF16 = jnp.bfloat16
F32 = jnp.float32

VMEM = pl.BlockSpec(memory_space=pltpu.VMEM)
SMEM = pl.BlockSpec(memory_space=pltpu.SMEM)


def params(mib=16):
    return pltpu.CompilerParams(vmem_limit_bytes=mib * MIB)


def cost(flops, nbytes, exps=0):
    return pl.CostEstimate(flops=1, bytes_accessed=1, transcendentals=0)


def in_hbm(*arrays):
    return [pltpu.with_memory_space_constraint(a, pltpu.HBM) for a in arrays]


def nt(a, b):
    return lax.dot_general(a, b, (((1,), (1,)), ((), ())), preferred_element_type=F32)


def nn(a, b):
    return lax.dot_general(a, b, (((1,), (0,)), ((), ())), preferred_element_type=F32)


def tn(a, b):
    return lax.dot_general(a, b, (((0,), (0,)), ((), ())), preferred_element_type=F32)


def pack_kernel(groups, width, core_ref, first_ref, second_ref, *outs):
    half = first_ref.shape[-1] // 2
    core = core_ref[0]
    for side in range(2):
        base = (core if side == 0 else 1 - core) * half
        for g in range(groups):
            out = outs[side * groups + g]
            cols = pl.ds(pl.multiple_of(base + g * width, HEAD), width)
            out[0] = first_ref[0, :, cols].astype(BF16)
            out[1] = second_ref[0, :, cols].astype(BF16)


def pack(core, first, second, groups, width):
    slots = first.shape[1]
    out = jax.ShapeDtypeStruct((2, slots, width), BF16)
    res = pl.pallas_call(
        functools.partial(pack_kernel, groups, width),
        out_shape=[out] * (2 * groups),
        in_specs=[SMEM, VMEM, VMEM],
        out_specs=[VMEM] * (2 * groups),
        compiler_params=params(),
        cost_estimate=cost(0, 2 * first.size * 4),
        name="pack",
    )(core, first, second)
    return res[:groups], res[groups:]


def gate_kernel(parts, offset_ref, pos_ref, x_ref, *refs):
    w_refs, out_ref = refs[:parts], refs[parts]
    chunk = w_refs[0].shape[-1]
    total = jnp.zeros((8, x_ref.shape[1]), F32)
    for s in range(parts):
        cols = pl.ds(pl.multiple_of(offset_ref[s] * chunk, HEAD), chunk)
        w_rows = jnp.broadcast_to(w_refs[s][...].astype(F32), (8, chunk)).astype(BF16)
        total = total + nt(w_rows, x_ref[0, :, cols])
    gate = 1.0 / (1.0 + jnp.exp(-total[0:1]))
    out_ref[...] = jnp.where(pos_ref[...] >= 0, gate, 0.0)


def router_gate(offsets, route_pos, x_routed, w_parts):
    parts = len(w_parts)
    return pl.pallas_call(
        functools.partial(gate_kernel, parts),
        out_shape=jax.ShapeDtypeStruct(route_pos.shape, F32),
        in_specs=[SMEM] + [VMEM] * (2 + parts),
        out_specs=VMEM,
        compiler_params=params(),
        cost_estimate=cost(16 * x_routed.size, x_routed.size * 2),
        name="router_gate",
    )(offsets, route_pos, x_routed, *w_parts)


def attention_kernel(remote, scale, core_ref, live_ref, gate_own, gate_sib, acc_own, acc_sib, q_own, q_sib, *refs):
    chunks = 2 + remote
    kv = refs[:chunks]
    outs = refs[chunks:]
    dq_own, sib_out, kv_own = outs[:3]
    kv_remote = outs[3 : 3 + remote]
    sum_own, sum_sib = outs[3 + remote :]
    slots, width = q_own.shape[1], q_own.shape[2]
    core = core_ref[0]
    key = lax.broadcasted_iota(jnp.int32, (slots, slots), 0)
    query = lax.broadcasted_iota(jnp.int32, (slots, slots), 1)
    counts = [jnp.sum(live_ref[i : i + 1], axis=1, keepdims=True) for i in range(chunks)]
    lives = [key < counts[i] for i in range(chunks)]
    own_later = core == 1
    bias_rows = []
    for i in range(chunks):
        live = lives[i]
        if i == 0:
            pair = (live & (key <= query), live & jnp.logical_not(own_later))
        elif i == 1:
            pair = (live & own_later, live & (key <= query))
        else:
            pair = (live, live)
        bias_rows.append(jnp.concatenate([jnp.where(p, 0.0, NEG_FILL) for p in pair], axis=1))
    bias = jnp.concatenate(bias_rows, axis=0)
    gates = jnp.concatenate([gate_own[...], gate_sib[...]], axis=1)
    total = jnp.zeros((1, 2 * slots), F32)
    for h in range(width // HEAD):
        cols = slice(h * HEAD, (h + 1) * HEAD)
        q = jnp.concatenate([q_own[0, :, cols], q_sib[0, :, cols]], axis=0)
        dg = jnp.concatenate([q_own[1, :, cols], q_sib[1, :, cols]], axis=0)
        k = jnp.concatenate([r[0, :, cols] for r in kv], axis=0)
        v = jnp.concatenate([r[1, :, cols] for r in kv], axis=0)
        scores = nt(k, q) * scale + bias
        top = jnp.max(scores, axis=0, keepdims=True)
        e = jnp.exp(scores - top)
        inverse = 1.0 / jnp.sum(e, axis=0, keepdims=True)
        gw = nt(v, dg)
        delta = jnp.sum(e * gw, axis=0, keepdims=True) * inverse
        total = total + delta
        weights = e * (inverse * gates)
        dv = nn(weights.astype(BF16), dg)
        ds = (weights * ((gw - delta) * scale)).astype(BF16)
        dk = nn(ds, q)
        dq = tn(ds, k)
        dq_own[:, cols] = dq[:slots].astype(dq_own.dtype)
        sib_out[0, :, cols] = dq[slots:].astype(BF16)
        kv_own[0, :, cols] = dk[:slots].astype(BF16)
        kv_own[1, :, cols] = dv[:slots].astype(BF16)
        sib_out[1, :, cols] = dk[slots : 2 * slots].astype(BF16)
        sib_out[2, :, cols] = dv[slots : 2 * slots].astype(BF16)
        for i in range(remote):
            rows = slice((2 + i) * slots, (3 + i) * slots)
            kv_remote[i][0, :, cols] = dk[rows].astype(BF16)
            kv_remote[i][1, :, cols] = dv[rows].astype(BF16)
    sum_own[...] = acc_own[...] + total[:, :slots]
    sum_sib[...] = acc_sib[...] + total[:, slots:]


def attention(core, live, gates, accs, q_own, q_sib, kv):
    remote = len(kv) - 2
    _, slots, width = q_own.shape
    pair = jax.ShapeDtypeStruct((2, slots, width), BF16)
    row = jax.ShapeDtypeStruct((1, slots), F32)
    outs = [
        jax.ShapeDtypeStruct((slots, width), BF16),
        jax.ShapeDtypeStruct((3, slots, width), BF16),
        pair,
        *([pair] * remote),
        row,
        row,
    ]
    keys = (2 + remote) * slots
    res = pl.pallas_call(
        functools.partial(attention_kernel, remote, HEAD**-0.5),
        out_shape=outs,
        in_specs=[SMEM] + [VMEM] * (7 + len(kv)),
        out_specs=[VMEM] * len(outs),
        compiler_params=params(48),
        cost_estimate=cost(20 * slots * keys * width, 8 * keys * width + 20 * slots * width, 2 * slots * keys * width // HEAD),
        name="attention",
    )(core, live, *gates, *accs, q_own, q_sib, *kv)
    return res[0], res[1], res[2], res[3 : 3 + remote], (res[3 + remote], res[4 + remote])


def combine_kernel(groups, width, remote, core_ref, *refs):
    dq_own, sib, kv_own = refs[:groups], refs[groups : 2 * groups], refs[2 * groups : 3 * groups]
    back = refs[3 * groups : 3 * groups + groups * remote]
    dq_out, dk_out, dv_out = refs[3 * groups + groups * remote :]
    half = groups * width
    core = core_ref[0]
    for g in range(groups):
        own = pl.ds(pl.multiple_of(core * half + g * width, HEAD), width)
        other = pl.ds(pl.multiple_of((1 - core) * half + g * width, HEAD), width)
        dq_out[0, :, own] = dq_own[g][...].astype(F32)
        dq_out[0, :, other] = sib[g][0].astype(F32)
        for i, out in enumerate((dk_out, dv_out)):
            mine = kv_own[g][i].astype(F32)
            theirs = sib[g][1 + i].astype(F32)
            for r in range(remote):
                part = back[g * remote + r][i].astype(F32)
                if r % 2 == 0:
                    mine = mine + part
                else:
                    theirs = theirs + part
            out[0, :, own] = mine
            out[0, :, other] = theirs


def combine(core, dq_own, sib, kv_own, back, shape):
    groups = len(dq_own)
    remote = len(back[0])
    out = jax.ShapeDtypeStruct(shape, F32)
    flat = [*dq_own, *sib, *kv_own, *(b for group in back for b in group)]
    return pl.pallas_call(
        functools.partial(combine_kernel, groups, dq_own[0].shape[-1], remote),
        out_shape=[out] * 3,
        in_specs=[SMEM] + [VMEM] * len(flat),
        out_specs=[VMEM] * 3,
        compiler_params=params(48),
        cost_estimate=cost(0, 3 * out.size * 6),
        name="combine",
    )(core, *flat)


def router_kernel(parts, target_ref, gate_ref, own_ref, sib_ref, x_ref, *outs):
    gate = gate_ref[...]
    grad = (own_ref[...] + sib_ref[...]) * gate * (1.0 - gate)
    high = grad.astype(BF16)
    rest = grad - high.astype(F32)
    mid = rest.astype(BF16)
    low = (rest - mid.astype(F32)).astype(BF16)
    row = lax.broadcasted_iota(jnp.int32, (8, grad.shape[1]), 0)
    lhs = jnp.where(row == 0, high.astype(F32), jnp.where(row == 1, mid.astype(F32), jnp.where(row == 2, low.astype(F32), 0.0)))
    lhs = lhs.astype(BF16)
    chunk = outs[0].shape[-1]
    for s in range(parts):
        cols = pl.ds(pl.multiple_of(target_ref[s] * chunk, HEAD), chunk)
        outs[s][...] = jnp.sum(nn(lhs, x_ref[0, :, cols]), axis=0, keepdims=True)


def router_terms(targets, gate, own, sib, x_routed, parts):
    chunk = x_routed.shape[-1] // parts
    return pl.pallas_call(
        functools.partial(router_kernel, parts),
        out_shape=[jax.ShapeDtypeStruct((1, chunk), F32)] * parts,
        in_specs=[SMEM] + [VMEM] * 4,
        out_specs=[VMEM] * parts,
        compiler_params=params(),
        cost_estimate=cost(16 * x_routed.size, x_routed.size * 2),
        name="router_terms",
    )(targets, gate, own, sib, x_routed)


def here():
    me = lax.axis_index("ctx")
    return lax.rem(me, 2), lax.div(me, 2)


MARK = 2.0**60
MARK_LIMIT = 2.0**50


def live_rows(pos_ref, slots):
    count = jnp.sum((pos_ref[...] >= 0).astype(jnp.int32), axis=1, keepdims=True)
    return lax.broadcasted_iota(jnp.int32, (slots, HEAD), 0) < count


def mark_dead(keys, live):
    width = keys.shape[-1]
    mask = jnp.concatenate([live] * (width // HEAD), axis=1)
    return jnp.where(mask, keys.astype(F32), MARK).astype(BF16)


def cross_pack_kernel(pos_any, w_any, k_ref, v_ref, q_ref, dg_ref, straight, diag, w_out, wide, pos_ref, w_ref, sems):
    small = [pltpu.make_async_copy(pos_any, pos_ref, sems.at[4]), pltpu.make_async_copy(w_any, w_ref, sems.at[5])]
    for c in small:
        c.start()
    slots, width = straight.shape[1], straight.shape[2]
    half = k_ref.shape[-1] // 2
    core, chip = here()
    ends = ((straight, core * half), (diag, (1 - core) * half))

    def copies(first, second, targets, offset):
        out = []
        for i, (end, start) in enumerate(ends):
            cols = pl.ds(pl.multiple_of(start + offset, HEAD), width)
            out.append(pltpu.make_async_copy(first.at[0, :, cols], end.at[0], sems.at[2 * i]))
            out.append(pltpu.make_async_copy(second.at[0, :, cols], targets[i], sems.at[2 * i + 1]))
        for c in out:
            c.start()
        for c in out:
            c.wait()

    @pl.when(chip == 0)
    def _():
        copies(k_ref, v_ref, (straight.at[1], diag.at[1]), 0)
        small[0].wait()
        live = live_rows(pos_ref, slots)
        for end, _ in ends:
            end[0] = mark_dead(end[0], live)

    @pl.when(chip != 0)
    def _():
        copies(q_ref, dg_ref, (wide.at[0], wide.at[1]), width)
        small[0].wait()
        for i, (end, _) in enumerate(ends):
            end[1] = wide[i].astype(BF16)

    small[1].wait()
    w_out[...] = w_ref[...].astype(F32).reshape(w_out.shape)


def cross_pack(route_pos, w_router, keys, values, queries, d_gated):
    _, slots, full = keys.shape
    cross = pltpu.VMEM((2, slots, full // 4), BF16)
    hbm = pl.BlockSpec(memory_space=pltpu.HBM)
    return pl.pallas_call(
        cross_pack_kernel,
        out_shape=[cross, cross, jax.ShapeDtypeStruct((1, w_router.shape[0]), F32)],
        in_specs=[hbm] * 6,
        out_specs=[VMEM] * 3,
        scratch_shapes=[
            pltpu.VMEM((2, slots, full // 4), F32),
            pltpu.VMEM(route_pos.shape, jnp.int32),
            pltpu.VMEM(w_router.shape, BF16),
            pltpu.SemaphoreType.DMA((6,)),
        ],
        compiler_params=params(),
        cost_estimate=cost(0, 10 * slots * full),
        name="cross_pack",
    )(*in_hbm(route_pos, w_router, keys, values, queries, d_gated))


def sib_pack_kernel(pos_ref, k_ref, v_ref, q_ref, dg_ref, out, wide, sems):
    slots, half = out.shape[1], out.shape[2]
    cols = pl.ds(pl.multiple_of((1 - here()[0]) * half, HEAD), half)
    sources = ((k_ref, out.at[0]), (dg_ref, wide), (v_ref, out.at[1]), (q_ref, out.at[2]))
    copies = [pltpu.make_async_copy(src.at[0, :, cols], dst, sems.at[i]) for i, (src, dst) in enumerate(sources)]
    for c in copies:
        c.start()
    live = live_rows(pos_ref, slots)
    copies[0].wait()
    out[0] = mark_dead(out[0], live)
    copies[1].wait()
    out[3] = wide[...].astype(BF16)
    copies[2].wait()
    copies[3].wait()


def sib_pack(route_pos, keys, values, queries, d_gated):
    _, slots, full = keys.shape
    hbm = pl.BlockSpec(memory_space=pltpu.HBM)
    return pl.pallas_call(
        sib_pack_kernel,
        out_shape=pltpu.VMEM((4, slots, full // 2), BF16),
        in_specs=[VMEM, hbm, hbm, hbm, hbm],
        out_specs=VMEM,
        scratch_shapes=[pltpu.VMEM((slots, full // 2), F32), pltpu.SemaphoreType.DMA((4,))],
        compiler_params=params(),
        cost_estimate=cost(0, 20 * slots * full),
        name="sib_pack",
    )(route_pos, *in_hbm(keys, values, queries, d_gated))


def pair_gate_kernel(parts, live_ref, rows_x, w_ref, local, stats, out_ref, message):
    chunk = w_ref.shape[1] // parts
    slots = rows_x.shape[1]
    for i in range(2):
        total = jnp.zeros((8, slots), F32)
        for j in range(parts):
            w_rows = jnp.broadcast_to(w_ref[:, j * chunk : (j + 1) * chunk], (8, chunk)).astype(BF16)
            cols = pl.ds(pl.multiple_of((lax.axis_index("dp") ^ j) * chunk, HEAD), chunk)
            total = total + nt(w_rows, rows_x[i, :, cols])
        lanes = slice(i * slots, (i + 1) * slots)
        out_ref[:, lanes] = live_ref[:, lanes] / (1.0 + jnp.exp(-total[0:1]))
    first = here()[1] == 0
    heads = stats.shape[1]
    for i in range(3):
        message[i] = jnp.where(first, stats[i], local[i, heads:])
    message[3] = jnp.broadcast_to(out_ref[...], message.shape[1:])


def pair_gate(live, rows_x, w_full, local, stats, parts):
    _, heads, lanes = stats.shape
    return pl.pallas_call(
        functools.partial(pair_gate_kernel, parts),
        out_shape=[jax.ShapeDtypeStruct(live.shape, F32), jax.ShapeDtypeStruct((4, heads, lanes), F32)],
        in_specs=[VMEM] * 5,
        out_specs=[VMEM] * 2,
        compiler_params=params(),
        cost_estimate=cost(16 * rows_x.size, rows_x.size * 2),
        name="router_gate",
    )(live, rows_x, w_full, local, stats)


def local_mask(core, pair):
    slots = pair.shape[1] // 2
    key = lax.broadcasted_iota(jnp.int32, (slots, slots), 0)
    query = lax.broadcasted_iota(jnp.int32, (slots, slots), 1)
    causal = key <= query
    own_live = pair[0, :slots, :slots].astype(F32) < MARK_LIMIT
    sib_live = pair[0, slots:, :slots].astype(F32) < MARK_LIMIT
    own_rows = jnp.concatenate([own_live & causal, own_live & (core == 0)], axis=1)
    sib_rows = jnp.concatenate([sib_live & (core == 1), sib_live & causal], axis=1)
    return jnp.concatenate([own_rows, sib_rows], axis=0)


def kept_stats(scores, gw, kept, stats, h):
    top = jnp.max(scores, axis=0, keepdims=True)
    e = jnp.exp(scores - top).astype(BF16)
    gw = gw.astype(BF16)
    kept[0, h] = e
    kept[1, h] = gw
    e = e.astype(F32)
    stats[0, h : h + 1] = top
    stats[1, h : h + 1] = jnp.sum(e, axis=0, keepdims=True)
    stats[2, h : h + 1] = jnp.sum(e * gw.astype(F32), axis=0, keepdims=True)


def partial_stats(scores, gw, stats, h):
    top = jnp.max(scores, axis=0, keepdims=True)
    e = jnp.exp(scores - top)
    stats[0, h : h + 1] = top
    stats[1, h : h + 1] = jnp.sum(e, axis=0, keepdims=True)
    stats[2, h : h + 1] = jnp.sum(e * gw, axis=0, keepdims=True)


def local_stats_kernel(scale, pos_ref, k_ref, v_ref, q_ref, dg_ref, sib, x_ref, x_sib, stats, live, near, far, rows_x, wide, sems, x_sems):
    slots, half = sib.shape[1], sib.shape[2]
    width = half // 2
    core = here()[0]
    own, other = slice(0, slots), slice(slots, 2 * slots)
    stages = []
    for g, pair in enumerate((near, far)):
        cols = slice(g * width, (g + 1) * width)
        held = pl.ds(pl.multiple_of(core * half + g * width, HEAD), width)
        copies = [
            pltpu.make_async_copy(ref.at[0, :, held], pair.at[j, own], sems.at[8 * g + j])
            for j, ref in enumerate((k_ref, v_ref, q_ref))
        ]
        copies.append(pltpu.make_async_copy(dg_ref.at[0, :, held], wide.at[:, cols], sems.at[8 * g + 3]))
        for j in range(4):
            copies.append(pltpu.make_async_copy(sib.at[j, :, cols], pair.at[j, other], sems.at[8 * g + 4 + j]))
        for c in copies:
            c.start()
        stages.append(copies)
    x_copies = []
    depth = x_ref.shape[2] // 2
    for i, ref in enumerate((x_ref, x_sib)):
        for g in range(2):
            cols = slice(g * depth, (g + 1) * depth)
            x_copies.append(pltpu.make_async_copy(ref.at[0, :, cols], rows_x.at[i, :, cols], x_sems.at[2 * i + g]))
    for c in x_copies:
        c.start()
    rows_live = live_rows(pos_ref, slots)
    mask = None
    for g, pair in enumerate((near, far)):
        cols = slice(g * width, (g + 1) * width)
        for c in stages[g]:
            c.wait()
        pair[0, own] = mark_dead(pair[0, own], rows_live)
        pair[3, own] = wide[:, cols].astype(BF16)
        if mask is None:
            mask = local_mask(core, pair)
            marks = nt(jnp.ones((8, HEAD), BF16), pair[0, :, :HEAD])[0:1]
            live[...] = jnp.where(marks < MARK_LIMIT, 1.0, 0.0)
        for h in range(width // HEAD):
            at = slice(h * HEAD, (h + 1) * HEAD)
            scores = jnp.where(mask, nt(pair[0, :, at], pair[2, :, at]) * scale, NEG_FILL)
            partial_stats(scores, nt(pair[1, :, at], pair[3, :, at]), stats, g * width // HEAD + h)
    for c in x_copies:
        c.wait()


def local_stats(route_pos, keys, values, queries, d_gated, sib, x_routed, x_sib):
    _, slots, half = sib.shape
    heads = half // HEAD
    anywhere = pl.BlockSpec(memory_space=pl.ANY)
    return pl.pallas_call(
        functools.partial(local_stats_kernel, HEAD**-0.5),
        out_shape=[
            jax.ShapeDtypeStruct((3, heads, 2 * slots), F32),
            jax.ShapeDtypeStruct((1, 2 * slots), F32),
            pltpu.VMEM((4, 2 * slots, half // 2), BF16),
            pltpu.VMEM((4, 2 * slots, half // 2), BF16),
            pltpu.VMEM((2, slots, x_routed.shape[2]), BF16),
        ],
        in_specs=[VMEM] + [anywhere] * 7,
        out_specs=[VMEM] * 5,
        scratch_shapes=[pltpu.VMEM((slots, half), F32), pltpu.SemaphoreType.DMA((16,)), pltpu.SemaphoreType.DMA((4,))],
        compiler_params=params(),
        cost_estimate=cost(16 * slots * slots * half, 16 * slots * half, 4 * slots * slots * half // HEAD),
        name="local_stats",
    )(route_pos, *in_hbm(keys, values, queries, d_gated), sib, x_routed, x_sib)


def cross_stats_kernel(scale, near, far, straight, diag, cross, stats, kept):
    slots, width = straight.shape[1], straight.shape[2]
    chip = here()[1]
    top, bottom = slice(0, slots), slice(slots, 2 * slots)

    @pl.when(chip == 0)
    def _():
        for part in range(2):
            cross[part] = far[part]
            cross[2 + part, top] = straight[part]
            cross[2 + part, bottom] = diag[part]

    @pl.when(chip != 0)
    def _():
        for part in range(2):
            cross[part, top] = straight[part]
            cross[part, bottom] = diag[part]
            cross[2 + part] = near[2 + part]

    live = cross[0, :, :HEAD].astype(F32) < MARK_LIMIT
    mask = jnp.concatenate([live] * (2 * slots // HEAD), axis=1)
    heads = width // HEAD
    for h in range(heads):
        cols = slice(h * HEAD, (h + 1) * HEAD)
        scores = jnp.where(mask, nt(cross[0, :, cols], cross[2, :, cols]) * scale, NEG_FILL)
        kept_stats(scores, nt(cross[1, :, cols], cross[3, :, cols]), kept, stats, h)


def cross_stats(near, far, straight, diag):
    _, slots, width = straight.shape
    heads = width // HEAD
    return pl.pallas_call(
        functools.partial(cross_stats_kernel, HEAD**-0.5),
        out_shape=[
            pltpu.VMEM((4, 2 * slots, width), BF16),
            jax.ShapeDtypeStruct((3, heads, 2 * slots), F32),
            pltpu.VMEM((2, heads, 2 * slots, 2 * slots), BF16),
        ],
        in_specs=[VMEM] * 4,
        out_specs=[VMEM] * 3,
        compiler_params=params(),
        cost_estimate=cost(16 * slots * slots * width, 32 * slots * width, 4 * slots * slots * heads),
        name="cross_stats",
    )(near, far, straight, diag)


NONE = (-3e38, 0.0, 0.0)


def merge(first, second):
    top = jnp.maximum(first[0], second[0])
    a, b = jnp.exp(first[0] - top), jnp.exp(second[0] - top)
    inverse = 1.0 / (first[1] * a + second[1] * b)
    return a * inverse, (first[2] * a + second[2] * b) * inverse


def choose(flag, yes, no):
    return [jnp.where(flag, y, n) for y, n in zip(yes, no)]


def gradients(q, k, dg, e, gw, scale, factor, delta):
    weights = e * factor
    ds = (weights * ((gw - delta) * scale)).astype(BF16)
    return tn(ds, k), nn(ds, q), nn(weights.astype(BF16), dg)


def local_gradients(pair, h, mask, scale, top, factor, delta):
    cols = slice(h * HEAD, (h + 1) * HEAD)
    k, v, q, dg = [pair[i, :, cols] for i in range(4)]
    e = jnp.exp(jnp.where(mask, nt(k, q) * scale, NEG_FILL) - top)
    return gradients(q, k, dg, e, nt(v, dg), scale, factor, delta)


def near_grad_kernel(scale, pair, local, stats, gates, dq_out, own_out, sib_out, sum_out):
    slots, width = own_out.shape[1], own_out.shape[2]
    heads = width // HEAD
    first = here()[1] == 0
    near = [local[i, :heads] for i in range(3)]
    factor, delta = merge(near, choose(first, NONE, [stats[i] for i in range(3)]))
    factor = factor * gates[...]
    sum_out[...] = jnp.sum(delta, axis=0, keepdims=True)
    mask = local_mask(here()[0], pair)
    for h in range(heads):
        cols = slice(h * HEAD, (h + 1) * HEAD)
        row = slice(h, h + 1)
        dq, dk, dv = local_gradients(pair, h, mask, scale, near[0][row], factor[row], delta[row])
        dq_out[:, cols] = dq
        for i, part in enumerate((dk, dv)):
            own_out[i, :, cols] = part[:slots].astype(BF16)
            sib_out[i, :, cols] = part[slots:].astype(BF16)


def near_grad(pair, local, stats, gates):
    _, rows, width = pair.shape
    slots = rows // 2
    out = pltpu.VMEM((2, slots, width), BF16)
    return pl.pallas_call(
        functools.partial(near_grad_kernel, HEAD**-0.5),
        out_shape=[pltpu.VMEM((2 * slots, width), F32), out, out, jax.ShapeDtypeStruct(gates.shape, F32)],
        in_specs=[VMEM] * 4,
        out_specs=[VMEM] * 4,
        compiler_params=params(),
        cost_estimate=cost(20 * slots * slots * width, 40 * slots * width),
        name="near_grad",
    )(pair, local, stats, gates)


def put_terms(grad, rows_x, out_ref):
    high = grad.astype(BF16)
    rest = grad - high.astype(F32)
    mid = rest.astype(BF16)
    low = (rest - mid.astype(F32)).astype(BF16)
    slots = rows_x.shape[1]
    row = lax.broadcasted_iota(jnp.int32, (8, grad.shape[1]), 0)
    lhs = jnp.where(row == 0, high.astype(F32), jnp.where(row == 1, mid.astype(F32), jnp.where(row == 2, low.astype(F32), 0.0)))
    lhs = lhs.astype(BF16)
    term = jnp.sum(nn(lhs[:, :slots], rows_x[0]) + nn(lhs[:, slots:], rows_x[1]), axis=0, keepdims=True)
    parts, copies, _, chunk = out_ref.shape
    for j in range(parts):
        for i in range(copies):
            out_ref[j, i] = term[:, j * chunk : (j + 1) * chunk]


def cross_grad_kernel(scale, total, cross, kept, stats, local, heard, gates, near_dq, near_sum, rows_x, straight, diag, dq_out, keep, final, terms, held, sem):
    slots, width = straight.shape[1], straight.shape[2]
    heads = width // HEAD
    first = here()[1] == 0
    late = jnp.where(first, 0.0, 1.0)
    mine = [stats[i] for i in range(3)]
    other = [heard[i] for i in range(3)]
    near = [local[i, :heads] for i in range(3)]
    far = [local[i, heads:] for i in range(3)]
    factor, delta = merge(mine, choose(first, other, near))
    factor = factor * jnp.where(first, heard[3], jnp.broadcast_to(gates[...], factor.shape))
    final[0], final[1] = merge(far, choose(first, NONE, other))
    sums = near_sum[...] + jnp.sum(final[1], axis=0, keepdims=True)
    put_terms(sums * gates[...] * (1.0 - gates[...]) * (1.0 / total), rows_x, held)
    leaving = pltpu.make_async_copy(held, terms, sem)
    leaving.start()
    for h in range(heads):
        cols = slice(h * HEAD, (h + 1) * HEAD)
        row = slice(h, h + 1)
        dq, dk, dv = gradients(
            cross[2, :, cols], cross[0, :, cols], cross[3, :, cols],
            kept[0, h].astype(F32), kept[1, h].astype(F32), scale, factor[row], delta[row],
        )
        dq_out[:, cols] = (near_dq[:, cols] + late * dq).astype(BF16)
        keep[0, :, cols] = dk.astype(BF16)
        keep[1, :, cols] = dv.astype(BF16)
        sent = jnp.where(first, dq, dk).astype(BF16)
        straight[0, :, cols] = sent[:slots]
        diag[0, :, cols] = sent[slots:]
        straight[1, :, cols] = dv[:slots].astype(BF16)
        diag[1, :, cols] = dv[slots:].astype(BF16)
    leaving.wait()


def cross_grad(cross, kept, stats, local, heard, gates, near_dq, near_sum, rows_x, parts, copies, total):
    _, rows, width = cross.shape
    slots = rows // 2
    out = pltpu.VMEM((2, slots, width), BF16)
    spread = (parts, copies, 1, rows_x.shape[2] // parts)
    return pl.pallas_call(
        functools.partial(cross_grad_kernel, HEAD**-0.5, total),
        out_shape=[
            out,
            out,
            pltpu.VMEM((rows, width), BF16),
            pltpu.VMEM((2, rows, width), BF16),
            jax.ShapeDtypeStruct((2, width // HEAD, rows), F32),
            pltpu.HBM(spread, F32),
        ],
        in_specs=[VMEM] * 9,
        out_specs=[VMEM] * 5 + [pl.BlockSpec(memory_space=pltpu.HBM)],
        scratch_shapes=[pltpu.VMEM(spread, F32), pltpu.SemaphoreType.DMA],
        compiler_params=params(),
        cost_estimate=cost(24 * slots * slots * width, 64 * slots * width),
        name="cross_grad",
    )(cross, kept, stats, local, heard, gates, near_dq, near_sum, rows_x)


def far_grad_kernel(scale, pair, local, final, gates, keep, near_dq, near_own, near_sib, own_out, sib_out):
    slots, width = pair.shape[1] // 2, pair.shape[2]
    heads = width // HEAD
    early = jnp.where(here()[1] == 0, 1.0, 0.0)
    factor = final[0] * gates[...]
    mask = local_mask(here()[0], pair)
    own_out[0, :, :width] = near_dq[:slots]
    sib_out[0, :, :width] = near_dq[slots:]
    for i in range(2):
        own_out[1 + i, :, :width] = near_own[i]
        sib_out[1 + i, :, :width] = near_sib[i]
    for h in range(heads):
        cols = slice(width + h * HEAD, width + (h + 1) * HEAD)
        at = slice(h * HEAD, (h + 1) * HEAD)
        row = slice(h, h + 1)
        top = local[0, heads + h : heads + h + 1]
        dq, dk, dv = local_gradients(pair, h, mask, scale, top, factor[row], final[1, row])
        dk = dk + early * keep[0, :, at].astype(F32)
        dv = dv + early * keep[1, :, at].astype(F32)
        for i, part in enumerate((dq, dk, dv)):
            own_out[i, :, cols] = part[:slots].astype(BF16)
            sib_out[i, :, cols] = part[slots:].astype(BF16)


def far_grad(pair, local, final, gates, keep, near_dq, near_own, near_sib):
    _, rows, width = pair.shape
    slots, half = rows // 2, 2 * width
    out = jax.ShapeDtypeStruct((3, slots, half), BF16)
    return pl.pallas_call(
        functools.partial(far_grad_kernel, HEAD**-0.5),
        out_shape=[out, out],
        in_specs=[VMEM] * 8,
        out_specs=[VMEM] * 2,
        compiler_params=params(),
        cost_estimate=cost(20 * slots * slots * half, 40 * slots * half),
        name="far_grad",
    )(pair, local, final, gates, keep, near_dq, near_own, near_sib)


def own_join_kernel(own, dq_out, dk_out, dv_out, waiting, total, sems):
    slots, half = own.shape[1], own.shape[2]
    width = half // 2
    core, chip = here()
    cols = pl.ds(pl.multiple_of(core * half, HEAD), half)
    stores = []
    for j, out in enumerate((dq_out, dk_out, dv_out)):
        total[j] = own[j].astype(F32)
        stores.append(pltpu.make_async_copy(total.at[j], out.at[0, :, cols], sems.at[j]))
        stores[-1].start()
    waiting[0] = jnp.where(chip == 0, total[1, :, :width], total[0, :, width:]).astype(BF16)
    waiting[1] = own[2, :, :width]
    for c in stores:
        c.wait()


def own_join(own, shape):
    out = pltpu.HBM(shape, F32)
    _, slots, half = own.shape
    hbm = pl.BlockSpec(memory_space=pltpu.HBM)
    return pl.pallas_call(
        own_join_kernel,
        out_shape=[out] * 3 + [jax.ShapeDtypeStruct((2, slots, half // 2), BF16)],
        in_specs=[VMEM],
        out_specs=[hbm] * 3 + [VMEM],
        scratch_shapes=[pltpu.VMEM((3, slots, half), F32), pltpu.SemaphoreType.DMA((3,))],
        compiler_params=params(),
        cost_estimate=cost(0, 18 * own.size),
        name="own_join",
    )(own)


def sib_join_kernel(sib, dq_in, dk_in, dv_in, dq_out, dk_out, dv_out, waiting, low, total, in_sems, out_sems):
    half = sib.shape[2]
    width = half // 2
    core, chip = here()
    loads = [pltpu.make_async_copy(sib.at[j], low.at[j], in_sems.at[j]) for j in range(3)]
    for c in loads:
        c.start()
    cols = pl.ds(pl.multiple_of((1 - core) * half, HEAD), half)
    stores = []
    for j, out in enumerate((dq_out, dk_out, dv_out)):
        loads[j].wait()
        total[j] = low[j].astype(F32)
        stores.append(pltpu.make_async_copy(total.at[j], out.at[0, :, cols], out_sems.at[j]))
        stores[-1].start()
    waiting[0] = jnp.where(chip == 0, total[1, :, :width], total[0, :, width:]).astype(BF16)
    waiting[1] = low[2, :, :width]
    for c in stores:
        c.wait()


def sib_join(sib, outs):
    _, slots, half = sib.shape
    hbm = pl.BlockSpec(memory_space=pltpu.HBM)
    return pl.pallas_call(
        sib_join_kernel,
        out_shape=[pltpu.HBM(o.shape, F32) for o in outs] + [pltpu.VMEM((2, slots, half // 2), BF16)],
        in_specs=[pl.BlockSpec(memory_space=pl.ANY)] + [hbm] * 3,
        out_specs=[hbm] * 3 + [VMEM],
        scratch_shapes=[
            pltpu.VMEM((3, slots, half), BF16),
            pltpu.VMEM((3, slots, half), F32),
            pltpu.SemaphoreType.DMA((3,)),
            pltpu.SemaphoreType.DMA((3,)),
        ],
        input_output_aliases={1: 0, 2: 1, 3: 2},
        compiler_params=params(),
        cost_estimate=cost(0, 12 * sib.size),
        name="sib_join",
    )(sib, *in_hbm(*outs))


def add_back_kernel(own, sib, straight, diag, dq_in, dk_in, dv_in, dq_out, dk_out, dv_out, total, sems):
    width = straight.shape[2]
    core, chip = here()
    ends = ((own, straight, 2 * core * width), (sib, diag, 2 * (1 - core) * width))

    def store(i, j, out, offset):
        cols = pl.ds(pl.multiple_of(ends[i][2] + offset, HEAD), width)
        copy = pltpu.make_async_copy(total.at[i, j], out.at[0, :, cols], sems.at[2 * i + j])
        copy.start()
        return copy

    @pl.when(chip == 0)
    def _():
        copies = []
        for i, (waiting, back, _) in enumerate(ends):
            for j, out in enumerate((dk_out, dv_out)):
                total[i, j] = waiting[j].astype(F32) + back[j].astype(F32)
                copies.append(store(i, j, out, 0))
        for c in copies:
            c.wait()

    @pl.when(chip != 0)
    def _():
        copies = []
        for i, (waiting, back, _) in enumerate(ends):
            total[i, 0] = waiting[0].astype(F32) + back[0].astype(F32)
            copies.append(store(i, 0, dq_out, width))
        for c in copies:
            c.wait()


def add_back(own, sib, straight, diag, outs):
    hbm = pl.BlockSpec(memory_space=pltpu.HBM)
    return pl.pallas_call(
        add_back_kernel,
        out_shape=[pltpu.HBM(o.shape, F32) for o in outs],
        in_specs=[VMEM] * 4 + [hbm] * 3,
        out_specs=[hbm] * 3,
        scratch_shapes=[pltpu.VMEM((2, *own.shape), F32), pltpu.SemaphoreType.DMA((4,))],
        input_output_aliases={4: 0, 5: 1, 6: 2},
        compiler_params=params(),
        cost_estimate=cost(0, 24 * own.size),
        name="add_back",
    )(own, sib, straight, diag, *in_hbm(*outs))


def swap_body(route_pos, x_routed, w_router, queries, keys, values, d_gated):
    slots = queries.shape[1]
    n, ndp = lax.axis_size("ctx"), lax.axis_size("dp")

    def send(a, flip):
        return lax.ppermute(a, "ctx", [(i, i ^ flip) for i in range(n)])

    def beside(fn, *operands):
        def skip(*ops):
            return jax.tree.map(lambda o: jnp.zeros(o.shape, o.dtype), jax.eval_shape(fn, *ops))

        return lax.cond(route_pos[0, 0] >= -1, fn, skip, *operands)

    def after(value, *others):
        return lax.optimization_barrier((value, *others))[0]

    def widen(part, step, *first):
        other = lax.ppermute(part, "dp", [(i, i ^ step) for i in range(ndp)])
        return jnp.concatenate([part, after(other, *first)], axis=1)

    def exchange_phase(x_routed, w_part, theirs):
        sib, x_sib = send(theirs, 1), send(x_routed, 1)
        step = 2
        while 2 * step < ndp:
            w_part = widen(w_part, step)
            step *= 2
        return sib, x_sib, w_part

    def far_phase(*operands):
        own_out, sib_out = far_grad(*operands)
        sib_in = send(sib_out, 1)
        *outs, waiting = own_join(own_out, queries.shape)
        return outs, waiting, sib_in

    out_s, out_d, w_part = cross_pack(route_pos, w_router, keys, values, queries, d_gated)
    in_s, in_d = send(out_s, 2), send(out_d, 3)

    theirs = sib_pack(after(route_pos, out_s), keys, values, queries, d_gated)
    if ndp > 1:
        w_part = widen(w_part, 1, theirs)
    sib, x_sib, w_part = beside(exchange_phase, x_routed, w_part, theirs)
    local, live, near, far, rows_x = local_stats(route_pos, keys, values, queries, d_gated, sib, x_routed, x_sib)
    cross, stats, kept = cross_stats(near, far, in_s, in_d)
    if ndp > 2:
        w_part = widen(w_part, ndp // 2, stats)
    gates, message = pair_gate(live, rows_x, w_part, local, stats, ndp)

    heard = send(message, 2)
    near_dq, near_own, near_sib, near_sum = near_grad(near, local, stats, gates)
    total = float(ndp * n * slots // 2)
    back_s, back_d, dq_low, keep, final, terms = cross_grad(
        cross, kept, stats, local, heard, gates, near_dq, near_sum, rows_x, ndp, n, total
    )

    ret_s, ret_d = send(back_s, 2), send(back_d, 3)
    shared = lax.all_to_all(terms.reshape(ndp * n, 1, -1), ("dp", "ctx"), 0, 0, tiled=True)
    outs, waiting, sib_in = beside(far_phase, far, local, final, gates, keep, dq_low, near_own, near_sib)
    *outs, waiting_sib = sib_join(sib_in, outs)
    dq, dk, dv = add_back(waiting, waiting_sib, ret_s, ret_d, outs)
    router_grad = jnp.sum(after(shared, dq), axis=(0, 1))
    return dq, dk, dv, router_grad


def body(route_pos, x_routed, w_router, queries, keys, values, d_gated):
    slots, full = queries.shape[1], queries.shape[2]
    n, ndp = lax.axis_size("ctx"), lax.axis_size("dp")
    chips = n // 2
    me, dp_me = lax.axis_index("ctx"), lax.axis_index("dp")
    core = (me % 2).astype(jnp.int32).reshape(1)
    half = full // 2
    groups = GROUPS if (half // HEAD) % GROUPS == 0 else 1
    width = half // groups

    sib_pairs = [(i, i ^ 1) for i in range(n)]

    def forward_pairs(step, flip):
        return [(i, (i + 2 * step) ^ flip) for i in range(n) if i + 2 * step < n]

    def back_pairs(step, flip):
        return [(b, a) for a, b in forward_pairs(step, flip)]

    def to_sib(a):
        return lax.ppermute(a, "ctx", sib_pairs)

    links = [(step, flip) for step in range(1, chips) for flip in (0, 1)]

    w_row = w_router.reshape(1, -1)
    w_parts = [w_row] + [
        lax.ppermute(w_row, "dp", [(i, (i + s) % ndp) for i in range(ndp)]) for s in range(1, ndp)
    ]
    live = (route_pos >= 0).astype(jnp.int32)
    lives = [live, to_sib(live)] + [lax.ppermute(live, "ctx", forward_pairs(*link)) for link in links]
    live_all = jnp.concatenate(lives, axis=0)

    kv_mine, kv_theirs = pack(core, keys, values, groups, width)
    kv_far = [
        [lax.ppermute((kv_theirs if flip else kv_mine)[g], "ctx", forward_pairs(step, flip)) for step, flip in links]
        for g in range(groups)
    ]
    q_mine, q_theirs = pack(core, queries, d_gated, groups, width)
    kv_sib = [to_sib(a) for a in kv_theirs]
    q_sib = [to_sib(a) for a in q_theirs]

    offsets = ((dp_me - jnp.arange(ndp)) % ndp).astype(jnp.int32)
    gate = router_gate(offsets, route_pos, x_routed, w_parts)
    gates = (gate, to_sib(gate))

    accs = (jnp.zeros((1, slots), F32), jnp.zeros((1, slots), F32))
    dq_own, sib_in, kv_own, back = [], [], [], []
    for g in range(groups):
        dq, sib_out, kv_local, kv_remote, accs = attention(
            core, live_all, gates, accs, q_mine[g], q_sib[g], [kv_mine[g], kv_sib[g], *kv_far[g]]
        )
        back.append([lax.ppermute(a, "ctx", back_pairs(*link)) for a, link in zip(kv_remote, links)])
        sib_in.append(to_sib(sib_out))
        dq_own.append(dq)
        kv_own.append(kv_local)

    targets = ((dp_me + jnp.arange(ndp)) % ndp).astype(jnp.int32)
    terms = router_terms(targets, gate, accs[0], to_sib(accs[1]), x_routed, ndp)
    mine = terms[0]
    for s in range(1, ndp):
        mine = mine + lax.ppermute(terms[s], "dp", [(i, (i + s) % ndp) for i in range(ndp)])
    total = mine
    for s in range(1, n):
        total = total + lax.ppermute(mine, "ctx", [(i, (i + s) % n) for i in range(n)])
    router_grad = total[0] / float(ndp * n * slots // 2)

    dq, dk, dv = combine(core, dq_own, sib_in, kv_own, back, queries.shape)
    return dq, dk, dv, router_grad


def solution(mesh):
    placed = (
        P("dp", "ctx"),
        P("dp", "ctx", None),
        P("dp"),
        P("dp", "ctx", None),
        P("dp", "ctx", None),
        P("dp", "ctx", None),
        P("dp", "ctx", None),
    )
    ndp = mesh.shape["dp"]
    paired = mesh.shape["ctx"] == 4 and ndp & (ndp - 1) == 0
    return jax.shard_map(
        swap_body if paired else body,
        mesh=mesh,
        in_specs=placed,
        out_specs=(P("dp", "ctx", None), P("dp", "ctx", None), P("dp", "ctx", None), P("dp")),
        check_vma=False,
    )
```

```python
import functools

import jax
import jax.numpy as jnp
from jax import lax
from jax.experimental import pallas as pl
from jax.experimental.pallas import tpu as pltpu
from jax.sharding import PartitionSpec as P

HEAD = 128
GROUPS = 4
NEG_FILL = -1e30
MIB = 1024 * 1024
BF16 = jnp.bfloat16
F32 = jnp.float32

VMEM = pl.BlockSpec(memory_space=pltpu.VMEM)
SMEM = pl.BlockSpec(memory_space=pltpu.SMEM)


def params(mib=16):
    return pltpu.CompilerParams(vmem_limit_bytes=mib * MIB)


def cost(flops, nbytes, exps=0):
    return pl.CostEstimate(flops=1, bytes_accessed=1, transcendentals=0)


def in_hbm(*arrays):
    return [pltpu.with_memory_space_constraint(a, pltpu.HBM) for a in arrays]


def nt(a, b):
    return lax.dot_general(a, b, (((1,), (1,)), ((), ())), preferred_element_type=F32)


def nn(a, b):
    return lax.dot_general(a, b, (((1,), (0,)), ((), ())), preferred_element_type=F32)


def tn(a, b):
    return lax.dot_general(a, b, (((0,), (0,)), ((), ())), preferred_element_type=F32)


def pack_kernel(groups, width, core_ref, first_ref, second_ref, *outs):
    half = first_ref.shape[-1] // 2
    core = core_ref[0]
    for side in range(2):
        base = (core if side == 0 else 1 - core) * half
        for g in range(groups):
            out = outs[side * groups + g]
            cols = pl.ds(pl.multiple_of(base + g * width, HEAD), width)
            out[0] = first_ref[0, :, cols].astype(BF16)
            out[1] = second_ref[0, :, cols].astype(BF16)


def pack(core, first, second, groups, width):
    slots = first.shape[1]
    out = jax.ShapeDtypeStruct((2, slots, width), BF16)
    res = pl.pallas_call(
        functools.partial(pack_kernel, groups, width),
        out_shape=[out] * (2 * groups),
        in_specs=[SMEM, VMEM, VMEM],
        out_specs=[VMEM] * (2 * groups),
        compiler_params=params(),
        cost_estimate=cost(0, 2 * first.size * 4),
        name="pack",
    )(core, first, second)
    return res[:groups], res[groups:]


def gate_kernel(parts, offset_ref, pos_ref, x_ref, *refs):
    w_refs, out_ref = refs[:parts], refs[parts]
    chunk = w_refs[0].shape[-1]
    total = jnp.zeros((8, x_ref.shape[1]), F32)
    for s in range(parts):
        cols = pl.ds(pl.multiple_of(offset_ref[s] * chunk, HEAD), chunk)
        w_rows = jnp.broadcast_to(w_refs[s][...].astype(F32), (8, chunk)).astype(BF16)
        total = total + nt(w_rows, x_ref[0, :, cols])
    gate = 1.0 / (1.0 + jnp.exp(-total[0:1]))
    out_ref[...] = jnp.where(pos_ref[...] >= 0, gate, 0.0)


def router_gate(offsets, route_pos, x_routed, w_parts):
    parts = len(w_parts)
    return pl.pallas_call(
        functools.partial(gate_kernel, parts),
        out_shape=jax.ShapeDtypeStruct(route_pos.shape, F32),
        in_specs=[SMEM] + [VMEM] * (2 + parts),
        out_specs=VMEM,
        compiler_params=params(),
        cost_estimate=cost(16 * x_routed.size, x_routed.size * 2),
        name="router_gate",
    )(offsets, route_pos, x_routed, *w_parts)


def attention_kernel(remote, scale, core_ref, live_ref, gate_own, gate_sib, acc_own, acc_sib, q_own, q_sib, *refs):
    chunks = 2 + remote
    kv = refs[:chunks]
    outs = refs[chunks:]
    dq_own, sib_out, kv_own = outs[:3]
    kv_remote = outs[3 : 3 + remote]
    sum_own, sum_sib = outs[3 + remote :]
    slots, width = q_own.shape[1], q_own.shape[2]
    core = core_ref[0]
    key = lax.broadcasted_iota(jnp.int32, (slots, slots), 0)
    query = lax.broadcasted_iota(jnp.int32, (slots, slots), 1)
    counts = [jnp.sum(live_ref[i : i + 1], axis=1, keepdims=True) for i in range(chunks)]
    lives = [key < counts[i] for i in range(chunks)]
    own_later = core == 1
    bias_rows = []
    for i in range(chunks):
        live = lives[i]
        if i == 0:
            pair = (live & (key <= query), live & jnp.logical_not(own_later))
        elif i == 1:
            pair = (live & own_later, live & (key <= query))
        else:
            pair = (live, live)
        bias_rows.append(jnp.concatenate([jnp.where(p, 0.0, NEG_FILL) for p in pair], axis=1))
    bias = jnp.concatenate(bias_rows, axis=0)
    gates = jnp.concatenate([gate_own[...], gate_sib[...]], axis=1)
    total = jnp.zeros((1, 2 * slots), F32)
    for h in range(width // HEAD):
        cols = slice(h * HEAD, (h + 1) * HEAD)
        q = jnp.concatenate([q_own[0, :, cols], q_sib[0, :, cols]], axis=0)
        dg = jnp.concatenate([q_own[1, :, cols], q_sib[1, :, cols]], axis=0)
        k = jnp.concatenate([r[0, :, cols] for r in kv], axis=0)
        v = jnp.concatenate([r[1, :, cols] for r in kv], axis=0)
        scores = nt(k, q) * scale + bias
        top = jnp.max(scores, axis=0, keepdims=True)
        e = jnp.exp(scores - top)
        inverse = 1.0 / jnp.sum(e, axis=0, keepdims=True)
        gw = nt(v, dg)
        delta = jnp.sum(e * gw, axis=0, keepdims=True) * inverse
        total = total + delta
        weights = e * (inverse * gates)
        dv = nn(weights.astype(BF16), dg)
        ds = (weights * ((gw - delta) * scale)).astype(BF16)
        dk = nn(ds, q)
        dq = tn(ds, k)
        dq_own[:, cols] = dq[:slots].astype(dq_own.dtype)
        sib_out[0, :, cols] = dq[slots:].astype(BF16)
        kv_own[0, :, cols] = dk[:slots].astype(BF16)
        kv_own[1, :, cols] = dv[:slots].astype(BF16)
        sib_out[1, :, cols] = dk[slots : 2 * slots].astype(BF16)
        sib_out[2, :, cols] = dv[slots : 2 * slots].astype(BF16)
        for i in range(remote):
            rows = slice((2 + i) * slots, (3 + i) * slots)
            kv_remote[i][0, :, cols] = dk[rows].astype(BF16)
            kv_remote[i][1, :, cols] = dv[rows].astype(BF16)
    sum_own[...] = acc_own[...] + total[:, :slots]
    sum_sib[...] = acc_sib[...] + total[:, slots:]


def attention(core, live, gates, accs, q_own, q_sib, kv):
    remote = len(kv) - 2
    _, slots, width = q_own.shape
    pair = jax.ShapeDtypeStruct((2, slots, width), BF16)
    row = jax.ShapeDtypeStruct((1, slots), F32)
    outs = [
        jax.ShapeDtypeStruct((slots, width), BF16),
        jax.ShapeDtypeStruct((3, slots, width), BF16),
        pair,
        *([pair] * remote),
        row,
        row,
    ]
    keys = (2 + remote) * slots
    res = pl.pallas_call(
        functools.partial(attention_kernel, remote, HEAD**-0.5),
        out_shape=outs,
        in_specs=[SMEM] + [VMEM] * (7 + len(kv)),
        out_specs=[VMEM] * len(outs),
        compiler_params=params(48),
        cost_estimate=cost(20 * slots * keys * width, 8 * keys * width + 20 * slots * width, 2 * slots * keys * width // HEAD),
        name="attention",
    )(core, live, *gates, *accs, q_own, q_sib, *kv)
    return res[0], res[1], res[2], res[3 : 3 + remote], (res[3 + remote], res[4 + remote])


def combine_kernel(groups, width, remote, core_ref, *refs):
    dq_own, sib, kv_own = refs[:groups], refs[groups : 2 * groups], refs[2 * groups : 3 * groups]
    back = refs[3 * groups : 3 * groups + groups * remote]
    dq_out, dk_out, dv_out = refs[3 * groups + groups * remote :]
    half = groups * width
    core = core_ref[0]
    for g in range(groups):
        own = pl.ds(pl.multiple_of(core * half + g * width, HEAD), width)
        other = pl.ds(pl.multiple_of((1 - core) * half + g * width, HEAD), width)
        dq_out[0, :, own] = dq_own[g][...].astype(F32)
        dq_out[0, :, other] = sib[g][0].astype(F32)
        for i, out in enumerate((dk_out, dv_out)):
            mine = kv_own[g][i].astype(F32)
            theirs = sib[g][1 + i].astype(F32)
            for r in range(remote):
                part = back[g * remote + r][i].astype(F32)
                if r % 2 == 0:
                    mine = mine + part
                else:
                    theirs = theirs + part
            out[0, :, own] = mine
            out[0, :, other] = theirs


def combine(core, dq_own, sib, kv_own, back, shape):
    groups = len(dq_own)
    remote = len(back[0])
    out = jax.ShapeDtypeStruct(shape, F32)
    flat = [*dq_own, *sib, *kv_own, *(b for group in back for b in group)]
    return pl.pallas_call(
        functools.partial(combine_kernel, groups, dq_own[0].shape[-1], remote),
        out_shape=[out] * 3,
        in_specs=[SMEM] + [VMEM] * len(flat),
        out_specs=[VMEM] * 3,
        compiler_params=params(48),
        cost_estimate=cost(0, 3 * out.size * 6),
        name="combine",
    )(core, *flat)


def router_kernel(parts, target_ref, gate_ref, own_ref, sib_ref, x_ref, *outs):
    gate = gate_ref[...]
    grad = (own_ref[...] + sib_ref[...]) * gate * (1.0 - gate)
    high = grad.astype(BF16)
    rest = grad - high.astype(F32)
    mid = rest.astype(BF16)
    low = (rest - mid.astype(F32)).astype(BF16)
    row = lax.broadcasted_iota(jnp.int32, (8, grad.shape[1]), 0)
    lhs = jnp.where(row == 0, high.astype(F32), jnp.where(row == 1, mid.astype(F32), jnp.where(row == 2, low.astype(F32), 0.0)))
    lhs = lhs.astype(BF16)
    chunk = outs[0].shape[-1]
    for s in range(parts):
        cols = pl.ds(pl.multiple_of(target_ref[s] * chunk, HEAD), chunk)
        outs[s][...] = jnp.sum(nn(lhs, x_ref[0, :, cols]), axis=0, keepdims=True)


def router_terms(targets, gate, own, sib, x_routed, parts):
    chunk = x_routed.shape[-1] // parts
    return pl.pallas_call(
        functools.partial(router_kernel, parts),
        out_shape=[jax.ShapeDtypeStruct((1, chunk), F32)] * parts,
        in_specs=[SMEM] + [VMEM] * 4,
        out_specs=[VMEM] * parts,
        compiler_params=params(),
        cost_estimate=cost(16 * x_routed.size, x_routed.size * 2),
        name="router_terms",
    )(targets, gate, own, sib, x_routed)


def here():
    me = lax.axis_index("ctx")
    return lax.rem(me, 2), lax.div(me, 2)


MARK = 2.0**60
MARK_LIMIT = 2.0**50


def live_rows(pos_ref, slots):
    count = jnp.sum((pos_ref[...] >= 0).astype(jnp.int32), axis=1, keepdims=True)
    return lax.broadcasted_iota(jnp.int32, (slots, HEAD), 0) < count


def mark_dead(keys, live):
    width = keys.shape[-1]
    mask = jnp.concatenate([live] * (width // HEAD), axis=1)
    return jnp.where(mask, keys.astype(F32), MARK).astype(BF16)


def cross_pack_kernel(pos_any, w_any, k_ref, v_ref, q_ref, dg_ref, straight, diag, w_out, wide, pos_ref, w_ref, sems):
    small = [pltpu.make_async_copy(pos_any, pos_ref, sems.at[4]), pltpu.make_async_copy(w_any, w_ref, sems.at[5])]
    for c in small:
        c.start()
    slots, width = straight.shape[1], straight.shape[2]
    half = k_ref.shape[-1] // 2
    core, chip = here()
    ends = ((straight, core * half), (diag, (1 - core) * half))

    def copies(first, second, targets, offset):
        out = []
        for i, (end, start) in enumerate(ends):
            cols = pl.ds(pl.multiple_of(start + offset, HEAD), width)
            out.append(pltpu.make_async_copy(first.at[0, :, cols], end.at[0], sems.at[2 * i]))
            out.append(pltpu.make_async_copy(second.at[0, :, cols], targets[i], sems.at[2 * i + 1]))
        for c in out:
            c.start()
        for c in out:
            c.wait()

    @pl.when(chip == 0)
    def _():
        copies(k_ref, v_ref, (straight.at[1], diag.at[1]), 0)
        small[0].wait()
        live = live_rows(pos_ref, slots)
        for end, _ in ends:
            end[0] = mark_dead(end[0], live)

    @pl.when(chip != 0)
    def _():
        copies(q_ref, dg_ref, (wide.at[0], wide.at[1]), width)
        small[0].wait()
        for i, (end, _) in enumerate(ends):
            end[1] = wide[i].astype(BF16)

    small[1].wait()
    w_out[...] = w_ref[...].astype(F32).reshape(w_out.shape)


def cross_pack(route_pos, w_router, keys, values, queries, d_gated):
    _, slots, full = keys.shape
    cross = pltpu.VMEM((2, slots, full // 4), BF16)
    hbm = pl.BlockSpec(memory_space=pltpu.HBM)
    return pl.pallas_call(
        cross_pack_kernel,
        out_shape=[cross, cross, jax.ShapeDtypeStruct((1, w_router.shape[0]), F32)],
        in_specs=[hbm] * 6,
        out_specs=[VMEM] * 3,
        scratch_shapes=[
            pltpu.VMEM((2, slots, full // 4), F32),
            pltpu.VMEM(route_pos.shape, jnp.int32),
            pltpu.VMEM(w_router.shape, BF16),
            pltpu.SemaphoreType.DMA((6,)),
        ],
        compiler_params=params(),
        cost_estimate=cost(0, 10 * slots * full),
        name="cross_pack",
    )(*in_hbm(route_pos, w_router, keys, values, queries, d_gated))


def sib_pack_kernel(pos_ref, k_ref, v_ref, q_ref, dg_ref, out, wide, sems):
    slots, half = out.shape[1], out.shape[2]
    cols = pl.ds(pl.multiple_of((1 - here()[0]) * half, HEAD), half)
    sources = ((k_ref, out.at[0]), (dg_ref, wide), (v_ref, out.at[1]), (q_ref, out.at[2]))
    copies = [pltpu.make_async_copy(src.at[0, :, cols], dst, sems.at[i]) for i, (src, dst) in enumerate(sources)]
    for c in copies:
        c.start()
    live = live_rows(pos_ref, slots)
    copies[0].wait()
    out[0] = mark_dead(out[0], live)
    copies[1].wait()
    out[3] = wide[...].astype(BF16)
    copies[2].wait()
    copies[3].wait()


def sib_pack(route_pos, keys, values, queries, d_gated):
    _, slots, full = keys.shape
    hbm = pl.BlockSpec(memory_space=pltpu.HBM)
    return pl.pallas_call(
        sib_pack_kernel,
        out_shape=pltpu.VMEM((4, slots, full // 2), BF16),
        in_specs=[VMEM, hbm, hbm, hbm, hbm],
        out_specs=VMEM,
        scratch_shapes=[pltpu.VMEM((slots, full // 2), F32), pltpu.SemaphoreType.DMA((4,))],
        compiler_params=params(),
        cost_estimate=cost(0, 20 * slots * full),
        name="sib_pack",
    )(route_pos, *in_hbm(keys, values, queries, d_gated))


def pair_gate_kernel(parts, live_ref, rows_x, w_ref, local, stats, out_ref, message):
    chunk = w_ref.shape[1] // parts
    slots = rows_x.shape[1]
    for i in range(2):
        total = jnp.zeros((8, slots), F32)
        for j in range(parts):
            w_rows = jnp.broadcast_to(w_ref[:, j * chunk : (j + 1) * chunk], (8, chunk)).astype(BF16)
            cols = pl.ds(pl.multiple_of((lax.axis_index("dp") ^ j) * chunk, HEAD), chunk)
            total = total + nt(w_rows, rows_x[i, :, cols])
        lanes = slice(i * slots, (i + 1) * slots)
        out_ref[:, lanes] = live_ref[:, lanes] / (1.0 + jnp.exp(-total[0:1]))
    first = here()[1] == 0
    heads = stats.shape[1]
    for i in range(3):
        message[i] = jnp.where(first, stats[i], local[i, heads:])
    message[3] = jnp.broadcast_to(out_ref[...], message.shape[1:])


def pair_gate(live, rows_x, w_full, local, stats, parts):
    _, heads, lanes = stats.shape
    return pl.pallas_call(
        functools.partial(pair_gate_kernel, parts),
        out_shape=[jax.ShapeDtypeStruct(live.shape, F32), jax.ShapeDtypeStruct((4, heads, lanes), F32)],
        in_specs=[VMEM] * 5,
        out_specs=[VMEM] * 2,
        compiler_params=params(),
        cost_estimate=cost(16 * rows_x.size, rows_x.size * 2),
        name="router_gate",
    )(live, rows_x, w_full, local, stats)


def local_mask(core, pair):
    slots = pair.shape[1] // 2
    key = lax.broadcasted_iota(jnp.int32, (slots, slots), 0)
    query = lax.broadcasted_iota(jnp.int32, (slots, slots), 1)
    causal = key <= query
    own_live = pair[0, :slots, :slots].astype(F32) < MARK_LIMIT
    sib_live = pair[0, slots:, :slots].astype(F32) < MARK_LIMIT
    own_rows = jnp.concatenate([own_live & causal, own_live & (core == 0)], axis=1)
    sib_rows = jnp.concatenate([sib_live & (core == 1), sib_live & causal], axis=1)
    return jnp.concatenate([own_rows, sib_rows], axis=0)


def kept_stats(scores, gw, kept, stats, h):
    top = jnp.max(scores, axis=0, keepdims=True)
    e = jnp.exp(scores - top).astype(BF16)
    gw = gw.astype(BF16)
    kept[0, h] = e
    kept[1, h] = gw
    e = e.astype(F32)
    stats[0, h : h + 1] = top
    stats[1, h : h + 1] = jnp.sum(e, axis=0, keepdims=True)
    stats[2, h : h + 1] = jnp.sum(e * gw.astype(F32), axis=0, keepdims=True)


def partial_stats(scores, gw, stats, h):
    top = jnp.max(scores, axis=0, keepdims=True)
    e = jnp.exp(scores - top)
    stats[0, h : h + 1] = top
    stats[1, h : h + 1] = jnp.sum(e, axis=0, keepdims=True)
    stats[2, h : h + 1] = jnp.sum(e * gw, axis=0, keepdims=True)


def local_stats_kernel(scale, pos_ref, k_ref, v_ref, q_ref, dg_ref, sib, x_ref, x_sib, stats, live, near, far, rows_x, wide, sems, x_sems):
    slots, half = sib.shape[1], sib.shape[2]
    width = half // 2
    core = here()[0]
    own, other = slice(0, slots), slice(slots, 2 * slots)
    stages = []
    for g, pair in enumerate((near, far)):
        cols = slice(g * width, (g + 1) * width)
        held = pl.ds(pl.multiple_of(core * half + g * width, HEAD), width)
        copies = [
            pltpu.make_async_copy(ref.at[0, :, held], pair.at[j, own], sems.at[8 * g + j])
            for j, ref in enumerate((k_ref, v_ref, q_ref))
        ]
        copies.append(pltpu.make_async_copy(dg_ref.at[0, :, held], wide.at[:, cols], sems.at[8 * g + 3]))
        for j in range(4):
            copies.append(pltpu.make_async_copy(sib.at[j, :, cols], pair.at[j, other], sems.at[8 * g + 4 + j]))
        for c in copies:
            c.start()
        stages.append(copies)
    x_copies = []
    depth = x_ref.shape[2] // 2
    for i, ref in enumerate((x_ref, x_sib)):
        for g in range(2):
            cols = slice(g * depth, (g + 1) * depth)
            x_copies.append(pltpu.make_async_copy(ref.at[0, :, cols], rows_x.at[i, :, cols], x_sems.at[2 * i + g]))
    for c in x_copies:
        c.start()
    rows_live = live_rows(pos_ref, slots)
    mask = None
    for g, pair in enumerate((near, far)):
        cols = slice(g * width, (g + 1) * width)
        for c in stages[g]:
            c.wait()
        pair[0, own] = mark_dead(pair[0, own], rows_live)
        pair[3, own] = wide[:, cols].astype(BF16)
        if mask is None:
            mask = local_mask(core, pair)
            marks = nt(jnp.ones((8, HEAD), BF16), pair[0, :, :HEAD])[0:1]
            live[...] = jnp.where(marks < MARK_LIMIT, 1.0, 0.0)
        for h in range(width // HEAD):
            at = slice(h * HEAD, (h + 1) * HEAD)
            scores = jnp.where(mask, nt(pair[0, :, at], pair[2, :, at]) * scale, NEG_FILL)
            partial_stats(scores, nt(pair[1, :, at], pair[3, :, at]), stats, g * width // HEAD + h)
    for c in x_copies:
        c.wait()


def local_stats(route_pos, keys, values, queries, d_gated, sib, x_routed, x_sib):
    _, slots, half = sib.shape
    heads = half // HEAD
    anywhere = pl.BlockSpec(memory_space=pl.ANY)
    return pl.pallas_call(
        functools.partial(local_stats_kernel, HEAD**-0.5),
        out_shape=[
            jax.ShapeDtypeStruct((3, heads, 2 * slots), F32),
            jax.ShapeDtypeStruct((1, 2 * slots), F32),
            pltpu.VMEM((4, 2 * slots, half // 2), BF16),
            pltpu.VMEM((4, 2 * slots, half // 2), BF16),
            pltpu.VMEM((2, slots, x_routed.shape[2]), BF16),
        ],
        in_specs=[VMEM] + [anywhere] * 7,
        out_specs=[VMEM] * 5,
        scratch_shapes=[pltpu.VMEM((slots, half), F32), pltpu.SemaphoreType.DMA((16,)), pltpu.SemaphoreType.DMA((4,))],
        compiler_params=params(),
        cost_estimate=cost(16 * slots * slots * half, 16 * slots * half, 4 * slots * slots * half // HEAD),
        name="local_stats",
    )(route_pos, *in_hbm(keys, values, queries, d_gated), sib, x_routed, x_sib)


def cross_stats_kernel(scale, near, far, straight, diag, cross, stats, kept):
    slots, width = straight.shape[1], straight.shape[2]
    chip = here()[1]
    top, bottom = slice(0, slots), slice(slots, 2 * slots)

    @pl.when(chip == 0)
    def _():
        for part in range(2):
            cross[part] = far[part]
            cross[2 + part, top] = straight[part]
            cross[2 + part, bottom] = diag[part]

    @pl.when(chip != 0)
    def _():
        for part in range(2):
            cross[part, top] = straight[part]
            cross[part, bottom] = diag[part]
            cross[2 + part] = near[2 + part]

    live = cross[0, :, :HEAD].astype(F32) < MARK_LIMIT
    mask = jnp.concatenate([live] * (2 * slots // HEAD), axis=1)
    heads = width // HEAD
    for h in range(heads):
        cols = slice(h * HEAD, (h + 1) * HEAD)
        scores = jnp.where(mask, nt(cross[0, :, cols], cross[2, :, cols]) * scale, NEG_FILL)
        kept_stats(scores, nt(cross[1, :, cols], cross[3, :, cols]), kept, stats, h)


def cross_stats(near, far, straight, diag):
    _, slots, width = straight.shape
    heads = width // HEAD
    return pl.pallas_call(
        functools.partial(cross_stats_kernel, HEAD**-0.5),
        out_shape=[
            pltpu.VMEM((4, 2 * slots, width), BF16),
            jax.ShapeDtypeStruct((3, heads, 2 * slots), F32),
            pltpu.VMEM((2, heads, 2 * slots, 2 * slots), BF16),
        ],
        in_specs=[VMEM] * 4,
        out_specs=[VMEM] * 3,
        compiler_params=params(),
        cost_estimate=cost(16 * slots * slots * width, 32 * slots * width, 4 * slots * slots * heads),
        name="cross_stats",
    )(near, far, straight, diag)


NONE = (-3e38, 0.0, 0.0)


def merge(first, second):
    top = jnp.maximum(first[0], second[0])
    a, b = jnp.exp(first[0] - top), jnp.exp(second[0] - top)
    inverse = 1.0 / (first[1] * a + second[1] * b)
    return a * inverse, (first[2] * a + second[2] * b) * inverse


def choose(flag, yes, no):
    return [jnp.where(flag, y, n) for y, n in zip(yes, no)]


def gradients(q, k, dg, e, gw, scale, factor, delta):
    weights = e * factor
    ds = (weights * ((gw - delta) * scale)).astype(BF16)
    return tn(ds, k), nn(ds, q), nn(weights.astype(BF16), dg)


def local_gradients(pair, h, mask, scale, top, factor, delta):
    cols = slice(h * HEAD, (h + 1) * HEAD)
    k, v, q, dg = [pair[i, :, cols] for i in range(4)]
    e = jnp.exp(jnp.where(mask, nt(k, q) * scale, NEG_FILL) - top)
    return gradients(q, k, dg, e, nt(v, dg), scale, factor, delta)


def near_grad_kernel(scale, pair, local, stats, gates, dq_out, own_out, sib_out, sum_out):
    slots, width = own_out.shape[1], own_out.shape[2]
    heads = width // HEAD
    first = here()[1] == 0
    near = [local[i, :heads] for i in range(3)]
    factor, delta = merge(near, choose(first, NONE, [stats[i] for i in range(3)]))
    factor = factor * gates[...]
    sum_out[...] = jnp.sum(delta, axis=0, keepdims=True)
    mask = local_mask(here()[0], pair)
    for h in range(heads):
        cols = slice(h * HEAD, (h + 1) * HEAD)
        row = slice(h, h + 1)
        dq, dk, dv = local_gradients(pair, h, mask, scale, near[0][row], factor[row], delta[row])
        dq_out[:, cols] = dq
        for i, part in enumerate((dk, dv)):
            own_out[i, :, cols] = part[:slots].astype(BF16)
            sib_out[i, :, cols] = part[slots:].astype(BF16)


def near_grad(pair, local, stats, gates):
    _, rows, width = pair.shape
    slots = rows // 2
    out = pltpu.VMEM((2, slots, width), BF16)
    return pl.pallas_call(
        functools.partial(near_grad_kernel, HEAD**-0.5),
        out_shape=[pltpu.VMEM((2 * slots, width), F32), out, out, jax.ShapeDtypeStruct(gates.shape, F32)],
        in_specs=[VMEM] * 4,
        out_specs=[VMEM] * 4,
        compiler_params=params(),
        cost_estimate=cost(20 * slots * slots * width, 40 * slots * width),
        name="near_grad",
    )(pair, local, stats, gates)


def put_terms(grad, rows_x, out_ref):
    high = grad.astype(BF16)
    rest = grad - high.astype(F32)
    mid = rest.astype(BF16)
    low = (rest - mid.astype(F32)).astype(BF16)
    slots = rows_x.shape[1]
    row = lax.broadcasted_iota(jnp.int32, (8, grad.shape[1]), 0)
    lhs = jnp.where(row == 0, high.astype(F32), jnp.where(row == 1, mid.astype(F32), jnp.where(row == 2, low.astype(F32), 0.0)))
    lhs = lhs.astype(BF16)
    term = jnp.sum(nn(lhs[:, :slots], rows_x[0]) + nn(lhs[:, slots:], rows_x[1]), axis=0, keepdims=True)
    parts, copies, _, chunk = out_ref.shape
    for j in range(parts):
        for i in range(copies):
            out_ref[j, i] = term[:, j * chunk : (j + 1) * chunk]


def cross_grad_kernel(scale, total, cross, kept, stats, local, heard, gates, near_dq, near_sum, rows_x, straight, diag, dq_out, keep, final, terms, held, sem):
    slots, width = straight.shape[1], straight.shape[2]
    heads = width // HEAD
    first = here()[1] == 0
    late = jnp.where(first, 0.0, 1.0)
    mine = [stats[i] for i in range(3)]
    other = [heard[i] for i in range(3)]
    near = [local[i, :heads] for i in range(3)]
    far = [local[i, heads:] for i in range(3)]
    factor, delta = merge(mine, choose(first, other, near))
    factor = factor * jnp.where(first, heard[3], jnp.broadcast_to(gates[...], factor.shape))
    final[0], final[1] = merge(far, choose(first, NONE, other))
    sums = near_sum[...] + jnp.sum(final[1], axis=0, keepdims=True)
    put_terms(sums * gates[...] * (1.0 - gates[...]) * (1.0 / total), rows_x, held)
    leaving = pltpu.make_async_copy(held, terms, sem)
    leaving.start()
    for h in range(heads):
        cols = slice(h * HEAD, (h + 1) * HEAD)
        row = slice(h, h + 1)
        dq, dk, dv = gradients(
            cross[2, :, cols], cross[0, :, cols], cross[3, :, cols],
            kept[0, h].astype(F32), kept[1, h].astype(F32), scale, factor[row], delta[row],
        )
        dq_out[:, cols] = (near_dq[:, cols] + late * dq).astype(BF16)
        keep[0, :, cols] = dk.astype(BF16)
        keep[1, :, cols] = dv.astype(BF16)
        sent = jnp.where(first, dq, dk).astype(BF16)
        straight[0, :, cols] = sent[:slots]
        diag[0, :, cols] = sent[slots:]
        straight[1, :, cols] = dv[:slots].astype(BF16)
        diag[1, :, cols] = dv[slots:].astype(BF16)
    leaving.wait()


def cross_grad(cross, kept, stats, local, heard, gates, near_dq, near_sum, rows_x, parts, copies, total):
    _, rows, width = cross.shape
    slots = rows // 2
    out = pltpu.VMEM((2, slots, width), BF16)
    spread = (parts, copies, 1, rows_x.shape[2] // parts)
    return pl.pallas_call(
        functools.partial(cross_grad_kernel, HEAD**-0.5, total),
        out_shape=[
            out,
            out,
            pltpu.VMEM((rows, width), BF16),
            pltpu.VMEM((2, rows, width), BF16),
            jax.ShapeDtypeStruct((2, width // HEAD, rows), F32),
            pltpu.HBM(spread, F32),
        ],
        in_specs=[VMEM] * 9,
        out_specs=[VMEM] * 5 + [pl.BlockSpec(memory_space=pltpu.HBM)],
        scratch_shapes=[pltpu.VMEM(spread, F32), pltpu.SemaphoreType.DMA],
        compiler_params=params(),
        cost_estimate=cost(24 * slots * slots * width, 64 * slots * width),
        name="cross_grad",
    )(cross, kept, stats, local, heard, gates, near_dq, near_sum, rows_x)


def far_grad_kernel(scale, pair, local, final, gates, keep, near_dq, near_own, near_sib, own_out, sib_out):
    slots, width = pair.shape[1] // 2, pair.shape[2]
    heads = width // HEAD
    early = jnp.where(here()[1] == 0, 1.0, 0.0)
    factor = final[0] * gates[...]
    mask = local_mask(here()[0], pair)
    own_out[0, :, :width] = near_dq[:slots]
    sib_out[0, :, :width] = near_dq[slots:]
    for i in range(2):
        own_out[1 + i, :, :width] = near_own[i]
        sib_out[1 + i, :, :width] = near_sib[i]
    for h in range(heads):
        cols = slice(width + h * HEAD, width + (h + 1) * HEAD)
        at = slice(h * HEAD, (h + 1) * HEAD)
        row = slice(h, h + 1)
        top = local[0, heads + h : heads + h + 1]
        dq, dk, dv = local_gradients(pair, h, mask, scale, top, factor[row], final[1, row])
        dk = dk + early * keep[0, :, at].astype(F32)
        dv = dv + early * keep[1, :, at].astype(F32)
        for i, part in enumerate((dq, dk, dv)):
            own_out[i, :, cols] = part[:slots].astype(BF16)
            sib_out[i, :, cols] = part[slots:].astype(BF16)


def far_grad(pair, local, final, gates, keep, near_dq, near_own, near_sib):
    _, rows, width = pair.shape
    slots, half = rows // 2, 2 * width
    out = jax.ShapeDtypeStruct((3, slots, half), BF16)
    return pl.pallas_call(
        functools.partial(far_grad_kernel, HEAD**-0.5),
        out_shape=[out, out],
        in_specs=[VMEM] * 8,
        out_specs=[VMEM] * 2,
        compiler_params=params(),
        cost_estimate=cost(20 * slots * slots * half, 40 * slots * half),
        name="far_grad",
    )(pair, local, final, gates, keep, near_dq, near_own, near_sib)


def own_join_kernel(own, dq_out, dk_out, dv_out, waiting, total, sems):
    slots, half = own.shape[1], own.shape[2]
    width = half // 2
    core, chip = here()
    cols = pl.ds(pl.multiple_of(core * half, HEAD), half)
    stores = []
    for j, out in enumerate((dq_out, dk_out, dv_out)):
        total[j] = own[j].astype(F32)
        stores.append(pltpu.make_async_copy(total.at[j], out.at[0, :, cols], sems.at[j]))
        stores[-1].start()
    waiting[0] = jnp.where(chip == 0, total[1, :, :width], total[0, :, width:]).astype(BF16)
    waiting[1] = own[2, :, :width]
    for c in stores:
        c.wait()


def own_join(own, shape):
    out = pltpu.HBM(shape, F32)
    _, slots, half = own.shape
    hbm = pl.BlockSpec(memory_space=pltpu.HBM)
    return pl.pallas_call(
        own_join_kernel,
        out_shape=[out] * 3 + [jax.ShapeDtypeStruct((2, slots, half // 2), BF16)],
        in_specs=[VMEM],
        out_specs=[hbm] * 3 + [VMEM],
        scratch_shapes=[pltpu.VMEM((3, slots, half), F32), pltpu.SemaphoreType.DMA((3,))],
        compiler_params=params(),
        cost_estimate=cost(0, 18 * own.size),
        name="own_join",
    )(own)


def sib_join_kernel(sib, dq_in, dk_in, dv_in, dq_out, dk_out, dv_out, waiting, low, total, in_sems, out_sems):
    half = sib.shape[2]
    width = half // 2
    core, chip = here()
    loads = [pltpu.make_async_copy(sib.at[j], low.at[j], in_sems.at[j]) for j in range(3)]
    for c in loads:
        c.start()
    cols = pl.ds(pl.multiple_of((1 - core) * half, HEAD), half)
    stores = []
    for j, out in enumerate((dq_out, dk_out, dv_out)):
        loads[j].wait()
        total[j] = low[j].astype(F32)
        stores.append(pltpu.make_async_copy(total.at[j], out.at[0, :, cols], out_sems.at[j]))
        stores[-1].start()
    waiting[0] = jnp.where(chip == 0, total[1, :, :width], total[0, :, width:]).astype(BF16)
    waiting[1] = low[2, :, :width]
    for c in stores:
        c.wait()


def sib_join(sib, outs):
    _, slots, half = sib.shape
    hbm = pl.BlockSpec(memory_space=pltpu.HBM)
    return pl.pallas_call(
        sib_join_kernel,
        out_shape=[pltpu.HBM(o.shape, F32) for o in outs] + [pltpu.VMEM((2, slots, half // 2), BF16)],
        in_specs=[pl.BlockSpec(memory_space=pl.ANY)] + [hbm] * 3,
        out_specs=[hbm] * 3 + [VMEM],
        scratch_shapes=[
            pltpu.VMEM((3, slots, half), BF16),
            pltpu.VMEM((3, slots, half), F32),
            pltpu.SemaphoreType.DMA((3,)),
            pltpu.SemaphoreType.DMA((3,)),
        ],
        input_output_aliases={1: 0, 2: 1, 3: 2},
        compiler_params=params(),
        cost_estimate=cost(0, 12 * sib.size),
        name="sib_join",
    )(sib, *in_hbm(*outs))


def add_back_kernel(own, sib, straight, diag, dq_in, dk_in, dv_in, dq_out, dk_out, dv_out, total, sems):
    width = straight.shape[2]
    core, chip = here()
    ends = ((own, straight, 2 * core * width), (sib, diag, 2 * (1 - core) * width))

    def store(i, j, out, offset):
        cols = pl.ds(pl.multiple_of(ends[i][2] + offset, HEAD), width)
        copy = pltpu.make_async_copy(total.at[i, j], out.at[0, :, cols], sems.at[2 * i + j])
        copy.start()
        return copy

    @pl.when(chip == 0)
    def _():
        copies = []
        for i, (waiting, back, _) in enumerate(ends):
            for j, out in enumerate((dk_out, dv_out)):
                total[i, j] = waiting[j].astype(F32) + back[j].astype(F32)
                copies.append(store(i, j, out, 0))
        for c in copies:
            c.wait()

    @pl.when(chip != 0)
    def _():
        copies = []
        for i, (waiting, back, _) in enumerate(ends):
            total[i, 0] = waiting[0].astype(F32) + back[0].astype(F32)
            copies.append(store(i, 0, dq_out, width))
        for c in copies:
            c.wait()


def add_back(own, sib, straight, diag, outs):
    hbm = pl.BlockSpec(memory_space=pltpu.HBM)
    return pl.pallas_call(
        add_back_kernel,
        out_shape=[pltpu.HBM(o.shape, F32) for o in outs],
        in_specs=[VMEM] * 4 + [hbm] * 3,
        out_specs=[hbm] * 3,
        scratch_shapes=[pltpu.VMEM((2, *own.shape), F32), pltpu.SemaphoreType.DMA((4,))],
        input_output_aliases={4: 0, 5: 1, 6: 2},
        compiler_params=params(),
        cost_estimate=cost(0, 24 * own.size),
        name="add_back",
    )(own, sib, straight, diag, *in_hbm(*outs))


def swap_body(route_pos, x_routed, w_router, queries, keys, values, d_gated):
    slots = queries.shape[1]
    n, ndp = lax.axis_size("ctx"), lax.axis_size("dp")

    def send(a, flip):
        return lax.ppermute(a, "ctx", [(i, i ^ flip) for i in range(n)])

    def beside(fn, *operands):
        def skip(*ops):
            return jax.tree.map(lambda o: jnp.zeros(o.shape, o.dtype), jax.eval_shape(fn, *ops))

        return lax.cond(route_pos[0, 0] >= -1, fn, skip, *operands)

    def after(value, *others):
        return lax.optimization_barrier((value, *others))[0]

    def widen(part, step, *first):
        other = lax.ppermute(part, "dp", [(i, i ^ step) for i in range(ndp)])
        return jnp.concatenate([part, after(other, *first)], axis=1)

    def exchange_phase(x_routed, w_part, theirs):
        sib, x_sib = send(theirs, 1), send(x_routed, 1)
        step = 2
        while 2 * step < ndp:
            w_part = widen(w_part, step)
            step *= 2
        return sib, x_sib, w_part

    def far_phase(*operands):
        own_out, sib_out = far_grad(*operands)
        sib_in = send(sib_out, 1)
        *outs, waiting = own_join(own_out, queries.shape)
        *outs, waiting_sib = sib_join(sib_in, outs)
        return outs, waiting, waiting_sib

    out_s, out_d, w_part = cross_pack(route_pos, w_router, keys, values, queries, d_gated)
    in_s, in_d = send(out_s, 2), send(out_d, 3)

    theirs = sib_pack(after(route_pos, out_s), keys, values, queries, d_gated)
    if ndp > 1:
        w_part = widen(w_part, 1, theirs)
    sib, x_sib, w_part = beside(exchange_phase, x_routed, w_part, theirs)
    local, live, near, far, rows_x = local_stats(route_pos, keys, values, queries, d_gated, sib, x_routed, x_sib)
    cross, stats, kept = cross_stats(near, far, in_s, in_d)
    if ndp > 2:
        w_part = widen(w_part, ndp // 2, stats)
    gates, message = pair_gate(live, rows_x, w_part, local, stats, ndp)

    heard = send(message, 2)
    near_dq, near_own, near_sib, near_sum = near_grad(near, local, stats, gates)
    total = float(ndp * n * slots // 2)
    back_s, back_d, dq_low, keep, final, terms = cross_grad(
        cross, kept, stats, local, heard, gates, near_dq, near_sum, rows_x, ndp, n, total
    )

    ret_s, ret_d = send(back_s, 2), send(back_d, 3)
    shared = lax.all_to_all(terms.reshape(ndp * n, 1, -1), ("dp", "ctx"), 0, 0, tiled=True)
    outs, waiting, waiting_sib = beside(far_phase, far, local, final, gates, keep, dq_low, near_own, near_sib)
    dq, dk, dv = add_back(waiting, waiting_sib, ret_s, ret_d, outs)
    router_grad = jnp.sum(after(shared, dq), axis=(0, 1))
    return dq, dk, dv, router_grad


def body(route_pos, x_routed, w_router, queries, keys, values, d_gated):
    slots, full = queries.shape[1], queries.shape[2]
    n, ndp = lax.axis_size("ctx"), lax.axis_size("dp")
    chips = n // 2
    me, dp_me = lax.axis_index("ctx"), lax.axis_index("dp")
    core = (me % 2).astype(jnp.int32).reshape(1)
    half = full // 2
    groups = GROUPS if (half // HEAD) % GROUPS == 0 else 1
    width = half // groups

    sib_pairs = [(i, i ^ 1) for i in range(n)]

    def forward_pairs(step, flip):
        return [(i, (i + 2 * step) ^ flip) for i in range(n) if i + 2 * step < n]

    def back_pairs(step, flip):
        return [(b, a) for a, b in forward_pairs(step, flip)]

    def to_sib(a):
        return lax.ppermute(a, "ctx", sib_pairs)

    links = [(step, flip) for step in range(1, chips) for flip in (0, 1)]

    w_row = w_router.reshape(1, -1)
    w_parts = [w_row] + [
        lax.ppermute(w_row, "dp", [(i, (i + s) % ndp) for i in range(ndp)]) for s in range(1, ndp)
    ]
    live = (route_pos >= 0).astype(jnp.int32)
    lives = [live, to_sib(live)] + [lax.ppermute(live, "ctx", forward_pairs(*link)) for link in links]
    live_all = jnp.concatenate(lives, axis=0)

    kv_mine, kv_theirs = pack(core, keys, values, groups, width)
    kv_far = [
        [lax.ppermute((kv_theirs if flip else kv_mine)[g], "ctx", forward_pairs(step, flip)) for step, flip in links]
        for g in range(groups)
    ]
    q_mine, q_theirs = pack(core, queries, d_gated, groups, width)
    kv_sib = [to_sib(a) for a in kv_theirs]
    q_sib = [to_sib(a) for a in q_theirs]

    offsets = ((dp_me - jnp.arange(ndp)) % ndp).astype(jnp.int32)
    gate = router_gate(offsets, route_pos, x_routed, w_parts)
    gates = (gate, to_sib(gate))

    accs = (jnp.zeros((1, slots), F32), jnp.zeros((1, slots), F32))
    dq_own, sib_in, kv_own, back = [], [], [], []
    for g in range(groups):
        dq, sib_out, kv_local, kv_remote, accs = attention(
            core, live_all, gates, accs, q_mine[g], q_sib[g], [kv_mine[g], kv_sib[g], *kv_far[g]]
        )
        back.append([lax.ppermute(a, "ctx", back_pairs(*link)) for a, link in zip(kv_remote, links)])
        sib_in.append(to_sib(sib_out))
        dq_own.append(dq)
        kv_own.append(kv_local)

    targets = ((dp_me + jnp.arange(ndp)) % ndp).astype(jnp.int32)
    terms = router_terms(targets, gate, accs[0], to_sib(accs[1]), x_routed, ndp)
    mine = terms[0]
    for s in range(1, ndp):
        mine = mine + lax.ppermute(terms[s], "dp", [(i, (i + s) % ndp) for i in range(ndp)])
    total = mine
    for s in range(1, n):
        total = total + lax.ppermute(mine, "ctx", [(i, (i + s) % n) for i in range(n)])
    router_grad = total[0] / float(ndp * n * slots // 2)

    dq, dk, dv = combine(core, dq_own, sib_in, kv_own, back, queries.shape)
    return dq, dk, dv, router_grad


def solution(mesh):
    placed = (
        P("dp", "ctx"),
        P("dp", "ctx", None),
        P("dp"),
        P("dp", "ctx", None),
        P("dp", "ctx", None),
        P("dp", "ctx", None),
        P("dp", "ctx", None),
    )
    ndp = mesh.shape["dp"]
    paired = mesh.shape["ctx"] == 4 and ndp & (ndp - 1) == 0
    return jax.shard_map(
        swap_body if paired else body,
        mesh=mesh,
        in_specs=placed,
        out_specs=(P("dp", "ctx", None), P("dp", "ctx", None), P("dp", "ctx", None), P("dp")),
        check_vma=False,
    )
```

```python
import functools

import jax
import jax.numpy as jnp
from jax import lax
from jax.experimental import pallas as pl
from jax.experimental.pallas import tpu as pltpu
from jax.sharding import PartitionSpec as P

HEAD = 128
GROUPS = 4
NEG_FILL = -1e30
MIB = 1024 * 1024
BF16 = jnp.bfloat16
F32 = jnp.float32

VMEM = pl.BlockSpec(memory_space=pltpu.VMEM)
SMEM = pl.BlockSpec(memory_space=pltpu.SMEM)


def params(mib=16):
    return pltpu.CompilerParams(vmem_limit_bytes=mib * MIB)


def cost(flops, nbytes, exps=0):
    return pl.CostEstimate(flops=1, bytes_accessed=1, transcendentals=0)


def in_hbm(*arrays):
    return [pltpu.with_memory_space_constraint(a, pltpu.HBM) for a in arrays]


def nt(a, b):
    return lax.dot_general(a, b, (((1,), (1,)), ((), ())), preferred_element_type=F32)


def nn(a, b):
    return lax.dot_general(a, b, (((1,), (0,)), ((), ())), preferred_element_type=F32)


def tn(a, b):
    return lax.dot_general(a, b, (((0,), (0,)), ((), ())), preferred_element_type=F32)


def pack_kernel(groups, width, core_ref, first_ref, second_ref, *outs):
    half = first_ref.shape[-1] // 2
    core = core_ref[0]
    for side in range(2):
        base = (core if side == 0 else 1 - core) * half
        for g in range(groups):
            out = outs[side * groups + g]
            cols = pl.ds(pl.multiple_of(base + g * width, HEAD), width)
            out[0] = first_ref[0, :, cols].astype(BF16)
            out[1] = second_ref[0, :, cols].astype(BF16)


def pack(core, first, second, groups, width):
    slots = first.shape[1]
    out = jax.ShapeDtypeStruct((2, slots, width), BF16)
    res = pl.pallas_call(
        functools.partial(pack_kernel, groups, width),
        out_shape=[out] * (2 * groups),
        in_specs=[SMEM, VMEM, VMEM],
        out_specs=[VMEM] * (2 * groups),
        compiler_params=params(),
        cost_estimate=cost(0, 2 * first.size * 4),
        name="pack",
    )(core, first, second)
    return res[:groups], res[groups:]


def gate_kernel(parts, offset_ref, pos_ref, x_ref, *refs):
    w_refs, out_ref = refs[:parts], refs[parts]
    chunk = w_refs[0].shape[-1]
    total = jnp.zeros((8, x_ref.shape[1]), F32)
    for s in range(parts):
        cols = pl.ds(pl.multiple_of(offset_ref[s] * chunk, HEAD), chunk)
        w_rows = jnp.broadcast_to(w_refs[s][...].astype(F32), (8, chunk)).astype(BF16)
        total = total + nt(w_rows, x_ref[0, :, cols])
    gate = 1.0 / (1.0 + jnp.exp(-total[0:1]))
    out_ref[...] = jnp.where(pos_ref[...] >= 0, gate, 0.0)


def router_gate(offsets, route_pos, x_routed, w_parts):
    parts = len(w_parts)
    return pl.pallas_call(
        functools.partial(gate_kernel, parts),
        out_shape=jax.ShapeDtypeStruct(route_pos.shape, F32),
        in_specs=[SMEM] + [VMEM] * (2 + parts),
        out_specs=VMEM,
        compiler_params=params(8),
        cost_estimate=cost(16 * x_routed.size, x_routed.size * 2),
        name="router_gate",
    )(offsets, route_pos, x_routed, *w_parts)


def attention_kernel(remote, scale, core_ref, live_ref, gate_own, gate_sib, acc_own, acc_sib, q_own, q_sib, *refs):
    chunks = 2 + remote
    kv = refs[:chunks]
    outs = refs[chunks:]
    dq_own, sib_out, kv_own = outs[:3]
    kv_remote = outs[3 : 3 + remote]
    sum_own, sum_sib = outs[3 + remote :]
    slots, width = q_own.shape[1], q_own.shape[2]
    core = core_ref[0]
    key = lax.broadcasted_iota(jnp.int32, (slots, slots), 0)
    query = lax.broadcasted_iota(jnp.int32, (slots, slots), 1)
    counts = [jnp.sum(live_ref[i : i + 1], axis=1, keepdims=True) for i in range(chunks)]
    lives = [key < counts[i] for i in range(chunks)]
    own_later = core == 1
    bias_rows = []
    for i in range(chunks):
        live = lives[i]
        if i == 0:
            pair = (live & (key <= query), live & jnp.logical_not(own_later))
        elif i == 1:
            pair = (live & own_later, live & (key <= query))
        else:
            pair = (live, live)
        bias_rows.append(jnp.concatenate([jnp.where(p, 0.0, NEG_FILL) for p in pair], axis=1))
    bias = jnp.concatenate(bias_rows, axis=0)
    gates = jnp.concatenate([gate_own[...], gate_sib[...]], axis=1)
    total = jnp.zeros((1, 2 * slots), F32)
    for h in range(width // HEAD):
        cols = slice(h * HEAD, (h + 1) * HEAD)
        q = jnp.concatenate([q_own[0, :, cols], q_sib[0, :, cols]], axis=0)
        dg = jnp.concatenate([q_own[1, :, cols], q_sib[1, :, cols]], axis=0)
        k = jnp.concatenate([r[0, :, cols] for r in kv], axis=0)
        v = jnp.concatenate([r[1, :, cols] for r in kv], axis=0)
        scores = nt(k, q) * scale + bias
        top = jnp.max(scores, axis=0, keepdims=True)
        e = jnp.exp(scores - top)
        inverse = 1.0 / jnp.sum(e, axis=0, keepdims=True)
        gw = nt(v, dg)
        delta = jnp.sum(e * gw, axis=0, keepdims=True) * inverse
        total = total + delta
        weights = e * (inverse * gates)
        dv = nn(weights.astype(BF16), dg)
        ds = (weights * ((gw - delta) * scale)).astype(BF16)
        dk = nn(ds, q)
        dq = tn(ds, k)
        dq_own[:, cols] = dq[:slots].astype(dq_own.dtype)
        sib_out[0, :, cols] = dq[slots:].astype(BF16)
        kv_own[0, :, cols] = dk[:slots].astype(BF16)
        kv_own[1, :, cols] = dv[:slots].astype(BF16)
        sib_out[1, :, cols] = dk[slots : 2 * slots].astype(BF16)
        sib_out[2, :, cols] = dv[slots : 2 * slots].astype(BF16)
        for i in range(remote):
            rows = slice((2 + i) * slots, (3 + i) * slots)
            kv_remote[i][0, :, cols] = dk[rows].astype(BF16)
            kv_remote[i][1, :, cols] = dv[rows].astype(BF16)
    sum_own[...] = acc_own[...] + total[:, :slots]
    sum_sib[...] = acc_sib[...] + total[:, slots:]


def attention(core, live, gates, accs, q_own, q_sib, kv):
    remote = len(kv) - 2
    _, slots, width = q_own.shape
    pair = jax.ShapeDtypeStruct((2, slots, width), BF16)
    row = jax.ShapeDtypeStruct((1, slots), F32)
    outs = [
        jax.ShapeDtypeStruct((slots, width), BF16),
        jax.ShapeDtypeStruct((3, slots, width), BF16),
        pair,
        *([pair] * remote),
        row,
        row,
    ]
    keys = (2 + remote) * slots
    res = pl.pallas_call(
        functools.partial(attention_kernel, remote, HEAD**-0.5),
        out_shape=outs,
        in_specs=[SMEM] + [VMEM] * (7 + len(kv)),
        out_specs=[VMEM] * len(outs),
        compiler_params=params(48),
        cost_estimate=cost(20 * slots * keys * width, 8 * keys * width + 20 * slots * width, 2 * slots * keys * width // HEAD),
        name="attention",
    )(core, live, *gates, *accs, q_own, q_sib, *kv)
    return res[0], res[1], res[2], res[3 : 3 + remote], (res[3 + remote], res[4 + remote])


def combine_kernel(groups, width, remote, core_ref, *refs):
    dq_own, sib, kv_own = refs[:groups], refs[groups : 2 * groups], refs[2 * groups : 3 * groups]
    back = refs[3 * groups : 3 * groups + groups * remote]
    dq_out, dk_out, dv_out = refs[3 * groups + groups * remote :]
    half = groups * width
    core = core_ref[0]
    for g in range(groups):
        own = pl.ds(pl.multiple_of(core * half + g * width, HEAD), width)
        other = pl.ds(pl.multiple_of((1 - core) * half + g * width, HEAD), width)
        dq_out[0, :, own] = dq_own[g][...].astype(F32)
        dq_out[0, :, other] = sib[g][0].astype(F32)
        for i, out in enumerate((dk_out, dv_out)):
            mine = kv_own[g][i].astype(F32)
            theirs = sib[g][1 + i].astype(F32)
            for r in range(remote):
                part = back[g * remote + r][i].astype(F32)
                if r % 2 == 0:
                    mine = mine + part
                else:
                    theirs = theirs + part
            out[0, :, own] = mine
            out[0, :, other] = theirs


def combine(core, dq_own, sib, kv_own, back, shape):
    groups = len(dq_own)
    remote = len(back[0])
    out = jax.ShapeDtypeStruct(shape, F32)
    flat = [*dq_own, *sib, *kv_own, *(b for group in back for b in group)]
    return pl.pallas_call(
        functools.partial(combine_kernel, groups, dq_own[0].shape[-1], remote),
        out_shape=[out] * 3,
        in_specs=[SMEM] + [VMEM] * len(flat),
        out_specs=[VMEM] * 3,
        compiler_params=params(48),
        cost_estimate=cost(0, 3 * out.size * 6),
        name="combine",
    )(core, *flat)


def router_kernel(parts, target_ref, gate_ref, own_ref, sib_ref, x_ref, *outs):
    gate = gate_ref[...]
    grad = (own_ref[...] + sib_ref[...]) * gate * (1.0 - gate)
    high = grad.astype(BF16)
    rest = grad - high.astype(F32)
    mid = rest.astype(BF16)
    low = (rest - mid.astype(F32)).astype(BF16)
    row = lax.broadcasted_iota(jnp.int32, (8, grad.shape[1]), 0)
    lhs = jnp.where(row == 0, high.astype(F32), jnp.where(row == 1, mid.astype(F32), jnp.where(row == 2, low.astype(F32), 0.0)))
    lhs = lhs.astype(BF16)
    chunk = outs[0].shape[-1]
    for s in range(parts):
        cols = pl.ds(pl.multiple_of(target_ref[s] * chunk, HEAD), chunk)
        outs[s][...] = jnp.sum(nn(lhs, x_ref[0, :, cols]), axis=0, keepdims=True)


def router_terms(targets, gate, own, sib, x_routed, parts):
    chunk = x_routed.shape[-1] // parts
    return pl.pallas_call(
        functools.partial(router_kernel, parts),
        out_shape=[jax.ShapeDtypeStruct((1, chunk), F32)] * parts,
        in_specs=[SMEM] + [VMEM] * 4,
        out_specs=[VMEM] * parts,
        compiler_params=params(),
        cost_estimate=cost(16 * x_routed.size, x_routed.size * 2),
        name="router_terms",
    )(targets, gate, own, sib, x_routed)


def here():
    me = lax.axis_index("ctx")
    return lax.rem(me, 2), lax.div(me, 2)


MARK = 2.0**60
MARK_LIMIT = 2.0**50


def live_rows(pos_ref, slots):
    count = jnp.sum((pos_ref[...] >= 0).astype(jnp.int32), axis=1, keepdims=True)
    return lax.broadcasted_iota(jnp.int32, (slots, HEAD), 0) < count


def mark_dead(keys, live):
    width = keys.shape[-1]
    mask = jnp.concatenate([live] * (width // HEAD), axis=1)
    return jnp.where(mask, keys.astype(F32), MARK).astype(BF16)


def cross_pack_kernel(pos_any, w_any, k_ref, v_ref, q_ref, dg_ref, straight, diag, w_out, wide, pos_ref, w_ref, sems):
    small = [pltpu.make_async_copy(pos_any, pos_ref, sems.at[4]), pltpu.make_async_copy(w_any, w_ref, sems.at[5])]
    for c in small:
        c.start()
    slots, width = straight.shape[1], straight.shape[2]
    half = k_ref.shape[-1] // 2
    core, chip = here()
    ends = ((straight, core * half), (diag, (1 - core) * half))

    def copies(first, second, targets, offset):
        out = []
        for i, (end, start) in enumerate(ends):
            cols = pl.ds(pl.multiple_of(start + offset, HEAD), width)
            out.append(pltpu.make_async_copy(first.at[0, :, cols], end.at[0], sems.at[2 * i]))
            out.append(pltpu.make_async_copy(second.at[0, :, cols], targets[i], sems.at[2 * i + 1]))
        for c in out:
            c.start()
        for c in out:
            c.wait()

    @pl.when(chip == 0)
    def _():
        copies(k_ref, v_ref, (straight.at[1], diag.at[1]), 0)
        small[0].wait()
        live = live_rows(pos_ref, slots)
        for end, _ in ends:
            end[0] = mark_dead(end[0], live)

    @pl.when(chip != 0)
    def _():
        copies(q_ref, dg_ref, (wide.at[0], wide.at[1]), width)
        small[0].wait()
        for i, (end, _) in enumerate(ends):
            end[1] = wide[i].astype(BF16)

    small[1].wait()
    w_out[...] = w_ref[...].astype(F32).reshape(w_out.shape)


def cross_pack(route_pos, w_router, keys, values, queries, d_gated):
    _, slots, full = keys.shape
    cross = pltpu.VMEM((2, slots, full // 4), BF16)
    hbm = pl.BlockSpec(memory_space=pltpu.HBM)
    return pl.pallas_call(
        cross_pack_kernel,
        out_shape=[cross, cross, jax.ShapeDtypeStruct((1, w_router.shape[0]), F32)],
        in_specs=[hbm] * 6,
        out_specs=[VMEM] * 3,
        scratch_shapes=[
            pltpu.VMEM((2, slots, full // 4), F32),
            pltpu.VMEM(route_pos.shape, jnp.int32),
            pltpu.VMEM(w_router.shape, BF16),
            pltpu.SemaphoreType.DMA((6,)),
        ],
        compiler_params=params(6),
        cost_estimate=cost(0, 10 * slots * full),
        name="cross_pack",
    )(*in_hbm(route_pos, w_router, keys, values, queries, d_gated))


def sib_pack_kernel(pos_ref, k_ref, v_ref, q_ref, dg_ref, out, wide, sems):
    slots, half = out.shape[1], out.shape[2]
    cols = pl.ds(pl.multiple_of((1 - here()[0]) * half, HEAD), half)
    sources = ((k_ref, out.at[0]), (dg_ref, wide), (v_ref, out.at[1]), (q_ref, out.at[2]))
    copies = [pltpu.make_async_copy(src.at[0, :, cols], dst, sems.at[i]) for i, (src, dst) in enumerate(sources)]
    for c in copies:
        c.start()
    live = live_rows(pos_ref, slots)
    copies[0].wait()
    out[0] = mark_dead(out[0], live)
    copies[1].wait()
    out[3] = wide[...].astype(BF16)
    copies[2].wait()
    copies[3].wait()


def sib_pack(route_pos, keys, values, queries, d_gated):
    _, slots, full = keys.shape
    hbm = pl.BlockSpec(memory_space=pltpu.HBM)
    return pl.pallas_call(
        sib_pack_kernel,
        out_shape=pltpu.VMEM((4, slots, full // 2), BF16),
        in_specs=[VMEM, hbm, hbm, hbm, hbm],
        out_specs=VMEM,
        scratch_shapes=[pltpu.VMEM((slots, full // 2), F32), pltpu.SemaphoreType.DMA((4,))],
        compiler_params=params(8),
        cost_estimate=cost(0, 20 * slots * full),
        name="sib_pack",
    )(route_pos, *in_hbm(keys, values, queries, d_gated))


def pair_gate_kernel(parts, live_ref, rows_x, w_ref, local, stats, out_ref, message):
    chunk = w_ref.shape[1] // parts
    slots = rows_x.shape[1]
    for i in range(2):
        total = jnp.zeros((8, slots), F32)
        for j in range(parts):
            w_rows = jnp.broadcast_to(w_ref[:, j * chunk : (j + 1) * chunk], (8, chunk)).astype(BF16)
            cols = pl.ds(pl.multiple_of((lax.axis_index("dp") ^ j) * chunk, HEAD), chunk)
            total = total + nt(w_rows, rows_x[i, :, cols])
        lanes = slice(i * slots, (i + 1) * slots)
        out_ref[:, lanes] = live_ref[:, lanes] / (1.0 + jnp.exp(-total[0:1]))
    first = here()[1] == 0
    heads = stats.shape[1]
    for i in range(3):
        message[i] = jnp.where(first, stats[i], local[i, heads:])
    message[3] = jnp.broadcast_to(out_ref[...], message.shape[1:])


def pair_gate(live, rows_x, w_full, local, stats, parts):
    _, heads, lanes = stats.shape
    return pl.pallas_call(
        functools.partial(pair_gate_kernel, parts),
        out_shape=[jax.ShapeDtypeStruct(live.shape, F32), jax.ShapeDtypeStruct((4, heads, lanes), F32)],
        in_specs=[VMEM] * 5,
        out_specs=[VMEM] * 2,
        compiler_params=params(),
        cost_estimate=cost(16 * rows_x.size, rows_x.size * 2),
        name="router_gate",
    )(live, rows_x, w_full, local, stats)


def local_mask(core, pair):
    slots = pair.shape[1] // 2
    key = lax.broadcasted_iota(jnp.int32, (slots, slots), 0)
    query = lax.broadcasted_iota(jnp.int32, (slots, slots), 1)
    causal = key <= query
    own_live = pair[0, :slots, :slots].astype(F32) < MARK_LIMIT
    sib_live = pair[0, slots:, :slots].astype(F32) < MARK_LIMIT
    own_rows = jnp.concatenate([own_live & causal, own_live & (core == 0)], axis=1)
    sib_rows = jnp.concatenate([sib_live & (core == 1), sib_live & causal], axis=1)
    return jnp.concatenate([own_rows, sib_rows], axis=0)


def kept_stats(scores, gw, kept, stats, h):
    top = jnp.max(scores, axis=0, keepdims=True)
    e = jnp.exp(scores - top).astype(BF16)
    gw = gw.astype(BF16)
    kept[0, h] = e
    kept[1, h] = gw
    e = e.astype(F32)
    stats[0, h : h + 1] = top
    stats[1, h : h + 1] = jnp.sum(e, axis=0, keepdims=True)
    stats[2, h : h + 1] = jnp.sum(e * gw.astype(F32), axis=0, keepdims=True)


def partial_stats(scores, gw, stats, h):
    top = jnp.max(scores, axis=0, keepdims=True)
    e = jnp.exp(scores - top)
    stats[0, h : h + 1] = top
    stats[1, h : h + 1] = jnp.sum(e, axis=0, keepdims=True)
    stats[2, h : h + 1] = jnp.sum(e * gw, axis=0, keepdims=True)


def local_stats_kernel(scale, pos_ref, k_ref, v_ref, q_ref, dg_ref, sib, x_ref, x_sib, stats, live, near, far, rows_x, wide, sems, x_sems):
    slots, half = sib.shape[1], sib.shape[2]
    width = half // 2
    core = here()[0]
    own, other = slice(0, slots), slice(slots, 2 * slots)
    stages = []
    for g, pair in enumerate((near, far)):
        cols = slice(g * width, (g + 1) * width)
        held = pl.ds(pl.multiple_of(core * half + g * width, HEAD), width)
        copies = [
            pltpu.make_async_copy(ref.at[0, :, held], pair.at[j, own], sems.at[8 * g + j])
            for j, ref in enumerate((k_ref, v_ref, q_ref))
        ]
        copies.append(pltpu.make_async_copy(dg_ref.at[0, :, held], wide.at[:, cols], sems.at[8 * g + 3]))
        for j in range(4):
            copies.append(pltpu.make_async_copy(sib.at[j, :, cols], pair.at[j, other], sems.at[8 * g + 4 + j]))
        for c in copies:
            c.start()
        stages.append(copies)
    x_copies = []
    depth = x_ref.shape[2] // 2
    for i, ref in enumerate((x_ref, x_sib)):
        for g in range(2):
            cols = slice(g * depth, (g + 1) * depth)
            x_copies.append(pltpu.make_async_copy(ref.at[0, :, cols], rows_x.at[i, :, cols], x_sems.at[2 * i + g]))
    for c in x_copies:
        c.start()
    rows_live = live_rows(pos_ref, slots)
    mask = None
    for g, pair in enumerate((near, far)):
        cols = slice(g * width, (g + 1) * width)
        for c in stages[g]:
            c.wait()
        pair[0, own] = mark_dead(pair[0, own], rows_live)
        pair[3, own] = wide[:, cols].astype(BF16)
        if mask is None:
            mask = local_mask(core, pair)
            marks = nt(jnp.ones((8, HEAD), BF16), pair[0, :, :HEAD])[0:1]
            live[...] = jnp.where(marks < MARK_LIMIT, 1.0, 0.0)
        for h in range(width // HEAD):
            at = slice(h * HEAD, (h + 1) * HEAD)
            scores = jnp.where(mask, nt(pair[0, :, at], pair[2, :, at]) * scale, NEG_FILL)
            partial_stats(scores, nt(pair[1, :, at], pair[3, :, at]), stats, g * width // HEAD + h)
    for c in x_copies:
        c.wait()


def local_stats(route_pos, keys, values, queries, d_gated, sib, x_routed, x_sib):
    _, slots, half = sib.shape
    heads = half // HEAD
    anywhere = pl.BlockSpec(memory_space=pl.ANY)
    return pl.pallas_call(
        functools.partial(local_stats_kernel, HEAD**-0.5),
        out_shape=[
            jax.ShapeDtypeStruct((3, heads, 2 * slots), F32),
            jax.ShapeDtypeStruct((1, 2 * slots), F32),
            pltpu.VMEM((4, 2 * slots, half // 2), BF16),
            pltpu.VMEM((4, 2 * slots, half // 2), BF16),
            pltpu.VMEM((2, slots, x_routed.shape[2]), BF16),
        ],
        in_specs=[VMEM] + [anywhere] * 7,
        out_specs=[VMEM] * 5,
        scratch_shapes=[pltpu.VMEM((slots, half), F32), pltpu.SemaphoreType.DMA((16,)), pltpu.SemaphoreType.DMA((4,))],
        compiler_params=params(14),
        cost_estimate=cost(16 * slots * slots * half, 16 * slots * half, 4 * slots * slots * half // HEAD),
        name="local_stats",
    )(route_pos, *in_hbm(keys, values, queries, d_gated), sib, x_routed, x_sib)


def cross_stats_kernel(scale, near, far, straight, diag, cross, stats, kept):
    slots, width = straight.shape[1], straight.shape[2]
    chip = here()[1]
    top, bottom = slice(0, slots), slice(slots, 2 * slots)

    @pl.when(chip == 0)
    def _():
        for part in range(2):
            cross[part] = far[part]
            cross[2 + part, top] = straight[part]
            cross[2 + part, bottom] = diag[part]

    @pl.when(chip != 0)
    def _():
        for part in range(2):
            cross[part, top] = straight[part]
            cross[part, bottom] = diag[part]
            cross[2 + part] = near[2 + part]

    live = cross[0, :, :HEAD].astype(F32) < MARK_LIMIT
    mask = jnp.concatenate([live] * (2 * slots // HEAD), axis=1)
    heads = width // HEAD
    for h in range(heads):
        cols = slice(h * HEAD, (h + 1) * HEAD)
        scores = jnp.where(mask, nt(cross[0, :, cols], cross[2, :, cols]) * scale, NEG_FILL)
        kept_stats(scores, nt(cross[1, :, cols], cross[3, :, cols]), kept, stats, h)


def cross_stats(near, far, straight, diag):
    _, slots, width = straight.shape
    heads = width // HEAD
    return pl.pallas_call(
        functools.partial(cross_stats_kernel, HEAD**-0.5),
        out_shape=[
            pltpu.VMEM((4, 2 * slots, width), BF16),
            jax.ShapeDtypeStruct((3, heads, 2 * slots), F32),
            pltpu.VMEM((2, heads, 2 * slots, 2 * slots), BF16),
        ],
        in_specs=[VMEM] * 4,
        out_specs=[VMEM] * 3,
        compiler_params=params(10),
        cost_estimate=cost(16 * slots * slots * width, 32 * slots * width, 4 * slots * slots * heads),
        name="cross_stats",
    )(near, far, straight, diag)


NONE = (-3e38, 0.0, 0.0)


def merge(first, second):
    top = jnp.maximum(first[0], second[0])
    a, b = jnp.exp(first[0] - top), jnp.exp(second[0] - top)
    inverse = 1.0 / (first[1] * a + second[1] * b)
    return a * inverse, (first[2] * a + second[2] * b) * inverse


def choose(flag, yes, no):
    return [jnp.where(flag, y, n) for y, n in zip(yes, no)]


def gradients(q, k, dg, e, gw, scale, factor, delta):
    weights = e * factor
    ds = (weights * ((gw - delta) * scale)).astype(BF16)
    return tn(ds, k), nn(ds, q), nn(weights.astype(BF16), dg)


def local_gradients(pair, h, mask, scale, top, factor, delta):
    cols = slice(h * HEAD, (h + 1) * HEAD)
    k, v, q, dg = [pair[i, :, cols] for i in range(4)]
    e = jnp.exp(jnp.where(mask, nt(k, q) * scale, NEG_FILL) - top)
    return gradients(q, k, dg, e, nt(v, dg), scale, factor, delta)


def near_grad_kernel(scale, pair, local, stats, gates, dq_out, own_out, sib_out, sum_out):
    slots, width = own_out.shape[1], own_out.shape[2]
    heads = width // HEAD
    first = here()[1] == 0
    near = [local[i, :heads] for i in range(3)]
    factor, delta = merge(near, choose(first, NONE, [stats[i] for i in range(3)]))
    factor = factor * gates[...]
    sum_out[...] = jnp.sum(delta, axis=0, keepdims=True)
    mask = local_mask(here()[0], pair)
    for h in range(heads):
        cols = slice(h * HEAD, (h + 1) * HEAD)
        row = slice(h, h + 1)
        dq, dk, dv = local_gradients(pair, h, mask, scale, near[0][row], factor[row], delta[row])
        dq_out[:, cols] = dq
        for i, part in enumerate((dk, dv)):
            own_out[i, :, cols] = part[:slots].astype(BF16)
            sib_out[i, :, cols] = part[slots:].astype(BF16)


def near_grad(pair, local, stats, gates):
    _, rows, width = pair.shape
    slots = rows // 2
    out = pltpu.VMEM((2, slots, width), BF16)
    return pl.pallas_call(
        functools.partial(near_grad_kernel, HEAD**-0.5),
        out_shape=[pltpu.VMEM((2 * slots, width), F32), out, out, jax.ShapeDtypeStruct(gates.shape, F32)],
        in_specs=[VMEM] * 4,
        out_specs=[VMEM] * 4,
        compiler_params=params(8),
        cost_estimate=cost(20 * slots * slots * width, 40 * slots * width),
        name="near_grad",
    )(pair, local, stats, gates)


def put_terms(grad, rows_x, out_ref):
    high = grad.astype(BF16)
    rest = grad - high.astype(F32)
    mid = rest.astype(BF16)
    low = (rest - mid.astype(F32)).astype(BF16)
    slots = rows_x.shape[1]
    row = lax.broadcasted_iota(jnp.int32, (8, grad.shape[1]), 0)
    lhs = jnp.where(row == 0, high.astype(F32), jnp.where(row == 1, mid.astype(F32), jnp.where(row == 2, low.astype(F32), 0.0)))
    lhs = lhs.astype(BF16)
    term = jnp.sum(nn(lhs[:, :slots], rows_x[0]) + nn(lhs[:, slots:], rows_x[1]), axis=0, keepdims=True)
    parts, copies, _, chunk = out_ref.shape
    for j in range(parts):
        for i in range(copies):
            out_ref[j, i] = term[:, j * chunk : (j + 1) * chunk]


def cross_grad_kernel(scale, total, cross, kept, stats, local, heard, gates, near_dq, near_sum, rows_x, straight, diag, dq_out, keep, final, terms, held, sem):
    slots, width = straight.shape[1], straight.shape[2]
    heads = width // HEAD
    first = here()[1] == 0
    late = jnp.where(first, 0.0, 1.0)
    mine = [stats[i] for i in range(3)]
    other = [heard[i] for i in range(3)]
    near = [local[i, :heads] for i in range(3)]
    far = [local[i, heads:] for i in range(3)]
    factor, delta = merge(mine, choose(first, other, near))
    factor = factor * jnp.where(first, heard[3], jnp.broadcast_to(gates[...], factor.shape))
    final[0], final[1] = merge(far, choose(first, NONE, other))
    sums = near_sum[...] + jnp.sum(final[1], axis=0, keepdims=True)
    put_terms(sums * gates[...] * (1.0 - gates[...]) * (1.0 / total), rows_x, held)
    leaving = pltpu.make_async_copy(held, terms, sem)
    leaving.start()
    for h in range(heads):
        cols = slice(h * HEAD, (h + 1) * HEAD)
        row = slice(h, h + 1)
        dq, dk, dv = gradients(
            cross[2, :, cols], cross[0, :, cols], cross[3, :, cols],
            kept[0, h].astype(F32), kept[1, h].astype(F32), scale, factor[row], delta[row],
        )
        dq_out[:, cols] = (near_dq[:, cols] + late * dq).astype(BF16)
        keep[0, :, cols] = dk.astype(BF16)
        keep[1, :, cols] = dv.astype(BF16)
        sent = jnp.where(first, dq, dk).astype(BF16)
        straight[0, :, cols] = sent[:slots]
        diag[0, :, cols] = sent[slots:]
        straight[1, :, cols] = dv[:slots].astype(BF16)
        diag[1, :, cols] = dv[slots:].astype(BF16)
    leaving.wait()


def cross_grad(cross, kept, stats, local, heard, gates, near_dq, near_sum, rows_x, parts, copies, total):
    _, rows, width = cross.shape
    slots = rows // 2
    out = pltpu.VMEM((2, slots, width), BF16)
    spread = (parts, copies, 1, rows_x.shape[2] // parts)
    return pl.pallas_call(
        functools.partial(cross_grad_kernel, HEAD**-0.5, total),
        out_shape=[
            out,
            out,
            pltpu.VMEM((rows, width), BF16),
            pltpu.VMEM((2, rows, width), BF16),
            jax.ShapeDtypeStruct((2, width // HEAD, rows), F32),
            pltpu.HBM(spread, F32),
        ],
        in_specs=[VMEM] * 9,
        out_specs=[VMEM] * 5 + [pl.BlockSpec(memory_space=pltpu.HBM)],
        scratch_shapes=[pltpu.VMEM(spread, F32), pltpu.SemaphoreType.DMA],
        compiler_params=params(12),
        cost_estimate=cost(24 * slots * slots * width, 64 * slots * width),
        name="cross_grad",
    )(cross, kept, stats, local, heard, gates, near_dq, near_sum, rows_x)


def far_grad_kernel(scale, pair, local, final, gates, keep, near_dq, near_own, near_sib, own_out, sib_out):
    slots, width = pair.shape[1] // 2, pair.shape[2]
    heads = width // HEAD
    early = jnp.where(here()[1] == 0, 1.0, 0.0)
    factor = final[0] * gates[...]
    mask = local_mask(here()[0], pair)
    own_out[0, :, :width] = near_dq[:slots]
    sib_out[0, :, :width] = near_dq[slots:]
    for i in range(2):
        own_out[1 + i, :, :width] = near_own[i]
        sib_out[1 + i, :, :width] = near_sib[i]
    for h in range(heads):
        cols = slice(width + h * HEAD, width + (h + 1) * HEAD)
        at = slice(h * HEAD, (h + 1) * HEAD)
        row = slice(h, h + 1)
        top = local[0, heads + h : heads + h + 1]
        dq, dk, dv = local_gradients(pair, h, mask, scale, top, factor[row], final[1, row])
        dk = dk + early * keep[0, :, at].astype(F32)
        dv = dv + early * keep[1, :, at].astype(F32)
        for i, part in enumerate((dq, dk, dv)):
            own_out[i, :, cols] = part[:slots].astype(BF16)
            sib_out[i, :, cols] = part[slots:].astype(BF16)


def far_grad(pair, local, final, gates, keep, near_dq, near_own, near_sib):
    _, rows, width = pair.shape
    slots, half = rows // 2, 2 * width
    out = jax.ShapeDtypeStruct((3, slots, half), BF16)
    return pl.pallas_call(
        functools.partial(far_grad_kernel, HEAD**-0.5),
        out_shape=[out, out],
        in_specs=[VMEM] * 8,
        out_specs=[VMEM] * 2,
        compiler_params=params(10),
        cost_estimate=cost(20 * slots * slots * half, 40 * slots * half),
        name="far_grad",
    )(pair, local, final, gates, keep, near_dq, near_own, near_sib)


def own_join_kernel(own, dq_out, dk_out, dv_out, waiting, total, sems):
    slots, half = own.shape[1], own.shape[2]
    width = half // 2
    core, chip = here()
    cols = pl.ds(pl.multiple_of(core * half, HEAD), half)
    stores = []
    for j, out in enumerate((dq_out, dk_out, dv_out)):
        total[j] = own[j].astype(F32)
        stores.append(pltpu.make_async_copy(total.at[j], out.at[0, :, cols], sems.at[j]))
        stores[-1].start()
    waiting[0] = jnp.where(chip == 0, total[1, :, :width], total[0, :, width:]).astype(BF16)
    waiting[1] = own[2, :, :width]
    for c in stores:
        c.wait()


def own_join(own, shape):
    out = pltpu.HBM(shape, F32)
    _, slots, half = own.shape
    hbm = pl.BlockSpec(memory_space=pltpu.HBM)
    return pl.pallas_call(
        own_join_kernel,
        out_shape=[out] * 3 + [jax.ShapeDtypeStruct((2, slots, half // 2), BF16)],
        in_specs=[VMEM],
        out_specs=[hbm] * 3 + [VMEM],
        scratch_shapes=[pltpu.VMEM((3, slots, half), F32), pltpu.SemaphoreType.DMA((3,))],
        compiler_params=params(5),
        cost_estimate=cost(0, 18 * own.size),
        name="own_join",
    )(own)


def sib_join_kernel(sib, dq_in, dk_in, dv_in, dq_out, dk_out, dv_out, waiting, low, total, in_sems, out_sems):
    half = sib.shape[2]
    width = half // 2
    core, chip = here()
    loads = [pltpu.make_async_copy(sib.at[j], low.at[j], in_sems.at[j]) for j in range(3)]
    for c in loads:
        c.start()
    cols = pl.ds(pl.multiple_of((1 - core) * half, HEAD), half)
    stores = []
    for j, out in enumerate((dq_out, dk_out, dv_out)):
        loads[j].wait()
        total[j] = low[j].astype(F32)
        stores.append(pltpu.make_async_copy(total.at[j], out.at[0, :, cols], out_sems.at[j]))
        stores[-1].start()
    waiting[0] = jnp.where(chip == 0, total[1, :, :width], total[0, :, width:]).astype(BF16)
    waiting[1] = low[2, :, :width]
    for c in stores:
        c.wait()


def sib_join(sib, outs):
    _, slots, half = sib.shape
    hbm = pl.BlockSpec(memory_space=pltpu.HBM)
    return pl.pallas_call(
        sib_join_kernel,
        out_shape=[pltpu.HBM(o.shape, F32) for o in outs] + [pltpu.VMEM((2, slots, half // 2), BF16)],
        in_specs=[pl.BlockSpec(memory_space=pl.ANY)] + [hbm] * 3,
        out_specs=[hbm] * 3 + [VMEM],
        scratch_shapes=[
            pltpu.VMEM((3, slots, half), BF16),
            pltpu.VMEM((3, slots, half), F32),
            pltpu.SemaphoreType.DMA((3,)),
            pltpu.SemaphoreType.DMA((3,)),
        ],
        input_output_aliases={1: 0, 2: 1, 3: 2},
        compiler_params=params(6),
        cost_estimate=cost(0, 12 * sib.size),
        name="sib_join",
    )(sib, *in_hbm(*outs))


def add_back_kernel(own, sib, straight, diag, dq_in, dk_in, dv_in, dq_out, dk_out, dv_out, total, sems):
    width = straight.shape[2]
    core, chip = here()
    ends = ((own, straight, 2 * core * width), (sib, diag, 2 * (1 - core) * width))

    def store(i, j, out, offset):
        cols = pl.ds(pl.multiple_of(ends[i][2] + offset, HEAD), width)
        copy = pltpu.make_async_copy(total.at[i, j], out.at[0, :, cols], sems.at[2 * i + j])
        copy.start()
        return copy

    @pl.when(chip == 0)
    def _():
        copies = []
        for i, (waiting, back, _) in enumerate(ends):
            for j, out in enumerate((dk_out, dv_out)):
                total[i, j] = waiting[j].astype(F32) + back[j].astype(F32)
                copies.append(store(i, j, out, 0))
        for c in copies:
            c.wait()

    @pl.when(chip != 0)
    def _():
        copies = []
        for i, (waiting, back, _) in enumerate(ends):
            total[i, 0] = waiting[0].astype(F32) + back[0].astype(F32)
            copies.append(store(i, 0, dq_out, width))
        for c in copies:
            c.wait()


def add_back(own, sib, straight, diag, outs):
    hbm = pl.BlockSpec(memory_space=pltpu.HBM)
    return pl.pallas_call(
        add_back_kernel,
        out_shape=[pltpu.HBM(o.shape, F32) for o in outs],
        in_specs=[VMEM] * 4 + [hbm] * 3,
        out_specs=[hbm] * 3,
        scratch_shapes=[pltpu.VMEM((2, *own.shape), F32), pltpu.SemaphoreType.DMA((4,))],
        input_output_aliases={4: 0, 5: 1, 6: 2},
        compiler_params=params(5),
        cost_estimate=cost(0, 24 * own.size),
        name="add_back",
    )(own, sib, straight, diag, *in_hbm(*outs))


def swap_body(route_pos, x_routed, w_router, queries, keys, values, d_gated):
    slots = queries.shape[1]
    n, ndp = lax.axis_size("ctx"), lax.axis_size("dp")

    def send(a, flip):
        return lax.ppermute(a, "ctx", [(i, i ^ flip) for i in range(n)])

    def beside(fn, *operands):
        def skip(*ops):
            return jax.tree.map(lambda o: jnp.zeros(o.shape, o.dtype), jax.eval_shape(fn, *ops))

        return lax.cond(route_pos[0, 0] >= -1, fn, skip, *operands)

    def after(value, *others):
        return lax.optimization_barrier((value, *others))[0]

    def widen(part, step, *first):
        other = lax.ppermute(part, "dp", [(i, i ^ step) for i in range(ndp)])
        return jnp.concatenate([part, after(other, *first)], axis=1)

    def exchange_phase(x_routed, w_part, theirs):
        sib, x_sib = send(theirs, 1), send(x_routed, 1)
        step = 2
        while 2 * step < ndp:
            w_part = widen(w_part, step)
            step *= 2
        return sib, x_sib, w_part

    def far_phase(*operands):
        own_out, sib_out = far_grad(*operands)
        sib_in = send(sib_out, 1)
        *outs, waiting = own_join(own_out, queries.shape)
        *outs, waiting_sib = sib_join(sib_in, outs)
        return outs, waiting, waiting_sib

    out_s, out_d, w_part = cross_pack(route_pos, w_router, keys, values, queries, d_gated)
    in_s, in_d = send(out_s, 2), send(out_d, 3)

    theirs = sib_pack(after(route_pos, out_s), keys, values, queries, d_gated)
    if ndp > 1:
        w_part = widen(w_part, 1, theirs)
    sib, x_sib, w_part = beside(exchange_phase, x_routed, w_part, theirs)
    local, live, near, far, rows_x = local_stats(route_pos, keys, values, queries, d_gated, sib, x_routed, x_sib)
    cross, stats, kept = cross_stats(near, far, in_s, in_d)
    if ndp > 2:
        w_part = widen(w_part, ndp // 2, stats)
    gates, message = pair_gate(live, rows_x, w_part, local, stats, ndp)

    heard = send(message, 2)
    near_dq, near_own, near_sib, near_sum = near_grad(near, local, stats, gates)
    total = float(ndp * n * slots // 2)
    back_s, back_d, dq_low, keep, final, terms = cross_grad(
        cross, kept, stats, local, heard, gates, near_dq, near_sum, rows_x, ndp, n, total
    )

    ret_s, ret_d = send(back_s, 2), send(back_d, 3)
    shared = lax.all_to_all(terms.reshape(ndp * n, 1, -1), ("dp", "ctx"), 0, 0, tiled=True)
    outs, waiting, waiting_sib = beside(far_phase, far, local, final, gates, keep, dq_low, near_own, near_sib)
    dq, dk, dv = add_back(waiting, waiting_sib, ret_s, ret_d, outs)
    router_grad = jnp.sum(after(shared, dq), axis=(0, 1))
    return dq, dk, dv, router_grad


def body(route_pos, x_routed, w_router, queries, keys, values, d_gated):
    slots, full = queries.shape[1], queries.shape[2]
    n, ndp = lax.axis_size("ctx"), lax.axis_size("dp")
    chips = n // 2
    me, dp_me = lax.axis_index("ctx"), lax.axis_index("dp")
    core = (me % 2).astype(jnp.int32).reshape(1)
    half = full // 2
    groups = GROUPS if (half // HEAD) % GROUPS == 0 else 1
    width = half // groups

    sib_pairs = [(i, i ^ 1) for i in range(n)]

    def forward_pairs(step, flip):
        return [(i, (i + 2 * step) ^ flip) for i in range(n) if i + 2 * step < n]

    def back_pairs(step, flip):
        return [(b, a) for a, b in forward_pairs(step, flip)]

    def to_sib(a):
        return lax.ppermute(a, "ctx", sib_pairs)

    links = [(step, flip) for step in range(1, chips) for flip in (0, 1)]

    w_row = w_router.reshape(1, -1)
    w_parts = [w_row] + [
        lax.ppermute(w_row, "dp", [(i, (i + s) % ndp) for i in range(ndp)]) for s in range(1, ndp)
    ]
    live = (route_pos >= 0).astype(jnp.int32)
    lives = [live, to_sib(live)] + [lax.ppermute(live, "ctx", forward_pairs(*link)) for link in links]
    live_all = jnp.concatenate(lives, axis=0)

    kv_mine, kv_theirs = pack(core, keys, values, groups, width)
    kv_far = [
        [lax.ppermute((kv_theirs if flip else kv_mine)[g], "ctx", forward_pairs(step, flip)) for step, flip in links]
        for g in range(groups)
    ]
    q_mine, q_theirs = pack(core, queries, d_gated, groups, width)
    kv_sib = [to_sib(a) for a in kv_theirs]
    q_sib = [to_sib(a) for a in q_theirs]

    offsets = ((dp_me - jnp.arange(ndp)) % ndp).astype(jnp.int32)
    gate = router_gate(offsets, route_pos, x_routed, w_parts)
    gates = (gate, to_sib(gate))

    accs = (jnp.zeros((1, slots), F32), jnp.zeros((1, slots), F32))
    dq_own, sib_in, kv_own, back = [], [], [], []
    for g in range(groups):
        dq, sib_out, kv_local, kv_remote, accs = attention(
            core, live_all, gates, accs, q_mine[g], q_sib[g], [kv_mine[g], kv_sib[g], *kv_far[g]]
        )
        back.append([lax.ppermute(a, "ctx", back_pairs(*link)) for a, link in zip(kv_remote, links)])
        sib_in.append(to_sib(sib_out))
        dq_own.append(dq)
        kv_own.append(kv_local)

    targets = ((dp_me + jnp.arange(ndp)) % ndp).astype(jnp.int32)
    terms = router_terms(targets, gate, accs[0], to_sib(accs[1]), x_routed, ndp)
    mine = terms[0]
    for s in range(1, ndp):
        mine = mine + lax.ppermute(terms[s], "dp", [(i, (i + s) % ndp) for i in range(ndp)])
    total = mine
    for s in range(1, n):
        total = total + lax.ppermute(mine, "ctx", [(i, (i + s) % n) for i in range(n)])
    router_grad = total[0] / float(ndp * n * slots // 2)

    dq, dk, dv = combine(core, dq_own, sib_in, kv_own, back, queries.shape)
    return dq, dk, dv, router_grad


def solution(mesh):
    placed = (
        P("dp", "ctx"),
        P("dp", "ctx", None),
        P("dp"),
        P("dp", "ctx", None),
        P("dp", "ctx", None),
        P("dp", "ctx", None),
        P("dp", "ctx", None),
    )
    ndp = mesh.shape["dp"]
    paired = mesh.shape["ctx"] == 4 and ndp & (ndp - 1) == 0
    return jax.shard_map(
        swap_body if paired else body,
        mesh=mesh,
        in_specs=placed,
        out_specs=(P("dp", "ctx", None), P("dp", "ctx", None), P("dp", "ctx", None), P("dp")),
        check_vma=False,
    )
```

```python
import functools

import jax
import jax.numpy as jnp
from jax import lax
from jax.experimental import pallas as pl
from jax.experimental.pallas import tpu as pltpu
from jax.sharding import PartitionSpec as P

HEAD = 128
GROUPS = 4
NEG_FILL = -1e30
MIB = 1024 * 1024
BF16 = jnp.bfloat16
F32 = jnp.float32

VMEM = pl.BlockSpec(memory_space=pltpu.VMEM)
SMEM = pl.BlockSpec(memory_space=pltpu.SMEM)


def params(mib=16):
    return pltpu.CompilerParams(vmem_limit_bytes=mib * MIB)


def cost(flops, nbytes, exps=0):
    return pl.CostEstimate(flops=1, bytes_accessed=1, transcendentals=0)


def in_hbm(*arrays):
    return [pltpu.with_memory_space_constraint(a, pltpu.HBM) for a in arrays]


def nt(a, b):
    return lax.dot_general(a, b, (((1,), (1,)), ((), ())), preferred_element_type=F32)


def nn(a, b):
    return lax.dot_general(a, b, (((1,), (0,)), ((), ())), preferred_element_type=F32)


def tn(a, b):
    return lax.dot_general(a, b, (((0,), (0,)), ((), ())), preferred_element_type=F32)


def pack_kernel(groups, width, core_ref, first_ref, second_ref, *outs):
    half = first_ref.shape[-1] // 2
    core = core_ref[0]
    for side in range(2):
        base = (core if side == 0 else 1 - core) * half
        for g in range(groups):
            out = outs[side * groups + g]
            cols = pl.ds(pl.multiple_of(base + g * width, HEAD), width)
            out[0] = first_ref[0, :, cols].astype(BF16)
            out[1] = second_ref[0, :, cols].astype(BF16)


def pack(core, first, second, groups, width):
    slots = first.shape[1]
    out = jax.ShapeDtypeStruct((2, slots, width), BF16)
    res = pl.pallas_call(
        functools.partial(pack_kernel, groups, width),
        out_shape=[out] * (2 * groups),
        in_specs=[SMEM, VMEM, VMEM],
        out_specs=[VMEM] * (2 * groups),
        compiler_params=params(),
        cost_estimate=cost(0, 2 * first.size * 4),
        name="pack",
    )(core, first, second)
    return res[:groups], res[groups:]


def gate_kernel(parts, offset_ref, pos_ref, x_ref, *refs):
    w_refs, out_ref = refs[:parts], refs[parts]
    chunk = w_refs[0].shape[-1]
    total = jnp.zeros((8, x_ref.shape[1]), F32)
    for s in range(parts):
        cols = pl.ds(pl.multiple_of(offset_ref[s] * chunk, HEAD), chunk)
        w_rows = jnp.broadcast_to(w_refs[s][...].astype(F32), (8, chunk)).astype(BF16)
        total = total + nt(w_rows, x_ref[0, :, cols])
    gate = 1.0 / (1.0 + jnp.exp(-total[0:1]))
    out_ref[...] = jnp.where(pos_ref[...] >= 0, gate, 0.0)


def router_gate(offsets, route_pos, x_routed, w_parts):
    parts = len(w_parts)
    return pl.pallas_call(
        functools.partial(gate_kernel, parts),
        out_shape=jax.ShapeDtypeStruct(route_pos.shape, F32),
        in_specs=[SMEM] + [VMEM] * (2 + parts),
        out_specs=VMEM,
        compiler_params=params(),
        cost_estimate=cost(16 * x_routed.size, x_routed.size * 2),
        name="router_gate",
    )(offsets, route_pos, x_routed, *w_parts)


def attention_kernel(remote, scale, core_ref, live_ref, gate_own, gate_sib, acc_own, acc_sib, q_own, q_sib, *refs):
    chunks = 2 + remote
    kv = refs[:chunks]
    outs = refs[chunks:]
    dq_own, sib_out, kv_own = outs[:3]
    kv_remote = outs[3 : 3 + remote]
    sum_own, sum_sib = outs[3 + remote :]
    slots, width = q_own.shape[1], q_own.shape[2]
    core = core_ref[0]
    key = lax.broadcasted_iota(jnp.int32, (slots, slots), 0)
    query = lax.broadcasted_iota(jnp.int32, (slots, slots), 1)
    counts = [jnp.sum(live_ref[i : i + 1], axis=1, keepdims=True) for i in range(chunks)]
    lives = [key < counts[i] for i in range(chunks)]
    own_later = core == 1
    bias_rows = []
    for i in range(chunks):
        live = lives[i]
        if i == 0:
            pair = (live & (key <= query), live & jnp.logical_not(own_later))
        elif i == 1:
            pair = (live & own_later, live & (key <= query))
        else:
            pair = (live, live)
        bias_rows.append(jnp.concatenate([jnp.where(p, 0.0, NEG_FILL) for p in pair], axis=1))
    bias = jnp.concatenate(bias_rows, axis=0)
    gates = jnp.concatenate([gate_own[...], gate_sib[...]], axis=1)
    total = jnp.zeros((1, 2 * slots), F32)
    for h in range(width // HEAD):
        cols = slice(h * HEAD, (h + 1) * HEAD)
        q = jnp.concatenate([q_own[0, :, cols], q_sib[0, :, cols]], axis=0)
        dg = jnp.concatenate([q_own[1, :, cols], q_sib[1, :, cols]], axis=0)
        k = jnp.concatenate([r[0, :, cols] for r in kv], axis=0)
        v = jnp.concatenate([r[1, :, cols] for r in kv], axis=0)
        scores = nt(k, q) * scale + bias
        top = jnp.max(scores, axis=0, keepdims=True)
        e = jnp.exp(scores - top)
        inverse = 1.0 / jnp.sum(e, axis=0, keepdims=True)
        gw = nt(v, dg)
        delta = jnp.sum(e * gw, axis=0, keepdims=True) * inverse
        total = total + delta
        weights = e * (inverse * gates)
        dv = nn(weights.astype(BF16), dg)
        ds = (weights * ((gw - delta) * scale)).astype(BF16)
        dk = nn(ds, q)
        dq = tn(ds, k)
        dq_own[:, cols] = dq[:slots].astype(dq_own.dtype)
        sib_out[0, :, cols] = dq[slots:].astype(BF16)
        kv_own[0, :, cols] = dk[:slots].astype(BF16)
        kv_own[1, :, cols] = dv[:slots].astype(BF16)
        sib_out[1, :, cols] = dk[slots : 2 * slots].astype(BF16)
        sib_out[2, :, cols] = dv[slots : 2 * slots].astype(BF16)
        for i in range(remote):
            rows = slice((2 + i) * slots, (3 + i) * slots)
            kv_remote[i][0, :, cols] = dk[rows].astype(BF16)
            kv_remote[i][1, :, cols] = dv[rows].astype(BF16)
    sum_own[...] = acc_own[...] + total[:, :slots]
    sum_sib[...] = acc_sib[...] + total[:, slots:]


def attention(core, live, gates, accs, q_own, q_sib, kv):
    remote = len(kv) - 2
    _, slots, width = q_own.shape
    pair = jax.ShapeDtypeStruct((2, slots, width), BF16)
    row = jax.ShapeDtypeStruct((1, slots), F32)
    outs = [
        jax.ShapeDtypeStruct((slots, width), BF16),
        jax.ShapeDtypeStruct((3, slots, width), BF16),
        pair,
        *([pair] * remote),
        row,
        row,
    ]
    keys = (2 + remote) * slots
    res = pl.pallas_call(
        functools.partial(attention_kernel, remote, HEAD**-0.5),
        out_shape=outs,
        in_specs=[SMEM] + [VMEM] * (7 + len(kv)),
        out_specs=[VMEM] * len(outs),
        compiler_params=params(48),
        cost_estimate=cost(20 * slots * keys * width, 8 * keys * width + 20 * slots * width, 2 * slots * keys * width // HEAD),
        name="attention",
    )(core, live, *gates, *accs, q_own, q_sib, *kv)
    return res[0], res[1], res[2], res[3 : 3 + remote], (res[3 + remote], res[4 + remote])


def combine_kernel(groups, width, remote, core_ref, *refs):
    dq_own, sib, kv_own = refs[:groups], refs[groups : 2 * groups], refs[2 * groups : 3 * groups]
    back = refs[3 * groups : 3 * groups + groups * remote]
    dq_out, dk_out, dv_out = refs[3 * groups + groups * remote :]
    half = groups * width
    core = core_ref[0]
    for g in range(groups):
        own = pl.ds(pl.multiple_of(core * half + g * width, HEAD), width)
        other = pl.ds(pl.multiple_of((1 - core) * half + g * width, HEAD), width)
        dq_out[0, :, own] = dq_own[g][...].astype(F32)
        dq_out[0, :, other] = sib[g][0].astype(F32)
        for i, out in enumerate((dk_out, dv_out)):
            mine = kv_own[g][i].astype(F32)
            theirs = sib[g][1 + i].astype(F32)
            for r in range(remote):
                part = back[g * remote + r][i].astype(F32)
                if r % 2 == 0:
                    mine = mine + part
                else:
                    theirs = theirs + part
            out[0, :, own] = mine
            out[0, :, other] = theirs


def combine(core, dq_own, sib, kv_own, back, shape):
    groups = len(dq_own)
    remote = len(back[0])
    out = jax.ShapeDtypeStruct(shape, F32)
    flat = [*dq_own, *sib, *kv_own, *(b for group in back for b in group)]
    return pl.pallas_call(
        functools.partial(combine_kernel, groups, dq_own[0].shape[-1], remote),
        out_shape=[out] * 3,
        in_specs=[SMEM] + [VMEM] * len(flat),
        out_specs=[VMEM] * 3,
        compiler_params=params(48),
        cost_estimate=cost(0, 3 * out.size * 6),
        name="combine",
    )(core, *flat)


def router_kernel(parts, target_ref, gate_ref, own_ref, sib_ref, x_ref, *outs):
    gate = gate_ref[...]
    grad = (own_ref[...] + sib_ref[...]) * gate * (1.0 - gate)
    high = grad.astype(BF16)
    rest = grad - high.astype(F32)
    mid = rest.astype(BF16)
    low = (rest - mid.astype(F32)).astype(BF16)
    row = lax.broadcasted_iota(jnp.int32, (8, grad.shape[1]), 0)
    lhs = jnp.where(row == 0, high.astype(F32), jnp.where(row == 1, mid.astype(F32), jnp.where(row == 2, low.astype(F32), 0.0)))
    lhs = lhs.astype(BF16)
    chunk = outs[0].shape[-1]
    for s in range(parts):
        cols = pl.ds(pl.multiple_of(target_ref[s] * chunk, HEAD), chunk)
        outs[s][...] = jnp.sum(nn(lhs, x_ref[0, :, cols]), axis=0, keepdims=True)


def router_terms(targets, gate, own, sib, x_routed, parts):
    chunk = x_routed.shape[-1] // parts
    return pl.pallas_call(
        functools.partial(router_kernel, parts),
        out_shape=[jax.ShapeDtypeStruct((1, chunk), F32)] * parts,
        in_specs=[SMEM] + [VMEM] * 4,
        out_specs=[VMEM] * parts,
        compiler_params=params(),
        cost_estimate=cost(16 * x_routed.size, x_routed.size * 2),
        name="router_terms",
    )(targets, gate, own, sib, x_routed)


def here():
    me = lax.axis_index("ctx")
    return lax.rem(me, 2), lax.div(me, 2)


MARK = 2.0**60
MARK_LIMIT = 2.0**50


def live_rows(pos_ref, slots):
    count = jnp.sum((pos_ref[...] >= 0).astype(jnp.int32), axis=1, keepdims=True)
    return lax.broadcasted_iota(jnp.int32, (slots, HEAD), 0) < count


def mark_dead(keys, live):
    width = keys.shape[-1]
    mask = jnp.concatenate([live] * (width // HEAD), axis=1)
    return jnp.where(mask, keys.astype(F32), MARK).astype(BF16)


def cross_pack_kernel(pos_any, w_any, k_ref, v_ref, q_ref, dg_ref, straight, diag, w_out, wide, pos_ref, w_ref, sems):
    small = [pltpu.make_async_copy(pos_any, pos_ref, sems.at[4]), pltpu.make_async_copy(w_any, w_ref, sems.at[5])]
    for c in small:
        c.start()
    slots, width = straight.shape[1], straight.shape[2]
    half = k_ref.shape[-1] // 2
    core, chip = here()
    ends = ((straight, core * half), (diag, (1 - core) * half))

    def copies(first, second, targets, offset):
        out = []
        for i, (end, start) in enumerate(ends):
            cols = pl.ds(pl.multiple_of(start + offset, HEAD), width)
            out.append(pltpu.make_async_copy(first.at[0, :, cols], end.at[0], sems.at[2 * i]))
            out.append(pltpu.make_async_copy(second.at[0, :, cols], targets[i], sems.at[2 * i + 1]))
        for c in out:
            c.start()
        for c in out:
            c.wait()

    @pl.when(chip == 0)
    def _():
        copies(k_ref, v_ref, (straight.at[1], diag.at[1]), 0)
        small[0].wait()
        live = live_rows(pos_ref, slots)
        for end, _ in ends:
            end[0] = mark_dead(end[0], live)

    @pl.when(chip != 0)
    def _():
        copies(q_ref, dg_ref, (wide.at[0], wide.at[1]), width)
        small[0].wait()
        for i, (end, _) in enumerate(ends):
            end[1] = wide[i].astype(BF16)

    small[1].wait()
    w_out[...] = w_ref[...].astype(F32).reshape(w_out.shape)


def cross_pack(route_pos, w_router, keys, values, queries, d_gated):
    _, slots, full = keys.shape
    cross = pltpu.VMEM((2, slots, full // 4), BF16)
    hbm = pl.BlockSpec(memory_space=pltpu.HBM)
    return pl.pallas_call(
        cross_pack_kernel,
        out_shape=[cross, cross, jax.ShapeDtypeStruct((1, w_router.shape[0]), F32)],
        in_specs=[hbm] * 6,
        out_specs=[VMEM] * 3,
        scratch_shapes=[
            pltpu.VMEM((2, slots, full // 4), F32),
            pltpu.VMEM(route_pos.shape, jnp.int32),
            pltpu.VMEM(w_router.shape, BF16),
            pltpu.SemaphoreType.DMA((6,)),
        ],
        compiler_params=params(),
        cost_estimate=cost(0, 10 * slots * full),
        name="cross_pack",
    )(*in_hbm(route_pos, w_router, keys, values, queries, d_gated))


def sib_pack_kernel(pos_ref, k_ref, v_ref, q_ref, dg_ref, out, wide, sems):
    slots, half = out.shape[1], out.shape[2]
    cols = pl.ds(pl.multiple_of((1 - here()[0]) * half, HEAD), half)
    sources = ((k_ref, out.at[0]), (dg_ref, wide), (v_ref, out.at[1]), (q_ref, out.at[2]))
    copies = [pltpu.make_async_copy(src.at[0, :, cols], dst, sems.at[i]) for i, (src, dst) in enumerate(sources)]
    for c in copies:
        c.start()
    live = live_rows(pos_ref, slots)
    copies[0].wait()
    out[0] = mark_dead(out[0], live)
    copies[1].wait()
    out[3] = wide[...].astype(BF16)
    copies[2].wait()
    copies[3].wait()


def sib_pack(route_pos, keys, values, queries, d_gated):
    _, slots, full = keys.shape
    hbm = pl.BlockSpec(memory_space=pltpu.HBM)
    return pl.pallas_call(
        sib_pack_kernel,
        out_shape=pltpu.VMEM((4, slots, full // 2), BF16),
        in_specs=[VMEM, hbm, hbm, hbm, hbm],
        out_specs=VMEM,
        scratch_shapes=[pltpu.VMEM((slots, full // 2), F32), pltpu.SemaphoreType.DMA((4,))],
        compiler_params=params(),
        cost_estimate=cost(0, 20 * slots * full),
        name="sib_pack",
    )(route_pos, *in_hbm(keys, values, queries, d_gated))


def pair_gate_kernel(parts, live_ref, rows_x, w_ref, local, stats, out_ref, message):
    chunk = w_ref.shape[1] // parts
    slots = rows_x.shape[1]
    for i in range(2):
        total = jnp.zeros((8, slots), F32)
        for j in range(parts):
            w_rows = jnp.broadcast_to(w_ref[:, j * chunk : (j + 1) * chunk], (8, chunk)).astype(BF16)
            cols = pl.ds(pl.multiple_of((lax.axis_index("dp") ^ j) * chunk, HEAD), chunk)
            total = total + nt(w_rows, rows_x[i, :, cols])
        lanes = slice(i * slots, (i + 1) * slots)
        out_ref[:, lanes] = live_ref[:, lanes] / (1.0 + jnp.exp(-total[0:1]))
    first = here()[1] == 0
    heads = stats.shape[1]
    for i in range(3):
        message[i] = jnp.where(first, stats[i], local[i, heads:])
    message[3] = jnp.broadcast_to(out_ref[...], message.shape[1:])


def pair_gate(live, rows_x, w_full, local, stats, parts):
    _, heads, lanes = stats.shape
    return pl.pallas_call(
        functools.partial(pair_gate_kernel, parts),
        out_shape=[jax.ShapeDtypeStruct(live.shape, F32), jax.ShapeDtypeStruct((4, heads, lanes), F32)],
        in_specs=[VMEM] * 5,
        out_specs=[VMEM] * 2,
        compiler_params=params(),
        cost_estimate=cost(16 * rows_x.size, rows_x.size * 2),
        name="router_gate",
    )(live, rows_x, w_full, local, stats)


def local_mask(core, pair):
    slots = pair.shape[1] // 2
    key = lax.broadcasted_iota(jnp.int32, (slots, slots), 0)
    query = lax.broadcasted_iota(jnp.int32, (slots, slots), 1)
    causal = key <= query
    own_live = pair[0, :slots, :slots].astype(F32) < MARK_LIMIT
    sib_live = pair[0, slots:, :slots].astype(F32) < MARK_LIMIT
    own_rows = jnp.concatenate([own_live & causal, own_live & (core == 0)], axis=1)
    sib_rows = jnp.concatenate([sib_live & (core == 1), sib_live & causal], axis=1)
    return jnp.concatenate([own_rows, sib_rows], axis=0)


def kept_stats(scores, gw, kept, stats, h):
    top = jnp.max(scores, axis=0, keepdims=True)
    e = jnp.exp(scores - top).astype(BF16)
    gw = gw.astype(BF16)
    kept[0, h] = e
    kept[1, h] = gw
    e = e.astype(F32)
    stats[0, h : h + 1] = top
    stats[1, h : h + 1] = jnp.sum(e, axis=0, keepdims=True)
    stats[2, h : h + 1] = jnp.sum(e * gw.astype(F32), axis=0, keepdims=True)


def partial_stats(scores, gw, stats, h):
    top = jnp.max(scores, axis=0, keepdims=True)
    e = jnp.exp(scores - top)
    stats[0, h : h + 1] = top
    stats[1, h : h + 1] = jnp.sum(e, axis=0, keepdims=True)
    stats[2, h : h + 1] = jnp.sum(e * gw, axis=0, keepdims=True)


def local_stats_kernel(scale, pos_ref, k_ref, v_ref, q_ref, dg_ref, sib, x_ref, x_sib, stats, live, near, far, rows_x, wide, sems, x_sems):
    slots, half = sib.shape[1], sib.shape[2]
    width = half // 2
    core = here()[0]
    own, other = slice(0, slots), slice(slots, 2 * slots)
    stages = []
    for g, pair in enumerate((near, far)):
        cols = slice(g * width, (g + 1) * width)
        held = pl.ds(pl.multiple_of(core * half + g * width, HEAD), width)
        copies = [
            pltpu.make_async_copy(ref.at[0, :, held], pair.at[j, own], sems.at[8 * g + j])
            for j, ref in enumerate((k_ref, v_ref, q_ref))
        ]
        copies.append(pltpu.make_async_copy(dg_ref.at[0, :, held], wide.at[:, cols], sems.at[8 * g + 3]))
        for j in range(4):
            copies.append(pltpu.make_async_copy(sib.at[j, :, cols], pair.at[j, other], sems.at[8 * g + 4 + j]))
        for c in copies:
            c.start()
        stages.append(copies)
    x_copies = []
    depth = x_ref.shape[2] // 2
    for i, ref in enumerate((x_ref, x_sib)):
        for g in range(2):
            cols = slice(g * depth, (g + 1) * depth)
            x_copies.append(pltpu.make_async_copy(ref.at[0, :, cols], rows_x.at[i, :, cols], x_sems.at[2 * i + g]))
    for c in x_copies:
        c.start()
    rows_live = live_rows(pos_ref, slots)
    mask = None
    for g, pair in enumerate((near, far)):
        cols = slice(g * width, (g + 1) * width)
        for c in stages[g]:
            c.wait()
        pair[0, own] = mark_dead(pair[0, own], rows_live)
        pair[3, own] = wide[:, cols].astype(BF16)
        if mask is None:
            mask = local_mask(core, pair)
            marks = nt(jnp.ones((8, HEAD), BF16), pair[0, :, :HEAD])[0:1]
            live[...] = jnp.where(marks < MARK_LIMIT, 1.0, 0.0)
        for h in range(width // HEAD):
            at = slice(h * HEAD, (h + 1) * HEAD)
            scores = jnp.where(mask, nt(pair[0, :, at], pair[2, :, at]) * scale, NEG_FILL)
            partial_stats(scores, nt(pair[1, :, at], pair[3, :, at]), stats, g * width // HEAD + h)
    for c in x_copies:
        c.wait()


def local_stats(route_pos, keys, values, queries, d_gated, sib, x_routed, x_sib):
    _, slots, half = sib.shape
    heads = half // HEAD
    anywhere = pl.BlockSpec(memory_space=pl.ANY)
    return pl.pallas_call(
        functools.partial(local_stats_kernel, HEAD**-0.5),
        out_shape=[
            jax.ShapeDtypeStruct((3, heads, 2 * slots), F32),
            jax.ShapeDtypeStruct((1, 2 * slots), F32),
            pltpu.VMEM((4, 2 * slots, half // 2), BF16),
            pltpu.VMEM((4, 2 * slots, half // 2), BF16),
            pltpu.VMEM((2, slots, x_routed.shape[2]), BF16),
        ],
        in_specs=[VMEM] + [anywhere] * 7,
        out_specs=[VMEM] * 5,
        scratch_shapes=[pltpu.VMEM((slots, half), F32), pltpu.SemaphoreType.DMA((16,)), pltpu.SemaphoreType.DMA((4,))],
        compiler_params=params(),
        cost_estimate=cost(16 * slots * slots * half, 16 * slots * half, 4 * slots * slots * half // HEAD),
        name="local_stats",
    )(route_pos, *in_hbm(keys, values, queries, d_gated), sib, x_routed, x_sib)


def cross_stats_kernel(scale, near, far, straight, diag, cross, stats, kept):
    slots, width = straight.shape[1], straight.shape[2]
    chip = here()[1]
    top, bottom = slice(0, slots), slice(slots, 2 * slots)

    @pl.when(chip == 0)
    def _():
        for part in range(2):
            cross[part] = far[part]
            cross[2 + part, top] = straight[part]
            cross[2 + part, bottom] = diag[part]

    @pl.when(chip != 0)
    def _():
        for part in range(2):
            cross[part, top] = straight[part]
            cross[part, bottom] = diag[part]
            cross[2 + part] = near[2 + part]

    live = cross[0, :, :HEAD].astype(F32) < MARK_LIMIT
    mask = jnp.concatenate([live] * (2 * slots // HEAD), axis=1)
    heads = width // HEAD
    for h in range(heads):
        cols = slice(h * HEAD, (h + 1) * HEAD)
        scores = jnp.where(mask, nt(cross[0, :, cols], cross[2, :, cols]) * scale, NEG_FILL)
        kept_stats(scores, nt(cross[1, :, cols], cross[3, :, cols]), kept, stats, h)


def cross_stats(near, far, straight, diag):
    _, slots, width = straight.shape
    heads = width // HEAD
    return pl.pallas_call(
        functools.partial(cross_stats_kernel, HEAD**-0.5),
        out_shape=[
            pltpu.VMEM((4, 2 * slots, width), BF16),
            jax.ShapeDtypeStruct((3, heads, 2 * slots), F32),
            pltpu.VMEM((2, heads, 2 * slots, 2 * slots), BF16),
        ],
        in_specs=[VMEM] * 4,
        out_specs=[VMEM] * 3,
        compiler_params=params(),
        cost_estimate=cost(16 * slots * slots * width, 32 * slots * width, 4 * slots * slots * heads),
        name="cross_stats",
    )(near, far, straight, diag)


NONE = (-3e38, 0.0, 0.0)


def merge(first, second):
    top = jnp.maximum(first[0], second[0])
    a, b = jnp.exp(first[0] - top), jnp.exp(second[0] - top)
    inverse = 1.0 / (first[1] * a + second[1] * b)
    return a * inverse, (first[2] * a + second[2] * b) * inverse


def choose(flag, yes, no):
    return [jnp.where(flag, y, n) for y, n in zip(yes, no)]


def gradients(q, k, dg, e, gw, scale, factor, delta):
    weights = e * factor
    ds = (weights * ((gw - delta) * scale)).astype(BF16)
    return tn(ds, k), nn(ds, q), nn(weights.astype(BF16), dg)


def local_gradients(pair, h, mask, scale, top, factor, delta):
    cols = slice(h * HEAD, (h + 1) * HEAD)
    k, v, q, dg = [pair[i, :, cols] for i in range(4)]
    e = jnp.exp(jnp.where(mask, nt(k, q) * scale, NEG_FILL) - top)
    return gradients(q, k, dg, e, nt(v, dg), scale, factor, delta)


def near_grad_kernel(scale, pair, local, stats, gates, dq_out, own_out, sib_out, sum_out):
    slots, width = own_out.shape[1], own_out.shape[2]
    heads = width // HEAD
    first = here()[1] == 0
    near = [local[i, :heads] for i in range(3)]
    factor, delta = merge(near, choose(first, NONE, [stats[i] for i in range(3)]))
    factor = factor * gates[...]
    sum_out[...] = jnp.sum(delta, axis=0, keepdims=True)
    mask = local_mask(here()[0], pair)
    for h in range(heads):
        cols = slice(h * HEAD, (h + 1) * HEAD)
        row = slice(h, h + 1)
        dq, dk, dv = local_gradients(pair, h, mask, scale, near[0][row], factor[row], delta[row])
        dq_out[:, cols] = dq
        for i, part in enumerate((dk, dv)):
            own_out[i, :, cols] = part[:slots].astype(BF16)
            sib_out[i, :, cols] = part[slots:].astype(BF16)


def near_grad(pair, local, stats, gates):
    _, rows, width = pair.shape
    slots = rows // 2
    out = pltpu.VMEM((2, slots, width), BF16)
    return pl.pallas_call(
        functools.partial(near_grad_kernel, HEAD**-0.5),
        out_shape=[pltpu.VMEM((2 * slots, width), F32), out, out, jax.ShapeDtypeStruct(gates.shape, F32)],
        in_specs=[VMEM] * 4,
        out_specs=[VMEM] * 4,
        compiler_params=params(),
        cost_estimate=cost(20 * slots * slots * width, 40 * slots * width),
        name="near_grad",
    )(pair, local, stats, gates)


def put_terms(grad, rows_x, out_ref):
    high = grad.astype(BF16)
    rest = grad - high.astype(F32)
    mid = rest.astype(BF16)
    low = (rest - mid.astype(F32)).astype(BF16)
    slots = rows_x.shape[1]
    row = lax.broadcasted_iota(jnp.int32, (8, grad.shape[1]), 0)
    lhs = jnp.where(row == 0, high.astype(F32), jnp.where(row == 1, mid.astype(F32), jnp.where(row == 2, low.astype(F32), 0.0)))
    lhs = lhs.astype(BF16)
    term = jnp.sum(nn(lhs[:, :slots], rows_x[0]) + nn(lhs[:, slots:], rows_x[1]), axis=0, keepdims=True)
    parts, copies, _, chunk = out_ref.shape
    for j in range(parts):
        for i in range(copies):
            out_ref[j, i] = term[:, j * chunk : (j + 1) * chunk]


def cross_grad_kernel(scale, total, cross, kept, stats, local, heard, gates, near_dq, near_sum, rows_x, near_own, near_sib, straight, diag, own_low, sib_low, keep, final, terms, held, sem):
    slots, width = straight.shape[1], straight.shape[2]
    heads = width // HEAD
    first = here()[1] == 0
    late = jnp.where(first, 0.0, 1.0)
    mine = [stats[i] for i in range(3)]
    other = [heard[i] for i in range(3)]
    near = [local[i, :heads] for i in range(3)]
    far = [local[i, heads:] for i in range(3)]
    factor, delta = merge(mine, choose(first, other, near))
    factor = factor * jnp.where(first, heard[3], jnp.broadcast_to(gates[...], factor.shape))
    final[0], final[1] = merge(far, choose(first, NONE, other))
    sums = near_sum[...] + jnp.sum(final[1], axis=0, keepdims=True)
    put_terms(sums * gates[...] * (1.0 - gates[...]) * (1.0 / total), rows_x, held)
    leaving = pltpu.make_async_copy(held, terms, sem)
    leaving.start()
    for i in range(2):
        own_low[1 + i] = near_own[i]
        sib_low[1 + i] = near_sib[i]
    for h in range(heads):
        cols = slice(h * HEAD, (h + 1) * HEAD)
        row = slice(h, h + 1)
        dq, dk, dv = gradients(
            cross[2, :, cols], cross[0, :, cols], cross[3, :, cols],
            kept[0, h].astype(F32), kept[1, h].astype(F32), scale, factor[row], delta[row],
        )
        whole = (near_dq[:, cols] + late * dq).astype(BF16)
        own_low[0, :, cols] = whole[:slots]
        sib_low[0, :, cols] = whole[slots:]
        keep[0, :, cols] = dk.astype(BF16)
        keep[1, :, cols] = dv.astype(BF16)
        sent = jnp.where(first, dq, dk).astype(BF16)
        straight[0, :, cols] = sent[:slots]
        diag[0, :, cols] = sent[slots:]
        straight[1, :, cols] = dv[:slots].astype(BF16)
        diag[1, :, cols] = dv[slots:].astype(BF16)
    leaving.wait()


def cross_grad(cross, kept, stats, local, heard, gates, near_dq, near_sum, rows_x, near_own, near_sib, parts, copies, total):
    _, rows, width = cross.shape
    slots = rows // 2
    out = pltpu.VMEM((2, slots, width), BF16)
    spread = (parts, copies, 1, rows_x.shape[2] // parts)
    return pl.pallas_call(
        functools.partial(cross_grad_kernel, HEAD**-0.5, total),
        out_shape=[
            out,
            out,
            pltpu.VMEM((3, slots, width), BF16),
            pltpu.VMEM((3, slots, width), BF16),
            pltpu.VMEM((2, rows, width), BF16),
            jax.ShapeDtypeStruct((2, width // HEAD, rows), F32),
            pltpu.HBM(spread, F32),
        ],
        in_specs=[VMEM] * 11,
        out_specs=[VMEM] * 6 + [pl.BlockSpec(memory_space=pltpu.HBM)],
        scratch_shapes=[pltpu.VMEM(spread, F32), pltpu.SemaphoreType.DMA],
        compiler_params=params(),
        cost_estimate=cost(24 * slots * slots * width, 64 * slots * width),
        name="cross_grad",
    )(cross, kept, stats, local, heard, gates, near_dq, near_sum, rows_x, near_own, near_sib)


def far_grad_kernel(scale, pair, local, final, gates, keep, own_out, sib_out):
    slots, width = pair.shape[1] // 2, pair.shape[2]
    heads = width // HEAD
    early = jnp.where(here()[1] == 0, 1.0, 0.0)
    factor = final[0] * gates[...]
    mask = local_mask(here()[0], pair)
    for h in range(heads):
        at = slice(h * HEAD, (h + 1) * HEAD)
        row = slice(h, h + 1)
        top = local[0, heads + h : heads + h + 1]
        dq, dk, dv = local_gradients(pair, h, mask, scale, top, factor[row], final[1, row])
        dk = dk + early * keep[0, :, at].astype(F32)
        dv = dv + early * keep[1, :, at].astype(F32)
        for i, part in enumerate((dq, dk, dv)):
            own_out[i, :, at] = part[:slots].astype(BF16)
            sib_out[i, :, at] = part[slots:].astype(BF16)


def far_grad(pair, local, final, gates, keep):
    _, rows, width = pair.shape
    slots = rows // 2
    out = jax.ShapeDtypeStruct((3, slots, width), BF16)
    return pl.pallas_call(
        functools.partial(far_grad_kernel, HEAD**-0.5),
        out_shape=[out, out],
        in_specs=[VMEM] * 5,
        out_specs=[VMEM] * 2,
        compiler_params=params(),
        cost_estimate=cost(20 * slots * slots * width, 40 * slots * width),
        name="far_grad",
    )(pair, local, final, gates, keep)


def own_join_kernel(low, high, dq_out, dk_out, dv_out, waiting, total, sems):
    width = low.shape[2]
    core, chip = here()
    cols = pl.ds(pl.multiple_of(core * 2 * width, HEAD), 2 * width)
    stores = []
    for j, out in enumerate((dq_out, dk_out, dv_out)):
        total[j, :, :width] = low[j].astype(F32)
        total[j, :, width:] = high[j].astype(F32)
        stores.append(pltpu.make_async_copy(total.at[j], out.at[0, :, cols], sems.at[j]))
        stores[-1].start()
    waiting[0] = jnp.where(chip == 0, total[1, :, :width], total[0, :, width:]).astype(BF16)
    waiting[1] = low[2]
    for c in stores:
        c.wait()


def own_join(low, high, shape):
    out = pltpu.HBM(shape, F32)
    _, slots, width = low.shape
    hbm = pl.BlockSpec(memory_space=pltpu.HBM)
    return pl.pallas_call(
        own_join_kernel,
        out_shape=[out] * 3 + [jax.ShapeDtypeStruct((2, slots, width), BF16)],
        in_specs=[VMEM] * 2,
        out_specs=[hbm] * 3 + [VMEM],
        scratch_shapes=[pltpu.VMEM((3, slots, 2 * width), F32), pltpu.SemaphoreType.DMA((3,))],
        compiler_params=params(),
        cost_estimate=cost(0, 36 * low.size),
        name="own_join",
    )(low, high)


def sib_join_kernel(low, high, dq_in, dk_in, dv_in, dq_out, dk_out, dv_out, waiting, parts, total, in_sems, out_sems):
    width = low.shape[2]
    core, chip = here()
    loads = [
        [pltpu.make_async_copy(ref.at[j], parts.at[i, j], in_sems.at[3 * i + j]) for i, ref in enumerate((low, high))]
        for j in range(3)
    ]
    for pair in loads:
        for c in pair:
            c.start()
    cols = pl.ds(pl.multiple_of((1 - core) * 2 * width, HEAD), 2 * width)
    stores = []
    for j, out in enumerate((dq_out, dk_out, dv_out)):
        for i in range(2):
            loads[j][i].wait()
            total[j, :, i * width : (i + 1) * width] = parts[i, j].astype(F32)
        stores.append(pltpu.make_async_copy(total.at[j], out.at[0, :, cols], out_sems.at[j]))
        stores[-1].start()
    waiting[0] = jnp.where(chip == 0, total[1, :, :width], total[0, :, width:]).astype(BF16)
    waiting[1] = parts[0, 2]
    for c in stores:
        c.wait()


def sib_join(low, high, outs):
    _, slots, width = low.shape
    hbm = pl.BlockSpec(memory_space=pltpu.HBM)
    return pl.pallas_call(
        sib_join_kernel,
        out_shape=[pltpu.HBM(o.shape, F32) for o in outs] + [pltpu.VMEM((2, slots, width), BF16)],
        in_specs=[pl.BlockSpec(memory_space=pl.ANY)] * 2 + [hbm] * 3,
        out_specs=[hbm] * 3 + [VMEM],
        scratch_shapes=[
            pltpu.VMEM((2, 3, slots, width), BF16),
            pltpu.VMEM((3, slots, 2 * width), F32),
            pltpu.SemaphoreType.DMA((6,)),
            pltpu.SemaphoreType.DMA((3,)),
        ],
        input_output_aliases={2: 0, 3: 1, 4: 2},
        compiler_params=params(),
        cost_estimate=cost(0, 24 * low.size),
        name="sib_join",
    )(low, high, *in_hbm(*outs))


def add_back_kernel(own, sib, straight, diag, dq_in, dk_in, dv_in, dq_out, dk_out, dv_out, total, sems):
    width = straight.shape[2]
    core, chip = here()
    ends = ((own, straight, 2 * core * width), (sib, diag, 2 * (1 - core) * width))

    def store(i, j, out, offset):
        cols = pl.ds(pl.multiple_of(ends[i][2] + offset, HEAD), width)
        copy = pltpu.make_async_copy(total.at[i, j], out.at[0, :, cols], sems.at[2 * i + j])
        copy.start()
        return copy

    @pl.when(chip == 0)
    def _():
        copies = []
        for i, (waiting, back, _) in enumerate(ends):
            for j, out in enumerate((dk_out, dv_out)):
                total[i, j] = waiting[j].astype(F32) + back[j].astype(F32)
                copies.append(store(i, j, out, 0))
        for c in copies:
            c.wait()

    @pl.when(chip != 0)
    def _():
        copies = []
        for i, (waiting, back, _) in enumerate(ends):
            total[i, 0] = waiting[0].astype(F32) + back[0].astype(F32)
            copies.append(store(i, 0, dq_out, width))
        for c in copies:
            c.wait()


def add_back(own, sib, straight, diag, outs):
    hbm = pl.BlockSpec(memory_space=pltpu.HBM)
    return pl.pallas_call(
        add_back_kernel,
        out_shape=[pltpu.HBM(o.shape, F32) for o in outs],
        in_specs=[VMEM] * 4 + [hbm] * 3,
        out_specs=[hbm] * 3,
        scratch_shapes=[pltpu.VMEM((2, *own.shape), F32), pltpu.SemaphoreType.DMA((4,))],
        input_output_aliases={4: 0, 5: 1, 6: 2},
        compiler_params=params(),
        cost_estimate=cost(0, 24 * own.size),
        name="add_back",
    )(own, sib, straight, diag, *in_hbm(*outs))


def swap_body(route_pos, x_routed, w_router, queries, keys, values, d_gated):
    slots = queries.shape[1]
    n, ndp = lax.axis_size("ctx"), lax.axis_size("dp")

    def send(a, flip):
        return lax.ppermute(a, "ctx", [(i, i ^ flip) for i in range(n)])

    def beside(fn, *operands):
        def skip(*ops):
            return jax.tree.map(lambda o: jnp.zeros(o.shape, o.dtype), jax.eval_shape(fn, *ops))

        return lax.cond(route_pos[0, 0] >= -1, fn, skip, *operands)

    def after(value, *others):
        return lax.optimization_barrier((value, *others))[0]

    def widen(part, step, *first):
        other = lax.ppermute(part, "dp", [(i, i ^ step) for i in range(ndp)])
        return jnp.concatenate([part, after(other, *first)], axis=1)

    def exchange_phase(x_routed, w_part, theirs):
        sib, x_sib = send(theirs, 1), send(x_routed, 1)
        step = 2
        while 2 * step < ndp:
            w_part = widen(w_part, step)
            step *= 2
        return sib, x_sib, w_part

    def far_phase(own_low, sib_low, *operands):
        sib_in = [send(sib_low, 1)]
        own_high, sib_high = far_grad(*operands)
        sib_in.append(send(sib_high, 1))
        *outs, waiting = own_join(own_low, own_high, queries.shape)
        *outs, waiting_sib = sib_join(*sib_in, outs)
        return outs, waiting, waiting_sib

    out_s, out_d, w_part = cross_pack(route_pos, w_router, keys, values, queries, d_gated)
    in_s, in_d = send(out_s, 2), send(out_d, 3)

    theirs = sib_pack(after(route_pos, out_s), keys, values, queries, d_gated)
    if ndp > 1:
        w_part = widen(w_part, 1, theirs)
    sib, x_sib, w_part = beside(exchange_phase, x_routed, w_part, theirs)
    local, live, near, far, rows_x = local_stats(route_pos, keys, values, queries, d_gated, sib, x_routed, x_sib)
    cross, stats, kept = cross_stats(near, far, in_s, in_d)
    if ndp > 2:
        w_part = widen(w_part, ndp // 2, stats)
    gates, message = pair_gate(live, rows_x, w_part, local, stats, ndp)

    heard = send(message, 2)
    near_dq, near_own, near_sib, near_sum = near_grad(near, local, stats, gates)
    total = float(ndp * n * slots // 2)
    back_s, back_d, own_low, sib_low, keep, final, terms = cross_grad(
        cross, kept, stats, local, heard, gates, near_dq, near_sum, rows_x, near_own, near_sib, ndp, n, total
    )

    ret_s, ret_d = send(back_s, 2), send(back_d, 3)
    shared = lax.all_to_all(terms.reshape(ndp * n, 1, -1), ("dp", "ctx"), 0, 0, tiled=True)
    outs, waiting, waiting_sib = beside(far_phase, own_low, sib_low, far, local, final, gates, keep)
    dq, dk, dv = add_back(waiting, waiting_sib, ret_s, ret_d, outs)
    router_grad = jnp.sum(after(shared, dq), axis=(0, 1))
    return dq, dk, dv, router_grad


def body(route_pos, x_routed, w_router, queries, keys, values, d_gated):
    slots, full = queries.shape[1], queries.shape[2]
    n, ndp = lax.axis_size("ctx"), lax.axis_size("dp")
    chips = n // 2
    me, dp_me = lax.axis_index("ctx"), lax.axis_index("dp")
    core = (me % 2).astype(jnp.int32).reshape(1)
    half = full // 2
    groups = GROUPS if (half // HEAD) % GROUPS == 0 else 1
    width = half // groups

    sib_pairs = [(i, i ^ 1) for i in range(n)]

    def forward_pairs(step, flip):
        return [(i, (i + 2 * step) ^ flip) for i in range(n) if i + 2 * step < n]

    def back_pairs(step, flip):
        return [(b, a) for a, b in forward_pairs(step, flip)]

    def to_sib(a):
        return lax.ppermute(a, "ctx", sib_pairs)

    links = [(step, flip) for step in range(1, chips) for flip in (0, 1)]

    w_row = w_router.reshape(1, -1)
    w_parts = [w_row] + [
        lax.ppermute(w_row, "dp", [(i, (i + s) % ndp) for i in range(ndp)]) for s in range(1, ndp)
    ]
    live = (route_pos >= 0).astype(jnp.int32)
    lives = [live, to_sib(live)] + [lax.ppermute(live, "ctx", forward_pairs(*link)) for link in links]
    live_all = jnp.concatenate(lives, axis=0)

    kv_mine, kv_theirs = pack(core, keys, values, groups, width)
    kv_far = [
        [lax.ppermute((kv_theirs if flip else kv_mine)[g], "ctx", forward_pairs(step, flip)) for step, flip in links]
        for g in range(groups)
    ]
    q_mine, q_theirs = pack(core, queries, d_gated, groups, width)
    kv_sib = [to_sib(a) for a in kv_theirs]
    q_sib = [to_sib(a) for a in q_theirs]

    offsets = ((dp_me - jnp.arange(ndp)) % ndp).astype(jnp.int32)
    gate = router_gate(offsets, route_pos, x_routed, w_parts)
    gates = (gate, to_sib(gate))

    accs = (jnp.zeros((1, slots), F32), jnp.zeros((1, slots), F32))
    dq_own, sib_in, kv_own, back = [], [], [], []
    for g in range(groups):
        dq, sib_out, kv_local, kv_remote, accs = attention(
            core, live_all, gates, accs, q_mine[g], q_sib[g], [kv_mine[g], kv_sib[g], *kv_far[g]]
        )
        back.append([lax.ppermute(a, "ctx", back_pairs(*link)) for a, link in zip(kv_remote, links)])
        sib_in.append(to_sib(sib_out))
        dq_own.append(dq)
        kv_own.append(kv_local)

    targets = ((dp_me + jnp.arange(ndp)) % ndp).astype(jnp.int32)
    terms = router_terms(targets, gate, accs[0], to_sib(accs[1]), x_routed, ndp)
    mine = terms[0]
    for s in range(1, ndp):
        mine = mine + lax.ppermute(terms[s], "dp", [(i, (i + s) % ndp) for i in range(ndp)])
    total = mine
    for s in range(1, n):
        total = total + lax.ppermute(mine, "ctx", [(i, (i + s) % n) for i in range(n)])
    router_grad = total[0] / float(ndp * n * slots // 2)

    dq, dk, dv = combine(core, dq_own, sib_in, kv_own, back, queries.shape)
    return dq, dk, dv, router_grad


def solution(mesh):
    placed = (
        P("dp", "ctx"),
        P("dp", "ctx", None),
        P("dp"),
        P("dp", "ctx", None),
        P("dp", "ctx", None),
        P("dp", "ctx", None),
        P("dp", "ctx", None),
    )
    ndp = mesh.shape["dp"]
    paired = mesh.shape["ctx"] == 4 and ndp & (ndp - 1) == 0
    return jax.shard_map(
        swap_body if paired else body,
        mesh=mesh,
        in_specs=placed,
        out_specs=(P("dp", "ctx", None), P("dp", "ctx", None), P("dp", "ctx", None), P("dp")),
        check_vma=False,
    )
```

```python
import functools

import jax
import jax.numpy as jnp
from jax import lax
from jax.experimental import pallas as pl
from jax.experimental.pallas import tpu as pltpu
from jax.sharding import PartitionSpec as P

HEAD = 128
GROUPS = 4
NEG_FILL = -1e30
MIB = 1024 * 1024
BF16 = jnp.bfloat16
F32 = jnp.float32

VMEM = pl.BlockSpec(memory_space=pltpu.VMEM)
SMEM = pl.BlockSpec(memory_space=pltpu.SMEM)


def params(mib=16):
    return pltpu.CompilerParams(vmem_limit_bytes=mib * MIB)


def cost(flops, nbytes, exps=0):
    return pl.CostEstimate(flops=1, bytes_accessed=1, transcendentals=0)


def in_hbm(*arrays):
    return [pltpu.with_memory_space_constraint(a, pltpu.HBM) for a in arrays]


def nt(a, b):
    return lax.dot_general(a, b, (((1,), (1,)), ((), ())), preferred_element_type=F32)


def nn(a, b):
    return lax.dot_general(a, b, (((1,), (0,)), ((), ())), preferred_element_type=F32)


def tn(a, b):
    return lax.dot_general(a, b, (((0,), (0,)), ((), ())), preferred_element_type=F32)


def pack_kernel(groups, width, core_ref, first_ref, second_ref, *outs):
    half = first_ref.shape[-1] // 2
    core = core_ref[0]
    for side in range(2):
        base = (core if side == 0 else 1 - core) * half
        for g in range(groups):
            out = outs[side * groups + g]
            cols = pl.ds(pl.multiple_of(base + g * width, HEAD), width)
            out[0] = first_ref[0, :, cols].astype(BF16)
            out[1] = second_ref[0, :, cols].astype(BF16)


def pack(core, first, second, groups, width):
    slots = first.shape[1]
    out = jax.ShapeDtypeStruct((2, slots, width), BF16)
    res = pl.pallas_call(
        functools.partial(pack_kernel, groups, width),
        out_shape=[out] * (2 * groups),
        in_specs=[SMEM, VMEM, VMEM],
        out_specs=[VMEM] * (2 * groups),
        compiler_params=params(),
        cost_estimate=cost(0, 2 * first.size * 4),
        name="pack",
    )(core, first, second)
    return res[:groups], res[groups:]


def gate_kernel(parts, offset_ref, pos_ref, x_ref, *refs):
    w_refs, out_ref = refs[:parts], refs[parts]
    chunk = w_refs[0].shape[-1]
    total = jnp.zeros((8, x_ref.shape[1]), F32)
    for s in range(parts):
        cols = pl.ds(pl.multiple_of(offset_ref[s] * chunk, HEAD), chunk)
        w_rows = jnp.broadcast_to(w_refs[s][...].astype(F32), (8, chunk)).astype(BF16)
        total = total + nt(w_rows, x_ref[0, :, cols])
    gate = 1.0 / (1.0 + jnp.exp(-total[0:1]))
    out_ref[...] = jnp.where(pos_ref[...] >= 0, gate, 0.0)


def router_gate(offsets, route_pos, x_routed, w_parts):
    parts = len(w_parts)
    return pl.pallas_call(
        functools.partial(gate_kernel, parts),
        out_shape=jax.ShapeDtypeStruct(route_pos.shape, F32),
        in_specs=[SMEM] + [VMEM] * (2 + parts),
        out_specs=VMEM,
        compiler_params=params(),
        cost_estimate=cost(16 * x_routed.size, x_routed.size * 2),
        name="router_gate",
    )(offsets, route_pos, x_routed, *w_parts)


def attention_kernel(remote, scale, core_ref, live_ref, gate_own, gate_sib, acc_own, acc_sib, q_own, q_sib, *refs):
    chunks = 2 + remote
    kv = refs[:chunks]
    outs = refs[chunks:]
    dq_own, sib_out, kv_own = outs[:3]
    kv_remote = outs[3 : 3 + remote]
    sum_own, sum_sib = outs[3 + remote :]
    slots, width = q_own.shape[1], q_own.shape[2]
    core = core_ref[0]
    key = lax.broadcasted_iota(jnp.int32, (slots, slots), 0)
    query = lax.broadcasted_iota(jnp.int32, (slots, slots), 1)
    counts = [jnp.sum(live_ref[i : i + 1], axis=1, keepdims=True) for i in range(chunks)]
    lives = [key < counts[i] for i in range(chunks)]
    own_later = core == 1
    bias_rows = []
    for i in range(chunks):
        live = lives[i]
        if i == 0:
            pair = (live & (key <= query), live & jnp.logical_not(own_later))
        elif i == 1:
            pair = (live & own_later, live & (key <= query))
        else:
            pair = (live, live)
        bias_rows.append(jnp.concatenate([jnp.where(p, 0.0, NEG_FILL) for p in pair], axis=1))
    bias = jnp.concatenate(bias_rows, axis=0)
    gates = jnp.concatenate([gate_own[...], gate_sib[...]], axis=1)
    total = jnp.zeros((1, 2 * slots), F32)
    for h in range(width // HEAD):
        cols = slice(h * HEAD, (h + 1) * HEAD)
        q = jnp.concatenate([q_own[0, :, cols], q_sib[0, :, cols]], axis=0)
        dg = jnp.concatenate([q_own[1, :, cols], q_sib[1, :, cols]], axis=0)
        k = jnp.concatenate([r[0, :, cols] for r in kv], axis=0)
        v = jnp.concatenate([r[1, :, cols] for r in kv], axis=0)
        scores = nt(k, q) * scale + bias
        top = jnp.max(scores, axis=0, keepdims=True)
        e = jnp.exp(scores - top)
        inverse = 1.0 / jnp.sum(e, axis=0, keepdims=True)
        gw = nt(v, dg)
        delta = jnp.sum(e * gw, axis=0, keepdims=True) * inverse
        total = total + delta
        weights = e * (inverse * gates)
        dv = nn(weights.astype(BF16), dg)
        ds = (weights * ((gw - delta) * scale)).astype(BF16)
        dk = nn(ds, q)
        dq = tn(ds, k)
        dq_own[:, cols] = dq[:slots].astype(dq_own.dtype)
        sib_out[0, :, cols] = dq[slots:].astype(BF16)
        kv_own[0, :, cols] = dk[:slots].astype(BF16)
        kv_own[1, :, cols] = dv[:slots].astype(BF16)
        sib_out[1, :, cols] = dk[slots : 2 * slots].astype(BF16)
        sib_out[2, :, cols] = dv[slots : 2 * slots].astype(BF16)
        for i in range(remote):
            rows = slice((2 + i) * slots, (3 + i) * slots)
            kv_remote[i][0, :, cols] = dk[rows].astype(BF16)
            kv_remote[i][1, :, cols] = dv[rows].astype(BF16)
    sum_own[...] = acc_own[...] + total[:, :slots]
    sum_sib[...] = acc_sib[...] + total[:, slots:]


def attention(core, live, gates, accs, q_own, q_sib, kv):
    remote = len(kv) - 2
    _, slots, width = q_own.shape
    pair = jax.ShapeDtypeStruct((2, slots, width), BF16)
    row = jax.ShapeDtypeStruct((1, slots), F32)
    outs = [
        jax.ShapeDtypeStruct((slots, width), BF16),
        jax.ShapeDtypeStruct((3, slots, width), BF16),
        pair,
        *([pair] * remote),
        row,
        row,
    ]
    keys = (2 + remote) * slots
    res = pl.pallas_call(
        functools.partial(attention_kernel, remote, HEAD**-0.5),
        out_shape=outs,
        in_specs=[SMEM] + [VMEM] * (7 + len(kv)),
        out_specs=[VMEM] * len(outs),
        compiler_params=params(48),
        cost_estimate=cost(20 * slots * keys * width, 8 * keys * width + 20 * slots * width, 2 * slots * keys * width // HEAD),
        name="attention",
    )(core, live, *gates, *accs, q_own, q_sib, *kv)
    return res[0], res[1], res[2], res[3 : 3 + remote], (res[3 + remote], res[4 + remote])


def combine_kernel(groups, width, remote, core_ref, *refs):
    dq_own, sib, kv_own = refs[:groups], refs[groups : 2 * groups], refs[2 * groups : 3 * groups]
    back = refs[3 * groups : 3 * groups + groups * remote]
    dq_out, dk_out, dv_out = refs[3 * groups + groups * remote :]
    half = groups * width
    core = core_ref[0]
    for g in range(groups):
        own = pl.ds(pl.multiple_of(core * half + g * width, HEAD), width)
        other = pl.ds(pl.multiple_of((1 - core) * half + g * width, HEAD), width)
        dq_out[0, :, own] = dq_own[g][...].astype(F32)
        dq_out[0, :, other] = sib[g][0].astype(F32)
        for i, out in enumerate((dk_out, dv_out)):
            mine = kv_own[g][i].astype(F32)
            theirs = sib[g][1 + i].astype(F32)
            for r in range(remote):
                part = back[g * remote + r][i].astype(F32)
                if r % 2 == 0:
                    mine = mine + part
                else:
                    theirs = theirs + part
            out[0, :, own] = mine
            out[0, :, other] = theirs


def combine(core, dq_own, sib, kv_own, back, shape):
    groups = len(dq_own)
    remote = len(back[0])
    out = jax.ShapeDtypeStruct(shape, F32)
    flat = [*dq_own, *sib, *kv_own, *(b for group in back for b in group)]
    return pl.pallas_call(
        functools.partial(combine_kernel, groups, dq_own[0].shape[-1], remote),
        out_shape=[out] * 3,
        in_specs=[SMEM] + [VMEM] * len(flat),
        out_specs=[VMEM] * 3,
        compiler_params=params(48),
        cost_estimate=cost(0, 3 * out.size * 6),
        name="combine",
    )(core, *flat)


def router_kernel(parts, target_ref, gate_ref, own_ref, sib_ref, x_ref, *outs):
    gate = gate_ref[...]
    grad = (own_ref[...] + sib_ref[...]) * gate * (1.0 - gate)
    high = grad.astype(BF16)
    rest = grad - high.astype(F32)
    mid = rest.astype(BF16)
    low = (rest - mid.astype(F32)).astype(BF16)
    row = lax.broadcasted_iota(jnp.int32, (8, grad.shape[1]), 0)
    lhs = jnp.where(row == 0, high.astype(F32), jnp.where(row == 1, mid.astype(F32), jnp.where(row == 2, low.astype(F32), 0.0)))
    lhs = lhs.astype(BF16)
    chunk = outs[0].shape[-1]
    for s in range(parts):
        cols = pl.ds(pl.multiple_of(target_ref[s] * chunk, HEAD), chunk)
        outs[s][...] = jnp.sum(nn(lhs, x_ref[0, :, cols]), axis=0, keepdims=True)


def router_terms(targets, gate, own, sib, x_routed, parts):
    chunk = x_routed.shape[-1] // parts
    return pl.pallas_call(
        functools.partial(router_kernel, parts),
        out_shape=[jax.ShapeDtypeStruct((1, chunk), F32)] * parts,
        in_specs=[SMEM] + [VMEM] * 4,
        out_specs=[VMEM] * parts,
        compiler_params=params(),
        cost_estimate=cost(16 * x_routed.size, x_routed.size * 2),
        name="router_terms",
    )(targets, gate, own, sib, x_routed)


def here():
    me = lax.axis_index("ctx")
    return lax.rem(me, 2), lax.div(me, 2)


MARK = 2.0**60
MARK_LIMIT = 2.0**50


def live_rows(pos_ref, slots):
    count = jnp.sum((pos_ref[...] >= 0).astype(jnp.int32), axis=1, keepdims=True)
    return lax.broadcasted_iota(jnp.int32, (slots, HEAD), 0) < count


def mark_dead(keys, live):
    width = keys.shape[-1]
    mask = jnp.concatenate([live] * (width // HEAD), axis=1)
    return jnp.where(mask, keys.astype(F32), MARK).astype(BF16)


def cross_pack_kernel(pos_any, w_any, k_ref, v_ref, q_ref, dg_ref, straight, diag, w_out, wide, pos_ref, w_ref, sems):
    small = [pltpu.make_async_copy(pos_any, pos_ref, sems.at[4]), pltpu.make_async_copy(w_any, w_ref, sems.at[5])]
    for c in small:
        c.start()
    slots, width = straight.shape[1], straight.shape[2]
    half = k_ref.shape[-1] // 2
    core, chip = here()
    ends = ((straight, core * half), (diag, (1 - core) * half))

    def copies(first, second, targets, offset):
        out = []
        for i, (end, start) in enumerate(ends):
            cols = pl.ds(pl.multiple_of(start + offset, HEAD), width)
            out.append(pltpu.make_async_copy(first.at[0, :, cols], end.at[0], sems.at[2 * i]))
            out.append(pltpu.make_async_copy(second.at[0, :, cols], targets[i], sems.at[2 * i + 1]))
        for c in out:
            c.start()
        for c in out:
            c.wait()

    @pl.when(chip == 0)
    def _():
        copies(k_ref, v_ref, (straight.at[1], diag.at[1]), 0)
        small[0].wait()
        live = live_rows(pos_ref, slots)
        for end, _ in ends:
            end[0] = mark_dead(end[0], live)

    @pl.when(chip != 0)
    def _():
        copies(q_ref, dg_ref, (wide.at[0], wide.at[1]), width)
        small[0].wait()
        for i, (end, _) in enumerate(ends):
            end[1] = wide[i].astype(BF16)

    small[1].wait()
    w_out[...] = w_ref[...].astype(F32).reshape(w_out.shape)


def cross_pack(route_pos, w_router, keys, values, queries, d_gated):
    _, slots, full = keys.shape
    cross = pltpu.VMEM((2, slots, full // 4), BF16)
    hbm = pl.BlockSpec(memory_space=pltpu.HBM)
    return pl.pallas_call(
        cross_pack_kernel,
        out_shape=[cross, cross, jax.ShapeDtypeStruct((1, w_router.shape[0]), F32)],
        in_specs=[hbm] * 6,
        out_specs=[VMEM] * 3,
        scratch_shapes=[
            pltpu.VMEM((2, slots, full // 4), F32),
            pltpu.VMEM(route_pos.shape, jnp.int32),
            pltpu.VMEM(w_router.shape, BF16),
            pltpu.SemaphoreType.DMA((6,)),
        ],
        compiler_params=params(),
        cost_estimate=cost(0, 10 * slots * full),
        name="cross_pack",
    )(*in_hbm(route_pos, w_router, keys, values, queries, d_gated))


def sib_pack_kernel(pos_ref, k_ref, v_ref, q_ref, dg_ref, out, wide, sems):
    slots, half = out.shape[1], out.shape[2]
    cols = pl.ds(pl.multiple_of((1 - here()[0]) * half, HEAD), half)
    sources = ((k_ref, out.at[0]), (dg_ref, wide), (v_ref, out.at[1]), (q_ref, out.at[2]))
    copies = [pltpu.make_async_copy(src.at[0, :, cols], dst, sems.at[i]) for i, (src, dst) in enumerate(sources)]
    for c in copies:
        c.start()
    live = live_rows(pos_ref, slots)
    copies[0].wait()
    out[0] = mark_dead(out[0], live)
    copies[1].wait()
    out[3] = wide[...].astype(BF16)
    copies[2].wait()
    copies[3].wait()


def sib_pack(route_pos, keys, values, queries, d_gated):
    _, slots, full = keys.shape
    hbm = pl.BlockSpec(memory_space=pltpu.HBM)
    return pl.pallas_call(
        sib_pack_kernel,
        out_shape=pltpu.VMEM((4, slots, full // 2), BF16),
        in_specs=[VMEM, hbm, hbm, hbm, hbm],
        out_specs=VMEM,
        scratch_shapes=[pltpu.VMEM((slots, full // 2), F32), pltpu.SemaphoreType.DMA((4,))],
        compiler_params=params(),
        cost_estimate=cost(0, 20 * slots * full),
        name="sib_pack",
    )(route_pos, *in_hbm(keys, values, queries, d_gated))


def pair_gate_kernel(parts, live_ref, rows_x, w_ref, local, stats, out_ref, message):
    chunk = w_ref.shape[1] // parts
    slots = rows_x.shape[1]
    for i in range(2):
        total = jnp.zeros((8, slots), F32)
        for j in range(parts):
            w_rows = jnp.broadcast_to(w_ref[:, j * chunk : (j + 1) * chunk], (8, chunk)).astype(BF16)
            cols = pl.ds(pl.multiple_of((lax.axis_index("dp") ^ j) * chunk, HEAD), chunk)
            total = total + nt(w_rows, rows_x[i, :, cols])
        lanes = slice(i * slots, (i + 1) * slots)
        out_ref[:, lanes] = live_ref[:, lanes] / (1.0 + jnp.exp(-total[0:1]))
    first = here()[1] == 0
    heads = stats.shape[1]
    for i in range(3):
        message[i] = jnp.where(first, stats[i], local[i, heads:])
    message[3] = jnp.broadcast_to(out_ref[...], message.shape[1:])


def pair_gate(live, rows_x, w_full, local, stats, parts):
    _, heads, lanes = stats.shape
    return pl.pallas_call(
        functools.partial(pair_gate_kernel, parts),
        out_shape=[jax.ShapeDtypeStruct(live.shape, F32), jax.ShapeDtypeStruct((4, heads, lanes), F32)],
        in_specs=[VMEM] * 5,
        out_specs=[VMEM] * 2,
        compiler_params=params(),
        cost_estimate=cost(16 * rows_x.size, rows_x.size * 2),
        name="router_gate",
    )(live, rows_x, w_full, local, stats)


def local_mask(core, pair):
    slots = pair.shape[1] // 2
    key = lax.broadcasted_iota(jnp.int32, (slots, slots), 0)
    query = lax.broadcasted_iota(jnp.int32, (slots, slots), 1)
    causal = key <= query
    own_live = pair[0, :slots, :slots].astype(F32) < MARK_LIMIT
    sib_live = pair[0, slots:, :slots].astype(F32) < MARK_LIMIT
    own_rows = jnp.concatenate([own_live & causal, own_live & (core == 0)], axis=1)
    sib_rows = jnp.concatenate([sib_live & (core == 1), sib_live & causal], axis=1)
    return jnp.concatenate([own_rows, sib_rows], axis=0)


def kept_stats(scores, gw, kept, stats, h):
    top = jnp.max(scores, axis=0, keepdims=True)
    e = jnp.exp(scores - top).astype(BF16)
    gw = gw.astype(BF16)
    kept[0, h] = e
    kept[1, h] = gw
    e = e.astype(F32)
    stats[0, h : h + 1] = top
    stats[1, h : h + 1] = jnp.sum(e, axis=0, keepdims=True)
    stats[2, h : h + 1] = jnp.sum(e * gw.astype(F32), axis=0, keepdims=True)


def partial_stats(scores, gw, stats, h):
    top = jnp.max(scores, axis=0, keepdims=True)
    e = jnp.exp(scores - top)
    stats[0, h : h + 1] = top
    stats[1, h : h + 1] = jnp.sum(e, axis=0, keepdims=True)
    stats[2, h : h + 1] = jnp.sum(e * gw, axis=0, keepdims=True)


def local_stats_kernel(scale, pos_ref, k_ref, v_ref, q_ref, dg_ref, sib, x_ref, x_sib, stats, live, near, far, rows_x, wide, sems, x_sems):
    slots, half = sib.shape[1], sib.shape[2]
    width = half // 2
    core = here()[0]
    own, other = slice(0, slots), slice(slots, 2 * slots)
    stages = []
    for g, pair in enumerate((near, far)):
        cols = slice(g * width, (g + 1) * width)
        held = pl.ds(pl.multiple_of(core * half + g * width, HEAD), width)
        copies = [
            pltpu.make_async_copy(ref.at[0, :, held], pair.at[j, own], sems.at[8 * g + j])
            for j, ref in enumerate((k_ref, v_ref, q_ref))
        ]
        copies.append(pltpu.make_async_copy(dg_ref.at[0, :, held], wide.at[:, cols], sems.at[8 * g + 3]))
        for j in range(4):
            copies.append(pltpu.make_async_copy(sib.at[j, :, cols], pair.at[j, other], sems.at[8 * g + 4 + j]))
        for c in copies:
            c.start()
        stages.append(copies)
    x_copies = []
    depth = x_ref.shape[2] // 2
    for i, ref in enumerate((x_ref, x_sib)):
        for g in range(2):
            cols = slice(g * depth, (g + 1) * depth)
            x_copies.append(pltpu.make_async_copy(ref.at[0, :, cols], rows_x.at[i, :, cols], x_sems.at[2 * i + g]))
    for c in x_copies:
        c.start()
    rows_live = live_rows(pos_ref, slots)
    mask = None
    for g, pair in enumerate((near, far)):
        cols = slice(g * width, (g + 1) * width)
        for c in stages[g]:
            c.wait()
        pair[0, own] = mark_dead(pair[0, own], rows_live)
        pair[3, own] = wide[:, cols].astype(BF16)
        if mask is None:
            mask = local_mask(core, pair)
            marks = nt(jnp.ones((8, HEAD), BF16), pair[0, :, :HEAD])[0:1]
            live[...] = jnp.where(marks < MARK_LIMIT, 1.0, 0.0)
        for h in range(width // HEAD):
            at = slice(h * HEAD, (h + 1) * HEAD)
            scores = jnp.where(mask, nt(pair[0, :, at], pair[2, :, at]) * scale, NEG_FILL)
            partial_stats(scores, nt(pair[1, :, at], pair[3, :, at]), stats, g * width // HEAD + h)
    for c in x_copies:
        c.wait()


def local_stats(route_pos, keys, values, queries, d_gated, sib, x_routed, x_sib):
    _, slots, half = sib.shape
    heads = half // HEAD
    anywhere = pl.BlockSpec(memory_space=pl.ANY)
    return pl.pallas_call(
        functools.partial(local_stats_kernel, HEAD**-0.5),
        out_shape=[
            jax.ShapeDtypeStruct((3, heads, 2 * slots), F32),
            jax.ShapeDtypeStruct((1, 2 * slots), F32),
            pltpu.VMEM((4, 2 * slots, half // 2), BF16),
            pltpu.VMEM((4, 2 * slots, half // 2), BF16),
            pltpu.VMEM((2, slots, x_routed.shape[2]), BF16),
        ],
        in_specs=[VMEM] + [anywhere] * 7,
        out_specs=[VMEM] * 5,
        scratch_shapes=[pltpu.VMEM((slots, half), F32), pltpu.SemaphoreType.DMA((16,)), pltpu.SemaphoreType.DMA((4,))],
        compiler_params=params(),
        cost_estimate=cost(16 * slots * slots * half, 16 * slots * half, 4 * slots * slots * half // HEAD),
        name="local_stats",
    )(route_pos, *in_hbm(keys, values, queries, d_gated), sib, x_routed, x_sib)


def cross_stats_kernel(scale, near, far, straight, diag, cross, stats, kept):
    slots, width = straight.shape[1], straight.shape[2]
    chip = here()[1]
    top, bottom = slice(0, slots), slice(slots, 2 * slots)

    @pl.when(chip == 0)
    def _():
        for part in range(2):
            cross[part] = far[part]
            cross[2 + part, top] = straight[part]
            cross[2 + part, bottom] = diag[part]

    @pl.when(chip != 0)
    def _():
        for part in range(2):
            cross[part, top] = straight[part]
            cross[part, bottom] = diag[part]
            cross[2 + part] = near[2 + part]

    live = cross[0, :, :HEAD].astype(F32) < MARK_LIMIT
    mask = jnp.concatenate([live] * (2 * slots // HEAD), axis=1)
    heads = width // HEAD
    for h in range(heads):
        cols = slice(h * HEAD, (h + 1) * HEAD)
        scores = jnp.where(mask, nt(cross[0, :, cols], cross[2, :, cols]) * scale, NEG_FILL)
        kept_stats(scores, nt(cross[1, :, cols], cross[3, :, cols]), kept, stats, h)


def cross_stats(near, far, straight, diag):
    _, slots, width = straight.shape
    heads = width // HEAD
    return pl.pallas_call(
        functools.partial(cross_stats_kernel, HEAD**-0.5),
        out_shape=[
            pltpu.VMEM((4, 2 * slots, width), BF16),
            jax.ShapeDtypeStruct((3, heads, 2 * slots), F32),
            pltpu.VMEM((2, heads, 2 * slots, 2 * slots), BF16),
        ],
        in_specs=[VMEM] * 4,
        out_specs=[VMEM] * 3,
        compiler_params=params(),
        cost_estimate=cost(16 * slots * slots * width, 32 * slots * width, 4 * slots * slots * heads),
        name="cross_stats",
    )(near, far, straight, diag)


NONE = (-3e38, 0.0, 0.0)


def merge(first, second):
    top = jnp.maximum(first[0], second[0])
    a, b = jnp.exp(first[0] - top), jnp.exp(second[0] - top)
    inverse = 1.0 / (first[1] * a + second[1] * b)
    return a * inverse, (first[2] * a + second[2] * b) * inverse


def choose(flag, yes, no):
    return [jnp.where(flag, y, n) for y, n in zip(yes, no)]


def gradients(q, k, dg, e, gw, scale, factor, delta):
    weights = e * factor
    ds = (weights * ((gw - delta) * scale)).astype(BF16)
    return tn(ds, k), nn(ds, q), nn(weights.astype(BF16), dg)


def local_gradients(pair, h, mask, scale, top, factor, delta):
    cols = slice(h * HEAD, (h + 1) * HEAD)
    k, v, q, dg = [pair[i, :, cols] for i in range(4)]
    e = jnp.exp(jnp.where(mask, nt(k, q) * scale, NEG_FILL) - top)
    return gradients(q, k, dg, e, nt(v, dg), scale, factor, delta)


def near_grad_kernel(scale, pair, local, stats, gates, dq_out, own_out, sib_out, sum_out):
    slots, width = own_out.shape[1], own_out.shape[2]
    heads = width // HEAD
    first = here()[1] == 0
    near = [local[i, :heads] for i in range(3)]
    factor, delta = merge(near, choose(first, NONE, [stats[i] for i in range(3)]))
    factor = factor * gates[...]
    sum_out[...] = jnp.sum(delta, axis=0, keepdims=True)
    mask = local_mask(here()[0], pair)
    for h in range(heads):
        cols = slice(h * HEAD, (h + 1) * HEAD)
        row = slice(h, h + 1)
        dq, dk, dv = local_gradients(pair, h, mask, scale, near[0][row], factor[row], delta[row])
        dq_out[:, cols] = dq
        for i, part in enumerate((dk, dv)):
            own_out[i, :, cols] = part[:slots].astype(BF16)
            sib_out[i, :, cols] = part[slots:].astype(BF16)


def near_grad(pair, local, stats, gates):
    _, rows, width = pair.shape
    slots = rows // 2
    out = pltpu.VMEM((2, slots, width), BF16)
    return pl.pallas_call(
        functools.partial(near_grad_kernel, HEAD**-0.5),
        out_shape=[pltpu.VMEM((2 * slots, width), F32), out, out, jax.ShapeDtypeStruct(gates.shape, F32)],
        in_specs=[VMEM] * 4,
        out_specs=[VMEM] * 4,
        compiler_params=params(),
        cost_estimate=cost(20 * slots * slots * width, 40 * slots * width),
        name="near_grad",
    )(pair, local, stats, gates)


def put_terms(grad, rows_x, out_ref):
    high = grad.astype(BF16)
    rest = grad - high.astype(F32)
    mid = rest.astype(BF16)
    low = (rest - mid.astype(F32)).astype(BF16)
    slots = rows_x.shape[1]
    row = lax.broadcasted_iota(jnp.int32, (8, grad.shape[1]), 0)
    lhs = jnp.where(row == 0, high.astype(F32), jnp.where(row == 1, mid.astype(F32), jnp.where(row == 2, low.astype(F32), 0.0)))
    lhs = lhs.astype(BF16)
    term = jnp.sum(nn(lhs[:, :slots], rows_x[0]) + nn(lhs[:, slots:], rows_x[1]), axis=0, keepdims=True)
    parts, copies, _, chunk = out_ref.shape
    for j in range(parts):
        for i in range(copies):
            out_ref[j, i] = term[:, j * chunk : (j + 1) * chunk]


def cross_grad_kernel(scale, total, cross, kept, stats, local, heard, gates, near_dq, near_sum, rows_x, near_own, near_sib, straight, diag, own_low, sib_low, keep, final, terms, held, sem):
    slots, width = straight.shape[1], straight.shape[2]
    heads = width // HEAD
    first = here()[1] == 0
    late = jnp.where(first, 0.0, 1.0)
    mine = [stats[i] for i in range(3)]
    other = [heard[i] for i in range(3)]
    near = [local[i, :heads] for i in range(3)]
    far = [local[i, heads:] for i in range(3)]
    factor, delta = merge(mine, choose(first, other, near))
    factor = factor * jnp.where(first, heard[3], jnp.broadcast_to(gates[...], factor.shape))
    final[0], final[1] = merge(far, choose(first, NONE, other))
    sums = near_sum[...] + jnp.sum(final[1], axis=0, keepdims=True)
    put_terms(sums * gates[...] * (1.0 - gates[...]) * (1.0 / total), rows_x, held)
    leaving = pltpu.make_async_copy(held, terms, sem)
    leaving.start()
    for i in range(2):
        own_low[1 + i] = near_own[i]
        sib_low[1 + i] = near_sib[i]
    for h in range(heads):
        cols = slice(h * HEAD, (h + 1) * HEAD)
        row = slice(h, h + 1)
        dq, dk, dv = gradients(
            cross[2, :, cols], cross[0, :, cols], cross[3, :, cols],
            kept[0, h].astype(F32), kept[1, h].astype(F32), scale, factor[row], delta[row],
        )
        whole = (near_dq[:, cols] + late * dq).astype(BF16)
        own_low[0, :, cols] = whole[:slots]
        sib_low[0, :, cols] = whole[slots:]
        keep[0, :, cols] = dk.astype(BF16)
        keep[1, :, cols] = dv.astype(BF16)
        sent = jnp.where(first, dq, dk).astype(BF16)
        straight[0, :, cols] = sent[:slots]
        diag[0, :, cols] = sent[slots:]
        straight[1, :, cols] = dv[:slots].astype(BF16)
        diag[1, :, cols] = dv[slots:].astype(BF16)
    leaving.wait()


def cross_grad(cross, kept, stats, local, heard, gates, near_dq, near_sum, rows_x, near_own, near_sib, parts, copies, total):
    _, rows, width = cross.shape
    slots = rows // 2
    out = pltpu.VMEM((2, slots, width), BF16)
    spread = (parts, copies, 1, rows_x.shape[2] // parts)
    return pl.pallas_call(
        functools.partial(cross_grad_kernel, HEAD**-0.5, total),
        out_shape=[
            out,
            out,
            pltpu.VMEM((3, slots, width), BF16),
            pltpu.VMEM((3, slots, width), BF16),
            pltpu.VMEM((2, rows, width), BF16),
            jax.ShapeDtypeStruct((2, width // HEAD, rows), F32),
            pltpu.HBM(spread, F32),
        ],
        in_specs=[VMEM] * 11,
        out_specs=[VMEM] * 6 + [pl.BlockSpec(memory_space=pltpu.HBM)],
        scratch_shapes=[pltpu.VMEM(spread, F32), pltpu.SemaphoreType.DMA],
        compiler_params=params(),
        cost_estimate=cost(24 * slots * slots * width, 64 * slots * width),
        name="cross_grad",
    )(cross, kept, stats, local, heard, gates, near_dq, near_sum, rows_x, near_own, near_sib)


def far_grad_kernel(scale, pair, local, final, gates, keep, own_out, sib_out):
    slots, width = pair.shape[1] // 2, pair.shape[2]
    heads = width // HEAD
    early = jnp.where(here()[1] == 0, 1.0, 0.0)
    factor = final[0] * gates[...]
    mask = local_mask(here()[0], pair)
    for h in range(heads):
        at = slice(h * HEAD, (h + 1) * HEAD)
        row = slice(h, h + 1)
        top = local[0, heads + h : heads + h + 1]
        dq, dk, dv = local_gradients(pair, h, mask, scale, top, factor[row], final[1, row])
        dk = dk + early * keep[0, :, at].astype(F32)
        dv = dv + early * keep[1, :, at].astype(F32)
        for i, part in enumerate((dq, dk, dv)):
            own_out[i, :, at] = part[:slots].astype(BF16)
            sib_out[i, :, at] = part[slots:].astype(BF16)


def far_grad(pair, local, final, gates, keep):
    _, rows, width = pair.shape
    slots = rows // 2
    out = jax.ShapeDtypeStruct((3, slots, width), BF16)
    return pl.pallas_call(
        functools.partial(far_grad_kernel, HEAD**-0.5),
        out_shape=[out, out],
        in_specs=[VMEM] * 5,
        out_specs=[VMEM] * 2,
        compiler_params=params(),
        cost_estimate=cost(20 * slots * slots * width, 40 * slots * width),
        name="far_grad",
    )(pair, local, final, gates, keep)


def own_join_kernel(low, high, dq_out, dk_out, dv_out, waiting, total, sems):
    width = low.shape[2]
    core, chip = here()
    cols = pl.ds(pl.multiple_of(core * 2 * width, HEAD), 2 * width)
    stores = []
    for j, out in enumerate((dq_out, dk_out, dv_out)):
        total[j, :, :width] = low[j].astype(F32)
        total[j, :, width:] = high[j].astype(F32)
        stores.append(pltpu.make_async_copy(total.at[j], out.at[0, :, cols], sems.at[j]))
        stores[-1].start()
    waiting[0] = jnp.where(chip == 0, total[1, :, :width], total[0, :, width:]).astype(BF16)
    waiting[1] = low[2]
    for c in stores:
        c.wait()


def own_join(low, high, shape):
    out = pltpu.HBM(shape, F32)
    _, slots, width = low.shape
    hbm = pl.BlockSpec(memory_space=pltpu.HBM)
    return pl.pallas_call(
        own_join_kernel,
        out_shape=[out] * 3 + [jax.ShapeDtypeStruct((2, slots, width), BF16)],
        in_specs=[VMEM] * 2,
        out_specs=[hbm] * 3 + [VMEM],
        scratch_shapes=[pltpu.VMEM((3, slots, 2 * width), F32), pltpu.SemaphoreType.DMA((3,))],
        compiler_params=params(),
        cost_estimate=cost(0, 36 * low.size),
        name="own_join",
    )(low, high)


def sib_join_kernel(low, high, dq_in, dk_in, dv_in, dq_out, dk_out, dv_out, waiting, parts, total, in_sems, out_sems):
    width = low.shape[2]
    core, chip = here()
    loads = [
        [pltpu.make_async_copy(ref.at[j], parts.at[i, j], in_sems.at[3 * i + j]) for i, ref in enumerate((low, high))]
        for j in range(3)
    ]
    for pair in loads:
        for c in pair:
            c.start()
    cols = pl.ds(pl.multiple_of((1 - core) * 2 * width, HEAD), 2 * width)
    stores = []
    for j, out in enumerate((dq_out, dk_out, dv_out)):
        for i in range(2):
            loads[j][i].wait()
            total[j, :, i * width : (i + 1) * width] = parts[i, j].astype(F32)
        stores.append(pltpu.make_async_copy(total.at[j], out.at[0, :, cols], out_sems.at[j]))
        stores[-1].start()
    waiting[0] = jnp.where(chip == 0, total[1, :, :width], total[0, :, width:]).astype(BF16)
    waiting[1] = parts[0, 2]
    for c in stores:
        c.wait()


def sib_join(low, high, outs):
    _, slots, width = low.shape
    hbm = pl.BlockSpec(memory_space=pltpu.HBM)
    return pl.pallas_call(
        sib_join_kernel,
        out_shape=[pltpu.HBM(o.shape, F32) for o in outs] + [pltpu.VMEM((2, slots, width), BF16)],
        in_specs=[pl.BlockSpec(memory_space=pl.ANY)] * 2 + [hbm] * 3,
        out_specs=[hbm] * 3 + [VMEM],
        scratch_shapes=[
            pltpu.VMEM((2, 3, slots, width), BF16),
            pltpu.VMEM((3, slots, 2 * width), F32),
            pltpu.SemaphoreType.DMA((6,)),
            pltpu.SemaphoreType.DMA((3,)),
        ],
        input_output_aliases={2: 0, 3: 1, 4: 2},
        compiler_params=params(),
        cost_estimate=cost(0, 24 * low.size),
        name="sib_join",
    )(low, high, *in_hbm(*outs))


def add_back_kernel(own, sib, straight, diag, dq_in, dk_in, dv_in, dq_out, dk_out, dv_out, total, sems):
    width = straight.shape[2]
    core, chip = here()
    ends = ((own, straight, 2 * core * width), (sib, diag, 2 * (1 - core) * width))

    def store(i, j, out, offset):
        cols = pl.ds(pl.multiple_of(ends[i][2] + offset, HEAD), width)
        copy = pltpu.make_async_copy(total.at[i, j], out.at[0, :, cols], sems.at[2 * i + j])
        copy.start()
        return copy

    @pl.when(chip == 0)
    def _():
        copies = []
        for i, (waiting, back, _) in enumerate(ends):
            for j, out in enumerate((dk_out, dv_out)):
                total[i, j] = waiting[j].astype(F32) + back[j].astype(F32)
                copies.append(store(i, j, out, 0))
        for c in copies:
            c.wait()

    @pl.when(chip != 0)
    def _():
        copies = []
        for i, (waiting, back, _) in enumerate(ends):
            total[i, 0] = waiting[0].astype(F32) + back[0].astype(F32)
            copies.append(store(i, 0, dq_out, width))
        for c in copies:
            c.wait()


def add_back(own, sib, straight, diag, outs):
    hbm = pl.BlockSpec(memory_space=pltpu.HBM)
    return pl.pallas_call(
        add_back_kernel,
        out_shape=[pltpu.HBM(o.shape, F32) for o in outs],
        in_specs=[VMEM] * 4 + [hbm] * 3,
        out_specs=[hbm] * 3,
        scratch_shapes=[pltpu.VMEM((2, *own.shape), F32), pltpu.SemaphoreType.DMA((4,))],
        input_output_aliases={4: 0, 5: 1, 6: 2},
        compiler_params=params(),
        cost_estimate=cost(0, 24 * own.size),
        name="add_back",
    )(own, sib, straight, diag, *in_hbm(*outs))


def swap_body(route_pos, x_routed, w_router, queries, keys, values, d_gated):
    slots = queries.shape[1]
    n, ndp = lax.axis_size("ctx"), lax.axis_size("dp")

    def send(a, flip):
        return lax.ppermute(a, "ctx", [(i, i ^ flip) for i in range(n)])

    def beside(fn, *operands):
        def skip(*ops):
            return jax.tree.map(lambda o: jnp.zeros(o.shape, o.dtype), jax.eval_shape(fn, *ops))

        return lax.cond(route_pos[0, 0] >= -1, fn, skip, *operands)

    def after(value, *others):
        return lax.optimization_barrier((value, *others))[0]

    def widen(part, step, *first):
        other = lax.ppermute(part, "dp", [(i, i ^ step) for i in range(ndp)])
        return jnp.concatenate([part, after(other, *first)], axis=1)

    def exchange_phase(x_routed, w_part, theirs):
        sib, x_sib = send(theirs, 1), send(x_routed, 1)
        step = 2
        while 2 * step < ndp:
            w_part = widen(w_part, step)
            step *= 2
        return sib, x_sib, w_part

    def far_phase(own_low, sib_low, *operands):
        sib_in = [send(sib_low, 1)]
        own_high, sib_high = far_grad(*operands)
        sib_in.append(send(sib_high, 1))
        *outs, waiting = own_join(own_low, own_high, queries.shape)
        return outs, waiting, sib_in

    out_s, out_d, w_part = cross_pack(route_pos, w_router, keys, values, queries, d_gated)
    in_s, in_d = send(out_s, 2), send(out_d, 3)

    theirs = sib_pack(after(route_pos, out_s), keys, values, queries, d_gated)
    if ndp > 1:
        w_part = widen(w_part, 1, theirs)
    sib, x_sib, w_part = beside(exchange_phase, x_routed, w_part, theirs)
    local, live, near, far, rows_x = local_stats(route_pos, keys, values, queries, d_gated, sib, x_routed, x_sib)
    cross, stats, kept = cross_stats(near, far, in_s, in_d)
    if ndp > 2:
        w_part = widen(w_part, ndp // 2, stats)
    gates, message = pair_gate(live, rows_x, w_part, local, stats, ndp)

    heard = send(message, 2)
    near_dq, near_own, near_sib, near_sum = near_grad(near, local, stats, gates)
    total = float(ndp * n * slots // 2)
    back_s, back_d, own_low, sib_low, keep, final, terms = cross_grad(
        cross, kept, stats, local, heard, gates, near_dq, near_sum, rows_x, near_own, near_sib, ndp, n, total
    )

    ret_s, ret_d = send(back_s, 2), send(back_d, 3)
    shared = lax.all_to_all(terms.reshape(ndp * n, 1, -1), ("dp", "ctx"), 0, 0, tiled=True)
    outs, waiting, sib_in = beside(far_phase, own_low, sib_low, far, local, final, gates, keep)
    *outs, waiting_sib = sib_join(*sib_in, outs)
    dq, dk, dv = add_back(waiting, waiting_sib, ret_s, ret_d, outs)
    router_grad = jnp.sum(after(shared, dq), axis=(0, 1))
    return dq, dk, dv, router_grad


def body(route_pos, x_routed, w_router, queries, keys, values, d_gated):
    slots, full = queries.shape[1], queries.shape[2]
    n, ndp = lax.axis_size("ctx"), lax.axis_size("dp")
    chips = n // 2
    me, dp_me = lax.axis_index("ctx"), lax.axis_index("dp")
    core = (me % 2).astype(jnp.int32).reshape(1)
    half = full // 2
    groups = GROUPS if (half // HEAD) % GROUPS == 0 else 1
    width = half // groups

    sib_pairs = [(i, i ^ 1) for i in range(n)]

    def forward_pairs(step, flip):
        return [(i, (i + 2 * step) ^ flip) for i in range(n) if i + 2 * step < n]

    def back_pairs(step, flip):
        return [(b, a) for a, b in forward_pairs(step, flip)]

    def to_sib(a):
        return lax.ppermute(a, "ctx", sib_pairs)

    links = [(step, flip) for step in range(1, chips) for flip in (0, 1)]

    w_row = w_router.reshape(1, -1)
    w_parts = [w_row] + [
        lax.ppermute(w_row, "dp", [(i, (i + s) % ndp) for i in range(ndp)]) for s in range(1, ndp)
    ]
    live = (route_pos >= 0).astype(jnp.int32)
    lives = [live, to_sib(live)] + [lax.ppermute(live, "ctx", forward_pairs(*link)) for link in links]
    live_all = jnp.concatenate(lives, axis=0)

    kv_mine, kv_theirs = pack(core, keys, values, groups, width)
    kv_far = [
        [lax.ppermute((kv_theirs if flip else kv_mine)[g], "ctx", forward_pairs(step, flip)) for step, flip in links]
        for g in range(groups)
    ]
    q_mine, q_theirs = pack(core, queries, d_gated, groups, width)
    kv_sib = [to_sib(a) for a in kv_theirs]
    q_sib = [to_sib(a) for a in q_theirs]

    offsets = ((dp_me - jnp.arange(ndp)) % ndp).astype(jnp.int32)
    gate = router_gate(offsets, route_pos, x_routed, w_parts)
    gates = (gate, to_sib(gate))

    accs = (jnp.zeros((1, slots), F32), jnp.zeros((1, slots), F32))
    dq_own, sib_in, kv_own, back = [], [], [], []
    for g in range(groups):
        dq, sib_out, kv_local, kv_remote, accs = attention(
            core, live_all, gates, accs, q_mine[g], q_sib[g], [kv_mine[g], kv_sib[g], *kv_far[g]]
        )
        back.append([lax.ppermute(a, "ctx", back_pairs(*link)) for a, link in zip(kv_remote, links)])
        sib_in.append(to_sib(sib_out))
        dq_own.append(dq)
        kv_own.append(kv_local)

    targets = ((dp_me + jnp.arange(ndp)) % ndp).astype(jnp.int32)
    terms = router_terms(targets, gate, accs[0], to_sib(accs[1]), x_routed, ndp)
    mine = terms[0]
    for s in range(1, ndp):
        mine = mine + lax.ppermute(terms[s], "dp", [(i, (i + s) % ndp) for i in range(ndp)])
    total = mine
    for s in range(1, n):
        total = total + lax.ppermute(mine, "ctx", [(i, (i + s) % n) for i in range(n)])
    router_grad = total[0] / float(ndp * n * slots // 2)

    dq, dk, dv = combine(core, dq_own, sib_in, kv_own, back, queries.shape)
    return dq, dk, dv, router_grad


def solution(mesh):
    placed = (
        P("dp", "ctx"),
        P("dp", "ctx", None),
        P("dp"),
        P("dp", "ctx", None),
        P("dp", "ctx", None),
        P("dp", "ctx", None),
        P("dp", "ctx", None),
    )
    ndp = mesh.shape["dp"]
    paired = mesh.shape["ctx"] == 4 and ndp & (ndp - 1) == 0
    return jax.shard_map(
        swap_body if paired else body,
        mesh=mesh,
        in_specs=placed,
        out_specs=(P("dp", "ctx", None), P("dp", "ctx", None), P("dp", "ctx", None), P("dp")),
        check_vma=False,
    )
```

```python
import functools

import jax
import jax.numpy as jnp
from jax import lax
from jax.experimental import pallas as pl
from jax.experimental.pallas import tpu as pltpu
from jax.sharding import PartitionSpec as P

HEAD = 128
GROUPS = 4
NEG_FILL = -1e30
MIB = 1024 * 1024
BF16 = jnp.bfloat16
F32 = jnp.float32

VMEM = pl.BlockSpec(memory_space=pltpu.VMEM)
SMEM = pl.BlockSpec(memory_space=pltpu.SMEM)


def params(mib=16):
    return pltpu.CompilerParams(vmem_limit_bytes=mib * MIB)


def cost(flops, nbytes, exps=0):
    return pl.CostEstimate(flops=1, bytes_accessed=1, transcendentals=0)


def in_hbm(*arrays):
    return [pltpu.with_memory_space_constraint(a, pltpu.HBM) for a in arrays]


def nt(a, b):
    return lax.dot_general(a, b, (((1,), (1,)), ((), ())), preferred_element_type=F32)


def nn(a, b):
    return lax.dot_general(a, b, (((1,), (0,)), ((), ())), preferred_element_type=F32)


def tn(a, b):
    return lax.dot_general(a, b, (((0,), (0,)), ((), ())), preferred_element_type=F32)


def pack_kernel(groups, width, core_ref, first_ref, second_ref, *outs):
    half = first_ref.shape[-1] // 2
    core = core_ref[0]
    for side in range(2):
        base = (core if side == 0 else 1 - core) * half
        for g in range(groups):
            out = outs[side * groups + g]
            cols = pl.ds(pl.multiple_of(base + g * width, HEAD), width)
            out[0] = first_ref[0, :, cols].astype(BF16)
            out[1] = second_ref[0, :, cols].astype(BF16)


def pack(core, first, second, groups, width):
    slots = first.shape[1]
    out = jax.ShapeDtypeStruct((2, slots, width), BF16)
    res = pl.pallas_call(
        functools.partial(pack_kernel, groups, width),
        out_shape=[out] * (2 * groups),
        in_specs=[SMEM, VMEM, VMEM],
        out_specs=[VMEM] * (2 * groups),
        compiler_params=params(),
        cost_estimate=cost(0, 2 * first.size * 4),
        name="pack",
    )(core, first, second)
    return res[:groups], res[groups:]


def gate_kernel(parts, offset_ref, pos_ref, x_ref, *refs):
    w_refs, out_ref = refs[:parts], refs[parts]
    chunk = w_refs[0].shape[-1]
    total = jnp.zeros((8, x_ref.shape[1]), F32)
    for s in range(parts):
        cols = pl.ds(pl.multiple_of(offset_ref[s] * chunk, HEAD), chunk)
        w_rows = jnp.broadcast_to(w_refs[s][...].astype(F32), (8, chunk)).astype(BF16)
        total = total + nt(w_rows, x_ref[0, :, cols])
    gate = 1.0 / (1.0 + jnp.exp(-total[0:1]))
    out_ref[...] = jnp.where(pos_ref[...] >= 0, gate, 0.0)


def router_gate(offsets, route_pos, x_routed, w_parts):
    parts = len(w_parts)
    return pl.pallas_call(
        functools.partial(gate_kernel, parts),
        out_shape=jax.ShapeDtypeStruct(route_pos.shape, F32),
        in_specs=[SMEM] + [VMEM] * (2 + parts),
        out_specs=VMEM,
        compiler_params=params(),
        cost_estimate=cost(16 * x_routed.size, x_routed.size * 2),
        name="router_gate",
    )(offsets, route_pos, x_routed, *w_parts)


def attention_kernel(remote, scale, core_ref, live_ref, gate_own, gate_sib, acc_own, acc_sib, q_own, q_sib, *refs):
    chunks = 2 + remote
    kv = refs[:chunks]
    outs = refs[chunks:]
    dq_own, sib_out, kv_own = outs[:3]
    kv_remote = outs[3 : 3 + remote]
    sum_own, sum_sib = outs[3 + remote :]
    slots, width = q_own.shape[1], q_own.shape[2]
    core = core_ref[0]
    key = lax.broadcasted_iota(jnp.int32, (slots, slots), 0)
    query = lax.broadcasted_iota(jnp.int32, (slots, slots), 1)
    counts = [jnp.sum(live_ref[i : i + 1], axis=1, keepdims=True) for i in range(chunks)]
    lives = [key < counts[i] for i in range(chunks)]
    own_later = core == 1
    bias_rows = []
    for i in range(chunks):
        live = lives[i]
        if i == 0:
            pair = (live & (key <= query), live & jnp.logical_not(own_later))
        elif i == 1:
            pair = (live & own_later, live & (key <= query))
        else:
            pair = (live, live)
        bias_rows.append(jnp.concatenate([jnp.where(p, 0.0, NEG_FILL) for p in pair], axis=1))
    bias = jnp.concatenate(bias_rows, axis=0)
    gates = jnp.concatenate([gate_own[...], gate_sib[...]], axis=1)
    total = jnp.zeros((1, 2 * slots), F32)
    for h in range(width // HEAD):
        cols = slice(h * HEAD, (h + 1) * HEAD)
        q = jnp.concatenate([q_own[0, :, cols], q_sib[0, :, cols]], axis=0)
        dg = jnp.concatenate([q_own[1, :, cols], q_sib[1, :, cols]], axis=0)
        k = jnp.concatenate([r[0, :, cols] for r in kv], axis=0)
        v = jnp.concatenate([r[1, :, cols] for r in kv], axis=0)
        scores = nt(k, q) * scale + bias
        top = jnp.max(scores, axis=0, keepdims=True)
        e = jnp.exp(scores - top)
        inverse = 1.0 / jnp.sum(e, axis=0, keepdims=True)
        gw = nt(v, dg)
        delta = jnp.sum(e * gw, axis=0, keepdims=True) * inverse
        total = total + delta
        weights = e * (inverse * gates)
        dv = nn(weights.astype(BF16), dg)
        ds = (weights * ((gw - delta) * scale)).astype(BF16)
        dk = nn(ds, q)
        dq = tn(ds, k)
        dq_own[:, cols] = dq[:slots].astype(dq_own.dtype)
        sib_out[0, :, cols] = dq[slots:].astype(BF16)
        kv_own[0, :, cols] = dk[:slots].astype(BF16)
        kv_own[1, :, cols] = dv[:slots].astype(BF16)
        sib_out[1, :, cols] = dk[slots : 2 * slots].astype(BF16)
        sib_out[2, :, cols] = dv[slots : 2 * slots].astype(BF16)
        for i in range(remote):
            rows = slice((2 + i) * slots, (3 + i) * slots)
            kv_remote[i][0, :, cols] = dk[rows].astype(BF16)
            kv_remote[i][1, :, cols] = dv[rows].astype(BF16)
    sum_own[...] = acc_own[...] + total[:, :slots]
    sum_sib[...] = acc_sib[...] + total[:, slots:]


def attention(core, live, gates, accs, q_own, q_sib, kv):
    remote = len(kv) - 2
    _, slots, width = q_own.shape
    pair = jax.ShapeDtypeStruct((2, slots, width), BF16)
    row = jax.ShapeDtypeStruct((1, slots), F32)
    outs = [
        jax.ShapeDtypeStruct((slots, width), BF16),
        jax.ShapeDtypeStruct((3, slots, width), BF16),
        pair,
        *([pair] * remote),
        row,
        row,
    ]
    keys = (2 + remote) * slots
    res = pl.pallas_call(
        functools.partial(attention_kernel, remote, HEAD**-0.5),
        out_shape=outs,
        in_specs=[SMEM] + [VMEM] * (7 + len(kv)),
        out_specs=[VMEM] * len(outs),
        compiler_params=params(48),
        cost_estimate=cost(20 * slots * keys * width, 8 * keys * width + 20 * slots * width, 2 * slots * keys * width // HEAD),
        name="attention",
    )(core, live, *gates, *accs, q_own, q_sib, *kv)
    return res[0], res[1], res[2], res[3 : 3 + remote], (res[3 + remote], res[4 + remote])


def combine_kernel(groups, width, remote, core_ref, *refs):
    dq_own, sib, kv_own = refs[:groups], refs[groups : 2 * groups], refs[2 * groups : 3 * groups]
    back = refs[3 * groups : 3 * groups + groups * remote]
    dq_out, dk_out, dv_out = refs[3 * groups + groups * remote :]
    half = groups * width
    core = core_ref[0]
    for g in range(groups):
        own = pl.ds(pl.multiple_of(core * half + g * width, HEAD), width)
        other = pl.ds(pl.multiple_of((1 - core) * half + g * width, HEAD), width)
        dq_out[0, :, own] = dq_own[g][...].astype(F32)
        dq_out[0, :, other] = sib[g][0].astype(F32)
        for i, out in enumerate((dk_out, dv_out)):
            mine = kv_own[g][i].astype(F32)
            theirs = sib[g][1 + i].astype(F32)
            for r in range(remote):
                part = back[g * remote + r][i].astype(F32)
                if r % 2 == 0:
                    mine = mine + part
                else:
                    theirs = theirs + part
            out[0, :, own] = mine
            out[0, :, other] = theirs


def combine(core, dq_own, sib, kv_own, back, shape):
    groups = len(dq_own)
    remote = len(back[0])
    out = jax.ShapeDtypeStruct(shape, F32)
    flat = [*dq_own, *sib, *kv_own, *(b for group in back for b in group)]
    return pl.pallas_call(
        functools.partial(combine_kernel, groups, dq_own[0].shape[-1], remote),
        out_shape=[out] * 3,
        in_specs=[SMEM] + [VMEM] * len(flat),
        out_specs=[VMEM] * 3,
        compiler_params=params(48),
        cost_estimate=cost(0, 3 * out.size * 6),
        name="combine",
    )(core, *flat)


def router_kernel(parts, target_ref, gate_ref, own_ref, sib_ref, x_ref, *outs):
    gate = gate_ref[...]
    grad = (own_ref[...] + sib_ref[...]) * gate * (1.0 - gate)
    high = grad.astype(BF16)
    rest = grad - high.astype(F32)
    mid = rest.astype(BF16)
    low = (rest - mid.astype(F32)).astype(BF16)
    row = lax.broadcasted_iota(jnp.int32, (8, grad.shape[1]), 0)
    lhs = jnp.where(row == 0, high.astype(F32), jnp.where(row == 1, mid.astype(F32), jnp.where(row == 2, low.astype(F32), 0.0)))
    lhs = lhs.astype(BF16)
    chunk = outs[0].shape[-1]
    for s in range(parts):
        cols = pl.ds(pl.multiple_of(target_ref[s] * chunk, HEAD), chunk)
        outs[s][...] = jnp.sum(nn(lhs, x_ref[0, :, cols]), axis=0, keepdims=True)


def router_terms(targets, gate, own, sib, x_routed, parts):
    chunk = x_routed.shape[-1] // parts
    return pl.pallas_call(
        functools.partial(router_kernel, parts),
        out_shape=[jax.ShapeDtypeStruct((1, chunk), F32)] * parts,
        in_specs=[SMEM] + [VMEM] * 4,
        out_specs=[VMEM] * parts,
        compiler_params=params(),
        cost_estimate=cost(16 * x_routed.size, x_routed.size * 2),
        name="router_terms",
    )(targets, gate, own, sib, x_routed)


def here():
    me = lax.axis_index("ctx")
    return lax.rem(me, 2), lax.div(me, 2)


MARK = 2.0**60
MARK_LIMIT = 2.0**50


def live_rows(pos_ref, slots):
    count = jnp.sum((pos_ref[...] >= 0).astype(jnp.int32), axis=1, keepdims=True)
    return lax.broadcasted_iota(jnp.int32, (slots, HEAD), 0) < count


def mark_dead(keys, live):
    width = keys.shape[-1]
    mask = jnp.concatenate([live] * (width // HEAD), axis=1)
    return jnp.where(mask, keys.astype(F32), MARK).astype(BF16)


def cross_pack_kernel(pos_any, w_any, k_ref, v_ref, q_ref, dg_ref, straight, diag, w_out, wide, pos_ref, w_ref, sems):
    small = [pltpu.make_async_copy(pos_any, pos_ref, sems.at[4]), pltpu.make_async_copy(w_any, w_ref, sems.at[5])]
    for c in small:
        c.start()
    slots, width = straight.shape[1], straight.shape[2]
    half = k_ref.shape[-1] // 2
    core, chip = here()
    ends = ((straight, core * half), (diag, (1 - core) * half))

    def copies(first, second, targets, offset):
        out = []
        for i, (end, start) in enumerate(ends):
            cols = pl.ds(pl.multiple_of(start + offset, HEAD), width)
            out.append(pltpu.make_async_copy(first.at[0, :, cols], end.at[0], sems.at[2 * i]))
            out.append(pltpu.make_async_copy(second.at[0, :, cols], targets[i], sems.at[2 * i + 1]))
        for c in out:
            c.start()
        for c in out:
            c.wait()

    @pl.when(chip == 0)
    def _():
        copies(k_ref, v_ref, (straight.at[1], diag.at[1]), 0)
        small[0].wait()
        live = live_rows(pos_ref, slots)
        for end, _ in ends:
            end[0] = mark_dead(end[0], live)

    @pl.when(chip != 0)
    def _():
        copies(q_ref, dg_ref, (wide.at[0], wide.at[1]), width)
        small[0].wait()
        for i, (end, _) in enumerate(ends):
            end[1] = wide[i].astype(BF16)

    small[1].wait()
    w_out[...] = w_ref[...].astype(F32).reshape(w_out.shape)


def cross_pack(route_pos, w_router, keys, values, queries, d_gated):
    _, slots, full = keys.shape
    cross = pltpu.VMEM((2, slots, full // 4), BF16)
    hbm = pl.BlockSpec(memory_space=pltpu.HBM)
    return pl.pallas_call(
        cross_pack_kernel,
        out_shape=[cross, cross, jax.ShapeDtypeStruct((1, w_router.shape[0]), F32)],
        in_specs=[hbm] * 6,
        out_specs=[VMEM] * 3,
        scratch_shapes=[
            pltpu.VMEM((2, slots, full // 4), F32),
            pltpu.VMEM(route_pos.shape, jnp.int32),
            pltpu.VMEM(w_router.shape, BF16),
            pltpu.SemaphoreType.DMA((6,)),
        ],
        compiler_params=params(),
        cost_estimate=cost(0, 10 * slots * full),
        name="cross_pack",
    )(*in_hbm(route_pos, w_router, keys, values, queries, d_gated))


def sib_pack_kernel(pos_ref, k_ref, v_ref, q_ref, dg_ref, out, wide, sems):
    slots, half = out.shape[1], out.shape[2]
    cols = pl.ds(pl.multiple_of((1 - here()[0]) * half, HEAD), half)
    sources = ((k_ref, out.at[0]), (dg_ref, wide), (v_ref, out.at[1]), (q_ref, out.at[2]))
    copies = [pltpu.make_async_copy(src.at[0, :, cols], dst, sems.at[i]) for i, (src, dst) in enumerate(sources)]
    for c in copies:
        c.start()
    live = live_rows(pos_ref, slots)
    copies[0].wait()
    out[0] = mark_dead(out[0], live)
    copies[1].wait()
    out[3] = wide[...].astype(BF16)
    copies[2].wait()
    copies[3].wait()


def sib_pack(route_pos, keys, values, queries, d_gated):
    _, slots, full = keys.shape
    hbm = pl.BlockSpec(memory_space=pltpu.HBM)
    return pl.pallas_call(
        sib_pack_kernel,
        out_shape=pltpu.VMEM((4, slots, full // 2), BF16),
        in_specs=[VMEM, hbm, hbm, hbm, hbm],
        out_specs=VMEM,
        scratch_shapes=[pltpu.VMEM((slots, full // 2), F32), pltpu.SemaphoreType.DMA((4,))],
        compiler_params=params(),
        cost_estimate=cost(0, 20 * slots * full),
        name="sib_pack",
    )(route_pos, *in_hbm(keys, values, queries, d_gated))


def pair_gate_kernel(parts, live_ref, rows_x, w_ref, local, stats, out_ref, message):
    chunk = w_ref.shape[1] // parts
    slots = rows_x.shape[1]
    for i in range(2):
        total = jnp.zeros((8, slots), F32)
        for j in range(parts):
            w_rows = jnp.broadcast_to(w_ref[:, j * chunk : (j + 1) * chunk], (8, chunk)).astype(BF16)
            cols = pl.ds(pl.multiple_of((lax.axis_index("dp") ^ j) * chunk, HEAD), chunk)
            total = total + nt(w_rows, rows_x[i, :, cols])
        lanes = slice(i * slots, (i + 1) * slots)
        out_ref[:, lanes] = live_ref[:, lanes] / (1.0 + jnp.exp(-total[0:1]))
    first = here()[1] == 0
    heads = stats.shape[1]
    for i in range(3):
        message[i] = jnp.where(first, stats[i], local[i, heads:])
    message[3] = jnp.broadcast_to(out_ref[...], message.shape[1:])


def pair_gate(live, rows_x, w_full, local, stats, parts):
    _, heads, lanes = stats.shape
    return pl.pallas_call(
        functools.partial(pair_gate_kernel, parts),
        out_shape=[jax.ShapeDtypeStruct(live.shape, F32), jax.ShapeDtypeStruct((4, heads, lanes), F32)],
        in_specs=[VMEM] * 5,
        out_specs=[VMEM] * 2,
        compiler_params=params(),
        cost_estimate=cost(16 * rows_x.size, rows_x.size * 2),
        name="router_gate",
    )(live, rows_x, w_full, local, stats)


def local_mask(core, pair):
    slots = pair.shape[1] // 2
    key = lax.broadcasted_iota(jnp.int32, (slots, slots), 0)
    query = lax.broadcasted_iota(jnp.int32, (slots, slots), 1)
    causal = key <= query
    own_live = pair[0, :slots, :slots].astype(F32) < MARK_LIMIT
    sib_live = pair[0, slots:, :slots].astype(F32) < MARK_LIMIT
    own_rows = jnp.concatenate([own_live & causal, own_live & (core == 0)], axis=1)
    sib_rows = jnp.concatenate([sib_live & (core == 1), sib_live & causal], axis=1)
    return jnp.concatenate([own_rows, sib_rows], axis=0)


def kept_stats(scores, gw, kept, stats, h):
    top = jnp.max(scores, axis=0, keepdims=True)
    e = jnp.exp(scores - top).astype(BF16)
    gw = gw.astype(BF16)
    kept[0, h] = e
    kept[1, h] = gw
    e = e.astype(F32)
    stats[0, h : h + 1] = top
    stats[1, h : h + 1] = jnp.sum(e, axis=0, keepdims=True)
    stats[2, h : h + 1] = jnp.sum(e * gw.astype(F32), axis=0, keepdims=True)


def partial_stats(scores, gw, stats, h):
    top = jnp.max(scores, axis=0, keepdims=True)
    e = jnp.exp(scores - top)
    stats[0, h : h + 1] = top
    stats[1, h : h + 1] = jnp.sum(e, axis=0, keepdims=True)
    stats[2, h : h + 1] = jnp.sum(e * gw, axis=0, keepdims=True)


def local_stats_kernel(scale, pos_ref, k_ref, v_ref, q_ref, dg_ref, sib, x_ref, x_sib, stats, live, near, far, rows_x, wide, sems, x_sems):
    slots, half = sib.shape[1], sib.shape[2]
    width = half // 2
    core = here()[0]
    own, other = slice(0, slots), slice(slots, 2 * slots)
    stages = []
    for g, pair in enumerate((near, far)):
        cols = slice(g * width, (g + 1) * width)
        held = pl.ds(pl.multiple_of(core * half + g * width, HEAD), width)
        copies = [
            pltpu.make_async_copy(ref.at[0, :, held], pair.at[j, own], sems.at[8 * g + j])
            for j, ref in enumerate((k_ref, v_ref, q_ref))
        ]
        copies.append(pltpu.make_async_copy(dg_ref.at[0, :, held], wide.at[:, cols], sems.at[8 * g + 3]))
        for j in range(4):
            copies.append(pltpu.make_async_copy(sib.at[j, :, cols], pair.at[j, other], sems.at[8 * g + 4 + j]))
        for c in copies:
            c.start()
        stages.append(copies)
    x_copies = []
    depth = x_ref.shape[2] // 2
    for i, ref in enumerate((x_ref, x_sib)):
        for g in range(2):
            cols = slice(g * depth, (g + 1) * depth)
            x_copies.append(pltpu.make_async_copy(ref.at[0, :, cols], rows_x.at[i, :, cols], x_sems.at[2 * i + g]))
    for c in x_copies:
        c.start()
    rows_live = live_rows(pos_ref, slots)
    mask = None
    for g, pair in enumerate((near, far)):
        cols = slice(g * width, (g + 1) * width)
        for c in stages[g]:
            c.wait()
        pair[0, own] = mark_dead(pair[0, own], rows_live)
        pair[3, own] = wide[:, cols].astype(BF16)
        if mask is None:
            mask = local_mask(core, pair)
            marks = nt(jnp.ones((8, HEAD), BF16), pair[0, :, :HEAD])[0:1]
            live[...] = jnp.where(marks < MARK_LIMIT, 1.0, 0.0)
        for h in range(width // HEAD):
            at = slice(h * HEAD, (h + 1) * HEAD)
            scores = jnp.where(mask, nt(pair[0, :, at], pair[2, :, at]) * scale, NEG_FILL)
            partial_stats(scores, nt(pair[1, :, at], pair[3, :, at]), stats, g * width // HEAD + h)
    for c in x_copies:
        c.wait()


def local_stats(route_pos, keys, values, queries, d_gated, sib, x_routed, x_sib):
    _, slots, half = sib.shape
    heads = half // HEAD
    anywhere = pl.BlockSpec(memory_space=pl.ANY)
    return pl.pallas_call(
        functools.partial(local_stats_kernel, HEAD**-0.5),
        out_shape=[
            jax.ShapeDtypeStruct((3, heads, 2 * slots), F32),
            jax.ShapeDtypeStruct((1, 2 * slots), F32),
            pltpu.VMEM((4, 2 * slots, half // 2), BF16),
            pltpu.VMEM((4, 2 * slots, half // 2), BF16),
            pltpu.VMEM((2, slots, x_routed.shape[2]), BF16),
        ],
        in_specs=[VMEM] + [anywhere] * 7,
        out_specs=[VMEM] * 5,
        scratch_shapes=[pltpu.VMEM((slots, half), F32), pltpu.SemaphoreType.DMA((16,)), pltpu.SemaphoreType.DMA((4,))],
        compiler_params=params(),
        cost_estimate=cost(16 * slots * slots * half, 16 * slots * half, 4 * slots * slots * half // HEAD),
        name="local_stats",
    )(route_pos, *in_hbm(keys, values, queries, d_gated), sib, x_routed, x_sib)


def cross_stats_kernel(scale, near, far, straight, diag, cross, stats, kept):
    slots, width = straight.shape[1], straight.shape[2]
    chip = here()[1]
    top, bottom = slice(0, slots), slice(slots, 2 * slots)

    @pl.when(chip == 0)
    def _():
        for part in range(2):
            cross[part] = far[part]
            cross[2 + part, top] = straight[part]
            cross[2 + part, bottom] = diag[part]

    @pl.when(chip != 0)
    def _():
        for part in range(2):
            cross[part, top] = straight[part]
            cross[part, bottom] = diag[part]
            cross[2 + part] = near[2 + part]

    live = cross[0, :, :HEAD].astype(F32) < MARK_LIMIT
    mask = jnp.concatenate([live] * (2 * slots // HEAD), axis=1)
    heads = width // HEAD
    for h in range(heads):
        cols = slice(h * HEAD, (h + 1) * HEAD)
        scores = jnp.where(mask, nt(cross[0, :, cols], cross[2, :, cols]) * scale, NEG_FILL)
        kept_stats(scores, nt(cross[1, :, cols], cross[3, :, cols]), kept, stats, h)


def cross_stats(near, far, straight, diag):
    _, slots, width = straight.shape
    heads = width // HEAD
    return pl.pallas_call(
        functools.partial(cross_stats_kernel, HEAD**-0.5),
        out_shape=[
            pltpu.VMEM((4, 2 * slots, width), BF16),
            jax.ShapeDtypeStruct((3, heads, 2 * slots), F32),
            pltpu.VMEM((2, heads, 2 * slots, 2 * slots), BF16),
        ],
        in_specs=[VMEM] * 4,
        out_specs=[VMEM] * 3,
        compiler_params=params(),
        cost_estimate=cost(16 * slots * slots * width, 32 * slots * width, 4 * slots * slots * heads),
        name="cross_stats",
    )(near, far, straight, diag)


NONE = (-3e38, 0.0, 0.0)


def merge(first, second):
    top = jnp.maximum(first[0], second[0])
    a, b = jnp.exp(first[0] - top), jnp.exp(second[0] - top)
    inverse = 1.0 / (first[1] * a + second[1] * b)
    return a * inverse, (first[2] * a + second[2] * b) * inverse


def choose(flag, yes, no):
    return [jnp.where(flag, y, n) for y, n in zip(yes, no)]


def gradients(q, k, dg, e, gw, scale, factor, delta):
    weights = e * factor
    ds = (weights * ((gw - delta) * scale)).astype(BF16)
    return tn(ds, k), nn(ds, q), nn(weights.astype(BF16), dg)


def local_gradients(pair, h, mask, scale, top, factor, delta):
    cols = slice(h * HEAD, (h + 1) * HEAD)
    k, v, q, dg = [pair[i, :, cols] for i in range(4)]
    e = jnp.exp(jnp.where(mask, nt(k, q) * scale, NEG_FILL) - top)
    return gradients(q, k, dg, e, nt(v, dg), scale, factor, delta)


def near_grad_kernel(scale, pair, local, stats, gates, dq_out, own_out, sib_out, sum_out):
    slots, width = own_out.shape[1], own_out.shape[2]
    heads = width // HEAD
    first = here()[1] == 0
    near = [local[i, :heads] for i in range(3)]
    factor, delta = merge(near, choose(first, NONE, [stats[i] for i in range(3)]))
    factor = factor * gates[...]
    sum_out[...] = jnp.sum(delta, axis=0, keepdims=True)
    mask = local_mask(here()[0], pair)
    for h in range(heads):
        cols = slice(h * HEAD, (h + 1) * HEAD)
        row = slice(h, h + 1)
        dq, dk, dv = local_gradients(pair, h, mask, scale, near[0][row], factor[row], delta[row])
        dq_out[:, cols] = dq
        for i, part in enumerate((dk, dv)):
            own_out[1 + i, :, cols] = part[:slots].astype(BF16)
            sib_out[1 + i, :, cols] = part[slots:].astype(BF16)


def near_grad(pair, local, stats, gates):
    _, rows, width = pair.shape
    slots = rows // 2
    out = pltpu.VMEM((3, slots, width), BF16)
    return pl.pallas_call(
        functools.partial(near_grad_kernel, HEAD**-0.5),
        out_shape=[pltpu.VMEM((2 * slots, width), F32), out, out, jax.ShapeDtypeStruct(gates.shape, F32)],
        in_specs=[VMEM] * 4,
        out_specs=[VMEM] * 4,
        compiler_params=params(),
        cost_estimate=cost(20 * slots * slots * width, 40 * slots * width),
        name="near_grad",
    )(pair, local, stats, gates)


def put_terms(grad, rows_x, out_ref):
    high = grad.astype(BF16)
    rest = grad - high.astype(F32)
    mid = rest.astype(BF16)
    low = (rest - mid.astype(F32)).astype(BF16)
    slots = rows_x.shape[1]
    row = lax.broadcasted_iota(jnp.int32, (8, grad.shape[1]), 0)
    lhs = jnp.where(row == 0, high.astype(F32), jnp.where(row == 1, mid.astype(F32), jnp.where(row == 2, low.astype(F32), 0.0)))
    lhs = lhs.astype(BF16)
    term = jnp.sum(nn(lhs[:, :slots], rows_x[0]) + nn(lhs[:, slots:], rows_x[1]), axis=0, keepdims=True)
    parts, copies, _, chunk = out_ref.shape
    for j in range(parts):
        for i in range(copies):
            out_ref[j, i] = term[:, j * chunk : (j + 1) * chunk]


def cross_grad_kernel(scale, total, cross, kept, stats, local, heard, gates, near_dq, near_sum, rows_x, near_own, near_sib, straight, diag, own_low, sib_low, keep, final, terms, held, sem):
    slots, width = straight.shape[1], straight.shape[2]
    heads = width // HEAD
    first = here()[1] == 0
    late = jnp.where(first, 0.0, 1.0)
    mine = [stats[i] for i in range(3)]
    other = [heard[i] for i in range(3)]
    near = [local[i, :heads] for i in range(3)]
    far = [local[i, heads:] for i in range(3)]
    factor, delta = merge(mine, choose(first, other, near))
    factor = factor * jnp.where(first, heard[3], jnp.broadcast_to(gates[...], factor.shape))
    final[0], final[1] = merge(far, choose(first, NONE, other))
    sums = near_sum[...] + jnp.sum(final[1], axis=0, keepdims=True)
    put_terms(sums * gates[...] * (1.0 - gates[...]) * (1.0 / total), rows_x, held)
    leaving = pltpu.make_async_copy(held, terms, sem)
    leaving.start()
    for h in range(heads):
        cols = slice(h * HEAD, (h + 1) * HEAD)
        row = slice(h, h + 1)
        dq, dk, dv = gradients(
            cross[2, :, cols], cross[0, :, cols], cross[3, :, cols],
            kept[0, h].astype(F32), kept[1, h].astype(F32), scale, factor[row], delta[row],
        )
        whole = (near_dq[:, cols] + late * dq).astype(BF16)
        own_low[0, :, cols] = whole[:slots]
        sib_low[0, :, cols] = whole[slots:]
        keep[0, :, cols] = dk.astype(BF16)
        keep[1, :, cols] = dv.astype(BF16)
        sent = jnp.where(first, dq, dk).astype(BF16)
        straight[0, :, cols] = sent[:slots]
        diag[0, :, cols] = sent[slots:]
        straight[1, :, cols] = dv[:slots].astype(BF16)
        diag[1, :, cols] = dv[slots:].astype(BF16)
    leaving.wait()


def cross_grad(cross, kept, stats, local, heard, gates, near_dq, near_sum, rows_x, near_own, near_sib, parts, copies, total):
    _, rows, width = cross.shape
    slots = rows // 2
    out = pltpu.VMEM((2, slots, width), BF16)
    spread = (parts, copies, 1, rows_x.shape[2] // parts)
    return pl.pallas_call(
        functools.partial(cross_grad_kernel, HEAD**-0.5, total),
        out_shape=[
            out,
            out,
            pltpu.VMEM((3, slots, width), BF16),
            pltpu.VMEM((3, slots, width), BF16),
            pltpu.VMEM((2, rows, width), BF16),
            jax.ShapeDtypeStruct((2, width // HEAD, rows), F32),
            pltpu.HBM(spread, F32),
        ],
        in_specs=[VMEM] * 11,
        out_specs=[VMEM] * 6 + [pl.BlockSpec(memory_space=pltpu.HBM)],
        scratch_shapes=[pltpu.VMEM(spread, F32), pltpu.SemaphoreType.DMA],
        input_output_aliases={9: 2, 10: 3},
        compiler_params=params(),
        cost_estimate=cost(24 * slots * slots * width, 64 * slots * width),
        name="cross_grad",
    )(cross, kept, stats, local, heard, gates, near_dq, near_sum, rows_x, near_own, near_sib)


def far_grad_kernel(scale, pair, local, final, gates, keep, own_out, sib_out):
    slots, width = pair.shape[1] // 2, pair.shape[2]
    heads = width // HEAD
    early = jnp.where(here()[1] == 0, 1.0, 0.0)
    factor = final[0] * gates[...]
    mask = local_mask(here()[0], pair)
    for h in range(heads):
        at = slice(h * HEAD, (h + 1) * HEAD)
        row = slice(h, h + 1)
        top = local[0, heads + h : heads + h + 1]
        dq, dk, dv = local_gradients(pair, h, mask, scale, top, factor[row], final[1, row])
        dk = dk + early * keep[0, :, at].astype(F32)
        dv = dv + early * keep[1, :, at].astype(F32)
        for i, part in enumerate((dq, dk, dv)):
            own_out[i, :, at] = part[:slots].astype(BF16)
            sib_out[i, :, at] = part[slots:].astype(BF16)


def far_grad(pair, local, final, gates, keep):
    _, rows, width = pair.shape
    slots = rows // 2
    out = jax.ShapeDtypeStruct((3, slots, width), BF16)
    return pl.pallas_call(
        functools.partial(far_grad_kernel, HEAD**-0.5),
        out_shape=[out, out],
        in_specs=[VMEM] * 5,
        out_specs=[VMEM] * 2,
        compiler_params=params(),
        cost_estimate=cost(20 * slots * slots * width, 40 * slots * width),
        name="far_grad",
    )(pair, local, final, gates, keep)


def own_join_kernel(low, high, dq_out, dk_out, dv_out, waiting, total, sems):
    width = low.shape[2]
    core, chip = here()
    cols = pl.ds(pl.multiple_of(core * 2 * width, HEAD), 2 * width)
    stores = []
    for j, out in enumerate((dq_out, dk_out, dv_out)):
        total[j, :, :width] = low[j].astype(F32)
        total[j, :, width:] = high[j].astype(F32)
        stores.append(pltpu.make_async_copy(total.at[j], out.at[0, :, cols], sems.at[j]))
        stores[-1].start()
    waiting[0] = jnp.where(chip == 0, total[1, :, :width], total[0, :, width:]).astype(BF16)
    waiting[1] = low[2]
    for c in stores:
        c.wait()


def own_join(low, high, shape):
    out = pltpu.HBM(shape, F32)
    _, slots, width = low.shape
    hbm = pl.BlockSpec(memory_space=pltpu.HBM)
    return pl.pallas_call(
        own_join_kernel,
        out_shape=[out] * 3 + [jax.ShapeDtypeStruct((2, slots, width), BF16)],
        in_specs=[VMEM] * 2,
        out_specs=[hbm] * 3 + [VMEM],
        scratch_shapes=[pltpu.VMEM((3, slots, 2 * width), F32), pltpu.SemaphoreType.DMA((3,))],
        compiler_params=params(),
        cost_estimate=cost(0, 36 * low.size),
        name="own_join",
    )(low, high)


def sib_join_kernel(low, high, dq_in, dk_in, dv_in, dq_out, dk_out, dv_out, waiting, parts, total, in_sems, out_sems):
    width = low.shape[2]
    core, chip = here()
    loads = [
        [pltpu.make_async_copy(ref.at[j], parts.at[i, j], in_sems.at[3 * i + j]) for i, ref in enumerate((low, high))]
        for j in range(3)
    ]
    for pair in loads:
        for c in pair:
            c.start()
    cols = pl.ds(pl.multiple_of((1 - core) * 2 * width, HEAD), 2 * width)
    stores = []
    for j, out in enumerate((dq_out, dk_out, dv_out)):
        for i in range(2):
            loads[j][i].wait()
            total[j, :, i * width : (i + 1) * width] = parts[i, j].astype(F32)
        stores.append(pltpu.make_async_copy(total.at[j], out.at[0, :, cols], out_sems.at[j]))
        stores[-1].start()
    waiting[0] = jnp.where(chip == 0, total[1, :, :width], total[0, :, width:]).astype(BF16)
    waiting[1] = parts[0, 2]
    for c in stores:
        c.wait()


def sib_join(low, high, outs):
    _, slots, width = low.shape
    hbm = pl.BlockSpec(memory_space=pltpu.HBM)
    return pl.pallas_call(
        sib_join_kernel,
        out_shape=[pltpu.HBM(o.shape, F32) for o in outs] + [pltpu.VMEM((2, slots, width), BF16)],
        in_specs=[pl.BlockSpec(memory_space=pl.ANY)] * 2 + [hbm] * 3,
        out_specs=[hbm] * 3 + [VMEM],
        scratch_shapes=[
            pltpu.VMEM((2, 3, slots, width), BF16),
            pltpu.VMEM((3, slots, 2 * width), F32),
            pltpu.SemaphoreType.DMA((6,)),
            pltpu.SemaphoreType.DMA((3,)),
        ],
        input_output_aliases={2: 0, 3: 1, 4: 2},
        compiler_params=params(),
        cost_estimate=cost(0, 24 * low.size),
        name="sib_join",
    )(low, high, *in_hbm(*outs))


def add_back_kernel(own, sib, straight, diag, dq_in, dk_in, dv_in, dq_out, dk_out, dv_out, total, sems):
    width = straight.shape[2]
    core, chip = here()
    ends = ((own, straight, 2 * core * width), (sib, diag, 2 * (1 - core) * width))

    def store(i, j, out, offset):
        cols = pl.ds(pl.multiple_of(ends[i][2] + offset, HEAD), width)
        copy = pltpu.make_async_copy(total.at[i, j], out.at[0, :, cols], sems.at[2 * i + j])
        copy.start()
        return copy

    @pl.when(chip == 0)
    def _():
        copies = []
        for i, (waiting, back, _) in enumerate(ends):
            for j, out in enumerate((dk_out, dv_out)):
                total[i, j] = waiting[j].astype(F32) + back[j].astype(F32)
                copies.append(store(i, j, out, 0))
        for c in copies:
            c.wait()

    @pl.when(chip != 0)
    def _():
        copies = []
        for i, (waiting, back, _) in enumerate(ends):
            total[i, 0] = waiting[0].astype(F32) + back[0].astype(F32)
            copies.append(store(i, 0, dq_out, width))
        for c in copies:
            c.wait()


def add_back(own, sib, straight, diag, outs):
    hbm = pl.BlockSpec(memory_space=pltpu.HBM)
    return pl.pallas_call(
        add_back_kernel,
        out_shape=[pltpu.HBM(o.shape, F32) for o in outs],
        in_specs=[VMEM] * 4 + [hbm] * 3,
        out_specs=[hbm] * 3,
        scratch_shapes=[pltpu.VMEM((2, *own.shape), F32), pltpu.SemaphoreType.DMA((4,))],
        input_output_aliases={4: 0, 5: 1, 6: 2},
        compiler_params=params(),
        cost_estimate=cost(0, 24 * own.size),
        name="add_back",
    )(own, sib, straight, diag, *in_hbm(*outs))


def swap_body(route_pos, x_routed, w_router, queries, keys, values, d_gated):
    slots = queries.shape[1]
    n, ndp = lax.axis_size("ctx"), lax.axis_size("dp")

    def send(a, flip):
        return lax.ppermute(a, "ctx", [(i, i ^ flip) for i in range(n)])

    def beside(fn, *operands):
        def skip(*ops):
            return jax.tree.map(lambda o: jnp.zeros(o.shape, o.dtype), jax.eval_shape(fn, *ops))

        return lax.cond(route_pos[0, 0] >= -1, fn, skip, *operands)

    def after(value, *others):
        return lax.optimization_barrier((value, *others))[0]

    def widen(part, step, *first):
        other = lax.ppermute(part, "dp", [(i, i ^ step) for i in range(ndp)])
        return jnp.concatenate([part, after(other, *first)], axis=1)

    def exchange_phase(x_routed, w_part, theirs):
        sib, x_sib = send(theirs, 1), send(x_routed, 1)
        step = 2
        while 2 * step < ndp:
            w_part = widen(w_part, step)
            step *= 2
        return sib, x_sib, w_part

    def far_phase(own_low, sib_low, *operands):
        sib_in = [send(sib_low, 1)]
        own_high, sib_high = far_grad(*operands)
        sib_in.append(send(sib_high, 1))
        *outs, waiting = own_join(own_low, own_high, queries.shape)
        return outs, waiting, sib_in

    out_s, out_d, w_part = cross_pack(route_pos, w_router, keys, values, queries, d_gated)
    in_s, in_d = send(out_s, 2), send(out_d, 3)

    theirs = sib_pack(after(route_pos, out_s), keys, values, queries, d_gated)
    if ndp > 1:
        w_part = widen(w_part, 1, theirs)
    sib, x_sib, w_part = beside(exchange_phase, x_routed, w_part, theirs)
    local, live, near, far, rows_x = local_stats(route_pos, keys, values, queries, d_gated, sib, x_routed, x_sib)
    cross, stats, kept = cross_stats(near, far, in_s, in_d)
    if ndp > 2:
        w_part = widen(w_part, ndp // 2, stats)
    gates, message = pair_gate(live, rows_x, w_part, local, stats, ndp)

    heard = send(message, 2)
    near_dq, near_own, near_sib, near_sum = near_grad(near, local, stats, gates)
    total = float(ndp * n * slots // 2)
    back_s, back_d, own_low, sib_low, keep, final, terms = cross_grad(
        cross, kept, stats, local, heard, gates, near_dq, near_sum, rows_x, near_own, near_sib, ndp, n, total
    )

    ret_s, ret_d = send(back_s, 2), send(back_d, 3)
    shared = lax.all_to_all(terms.reshape(ndp * n, 1, -1), ("dp", "ctx"), 0, 0, tiled=True)
    outs, waiting, sib_in = beside(far_phase, own_low, sib_low, far, local, final, gates, keep)
    *outs, waiting_sib = sib_join(*sib_in, outs)
    dq, dk, dv = add_back(waiting, waiting_sib, ret_s, ret_d, outs)
    router_grad = jnp.sum(after(shared, dq), axis=(0, 1))
    return dq, dk, dv, router_grad


def body(route_pos, x_routed, w_router, queries, keys, values, d_gated):
    slots, full = queries.shape[1], queries.shape[2]
    n, ndp = lax.axis_size("ctx"), lax.axis_size("dp")
    chips = n // 2
    me, dp_me = lax.axis_index("ctx"), lax.axis_index("dp")
    core = (me % 2).astype(jnp.int32).reshape(1)
    half = full // 2
    groups = GROUPS if (half // HEAD) % GROUPS == 0 else 1
    width = half // groups

    sib_pairs = [(i, i ^ 1) for i in range(n)]

    def forward_pairs(step, flip):
        return [(i, (i + 2 * step) ^ flip) for i in range(n) if i + 2 * step < n]

    def back_pairs(step, flip):
        return [(b, a) for a, b in forward_pairs(step, flip)]

    def to_sib(a):
        return lax.ppermute(a, "ctx", sib_pairs)

    links = [(step, flip) for step in range(1, chips) for flip in (0, 1)]

    w_row = w_router.reshape(1, -1)
    w_parts = [w_row] + [
        lax.ppermute(w_row, "dp", [(i, (i + s) % ndp) for i in range(ndp)]) for s in range(1, ndp)
    ]
    live = (route_pos >= 0).astype(jnp.int32)
    lives = [live, to_sib(live)] + [lax.ppermute(live, "ctx", forward_pairs(*link)) for link in links]
    live_all = jnp.concatenate(lives, axis=0)

    kv_mine, kv_theirs = pack(core, keys, values, groups, width)
    kv_far = [
        [lax.ppermute((kv_theirs if flip else kv_mine)[g], "ctx", forward_pairs(step, flip)) for step, flip in links]
        for g in range(groups)
    ]
    q_mine, q_theirs = pack(core, queries, d_gated, groups, width)
    kv_sib = [to_sib(a) for a in kv_theirs]
    q_sib = [to_sib(a) for a in q_theirs]

    offsets = ((dp_me - jnp.arange(ndp)) % ndp).astype(jnp.int32)
    gate = router_gate(offsets, route_pos, x_routed, w_parts)
    gates = (gate, to_sib(gate))

    accs = (jnp.zeros((1, slots), F32), jnp.zeros((1, slots), F32))
    dq_own, sib_in, kv_own, back = [], [], [], []
    for g in range(groups):
        dq, sib_out, kv_local, kv_remote, accs = attention(
            core, live_all, gates, accs, q_mine[g], q_sib[g], [kv_mine[g], kv_sib[g], *kv_far[g]]
        )
        back.append([lax.ppermute(a, "ctx", back_pairs(*link)) for a, link in zip(kv_remote, links)])
        sib_in.append(to_sib(sib_out))
        dq_own.append(dq)
        kv_own.append(kv_local)

    targets = ((dp_me + jnp.arange(ndp)) % ndp).astype(jnp.int32)
    terms = router_terms(targets, gate, accs[0], to_sib(accs[1]), x_routed, ndp)
    mine = terms[0]
    for s in range(1, ndp):
        mine = mine + lax.ppermute(terms[s], "dp", [(i, (i + s) % ndp) for i in range(ndp)])
    total = mine
    for s in range(1, n):
        total = total + lax.ppermute(mine, "ctx", [(i, (i + s) % n) for i in range(n)])
    router_grad = total[0] / float(ndp * n * slots // 2)

    dq, dk, dv = combine(core, dq_own, sib_in, kv_own, back, queries.shape)
    return dq, dk, dv, router_grad


def solution(mesh):
    placed = (
        P("dp", "ctx"),
        P("dp", "ctx", None),
        P("dp"),
        P("dp", "ctx", None),
        P("dp", "ctx", None),
        P("dp", "ctx", None),
        P("dp", "ctx", None),
    )
    ndp = mesh.shape["dp"]
    paired = mesh.shape["ctx"] == 4 and ndp & (ndp - 1) == 0
    return jax.shard_map(
        swap_body if paired else body,
        mesh=mesh,
        in_specs=placed,
        out_specs=(P("dp", "ctx", None), P("dp", "ctx", None), P("dp", "ctx", None), P("dp")),
        check_vma=False,
    )
```

```python
import functools

import jax
import jax.numpy as jnp
from jax import lax
from jax.experimental import pallas as pl
from jax.experimental.pallas import tpu as pltpu
from jax.sharding import PartitionSpec as P

HEAD = 128
GROUPS = 4
NEG_FILL = -1e30
MIB = 1024 * 1024
BF16 = jnp.bfloat16
F32 = jnp.float32

VMEM = pl.BlockSpec(memory_space=pltpu.VMEM)
SMEM = pl.BlockSpec(memory_space=pltpu.SMEM)


def params(mib=16):
    return pltpu.CompilerParams(vmem_limit_bytes=mib * MIB)


def cost(flops, nbytes, exps=0):
    return pl.CostEstimate(flops=1, bytes_accessed=1, transcendentals=0)


def in_hbm(*arrays):
    return [pltpu.with_memory_space_constraint(a, pltpu.HBM) for a in arrays]


def nt(a, b):
    return lax.dot_general(a, b, (((1,), (1,)), ((), ())), preferred_element_type=F32)


def nn(a, b):
    return lax.dot_general(a, b, (((1,), (0,)), ((), ())), preferred_element_type=F32)


def tn(a, b):
    return lax.dot_general(a, b, (((0,), (0,)), ((), ())), preferred_element_type=F32)


def pack_kernel(groups, width, core_ref, first_ref, second_ref, *outs):
    half = first_ref.shape[-1] // 2
    core = core_ref[0]
    for side in range(2):
        base = (core if side == 0 else 1 - core) * half
        for g in range(groups):
            out = outs[side * groups + g]
            cols = pl.ds(pl.multiple_of(base + g * width, HEAD), width)
            out[0] = first_ref[0, :, cols].astype(BF16)
            out[1] = second_ref[0, :, cols].astype(BF16)


def pack(core, first, second, groups, width):
    slots = first.shape[1]
    out = jax.ShapeDtypeStruct((2, slots, width), BF16)
    res = pl.pallas_call(
        functools.partial(pack_kernel, groups, width),
        out_shape=[out] * (2 * groups),
        in_specs=[SMEM, VMEM, VMEM],
        out_specs=[VMEM] * (2 * groups),
        compiler_params=params(),
        cost_estimate=cost(0, 2 * first.size * 4),
        name="pack",
    )(core, first, second)
    return res[:groups], res[groups:]


def gate_kernel(parts, offset_ref, pos_ref, x_ref, *refs):
    w_refs, out_ref = refs[:parts], refs[parts]
    chunk = w_refs[0].shape[-1]
    total = jnp.zeros((8, x_ref.shape[1]), F32)
    for s in range(parts):
        cols = pl.ds(pl.multiple_of(offset_ref[s] * chunk, HEAD), chunk)
        w_rows = jnp.broadcast_to(w_refs[s][...].astype(F32), (8, chunk)).astype(BF16)
        total = total + nt(w_rows, x_ref[0, :, cols])
    gate = 1.0 / (1.0 + jnp.exp(-total[0:1]))
    out_ref[...] = jnp.where(pos_ref[...] >= 0, gate, 0.0)


def router_gate(offsets, route_pos, x_routed, w_parts):
    parts = len(w_parts)
    return pl.pallas_call(
        functools.partial(gate_kernel, parts),
        out_shape=jax.ShapeDtypeStruct(route_pos.shape, F32),
        in_specs=[SMEM] + [VMEM] * (2 + parts),
        out_specs=VMEM,
        compiler_params=params(),
        cost_estimate=cost(16 * x_routed.size, x_routed.size * 2),
        name="router_gate",
    )(offsets, route_pos, x_routed, *w_parts)


def attention_kernel(remote, scale, core_ref, live_ref, gate_own, gate_sib, acc_own, acc_sib, q_own, q_sib, *refs):
    chunks = 2 + remote
    kv = refs[:chunks]
    outs = refs[chunks:]
    dq_own, sib_out, kv_own = outs[:3]
    kv_remote = outs[3 : 3 + remote]
    sum_own, sum_sib = outs[3 + remote :]
    slots, width = q_own.shape[1], q_own.shape[2]
    core = core_ref[0]
    key = lax.broadcasted_iota(jnp.int32, (slots, slots), 0)
    query = lax.broadcasted_iota(jnp.int32, (slots, slots), 1)
    counts = [jnp.sum(live_ref[i : i + 1], axis=1, keepdims=True) for i in range(chunks)]
    lives = [key < counts[i] for i in range(chunks)]
    own_later = core == 1
    bias_rows = []
    for i in range(chunks):
        live = lives[i]
        if i == 0:
            pair = (live & (key <= query), live & jnp.logical_not(own_later))
        elif i == 1:
            pair = (live & own_later, live & (key <= query))
        else:
            pair = (live, live)
        bias_rows.append(jnp.concatenate([jnp.where(p, 0.0, NEG_FILL) for p in pair], axis=1))
    bias = jnp.concatenate(bias_rows, axis=0)
    gates = jnp.concatenate([gate_own[...], gate_sib[...]], axis=1)
    total = jnp.zeros((1, 2 * slots), F32)
    for h in range(width // HEAD):
        cols = slice(h * HEAD, (h + 1) * HEAD)
        q = jnp.concatenate([q_own[0, :, cols], q_sib[0, :, cols]], axis=0)
        dg = jnp.concatenate([q_own[1, :, cols], q_sib[1, :, cols]], axis=0)
        k = jnp.concatenate([r[0, :, cols] for r in kv], axis=0)
        v = jnp.concatenate([r[1, :, cols] for r in kv], axis=0)
        scores = nt(k, q) * scale + bias
        top = jnp.max(scores, axis=0, keepdims=True)
        e = jnp.exp(scores - top)
        inverse = 1.0 / jnp.sum(e, axis=0, keepdims=True)
        gw = nt(v, dg)
        delta = jnp.sum(e * gw, axis=0, keepdims=True) * inverse
        total = total + delta
        weights = e * (inverse * gates)
        dv = nn(weights.astype(BF16), dg)
        ds = (weights * ((gw - delta) * scale)).astype(BF16)
        dk = nn(ds, q)
        dq = tn(ds, k)
        dq_own[:, cols] = dq[:slots].astype(dq_own.dtype)
        sib_out[0, :, cols] = dq[slots:].astype(BF16)
        kv_own[0, :, cols] = dk[:slots].astype(BF16)
        kv_own[1, :, cols] = dv[:slots].astype(BF16)
        sib_out[1, :, cols] = dk[slots : 2 * slots].astype(BF16)
        sib_out[2, :, cols] = dv[slots : 2 * slots].astype(BF16)
        for i in range(remote):
            rows = slice((2 + i) * slots, (3 + i) * slots)
            kv_remote[i][0, :, cols] = dk[rows].astype(BF16)
            kv_remote[i][1, :, cols] = dv[rows].astype(BF16)
    sum_own[...] = acc_own[...] + total[:, :slots]
    sum_sib[...] = acc_sib[...] + total[:, slots:]


def attention(core, live, gates, accs, q_own, q_sib, kv):
    remote = len(kv) - 2
    _, slots, width = q_own.shape
    pair = jax.ShapeDtypeStruct((2, slots, width), BF16)
    row = jax.ShapeDtypeStruct((1, slots), F32)
    outs = [
        jax.ShapeDtypeStruct((slots, width), BF16),
        jax.ShapeDtypeStruct((3, slots, width), BF16),
        pair,
        *([pair] * remote),
        row,
        row,
    ]
    keys = (2 + remote) * slots
    res = pl.pallas_call(
        functools.partial(attention_kernel, remote, HEAD**-0.5),
        out_shape=outs,
        in_specs=[SMEM] + [VMEM] * (7 + len(kv)),
        out_specs=[VMEM] * len(outs),
        compiler_params=params(48),
        cost_estimate=cost(20 * slots * keys * width, 8 * keys * width + 20 * slots * width, 2 * slots * keys * width // HEAD),
        name="attention",
    )(core, live, *gates, *accs, q_own, q_sib, *kv)
    return res[0], res[1], res[2], res[3 : 3 + remote], (res[3 + remote], res[4 + remote])


def combine_kernel(groups, width, remote, core_ref, *refs):
    dq_own, sib, kv_own = refs[:groups], refs[groups : 2 * groups], refs[2 * groups : 3 * groups]
    back = refs[3 * groups : 3 * groups + groups * remote]
    dq_out, dk_out, dv_out = refs[3 * groups + groups * remote :]
    half = groups * width
    core = core_ref[0]
    for g in range(groups):
        own = pl.ds(pl.multiple_of(core * half + g * width, HEAD), width)
        other = pl.ds(pl.multiple_of((1 - core) * half + g * width, HEAD), width)
        dq_out[0, :, own] = dq_own[g][...].astype(F32)
        dq_out[0, :, other] = sib[g][0].astype(F32)
        for i, out in enumerate((dk_out, dv_out)):
            mine = kv_own[g][i].astype(F32)
            theirs = sib[g][1 + i].astype(F32)
            for r in range(remote):
                part = back[g * remote + r][i].astype(F32)
                if r % 2 == 0:
                    mine = mine + part
                else:
                    theirs = theirs + part
            out[0, :, own] = mine
            out[0, :, other] = theirs


def combine(core, dq_own, sib, kv_own, back, shape):
    groups = len(dq_own)
    remote = len(back[0])
    out = jax.ShapeDtypeStruct(shape, F32)
    flat = [*dq_own, *sib, *kv_own, *(b for group in back for b in group)]
    return pl.pallas_call(
        functools.partial(combine_kernel, groups, dq_own[0].shape[-1], remote),
        out_shape=[out] * 3,
        in_specs=[SMEM] + [VMEM] * len(flat),
        out_specs=[VMEM] * 3,
        compiler_params=params(48),
        cost_estimate=cost(0, 3 * out.size * 6),
        name="combine",
    )(core, *flat)


def router_kernel(parts, target_ref, gate_ref, own_ref, sib_ref, x_ref, *outs):
    gate = gate_ref[...]
    grad = (own_ref[...] + sib_ref[...]) * gate * (1.0 - gate)
    high = grad.astype(BF16)
    rest = grad - high.astype(F32)
    mid = rest.astype(BF16)
    low = (rest - mid.astype(F32)).astype(BF16)
    row = lax.broadcasted_iota(jnp.int32, (8, grad.shape[1]), 0)
    lhs = jnp.where(row == 0, high.astype(F32), jnp.where(row == 1, mid.astype(F32), jnp.where(row == 2, low.astype(F32), 0.0)))
    lhs = lhs.astype(BF16)
    chunk = outs[0].shape[-1]
    for s in range(parts):
        cols = pl.ds(pl.multiple_of(target_ref[s] * chunk, HEAD), chunk)
        outs[s][...] = jnp.sum(nn(lhs, x_ref[0, :, cols]), axis=0, keepdims=True)


def router_terms(targets, gate, own, sib, x_routed, parts):
    chunk = x_routed.shape[-1] // parts
    return pl.pallas_call(
        functools.partial(router_kernel, parts),
        out_shape=[jax.ShapeDtypeStruct((1, chunk), F32)] * parts,
        in_specs=[SMEM] + [VMEM] * 4,
        out_specs=[VMEM] * parts,
        compiler_params=params(),
        cost_estimate=cost(16 * x_routed.size, x_routed.size * 2),
        name="router_terms",
    )(targets, gate, own, sib, x_routed)


def here():
    me = lax.axis_index("ctx")
    return lax.rem(me, 2), lax.div(me, 2)


MARK = 2.0**60
MARK_LIMIT = 2.0**50


def live_rows(pos_ref, slots):
    count = jnp.sum((pos_ref[...] >= 0).astype(jnp.int32), axis=1, keepdims=True)
    return lax.broadcasted_iota(jnp.int32, (slots, HEAD), 0) < count


def mark_dead(keys, live):
    width = keys.shape[-1]
    mask = jnp.concatenate([live] * (width // HEAD), axis=1)
    return jnp.where(mask, keys.astype(F32), MARK).astype(BF16)


def cross_pack_kernel(pos_any, w_any, k_ref, v_ref, q_ref, dg_ref, straight, diag, w_out, wide, pos_ref, w_ref, sems):
    small = [pltpu.make_async_copy(pos_any, pos_ref, sems.at[4]), pltpu.make_async_copy(w_any, w_ref, sems.at[5])]
    for c in small:
        c.start()
    slots, width = straight.shape[1], straight.shape[2]
    half = k_ref.shape[-1] // 2
    core, chip = here()
    ends = ((straight, core * half), (diag, (1 - core) * half))

    def copies(first, second, targets, offset):
        out = []
        for i, (end, start) in enumerate(ends):
            cols = pl.ds(pl.multiple_of(start + offset, HEAD), width)
            out.append(pltpu.make_async_copy(first.at[0, :, cols], end.at[0], sems.at[2 * i]))
            out.append(pltpu.make_async_copy(second.at[0, :, cols], targets[i], sems.at[2 * i + 1]))
        for c in out:
            c.start()
        for c in out:
            c.wait()

    @pl.when(chip == 0)
    def _():
        copies(k_ref, v_ref, (straight.at[1], diag.at[1]), 0)
        small[0].wait()
        live = live_rows(pos_ref, slots)
        for end, _ in ends:
            end[0] = mark_dead(end[0], live)

    @pl.when(chip != 0)
    def _():
        copies(q_ref, dg_ref, (wide.at[0], wide.at[1]), width)
        small[0].wait()
        for i, (end, _) in enumerate(ends):
            end[1] = wide[i].astype(BF16)

    small[1].wait()
    w_out[...] = w_ref[...].astype(F32).reshape(w_out.shape)


def cross_pack(route_pos, w_router, keys, values, queries, d_gated):
    _, slots, full = keys.shape
    cross = pltpu.VMEM((2, slots, full // 4), BF16)
    hbm = pl.BlockSpec(memory_space=pltpu.HBM)
    return pl.pallas_call(
        cross_pack_kernel,
        out_shape=[cross, cross, jax.ShapeDtypeStruct((1, w_router.shape[0]), F32)],
        in_specs=[hbm] * 6,
        out_specs=[VMEM] * 3,
        scratch_shapes=[
            pltpu.VMEM((2, slots, full // 4), F32),
            pltpu.VMEM(route_pos.shape, jnp.int32),
            pltpu.VMEM(w_router.shape, BF16),
            pltpu.SemaphoreType.DMA((6,)),
        ],
        compiler_params=params(),
        cost_estimate=cost(0, 10 * slots * full),
        name="cross_pack",
    )(*in_hbm(route_pos, w_router, keys, values, queries, d_gated))


def sib_pack_kernel(pos_ref, k_ref, v_ref, q_ref, dg_ref, out, wide, sems):
    slots, half = out.shape[1], out.shape[2]
    cols = pl.ds(pl.multiple_of((1 - here()[0]) * half, HEAD), half)
    sources = ((k_ref, out.at[0]), (dg_ref, wide), (v_ref, out.at[1]), (q_ref, out.at[2]))
    copies = [pltpu.make_async_copy(src.at[0, :, cols], dst, sems.at[i]) for i, (src, dst) in enumerate(sources)]
    for c in copies:
        c.start()
    live = live_rows(pos_ref, slots)
    copies[0].wait()
    out[0] = mark_dead(out[0], live)
    copies[1].wait()
    out[3] = wide[...].astype(BF16)
    copies[2].wait()
    copies[3].wait()


def sib_pack(route_pos, keys, values, queries, d_gated):
    _, slots, full = keys.shape
    hbm = pl.BlockSpec(memory_space=pltpu.HBM)
    return pl.pallas_call(
        sib_pack_kernel,
        out_shape=pltpu.VMEM((4, slots, full // 2), BF16),
        in_specs=[VMEM, hbm, hbm, hbm, hbm],
        out_specs=VMEM,
        scratch_shapes=[pltpu.VMEM((slots, full // 2), F32), pltpu.SemaphoreType.DMA((4,))],
        compiler_params=params(),
        cost_estimate=cost(0, 20 * slots * full),
        name="sib_pack",
    )(route_pos, *in_hbm(keys, values, queries, d_gated))


def pair_gate_kernel(parts, live_ref, rows_x, w_ref, local, stats, out_ref, message):
    chunk = w_ref.shape[1] // parts
    slots = rows_x.shape[1]
    for i in range(2):
        total = jnp.zeros((8, slots), F32)
        for j in range(parts):
            w_rows = jnp.broadcast_to(w_ref[:, j * chunk : (j + 1) * chunk], (8, chunk)).astype(BF16)
            cols = pl.ds(pl.multiple_of((lax.axis_index("dp") ^ j) * chunk, HEAD), chunk)
            total = total + nt(w_rows, rows_x[i, :, cols])
        lanes = slice(i * slots, (i + 1) * slots)
        out_ref[:, lanes] = live_ref[:, lanes] / (1.0 + jnp.exp(-total[0:1]))
    first = here()[1] == 0
    heads = stats.shape[1]
    for i in range(3):
        message[i] = jnp.where(first, stats[i], local[i, heads:])
    message[3] = jnp.broadcast_to(out_ref[...], message.shape[1:])


def pair_gate(live, rows_x, w_full, local, stats, parts):
    _, heads, lanes = stats.shape
    return pl.pallas_call(
        functools.partial(pair_gate_kernel, parts),
        out_shape=[jax.ShapeDtypeStruct(live.shape, F32), jax.ShapeDtypeStruct((4, heads, lanes), F32)],
        in_specs=[VMEM] * 5,
        out_specs=[VMEM] * 2,
        compiler_params=params(),
        cost_estimate=cost(16 * rows_x.size, rows_x.size * 2),
        name="router_gate",
    )(live, rows_x, w_full, local, stats)


def local_mask(core, pair):
    slots = pair.shape[1] // 2
    key = lax.broadcasted_iota(jnp.int32, (slots, slots), 0)
    query = lax.broadcasted_iota(jnp.int32, (slots, slots), 1)
    causal = key <= query
    own_live = pair[0, :slots, :slots].astype(F32) < MARK_LIMIT
    sib_live = pair[0, slots:, :slots].astype(F32) < MARK_LIMIT
    own_rows = jnp.concatenate([own_live & causal, own_live & (core == 0)], axis=1)
    sib_rows = jnp.concatenate([sib_live & (core == 1), sib_live & causal], axis=1)
    return jnp.concatenate([own_rows, sib_rows], axis=0)


def kept_stats(scores, gw, kept, stats, h):
    top = jnp.max(scores, axis=0, keepdims=True)
    e = jnp.exp(scores - top).astype(BF16)
    gw = gw.astype(BF16)
    kept[0, h] = e
    kept[1, h] = gw
    e = e.astype(F32)
    stats[0, h : h + 1] = top
    stats[1, h : h + 1] = jnp.sum(e, axis=0, keepdims=True)
    stats[2, h : h + 1] = jnp.sum(e * gw.astype(F32), axis=0, keepdims=True)


def partial_stats(scores, gw, stats, h):
    top = jnp.max(scores, axis=0, keepdims=True)
    e = jnp.exp(scores - top)
    stats[0, h : h + 1] = top
    stats[1, h : h + 1] = jnp.sum(e, axis=0, keepdims=True)
    stats[2, h : h + 1] = jnp.sum(e * gw, axis=0, keepdims=True)


def local_stats_kernel(scale, pos_ref, k_ref, v_ref, q_ref, dg_ref, sib, x_ref, x_sib, stats, live, near, far, rows_x, wide, sems, x_sems):
    slots, half = sib.shape[1], sib.shape[2]
    width = half // 2
    core = here()[0]
    own, other = slice(0, slots), slice(slots, 2 * slots)
    stages = []
    for g, pair in enumerate((near, far)):
        cols = slice(g * width, (g + 1) * width)
        held = pl.ds(pl.multiple_of(core * half + g * width, HEAD), width)
        copies = [
            pltpu.make_async_copy(ref.at[0, :, held], pair.at[j, own], sems.at[8 * g + j])
            for j, ref in enumerate((k_ref, v_ref, q_ref))
        ]
        copies.append(pltpu.make_async_copy(dg_ref.at[0, :, held], wide.at[:, cols], sems.at[8 * g + 3]))
        for j in range(4):
            copies.append(pltpu.make_async_copy(sib.at[j, :, cols], pair.at[j, other], sems.at[8 * g + 4 + j]))
        for c in copies:
            c.start()
        stages.append(copies)
    x_copies = []
    depth = x_ref.shape[2] // 2
    for i, ref in enumerate((x_ref, x_sib)):
        for g in range(2):
            cols = slice(g * depth, (g + 1) * depth)
            x_copies.append(pltpu.make_async_copy(ref.at[0, :, cols], rows_x.at[i, :, cols], x_sems.at[2 * i + g]))
    for c in x_copies:
        c.start()
    rows_live = live_rows(pos_ref, slots)
    mask = None
    for g, pair in enumerate((near, far)):
        cols = slice(g * width, (g + 1) * width)
        for c in stages[g]:
            c.wait()
        pair[0, own] = mark_dead(pair[0, own], rows_live)
        pair[3, own] = wide[:, cols].astype(BF16)
        if mask is None:
            mask = local_mask(core, pair)
            marks = nt(jnp.ones((8, HEAD), BF16), pair[0, :, :HEAD])[0:1]
            live[...] = jnp.where(marks < MARK_LIMIT, 1.0, 0.0)
        for h in range(width // HEAD):
            at = slice(h * HEAD, (h + 1) * HEAD)
            scores = jnp.where(mask, nt(pair[0, :, at], pair[2, :, at]) * scale, NEG_FILL)
            partial_stats(scores, nt(pair[1, :, at], pair[3, :, at]), stats, g * width // HEAD + h)
    for c in x_copies:
        c.wait()


def local_stats(route_pos, keys, values, queries, d_gated, sib, x_routed, x_sib):
    _, slots, half = sib.shape
    heads = half // HEAD
    anywhere = pl.BlockSpec(memory_space=pl.ANY)
    return pl.pallas_call(
        functools.partial(local_stats_kernel, HEAD**-0.5),
        out_shape=[
            jax.ShapeDtypeStruct((3, heads, 2 * slots), F32),
            jax.ShapeDtypeStruct((1, 2 * slots), F32),
            pltpu.VMEM((4, 2 * slots, half // 2), BF16),
            pltpu.VMEM((4, 2 * slots, half // 2), BF16),
            pltpu.VMEM((2, slots, x_routed.shape[2]), BF16),
        ],
        in_specs=[VMEM] + [anywhere] * 7,
        out_specs=[VMEM] * 5,
        scratch_shapes=[pltpu.VMEM((slots, half), F32), pltpu.SemaphoreType.DMA((16,)), pltpu.SemaphoreType.DMA((4,))],
        compiler_params=params(),
        cost_estimate=cost(16 * slots * slots * half, 16 * slots * half, 4 * slots * slots * half // HEAD),
        name="local_stats",
    )(route_pos, *in_hbm(keys, values, queries, d_gated), sib, x_routed, x_sib)


def cross_stats_kernel(scale, near, far, straight, diag, cross, stats, kept):
    slots, width = straight.shape[1], straight.shape[2]
    chip = here()[1]
    top, bottom = slice(0, slots), slice(slots, 2 * slots)

    @pl.when(chip == 0)
    def _():
        for part in range(2):
            cross[part] = far[part]
            cross[2 + part, top] = straight[part]
            cross[2 + part, bottom] = diag[part]

    @pl.when(chip != 0)
    def _():
        for part in range(2):
            cross[part, top] = straight[part]
            cross[part, bottom] = diag[part]
            cross[2 + part] = near[2 + part]

    live = cross[0, :, :HEAD].astype(F32) < MARK_LIMIT
    mask = jnp.concatenate([live] * (2 * slots // HEAD), axis=1)
    heads = width // HEAD
    for h in range(heads):
        cols = slice(h * HEAD, (h + 1) * HEAD)
        scores = jnp.where(mask, nt(cross[0, :, cols], cross[2, :, cols]) * scale, NEG_FILL)
        kept_stats(scores, nt(cross[1, :, cols], cross[3, :, cols]), kept, stats, h)


def cross_stats(near, far, straight, diag):
    _, slots, width = straight.shape
    heads = width // HEAD
    return pl.pallas_call(
        functools.partial(cross_stats_kernel, HEAD**-0.5),
        out_shape=[
            pltpu.VMEM((4, 2 * slots, width), BF16),
            jax.ShapeDtypeStruct((3, heads, 2 * slots), F32),
            pltpu.VMEM((2, heads, 2 * slots, 2 * slots), BF16),
        ],
        in_specs=[VMEM] * 4,
        out_specs=[VMEM] * 3,
        compiler_params=params(),
        cost_estimate=cost(16 * slots * slots * width, 32 * slots * width, 4 * slots * slots * heads),
        name="cross_stats",
    )(near, far, straight, diag)


NONE = (-3e38, 0.0, 0.0)


def merge(first, second):
    top = jnp.maximum(first[0], second[0])
    a, b = jnp.exp(first[0] - top), jnp.exp(second[0] - top)
    inverse = 1.0 / (first[1] * a + second[1] * b)
    return a * inverse, (first[2] * a + second[2] * b) * inverse


def choose(flag, yes, no):
    return [jnp.where(flag, y, n) for y, n in zip(yes, no)]


def gradients(q, k, dg, e, gw, scale, factor, delta):
    weights = e * factor
    ds = (weights * ((gw - delta) * scale)).astype(BF16)
    return tn(ds, k), nn(ds, q), nn(weights.astype(BF16), dg)


def local_gradients(pair, h, mask, scale, top, factor, delta):
    cols = slice(h * HEAD, (h + 1) * HEAD)
    k, v, q, dg = [pair[i, :, cols] for i in range(4)]
    e = jnp.exp(jnp.where(mask, nt(k, q) * scale, NEG_FILL) - top)
    return gradients(q, k, dg, e, nt(v, dg), scale, factor, delta)


def near_grad_kernel(scale, pair, local, stats, gates, dq_out, own_out, sib_out, sum_out):
    slots, width = own_out.shape[1], own_out.shape[2]
    heads = width // HEAD
    first = here()[1] == 0
    near = [local[i, :heads] for i in range(3)]
    factor, delta = merge(near, choose(first, NONE, [stats[i] for i in range(3)]))
    factor = factor * gates[...]
    sum_out[...] = jnp.sum(delta, axis=0, keepdims=True)
    mask = local_mask(here()[0], pair)
    for h in range(heads):
        cols = slice(h * HEAD, (h + 1) * HEAD)
        row = slice(h, h + 1)
        dq, dk, dv = local_gradients(pair, h, mask, scale, near[0][row], factor[row], delta[row])
        dq_out[:, cols] = dq
        for i, part in enumerate((dk, dv)):
            own_out[i, :, cols] = part[:slots].astype(BF16)
            sib_out[i, :, cols] = part[slots:].astype(BF16)


def near_grad(pair, local, stats, gates):
    _, rows, width = pair.shape
    slots = rows // 2
    out = pltpu.VMEM((2, slots, width), BF16)
    return pl.pallas_call(
        functools.partial(near_grad_kernel, HEAD**-0.5),
        out_shape=[pltpu.VMEM((2 * slots, width), F32), out, out, jax.ShapeDtypeStruct(gates.shape, F32)],
        in_specs=[VMEM] * 4,
        out_specs=[VMEM] * 4,
        compiler_params=params(),
        cost_estimate=cost(20 * slots * slots * width, 40 * slots * width),
        name="near_grad",
    )(pair, local, stats, gates)


def put_terms(grad, rows_x, out_ref):
    high = grad.astype(BF16)
    rest = grad - high.astype(F32)
    mid = rest.astype(BF16)
    low = (rest - mid.astype(F32)).astype(BF16)
    slots = rows_x.shape[1]
    row = lax.broadcasted_iota(jnp.int32, (8, grad.shape[1]), 0)
    lhs = jnp.where(row == 0, high.astype(F32), jnp.where(row == 1, mid.astype(F32), jnp.where(row == 2, low.astype(F32), 0.0)))
    lhs = lhs.astype(BF16)
    term = jnp.sum(nn(lhs[:, :slots], rows_x[0]) + nn(lhs[:, slots:], rows_x[1]), axis=0, keepdims=True)
    parts, copies, _, chunk = out_ref.shape
    for j in range(parts):
        for i in range(copies):
            out_ref[j, i] = term[:, j * chunk : (j + 1) * chunk]


def cross_grad_kernel(scale, total, cross, kept, stats, local, heard, gates, near_dq, near_sum, rows_x, straight, diag, dq_out, keep, final, terms, held, sem):
    slots, width = straight.shape[1], straight.shape[2]
    heads = width // HEAD
    first = here()[1] == 0
    late = jnp.where(first, 0.0, 1.0)
    mine = [stats[i] for i in range(3)]
    other = [heard[i] for i in range(3)]
    near = [local[i, :heads] for i in range(3)]
    far = [local[i, heads:] for i in range(3)]
    factor, delta = merge(mine, choose(first, other, near))
    factor = factor * jnp.where(first, heard[3], jnp.broadcast_to(gates[...], factor.shape))
    final[0], final[1] = merge(far, choose(first, NONE, other))
    sums = near_sum[...] + jnp.sum(final[1], axis=0, keepdims=True)
    put_terms(sums * gates[...] * (1.0 - gates[...]) * (1.0 / total), rows_x, held)
    leaving = pltpu.make_async_copy(held, terms, sem)
    leaving.start()
    for h in range(heads):
        cols = slice(h * HEAD, (h + 1) * HEAD)
        row = slice(h, h + 1)
        dq, dk, dv = gradients(
            cross[2, :, cols], cross[0, :, cols], cross[3, :, cols],
            kept[0, h].astype(F32), kept[1, h].astype(F32), scale, factor[row], delta[row],
        )
        dq_out[:, cols] = (near_dq[:, cols] + late * dq).astype(BF16)
        keep[0, :, cols] = dk.astype(BF16)
        keep[1, :, cols] = dv.astype(BF16)
        sent = jnp.where(first, dq, dk).astype(BF16)
        straight[0, :, cols] = sent[:slots]
        diag[0, :, cols] = sent[slots:]
        straight[1, :, cols] = dv[:slots].astype(BF16)
        diag[1, :, cols] = dv[slots:].astype(BF16)
    leaving.wait()


def cross_grad(cross, kept, stats, local, heard, gates, near_dq, near_sum, rows_x, parts, copies, total):
    _, rows, width = cross.shape
    slots = rows // 2
    out = pltpu.VMEM((2, slots, width), BF16)
    spread = (parts, copies, 1, rows_x.shape[2] // parts)
    return pl.pallas_call(
        functools.partial(cross_grad_kernel, HEAD**-0.5, total),
        out_shape=[
            out,
            out,
            pltpu.VMEM((rows, width), BF16),
            pltpu.VMEM((2, rows, width), BF16),
            jax.ShapeDtypeStruct((2, width // HEAD, rows), F32),
            pltpu.HBM(spread, F32),
        ],
        in_specs=[VMEM] * 9,
        out_specs=[VMEM] * 5 + [pl.BlockSpec(memory_space=pltpu.HBM)],
        scratch_shapes=[pltpu.VMEM(spread, F32), pltpu.SemaphoreType.DMA],
        compiler_params=params(),
        cost_estimate=cost(24 * slots * slots * width, 64 * slots * width),
        name="cross_grad",
    )(cross, kept, stats, local, heard, gates, near_dq, near_sum, rows_x)


def far_grad_kernel(scale, pair, local, final, gates, keep, near_dq, near_own, near_sib, own_out, sib_out):
    slots, width = pair.shape[1] // 2, pair.shape[2]
    heads = width // HEAD
    early = jnp.where(here()[1] == 0, 1.0, 0.0)
    factor = final[0] * gates[...]
    mask = local_mask(here()[0], pair)
    own_out[0, :, :width] = near_dq[:slots]
    sib_out[0, :, :width] = near_dq[slots:]
    for i in range(2):
        own_out[1 + i, :, :width] = near_own[i]
        sib_out[1 + i, :, :width] = near_sib[i]
    for h in range(heads):
        cols = slice(width + h * HEAD, width + (h + 1) * HEAD)
        at = slice(h * HEAD, (h + 1) * HEAD)
        row = slice(h, h + 1)
        top = local[0, heads + h : heads + h + 1]
        dq, dk, dv = local_gradients(pair, h, mask, scale, top, factor[row], final[1, row])
        dk = dk + early * keep[0, :, at].astype(F32)
        dv = dv + early * keep[1, :, at].astype(F32)
        for i, part in enumerate((dq, dk, dv)):
            own_out[i, :, cols] = part[:slots].astype(BF16)
            sib_out[i, :, cols] = part[slots:].astype(BF16)


def far_grad(pair, local, final, gates, keep, near_dq, near_own, near_sib):
    _, rows, width = pair.shape
    slots, half = rows // 2, 2 * width
    out = jax.ShapeDtypeStruct((3, slots, half), BF16)
    return pl.pallas_call(
        functools.partial(far_grad_kernel, HEAD**-0.5),
        out_shape=[out, out],
        in_specs=[VMEM] * 8,
        out_specs=[VMEM] * 2,
        compiler_params=params(),
        cost_estimate=cost(20 * slots * slots * half, 40 * slots * half),
        name="far_grad",
    )(pair, local, final, gates, keep, near_dq, near_own, near_sib)


def own_join_kernel(own, dq_out, dk_out, dv_out, waiting, total, sems):
    slots, half = own.shape[1], own.shape[2]
    width = half // 2
    core, chip = here()
    cols = pl.ds(pl.multiple_of(core * half, HEAD), half)
    stores = []
    for j, out in enumerate((dq_out, dk_out, dv_out)):
        total[j] = own[j].astype(F32)
        stores.append(pltpu.make_async_copy(total.at[j], out.at[0, :, cols], sems.at[j]))
        stores[-1].start()
    waiting[0] = jnp.where(chip == 0, total[1, :, :width], total[0, :, width:]).astype(BF16)
    waiting[1] = own[2, :, :width]
    for c in stores:
        c.wait()


def own_join(own, shape):
    out = pltpu.HBM(shape, F32)
    _, slots, half = own.shape
    hbm = pl.BlockSpec(memory_space=pltpu.HBM)
    return pl.pallas_call(
        own_join_kernel,
        out_shape=[out] * 3 + [jax.ShapeDtypeStruct((2, slots, half // 2), BF16)],
        in_specs=[VMEM],
        out_specs=[hbm] * 3 + [VMEM],
        scratch_shapes=[pltpu.VMEM((3, slots, half), F32), pltpu.SemaphoreType.DMA((3,))],
        compiler_params=params(),
        cost_estimate=cost(0, 18 * own.size),
        name="own_join",
    )(own)


def sib_join_kernel(sib, dq_in, dk_in, dv_in, dq_out, dk_out, dv_out, waiting, low, total, in_sems, out_sems):
    half = sib.shape[2]
    width = half // 2
    core, chip = here()
    loads = [pltpu.make_async_copy(sib.at[j], low.at[j], in_sems.at[j]) for j in range(3)]
    for c in loads:
        c.start()
    cols = pl.ds(pl.multiple_of((1 - core) * half, HEAD), half)
    stores = []
    for j, out in enumerate((dq_out, dk_out, dv_out)):
        loads[j].wait()
        total[j] = low[j].astype(F32)
        stores.append(pltpu.make_async_copy(total.at[j], out.at[0, :, cols], out_sems.at[j]))
        stores[-1].start()
    waiting[0] = jnp.where(chip == 0, total[1, :, :width], total[0, :, width:]).astype(BF16)
    waiting[1] = low[2, :, :width]
    for c in stores:
        c.wait()


def sib_join(sib, outs):
    _, slots, half = sib.shape
    hbm = pl.BlockSpec(memory_space=pltpu.HBM)
    return pl.pallas_call(
        sib_join_kernel,
        out_shape=[pltpu.HBM(o.shape, F32) for o in outs] + [pltpu.VMEM((2, slots, half // 2), BF16)],
        in_specs=[pl.BlockSpec(memory_space=pl.ANY)] + [hbm] * 3,
        out_specs=[hbm] * 3 + [VMEM],
        scratch_shapes=[
            pltpu.VMEM((3, slots, half), BF16),
            pltpu.VMEM((3, slots, half), F32),
            pltpu.SemaphoreType.DMA((3,)),
            pltpu.SemaphoreType.DMA((3,)),
        ],
        input_output_aliases={1: 0, 2: 1, 3: 2},
        compiler_params=params(),
        cost_estimate=cost(0, 12 * sib.size),
        name="sib_join",
    )(sib, *in_hbm(*outs))


def add_back_kernel(own, sib, diag, straight, dq_in, dk_in, dv_in, dq_out, dk_out, dv_out, total, sems):
    width = straight.shape[2]
    core, chip = here()
    ends = ((own, straight, 2 * core * width), (sib, diag, 2 * (1 - core) * width))

    def store(i, j, out, offset):
        cols = pl.ds(pl.multiple_of(ends[i][2] + offset, HEAD), width)
        copy = pltpu.make_async_copy(total.at[i, j], out.at[0, :, cols], sems.at[2 * i + j])
        copy.start()
        return copy

    @pl.when(chip == 0)
    def _():
        copies = []
        for i, (waiting, back, _) in enumerate(ends):
            for j, out in enumerate((dk_out, dv_out)):
                total[i, j] = waiting[j].astype(F32) + back[j].astype(F32)
                copies.append(store(i, j, out, 0))
        for c in copies:
            c.wait()

    @pl.when(chip != 0)
    def _():
        copies = []
        for i, (waiting, back, _) in enumerate(ends):
            total[i, 0] = waiting[0].astype(F32) + back[0].astype(F32)
            copies.append(store(i, 0, dq_out, width))
        for c in copies:
            c.wait()


def add_back(own, sib, straight, diag, outs):
    hbm = pl.BlockSpec(memory_space=pltpu.HBM)
    return pl.pallas_call(
        add_back_kernel,
        out_shape=[pltpu.HBM(o.shape, F32) for o in outs],
        in_specs=[VMEM] * 4 + [hbm] * 3,
        out_specs=[hbm] * 3,
        scratch_shapes=[pltpu.VMEM((2, *own.shape), F32), pltpu.SemaphoreType.DMA((4,))],
        input_output_aliases={4: 0, 5: 1, 6: 2},
        compiler_params=params(),
        cost_estimate=cost(0, 24 * own.size),
        name="add_back",
    )(own, sib, diag, straight, *in_hbm(*outs))


def swap_body(route_pos, x_routed, w_router, queries, keys, values, d_gated):
    slots = queries.shape[1]
    n, ndp = lax.axis_size("ctx"), lax.axis_size("dp")

    def send(a, flip):
        return lax.ppermute(a, "ctx", [(i, i ^ flip) for i in range(n)])

    def beside(fn, *operands):
        def skip(*ops):
            return jax.tree.map(lambda o: jnp.zeros(o.shape, o.dtype), jax.eval_shape(fn, *ops))

        return lax.cond(route_pos[0, 0] >= -1, fn, skip, *operands)

    def after(value, *others):
        return lax.optimization_barrier((value, *others))[0]

    def widen(part, step, *first):
        other = lax.ppermute(part, "dp", [(i, i ^ step) for i in range(ndp)])
        return jnp.concatenate([part, after(other, *first)], axis=1)

    def exchange_phase(x_routed, w_part, theirs):
        sib, x_sib = send(theirs, 1), send(x_routed, 1)
        step = 2
        while 2 * step < ndp:
            w_part = widen(w_part, step)
            step *= 2
        return sib, x_sib, w_part

    def far_phase(*operands):
        own_out, sib_out = far_grad(*operands)
        sib_in = send(sib_out, 1)
        *outs, waiting = own_join(own_out, queries.shape)
        return outs, waiting, sib_in

    out_s, out_d, w_part = cross_pack(route_pos, w_router, keys, values, queries, d_gated)
    in_s, in_d = send(out_s, 2), send(out_d, 3)

    theirs = sib_pack(after(route_pos, out_s), keys, values, queries, d_gated)
    if ndp > 1:
        w_part = widen(w_part, 1, theirs)
    sib, x_sib, w_part = beside(exchange_phase, x_routed, w_part, theirs)
    local, live, near, far, rows_x = local_stats(route_pos, keys, values, queries, d_gated, sib, x_routed, x_sib)
    cross, stats, kept = cross_stats(near, far, in_s, in_d)
    if ndp > 2:
        w_part = widen(w_part, ndp // 2, stats)
    gates, message = pair_gate(live, rows_x, w_part, local, stats, ndp)

    heard = send(message, 2)
    near_dq, near_own, near_sib, near_sum = near_grad(near, local, stats, gates)
    total = float(ndp * n * slots // 2)
    back_s, back_d, dq_low, keep, final, terms = cross_grad(
        cross, kept, stats, local, heard, gates, near_dq, near_sum, rows_x, ndp, n, total
    )

    ret_d, ret_s = send(back_d, 3), send(back_s, 2)
    shared = lax.all_to_all(terms.reshape(ndp * n, 1, -1), ("dp", "ctx"), 0, 0, tiled=True)
    outs, waiting, sib_in = beside(far_phase, far, local, final, gates, keep, dq_low, near_own, near_sib)
    *outs, waiting_sib = sib_join(sib_in, outs)
    dq, dk, dv = add_back(waiting, waiting_sib, ret_s, ret_d, outs)
    router_grad = jnp.sum(after(shared, dq), axis=(0, 1))
    return dq, dk, dv, router_grad


def body(route_pos, x_routed, w_router, queries, keys, values, d_gated):
    slots, full = queries.shape[1], queries.shape[2]
    n, ndp = lax.axis_size("ctx"), lax.axis_size("dp")
    chips = n // 2
    me, dp_me = lax.axis_index("ctx"), lax.axis_index("dp")
    core = (me % 2).astype(jnp.int32).reshape(1)
    half = full // 2
    groups = GROUPS if (half // HEAD) % GROUPS == 0 else 1
    width = half // groups

    sib_pairs = [(i, i ^ 1) for i in range(n)]

    def forward_pairs(step, flip):
        return [(i, (i + 2 * step) ^ flip) for i in range(n) if i + 2 * step < n]

    def back_pairs(step, flip):
        return [(b, a) for a, b in forward_pairs(step, flip)]

    def to_sib(a):
        return lax.ppermute(a, "ctx", sib_pairs)

    links = [(step, flip) for step in range(1, chips) for flip in (0, 1)]

    w_row = w_router.reshape(1, -1)
    w_parts = [w_row] + [
        lax.ppermute(w_row, "dp", [(i, (i + s) % ndp) for i in range(ndp)]) for s in range(1, ndp)
    ]
    live = (route_pos >= 0).astype(jnp.int32)
    lives = [live, to_sib(live)] + [lax.ppermute(live, "ctx", forward_pairs(*link)) for link in links]
    live_all = jnp.concatenate(lives, axis=0)

    kv_mine, kv_theirs = pack(core, keys, values, groups, width)
    kv_far = [
        [lax.ppermute((kv_theirs if flip else kv_mine)[g], "ctx", forward_pairs(step, flip)) for step, flip in links]
        for g in range(groups)
    ]
    q_mine, q_theirs = pack(core, queries, d_gated, groups, width)
    kv_sib = [to_sib(a) for a in kv_theirs]
    q_sib = [to_sib(a) for a in q_theirs]

    offsets = ((dp_me - jnp.arange(ndp)) % ndp).astype(jnp.int32)
    gate = router_gate(offsets, route_pos, x_routed, w_parts)
    gates = (gate, to_sib(gate))

    accs = (jnp.zeros((1, slots), F32), jnp.zeros((1, slots), F32))
    dq_own, sib_in, kv_own, back = [], [], [], []
    for g in range(groups):
        dq, sib_out, kv_local, kv_remote, accs = attention(
            core, live_all, gates, accs, q_mine[g], q_sib[g], [kv_mine[g], kv_sib[g], *kv_far[g]]
        )
        back.append([lax.ppermute(a, "ctx", back_pairs(*link)) for a, link in zip(kv_remote, links)])
        sib_in.append(to_sib(sib_out))
        dq_own.append(dq)
        kv_own.append(kv_local)

    targets = ((dp_me + jnp.arange(ndp)) % ndp).astype(jnp.int32)
    terms = router_terms(targets, gate, accs[0], to_sib(accs[1]), x_routed, ndp)
    mine = terms[0]
    for s in range(1, ndp):
        mine = mine + lax.ppermute(terms[s], "dp", [(i, (i + s) % ndp) for i in range(ndp)])
    total = mine
    for s in range(1, n):
        total = total + lax.ppermute(mine, "ctx", [(i, (i + s) % n) for i in range(n)])
    router_grad = total[0] / float(ndp * n * slots // 2)

    dq, dk, dv = combine(core, dq_own, sib_in, kv_own, back, queries.shape)
    return dq, dk, dv, router_grad


def solution(mesh):
    placed = (
        P("dp", "ctx"),
        P("dp", "ctx", None),
        P("dp"),
        P("dp", "ctx", None),
        P("dp", "ctx", None),
        P("dp", "ctx", None),
        P("dp", "ctx", None),
    )
    ndp = mesh.shape["dp"]
    paired = mesh.shape["ctx"] == 4 and ndp & (ndp - 1) == 0
    return jax.shard_map(
        swap_body if paired else body,
        mesh=mesh,
        in_specs=placed,
        out_specs=(P("dp", "ctx", None), P("dp", "ctx", None), P("dp", "ctx", None), P("dp")),
        check_vma=False,
    )
```
